32 devices in a mesh: grp: 2 (over y), res: 8 (over z, x), seq: 2 (over core).
Axes of the slice: x: 2, y: 2, z: 4, core: 2. Of those that a mesh axis runs over, the one named last changes fastest.
Arguments:
- homolog_matrix: bfloat16 [128, 32, 256], P(('grp', 'seq'), 'res'), parts along dimension 0, may hold values from -600 to 600
- standardizer_scaling: float32 [256], replicated, may hold values from 0.4 to 1.6
- standardizer_offset: float32 [256], replicated, may hold values from -3 to 3
- left_projection_matrix: bfloat16 [256, 32], replicated, may hold values from -0.375 to 0.375
- left_offset_vector: float32 [32], replicated, may hold values from -3 to 3
- right_projection_matrix: bfloat16 [256, 32], replicated, may hold values from -0.375 to 0.375
- right_offset_vector: float32 [32], replicated, may hold values from -3 to 3
- coupling_matrix: bfloat16 [1024, 128], replicated, may hold values from -0.75 to 0.75
- coupling_offset: float32 [128], replicated, may hold values from -3 to 3
- coupling_cotangent: bfloat16 [64, 32, 128], P(('grp', 'res'), 'seq'), parts along dimension 0, may hold values from -6 to 6
Outputs:
- pair_delta: bfloat16 [64, 32, 128], P(('grp', 'res'), 'seq'), parts along dimension 0
- alignment_gradient: bfloat16 [128, 32, 256], P(('grp', 'seq'), 'res'), parts along dimension 0
The draws below stay inside these ranges and needn't reach their ends.
There are 2 independent parts, one for each index of `grp`. The reference program is written for one: setup_inputs(seed, part) draws one part's arguments, and reference() takes and returns one part's arrays. A program takes and returns all parts, laid end to end along the dimension named above; an argument that names none is the same for every part. Nothing has to cross between parts.
All inputs are finite; a program needn't handle non-finite values.
Results may differ from the reference program's by a relative error of at most 0.0063.
Values may be sent and summed in bfloat16 or wider, within the bound.
No kernel may reach another device: no remote copies, remote signals or barrier semaphores. Data moves between devices by JAX's collectives and lax.ppermute only.
A program may use at most 128 MiB of HBM per device.

```python
import math
import jax
import jax.numpy as jnp
from jax import lax

C = 256
P_SIZE = 32
K = 128
SEQS = 64
RES = 32


def draw_homolog_matrix(key, part):
    key = jax.random.fold_in(key, 11)
    k_chan, k_row, k_noise = jax.random.split(key, 3)
    chan_scale = jnp.exp(jax.random.uniform(k_chan, (C,), jnp.float32, 0.0, math.log(10.0)))
    row_scale = jnp.exp(jax.random.uniform(k_row, (SEQS, RES, 1), jnp.float32, 0.0, math.log(10.0)))
    noise = jnp.clip(jax.random.normal(k_noise, (SEQS, RES, C), jnp.float32), -6.0, 6.0)
    return (noise * row_scale * chan_scale).astype(jnp.bfloat16)


def level_of(stream_key, shape, cuts, low, high):
    loudness = 1.0
    for position, blocks in cuts:
        steps = jax.random.uniform(jax.random.fold_in(jax.random.fold_in(stream_key, 6), position), (blocks,), jnp.float32, low / len(cuts), high / len(cuts))
        loudness = loudness * jnp.repeat(jnp.exp(steps), shape[position] // blocks).reshape((-1,) + (1,) * (len(shape) - 1 - position))
    return loudness


def gaussian(rng, dims, scale, reach, shards=(), dtype=jnp.bfloat16):
    values = scale * jax.random.normal(rng, dims, jnp.float32)
    if shards:
        values = values * level_of(rng, dims, shards, -0.22, 0.18)
    return jnp.clip(values, -reach, reach).astype(dtype)


def setup_inputs(seed: int = 0, part: int = 0) -> dict:
    seeds = jax.random.split(jax.random.key(seed), 11)
    part_splits = jax.random.split(jax.random.fold_in(seeds[10], part), 11)
    homolog_matrix = draw_homolog_matrix(jax.random.fold_in(jax.random.fold_in(seeds[10], part), 71), part)
    standardizer_scaling = jnp.clip(1.0 + 0.12 * jax.random.normal(seeds[1], (C,), jnp.float32), 0.4, 1.6)
    standardizer_offset = gaussian(seeds[2], (C,), 0.5, 3.0, (), jnp.float32)
    left_projection_matrix = gaussian(seeds[3], (C, P_SIZE), C ** -0.5, 0.375)
    left_offset_vector = gaussian(seeds[4], (P_SIZE,), 0.3, 3.0, (), jnp.float32)
    right_projection_matrix = gaussian(seeds[5], (C, P_SIZE), C ** -0.5, 0.375)
    right_offset_vector = gaussian(seeds[6], (P_SIZE,), 0.3, 3.0, (), jnp.float32)
    coupling_matrix = gaussian(seeds[7], (P_SIZE * P_SIZE, K), (P_SIZE * P_SIZE // 16) ** -0.5, 0.75)
    coupling_offset = gaussian(seeds[8], (K,), 0.5, 3.0, (), jnp.float32)
    coupling_cotangent = gaussian(part_splits[9], (RES, RES, K), 1.0, 6.0, ((0, 8), (1, 2)))
    return dict(homolog_matrix=homolog_matrix, standardizer_scaling=standardizer_scaling, standardizer_offset=standardizer_offset, left_projection_matrix=left_projection_matrix, left_offset_vector=left_offset_vector, right_projection_matrix=right_projection_matrix, right_offset_vector=right_offset_vector, coupling_matrix=coupling_matrix, coupling_offset=coupling_offset, coupling_cotangent=coupling_cotangent)


def standardize_features(homolog_matrix, scaling_multiplier, additive_offset):
    incoming_tensor = homolog_matrix.astype(jnp.float32)
    row_mean = lax.optimization_barrier(jnp.mean(incoming_tensor, axis=-1, keepdims=True))
    centred = incoming_tensor - row_mean
    reciprocal_spread = lax.rsqrt(lax.optimization_barrier(jnp.mean(centred * centred, axis=-1, keepdims=True)) + 1e-05)
    standardized_lines = centred * reciprocal_spread
    standardized_result = (standardized_lines * scaling_multiplier + additive_offset).astype(jnp.bfloat16)
    return (standardized_lines, reciprocal_spread, standardized_result)

def project(standardized_result, weight, additive_offset):
    shape_in = standardized_result.shape
    flat_rows = standardized_result.reshape(-1, shape_in[-1])
    result = jnp.dot(flat_rows, weight, preferred_element_type=jnp.float32) + additive_offset
    return result.astype(jnp.bfloat16).reshape(shape_in[:-1] + (weight.shape[1],))

def reference(homolog_matrix, standardizer_scaling, standardizer_offset, left_projection_matrix, left_offset_vector, right_projection_matrix, right_offset_vector, coupling_matrix, coupling_offset, coupling_cotangent):
    standardized_lines, reciprocal_spread, standardized_result = standardize_features(homolog_matrix, standardizer_scaling, standardizer_offset)
    left_proj = project(standardized_result, left_projection_matrix, left_offset_vector)
    right_proj = project(standardized_result, right_projection_matrix, right_offset_vector)
    wide_weight = coupling_matrix.astype(jnp.float32)
    step_rows = 8
    blocks = RES // step_rows
    left_blocks = left_proj.reshape(SEQS, blocks, step_rows, P_SIZE).transpose(1, 0, 2, 3)
    cot_blocks = coupling_cotangent.reshape(blocks, step_rows, RES, K)
    right_float = right_proj.astype(jnp.float32)

    def one_block(carry, items):
        left_block, cot_block = items
        left_float = left_block.astype(jnp.float32)
        outer_sum = jnp.einsum('sic,sjd->ijcd', left_float, right_float) / SEQS
        pair_block = jnp.dot(outer_sum.reshape(-1, P_SIZE * P_SIZE), wide_weight, precision=lax.Precision.HIGHEST) + coupling_offset
        pair_block = pair_block.astype(jnp.bfloat16).reshape(step_rows, RES, K)
        outer_cot = (jnp.dot(cot_block.reshape(-1, K), coupling_matrix.T, preferred_element_type=jnp.float32) / SEQS).astype(jnp.bfloat16)
        outer_cot = lax.optimization_barrier(outer_cot).astype(jnp.float32).reshape(step_rows, RES, P_SIZE, P_SIZE)
        left_cot_block = jnp.einsum('ijcd,sjd->sic', outer_cot, right_float)
        carry = carry + jnp.einsum('ijcd,sic->sjd', outer_cot, left_float)
        return (carry, (pair_block, left_cot_block))
    right_cot, (pair_blocks, left_cot_blocks) = lax.scan(one_block, jnp.zeros((SEQS, RES, P_SIZE), jnp.float32), (left_blocks, cot_blocks))
    pair_delta = pair_blocks.reshape(RES, RES, K)
    left_cot = left_cot_blocks.transpose(1, 0, 2, 3).reshape(SEQS, RES, P_SIZE)
    ln_cot = jnp.dot(left_cot.reshape(-1, P_SIZE), left_projection_matrix.astype(jnp.float32).T, precision=lax.Precision.HIGHEST)
    ln_cot = ln_cot + jnp.dot(right_cot.reshape(-1, P_SIZE), right_projection_matrix.astype(jnp.float32).T, precision=lax.Precision.HIGHEST)
    ln_cot = ln_cot.reshape(SEQS, RES, C)
    gain_gradient = ln_cot * standardizer_scaling
    alignment_gradient = reciprocal_spread * (gain_gradient - lax.optimization_barrier(jnp.mean(gain_gradient, axis=-1, keepdims=True)) - standardized_lines * lax.optimization_barrier(jnp.mean(gain_gradient * standardized_lines, axis=-1, keepdims=True)))
    return (pair_delta, alignment_gradient.astype(jnp.bfloat16))
```

```python
import jax
import jax.numpy as jnp
from jax import lax
from jax.sharding import PartitionSpec as P


def standardize_features(homolog_matrix, scaling_multiplier, additive_offset):
    incoming_tensor = homolog_matrix.astype(jnp.float32)
    row_mean = jnp.mean(incoming_tensor, axis=-1, keepdims=True)
    centred = incoming_tensor - row_mean
    reciprocal_spread = lax.rsqrt(jnp.mean(centred * centred, axis=-1, keepdims=True) + 1e-05)
    standardized_lines = centred * reciprocal_spread
    standardized_result = (standardized_lines * scaling_multiplier + additive_offset).astype(
        jnp.bfloat16
    )
    return (standardized_lines, reciprocal_spread, standardized_result)


def project_flat(flat_rows, weight, additive_offset):
    return (
        jnp.dot(flat_rows, weight, preferred_element_type=jnp.float32) + additive_offset
    ).astype(jnp.bfloat16)


def cot_outer(cot_block, coupling_matrix, seq_count, depth_p):
    first, second, pair_width = cot_block.shape
    result = (
        jnp.dot(
            cot_block.reshape(-1, pair_width), coupling_matrix.T, preferred_element_type=jnp.float32
        )
        / seq_count
    )
    return result.astype(jnp.bfloat16).reshape(first, second, depth_p, depth_p)


def body(
    homolog_matrix,
    standardizer_scaling,
    standardizer_offset,
    left_projection_matrix,
    left_offset_vector,
    right_projection_matrix,
    right_offset_vector,
    coupling_matrix,
    coupling_offset,
    coupling_cotangent,
):
    homolog_mesh_split, amino_mesh_split, feature_total = homolog_matrix.shape
    depth_p = left_projection_matrix.shape[1]
    pair_width = coupling_matrix.shape[1]
    seq_count = homolog_mesh_split * lax.axis_size("seq")
    res_count = amino_mesh_split * lax.axis_size("res")
    standardized_lines, reciprocal_spread, standardized_result = standardize_features(
        homolog_matrix, standardizer_scaling, standardizer_offset
    )
    flat_rows = standardized_result.reshape(homolog_mesh_split * amino_mesh_split, feature_total)
    left_proj = project_flat(flat_rows, left_projection_matrix, left_offset_vector).reshape(
        homolog_mesh_split, amino_mesh_split * depth_p
    )
    right_proj = project_flat(flat_rows, right_projection_matrix, right_offset_vector).reshape(
        homolog_mesh_split, amino_mesh_split * depth_p
    )
    seq_index = lax.axis_index("seq")
    swap = [(0, 1), (1, 0)]
    other_cot = lax.ppermute(coupling_cotangent, "seq", swap)
    cot_rows = jnp.where(
        seq_index == 0,
        jnp.concatenate([coupling_cotangent, other_cot], axis=1),
        jnp.concatenate([other_cot, coupling_cotangent], axis=1),
    )
    ranks = lax.axis_size("res")
    proj_both = jnp.concatenate([left_proj, right_proj], axis=0)
    cot_parts = cot_rows.reshape(amino_mesh_split, ranks, amino_mesh_split, pair_width)
    cot_parts = cot_parts.transpose(1, 0, 2, 3).reshape(
        ranks, amino_mesh_split * amino_mesh_split, pair_width
    )
    packed = jnp.concatenate(
        [jnp.broadcast_to(proj_both[None], (ranks,) + proj_both.shape), cot_parts], axis=1
    )
    packed = lax.all_to_all(packed, "res", split_axis=0, concat_axis=0, tiled=True)
    left_all = packed[:, :homolog_mesh_split].transpose(1, 0, 2).reshape(homolog_mesh_split, -1)
    right_all = (
        packed[:, homolog_mesh_split : 2 * homolog_mesh_split]
        .transpose(1, 0, 2)
        .reshape(homolog_mesh_split, -1)
    )
    cot_cols = packed[:, 2 * homolog_mesh_split :].reshape(res_count, amino_mesh_split, pair_width)
    left_own = left_proj.reshape(homolog_mesh_split, amino_mesh_split, depth_p)
    left_rows = left_all.reshape(homolog_mesh_split, res_count, depth_p)
    right_rows = right_all.reshape(homolog_mesh_split, res_count, depth_p)
    wide_weight = coupling_matrix.astype(jnp.float32)
    outer_sum = (
        jnp.einsum("sic,sjd->ijcd", left_own, right_rows, preferred_element_type=jnp.float32)
        / seq_count
    )
    pair_term = jnp.dot(
        outer_sum.reshape(-1, depth_p * depth_p), wide_weight, precision=lax.Precision.HIGHEST
    )
    pair_term = pair_term.reshape(amino_mesh_split, res_count, pair_width)
    half = res_count // 2
    own_half = lax.dynamic_slice_in_dim(pair_term, seq_index * half, half, axis=1)
    other_half = lax.dynamic_slice_in_dim(pair_term, (1 - seq_index) * half, half, axis=1)
    summed = own_half + lax.ppermute(other_half, "seq", swap)
    pair_delta = (summed + coupling_offset).astype(jnp.bfloat16)
    outer_rows = cot_outer(cot_rows, coupling_matrix, seq_count, depth_p)
    outer_cols = cot_outer(cot_cols, coupling_matrix, seq_count, depth_p)
    left_cot = jnp.einsum(
        "ijcd,sjd->sic", outer_rows, right_rows, preferred_element_type=jnp.float32
    )
    right_cot = jnp.einsum(
        "ijcd,sic->sjd", outer_cols, left_rows, preferred_element_type=jnp.float32
    )
    ln_cot = jnp.dot(
        left_cot.reshape(-1, depth_p),
        left_projection_matrix.astype(jnp.float32).T,
        precision=lax.Precision.HIGHEST,
    )
    ln_cot = ln_cot + jnp.dot(
        right_cot.reshape(-1, depth_p),
        right_projection_matrix.astype(jnp.float32).T,
        precision=lax.Precision.HIGHEST,
    )
    ln_cot = ln_cot.reshape(homolog_mesh_split, amino_mesh_split, feature_total)
    gain_gradient = ln_cot * standardizer_scaling
    alignment_gradient = reciprocal_spread * (
        gain_gradient
        - jnp.mean(gain_gradient, axis=-1, keepdims=True)
        - standardized_lines * jnp.mean(gain_gradient * standardized_lines, axis=-1, keepdims=True)
    )
    return (pair_delta, alignment_gradient.astype(jnp.bfloat16))


def solution(mesh):
    return jax.shard_map(
        body,
        mesh=mesh,
        in_specs=(
            P(("grp", "seq"), "res", None),
            P(),
            P(),
            P(),
            P(),
            P(),
            P(),
            P(),
            P(),
            P(("grp", "res"), "seq", None),
        ),
        out_specs=(P(("grp", "res"), "seq", None), P(("grp", "seq"), "res", None)),
        check_vma=False,
    )
```

```python
import jax
import jax.numpy as jnp
from jax import lax
from jax.sharding import PartitionSpec as P


def standardize_features(homolog_matrix, scaling_multiplier, additive_offset):
    incoming_tensor = homolog_matrix.astype(jnp.float32)
    row_mean = jnp.mean(incoming_tensor, axis=-1, keepdims=True)
    centred = incoming_tensor - row_mean
    reciprocal_spread = lax.rsqrt(jnp.mean(centred * centred, axis=-1, keepdims=True) + 1e-05)
    standardized_lines = centred * reciprocal_spread
    standardized_result = (standardized_lines * scaling_multiplier + additive_offset).astype(
        jnp.bfloat16
    )
    return (standardized_lines, reciprocal_spread, standardized_result)


def project_flat(flat_rows, weight, additive_offset):
    return (
        jnp.dot(flat_rows, weight, preferred_element_type=jnp.float32) + additive_offset
    ).astype(jnp.bfloat16)


def cot_outer(cot_block, coupling_matrix, seq_count, depth_p):
    first, second, pair_width = cot_block.shape
    result = (
        jnp.dot(
            cot_block.reshape(-1, pair_width), coupling_matrix.T, preferred_element_type=jnp.float32
        )
        / seq_count
    )
    return result.astype(jnp.bfloat16).reshape(first, second, depth_p, depth_p)


def exchange(packed, ranks):
    if ranks > 16:
        return lax.all_to_all(packed, "res", split_axis=0, concat_axis=0, tiled=True)
    rank = lax.axis_index("res")
    arrived = [lax.dynamic_index_in_dim(packed, rank, 0)]
    for shift in range(1, ranks):
        leaving = lax.dynamic_index_in_dim(packed, (rank - shift) % ranks, 0)
        pairs = [(source, (source - shift) % ranks) for source in range(ranks)]
        arrived.append(lax.ppermute(leaving, "res", pairs))
    twice = jnp.concatenate(arrived + arrived, axis=0)
    return lax.dynamic_slice_in_dim(twice, ranks - rank, ranks, axis=0)


def body(
    homolog_matrix,
    standardizer_scaling,
    standardizer_offset,
    left_projection_matrix,
    left_offset_vector,
    right_projection_matrix,
    right_offset_vector,
    coupling_matrix,
    coupling_offset,
    coupling_cotangent,
):
    homolog_mesh_split, amino_mesh_split, feature_total = homolog_matrix.shape
    depth_p = left_projection_matrix.shape[1]
    pair_width = coupling_matrix.shape[1]
    seq_count = homolog_mesh_split * lax.axis_size("seq")
    res_count = amino_mesh_split * lax.axis_size("res")
    standardized_lines, reciprocal_spread, standardized_result = standardize_features(
        homolog_matrix, standardizer_scaling, standardizer_offset
    )
    flat_rows = standardized_result.reshape(homolog_mesh_split * amino_mesh_split, feature_total)
    left_proj = project_flat(flat_rows, left_projection_matrix, left_offset_vector).reshape(
        homolog_mesh_split, amino_mesh_split * depth_p
    )
    right_proj = project_flat(flat_rows, right_projection_matrix, right_offset_vector).reshape(
        homolog_mesh_split, amino_mesh_split * depth_p
    )
    seq_index = lax.axis_index("seq")
    swap = [(0, 1), (1, 0)]
    other_cot = lax.ppermute(coupling_cotangent, "seq", swap)
    cot_rows = jnp.where(
        seq_index == 0,
        jnp.concatenate([coupling_cotangent, other_cot], axis=1),
        jnp.concatenate([other_cot, coupling_cotangent], axis=1),
    )
    ranks = lax.axis_size("res")
    proj_both = jnp.concatenate([left_proj, right_proj], axis=0)
    cot_parts = cot_rows.reshape(amino_mesh_split, ranks, amino_mesh_split, pair_width)
    cot_parts = cot_parts.transpose(1, 0, 2, 3).reshape(
        ranks, amino_mesh_split * amino_mesh_split, pair_width
    )
    packed = jnp.concatenate(
        [jnp.broadcast_to(proj_both[None], (ranks,) + proj_both.shape), cot_parts], axis=1
    )
    packed = exchange(packed, ranks)
    left_all = packed[:, :homolog_mesh_split].transpose(1, 0, 2).reshape(homolog_mesh_split, -1)
    right_all = (
        packed[:, homolog_mesh_split : 2 * homolog_mesh_split]
        .transpose(1, 0, 2)
        .reshape(homolog_mesh_split, -1)
    )
    cot_cols = packed[:, 2 * homolog_mesh_split :].reshape(res_count, amino_mesh_split, pair_width)
    left_own = left_proj.reshape(homolog_mesh_split, amino_mesh_split, depth_p)
    left_rows = left_all.reshape(homolog_mesh_split, res_count, depth_p)
    right_rows = right_all.reshape(homolog_mesh_split, res_count, depth_p)
    wide_weight = coupling_matrix.astype(jnp.float32)
    outer_sum = (
        jnp.einsum("sic,sjd->ijcd", left_own, right_rows, preferred_element_type=jnp.float32)
        / seq_count
    )
    pair_term = jnp.dot(
        outer_sum.reshape(-1, depth_p * depth_p), wide_weight, precision=lax.Precision.HIGHEST
    )
    pair_term = pair_term.reshape(amino_mesh_split, res_count, pair_width)
    half = res_count // 2
    own_half = lax.dynamic_slice_in_dim(pair_term, seq_index * half, half, axis=1)
    other_half = lax.dynamic_slice_in_dim(pair_term, (1 - seq_index) * half, half, axis=1)
    summed = own_half + lax.ppermute(other_half, "seq", swap)
    pair_delta = (summed + coupling_offset).astype(jnp.bfloat16)
    outer_rows = cot_outer(cot_rows, coupling_matrix, seq_count, depth_p)
    outer_cols = cot_outer(cot_cols, coupling_matrix, seq_count, depth_p)
    left_cot = jnp.einsum(
        "ijcd,sjd->sic", outer_rows, right_rows, preferred_element_type=jnp.float32
    )
    right_cot = jnp.einsum(
        "ijcd,sic->sjd", outer_cols, left_rows, preferred_element_type=jnp.float32
    )
    ln_cot = jnp.dot(
        left_cot.reshape(-1, depth_p),
        left_projection_matrix.astype(jnp.float32).T,
        precision=lax.Precision.HIGHEST,
    )
    ln_cot = ln_cot + jnp.dot(
        right_cot.reshape(-1, depth_p),
        right_projection_matrix.astype(jnp.float32).T,
        precision=lax.Precision.HIGHEST,
    )
    ln_cot = ln_cot.reshape(homolog_mesh_split, amino_mesh_split, feature_total)
    gain_gradient = ln_cot * standardizer_scaling
    alignment_gradient = reciprocal_spread * (
        gain_gradient
        - jnp.mean(gain_gradient, axis=-1, keepdims=True)
        - standardized_lines * jnp.mean(gain_gradient * standardized_lines, axis=-1, keepdims=True)
    )
    return (pair_delta, alignment_gradient.astype(jnp.bfloat16))


def solution(mesh):
    return jax.shard_map(
        body,
        mesh=mesh,
        in_specs=(
            P(("grp", "seq"), "res", None),
            P(),
            P(),
            P(),
            P(),
            P(),
            P(),
            P(),
            P(),
            P(("grp", "res"), "seq", None),
        ),
        out_specs=(P(("grp", "res"), "seq", None), P(("grp", "seq"), "res", None)),
        check_vma=False,
    )
```

```python
import functools

import jax
import jax.numpy as jnp
from jax import lax
from jax.experimental import pallas as pl
from jax.experimental.pallas import tpu as pltpu
from jax.sharding import PartitionSpec as P

LANES = 128
BF16 = jnp.bfloat16
F32 = jnp.float32
NT = (((1,), (1,)), ((), ()))
TN = (((0,), (0,)), ((), ()))


def lane_block(shape, width):
    return lax.broadcasted_iota(jnp.int32, shape, 1) // width


def pick(blocks, pieces):
    result = pieces[0]
    for place in range(1, len(pieces)):
        result = jnp.where(blocks == place, pieces[place], result)
    return result


def split_three(value):
    top = value.astype(BF16)
    rest = value - top.astype(F32)
    middle = rest.astype(BF16)
    low = (rest - middle.astype(F32)).astype(BF16)
    return top, middle, low


def normalise(rows):
    centred = rows - jnp.mean(rows, axis=-1, keepdims=True)
    inv_std = lax.rsqrt(jnp.mean(centred * centred, axis=-1, keepdims=True) + 1e-05)
    return centred * inv_std, inv_std


def residue_rows(x_ref):
    return jnp.concatenate(
        [x_ref[:, place, :].astype(F32) for place in range(x_ref.shape[1])], axis=0
    )


def project_kernel(
    x_ref, gain_ref, offset_ref, left_w_ref, left_b_ref, right_w_ref, right_b_ref, w_ref,
    left_ref, right_ref, sorted_w_ref, wide_ref,
):
    seqs, residues, _ = x_ref.shape
    depth = left_w_ref.shape[0]
    normed, _ = normalise(residue_rows(x_ref))
    ln_out = (normed * gain_ref[...] + offset_ref[...]).astype(BF16)
    blocks = lane_block((seqs, LANES), depth)
    for weight_ref, bias_ref, out_ref in (
        (left_w_ref, left_b_ref, left_ref),
        (right_w_ref, right_b_ref, right_ref),
    ):
        weight = jnp.concatenate([weight_ref[...]] * residues, axis=0)
        bias = jnp.concatenate([bias_ref[...]] * residues, axis=1)
        wide = lax.dot_general(ln_out, weight, NT, preferred_element_type=F32)
        own = pick(blocks, [wide[p * seqs : (p + 1) * seqs] for p in range(residues)])
        out_ref[...] = (own + bias).astype(BF16)
    wide_ref[...] = w_ref[...].astype(F32)
    for d in range(depth):
        sorted_w_ref[d * depth : (d + 1) * depth, :] = wide_ref[
            pl.ds(d, depth, stride=depth), :
        ].astype(BF16)


def cot_kernel(scale, own_ref, other_ref, sorted_w_ref, left_ref, right_ref,
               send_ref, outer_ref, turn_ref):
    residues, columns, _ = own_ref.shape
    depth = sorted_w_ref.shape[0] // (LANES // residues)
    depth = LANES // residues
    first = lax.axis_index("seq") == 0
    own = own_ref[...].reshape(residues * columns, LANES)
    other = other_ref[...].reshape(residues * columns, LANES)
    low = jnp.where(first, own, other)
    high = jnp.where(first, other, own)
    both = jnp.concatenate([low, high], axis=0)
    flat = lax.dot_general(both, sorted_w_ref[...], NT, preferred_element_type=F32) * scale
    blocks = lane_block((columns, LANES), depth)
    for half in range(2):
        for tile in range(depth * depth // LANES):
            block = flat[
                half * residues * columns : (half + 1) * residues * columns,
                tile * LANES : (tile + 1) * LANES,
            ]
            turned = [block] + [pltpu.roll(block, depth * t, 1) for t in range(1, residues)]
            for e in range(residues):
                piece = pick(
                    blocks,
                    [
                        turned[(i - e) % residues][i * columns : (i + 1) * columns]
                        for i in range(residues)
                    ],
                )
                turn_ref[pl.ds(half * columns * depth + tile * residues + e, columns, stride=depth), :] = piece
    outer = turn_ref[...].astype(BF16)
    half_rows = columns * depth
    partial = lax.dot_general(left_ref[...], outer, NT, preferred_element_type=F32).astype(BF16)
    seqs = left_ref.shape[0]
    ranks = columns // residues
    for half in range(2):
        outer_ref[half] = outer[half * half_rows : (half + 1) * half_rows]
        for rank in range(ranks):
            at = (half * ranks + rank) * LANES
            send_ref[half, rank, 0:seqs, :] = right_ref[...]
            send_ref[half, rank, seqs : 2 * seqs, :] = partial[:, at : at + LANES]


def grad_kernel(steps, got_ref, outer_ref, x_ref, gain_ref, left_w_ref, right_w_ref,
                grad_ref, left_cot_ref, right_cot_ref):
    step = pl.program_id(0)
    _, ranks, twice, _ = got_ref.shape
    seqs = twice // 2
    residues = x_ref.shape[1]
    depth = LANES // residues

    @pl.when(step == 0)
    def _():
        left_cot_ref[...] = jnp.zeros_like(left_cot_ref)
        right_cot_ref[...] = jnp.zeros_like(right_cot_ref)

    places = [(half, rank) for half in range(2) for rank in range(ranks)]
    right_all = jnp.concatenate([got_ref[h, r, 0:seqs, :] for h, r in places], axis=1)
    outer = jnp.concatenate([outer_ref[0], outer_ref[1]], axis=0)
    left_cot_ref[...] += jnp.dot(right_all, outer, preferred_element_type=F32)
    total = got_ref[0, 0, seqs:twice, :].astype(F32)
    for h, r in places[1:]:
        total = total + got_ref[h, r, seqs:twice, :].astype(F32)
    right_cot_ref[...] += total

    @pl.when(step == steps - 1)
    def _():
        blocks = lane_block((seqs, LANES), depth)
        left_cot, right_cot = left_cot_ref[...], right_cot_ref[...]
        spread = jnp.concatenate(
            [
                jnp.concatenate(
                    [
                        jnp.where(blocks == place, left_cot, 0.0),
                        jnp.where(blocks == place, right_cot, 0.0),
                    ],
                    axis=1,
                )
                for place in range(residues)
            ],
            axis=0,
        )
        weight = jnp.concatenate(
            [left_w_ref[...]] * residues + [right_w_ref[...]] * residues, axis=0
        )
        rows = residues * seqs
        parts = jnp.concatenate(split_three(spread), axis=0)
        ln_cot = jnp.dot(parts, weight, preferred_element_type=F32)
        ln_cot = ln_cot[0:rows] + (ln_cot[rows : 2 * rows] + ln_cot[2 * rows : 3 * rows])
        gained = ln_cot * gain_ref[...]
        normed, inv_std = normalise(residue_rows(x_ref))
        grad = inv_std * (
            gained
            - jnp.mean(gained, axis=-1, keepdims=True)
            - normed * jnp.mean(gained * normed, axis=-1, keepdims=True)
        )
        for place in range(residues):
            grad_ref[:, place, :] = grad[place * seqs : (place + 1) * seqs].astype(BF16)


def pair_kernel(scale, got_ref, far_ref, left_ref, far_left_ref, sorted_w_ref, offset_ref,
                pair_ref, turn_ref):
    residues, columns, _ = pair_ref.shape
    depth = LANES // residues
    ranks = columns // residues
    mine = lax.axis_index("seq")
    near = jnp.concatenate([got_ref[mine, r] for r in range(ranks)], axis=1)
    far = jnp.concatenate([far_ref[r] for r in range(ranks)], axis=1)
    right = jnp.concatenate([near, far], axis=0)
    left = jnp.concatenate([left_ref[...], far_left_ref[...]], axis=0)
    turn_ref[...] = lax.dot_general(right, left, TN, preferred_element_type=F32) * scale
    blocks = lane_block((columns, LANES), depth)
    tiles = []
    for tile in range(depth * depth // LANES):
        pieces = [
            turn_ref[pl.ds(tile * residues + e, columns, stride=depth), :]
            for e in range(residues)
        ]
        rows = jnp.concatenate(pieces, axis=0)
        turned = [rows] + [pltpu.roll(rows, depth * t, 1) for t in range(1, residues)]
        tiles.append(
            jnp.concatenate(
                [
                    pick(
                        blocks,
                        [
                            turned[(e - i) % residues][e * columns : (e + 1) * columns]
                            for e in range(residues)
                        ],
                    )
                    for i in range(residues)
                ],
                axis=0,
            )
        )
    flat = jnp.concatenate(tiles, axis=1)
    rows = residues * columns
    parts = jnp.concatenate(split_three(flat), axis=0)
    pair = jnp.dot(parts, sorted_w_ref[...], preferred_element_type=F32)
    pair = pair[0:rows] + (pair[rows : 2 * rows] + pair[2 * rows : 3 * rows])
    pair_ref[...] = (pair + offset_ref[...]).astype(BF16).reshape(pair_ref.shape)


def body(
    homolog_matrix,
    standardizer_scaling,
    standardizer_offset,
    left_projection_matrix,
    left_offset_vector,
    right_projection_matrix,
    right_offset_vector,
    coupling_matrix,
    coupling_offset,
    coupling_cotangent,
):
    seqs, residues, features = homolog_matrix.shape
    depth = left_projection_matrix.shape[1]
    ranks = lax.axis_size("res")
    scale = 1.0 / (seqs * lax.axis_size("seq"))
    half_ranks = ranks // 2
    half_columns = half_ranks * residues
    step_ranks = 4
    columns = step_ranks * residues
    steps = half_ranks // step_ranks
    mine = lax.axis_index("seq")
    swap = [(0, 1), (1, 0)]

    other_cot = lax.ppermute(coupling_cotangent, "seq", swap)
    gain = standardizer_scaling.reshape(1, -1)
    left_w = left_projection_matrix.T
    right_w = right_projection_matrix.T

    left, right, sorted_w = pl.pallas_call(
        project_kernel,
        out_shape=(
            jax.ShapeDtypeStruct((seqs, LANES), BF16),
            jax.ShapeDtypeStruct((seqs, LANES), BF16),
            jax.ShapeDtypeStruct(coupling_matrix.shape, BF16),
        ),
        scratch_shapes=[pltpu.VMEM(coupling_matrix.shape, F32)],
        name="project",
    )(
        homolog_matrix,
        gain,
        standardizer_offset.reshape(1, -1),
        left_w,
        left_offset_vector.reshape(1, -1),
        right_w,
        right_offset_vector.reshape(1, -1),
        coupling_matrix,
    )

    whole = lambda shape: pl.BlockSpec(shape, lambda g: (0,) * len(shape))
    cot_block = pl.BlockSpec((residues, columns, LANES), lambda g: (0, g, 0))
    outer_block = pl.BlockSpec((2, columns * depth, LANES), lambda g: (0, g, 0))
    send_block = pl.BlockSpec((2, step_ranks, 2 * seqs, LANES), lambda g: (0, g, 0, 0))
    send, outer = pl.pallas_call(
        functools.partial(cot_kernel, scale),
        grid=(steps,),
        in_specs=[
            cot_block,
            cot_block,
            whole(sorted_w.shape),
            whole(left.shape),
            whole(right.shape),
        ],
        out_specs=(send_block, outer_block),
        out_shape=(
            jax.ShapeDtypeStruct((2, half_ranks, 2 * seqs, LANES), BF16),
            jax.ShapeDtypeStruct((2, half_columns * depth, LANES), BF16),
        ),
        scratch_shapes=[pltpu.VMEM((2 * columns * depth, LANES), F32)],
        name="cotangent",
    )(coupling_cotangent, other_cot, sorted_w, left, right)

    got = lax.all_to_all(
        send.reshape(ranks, 2 * seqs, LANES), "res", split_axis=0, concat_axis=0, tiled=True
    ).reshape(send.shape)

    leaving = lax.dynamic_index_in_dim(got, 1 - mine, 0, keepdims=False)[:, 0:seqs, :]
    far = lax.ppermute(jnp.concatenate([leaving, left[None]], axis=0), "seq", swap)

    gradient = pl.pallas_call(
        functools.partial(grad_kernel, steps),
        grid=(steps,),
        in_specs=[
            send_block,
            outer_block,
            whole(homolog_matrix.shape),
            whole(gain.shape),
            whole(left_w.shape),
            whole(right_w.shape),
        ],
        out_specs=whole(homolog_matrix.shape),
        out_shape=jax.ShapeDtypeStruct(homolog_matrix.shape, BF16),
        scratch_shapes=[pltpu.VMEM((seqs, LANES), F32)] * 2,
        name="gradient",
    )(got, outer, homolog_matrix, gain, left_w, right_w)

    pair_delta = pl.pallas_call(
        functools.partial(pair_kernel, scale),
        grid=(steps,),
        in_specs=[
            pl.BlockSpec((2, step_ranks, seqs, LANES), lambda g: (0, g, 0, 0)),
            pl.BlockSpec((step_ranks, seqs, LANES), lambda g: (g, 0, 0)),
            whole(left.shape),
            pl.BlockSpec((None, seqs, LANES), lambda g: (half_ranks, 0, 0)),
            whole(sorted_w.shape),
            whole((1, LANES)),
        ],
        out_specs=cot_block,
        out_shape=jax.ShapeDtypeStruct(coupling_cotangent.shape, BF16),
        scratch_shapes=[pltpu.VMEM((columns * depth, LANES), F32)],
        name="pair",
    )(got, far, left, far, sorted_w, coupling_offset.reshape(1, -1))
    return (pair_delta, gradient)


def solution(mesh):
    return jax.shard_map(
        body,
        mesh=mesh,
        in_specs=(
            P(("grp", "seq"), "res", None),
            P(),
            P(),
            P(),
            P(),
            P(),
            P(),
            P(),
            P(),
            P(("grp", "res"), "seq", None),
        ),
        out_specs=(P(("grp", "res"), "seq", None), P(("grp", "seq"), "res", None)),
        check_vma=False,
    )
```

```python
import functools

import jax
import jax.numpy as jnp
from jax import lax
from jax.experimental import pallas as pl
from jax.experimental.pallas import tpu as pltpu
from jax.sharding import PartitionSpec as P

LANES = 128
BF16 = jnp.bfloat16
F32 = jnp.float32
NT = (((1,), (1,)), ((), ()))
TN = (((0,), (0,)), ((), ()))


def lane_block(shape, width):
    return lax.broadcasted_iota(jnp.int32, shape, 1) // width


def pick(blocks, pieces):
    result = pieces[0]
    for place in range(1, len(pieces)):
        result = jnp.where(blocks == place, pieces[place], result)
    return result


def split_three(value):
    top = value.astype(BF16)
    rest = value - top.astype(F32)
    middle = rest.astype(BF16)
    low = (rest - middle.astype(F32)).astype(BF16)
    return top, middle, low


def normalise(rows):
    centred = rows - jnp.mean(rows, axis=-1, keepdims=True)
    inv_std = lax.rsqrt(jnp.mean(centred * centred, axis=-1, keepdims=True) + 1e-05)
    return centred * inv_std, inv_std


def residue_rows(x_ref):
    return jnp.concatenate(
        [x_ref[:, place, :].astype(F32) for place in range(x_ref.shape[1])], axis=0
    )


def project_kernel(
    x_ref, gain_ref, offset_ref, left_w_ref, left_b_ref, right_w_ref, right_b_ref, w_ref,
    left_ref, right_ref, sorted_w_ref, wide_ref,
):
    seqs, residues, _ = x_ref.shape
    depth = left_w_ref.shape[0]
    normed, _ = normalise(residue_rows(x_ref))
    ln_out = (normed * gain_ref[...] + offset_ref[...]).astype(BF16)
    blocks = lane_block((seqs, LANES), depth)
    for weight_ref, bias_ref, out_ref in (
        (left_w_ref, left_b_ref, left_ref),
        (right_w_ref, right_b_ref, right_ref),
    ):
        weight = jnp.concatenate([weight_ref[...]] * residues, axis=0)
        bias = jnp.concatenate([bias_ref[...]] * residues, axis=1)
        wide = lax.dot_general(ln_out, weight, NT, preferred_element_type=F32)
        own = pick(blocks, [wide[p * seqs : (p + 1) * seqs] for p in range(residues)])
        out_ref[...] = (own + bias).astype(BF16)
    wide_ref[...] = w_ref[...].astype(F32)
    for d in range(depth):
        sorted_w_ref[d * depth : (d + 1) * depth, :] = wide_ref[
            pl.ds(d, depth, stride=depth), :
        ].astype(BF16)


def cot_kernel(scale, own_ref, other_ref, sorted_w_ref, left_ref, right_ref,
               send_ref, outer_ref, turn_ref):
    residues, columns, _ = own_ref.shape
    depth = sorted_w_ref.shape[0] // (LANES // residues)
    depth = LANES // residues
    first = lax.axis_index("seq") == 0
    own = own_ref[...].reshape(residues * columns, LANES)
    other = other_ref[...].reshape(residues * columns, LANES)
    low = jnp.where(first, own, other)
    high = jnp.where(first, other, own)
    both = jnp.concatenate([low, high], axis=0)
    flat = lax.dot_general(both, sorted_w_ref[...], NT, preferred_element_type=F32) * scale
    blocks = lane_block((columns, LANES), depth)
    for half in range(2):
        for tile in range(depth * depth // LANES):
            block = flat[
                half * residues * columns : (half + 1) * residues * columns,
                tile * LANES : (tile + 1) * LANES,
            ]
            turned = [block] + [pltpu.roll(block, depth * t, 1) for t in range(1, residues)]
            for e in range(residues):
                piece = pick(
                    blocks,
                    [
                        turned[(i - e) % residues][i * columns : (i + 1) * columns]
                        for i in range(residues)
                    ],
                )
                turn_ref[pl.ds(half * columns * depth + tile * residues + e, columns, stride=depth), :] = piece
    outer = turn_ref[...].astype(BF16)
    half_rows = columns * depth
    partial = lax.dot_general(left_ref[...], outer, NT, preferred_element_type=F32).astype(BF16)
    seqs = left_ref.shape[0]
    ranks = columns // residues
    for half in range(2):
        outer_ref[half] = outer[half * half_rows : (half + 1) * half_rows]
        for rank in range(ranks):
            at = (half * ranks + rank) * LANES
            send_ref[half, rank, 0:seqs, :] = right_ref[...]
            send_ref[half, rank, seqs : 2 * seqs, :] = partial[:, at : at + LANES]


def grad_kernel(steps, got_ref, outer_ref, x_ref, gain_ref, left_w_ref, right_w_ref,
                grad_ref, left_cot_ref, right_cot_ref):
    step = pl.program_id(0)
    _, ranks, twice, _ = got_ref.shape
    seqs = twice // 2
    residues = x_ref.shape[1]
    depth = LANES // residues

    @pl.when(step == 0)
    def _():
        left_cot_ref[...] = jnp.zeros_like(left_cot_ref)
        right_cot_ref[...] = jnp.zeros_like(right_cot_ref)

    places = [(half, rank) for half in range(2) for rank in range(ranks)]
    right_all = jnp.concatenate([got_ref[h, r, 0:seqs, :] for h, r in places], axis=1)
    outer = jnp.concatenate([outer_ref[0], outer_ref[1]], axis=0)
    left_cot_ref[...] += jnp.dot(right_all, outer, preferred_element_type=F32)
    total = got_ref[0, 0, seqs:twice, :].astype(F32)
    for h, r in places[1:]:
        total = total + got_ref[h, r, seqs:twice, :].astype(F32)
    right_cot_ref[...] += total

    @pl.when(step == steps - 1)
    def _():
        blocks = lane_block((seqs, LANES), depth)
        left_cot, right_cot = left_cot_ref[...], right_cot_ref[...]
        spread = jnp.concatenate(
            [
                jnp.concatenate(
                    [
                        jnp.where(blocks == place, left_cot, 0.0),
                        jnp.where(blocks == place, right_cot, 0.0),
                    ],
                    axis=1,
                )
                for place in range(residues)
            ],
            axis=0,
        )
        weight = jnp.concatenate(
            [left_w_ref[...]] * residues + [right_w_ref[...]] * residues, axis=0
        )
        rows = residues * seqs
        parts = jnp.concatenate(split_three(spread), axis=0)
        ln_cot = jnp.dot(parts, weight, preferred_element_type=F32)
        ln_cot = ln_cot[0:rows] + (ln_cot[rows : 2 * rows] + ln_cot[2 * rows : 3 * rows])
        gained = ln_cot * gain_ref[...]
        normed, inv_std = normalise(residue_rows(x_ref))
        grad = inv_std * (
            gained
            - jnp.mean(gained, axis=-1, keepdims=True)
            - normed * jnp.mean(gained * normed, axis=-1, keepdims=True)
        )
        for place in range(residues):
            grad_ref[:, place, :] = grad[place * seqs : (place + 1) * seqs].astype(BF16)


def pair_kernel(scale, got_ref, far_ref, left_ref, far_left_ref, sorted_w_ref, offset_ref,
                pair_ref, turn_ref):
    residues, columns, _ = pair_ref.shape
    depth = LANES // residues
    ranks = columns // residues
    mine = lax.axis_index("seq")
    near = jnp.concatenate([got_ref[mine, r] for r in range(ranks)], axis=1)
    far = jnp.concatenate([far_ref[r] for r in range(ranks)], axis=1)
    right = jnp.concatenate([near, far], axis=0)
    left = jnp.concatenate([left_ref[...], far_left_ref[...]], axis=0)
    turn_ref[...] = lax.dot_general(right, left, TN, preferred_element_type=F32) * scale
    blocks = lane_block((columns, LANES), depth)
    tiles = []
    for tile in range(depth * depth // LANES):
        pieces = [
            turn_ref[pl.ds(tile * residues + e, columns, stride=depth), :]
            for e in range(residues)
        ]
        rows = jnp.concatenate(pieces, axis=0)
        turned = [rows] + [pltpu.roll(rows, depth * t, 1) for t in range(1, residues)]
        tiles.append(
            jnp.concatenate(
                [
                    pick(
                        blocks,
                        [
                            turned[(e - i) % residues][e * columns : (e + 1) * columns]
                            for e in range(residues)
                        ],
                    )
                    for i in range(residues)
                ],
                axis=0,
            )
        )
    flat = jnp.concatenate(tiles, axis=1)
    rows = residues * columns
    parts = jnp.concatenate(split_three(flat), axis=0)
    pair = jnp.dot(parts, sorted_w_ref[...], preferred_element_type=F32)
    pair = pair[0:rows] + (pair[rows : 2 * rows] + pair[2 * rows : 3 * rows])
    pair_ref[...] = (pair + offset_ref[...]).astype(BF16).reshape(pair_ref.shape)


def wide_slice(
    homolog_matrix,
    standardizer_scaling,
    standardizer_offset,
    left_projection_matrix,
    left_offset_vector,
    right_projection_matrix,
    right_offset_vector,
    coupling_matrix,
    coupling_offset,
    coupling_cotangent,
):
    seqs, residues, features = homolog_matrix.shape
    depth = left_projection_matrix.shape[1]
    ranks = lax.axis_size("res")
    scale = 1.0 / (seqs * lax.axis_size("seq"))
    half_ranks = ranks // 2
    half_columns = half_ranks * residues
    step_ranks = 4
    columns = step_ranks * residues
    steps = half_ranks // step_ranks
    mine = lax.axis_index("seq")
    swap = [(0, 1), (1, 0)]

    other_cot = lax.ppermute(coupling_cotangent, "seq", swap)
    gain = standardizer_scaling.reshape(1, -1)
    left_w = left_projection_matrix.T
    right_w = right_projection_matrix.T

    left, right, sorted_w = pl.pallas_call(
        project_kernel,
        out_shape=(
            jax.ShapeDtypeStruct((seqs, LANES), BF16),
            jax.ShapeDtypeStruct((seqs, LANES), BF16),
            jax.ShapeDtypeStruct(coupling_matrix.shape, BF16),
        ),
        scratch_shapes=[pltpu.VMEM(coupling_matrix.shape, F32)],
        name="project",
    )(
        homolog_matrix,
        gain,
        standardizer_offset.reshape(1, -1),
        left_w,
        left_offset_vector.reshape(1, -1),
        right_w,
        right_offset_vector.reshape(1, -1),
        coupling_matrix,
    )

    whole = lambda shape: pl.BlockSpec(shape, lambda g: (0,) * len(shape))
    cot_block = pl.BlockSpec((residues, columns, LANES), lambda g: (0, g, 0))
    outer_block = pl.BlockSpec((2, columns * depth, LANES), lambda g: (0, g, 0))
    send_block = pl.BlockSpec((2, step_ranks, 2 * seqs, LANES), lambda g: (0, g, 0, 0))
    send, outer = pl.pallas_call(
        functools.partial(cot_kernel, scale),
        grid=(steps,),
        in_specs=[
            cot_block,
            cot_block,
            whole(sorted_w.shape),
            whole(left.shape),
            whole(right.shape),
        ],
        out_specs=(send_block, outer_block),
        out_shape=(
            jax.ShapeDtypeStruct((2, half_ranks, 2 * seqs, LANES), BF16),
            jax.ShapeDtypeStruct((2, half_columns * depth, LANES), BF16),
        ),
        scratch_shapes=[pltpu.VMEM((2 * columns * depth, LANES), F32)],
        name="cotangent",
    )(coupling_cotangent, other_cot, sorted_w, left, right)

    got = lax.all_to_all(
        send.reshape(ranks, 2 * seqs, LANES), "res", split_axis=0, concat_axis=0, tiled=True
    ).reshape(send.shape)

    leaving = lax.dynamic_index_in_dim(got, 1 - mine, 0, keepdims=False)[:, 0:seqs, :]
    far = lax.ppermute(jnp.concatenate([leaving, left[None]], axis=0), "seq", swap)

    gradient = pl.pallas_call(
        functools.partial(grad_kernel, steps),
        grid=(steps,),
        in_specs=[
            send_block,
            outer_block,
            whole(homolog_matrix.shape),
            whole(gain.shape),
            whole(left_w.shape),
            whole(right_w.shape),
        ],
        out_specs=whole(homolog_matrix.shape),
        out_shape=jax.ShapeDtypeStruct(homolog_matrix.shape, BF16),
        scratch_shapes=[pltpu.VMEM((seqs, LANES), F32)] * 2,
        name="gradient",
    )(got, outer, homolog_matrix, gain, left_w, right_w)

    pair_delta = pl.pallas_call(
        functools.partial(pair_kernel, scale),
        grid=(steps,),
        in_specs=[
            pl.BlockSpec((2, step_ranks, seqs, LANES), lambda g: (0, g, 0, 0)),
            pl.BlockSpec((step_ranks, seqs, LANES), lambda g: (g, 0, 0)),
            whole(left.shape),
            pl.BlockSpec((None, seqs, LANES), lambda g: (half_ranks, 0, 0)),
            whole(sorted_w.shape),
            whole((1, LANES)),
        ],
        out_specs=cot_block,
        out_shape=jax.ShapeDtypeStruct(coupling_cotangent.shape, BF16),
        scratch_shapes=[pltpu.VMEM((columns * depth, LANES), F32)],
        name="pair",
    )(got, far, left, far, sorted_w, coupling_offset.reshape(1, -1))
    return (pair_delta, gradient)


STEP_MASKS = (2, 4, 1)


def cube_place(mask):
    first, second, third = STEP_MASKS
    bit = lambda step: lax.shift_right_logical(mask, step.bit_length() - 1) & 1
    return bit(second) * 4 + bit(third) * 2 + bit(first)


def fetch(source, target, semaphore):
    copy = pltpu.make_async_copy(source, target, semaphore)
    copy.start()
    return copy


def cube_project_kernel(
    x_ref, gain_ref, offset_ref, left_w_ref, left_b_ref, right_w_ref, right_b_ref, w_hbm, pair_offset_ref,
    left_ref, right_ref, sorted_w_ref, normed_ref, inv_std_ref, spread_w_ref, gain_out_ref,
    pair_offset_out_ref, raw_ref, wide_ref, semaphore,
):
    copy = fetch(w_hbm, raw_ref, semaphore)
    seqs, residues, _ = x_ref.shape
    depth = left_w_ref.shape[0]
    normed, inv_std = normalise(residue_rows(x_ref))
    normed_ref[...] = normed
    inv_std_ref[...] = jnp.broadcast_to(inv_std, inv_std_ref.shape)
    ln_out = (normed * gain_ref[...] + offset_ref[...]).astype(BF16)
    blocks = lane_block((seqs, LANES), depth)
    spread = []
    for weight_ref, bias_ref, out_ref in (
        (left_w_ref, left_b_ref, left_ref),
        (right_w_ref, right_b_ref, right_ref),
    ):
        weight = jnp.concatenate([weight_ref[...]] * residues, axis=0)
        spread.append(weight)
        bias = jnp.concatenate([bias_ref[...]] * residues, axis=1)
        wide = lax.dot_general(ln_out, weight, NT, preferred_element_type=F32)
        own = pick(blocks, [wide[p * seqs : (p + 1) * seqs] for p in range(residues)])
        out_ref[...] = (own + bias).astype(BF16)
    spread_w_ref[...] = jnp.concatenate(spread, axis=0)
    gain_out_ref[...] = gain_ref[...]
    pair_offset_out_ref[...] = pair_offset_ref[...]
    copy.wait()
    wide_ref[...] = raw_ref[...].astype(F32)
    for d in range(depth):
        sorted_w_ref[d * depth : (d + 1) * depth, :] = wide_ref[
            pl.ds(d, depth, stride=depth), :
        ].astype(BF16)


def cube_cot_kernel(scale, own_ref, other_ref, sorted_w_ref, left_ref, right_ref,
                    send_ref, keep_ref, outer_ref, turn_ref):
    residues, columns, _ = own_ref.shape
    depth = LANES // residues
    first = lax.axis_index("seq") == 0
    own = own_ref[...].reshape(residues * columns, LANES)
    other = other_ref[...].reshape(residues * columns, LANES)
    both = jnp.concatenate([jnp.where(first, own, other), jnp.where(first, other, own)], axis=0)
    flat = lax.dot_general(both, sorted_w_ref[...], NT, preferred_element_type=F32) * scale
    blocks = lane_block((columns, LANES), depth)
    for half in range(2):
        for tile in range(depth * depth // LANES):
            block = flat[
                half * residues * columns : (half + 1) * residues * columns,
                tile * LANES : (tile + 1) * LANES,
            ]
            turned = [block] + [pltpu.roll(block, depth * t, 1) for t in range(1, residues)]
            for e in range(residues):
                start = half * columns * depth + tile * residues + e
                turn_ref[pl.ds(start, columns, stride=depth), :] = pick(
                    blocks,
                    [
                        turned[(i - e) % residues][i * columns : (i + 1) * columns]
                        for i in range(residues)
                    ],
                )
    outer = turn_ref[...].astype(BF16)
    outer_ref[...] = outer
    partial = lax.dot_general(left_ref[...], outer, NT, preferred_element_type=F32)
    rank = lax.axis_index("res")
    send_ref[0] = right_ref[...]
    for place in range(2 * columns // residues):
        distance = lax.bitwise_xor(rank, place)
        spot = cube_spot(distance)
        piece = partial[:, place * LANES : (place + 1) * LANES]

        @pl.when(spot >= 4)
        def _():
            send_ref[spot - 3] = piece.astype(BF16)

        @pl.when(spot < 4)
        def _():
            keep_ref[spot] = piece


def cube_spot(mask):
    first, second, third = STEP_MASKS
    bit = lambda step: lax.shift_right_logical(mask, step.bit_length() - 1) & 1
    return bit(first) * 4 + bit(second) * 2 + bit(third)


def cube_grad_kernel(right_ref, outer_ref, keep_ref, one_ref, two_ref, three_ref, normed_ref,
                     inv_std_ref, gain_ref, spread_w_ref, grad_ref):
    ranks, seqs, _ = right_ref.shape
    residues = grad_ref.shape[1]
    depth = LANES // residues
    rank = lax.axis_index("res")
    right_all = jnp.concatenate(
        [right_ref[cube_place(lax.bitwise_xor(rank, place))] for place in range(ranks)], axis=1
    )
    left_cot = jnp.dot(right_all, outer_ref[...], preferred_element_type=F32)
    right_cot = (
        keep_ref[0] + one_ref[1].astype(F32) + two_ref[2].astype(F32) + three_ref[4].astype(F32)
    )
    blocks = lane_block((seqs, LANES), depth)
    spread = jnp.concatenate(
        [
            jnp.concatenate(
                [jnp.where(blocks == place, cot, 0.0) for cot in (left_cot, right_cot)], axis=1
            )
            for place in range(residues)
        ],
        axis=0,
    )
    rows = residues * seqs
    parts = jnp.concatenate(split_three(spread), axis=0)
    ln_cot = jnp.dot(parts, spread_w_ref[...], preferred_element_type=F32)
    ln_cot = ln_cot[0:rows] + (ln_cot[rows : 2 * rows] + ln_cot[2 * rows : 3 * rows])
    gained = ln_cot * gain_ref[...]
    normed = normed_ref[...]
    grad = inv_std_ref[:, 0:1] * (
        gained
        - jnp.mean(gained, axis=-1, keepdims=True)
        - normed * jnp.mean(gained * normed, axis=-1, keepdims=True)
    )
    for place in range(residues):
        grad_ref[:, place, :] = grad[place * seqs : (place + 1) * seqs].astype(BF16)


def cube_pair_kernel(scale, right_ref, far_ref, left_ref, sorted_w_ref, offset_ref,
                     pair_ref, turn_ref):
    residues, columns, _ = pair_ref.shape
    depth = LANES // residues
    ranks = columns // residues
    rank = lax.axis_index("res")
    base = lax.axis_index("seq") * ranks
    near, far = [], []
    for place in range(ranks):
        spot = cube_place(lax.bitwise_xor(rank, base + place))
        near.append(right_ref[spot])
        far.append(far_ref[spot & (ranks - 1)])
    right = jnp.concatenate(
        [jnp.concatenate(near, axis=1), jnp.concatenate(far, axis=1)], axis=0
    )
    left = jnp.concatenate([left_ref[...], far_ref[ranks]], axis=0)
    turn_ref[...] = lax.dot_general(right, left, TN, preferred_element_type=F32) * scale
    blocks = lane_block((columns, LANES), depth)
    tiles = []
    for tile in range(depth * depth // LANES):
        pieces = [
            turn_ref[pl.ds(tile * residues + e, columns, stride=depth), :]
            for e in range(residues)
        ]
        rows = jnp.concatenate(pieces, axis=0)
        turned = [rows] + [pltpu.roll(rows, depth * t, 1) for t in range(1, residues)]
        tiles.append(
            jnp.concatenate(
                [
                    pick(
                        blocks,
                        [
                            turned[(e - i) % residues][e * columns : (e + 1) * columns]
                            for e in range(residues)
                        ],
                    )
                    for i in range(residues)
                ],
                axis=0,
            )
        )
    flat = jnp.concatenate(tiles, axis=1)
    rows = residues * columns
    parts = jnp.concatenate(split_three(flat), axis=0)
    pair = jnp.dot(parts, sorted_w_ref[...], preferred_element_type=F32)
    pair = pair[0:rows] + (pair[rows : 2 * rows] + pair[2 * rows : 3 * rows])
    pair_ref[...] = (pair + offset_ref[...]).astype(BF16).reshape(pair_ref.shape)


def cube_slice(
    homolog_matrix,
    standardizer_scaling,
    standardizer_offset,
    left_projection_matrix,
    left_offset_vector,
    right_projection_matrix,
    right_offset_vector,
    coupling_matrix,
    coupling_offset,
    coupling_cotangent,
):
    seqs, residues, features = homolog_matrix.shape
    ranks = lax.axis_size("res")
    rows = seqs * residues
    scale = 1.0 / (seqs * lax.axis_size("seq"))
    rank = lax.axis_index("res")
    mine = lax.axis_index("seq")
    swap = [(0, 1), (1, 0)]
    vmem = pl.BlockSpec(memory_space=pltpu.VMEM)
    like = jax.ShapeDtypeStruct

    other_cot = lax.ppermute(coupling_cotangent, "seq", swap)
    left, right, sorted_w, normed, inv_std, spread_w, gain, pair_offset = pl.pallas_call(
        cube_project_kernel,
        in_specs=[vmem] * 7 + [pl.BlockSpec(memory_space=pl.ANY), vmem],
        out_specs=[vmem] * 8,
        out_shape=(
            like((seqs, LANES), BF16),
            like((seqs, LANES), BF16),
            like(coupling_matrix.shape, BF16),
            like((rows, features), F32),
            like((rows, LANES), F32),
            like((2 * LANES, features), BF16),
            like((1, features), F32),
            like((1, LANES), F32),
        ),
        scratch_shapes=[
            pltpu.VMEM(coupling_matrix.shape, BF16),
            pltpu.VMEM(coupling_matrix.shape, F32),
            pltpu.SemaphoreType.DMA,
        ],
        name="project",
    )(
        homolog_matrix,
        standardizer_scaling.reshape(1, -1),
        standardizer_offset.reshape(1, -1),
        left_projection_matrix.T,
        left_offset_vector.reshape(1, -1),
        right_projection_matrix.T,
        right_offset_vector.reshape(1, -1),
        coupling_matrix,
        coupling_offset.reshape(1, -1),
    )

    send, keep, outer = pl.pallas_call(
        functools.partial(cube_cot_kernel, scale),
        in_specs=[vmem] * 5,
        out_specs=[vmem] * 3,
        out_shape=(
            like((1 + ranks // 2, seqs, LANES), BF16),
            like((ranks // 2, seqs, LANES), F32),
            like((ranks * LANES, LANES), BF16),
        ),
        scratch_shapes=[pltpu.VMEM((ranks * LANES, LANES), F32)],
        name="cotangent",
    )(coupling_cotangent, other_cot, sorted_w, left, right)

    def swap_over(mask, value):
        return lax.ppermute(value, "res", [(source, source ^ mask) for source in range(ranks)])

    own = right[None]
    one = swap_over(STEP_MASKS[0], send)
    send = jnp.concatenate([own, one[0:1], (keep[2:4] + one[3:5].astype(F32)).astype(BF16)])
    two = swap_over(STEP_MASKS[1], send)
    summed = keep[1:2] + one[2:3].astype(F32) + two[3:4].astype(F32)
    send = jnp.concatenate([own, one[0:1], two[0:2], summed.astype(BF16)])
    three = swap_over(STEP_MASKS[2], send)
    gathered = jnp.concatenate([own, one[0:1], three[0:2], two[0:2], three[2:4]])

    half = gathered.reshape(2, ranks // 2, seqs, LANES)
    beyond = 1 - lax.bitwise_xor(lax.shift_right_logical(rank, 2), mine)
    leaving = lax.dynamic_index_in_dim(half, beyond, 0, keepdims=False)
    far = lax.ppermute(jnp.concatenate([leaving, left[None]]), "seq", swap)

    gradient = pl.pallas_call(
        cube_grad_kernel,
        in_specs=[vmem] * 10,
        out_specs=vmem,
        out_shape=like(homolog_matrix.shape, BF16),
        name="gradient",
    )(gathered, outer, keep, one, two, three, normed, inv_std, gain, spread_w)

    pair_delta = pl.pallas_call(
        functools.partial(cube_pair_kernel, scale),
        in_specs=[vmem] * 5,
        out_specs=vmem,
        out_shape=like(coupling_cotangent.shape, BF16),
        scratch_shapes=[pltpu.VMEM((ranks // 2 * LANES, LANES), F32)],
        name="pair",
    )(gathered, far, left, sorted_w, pair_offset)
    return (pair_delta, gradient)


def body(*arrays):
    if lax.axis_size("res") == 8:
        return cube_slice(*arrays)
    return wide_slice(*arrays)


def solution(mesh):
    return jax.shard_map(
        body,
        mesh=mesh,
        in_specs=(
            P(("grp", "seq"), "res", None),
            P(),
            P(),
            P(),
            P(),
            P(),
            P(),
            P(),
            P(),
            P(("grp", "res"), "seq", None),
        ),
        out_specs=(P(("grp", "res"), "seq", None), P(("grp", "seq"), "res", None)),
        check_vma=False,
    )
```

```python
import functools

import jax
import jax.numpy as jnp
from jax import lax
from jax.experimental import pallas as pl
from jax.experimental.pallas import tpu as pltpu
from jax.sharding import PartitionSpec as P

LANES = 128
BF16 = jnp.bfloat16
F32 = jnp.float32
NT = (((1,), (1,)), ((), ()))
TN = (((0,), (0,)), ((), ()))


def lane_block(shape, width):
    return lax.broadcasted_iota(jnp.int32, shape, 1) // width


def pick(blocks, pieces):
    result = pieces[0]
    for place in range(1, len(pieces)):
        result = jnp.where(blocks == place, pieces[place], result)
    return result


def split_three(value):
    top = value.astype(BF16)
    rest = value - top.astype(F32)
    middle = rest.astype(BF16)
    low = (rest - middle.astype(F32)).astype(BF16)
    return top, middle, low


def normalise(rows):
    centred = rows - jnp.mean(rows, axis=-1, keepdims=True)
    inv_std = lax.rsqrt(jnp.mean(centred * centred, axis=-1, keepdims=True) + 1e-05)
    return centred * inv_std, inv_std


def residue_rows(x_ref):
    return jnp.concatenate(
        [x_ref[:, place, :].astype(F32) for place in range(x_ref.shape[1])], axis=0
    )


def project_kernel(
    x_ref, gain_ref, offset_ref, left_w_ref, left_b_ref, right_w_ref, right_b_ref, w_ref,
    left_ref, right_ref, sorted_w_ref, wide_ref,
):
    seqs, residues, _ = x_ref.shape
    depth = left_w_ref.shape[0]
    normed, _ = normalise(residue_rows(x_ref))
    ln_out = (normed * gain_ref[...] + offset_ref[...]).astype(BF16)
    blocks = lane_block((seqs, LANES), depth)
    for weight_ref, bias_ref, out_ref in (
        (left_w_ref, left_b_ref, left_ref),
        (right_w_ref, right_b_ref, right_ref),
    ):
        weight = jnp.concatenate([weight_ref[...]] * residues, axis=0)
        bias = jnp.concatenate([bias_ref[...]] * residues, axis=1)
        wide = lax.dot_general(ln_out, weight, NT, preferred_element_type=F32)
        own = pick(blocks, [wide[p * seqs : (p + 1) * seqs] for p in range(residues)])
        out_ref[...] = (own + bias).astype(BF16)
    wide_ref[...] = w_ref[...].astype(F32)
    for d in range(depth):
        sorted_w_ref[d * depth : (d + 1) * depth, :] = wide_ref[
            pl.ds(d, depth, stride=depth), :
        ].astype(BF16)


def cot_kernel(scale, own_ref, other_ref, sorted_w_ref, left_ref, right_ref,
               send_ref, outer_ref, turn_ref):
    residues, columns, _ = own_ref.shape
    depth = sorted_w_ref.shape[0] // (LANES // residues)
    depth = LANES // residues
    first = lax.axis_index("seq") == 0
    own = own_ref[...].reshape(residues * columns, LANES)
    other = other_ref[...].reshape(residues * columns, LANES)
    low = jnp.where(first, own, other)
    high = jnp.where(first, other, own)
    both = jnp.concatenate([low, high], axis=0)
    flat = lax.dot_general(both, sorted_w_ref[...], NT, preferred_element_type=F32) * scale
    blocks = lane_block((columns, LANES), depth)
    for half in range(2):
        for tile in range(depth * depth // LANES):
            block = flat[
                half * residues * columns : (half + 1) * residues * columns,
                tile * LANES : (tile + 1) * LANES,
            ]
            turned = [block] + [pltpu.roll(block, depth * t, 1) for t in range(1, residues)]
            for e in range(residues):
                piece = pick(
                    blocks,
                    [
                        turned[(i - e) % residues][i * columns : (i + 1) * columns]
                        for i in range(residues)
                    ],
                )
                turn_ref[pl.ds(half * columns * depth + tile * residues + e, columns, stride=depth), :] = piece
    outer = turn_ref[...].astype(BF16)
    half_rows = columns * depth
    partial = lax.dot_general(left_ref[...], outer, NT, preferred_element_type=F32).astype(BF16)
    seqs = left_ref.shape[0]
    ranks = columns // residues
    for half in range(2):
        outer_ref[half] = outer[half * half_rows : (half + 1) * half_rows]
        for rank in range(ranks):
            at = (half * ranks + rank) * LANES
            send_ref[half, rank, 0:seqs, :] = right_ref[...]
            send_ref[half, rank, seqs : 2 * seqs, :] = partial[:, at : at + LANES]


def grad_kernel(steps, got_ref, outer_ref, x_ref, gain_ref, left_w_ref, right_w_ref,
                grad_ref, left_cot_ref, right_cot_ref):
    step = pl.program_id(0)
    _, ranks, twice, _ = got_ref.shape
    seqs = twice // 2
    residues = x_ref.shape[1]
    depth = LANES // residues

    @pl.when(step == 0)
    def _():
        left_cot_ref[...] = jnp.zeros_like(left_cot_ref)
        right_cot_ref[...] = jnp.zeros_like(right_cot_ref)

    places = [(half, rank) for half in range(2) for rank in range(ranks)]
    right_all = jnp.concatenate([got_ref[h, r, 0:seqs, :] for h, r in places], axis=1)
    outer = jnp.concatenate([outer_ref[0], outer_ref[1]], axis=0)
    left_cot_ref[...] += jnp.dot(right_all, outer, preferred_element_type=F32)
    total = got_ref[0, 0, seqs:twice, :].astype(F32)
    for h, r in places[1:]:
        total = total + got_ref[h, r, seqs:twice, :].astype(F32)
    right_cot_ref[...] += total

    @pl.when(step == steps - 1)
    def _():
        blocks = lane_block((seqs, LANES), depth)
        left_cot, right_cot = left_cot_ref[...], right_cot_ref[...]
        spread = jnp.concatenate(
            [
                jnp.concatenate(
                    [
                        jnp.where(blocks == place, left_cot, 0.0),
                        jnp.where(blocks == place, right_cot, 0.0),
                    ],
                    axis=1,
                )
                for place in range(residues)
            ],
            axis=0,
        )
        weight = jnp.concatenate(
            [left_w_ref[...]] * residues + [right_w_ref[...]] * residues, axis=0
        )
        rows = residues * seqs
        parts = jnp.concatenate(split_three(spread), axis=0)
        ln_cot = jnp.dot(parts, weight, preferred_element_type=F32)
        ln_cot = ln_cot[0:rows] + (ln_cot[rows : 2 * rows] + ln_cot[2 * rows : 3 * rows])
        gained = ln_cot * gain_ref[...]
        normed, inv_std = normalise(residue_rows(x_ref))
        grad = inv_std * (
            gained
            - jnp.mean(gained, axis=-1, keepdims=True)
            - normed * jnp.mean(gained * normed, axis=-1, keepdims=True)
        )
        for place in range(residues):
            grad_ref[:, place, :] = grad[place * seqs : (place + 1) * seqs].astype(BF16)


def pair_kernel(scale, got_ref, far_ref, left_ref, far_left_ref, sorted_w_ref, offset_ref,
                pair_ref, turn_ref):
    residues, columns, _ = pair_ref.shape
    depth = LANES // residues
    ranks = columns // residues
    mine = lax.axis_index("seq")
    near = jnp.concatenate([got_ref[mine, r] for r in range(ranks)], axis=1)
    far = jnp.concatenate([far_ref[r] for r in range(ranks)], axis=1)
    right = jnp.concatenate([near, far], axis=0)
    left = jnp.concatenate([left_ref[...], far_left_ref[...]], axis=0)
    turn_ref[...] = lax.dot_general(right, left, TN, preferred_element_type=F32) * scale
    blocks = lane_block((columns, LANES), depth)
    tiles = []
    for tile in range(depth * depth // LANES):
        pieces = [
            turn_ref[pl.ds(tile * residues + e, columns, stride=depth), :]
            for e in range(residues)
        ]
        rows = jnp.concatenate(pieces, axis=0)
        turned = [rows] + [pltpu.roll(rows, depth * t, 1) for t in range(1, residues)]
        tiles.append(
            jnp.concatenate(
                [
                    pick(
                        blocks,
                        [
                            turned[(e - i) % residues][e * columns : (e + 1) * columns]
                            for e in range(residues)
                        ],
                    )
                    for i in range(residues)
                ],
                axis=0,
            )
        )
    flat = jnp.concatenate(tiles, axis=1)
    rows = residues * columns
    parts = jnp.concatenate(split_three(flat), axis=0)
    pair = jnp.dot(parts, sorted_w_ref[...], preferred_element_type=F32)
    pair = pair[0:rows] + (pair[rows : 2 * rows] + pair[2 * rows : 3 * rows])
    pair_ref[...] = (pair + offset_ref[...]).astype(BF16).reshape(pair_ref.shape)


def wide_slice(
    homolog_matrix,
    standardizer_scaling,
    standardizer_offset,
    left_projection_matrix,
    left_offset_vector,
    right_projection_matrix,
    right_offset_vector,
    coupling_matrix,
    coupling_offset,
    coupling_cotangent,
):
    seqs, residues, features = homolog_matrix.shape
    depth = left_projection_matrix.shape[1]
    ranks = lax.axis_size("res")
    scale = 1.0 / (seqs * lax.axis_size("seq"))
    half_ranks = ranks // 2
    half_columns = half_ranks * residues
    step_ranks = 4
    columns = step_ranks * residues
    steps = half_ranks // step_ranks
    mine = lax.axis_index("seq")
    swap = [(0, 1), (1, 0)]

    other_cot = lax.ppermute(coupling_cotangent, "seq", swap)
    gain = standardizer_scaling.reshape(1, -1)
    left_w = left_projection_matrix.T
    right_w = right_projection_matrix.T

    left, right, sorted_w = pl.pallas_call(
        project_kernel,
        out_shape=(
            jax.ShapeDtypeStruct((seqs, LANES), BF16),
            jax.ShapeDtypeStruct((seqs, LANES), BF16),
            jax.ShapeDtypeStruct(coupling_matrix.shape, BF16),
        ),
        scratch_shapes=[pltpu.VMEM(coupling_matrix.shape, F32)],
        name="project",
    )(
        homolog_matrix,
        gain,
        standardizer_offset.reshape(1, -1),
        left_w,
        left_offset_vector.reshape(1, -1),
        right_w,
        right_offset_vector.reshape(1, -1),
        coupling_matrix,
    )

    whole = lambda shape: pl.BlockSpec(shape, lambda g: (0,) * len(shape))
    cot_block = pl.BlockSpec((residues, columns, LANES), lambda g: (0, g, 0))
    outer_block = pl.BlockSpec((2, columns * depth, LANES), lambda g: (0, g, 0))
    send_block = pl.BlockSpec((2, step_ranks, 2 * seqs, LANES), lambda g: (0, g, 0, 0))
    send, outer = pl.pallas_call(
        functools.partial(cot_kernel, scale),
        grid=(steps,),
        in_specs=[
            cot_block,
            cot_block,
            whole(sorted_w.shape),
            whole(left.shape),
            whole(right.shape),
        ],
        out_specs=(send_block, outer_block),
        out_shape=(
            jax.ShapeDtypeStruct((2, half_ranks, 2 * seqs, LANES), BF16),
            jax.ShapeDtypeStruct((2, half_columns * depth, LANES), BF16),
        ),
        scratch_shapes=[pltpu.VMEM((2 * columns * depth, LANES), F32)],
        name="cotangent",
    )(coupling_cotangent, other_cot, sorted_w, left, right)

    got = lax.all_to_all(
        send.reshape(ranks, 2 * seqs, LANES), "res", split_axis=0, concat_axis=0, tiled=True
    ).reshape(send.shape)

    leaving = lax.dynamic_index_in_dim(got, 1 - mine, 0, keepdims=False)[:, 0:seqs, :]
    far = lax.ppermute(jnp.concatenate([leaving, left[None]], axis=0), "seq", swap)

    gradient = pl.pallas_call(
        functools.partial(grad_kernel, steps),
        grid=(steps,),
        in_specs=[
            send_block,
            outer_block,
            whole(homolog_matrix.shape),
            whole(gain.shape),
            whole(left_w.shape),
            whole(right_w.shape),
        ],
        out_specs=whole(homolog_matrix.shape),
        out_shape=jax.ShapeDtypeStruct(homolog_matrix.shape, BF16),
        scratch_shapes=[pltpu.VMEM((seqs, LANES), F32)] * 2,
        name="gradient",
    )(got, outer, homolog_matrix, gain, left_w, right_w)

    pair_delta = pl.pallas_call(
        functools.partial(pair_kernel, scale),
        grid=(steps,),
        in_specs=[
            pl.BlockSpec((2, step_ranks, seqs, LANES), lambda g: (0, g, 0, 0)),
            pl.BlockSpec((step_ranks, seqs, LANES), lambda g: (g, 0, 0)),
            whole(left.shape),
            pl.BlockSpec((None, seqs, LANES), lambda g: (half_ranks, 0, 0)),
            whole(sorted_w.shape),
            whole((1, LANES)),
        ],
        out_specs=cot_block,
        out_shape=jax.ShapeDtypeStruct(coupling_cotangent.shape, BF16),
        scratch_shapes=[pltpu.VMEM((columns * depth, LANES), F32)],
        name="pair",
    )(got, far, left, far, sorted_w, coupling_offset.reshape(1, -1))
    return (pair_delta, gradient)


def fetch(source, target, semaphore):
    copy = pltpu.make_async_copy(source, target, semaphore)
    copy.start()
    return copy


def small_project_kernel(
    x_ref, gain_ref, offset_ref, left_w_ref, left_b_ref, right_w_ref, right_b_ref, w_hbm, pair_offset_ref,
    left_ref, right_ref, sorted_w_ref, normed_ref, inv_std_ref, spread_w_ref, gain_out_ref,
    pair_offset_out_ref, raw_ref, wide_ref, semaphore,
):
    copy = fetch(w_hbm, raw_ref, semaphore)
    seqs, residues, _ = x_ref.shape
    depth = left_w_ref.shape[0]
    normed, inv_std = normalise(residue_rows(x_ref))
    normed_ref[...] = normed
    inv_std_ref[...] = jnp.broadcast_to(inv_std, inv_std_ref.shape)
    ln_out = (normed * gain_ref[...] + offset_ref[...]).astype(BF16)
    blocks = lane_block((seqs, LANES), depth)
    spread = []
    for weight_ref, bias_ref, out_ref in (
        (left_w_ref, left_b_ref, left_ref),
        (right_w_ref, right_b_ref, right_ref),
    ):
        weight = jnp.concatenate([weight_ref[...]] * residues, axis=0)
        spread.append(weight)
        bias = jnp.concatenate([bias_ref[...]] * residues, axis=1)
        wide = lax.dot_general(ln_out, weight, NT, preferred_element_type=F32)
        own = pick(blocks, [wide[p * seqs : (p + 1) * seqs] for p in range(residues)])
        out_ref[...] = (own + bias).astype(BF16)
    spread_w_ref[...] = jnp.concatenate(spread, axis=0)
    gain_out_ref[...] = gain_ref[...]
    pair_offset_out_ref[...] = pair_offset_ref[...]
    copy.wait()
    wide_ref[...] = raw_ref[...].astype(F32)
    for d in range(depth):
        sorted_w_ref[d * depth : (d + 1) * depth, :] = wide_ref[
            pl.ds(d, depth, stride=depth), :
        ].astype(BF16)


def small_cot_kernel(scale, own_ref, other_ref, sorted_w_ref, left_ref, right_ref,
                    send_ref, outer_ref, turn_ref):
    residues, columns, _ = own_ref.shape
    depth = LANES // residues
    first = lax.axis_index("seq") == 0
    own = own_ref[...].reshape(residues * columns, LANES)
    other = other_ref[...].reshape(residues * columns, LANES)
    both = jnp.concatenate([jnp.where(first, own, other), jnp.where(first, other, own)], axis=0)
    flat = lax.dot_general(both, sorted_w_ref[...], NT, preferred_element_type=F32) * scale
    blocks = lane_block((columns, LANES), depth)
    for half in range(2):
        for tile in range(depth * depth // LANES):
            block = flat[
                half * residues * columns : (half + 1) * residues * columns,
                tile * LANES : (tile + 1) * LANES,
            ]
            turned = [block] + [pltpu.roll(block, depth * t, 1) for t in range(1, residues)]
            for e in range(residues):
                start = half * columns * depth + tile * residues + e
                turn_ref[pl.ds(start, columns, stride=depth), :] = pick(
                    blocks,
                    [
                        turned[(i - e) % residues][i * columns : (i + 1) * columns]
                        for i in range(residues)
                    ],
                )
    outer = turn_ref[...].astype(BF16)
    outer_ref[...] = outer
    partial = lax.dot_general(left_ref[...], outer, NT, preferred_element_type=F32)
    seqs = left_ref.shape[0]
    partial = partial.astype(BF16)
    for place in range(2 * columns // residues):
        send_ref[place, 0:seqs, :] = right_ref[...]
        send_ref[place, seqs : 2 * seqs, :] = partial[:, place * LANES : (place + 1) * LANES]


def small_grad_kernel(got_ref, outer_ref, normed_ref, inv_std_ref, gain_ref, spread_w_ref, grad_ref):
    ranks, twice, _ = got_ref.shape
    seqs = twice // 2
    residues = grad_ref.shape[1]
    depth = LANES // residues
    right_all = jnp.concatenate([got_ref[place, 0:seqs, :] for place in range(ranks)], axis=1)
    left_cot = jnp.dot(right_all, outer_ref[...], preferred_element_type=F32)
    right_cot = got_ref[0, seqs:twice, :].astype(F32)
    for place in range(1, ranks):
        right_cot = right_cot + got_ref[place, seqs:twice, :].astype(F32)
    blocks = lane_block((seqs, LANES), depth)
    spread = jnp.concatenate(
        [
            jnp.concatenate(
                [jnp.where(blocks == place, cot, 0.0) for cot in (left_cot, right_cot)], axis=1
            )
            for place in range(residues)
        ],
        axis=0,
    )
    rows = residues * seqs
    parts = jnp.concatenate(split_three(spread), axis=0)
    ln_cot = jnp.dot(parts, spread_w_ref[...], preferred_element_type=F32)
    ln_cot = ln_cot[0:rows] + (ln_cot[rows : 2 * rows] + ln_cot[2 * rows : 3 * rows])
    gained = ln_cot * gain_ref[...]
    normed = normed_ref[...]
    grad = inv_std_ref[:, 0:1] * (
        gained
        - jnp.mean(gained, axis=-1, keepdims=True)
        - normed * jnp.mean(gained * normed, axis=-1, keepdims=True)
    )
    for place in range(residues):
        grad_ref[:, place, :] = grad[place * seqs : (place + 1) * seqs].astype(BF16)


def small_pair_kernel(scale, got_ref, far_ref, left_ref, sorted_w_ref, offset_ref,
                     pair_ref, turn_ref):
    residues, columns, _ = pair_ref.shape
    depth = LANES // residues
    ranks = columns // residues
    seqs = left_ref.shape[0]
    base = lax.axis_index("seq") * ranks
    near = jnp.concatenate([got_ref[base + place, 0:seqs, :] for place in range(ranks)], axis=1)
    far = jnp.concatenate([far_ref[place] for place in range(ranks)], axis=1)
    right = jnp.concatenate([near, far], axis=0)
    left = jnp.concatenate([left_ref[...], far_ref[ranks]], axis=0)
    turn_ref[...] = lax.dot_general(right, left, TN, preferred_element_type=F32) * scale
    blocks = lane_block((columns, LANES), depth)
    tiles = []
    for tile in range(depth * depth // LANES):
        pieces = [
            turn_ref[pl.ds(tile * residues + e, columns, stride=depth), :]
            for e in range(residues)
        ]
        rows = jnp.concatenate(pieces, axis=0)
        turned = [rows] + [pltpu.roll(rows, depth * t, 1) for t in range(1, residues)]
        tiles.append(
            jnp.concatenate(
                [
                    pick(
                        blocks,
                        [
                            turned[(e - i) % residues][e * columns : (e + 1) * columns]
                            for e in range(residues)
                        ],
                    )
                    for i in range(residues)
                ],
                axis=0,
            )
        )
    flat = jnp.concatenate(tiles, axis=1)
    rows = residues * columns
    parts = jnp.concatenate(split_three(flat), axis=0)
    pair = jnp.dot(parts, sorted_w_ref[...], preferred_element_type=F32)
    pair = pair[0:rows] + (pair[rows : 2 * rows] + pair[2 * rows : 3 * rows])
    pair_ref[...] = (pair + offset_ref[...]).astype(BF16).reshape(pair_ref.shape)


def small_slice(
    homolog_matrix,
    standardizer_scaling,
    standardizer_offset,
    left_projection_matrix,
    left_offset_vector,
    right_projection_matrix,
    right_offset_vector,
    coupling_matrix,
    coupling_offset,
    coupling_cotangent,
):
    seqs, residues, features = homolog_matrix.shape
    ranks = lax.axis_size("res")
    rows = seqs * residues
    scale = 1.0 / (seqs * lax.axis_size("seq"))
    mine = lax.axis_index("seq")
    swap = [(0, 1), (1, 0)]
    limit = pltpu.CompilerParams(vmem_limit_bytes=8 * 1024 * 1024)
    vmem = pl.BlockSpec(memory_space=pltpu.VMEM)
    like = jax.ShapeDtypeStruct

    other_cot = lax.ppermute(coupling_cotangent, "seq", swap)
    left, right, sorted_w, normed, inv_std, spread_w, gain, pair_offset = pl.pallas_call(
        small_project_kernel,
        in_specs=[vmem] * 7 + [pl.BlockSpec(memory_space=pl.ANY), vmem],
        out_specs=[vmem] * 8,
        out_shape=(
            like((seqs, LANES), BF16),
            like((seqs, LANES), BF16),
            like(coupling_matrix.shape, BF16),
            like((rows, features), F32),
            like((rows, LANES), F32),
            like((2 * LANES, features), BF16),
            like((1, features), F32),
            like((1, LANES), F32),
        ),
        scratch_shapes=[
            pltpu.VMEM(coupling_matrix.shape, BF16),
            pltpu.VMEM(coupling_matrix.shape, F32),
            pltpu.SemaphoreType.DMA,
        ],
        compiler_params=limit,
        name="project",
    )(
        homolog_matrix,
        standardizer_scaling.reshape(1, -1),
        standardizer_offset.reshape(1, -1),
        left_projection_matrix.T,
        left_offset_vector.reshape(1, -1),
        right_projection_matrix.T,
        right_offset_vector.reshape(1, -1),
        coupling_matrix,
        coupling_offset.reshape(1, -1),
    )

    send, outer = pl.pallas_call(
        functools.partial(small_cot_kernel, scale),
        in_specs=[vmem] * 5,
        out_specs=[vmem] * 2,
        out_shape=(
            like((ranks, 2 * seqs, LANES), BF16),
            like((ranks * LANES, LANES), BF16),
        ),
        scratch_shapes=[pltpu.VMEM((ranks * LANES, LANES), F32)],
        compiler_params=limit,
        name="cotangent",
    )(coupling_cotangent, other_cot, sorted_w, left, right)

    got = lax.all_to_all(send, "res", split_axis=0, concat_axis=0, tiled=True)
    half = got.reshape(2, ranks // 2, 2 * seqs, LANES)
    leaving = lax.dynamic_index_in_dim(half, 1 - mine, 0, keepdims=False)[:, 0:seqs, :]
    far = lax.ppermute(jnp.concatenate([leaving, left[None]]), "seq", swap)

    gradient = pl.pallas_call(
        small_grad_kernel,
        in_specs=[vmem] * 6,
        out_specs=vmem,
        out_shape=like(homolog_matrix.shape, BF16),
        compiler_params=limit,
        name="gradient",
    )(got, outer, normed, inv_std, gain, spread_w)

    pair_delta = pl.pallas_call(
        functools.partial(small_pair_kernel, scale),
        in_specs=[vmem] * 5,
        out_specs=vmem,
        out_shape=like(coupling_cotangent.shape, BF16),
        scratch_shapes=[pltpu.VMEM((ranks // 2 * LANES, LANES), F32)],
        compiler_params=limit,
        name="pair",
    )(got, far, left, sorted_w, pair_offset)
    return (pair_delta, gradient)


def body(*arrays):
    if lax.axis_size("res") == 8:
        return small_slice(*arrays)
    return wide_slice(*arrays)


def solution(mesh):
    return jax.shard_map(
        body,
        mesh=mesh,
        in_specs=(
            P(("grp", "seq"), "res", None),
            P(),
            P(),
            P(),
            P(),
            P(),
            P(),
            P(),
            P(),
            P(("grp", "res"), "seq", None),
        ),
        out_specs=(P(("grp", "res"), "seq", None), P(("grp", "seq"), "res", None)),
        check_vma=False,
    )
```

```python
import functools

import jax
import jax.numpy as jnp
from jax import lax
from jax.experimental import pallas as pl
from jax.experimental.pallas import tpu as pltpu
from jax.sharding import PartitionSpec as P

LANES = 128
BF16 = jnp.bfloat16
F32 = jnp.float32
NT = (((1,), (1,)), ((), ()))
TN = (((0,), (0,)), ((), ()))


def lane_block(shape, width):
    return lax.broadcasted_iota(jnp.int32, shape, 1) // width


def pick(blocks, pieces):
    result = pieces[0]
    for place in range(1, len(pieces)):
        result = jnp.where(blocks == place, pieces[place], result)
    return result


def split_three(value):
    top = value.astype(BF16)
    rest = value - top.astype(F32)
    middle = rest.astype(BF16)
    low = (rest - middle.astype(F32)).astype(BF16)
    return top, middle, low


def normalise(rows):
    centred = rows - jnp.mean(rows, axis=-1, keepdims=True)
    inv_std = lax.rsqrt(jnp.mean(centred * centred, axis=-1, keepdims=True) + 1e-05)
    return centred * inv_std, inv_std


def residue_rows(x_ref):
    return jnp.concatenate(
        [x_ref[:, place, :].astype(F32) for place in range(x_ref.shape[1])], axis=0
    )


def project_kernel(
    x_ref, gain_ref, offset_ref, left_w_ref, left_b_ref, right_w_ref, right_b_ref, w_ref,
    left_ref, right_ref, sorted_w_ref, wide_ref,
):
    seqs, residues, _ = x_ref.shape
    depth = left_w_ref.shape[0]
    normed, _ = normalise(residue_rows(x_ref))
    ln_out = (normed * gain_ref[...] + offset_ref[...]).astype(BF16)
    blocks = lane_block((seqs, LANES), depth)
    for weight_ref, bias_ref, out_ref in (
        (left_w_ref, left_b_ref, left_ref),
        (right_w_ref, right_b_ref, right_ref),
    ):
        weight = jnp.concatenate([weight_ref[...]] * residues, axis=0)
        bias = jnp.concatenate([bias_ref[...]] * residues, axis=1)
        wide = lax.dot_general(ln_out, weight, NT, preferred_element_type=F32)
        own = pick(blocks, [wide[p * seqs : (p + 1) * seqs] for p in range(residues)])
        out_ref[...] = (own + bias).astype(BF16)
    wide_ref[...] = w_ref[...].astype(F32)
    for d in range(depth):
        sorted_w_ref[d * depth : (d + 1) * depth, :] = wide_ref[
            pl.ds(d, depth, stride=depth), :
        ].astype(BF16)


def cot_kernel(scale, own_ref, other_ref, sorted_w_ref, left_ref, right_ref,
               send_ref, outer_ref, turn_ref):
    residues, columns, _ = own_ref.shape
    depth = sorted_w_ref.shape[0] // (LANES // residues)
    depth = LANES // residues
    first = lax.axis_index("seq") == 0
    own = own_ref[...].reshape(residues * columns, LANES)
    other = other_ref[...].reshape(residues * columns, LANES)
    low = jnp.where(first, own, other)
    high = jnp.where(first, other, own)
    both = jnp.concatenate([low, high], axis=0)
    flat = lax.dot_general(both, sorted_w_ref[...], NT, preferred_element_type=F32) * scale
    blocks = lane_block((columns, LANES), depth)
    for half in range(2):
        for tile in range(depth * depth // LANES):
            block = flat[
                half * residues * columns : (half + 1) * residues * columns,
                tile * LANES : (tile + 1) * LANES,
            ]
            turned = [block] + [pltpu.roll(block, depth * t, 1) for t in range(1, residues)]
            for e in range(residues):
                piece = pick(
                    blocks,
                    [
                        turned[(i - e) % residues][i * columns : (i + 1) * columns]
                        for i in range(residues)
                    ],
                )
                turn_ref[pl.ds(half * columns * depth + tile * residues + e, columns, stride=depth), :] = piece
    outer = turn_ref[...].astype(BF16)
    half_rows = columns * depth
    partial = lax.dot_general(left_ref[...], outer, NT, preferred_element_type=F32).astype(BF16)
    seqs = left_ref.shape[0]
    ranks = columns // residues
    for half in range(2):
        outer_ref[half] = outer[half * half_rows : (half + 1) * half_rows]
        for rank in range(ranks):
            at = (half * ranks + rank) * LANES
            send_ref[half, rank, 0:seqs, :] = right_ref[...]
            send_ref[half, rank, seqs : 2 * seqs, :] = partial[:, at : at + LANES]


def grad_kernel(steps, got_ref, outer_ref, x_ref, gain_ref, left_w_ref, right_w_ref,
                grad_ref, left_cot_ref, right_cot_ref):
    step = pl.program_id(0)
    _, ranks, twice, _ = got_ref.shape
    seqs = twice // 2
    residues = x_ref.shape[1]
    depth = LANES // residues

    @pl.when(step == 0)
    def _():
        left_cot_ref[...] = jnp.zeros_like(left_cot_ref)
        right_cot_ref[...] = jnp.zeros_like(right_cot_ref)

    places = [(half, rank) for half in range(2) for rank in range(ranks)]
    right_all = jnp.concatenate([got_ref[h, r, 0:seqs, :] for h, r in places], axis=1)
    outer = jnp.concatenate([outer_ref[0], outer_ref[1]], axis=0)
    left_cot_ref[...] += jnp.dot(right_all, outer, preferred_element_type=F32)
    total = got_ref[0, 0, seqs:twice, :].astype(F32)
    for h, r in places[1:]:
        total = total + got_ref[h, r, seqs:twice, :].astype(F32)
    right_cot_ref[...] += total

    @pl.when(step == steps - 1)
    def _():
        blocks = lane_block((seqs, LANES), depth)
        left_cot, right_cot = left_cot_ref[...], right_cot_ref[...]
        spread = jnp.concatenate(
            [
                jnp.concatenate(
                    [
                        jnp.where(blocks == place, left_cot, 0.0),
                        jnp.where(blocks == place, right_cot, 0.0),
                    ],
                    axis=1,
                )
                for place in range(residues)
            ],
            axis=0,
        )
        weight = jnp.concatenate(
            [left_w_ref[...]] * residues + [right_w_ref[...]] * residues, axis=0
        )
        rows = residues * seqs
        parts = jnp.concatenate(split_three(spread), axis=0)
        ln_cot = jnp.dot(parts, weight, preferred_element_type=F32)
        ln_cot = ln_cot[0:rows] + (ln_cot[rows : 2 * rows] + ln_cot[2 * rows : 3 * rows])
        gained = ln_cot * gain_ref[...]
        normed, inv_std = normalise(residue_rows(x_ref))
        grad = inv_std * (
            gained
            - jnp.mean(gained, axis=-1, keepdims=True)
            - normed * jnp.mean(gained * normed, axis=-1, keepdims=True)
        )
        for place in range(residues):
            grad_ref[:, place, :] = grad[place * seqs : (place + 1) * seqs].astype(BF16)


def pair_kernel(scale, got_ref, far_ref, left_ref, far_left_ref, sorted_w_ref, offset_ref,
                pair_ref, turn_ref):
    residues, columns, _ = pair_ref.shape
    depth = LANES // residues
    ranks = columns // residues
    mine = lax.axis_index("seq")
    near = jnp.concatenate([got_ref[mine, r] for r in range(ranks)], axis=1)
    far = jnp.concatenate([far_ref[r] for r in range(ranks)], axis=1)
    right = jnp.concatenate([near, far], axis=0)
    left = jnp.concatenate([left_ref[...], far_left_ref[...]], axis=0)
    turn_ref[...] = lax.dot_general(right, left, TN, preferred_element_type=F32) * scale
    blocks = lane_block((columns, LANES), depth)
    tiles = []
    for tile in range(depth * depth // LANES):
        pieces = [
            turn_ref[pl.ds(tile * residues + e, columns, stride=depth), :]
            for e in range(residues)
        ]
        rows = jnp.concatenate(pieces, axis=0)
        turned = [rows] + [pltpu.roll(rows, depth * t, 1) for t in range(1, residues)]
        tiles.append(
            jnp.concatenate(
                [
                    pick(
                        blocks,
                        [
                            turned[(e - i) % residues][e * columns : (e + 1) * columns]
                            for e in range(residues)
                        ],
                    )
                    for i in range(residues)
                ],
                axis=0,
            )
        )
    flat = jnp.concatenate(tiles, axis=1)
    rows = residues * columns
    parts = jnp.concatenate(split_three(flat), axis=0)
    pair = jnp.dot(parts, sorted_w_ref[...], preferred_element_type=F32)
    pair = pair[0:rows] + (pair[rows : 2 * rows] + pair[2 * rows : 3 * rows])
    pair_ref[...] = (pair + offset_ref[...]).astype(BF16).reshape(pair_ref.shape)


def wide_slice(
    homolog_matrix,
    standardizer_scaling,
    standardizer_offset,
    left_projection_matrix,
    left_offset_vector,
    right_projection_matrix,
    right_offset_vector,
    coupling_matrix,
    coupling_offset,
    coupling_cotangent,
):
    seqs, residues, features = homolog_matrix.shape
    depth = left_projection_matrix.shape[1]
    ranks = lax.axis_size("res")
    scale = 1.0 / (seqs * lax.axis_size("seq"))
    half_ranks = ranks // 2
    half_columns = half_ranks * residues
    step_ranks = 4
    columns = step_ranks * residues
    steps = half_ranks // step_ranks
    mine = lax.axis_index("seq")
    swap = [(0, 1), (1, 0)]

    other_cot = lax.ppermute(coupling_cotangent, "seq", swap)
    gain = standardizer_scaling.reshape(1, -1)
    left_w = left_projection_matrix.T
    right_w = right_projection_matrix.T

    left, right, sorted_w = pl.pallas_call(
        project_kernel,
        out_shape=(
            jax.ShapeDtypeStruct((seqs, LANES), BF16),
            jax.ShapeDtypeStruct((seqs, LANES), BF16),
            jax.ShapeDtypeStruct(coupling_matrix.shape, BF16),
        ),
        scratch_shapes=[pltpu.VMEM(coupling_matrix.shape, F32)],
        name="project",
    )(
        homolog_matrix,
        gain,
        standardizer_offset.reshape(1, -1),
        left_w,
        left_offset_vector.reshape(1, -1),
        right_w,
        right_offset_vector.reshape(1, -1),
        coupling_matrix,
    )

    whole = lambda shape: pl.BlockSpec(shape, lambda g: (0,) * len(shape))
    cot_block = pl.BlockSpec((residues, columns, LANES), lambda g: (0, g, 0))
    outer_block = pl.BlockSpec((2, columns * depth, LANES), lambda g: (0, g, 0))
    send_block = pl.BlockSpec((2, step_ranks, 2 * seqs, LANES), lambda g: (0, g, 0, 0))
    send, outer = pl.pallas_call(
        functools.partial(cot_kernel, scale),
        grid=(steps,),
        in_specs=[
            cot_block,
            cot_block,
            whole(sorted_w.shape),
            whole(left.shape),
            whole(right.shape),
        ],
        out_specs=(send_block, outer_block),
        out_shape=(
            jax.ShapeDtypeStruct((2, half_ranks, 2 * seqs, LANES), BF16),
            jax.ShapeDtypeStruct((2, half_columns * depth, LANES), BF16),
        ),
        scratch_shapes=[pltpu.VMEM((2 * columns * depth, LANES), F32)],
        name="cotangent",
    )(coupling_cotangent, other_cot, sorted_w, left, right)

    got = lax.all_to_all(
        send.reshape(ranks, 2 * seqs, LANES), "res", split_axis=0, concat_axis=0, tiled=True
    ).reshape(send.shape)

    leaving = lax.dynamic_index_in_dim(got, 1 - mine, 0, keepdims=False)[:, 0:seqs, :]
    far = lax.ppermute(jnp.concatenate([leaving, left[None]], axis=0), "seq", swap)

    gradient = pl.pallas_call(
        functools.partial(grad_kernel, steps),
        grid=(steps,),
        in_specs=[
            send_block,
            outer_block,
            whole(homolog_matrix.shape),
            whole(gain.shape),
            whole(left_w.shape),
            whole(right_w.shape),
        ],
        out_specs=whole(homolog_matrix.shape),
        out_shape=jax.ShapeDtypeStruct(homolog_matrix.shape, BF16),
        scratch_shapes=[pltpu.VMEM((seqs, LANES), F32)] * 2,
        name="gradient",
    )(got, outer, homolog_matrix, gain, left_w, right_w)

    pair_delta = pl.pallas_call(
        functools.partial(pair_kernel, scale),
        grid=(steps,),
        in_specs=[
            pl.BlockSpec((2, step_ranks, seqs, LANES), lambda g: (0, g, 0, 0)),
            pl.BlockSpec((step_ranks, seqs, LANES), lambda g: (g, 0, 0)),
            whole(left.shape),
            pl.BlockSpec((None, seqs, LANES), lambda g: (half_ranks, 0, 0)),
            whole(sorted_w.shape),
            whole((1, LANES)),
        ],
        out_specs=cot_block,
        out_shape=jax.ShapeDtypeStruct(coupling_cotangent.shape, BF16),
        scratch_shapes=[pltpu.VMEM((columns * depth, LANES), F32)],
        name="pair",
    )(got, far, left, far, sorted_w, coupling_offset.reshape(1, -1))
    return (pair_delta, gradient)


def fetch(source, target, semaphore):
    copy = pltpu.make_async_copy(source, target, semaphore)
    copy.start()
    return copy


def small_project_kernel(
    x_hbm, gain_hbm, offset_hbm, left_w_hbm, left_b_hbm, right_w_hbm, right_b_hbm, w_hbm, pair_offset_hbm,
    left_ref, right_ref, sorted_w_ref, normed_ref, inv_std_ref, spread_w_ref, gain_out_ref,
    pair_offset_out_ref,
    x_ref, offset_ref, left_w_ref, left_b_ref, right_w_ref, right_b_ref, raw_ref, wide_ref, semaphores,
):
    copies = [
        pltpu.make_async_copy(source, target, semaphores.at[place])
        for place, (source, target) in enumerate(
            (
                (x_hbm, x_ref),
                (gain_hbm, gain_out_ref),
                (offset_hbm, offset_ref),
                (left_w_hbm, left_w_ref),
                (left_b_hbm, left_b_ref),
                (right_w_hbm, right_w_ref),
                (right_b_hbm, right_b_ref),
                (w_hbm, raw_ref),
                (pair_offset_hbm, pair_offset_out_ref),
            )
        )
    ]
    for copy in copies:
        copy.start()
    seqs, residues, _ = x_ref.shape
    depth = left_w_ref.shape[0]
    copies[0].wait()
    normed, inv_std = normalise(residue_rows(x_ref))
    normed_ref[...] = normed
    inv_std_ref[...] = jnp.broadcast_to(inv_std, inv_std_ref.shape)
    for copy in copies[1:7]:
        copy.wait()
    ln_out = (normed * gain_out_ref[...] + offset_ref[...]).astype(BF16)
    blocks = lane_block((seqs, LANES), depth)
    spread = []
    for weight_ref, bias_ref, out_ref in (
        (left_w_ref, left_b_ref, left_ref),
        (right_w_ref, right_b_ref, right_ref),
    ):
        weight = jnp.concatenate([weight_ref[...]] * residues, axis=0)
        spread.append(weight)
        bias = jnp.concatenate([bias_ref[...]] * residues, axis=1)
        wide = lax.dot_general(ln_out, weight, NT, preferred_element_type=F32)
        own = pick(blocks, [wide[p * seqs : (p + 1) * seqs] for p in range(residues)])
        out_ref[...] = (own + bias).astype(BF16)
    spread_w_ref[...] = jnp.concatenate(spread, axis=0)
    for copy in copies[7:]:
        copy.wait()
    wide_ref[...] = raw_ref[...].astype(F32)
    for d in range(depth):
        sorted_w_ref[d * depth : (d + 1) * depth, :] = wide_ref[
            pl.ds(d, depth, stride=depth), :
        ].astype(BF16)


def small_cot_kernel(scale, own_ref, other_ref, sorted_w_ref, left_ref, right_ref,
                    send_ref, keep_ref, outer_ref, turn_ref):
    residues, columns, _ = own_ref.shape
    depth = LANES // residues
    first = lax.axis_index("seq") == 0
    own = own_ref[...].reshape(residues * columns, LANES)
    other = other_ref[...].reshape(residues * columns, LANES)
    both = jnp.concatenate([jnp.where(first, own, other), jnp.where(first, other, own)], axis=0)
    flat = lax.dot_general(both, sorted_w_ref[...], NT, preferred_element_type=F32) * scale
    blocks = lane_block((columns, LANES), depth)
    for half in range(2):
        for tile in range(depth * depth // LANES):
            block = flat[
                half * residues * columns : (half + 1) * residues * columns,
                tile * LANES : (tile + 1) * LANES,
            ]
            turned = [block] + [pltpu.roll(block, depth * t, 1) for t in range(1, residues)]
            for e in range(residues):
                start = half * columns * depth + tile * residues + e
                turn_ref[pl.ds(start, columns, stride=depth), :] = pick(
                    blocks,
                    [
                        turned[(i - e) % residues][i * columns : (i + 1) * columns]
                        for i in range(residues)
                    ],
                )
    outer = turn_ref[...].astype(BF16)
    outer_ref[...] = outer
    partial = lax.dot_general(left_ref[...], outer, NT, preferred_element_type=F32)
    rank = lax.axis_index("res")
    send_ref[0] = right_ref[...]
    for place in range(2 * columns // residues):
        piece = partial[:, place * LANES : (place + 1) * LANES]
        distance = lax.bitwise_xor(rank, place)
        spot = lax.shift_right_logical(distance, 1)

        @pl.when(distance & 1 == 1)
        def _():
            send_ref[spot + 1] = piece.astype(BF16)

        @pl.when(distance & 1 == 0)
        def _():
            keep_ref[spot] = piece


def small_grad_kernel(right_ref, outer_ref, keep_ref, beside_ref, far_refs, normed_ref, inv_std_ref,
                      gain_ref, spread_w_ref, grad_ref):
    ranks, seqs, _ = right_ref.shape
    residues = grad_ref.shape[1]
    depth = LANES // residues
    rank = lax.axis_index("res")
    right_all = jnp.concatenate(
        [right_ref[lax.bitwise_xor(rank, place)] for place in range(ranks)], axis=1
    )
    left_cot = jnp.dot(right_all, outer_ref[...], preferred_element_type=F32)
    right_cot = keep_ref[0] + beside_ref[1].astype(F32)
    for far_ref in far_refs:
        right_cot = right_cot + far_ref[2].astype(F32)
    blocks = lane_block((seqs, LANES), depth)
    spread = jnp.concatenate(
        [
            jnp.concatenate(
                [jnp.where(blocks == place, cot, 0.0) for cot in (left_cot, right_cot)], axis=1
            )
            for place in range(residues)
        ],
        axis=0,
    )
    rows = residues * seqs
    parts = jnp.concatenate(split_three(spread), axis=0)
    ln_cot = jnp.dot(parts, spread_w_ref[...], preferred_element_type=F32)
    ln_cot = ln_cot[0:rows] + (ln_cot[rows : 2 * rows] + ln_cot[2 * rows : 3 * rows])
    gained = ln_cot * gain_ref[...]
    normed = normed_ref[...]
    grad = inv_std_ref[:, 0:1] * (
        gained
        - jnp.mean(gained, axis=-1, keepdims=True)
        - normed * jnp.mean(gained * normed, axis=-1, keepdims=True)
    )
    for place in range(residues):
        grad_ref[:, place, :] = grad[place * seqs : (place + 1) * seqs].astype(BF16)


def small_pair_kernel(scale, right_ref, far_ref, left_ref, sorted_w_ref, offset_ref,
                     pair_ref, turn_ref):
    residues, columns, _ = pair_ref.shape
    depth = LANES // residues
    ranks = columns // residues
    rank = lax.axis_index("res")
    base = lax.axis_index("seq") * ranks
    near, far = [], []
    for place in range(ranks):
        distance = lax.bitwise_xor(rank, base + place)
        near.append(right_ref[distance])
        far.append(far_ref[distance & (ranks - 1)])
    right = jnp.concatenate(
        [jnp.concatenate(near, axis=1), jnp.concatenate(far, axis=1)], axis=0
    )
    left = jnp.concatenate([left_ref[...], far_ref[ranks]], axis=0)
    turn_ref[...] = lax.dot_general(right, left, TN, preferred_element_type=F32) * scale
    blocks = lane_block((columns, LANES), depth)
    tiles = []
    for tile in range(depth * depth // LANES):
        pieces = [
            turn_ref[pl.ds(tile * residues + e, columns, stride=depth), :]
            for e in range(residues)
        ]
        rows = jnp.concatenate(pieces, axis=0)
        turned = [rows] + [pltpu.roll(rows, depth * t, 1) for t in range(1, residues)]
        tiles.append(
            jnp.concatenate(
                [
                    pick(
                        blocks,
                        [
                            turned[(e - i) % residues][e * columns : (e + 1) * columns]
                            for e in range(residues)
                        ],
                    )
                    for i in range(residues)
                ],
                axis=0,
            )
        )
    flat = jnp.concatenate(tiles, axis=1)
    rows = residues * columns
    parts = jnp.concatenate(split_three(flat), axis=0)
    pair = jnp.dot(parts, sorted_w_ref[...], preferred_element_type=F32)
    pair = pair[0:rows] + (pair[rows : 2 * rows] + pair[2 * rows : 3 * rows])
    pair_ref[...] = (pair + offset_ref[...]).astype(BF16).reshape(pair_ref.shape)


def small_slice(
    homolog_matrix,
    standardizer_scaling,
    standardizer_offset,
    left_projection_matrix,
    left_offset_vector,
    right_projection_matrix,
    right_offset_vector,
    coupling_matrix,
    coupling_offset,
    coupling_cotangent,
):
    seqs, residues, features = homolog_matrix.shape
    depth = left_projection_matrix.shape[1]
    ranks = lax.axis_size("res")
    rows = seqs * residues
    scale = 1.0 / (seqs * lax.axis_size("seq"))
    rank = lax.axis_index("res")
    mine = lax.axis_index("seq")
    swap = [(0, 1), (1, 0)]
    limit = pltpu.CompilerParams(vmem_limit_bytes=8 * 1024 * 1024)
    vmem = pl.BlockSpec(memory_space=pltpu.VMEM)
    like = jax.ShapeDtypeStruct

    other_cot = lax.ppermute(coupling_cotangent, "seq", swap)
    left, right, sorted_w, normed, inv_std, spread_w, gain, pair_offset = pl.pallas_call(
        small_project_kernel,
        in_specs=[pl.BlockSpec(memory_space=pltpu.HBM)] * 9,
        out_specs=[vmem] * 8,
        out_shape=(
            like((seqs, LANES), BF16),
            like((seqs, LANES), BF16),
            like(coupling_matrix.shape, BF16),
            like((rows, features), F32),
            like((rows, LANES), F32),
            like((2 * LANES, features), BF16),
            like((1, features), F32),
            like((1, LANES), F32),
        ),
        scratch_shapes=[
            pltpu.VMEM(homolog_matrix.shape, BF16),
            pltpu.VMEM((1, features), F32),
            pltpu.VMEM((depth, features), BF16),
            pltpu.VMEM((1, depth), F32),
            pltpu.VMEM((depth, features), BF16),
            pltpu.VMEM((1, depth), F32),
            pltpu.VMEM(coupling_matrix.shape, BF16),
            pltpu.VMEM(coupling_matrix.shape, F32),
            pltpu.SemaphoreType.DMA((9,)),
        ],
        compiler_params=limit,
        name="project",
    )(
        homolog_matrix,
        standardizer_scaling.reshape(1, -1),
        standardizer_offset.reshape(1, -1),
        left_projection_matrix.T,
        left_offset_vector.reshape(1, -1),
        right_projection_matrix.T,
        right_offset_vector.reshape(1, -1),
        coupling_matrix,
        coupling_offset.reshape(1, -1),
    )

    send, keep, outer = pl.pallas_call(
        functools.partial(small_cot_kernel, scale),
        in_specs=[vmem] * 5,
        out_specs=[vmem] * 3,
        out_shape=(
            like((1 + ranks // 2, seqs, LANES), BF16),
            like((ranks // 2, seqs, LANES), F32),
            like((ranks * LANES, LANES), BF16),
        ),
        scratch_shapes=[pltpu.VMEM((ranks * LANES, LANES), F32)],
        compiler_params=limit,
        name="cotangent",
    )(coupling_cotangent, other_cot, sorted_w, left, right)

    def swap_over(mask, value):
        return lax.ppermute(value, "res", [(source, source ^ mask) for source in range(ranks)])

    own = right[None]
    beside = swap_over(1, send)
    both = jnp.concatenate([own, beside[0:1]])
    far_parts = {}
    for mask in (6, 4, 2):
        spot = mask // 2
        summed = (keep[spot] + beside[1 + spot].astype(F32)).astype(BF16)
        far_parts[mask] = swap_over(mask, jnp.concatenate([both, summed[None]]))
    far_parts = [far_parts[mask] for mask in (2, 4, 6)]
    gathered = jnp.concatenate([both] + [part[0:2] for part in far_parts])

    half = gathered.reshape(2, ranks // 2, seqs, LANES)
    beyond = 1 - lax.bitwise_xor(lax.shift_right_logical(rank, 2), mine)
    leaving = lax.dynamic_index_in_dim(half, beyond, 0, keepdims=False)
    far = lax.ppermute(jnp.concatenate([leaving, left[None]]), "seq", swap)

    gradient = pl.pallas_call(
        small_grad_kernel,
        in_specs=[vmem] * 4 + [[vmem] * 3] + [vmem] * 4,
        out_specs=vmem,
        out_shape=like(homolog_matrix.shape, BF16),
        compiler_params=limit,
        name="gradient",
    )(gathered, outer, keep, beside, far_parts, normed, inv_std, gain, spread_w)

    pair_delta = pl.pallas_call(
        functools.partial(small_pair_kernel, scale),
        in_specs=[vmem] * 5,
        out_specs=vmem,
        out_shape=like(coupling_cotangent.shape, BF16),
        scratch_shapes=[pltpu.VMEM((ranks // 2 * LANES, LANES), F32)],
        compiler_params=limit,
        name="pair",
    )(gathered, far, left, sorted_w, pair_offset)
    return (pair_delta, gradient)


def body(*arrays):
    if lax.axis_size("res") == 8:
        return small_slice(*arrays)
    return wide_slice(*arrays)


def solution(mesh):
    return jax.shard_map(
        body,
        mesh=mesh,
        in_specs=(
            P(("grp", "seq"), "res", None),
            P(),
            P(),
            P(),
            P(),
            P(),
            P(),
            P(),
            P(),
            P(("grp", "res"), "seq", None),
        ),
        out_specs=(P(("grp", "res"), "seq", None), P(("grp", "seq"), "res", None)),
        check_vma=False,
    )
```

```python
import functools

import jax
import jax.numpy as jnp
from jax import lax
from jax.experimental import pallas as pl
from jax.experimental.pallas import tpu as pltpu
from jax.sharding import PartitionSpec as P

LANES = 128
BF16 = jnp.bfloat16
F32 = jnp.float32
NT = (((1,), (1,)), ((), ()))
TN = (((0,), (0,)), ((), ()))


def lane_block(shape, width):
    return lax.broadcasted_iota(jnp.int32, shape, 1) // width


def pick(blocks, pieces):
    result = pieces[0]
    for place in range(1, len(pieces)):
        result = jnp.where(blocks == place, pieces[place], result)
    return result


def split_three(value):
    top = value.astype(BF16)
    rest = value - top.astype(F32)
    middle = rest.astype(BF16)
    low = (rest - middle.astype(F32)).astype(BF16)
    return top, middle, low


def normalise(rows):
    centred = rows - jnp.mean(rows, axis=-1, keepdims=True)
    inv_std = lax.rsqrt(jnp.mean(centred * centred, axis=-1, keepdims=True) + 1e-05)
    return centred * inv_std, inv_std


def residue_rows(x_ref):
    return jnp.concatenate(
        [x_ref[:, place, :].astype(F32) for place in range(x_ref.shape[1])], axis=0
    )


def project_kernel(
    x_ref, gain_ref, offset_ref, left_w_ref, left_b_ref, right_w_ref, right_b_ref, w_ref,
    left_ref, right_ref, sorted_w_ref, wide_ref,
):
    seqs, residues, _ = x_ref.shape
    depth = left_w_ref.shape[0]
    normed, _ = normalise(residue_rows(x_ref))
    ln_out = (normed * gain_ref[...] + offset_ref[...]).astype(BF16)
    blocks = lane_block((seqs, LANES), depth)
    for weight_ref, bias_ref, out_ref in (
        (left_w_ref, left_b_ref, left_ref),
        (right_w_ref, right_b_ref, right_ref),
    ):
        weight = jnp.concatenate([weight_ref[...]] * residues, axis=0)
        bias = jnp.concatenate([bias_ref[...]] * residues, axis=1)
        wide = lax.dot_general(ln_out, weight, NT, preferred_element_type=F32)
        own = pick(blocks, [wide[p * seqs : (p + 1) * seqs] for p in range(residues)])
        out_ref[...] = (own + bias).astype(BF16)
    wide_ref[...] = w_ref[...].astype(F32)
    for d in range(depth):
        sorted_w_ref[d * depth : (d + 1) * depth, :] = wide_ref[
            pl.ds(d, depth, stride=depth), :
        ].astype(BF16)


def cot_kernel(scale, own_ref, other_ref, sorted_w_ref, left_ref, right_ref,
               send_ref, outer_ref, turn_ref):
    residues, columns, _ = own_ref.shape
    depth = sorted_w_ref.shape[0] // (LANES // residues)
    depth = LANES // residues
    first = lax.axis_index("seq") == 0
    own = own_ref[...].reshape(residues * columns, LANES)
    other = other_ref[...].reshape(residues * columns, LANES)
    low = jnp.where(first, own, other)
    high = jnp.where(first, other, own)
    both = jnp.concatenate([low, high], axis=0)
    flat = lax.dot_general(both, sorted_w_ref[...], NT, preferred_element_type=F32) * scale
    blocks = lane_block((columns, LANES), depth)
    for half in range(2):
        for tile in range(depth * depth // LANES):
            block = flat[
                half * residues * columns : (half + 1) * residues * columns,
                tile * LANES : (tile + 1) * LANES,
            ]
            turned = [block] + [pltpu.roll(block, depth * t, 1) for t in range(1, residues)]
            for e in range(residues):
                piece = pick(
                    blocks,
                    [
                        turned[(i - e) % residues][i * columns : (i + 1) * columns]
                        for i in range(residues)
                    ],
                )
                turn_ref[pl.ds(half * columns * depth + tile * residues + e, columns, stride=depth), :] = piece
    outer = turn_ref[...].astype(BF16)
    half_rows = columns * depth
    partial = lax.dot_general(left_ref[...], outer, NT, preferred_element_type=F32).astype(BF16)
    seqs = left_ref.shape[0]
    ranks = columns // residues
    for half in range(2):
        outer_ref[half] = outer[half * half_rows : (half + 1) * half_rows]
        for rank in range(ranks):
            at = (half * ranks + rank) * LANES
            send_ref[half, rank, 0:seqs, :] = right_ref[...]
            send_ref[half, rank, seqs : 2 * seqs, :] = partial[:, at : at + LANES]


def grad_kernel(steps, got_ref, outer_ref, x_ref, gain_ref, left_w_ref, right_w_ref,
                grad_ref, left_cot_ref, right_cot_ref):
    step = pl.program_id(0)
    _, ranks, twice, _ = got_ref.shape
    seqs = twice // 2
    residues = x_ref.shape[1]
    depth = LANES // residues

    @pl.when(step == 0)
    def _():
        left_cot_ref[...] = jnp.zeros_like(left_cot_ref)
        right_cot_ref[...] = jnp.zeros_like(right_cot_ref)

    places = [(half, rank) for half in range(2) for rank in range(ranks)]
    right_all = jnp.concatenate([got_ref[h, r, 0:seqs, :] for h, r in places], axis=1)
    outer = jnp.concatenate([outer_ref[0], outer_ref[1]], axis=0)
    left_cot_ref[...] += jnp.dot(right_all, outer, preferred_element_type=F32)
    total = got_ref[0, 0, seqs:twice, :].astype(F32)
    for h, r in places[1:]:
        total = total + got_ref[h, r, seqs:twice, :].astype(F32)
    right_cot_ref[...] += total

    @pl.when(step == steps - 1)
    def _():
        blocks = lane_block((seqs, LANES), depth)
        left_cot, right_cot = left_cot_ref[...], right_cot_ref[...]
        spread = jnp.concatenate(
            [
                jnp.concatenate(
                    [
                        jnp.where(blocks == place, left_cot, 0.0),
                        jnp.where(blocks == place, right_cot, 0.0),
                    ],
                    axis=1,
                )
                for place in range(residues)
            ],
            axis=0,
        )
        weight = jnp.concatenate(
            [left_w_ref[...]] * residues + [right_w_ref[...]] * residues, axis=0
        )
        rows = residues * seqs
        parts = jnp.concatenate(split_three(spread), axis=0)
        ln_cot = jnp.dot(parts, weight, preferred_element_type=F32)
        ln_cot = ln_cot[0:rows] + (ln_cot[rows : 2 * rows] + ln_cot[2 * rows : 3 * rows])
        gained = ln_cot * gain_ref[...]
        normed, inv_std = normalise(residue_rows(x_ref))
        grad = inv_std * (
            gained
            - jnp.mean(gained, axis=-1, keepdims=True)
            - normed * jnp.mean(gained * normed, axis=-1, keepdims=True)
        )
        for place in range(residues):
            grad_ref[:, place, :] = grad[place * seqs : (place + 1) * seqs].astype(BF16)


def pair_kernel(scale, got_ref, far_ref, left_ref, far_left_ref, sorted_w_ref, offset_ref,
                pair_ref, turn_ref):
    residues, columns, _ = pair_ref.shape
    depth = LANES // residues
    ranks = columns // residues
    mine = lax.axis_index("seq")
    near = jnp.concatenate([got_ref[mine, r] for r in range(ranks)], axis=1)
    far = jnp.concatenate([far_ref[r] for r in range(ranks)], axis=1)
    right = jnp.concatenate([near, far], axis=0)
    left = jnp.concatenate([left_ref[...], far_left_ref[...]], axis=0)
    turn_ref[...] = lax.dot_general(right, left, TN, preferred_element_type=F32) * scale
    blocks = lane_block((columns, LANES), depth)
    tiles = []
    for tile in range(depth * depth // LANES):
        pieces = [
            turn_ref[pl.ds(tile * residues + e, columns, stride=depth), :]
            for e in range(residues)
        ]
        rows = jnp.concatenate(pieces, axis=0)
        turned = [rows] + [pltpu.roll(rows, depth * t, 1) for t in range(1, residues)]
        tiles.append(
            jnp.concatenate(
                [
                    pick(
                        blocks,
                        [
                            turned[(e - i) % residues][e * columns : (e + 1) * columns]
                            for e in range(residues)
                        ],
                    )
                    for i in range(residues)
                ],
                axis=0,
            )
        )
    flat = jnp.concatenate(tiles, axis=1)
    rows = residues * columns
    parts = jnp.concatenate(split_three(flat), axis=0)
    pair = jnp.dot(parts, sorted_w_ref[...], preferred_element_type=F32)
    pair = pair[0:rows] + (pair[rows : 2 * rows] + pair[2 * rows : 3 * rows])
    pair_ref[...] = (pair + offset_ref[...]).astype(BF16).reshape(pair_ref.shape)


def wide_slice(
    homolog_matrix,
    standardizer_scaling,
    standardizer_offset,
    left_projection_matrix,
    left_offset_vector,
    right_projection_matrix,
    right_offset_vector,
    coupling_matrix,
    coupling_offset,
    coupling_cotangent,
):
    seqs, residues, features = homolog_matrix.shape
    depth = left_projection_matrix.shape[1]
    ranks = lax.axis_size("res")
    scale = 1.0 / (seqs * lax.axis_size("seq"))
    half_ranks = ranks // 2
    half_columns = half_ranks * residues
    step_ranks = 4
    columns = step_ranks * residues
    steps = half_ranks // step_ranks
    mine = lax.axis_index("seq")
    swap = [(0, 1), (1, 0)]

    other_cot = lax.ppermute(coupling_cotangent, "seq", swap)
    gain = standardizer_scaling.reshape(1, -1)
    left_w = left_projection_matrix.T
    right_w = right_projection_matrix.T

    left, right, sorted_w = pl.pallas_call(
        project_kernel,
        out_shape=(
            jax.ShapeDtypeStruct((seqs, LANES), BF16),
            jax.ShapeDtypeStruct((seqs, LANES), BF16),
            jax.ShapeDtypeStruct(coupling_matrix.shape, BF16),
        ),
        scratch_shapes=[pltpu.VMEM(coupling_matrix.shape, F32)],
        name="project",
    )(
        homolog_matrix,
        gain,
        standardizer_offset.reshape(1, -1),
        left_w,
        left_offset_vector.reshape(1, -1),
        right_w,
        right_offset_vector.reshape(1, -1),
        coupling_matrix,
    )

    whole = lambda shape: pl.BlockSpec(shape, lambda g: (0,) * len(shape))
    cot_block = pl.BlockSpec((residues, columns, LANES), lambda g: (0, g, 0))
    outer_block = pl.BlockSpec((2, columns * depth, LANES), lambda g: (0, g, 0))
    send_block = pl.BlockSpec((2, step_ranks, 2 * seqs, LANES), lambda g: (0, g, 0, 0))
    send, outer = pl.pallas_call(
        functools.partial(cot_kernel, scale),
        grid=(steps,),
        in_specs=[
            cot_block,
            cot_block,
            whole(sorted_w.shape),
            whole(left.shape),
            whole(right.shape),
        ],
        out_specs=(send_block, outer_block),
        out_shape=(
            jax.ShapeDtypeStruct((2, half_ranks, 2 * seqs, LANES), BF16),
            jax.ShapeDtypeStruct((2, half_columns * depth, LANES), BF16),
        ),
        scratch_shapes=[pltpu.VMEM((2 * columns * depth, LANES), F32)],
        name="cotangent",
    )(coupling_cotangent, other_cot, sorted_w, left, right)

    got = lax.all_to_all(
        send.reshape(ranks, 2 * seqs, LANES), "res", split_axis=0, concat_axis=0, tiled=True
    ).reshape(send.shape)

    leaving = lax.dynamic_index_in_dim(got, 1 - mine, 0, keepdims=False)[:, 0:seqs, :]
    far = lax.ppermute(jnp.concatenate([leaving, left[None]], axis=0), "seq", swap)

    gradient = pl.pallas_call(
        functools.partial(grad_kernel, steps),
        grid=(steps,),
        in_specs=[
            send_block,
            outer_block,
            whole(homolog_matrix.shape),
            whole(gain.shape),
            whole(left_w.shape),
            whole(right_w.shape),
        ],
        out_specs=whole(homolog_matrix.shape),
        out_shape=jax.ShapeDtypeStruct(homolog_matrix.shape, BF16),
        scratch_shapes=[pltpu.VMEM((seqs, LANES), F32)] * 2,
        name="gradient",
    )(got, outer, homolog_matrix, gain, left_w, right_w)

    pair_delta = pl.pallas_call(
        functools.partial(pair_kernel, scale),
        grid=(steps,),
        in_specs=[
            pl.BlockSpec((2, step_ranks, seqs, LANES), lambda g: (0, g, 0, 0)),
            pl.BlockSpec((step_ranks, seqs, LANES), lambda g: (g, 0, 0)),
            whole(left.shape),
            pl.BlockSpec((None, seqs, LANES), lambda g: (half_ranks, 0, 0)),
            whole(sorted_w.shape),
            whole((1, LANES)),
        ],
        out_specs=cot_block,
        out_shape=jax.ShapeDtypeStruct(coupling_cotangent.shape, BF16),
        scratch_shapes=[pltpu.VMEM((columns * depth, LANES), F32)],
        name="pair",
    )(got, far, left, far, sorted_w, coupling_offset.reshape(1, -1))
    return (pair_delta, gradient)


def fetch(source, target, semaphore):
    copy = pltpu.make_async_copy(source, target, semaphore)
    copy.start()
    return copy


def small_project_kernel(
    x_hbm, gain_hbm, offset_hbm, left_w_hbm, left_b_hbm, right_w_hbm, right_b_hbm, w_hbm, pair_offset_hbm,
    left_ref, right_ref, sorted_w_ref, normed_ref, inv_std_ref, spread_w_ref, gain_out_ref,
    pair_offset_out_ref,
    x_ref, offset_ref, left_w_ref, left_b_ref, right_w_ref, right_b_ref, raw_ref, wide_ref, semaphores,
):
    copies = [
        pltpu.make_async_copy(source, target, semaphores.at[place])
        for place, (source, target) in enumerate(
            (
                (x_hbm, x_ref),
                (gain_hbm, gain_out_ref),
                (offset_hbm, offset_ref),
                (left_w_hbm, left_w_ref),
                (left_b_hbm, left_b_ref),
                (right_w_hbm, right_w_ref),
                (right_b_hbm, right_b_ref),
                (w_hbm, raw_ref),
                (pair_offset_hbm, pair_offset_out_ref),
            )
        )
    ]
    for copy in copies:
        copy.start()
    seqs, residues, _ = x_ref.shape
    depth = left_w_ref.shape[0]
    copies[0].wait()
    normed, inv_std = normalise(residue_rows(x_ref))
    normed_ref[...] = normed
    inv_std_ref[...] = jnp.broadcast_to(inv_std, inv_std_ref.shape)
    for copy in copies[1:7]:
        copy.wait()
    ln_out = (normed * gain_out_ref[...] + offset_ref[...]).astype(BF16)
    blocks = lane_block((seqs, LANES), depth)
    spread = []
    for weight_ref, bias_ref, out_ref in (
        (left_w_ref, left_b_ref, left_ref),
        (right_w_ref, right_b_ref, right_ref),
    ):
        weight = jnp.concatenate([weight_ref[...]] * residues, axis=0)
        spread.append(weight)
        bias = jnp.concatenate([bias_ref[...]] * residues, axis=1)
        wide = lax.dot_general(ln_out, weight, NT, preferred_element_type=F32)
        own = pick(blocks, [wide[p * seqs : (p + 1) * seqs] for p in range(residues)])
        out_ref[...] = (own + bias).astype(BF16)
    spread_w_ref[...] = jnp.concatenate(spread, axis=0)
    for copy in copies[7:]:
        copy.wait()
    wide_ref[...] = raw_ref[...].astype(F32)
    for d in range(depth):
        sorted_w_ref[d * depth : (d + 1) * depth, :] = wide_ref[
            pl.ds(d, depth, stride=depth), :
        ].astype(BF16)


def small_cot_kernel(scale, own_ref, other_ref, sorted_w_ref, left_ref, right_ref,
                    send_ref, keep_ref, outer_ref, turn_ref):
    residues, columns, _ = own_ref.shape
    depth = LANES // residues
    first = lax.axis_index("seq") == 0
    own = own_ref[...].reshape(residues * columns, LANES)
    other = other_ref[...].reshape(residues * columns, LANES)
    both = jnp.concatenate([jnp.where(first, own, other), jnp.where(first, other, own)], axis=0)
    flat = lax.dot_general(both, sorted_w_ref[...], NT, preferred_element_type=F32) * scale
    blocks = lane_block((columns, LANES), depth)
    for half in range(2):
        for tile in range(depth * depth // LANES):
            block = flat[
                half * residues * columns : (half + 1) * residues * columns,
                tile * LANES : (tile + 1) * LANES,
            ]
            turned = [block] + [pltpu.roll(block, depth * t, 1) for t in range(1, residues)]
            for e in range(residues):
                start = half * columns * depth + tile * residues + e
                turn_ref[pl.ds(start, columns, stride=depth), :] = pick(
                    blocks,
                    [
                        turned[(i - e) % residues][i * columns : (i + 1) * columns]
                        for i in range(residues)
                    ],
                )
    outer = turn_ref[...].astype(BF16)
    outer_ref[...] = outer
    partial = lax.dot_general(left_ref[...], outer, NT, preferred_element_type=F32)
    rank = lax.axis_index("res")
    send_ref[0] = right_ref[...]
    for place in range(2 * columns // residues):
        piece = partial[:, place * LANES : (place + 1) * LANES]
        distance = lax.bitwise_xor(rank, place)
        spot = distance & 3

        @pl.when(distance >= 4)
        def _():
            send_ref[spot + 1] = piece.astype(BF16)

        @pl.when(distance < 4)
        def _():
            keep_ref[spot] = piece


def small_grad_kernel(right_ref, outer_ref, keep_ref, far_ref, near_refs, normed_ref, inv_std_ref,
                      gain_ref, spread_w_ref, grad_ref):
    ranks, seqs, _ = right_ref.shape
    residues = grad_ref.shape[1]
    depth = LANES // residues
    rank = lax.axis_index("res")
    right_all = jnp.concatenate(
        [right_ref[lax.bitwise_xor(rank, place)] for place in range(ranks)], axis=1
    )
    left_cot = jnp.dot(right_all, outer_ref[...], preferred_element_type=F32)
    right_cot = keep_ref[0] + far_ref[1].astype(F32)
    for near_ref in near_refs:
        right_cot = right_cot + near_ref[2].astype(F32)
    blocks = lane_block((seqs, LANES), depth)
    spread = jnp.concatenate(
        [
            jnp.concatenate(
                [jnp.where(blocks == place, cot, 0.0) for cot in (left_cot, right_cot)], axis=1
            )
            for place in range(residues)
        ],
        axis=0,
    )
    rows = residues * seqs
    parts = jnp.concatenate(split_three(spread), axis=0)
    ln_cot = jnp.dot(parts, spread_w_ref[...], preferred_element_type=F32)
    ln_cot = ln_cot[0:rows] + (ln_cot[rows : 2 * rows] + ln_cot[2 * rows : 3 * rows])
    gained = ln_cot * gain_ref[...]
    normed = normed_ref[...]
    grad = inv_std_ref[:, 0:1] * (
        gained
        - jnp.mean(gained, axis=-1, keepdims=True)
        - normed * jnp.mean(gained * normed, axis=-1, keepdims=True)
    )
    for place in range(residues):
        grad_ref[:, place, :] = grad[place * seqs : (place + 1) * seqs].astype(BF16)


def small_pair_kernel(scale, right_ref, far_ref, left_ref, sorted_w_ref, offset_ref,
                     pair_ref, turn_ref):
    residues, columns, _ = pair_ref.shape
    depth = LANES // residues
    ranks = columns // residues
    rank = lax.axis_index("res")
    base = lax.axis_index("seq") * ranks
    near, far = [], []
    for place in range(ranks):
        distance = lax.bitwise_xor(rank, base + place)
        near.append(right_ref[distance])
        far.append(far_ref[distance & (ranks - 1)])
    right = jnp.concatenate(
        [jnp.concatenate(near, axis=1), jnp.concatenate(far, axis=1)], axis=0
    )
    left = jnp.concatenate([left_ref[...], far_ref[ranks]], axis=0)
    turn_ref[...] = lax.dot_general(right, left, TN, preferred_element_type=F32) * scale
    blocks = lane_block((columns, LANES), depth)
    tiles = []
    for tile in range(depth * depth // LANES):
        pieces = [
            turn_ref[pl.ds(tile * residues + e, columns, stride=depth), :]
            for e in range(residues)
        ]
        rows = jnp.concatenate(pieces, axis=0)
        turned = [rows] + [pltpu.roll(rows, depth * t, 1) for t in range(1, residues)]
        tiles.append(
            jnp.concatenate(
                [
                    pick(
                        blocks,
                        [
                            turned[(e - i) % residues][e * columns : (e + 1) * columns]
                            for e in range(residues)
                        ],
                    )
                    for i in range(residues)
                ],
                axis=0,
            )
        )
    flat = jnp.concatenate(tiles, axis=1)
    rows = residues * columns
    parts = jnp.concatenate(split_three(flat), axis=0)
    pair = jnp.dot(parts, sorted_w_ref[...], preferred_element_type=F32)
    pair = pair[0:rows] + (pair[rows : 2 * rows] + pair[2 * rows : 3 * rows])
    pair_ref[...] = (pair + offset_ref[...]).astype(BF16).reshape(pair_ref.shape)


def small_slice(
    homolog_matrix,
    standardizer_scaling,
    standardizer_offset,
    left_projection_matrix,
    left_offset_vector,
    right_projection_matrix,
    right_offset_vector,
    coupling_matrix,
    coupling_offset,
    coupling_cotangent,
):
    seqs, residues, features = homolog_matrix.shape
    depth = left_projection_matrix.shape[1]
    ranks = lax.axis_size("res")
    rows = seqs * residues
    scale = 1.0 / (seqs * lax.axis_size("seq"))
    rank = lax.axis_index("res")
    mine = lax.axis_index("seq")
    swap = [(0, 1), (1, 0)]
    limit = pltpu.CompilerParams(vmem_limit_bytes=8 * 1024 * 1024)
    vmem = pl.BlockSpec(memory_space=pltpu.VMEM)
    like = jax.ShapeDtypeStruct

    other_cot = lax.ppermute(coupling_cotangent, "seq", swap)
    left, right, sorted_w, normed, inv_std, spread_w, gain, pair_offset = pl.pallas_call(
        small_project_kernel,
        in_specs=[pl.BlockSpec(memory_space=pltpu.HBM)] * 9,
        out_specs=[vmem] * 8,
        out_shape=(
            like((seqs, LANES), BF16),
            like((seqs, LANES), BF16),
            like(coupling_matrix.shape, BF16),
            like((rows, features), F32),
            like((rows, LANES), F32),
            like((2 * LANES, features), BF16),
            like((1, features), F32),
            like((1, LANES), F32),
        ),
        scratch_shapes=[
            pltpu.VMEM(homolog_matrix.shape, BF16),
            pltpu.VMEM((1, features), F32),
            pltpu.VMEM((depth, features), BF16),
            pltpu.VMEM((1, depth), F32),
            pltpu.VMEM((depth, features), BF16),
            pltpu.VMEM((1, depth), F32),
            pltpu.VMEM(coupling_matrix.shape, BF16),
            pltpu.VMEM(coupling_matrix.shape, F32),
            pltpu.SemaphoreType.DMA((9,)),
        ],
        compiler_params=limit,
        name="project",
    )(
        *[
            pltpu.with_memory_space_constraint(array, pltpu.HBM)
            for array in (
                homolog_matrix,
                standardizer_scaling.reshape(1, -1),
                standardizer_offset.reshape(1, -1),
                left_projection_matrix.T,
                left_offset_vector.reshape(1, -1),
                right_projection_matrix.T,
                right_offset_vector.reshape(1, -1),
                coupling_matrix,
                coupling_offset.reshape(1, -1),
            )
        ]
    )

    send, keep, outer = pl.pallas_call(
        functools.partial(small_cot_kernel, scale),
        in_specs=[vmem] * 5,
        out_specs=[vmem] * 3,
        out_shape=(
            like((1 + ranks // 2, seqs, LANES), BF16),
            like((ranks // 2, seqs, LANES), F32),
            like((ranks * LANES, LANES), BF16),
        ),
        scratch_shapes=[pltpu.VMEM((ranks * LANES, LANES), F32)],
        compiler_params=limit,
        name="cotangent",
    )(coupling_cotangent, other_cot, sorted_w, left, right)

    def swap_over(mask, value):
        return lax.ppermute(value, "res", [(source, source ^ mask) for source in range(ranks)])

    own = right[None]
    beyond_two = swap_over(4, send)
    both = jnp.concatenate([own, beyond_two[0:1]])
    near_parts = {}
    gathered = jnp.concatenate(
        [own, jnp.zeros((3, seqs, LANES), BF16), beyond_two[0:1], jnp.zeros((3, seqs, LANES), BF16)]
    )
    for mask in (3, 2, 1):
        summed = (keep[mask] + beyond_two[1 + mask].astype(F32)).astype(BF16)
        part = swap_over(mask, jnp.concatenate([both, summed[None]]))
        near_parts[mask] = part
        gathered = lax.dynamic_update_slice_in_dim(gathered, part[0:1], mask, 0)
        gathered = lax.dynamic_update_slice_in_dim(gathered, part[1:2], 4 + mask, 0)
    near_parts = [near_parts[mask] for mask in (1, 2, 3)]

    half = gathered.reshape(2, ranks // 2, seqs, LANES)
    beyond = 1 - lax.bitwise_xor(lax.shift_right_logical(rank, 2), mine)
    leaving = lax.dynamic_index_in_dim(half, beyond, 0, keepdims=False)
    far = lax.ppermute(jnp.concatenate([leaving, left[None]]), "seq", swap)

    gradient = pl.pallas_call(
        small_grad_kernel,
        in_specs=[vmem] * 4 + [[vmem] * 3] + [vmem] * 4,
        out_specs=vmem,
        out_shape=like(homolog_matrix.shape, BF16),
        compiler_params=limit,
        name="gradient",
    )(gathered, outer, keep, beyond_two, near_parts, normed, inv_std, gain, spread_w)

    pair_delta = pl.pallas_call(
        functools.partial(small_pair_kernel, scale),
        in_specs=[vmem] * 5,
        out_specs=vmem,
        out_shape=like(coupling_cotangent.shape, BF16),
        scratch_shapes=[pltpu.VMEM((ranks // 2 * LANES, LANES), F32)],
        compiler_params=limit,
        name="pair",
    )(gathered, far, left, sorted_w, pair_offset)
    return (pair_delta, gradient)


def body(*arrays):
    if lax.axis_size("res") == 8:
        return small_slice(*arrays)
    return wide_slice(*arrays)


def solution(mesh):
    return jax.shard_map(
        body,
        mesh=mesh,
        in_specs=(
            P(("grp", "seq"), "res", None),
            P(),
            P(),
            P(),
            P(),
            P(),
            P(),
            P(),
            P(),
            P(("grp", "res"), "seq", None),
        ),
        out_specs=(P(("grp", "res"), "seq", None), P(("grp", "seq"), "res", None)),
        check_vma=False,
    )
```

```python
import functools

import jax
import jax.numpy as jnp
from jax import lax
from jax.experimental import pallas as pl
from jax.experimental.pallas import tpu as pltpu
from jax.sharding import PartitionSpec as P

LANES = 128
BF16 = jnp.bfloat16
F32 = jnp.float32
NT = (((1,), (1,)), ((), ()))
TN = (((0,), (0,)), ((), ()))


def lane_block(shape, width):
    return lax.broadcasted_iota(jnp.int32, shape, 1) // width


def pick(blocks, pieces):
    result = pieces[0]
    for place in range(1, len(pieces)):
        result = jnp.where(blocks == place, pieces[place], result)
    return result


def split_three(value):
    top = value.astype(BF16)
    rest = value - top.astype(F32)
    middle = rest.astype(BF16)
    low = (rest - middle.astype(F32)).astype(BF16)
    return top, middle, low


def normalise(rows):
    centred = rows - jnp.mean(rows, axis=-1, keepdims=True)
    inv_std = lax.rsqrt(jnp.mean(centred * centred, axis=-1, keepdims=True) + 1e-05)
    return centred * inv_std, inv_std


def residue_rows(x_ref):
    return jnp.concatenate(
        [x_ref[:, place, :].astype(F32) for place in range(x_ref.shape[1])], axis=0
    )


def project_kernel(
    x_ref, gain_ref, offset_ref, left_w_ref, left_b_ref, right_w_ref, right_b_ref, w_ref,
    left_ref, right_ref, sorted_w_ref, wide_ref,
):
    seqs, residues, _ = x_ref.shape
    depth = left_w_ref.shape[0]
    normed, _ = normalise(residue_rows(x_ref))
    ln_out = (normed * gain_ref[...] + offset_ref[...]).astype(BF16)
    blocks = lane_block((seqs, LANES), depth)
    for weight_ref, bias_ref, out_ref in (
        (left_w_ref, left_b_ref, left_ref),
        (right_w_ref, right_b_ref, right_ref),
    ):
        weight = jnp.concatenate([weight_ref[...]] * residues, axis=0)
        bias = jnp.concatenate([bias_ref[...]] * residues, axis=1)
        wide = lax.dot_general(ln_out, weight, NT, preferred_element_type=F32)
        own = pick(blocks, [wide[p * seqs : (p + 1) * seqs] for p in range(residues)])
        out_ref[...] = (own + bias).astype(BF16)
    wide_ref[...] = w_ref[...].astype(F32)
    for d in range(depth):
        sorted_w_ref[d * depth : (d + 1) * depth, :] = wide_ref[
            pl.ds(d, depth, stride=depth), :
        ].astype(BF16)


def cot_kernel(scale, own_ref, other_ref, sorted_w_ref, left_ref, right_ref,
               send_ref, outer_ref, turn_ref):
    residues, columns, _ = own_ref.shape
    depth = sorted_w_ref.shape[0] // (LANES // residues)
    depth = LANES // residues
    first = lax.axis_index("seq") == 0
    own = own_ref[...].reshape(residues * columns, LANES)
    other = other_ref[...].reshape(residues * columns, LANES)
    low = jnp.where(first, own, other)
    high = jnp.where(first, other, own)
    both = jnp.concatenate([low, high], axis=0)
    flat = lax.dot_general(both, sorted_w_ref[...], NT, preferred_element_type=F32) * scale
    blocks = lane_block((columns, LANES), depth)
    for half in range(2):
        for tile in range(depth * depth // LANES):
            block = flat[
                half * residues * columns : (half + 1) * residues * columns,
                tile * LANES : (tile + 1) * LANES,
            ]
            turned = [block] + [pltpu.roll(block, depth * t, 1) for t in range(1, residues)]
            for e in range(residues):
                piece = pick(
                    blocks,
                    [
                        turned[(i - e) % residues][i * columns : (i + 1) * columns]
                        for i in range(residues)
                    ],
                )
                turn_ref[pl.ds(half * columns * depth + tile * residues + e, columns, stride=depth), :] = piece
    outer = turn_ref[...].astype(BF16)
    half_rows = columns * depth
    partial = lax.dot_general(left_ref[...], outer, NT, preferred_element_type=F32).astype(BF16)
    seqs = left_ref.shape[0]
    ranks = columns // residues
    for half in range(2):
        outer_ref[half] = outer[half * half_rows : (half + 1) * half_rows]
        for rank in range(ranks):
            at = (half * ranks + rank) * LANES
            send_ref[half, rank, 0:seqs, :] = right_ref[...]
            send_ref[half, rank, seqs : 2 * seqs, :] = partial[:, at : at + LANES]


def grad_kernel(steps, got_ref, outer_ref, x_ref, gain_ref, left_w_ref, right_w_ref,
                grad_ref, left_cot_ref, right_cot_ref):
    step = pl.program_id(0)
    _, ranks, twice, _ = got_ref.shape
    seqs = twice // 2
    residues = x_ref.shape[1]
    depth = LANES // residues

    @pl.when(step == 0)
    def _():
        left_cot_ref[...] = jnp.zeros_like(left_cot_ref)
        right_cot_ref[...] = jnp.zeros_like(right_cot_ref)

    places = [(half, rank) for half in range(2) for rank in range(ranks)]
    right_all = jnp.concatenate([got_ref[h, r, 0:seqs, :] for h, r in places], axis=1)
    outer = jnp.concatenate([outer_ref[0], outer_ref[1]], axis=0)
    left_cot_ref[...] += jnp.dot(right_all, outer, preferred_element_type=F32)
    total = got_ref[0, 0, seqs:twice, :].astype(F32)
    for h, r in places[1:]:
        total = total + got_ref[h, r, seqs:twice, :].astype(F32)
    right_cot_ref[...] += total

    @pl.when(step == steps - 1)
    def _():
        blocks = lane_block((seqs, LANES), depth)
        left_cot, right_cot = left_cot_ref[...], right_cot_ref[...]
        spread = jnp.concatenate(
            [
                jnp.concatenate(
                    [
                        jnp.where(blocks == place, left_cot, 0.0),
                        jnp.where(blocks == place, right_cot, 0.0),
                    ],
                    axis=1,
                )
                for place in range(residues)
            ],
            axis=0,
        )
        weight = jnp.concatenate(
            [left_w_ref[...]] * residues + [right_w_ref[...]] * residues, axis=0
        )
        rows = residues * seqs
        parts = jnp.concatenate(split_three(spread), axis=0)
        ln_cot = jnp.dot(parts, weight, preferred_element_type=F32)
        ln_cot = ln_cot[0:rows] + (ln_cot[rows : 2 * rows] + ln_cot[2 * rows : 3 * rows])
        gained = ln_cot * gain_ref[...]
        normed, inv_std = normalise(residue_rows(x_ref))
        grad = inv_std * (
            gained
            - jnp.mean(gained, axis=-1, keepdims=True)
            - normed * jnp.mean(gained * normed, axis=-1, keepdims=True)
        )
        for place in range(residues):
            grad_ref[:, place, :] = grad[place * seqs : (place + 1) * seqs].astype(BF16)


def pair_kernel(scale, got_ref, far_ref, left_ref, far_left_ref, sorted_w_ref, offset_ref,
                pair_ref, turn_ref):
    residues, columns, _ = pair_ref.shape
    depth = LANES // residues
    ranks = columns // residues
    mine = lax.axis_index("seq")
    near = jnp.concatenate([got_ref[mine, r] for r in range(ranks)], axis=1)
    far = jnp.concatenate([far_ref[r] for r in range(ranks)], axis=1)
    right = jnp.concatenate([near, far], axis=0)
    left = jnp.concatenate([left_ref[...], far_left_ref[...]], axis=0)
    turn_ref[...] = lax.dot_general(right, left, TN, preferred_element_type=F32) * scale
    blocks = lane_block((columns, LANES), depth)
    tiles = []
    for tile in range(depth * depth // LANES):
        pieces = [
            turn_ref[pl.ds(tile * residues + e, columns, stride=depth), :]
            for e in range(residues)
        ]
        rows = jnp.concatenate(pieces, axis=0)
        turned = [rows] + [pltpu.roll(rows, depth * t, 1) for t in range(1, residues)]
        tiles.append(
            jnp.concatenate(
                [
                    pick(
                        blocks,
                        [
                            turned[(e - i) % residues][e * columns : (e + 1) * columns]
                            for e in range(residues)
                        ],
                    )
                    for i in range(residues)
                ],
                axis=0,
            )
        )
    flat = jnp.concatenate(tiles, axis=1)
    rows = residues * columns
    parts = jnp.concatenate(split_three(flat), axis=0)
    pair = jnp.dot(parts, sorted_w_ref[...], preferred_element_type=F32)
    pair = pair[0:rows] + (pair[rows : 2 * rows] + pair[2 * rows : 3 * rows])
    pair_ref[...] = (pair + offset_ref[...]).astype(BF16).reshape(pair_ref.shape)


def wide_slice(
    homolog_matrix,
    standardizer_scaling,
    standardizer_offset,
    left_projection_matrix,
    left_offset_vector,
    right_projection_matrix,
    right_offset_vector,
    coupling_matrix,
    coupling_offset,
    coupling_cotangent,
):
    seqs, residues, features = homolog_matrix.shape
    depth = left_projection_matrix.shape[1]
    ranks = lax.axis_size("res")
    scale = 1.0 / (seqs * lax.axis_size("seq"))
    half_ranks = ranks // 2
    half_columns = half_ranks * residues
    step_ranks = 4
    columns = step_ranks * residues
    steps = half_ranks // step_ranks
    mine = lax.axis_index("seq")
    swap = [(0, 1), (1, 0)]

    other_cot = lax.ppermute(coupling_cotangent, "seq", swap)
    gain = standardizer_scaling.reshape(1, -1)
    left_w = left_projection_matrix.T
    right_w = right_projection_matrix.T

    left, right, sorted_w = pl.pallas_call(
        project_kernel,
        out_shape=(
            jax.ShapeDtypeStruct((seqs, LANES), BF16),
            jax.ShapeDtypeStruct((seqs, LANES), BF16),
            jax.ShapeDtypeStruct(coupling_matrix.shape, BF16),
        ),
        scratch_shapes=[pltpu.VMEM(coupling_matrix.shape, F32)],
        name="project",
    )(
        homolog_matrix,
        gain,
        standardizer_offset.reshape(1, -1),
        left_w,
        left_offset_vector.reshape(1, -1),
        right_w,
        right_offset_vector.reshape(1, -1),
        coupling_matrix,
    )

    whole = lambda shape: pl.BlockSpec(shape, lambda g: (0,) * len(shape))
    cot_block = pl.BlockSpec((residues, columns, LANES), lambda g: (0, g, 0))
    outer_block = pl.BlockSpec((2, columns * depth, LANES), lambda g: (0, g, 0))
    send_block = pl.BlockSpec((2, step_ranks, 2 * seqs, LANES), lambda g: (0, g, 0, 0))
    send, outer = pl.pallas_call(
        functools.partial(cot_kernel, scale),
        grid=(steps,),
        in_specs=[
            cot_block,
            cot_block,
            whole(sorted_w.shape),
            whole(left.shape),
            whole(right.shape),
        ],
        out_specs=(send_block, outer_block),
        out_shape=(
            jax.ShapeDtypeStruct((2, half_ranks, 2 * seqs, LANES), BF16),
            jax.ShapeDtypeStruct((2, half_columns * depth, LANES), BF16),
        ),
        scratch_shapes=[pltpu.VMEM((2 * columns * depth, LANES), F32)],
        name="cotangent",
    )(coupling_cotangent, other_cot, sorted_w, left, right)

    got = lax.all_to_all(
        send.reshape(ranks, 2 * seqs, LANES), "res", split_axis=0, concat_axis=0, tiled=True
    ).reshape(send.shape)

    leaving = lax.dynamic_index_in_dim(got, 1 - mine, 0, keepdims=False)[:, 0:seqs, :]
    far = lax.ppermute(jnp.concatenate([leaving, left[None]], axis=0), "seq", swap)

    gradient = pl.pallas_call(
        functools.partial(grad_kernel, steps),
        grid=(steps,),
        in_specs=[
            send_block,
            outer_block,
            whole(homolog_matrix.shape),
            whole(gain.shape),
            whole(left_w.shape),
            whole(right_w.shape),
        ],
        out_specs=whole(homolog_matrix.shape),
        out_shape=jax.ShapeDtypeStruct(homolog_matrix.shape, BF16),
        scratch_shapes=[pltpu.VMEM((seqs, LANES), F32)] * 2,
        name="gradient",
    )(got, outer, homolog_matrix, gain, left_w, right_w)

    pair_delta = pl.pallas_call(
        functools.partial(pair_kernel, scale),
        grid=(steps,),
        in_specs=[
            pl.BlockSpec((2, step_ranks, seqs, LANES), lambda g: (0, g, 0, 0)),
            pl.BlockSpec((step_ranks, seqs, LANES), lambda g: (g, 0, 0)),
            whole(left.shape),
            pl.BlockSpec((None, seqs, LANES), lambda g: (half_ranks, 0, 0)),
            whole(sorted_w.shape),
            whole((1, LANES)),
        ],
        out_specs=cot_block,
        out_shape=jax.ShapeDtypeStruct(coupling_cotangent.shape, BF16),
        scratch_shapes=[pltpu.VMEM((columns * depth, LANES), F32)],
        name="pair",
    )(got, far, left, far, sorted_w, coupling_offset.reshape(1, -1))
    return (pair_delta, gradient)


def fetch(source, target, semaphore):
    copy = pltpu.make_async_copy(source, target, semaphore)
    copy.start()
    return copy


def start_copies(pairs, semaphores):
    copies = [
        pltpu.make_async_copy(source, target, semaphores.at[place])
        for place, (source, target) in enumerate(pairs)
    ]
    for copy in copies:
        copy.start()
    return copies


def small_project_kernel(
    x_hbm, gain_hbm, offset_hbm, left_w_hbm, left_b_hbm, right_w_hbm, right_b_hbm, w_hbm,
    left_ref, right_ref, sorted_w_ref,
    x_ref, gain_ref, offset_ref, left_w_ref, left_b_ref, right_w_ref, right_b_ref, raw_ref, wide_ref,
    semaphores,
):
    copies = start_copies(
        (
            (x_hbm, x_ref),
            (gain_hbm, gain_ref),
            (offset_hbm, offset_ref),
            (left_w_hbm, left_w_ref),
            (left_b_hbm, left_b_ref),
            (right_w_hbm, right_w_ref),
            (right_b_hbm, right_b_ref),
            (w_hbm, raw_ref),
        ),
        semaphores,
    )
    seqs, residues, _ = x_ref.shape
    depth = left_w_ref.shape[0]
    copies[0].wait()
    normed, _ = normalise(residue_rows(x_ref))
    for copy in copies[1:7]:
        copy.wait()
    ln_out = (normed * gain_ref[...] + offset_ref[...]).astype(BF16)
    blocks = lane_block((seqs, LANES), depth)
    for weight_ref, bias_ref, out_ref in (
        (left_w_ref, left_b_ref, left_ref),
        (right_w_ref, right_b_ref, right_ref),
    ):
        weight = jnp.concatenate([weight_ref[...]] * residues, axis=0)
        bias = jnp.concatenate([bias_ref[...]] * residues, axis=1)
        wide = lax.dot_general(ln_out, weight, NT, preferred_element_type=F32)
        own = pick(blocks, [wide[p * seqs : (p + 1) * seqs] for p in range(residues)])
        out_ref[...] = (own + bias).astype(BF16)
    copies[7].wait()
    wide_ref[...] = raw_ref[...].astype(F32)
    for d in range(depth):
        sorted_w_ref[d * depth : (d + 1) * depth, :] = wide_ref[
            pl.ds(d, depth, stride=depth), :
        ].astype(BF16)


def half_pieces(scale, half, own_ref, other_ref, sorted_w_ref, left_ref, turn_ref):
    residues, columns, _ = own_ref.shape
    depth = LANES // residues
    own = own_ref[...].reshape(residues * columns, LANES)
    other = other_ref[...].reshape(residues * columns, LANES)
    cot = jnp.where(lax.axis_index("seq") == half, own, other)
    flat = lax.dot_general(cot, sorted_w_ref[...], NT, preferred_element_type=F32) * scale
    blocks = lane_block((columns, LANES), depth)
    for tile in range(depth * depth // LANES):
        block = flat[:, tile * LANES : (tile + 1) * LANES]
        turned = [block] + [pltpu.roll(block, depth * t, 1) for t in range(1, residues)]
        for e in range(residues):
            turn_ref[pl.ds(tile * residues + e, columns, stride=depth), :] = pick(
                blocks,
                [
                    turned[(i - e) % residues][i * columns : (i + 1) * columns]
                    for i in range(residues)
                ],
            )
    outer = turn_ref[...].astype(BF16)
    partial = lax.dot_general(left_ref[...], outer, NT, preferred_element_type=F32)
    return outer, [
        partial[:, place * LANES : (place + 1) * LANES] for place in range(columns // residues)
    ]


def small_far_kernel(scale, own_ref, other_ref, sorted_w_ref, left_ref, right_ref,
                     send_ref, outer_ref, turn_ref):
    rank = lax.axis_index("res")
    half = 1 - lax.shift_right_logical(rank, 2)
    outer, pieces = half_pieces(scale, half, own_ref, other_ref, sorted_w_ref, left_ref, turn_ref)
    outer_ref[...] = outer
    send_ref[0] = right_ref[...]
    for place, piece in enumerate(pieces):
        send_ref[1 + lax.bitwise_xor(rank & 3, place)] = piece.astype(BF16)


def small_near_kernel(
    scale, x_hbm, gain_hbm, left_w_hbm, right_w_hbm, pair_offset_hbm,
    own_ref, other_ref, sorted_w_ref, left_ref,
    keep_ref, outer_ref, normed_ref, inv_std_ref, spread_w_ref, gain_ref, pair_offset_ref,
    x_ref, left_w_ref, right_w_ref, turn_ref, semaphores,
):
    copies = start_copies(
        (
            (x_hbm, x_ref),
            (gain_hbm, gain_ref),
            (left_w_hbm, left_w_ref),
            (right_w_hbm, right_w_ref),
            (pair_offset_hbm, pair_offset_ref),
        ),
        semaphores,
    )
    residues = x_ref.shape[1]
    rank = lax.axis_index("res")
    half = lax.shift_right_logical(rank, 2)
    outer, pieces = half_pieces(scale, half, own_ref, other_ref, sorted_w_ref, left_ref, turn_ref)
    outer_ref[...] = outer
    for place, piece in enumerate(pieces):
        keep_ref[lax.bitwise_xor(rank & 3, place)] = piece
    for copy in copies:
        copy.wait()
    normed, inv_std = normalise(residue_rows(x_ref))
    normed_ref[...] = normed
    inv_std_ref[...] = jnp.broadcast_to(inv_std, inv_std_ref.shape)
    spread_w_ref[...] = jnp.concatenate(
        [left_w_ref[...]] * residues + [right_w_ref[...]] * residues, axis=0
    )


def small_grad_kernel(right_ref, outer_near_ref, outer_far_ref, keep_ref, far_ref, near_refs, normed_ref, inv_std_ref,
                      gain_ref, spread_w_ref, grad_ref):
    ranks, seqs, _ = right_ref.shape
    residues = grad_ref.shape[1]
    depth = LANES // residues
    rank = lax.axis_index("res")
    places = [lax.bitwise_xor(rank & 3, place) for place in range(ranks // 2)]
    right_all = jnp.concatenate(
        [right_ref[place] for place in places] + [right_ref[4 + place] for place in places], axis=1
    )
    outer = jnp.concatenate([outer_near_ref[...], outer_far_ref[...]], axis=0)
    left_cot = jnp.dot(right_all, outer, preferred_element_type=F32)
    right_cot = keep_ref[0] + far_ref[1].astype(F32)
    for near_ref in near_refs:
        right_cot = right_cot + near_ref[2].astype(F32)
    blocks = lane_block((seqs, LANES), depth)
    spread = jnp.concatenate(
        [
            jnp.concatenate(
                [jnp.where(blocks == place, cot, 0.0) for cot in (left_cot, right_cot)], axis=1
            )
            for place in range(residues)
        ],
        axis=0,
    )
    rows = residues * seqs
    parts = jnp.concatenate(split_three(spread), axis=0)
    ln_cot = jnp.dot(parts, spread_w_ref[...], preferred_element_type=F32)
    ln_cot = ln_cot[0:rows] + (ln_cot[rows : 2 * rows] + ln_cot[2 * rows : 3 * rows])
    gained = ln_cot * gain_ref[...]
    normed = normed_ref[...]
    grad = inv_std_ref[:, 0:1] * (
        gained
        - jnp.mean(gained, axis=-1, keepdims=True)
        - normed * jnp.mean(gained * normed, axis=-1, keepdims=True)
    )
    for place in range(residues):
        grad_ref[:, place, :] = grad[place * seqs : (place + 1) * seqs].astype(BF16)


def small_pair_kernel(scale, right_ref, far_ref, left_ref, sorted_w_ref, offset_ref,
                     pair_ref, turn_ref):
    residues, columns, _ = pair_ref.shape
    depth = LANES // residues
    ranks = columns // residues
    rank = lax.axis_index("res")
    base = lax.axis_index("seq") * ranks
    near, far = [], []
    for place in range(ranks):
        distance = lax.bitwise_xor(rank, base + place)
        near.append(right_ref[distance])
        far.append(far_ref[distance & (ranks - 1)])
    right = jnp.concatenate(
        [jnp.concatenate(near, axis=1), jnp.concatenate(far, axis=1)], axis=0
    )
    left = jnp.concatenate([left_ref[...], far_ref[ranks]], axis=0)
    turn_ref[...] = lax.dot_general(right, left, TN, preferred_element_type=F32) * scale
    blocks = lane_block((columns, LANES), depth)
    tiles = []
    for tile in range(depth * depth // LANES):
        pieces = [
            turn_ref[pl.ds(tile * residues + e, columns, stride=depth), :]
            for e in range(residues)
        ]
        rows = jnp.concatenate(pieces, axis=0)
        turned = [rows] + [pltpu.roll(rows, depth * t, 1) for t in range(1, residues)]
        tiles.append(
            jnp.concatenate(
                [
                    pick(
                        blocks,
                        [
                            turned[(e - i) % residues][e * columns : (e + 1) * columns]
                            for e in range(residues)
                        ],
                    )
                    for i in range(residues)
                ],
                axis=0,
            )
        )
    flat = jnp.concatenate(tiles, axis=1)
    rows = residues * columns
    parts = jnp.concatenate(split_three(flat), axis=0)
    pair = jnp.dot(parts, sorted_w_ref[...], preferred_element_type=F32)
    pair = pair[0:rows] + (pair[rows : 2 * rows] + pair[2 * rows : 3 * rows])
    pair_ref[...] = (pair + offset_ref[...]).astype(BF16).reshape(pair_ref.shape)


def small_slice(
    homolog_matrix,
    standardizer_scaling,
    standardizer_offset,
    left_projection_matrix,
    left_offset_vector,
    right_projection_matrix,
    right_offset_vector,
    coupling_matrix,
    coupling_offset,
    coupling_cotangent,
):
    seqs, residues, features = homolog_matrix.shape
    depth = left_projection_matrix.shape[1]
    ranks = lax.axis_size("res")
    rows = seqs * residues
    scale = 1.0 / (seqs * lax.axis_size("seq"))
    rank = lax.axis_index("res")
    mine = lax.axis_index("seq")
    swap = [(0, 1), (1, 0)]
    limit = pltpu.CompilerParams(vmem_limit_bytes=8 * 1024 * 1024)
    vmem = pl.BlockSpec(memory_space=pltpu.VMEM)
    like = jax.ShapeDtypeStruct

    other_cot = lax.ppermute(coupling_cotangent, "seq", swap)
    hbm = pl.BlockSpec(memory_space=pltpu.HBM)
    pin = lambda array: pltpu.with_memory_space_constraint(array, pltpu.HBM)
    x = pin(homolog_matrix)
    gain_row = pin(standardizer_scaling.reshape(1, -1))
    left_w = pin(left_projection_matrix.T)
    right_w = pin(right_projection_matrix.T)
    left, right, sorted_w = pl.pallas_call(
        small_project_kernel,
        in_specs=[hbm] * 8,
        out_specs=[vmem] * 3,
        out_shape=(
            like((seqs, LANES), BF16),
            like((seqs, LANES), BF16),
            like(coupling_matrix.shape, BF16),
        ),
        scratch_shapes=[
            pltpu.VMEM(homolog_matrix.shape, BF16),
            pltpu.VMEM((1, features), F32),
            pltpu.VMEM((1, features), F32),
            pltpu.VMEM((depth, features), BF16),
            pltpu.VMEM((1, depth), F32),
            pltpu.VMEM((depth, features), BF16),
            pltpu.VMEM((1, depth), F32),
            pltpu.VMEM(coupling_matrix.shape, BF16),
            pltpu.VMEM(coupling_matrix.shape, F32),
            pltpu.SemaphoreType.DMA((8,)),
        ],
        compiler_params=limit,
        name="project",
    )(
        x,
        gain_row,
        pin(standardizer_offset.reshape(1, -1)),
        left_w,
        pin(left_offset_vector.reshape(1, -1)),
        right_w,
        pin(right_offset_vector.reshape(1, -1)),
        pin(coupling_matrix),
    )

    half_rows = ranks // 2 * LANES
    send, outer_far = pl.pallas_call(
        functools.partial(small_far_kernel, scale),
        in_specs=[vmem] * 5,
        out_specs=[vmem] * 2,
        out_shape=(
            like((1 + ranks // 2, seqs, LANES), BF16),
            like((half_rows, LANES), BF16),
        ),
        scratch_shapes=[pltpu.VMEM((half_rows, LANES), F32)],
        compiler_params=limit,
        name="far_pieces",
    )(coupling_cotangent, other_cot, sorted_w, left, right)

    keep, outer_near, normed, inv_std, spread_w, gain, pair_offset = pl.pallas_call(
        functools.partial(small_near_kernel, scale),
        in_specs=[hbm] * 5 + [vmem] * 4,
        out_specs=[vmem] * 7,
        out_shape=(
            like((ranks // 2, seqs, LANES), F32),
            like((half_rows, LANES), BF16),
            like((rows, features), F32),
            like((rows, LANES), F32),
            like((2 * LANES, features), BF16),
            like((1, features), F32),
            like((1, LANES), F32),
        ),
        scratch_shapes=[
            pltpu.VMEM(homolog_matrix.shape, BF16),
            pltpu.VMEM((depth, features), BF16),
            pltpu.VMEM((depth, features), BF16),
            pltpu.VMEM((half_rows, LANES), F32),
            pltpu.SemaphoreType.DMA((5,)),
        ],
        compiler_params=limit,
        name="near_pieces",
    )(
        x,
        gain_row,
        left_w,
        right_w,
        pin(coupling_offset.reshape(1, -1)),
        coupling_cotangent,
        other_cot,
        sorted_w,
        left,
    )

    def swap_over(mask, value):
        return lax.ppermute(value, "res", [(source, source ^ mask) for source in range(ranks)])

    own = right[None]
    beyond_two = swap_over(4, send)
    both = jnp.concatenate([own, beyond_two[0:1]])
    near_parts = {}
    gathered = jnp.concatenate(
        [own, jnp.zeros((3, seqs, LANES), BF16), beyond_two[0:1], jnp.zeros((3, seqs, LANES), BF16)]
    )
    for mask in (3, 2, 1):
        summed = (keep[mask] + beyond_two[1 + mask].astype(F32)).astype(BF16)
        part = swap_over(mask, jnp.concatenate([both, summed[None]]))
        near_parts[mask] = part
        gathered = lax.dynamic_update_slice_in_dim(gathered, part[0:1], mask, 0)
        gathered = lax.dynamic_update_slice_in_dim(gathered, part[1:2], 4 + mask, 0)
    near_parts = [near_parts[mask] for mask in (1, 2, 3)]

    half = gathered.reshape(2, ranks // 2, seqs, LANES)
    beyond = 1 - lax.bitwise_xor(lax.shift_right_logical(rank, 2), mine)
    leaving = lax.dynamic_index_in_dim(half, beyond, 0, keepdims=False)
    far = lax.ppermute(jnp.concatenate([leaving, left[None]]), "seq", swap)

    gradient = pl.pallas_call(
        small_grad_kernel,
        in_specs=[vmem] * 5 + [[vmem] * 3] + [vmem] * 4,
        out_specs=vmem,
        out_shape=like(homolog_matrix.shape, BF16),
        compiler_params=limit,
        name="gradient",
    )(gathered, outer_near, outer_far, keep, beyond_two, near_parts, normed, inv_std, gain, spread_w)

    pair_delta = pl.pallas_call(
        functools.partial(small_pair_kernel, scale),
        in_specs=[vmem] * 5,
        out_specs=vmem,
        out_shape=like(coupling_cotangent.shape, BF16),
        scratch_shapes=[pltpu.VMEM((ranks // 2 * LANES, LANES), F32)],
        compiler_params=limit,
        name="pair",
    )(gathered, far, left, sorted_w, pair_offset)
    return (pair_delta, gradient)


def body(*arrays):
    if lax.axis_size("res") == 8:
        return small_slice(*arrays)
    return wide_slice(*arrays)


def solution(mesh):
    return jax.shard_map(
        body,
        mesh=mesh,
        in_specs=(
            P(("grp", "seq"), "res", None),
            P(),
            P(),
            P(),
            P(),
            P(),
            P(),
            P(),
            P(),
            P(("grp", "res"), "seq", None),
        ),
        out_specs=(P(("grp", "res"), "seq", None), P(("grp", "seq"), "res", None)),
        check_vma=False,
    )
```

```python
import functools

import jax
import jax.numpy as jnp
from jax import lax
from jax.experimental import pallas as pl
from jax.experimental.pallas import tpu as pltpu
from jax.sharding import PartitionSpec as P

LANES = 128
BF16 = jnp.bfloat16
F32 = jnp.float32
NT = (((1,), (1,)), ((), ()))
TN = (((0,), (0,)), ((), ()))


def lane_block(shape, width):
    return lax.broadcasted_iota(jnp.int32, shape, 1) // width


def pick(blocks, pieces):
    result = pieces[0]
    for place in range(1, len(pieces)):
        result = jnp.where(blocks == place, pieces[place], result)
    return result


def split_three(value):
    top = value.astype(BF16)
    rest = value - top.astype(F32)
    middle = rest.astype(BF16)
    low = (rest - middle.astype(F32)).astype(BF16)
    return top, middle, low


def normalise(rows):
    centred = rows - jnp.mean(rows, axis=-1, keepdims=True)
    inv_std = lax.rsqrt(jnp.mean(centred * centred, axis=-1, keepdims=True) + 1e-05)
    return centred * inv_std, inv_std


def residue_rows(x_ref):
    return jnp.concatenate(
        [x_ref[:, place, :].astype(F32) for place in range(x_ref.shape[1])], axis=0
    )


def project_kernel(
    x_ref, gain_ref, offset_ref, left_w_ref, left_b_ref, right_w_ref, right_b_ref, w_ref,
    left_ref, right_ref, sorted_w_ref, wide_ref,
):
    seqs, residues, _ = x_ref.shape
    depth = left_w_ref.shape[0]
    normed, _ = normalise(residue_rows(x_ref))
    ln_out = (normed * gain_ref[...] + offset_ref[...]).astype(BF16)
    blocks = lane_block((seqs, LANES), depth)
    for weight_ref, bias_ref, out_ref in (
        (left_w_ref, left_b_ref, left_ref),
        (right_w_ref, right_b_ref, right_ref),
    ):
        weight = jnp.concatenate([weight_ref[...]] * residues, axis=0)
        bias = jnp.concatenate([bias_ref[...]] * residues, axis=1)
        wide = lax.dot_general(ln_out, weight, NT, preferred_element_type=F32)
        own = pick(blocks, [wide[p * seqs : (p + 1) * seqs] for p in range(residues)])
        out_ref[...] = (own + bias).astype(BF16)
    wide_ref[...] = w_ref[...].astype(F32)
    for d in range(depth):
        sorted_w_ref[d * depth : (d + 1) * depth, :] = wide_ref[
            pl.ds(d, depth, stride=depth), :
        ].astype(BF16)


def cot_kernel(scale, own_ref, other_ref, sorted_w_ref, left_ref, right_ref,
               send_ref, outer_ref, turn_ref):
    residues, columns, _ = own_ref.shape
    depth = sorted_w_ref.shape[0] // (LANES // residues)
    depth = LANES // residues
    first = lax.axis_index("seq") == 0
    own = own_ref[...].reshape(residues * columns, LANES)
    other = other_ref[...].reshape(residues * columns, LANES)
    low = jnp.where(first, own, other)
    high = jnp.where(first, other, own)
    both = jnp.concatenate([low, high], axis=0)
    flat = lax.dot_general(both, sorted_w_ref[...], NT, preferred_element_type=F32) * scale
    blocks = lane_block((columns, LANES), depth)
    for half in range(2):
        for tile in range(depth * depth // LANES):
            block = flat[
                half * residues * columns : (half + 1) * residues * columns,
                tile * LANES : (tile + 1) * LANES,
            ]
            turned = [block] + [pltpu.roll(block, depth * t, 1) for t in range(1, residues)]
            for e in range(residues):
                piece = pick(
                    blocks,
                    [
                        turned[(i - e) % residues][i * columns : (i + 1) * columns]
                        for i in range(residues)
                    ],
                )
                turn_ref[pl.ds(half * columns * depth + tile * residues + e, columns, stride=depth), :] = piece
    outer = turn_ref[...].astype(BF16)
    half_rows = columns * depth
    partial = lax.dot_general(left_ref[...], outer, NT, preferred_element_type=F32).astype(BF16)
    seqs = left_ref.shape[0]
    ranks = columns // residues
    for half in range(2):
        outer_ref[half] = outer[half * half_rows : (half + 1) * half_rows]
        for rank in range(ranks):
            at = (half * ranks + rank) * LANES
            send_ref[half, rank, 0:seqs, :] = right_ref[...]
            send_ref[half, rank, seqs : 2 * seqs, :] = partial[:, at : at + LANES]


def grad_kernel(steps, got_ref, outer_ref, x_ref, gain_ref, left_w_ref, right_w_ref,
                grad_ref, left_cot_ref, right_cot_ref):
    step = pl.program_id(0)
    _, ranks, twice, _ = got_ref.shape
    seqs = twice // 2
    residues = x_ref.shape[1]
    depth = LANES // residues

    @pl.when(step == 0)
    def _():
        left_cot_ref[...] = jnp.zeros_like(left_cot_ref)
        right_cot_ref[...] = jnp.zeros_like(right_cot_ref)

    places = [(half, rank) for half in range(2) for rank in range(ranks)]
    right_all = jnp.concatenate([got_ref[h, r, 0:seqs, :] for h, r in places], axis=1)
    outer = jnp.concatenate([outer_ref[0], outer_ref[1]], axis=0)
    left_cot_ref[...] += jnp.dot(right_all, outer, preferred_element_type=F32)
    total = got_ref[0, 0, seqs:twice, :].astype(F32)
    for h, r in places[1:]:
        total = total + got_ref[h, r, seqs:twice, :].astype(F32)
    right_cot_ref[...] += total

    @pl.when(step == steps - 1)
    def _():
        blocks = lane_block((seqs, LANES), depth)
        left_cot, right_cot = left_cot_ref[...], right_cot_ref[...]
        spread = jnp.concatenate(
            [
                jnp.concatenate(
                    [
                        jnp.where(blocks == place, left_cot, 0.0),
                        jnp.where(blocks == place, right_cot, 0.0),
                    ],
                    axis=1,
                )
                for place in range(residues)
            ],
            axis=0,
        )
        weight = jnp.concatenate(
            [left_w_ref[...]] * residues + [right_w_ref[...]] * residues, axis=0
        )
        rows = residues * seqs
        parts = jnp.concatenate(split_three(spread), axis=0)
        ln_cot = jnp.dot(parts, weight, preferred_element_type=F32)
        ln_cot = ln_cot[0:rows] + (ln_cot[rows : 2 * rows] + ln_cot[2 * rows : 3 * rows])
        gained = ln_cot * gain_ref[...]
        normed, inv_std = normalise(residue_rows(x_ref))
        grad = inv_std * (
            gained
            - jnp.mean(gained, axis=-1, keepdims=True)
            - normed * jnp.mean(gained * normed, axis=-1, keepdims=True)
        )
        for place in range(residues):
            grad_ref[:, place, :] = grad[place * seqs : (place + 1) * seqs].astype(BF16)


def pair_kernel(scale, got_ref, far_ref, left_ref, far_left_ref, sorted_w_ref, offset_ref,
                pair_ref, turn_ref):
    residues, columns, _ = pair_ref.shape
    depth = LANES // residues
    ranks = columns // residues
    mine = lax.axis_index("seq")
    near = jnp.concatenate([got_ref[mine, r] for r in range(ranks)], axis=1)
    far = jnp.concatenate([far_ref[r] for r in range(ranks)], axis=1)
    right = jnp.concatenate([near, far], axis=0)
    left = jnp.concatenate([left_ref[...], far_left_ref[...]], axis=0)
    turn_ref[...] = lax.dot_general(right, left, TN, preferred_element_type=F32) * scale
    blocks = lane_block((columns, LANES), depth)
    tiles = []
    for tile in range(depth * depth // LANES):
        pieces = [
            turn_ref[pl.ds(tile * residues + e, columns, stride=depth), :]
            for e in range(residues)
        ]
        rows = jnp.concatenate(pieces, axis=0)
        turned = [rows] + [pltpu.roll(rows, depth * t, 1) for t in range(1, residues)]
        tiles.append(
            jnp.concatenate(
                [
                    pick(
                        blocks,
                        [
                            turned[(e - i) % residues][e * columns : (e + 1) * columns]
                            for e in range(residues)
                        ],
                    )
                    for i in range(residues)
                ],
                axis=0,
            )
        )
    flat = jnp.concatenate(tiles, axis=1)
    rows = residues * columns
    parts = jnp.concatenate(split_three(flat), axis=0)
    pair = jnp.dot(parts, sorted_w_ref[...], preferred_element_type=F32)
    pair = pair[0:rows] + (pair[rows : 2 * rows] + pair[2 * rows : 3 * rows])
    pair_ref[...] = (pair + offset_ref[...]).astype(BF16).reshape(pair_ref.shape)


def wide_slice(
    homolog_matrix,
    standardizer_scaling,
    standardizer_offset,
    left_projection_matrix,
    left_offset_vector,
    right_projection_matrix,
    right_offset_vector,
    coupling_matrix,
    coupling_offset,
    coupling_cotangent,
):
    seqs, residues, features = homolog_matrix.shape
    depth = left_projection_matrix.shape[1]
    ranks = lax.axis_size("res")
    scale = 1.0 / (seqs * lax.axis_size("seq"))
    half_ranks = ranks // 2
    half_columns = half_ranks * residues
    step_ranks = 4
    columns = step_ranks * residues
    steps = half_ranks // step_ranks
    mine = lax.axis_index("seq")
    swap = [(0, 1), (1, 0)]

    other_cot = lax.ppermute(coupling_cotangent, "seq", swap)
    gain = standardizer_scaling.reshape(1, -1)
    left_w = left_projection_matrix.T
    right_w = right_projection_matrix.T

    left, right, sorted_w = pl.pallas_call(
        project_kernel,
        out_shape=(
            jax.ShapeDtypeStruct((seqs, LANES), BF16),
            jax.ShapeDtypeStruct((seqs, LANES), BF16),
            jax.ShapeDtypeStruct(coupling_matrix.shape, BF16),
        ),
        scratch_shapes=[pltpu.VMEM(coupling_matrix.shape, F32)],
        name="project",
    )(
        homolog_matrix,
        gain,
        standardizer_offset.reshape(1, -1),
        left_w,
        left_offset_vector.reshape(1, -1),
        right_w,
        right_offset_vector.reshape(1, -1),
        coupling_matrix,
    )

    whole = lambda shape: pl.BlockSpec(shape, lambda g: (0,) * len(shape))
    cot_block = pl.BlockSpec((residues, columns, LANES), lambda g: (0, g, 0))
    outer_block = pl.BlockSpec((2, columns * depth, LANES), lambda g: (0, g, 0))
    send_block = pl.BlockSpec((2, step_ranks, 2 * seqs, LANES), lambda g: (0, g, 0, 0))
    send, outer = pl.pallas_call(
        functools.partial(cot_kernel, scale),
        grid=(steps,),
        in_specs=[
            cot_block,
            cot_block,
            whole(sorted_w.shape),
            whole(left.shape),
            whole(right.shape),
        ],
        out_specs=(send_block, outer_block),
        out_shape=(
            jax.ShapeDtypeStruct((2, half_ranks, 2 * seqs, LANES), BF16),
            jax.ShapeDtypeStruct((2, half_columns * depth, LANES), BF16),
        ),
        scratch_shapes=[pltpu.VMEM((2 * columns * depth, LANES), F32)],
        name="cotangent",
    )(coupling_cotangent, other_cot, sorted_w, left, right)

    got = lax.all_to_all(
        send.reshape(ranks, 2 * seqs, LANES), "res", split_axis=0, concat_axis=0, tiled=True
    ).reshape(send.shape)

    leaving = lax.dynamic_index_in_dim(got, 1 - mine, 0, keepdims=False)[:, 0:seqs, :]
    far = lax.ppermute(jnp.concatenate([leaving, left[None]], axis=0), "seq", swap)

    gradient = pl.pallas_call(
        functools.partial(grad_kernel, steps),
        grid=(steps,),
        in_specs=[
            send_block,
            outer_block,
            whole(homolog_matrix.shape),
            whole(gain.shape),
            whole(left_w.shape),
            whole(right_w.shape),
        ],
        out_specs=whole(homolog_matrix.shape),
        out_shape=jax.ShapeDtypeStruct(homolog_matrix.shape, BF16),
        scratch_shapes=[pltpu.VMEM((seqs, LANES), F32)] * 2,
        name="gradient",
    )(got, outer, homolog_matrix, gain, left_w, right_w)

    pair_delta = pl.pallas_call(
        functools.partial(pair_kernel, scale),
        grid=(steps,),
        in_specs=[
            pl.BlockSpec((2, step_ranks, seqs, LANES), lambda g: (0, g, 0, 0)),
            pl.BlockSpec((step_ranks, seqs, LANES), lambda g: (g, 0, 0)),
            whole(left.shape),
            pl.BlockSpec((None, seqs, LANES), lambda g: (half_ranks, 0, 0)),
            whole(sorted_w.shape),
            whole((1, LANES)),
        ],
        out_specs=cot_block,
        out_shape=jax.ShapeDtypeStruct(coupling_cotangent.shape, BF16),
        scratch_shapes=[pltpu.VMEM((columns * depth, LANES), F32)],
        name="pair",
    )(got, far, left, far, sorted_w, coupling_offset.reshape(1, -1))
    return (pair_delta, gradient)


def fetch(source, target, semaphore):
    copy = pltpu.make_async_copy(source, target, semaphore)
    copy.start()
    return copy


def start_copies(pairs, semaphores):
    copies = [
        pltpu.make_async_copy(source, target, semaphores.at[place])
        for place, (source, target) in enumerate(pairs)
    ]
    for copy in copies:
        copy.start()
    return copies


def small_project_kernel(
    x_hbm, gain_hbm, offset_hbm, left_w_hbm, left_b_hbm, right_w_hbm, right_b_hbm, w_hbm,
    left_ref, right_ref, sorted_w_ref,
    x_ref, gain_ref, offset_ref, left_w_ref, left_b_ref, right_w_ref, right_b_ref, raw_ref, wide_ref,
    semaphores,
):
    copies = start_copies(
        (
            (x_hbm, x_ref),
            (gain_hbm, gain_ref),
            (offset_hbm, offset_ref),
            (left_w_hbm, left_w_ref),
            (left_b_hbm, left_b_ref),
            (right_w_hbm, right_w_ref),
            (right_b_hbm, right_b_ref),
            (w_hbm, raw_ref),
        ),
        semaphores,
    )
    seqs, residues, _ = x_ref.shape
    depth = left_w_ref.shape[0]
    copies[0].wait()
    normed, _ = normalise(residue_rows(x_ref))
    for copy in copies[1:7]:
        copy.wait()
    ln_out = (normed * gain_ref[...] + offset_ref[...]).astype(BF16)
    blocks = lane_block((seqs, LANES), depth)
    for weight_ref, bias_ref, out_ref in (
        (left_w_ref, left_b_ref, left_ref),
        (right_w_ref, right_b_ref, right_ref),
    ):
        weight = jnp.concatenate([weight_ref[...]] * residues, axis=0)
        bias = jnp.concatenate([bias_ref[...]] * residues, axis=1)
        wide = lax.dot_general(ln_out, weight, NT, preferred_element_type=F32)
        own = pick(blocks, [wide[p * seqs : (p + 1) * seqs] for p in range(residues)])
        out_ref[...] = (own + bias).astype(BF16)
    copies[7].wait()
    wide_ref[...] = raw_ref[...].astype(F32)
    for d in range(depth):
        sorted_w_ref[d * depth : (d + 1) * depth, :] = wide_ref[
            pl.ds(d, depth, stride=depth), :
        ].astype(BF16)


def half_pieces(scale, half, own_ref, other_ref, sorted_w_ref, left_ref, turn_ref):
    residues, columns, _ = own_ref.shape
    depth = LANES // residues
    own = own_ref[...].reshape(residues * columns, LANES)
    other = other_ref[...].reshape(residues * columns, LANES)
    cot = jnp.where(lax.axis_index("seq") == half, own, other)
    flat = lax.dot_general(cot, sorted_w_ref[...], NT, preferred_element_type=F32) * scale
    blocks = lane_block((columns, LANES), depth)
    for tile in range(depth * depth // LANES):
        block = flat[:, tile * LANES : (tile + 1) * LANES]
        turned = [block] + [pltpu.roll(block, depth * t, 1) for t in range(1, residues)]
        for e in range(residues):
            turn_ref[pl.ds(tile * residues + e, columns, stride=depth), :] = pick(
                blocks,
                [
                    turned[(i - e) % residues][i * columns : (i + 1) * columns]
                    for i in range(residues)
                ],
            )
    outer = turn_ref[...].astype(BF16)
    partial = lax.dot_general(left_ref[...], outer, NT, preferred_element_type=F32)
    return outer, [
        partial[:, place * LANES : (place + 1) * LANES] for place in range(columns // residues)
    ]


def small_far_kernel(scale, own_ref, other_ref, sorted_w_ref, left_ref, right_ref,
                     send_ref, outer_ref, turn_ref):
    rank = lax.axis_index("res")
    half = 1 - lax.shift_right_logical(rank, 2)
    outer, pieces = half_pieces(scale, half, own_ref, other_ref, sorted_w_ref, left_ref, turn_ref)
    outer_ref[...] = outer
    send_ref[0] = right_ref[...]
    for place, piece in enumerate(pieces):
        send_ref[1 + lax.bitwise_xor(rank & 3, place)] = piece.astype(BF16)


def small_near_kernel(
    scale, x_hbm, gain_hbm, left_w_hbm, right_w_hbm, pair_offset_hbm,
    own_ref, other_ref, sorted_w_ref, left_ref,
    keep_ref, outer_ref, normed_ref, inv_std_ref, spread_w_ref, gain_ref, pair_offset_ref,
    x_ref, left_w_ref, right_w_ref, turn_ref, semaphores,
):
    copies = start_copies(
        (
            (x_hbm, x_ref),
            (gain_hbm, gain_ref),
            (left_w_hbm, left_w_ref),
            (right_w_hbm, right_w_ref),
            (pair_offset_hbm, pair_offset_ref),
        ),
        semaphores,
    )
    residues = x_ref.shape[1]
    rank = lax.axis_index("res")
    half = lax.shift_right_logical(rank, 2)
    outer, pieces = half_pieces(scale, half, own_ref, other_ref, sorted_w_ref, left_ref, turn_ref)
    outer_ref[...] = outer
    for place, piece in enumerate(pieces):
        keep_ref[lax.bitwise_xor(rank & 3, place)] = piece
    for copy in copies:
        copy.wait()
    normed, inv_std = normalise(residue_rows(x_ref))
    normed_ref[...] = normed
    inv_std_ref[...] = jnp.broadcast_to(inv_std, inv_std_ref.shape)
    spread_w_ref[...] = jnp.concatenate(
        [left_w_ref[...]] * residues + [right_w_ref[...]] * residues, axis=0
    )


def small_grad_kernel(spots, right_ref, outer_near_ref, outer_far_ref, keep_ref, far_ref, near_refs, normed_ref, inv_std_ref,
                      gain_ref, spread_w_ref, grad_ref):
    ranks, seqs, _ = right_ref.shape
    residues = grad_ref.shape[1]
    depth = LANES // residues
    rank = lax.axis_index("res")
    places = [lax.bitwise_xor(rank & 3, place) for place in range(ranks // 2)]
    right_all = jnp.concatenate(
        [right_ref[place] for place in places] + [right_ref[4 + place] for place in places], axis=1
    )
    outer = jnp.concatenate([outer_near_ref[...], outer_far_ref[...]], axis=0)
    left_cot = jnp.dot(right_all, outer, preferred_element_type=F32)
    right_cot = keep_ref[0] + far_ref[1].astype(F32)
    for near_ref, spot in zip(near_refs, spots):
        right_cot = right_cot + near_ref[spot].astype(F32)
    blocks = lane_block((seqs, LANES), depth)
    spread = jnp.concatenate(
        [
            jnp.concatenate(
                [jnp.where(blocks == place, cot, 0.0) for cot in (left_cot, right_cot)], axis=1
            )
            for place in range(residues)
        ],
        axis=0,
    )
    rows = residues * seqs
    parts = jnp.concatenate(split_three(spread), axis=0)
    ln_cot = jnp.dot(parts, spread_w_ref[...], preferred_element_type=F32)
    ln_cot = ln_cot[0:rows] + (ln_cot[rows : 2 * rows] + ln_cot[2 * rows : 3 * rows])
    gained = ln_cot * gain_ref[...]
    normed = normed_ref[...]
    grad = inv_std_ref[:, 0:1] * (
        gained
        - jnp.mean(gained, axis=-1, keepdims=True)
        - normed * jnp.mean(gained * normed, axis=-1, keepdims=True)
    )
    for place in range(residues):
        grad_ref[:, place, :] = grad[place * seqs : (place + 1) * seqs].astype(BF16)


def small_pair_kernel(scale, right_ref, far_ref, left_ref, sorted_w_ref, offset_ref,
                     pair_ref, turn_ref):
    residues, columns, _ = pair_ref.shape
    depth = LANES // residues
    ranks = columns // residues
    rank = lax.axis_index("res")
    base = lax.axis_index("seq") * ranks
    near, far = [], []
    for place in range(ranks):
        distance = lax.bitwise_xor(rank, base + place)
        near.append(right_ref[distance])
        far.append(far_ref[distance & (ranks - 1)])
    right = jnp.concatenate(
        [jnp.concatenate(near, axis=1), jnp.concatenate(far, axis=1)], axis=0
    )
    left = jnp.concatenate([left_ref[...], far_ref[ranks]], axis=0)
    turn_ref[...] = lax.dot_general(right, left, TN, preferred_element_type=F32) * scale
    blocks = lane_block((columns, LANES), depth)
    tiles = []
    for tile in range(depth * depth // LANES):
        pieces = [
            turn_ref[pl.ds(tile * residues + e, columns, stride=depth), :]
            for e in range(residues)
        ]
        rows = jnp.concatenate(pieces, axis=0)
        turned = [rows] + [pltpu.roll(rows, depth * t, 1) for t in range(1, residues)]
        tiles.append(
            jnp.concatenate(
                [
                    pick(
                        blocks,
                        [
                            turned[(e - i) % residues][e * columns : (e + 1) * columns]
                            for e in range(residues)
                        ],
                    )
                    for i in range(residues)
                ],
                axis=0,
            )
        )
    flat = jnp.concatenate(tiles, axis=1)
    rows = residues * columns
    parts = jnp.concatenate(split_three(flat), axis=0)
    pair = jnp.dot(parts, sorted_w_ref[...], preferred_element_type=F32)
    pair = pair[0:rows] + (pair[rows : 2 * rows] + pair[2 * rows : 3 * rows])
    pair_ref[...] = (pair + offset_ref[...]).astype(BF16).reshape(pair_ref.shape)


def small_slice(
    homolog_matrix,
    standardizer_scaling,
    standardizer_offset,
    left_projection_matrix,
    left_offset_vector,
    right_projection_matrix,
    right_offset_vector,
    coupling_matrix,
    coupling_offset,
    coupling_cotangent,
):
    seqs, residues, features = homolog_matrix.shape
    depth = left_projection_matrix.shape[1]
    ranks = lax.axis_size("res")
    rows = seqs * residues
    scale = 1.0 / (seqs * lax.axis_size("seq"))
    rank = lax.axis_index("res")
    mine = lax.axis_index("seq")
    swap = [(0, 1), (1, 0)]
    limit = pltpu.CompilerParams(vmem_limit_bytes=8 * 1024 * 1024)
    vmem = pl.BlockSpec(memory_space=pltpu.VMEM)
    like = jax.ShapeDtypeStruct

    other_cot = lax.ppermute(coupling_cotangent, "seq", swap)
    hbm = pl.BlockSpec(memory_space=pltpu.HBM)
    pin = lambda array: pltpu.with_memory_space_constraint(array, pltpu.HBM)
    x = pin(homolog_matrix)
    gain_row = pin(standardizer_scaling.reshape(1, -1))
    left_w = pin(left_projection_matrix.T)
    right_w = pin(right_projection_matrix.T)
    left, right, sorted_w = pl.pallas_call(
        small_project_kernel,
        in_specs=[hbm] * 8,
        out_specs=[vmem] * 3,
        out_shape=(
            like((seqs, LANES), BF16),
            like((seqs, LANES), BF16),
            like(coupling_matrix.shape, BF16),
        ),
        scratch_shapes=[
            pltpu.VMEM(homolog_matrix.shape, BF16),
            pltpu.VMEM((1, features), F32),
            pltpu.VMEM((1, features), F32),
            pltpu.VMEM((depth, features), BF16),
            pltpu.VMEM((1, depth), F32),
            pltpu.VMEM((depth, features), BF16),
            pltpu.VMEM((1, depth), F32),
            pltpu.VMEM(coupling_matrix.shape, BF16),
            pltpu.VMEM(coupling_matrix.shape, F32),
            pltpu.SemaphoreType.DMA((8,)),
        ],
        compiler_params=limit,
        name="project",
    )(
        x,
        gain_row,
        pin(standardizer_offset.reshape(1, -1)),
        left_w,
        pin(left_offset_vector.reshape(1, -1)),
        right_w,
        pin(right_offset_vector.reshape(1, -1)),
        pin(coupling_matrix),
    )

    half_rows = ranks // 2 * LANES
    send, outer_far = pl.pallas_call(
        functools.partial(small_far_kernel, scale),
        in_specs=[vmem] * 5,
        out_specs=[vmem] * 2,
        out_shape=(
            like((1 + ranks // 2, seqs, LANES), BF16),
            like((half_rows, LANES), BF16),
        ),
        scratch_shapes=[pltpu.VMEM((half_rows, LANES), F32)],
        compiler_params=limit,
        name="far_pieces",
    )(coupling_cotangent, other_cot, sorted_w, left, right)

    keep, outer_near, normed, inv_std, spread_w, gain, pair_offset = pl.pallas_call(
        functools.partial(small_near_kernel, scale),
        in_specs=[hbm] * 5 + [vmem] * 4,
        out_specs=[vmem] * 7,
        out_shape=(
            like((ranks // 2, seqs, LANES), F32),
            like((half_rows, LANES), BF16),
            like((rows, features), F32),
            like((rows, LANES), F32),
            like((2 * LANES, features), BF16),
            like((1, features), F32),
            like((1, LANES), F32),
        ),
        scratch_shapes=[
            pltpu.VMEM(homolog_matrix.shape, BF16),
            pltpu.VMEM((depth, features), BF16),
            pltpu.VMEM((depth, features), BF16),
            pltpu.VMEM((half_rows, LANES), F32),
            pltpu.SemaphoreType.DMA((5,)),
        ],
        compiler_params=limit,
        name="near_pieces",
    )(
        x,
        gain_row,
        left_w,
        right_w,
        pin(coupling_offset.reshape(1, -1)),
        coupling_cotangent,
        other_cot,
        sorted_w,
        left,
    )

    def swap_over(mask, value, direction="both"):
        pairs = [(source, source ^ mask) for source in range(ranks)]
        if direction == "down":
            pairs = [(source, target) for source, target in pairs if source > target]
        if direction == "up":
            pairs = [(source, target) for source, target in pairs if source < target]
        return lax.ppermute(value, "res", pairs)

    own = right[None]
    beyond_two = swap_over(4, send)
    both = jnp.concatenate([own, beyond_two[0:1]])
    gathered = jnp.concatenate(
        [own, jnp.zeros((3, seqs, LANES), BF16), beyond_two[0:1], jnp.zeros((3, seqs, LANES), BF16)]
    ).reshape(2, ranks // 2, seqs, LANES)
    near_parts = []
    for mask, direction in ((3, "down"), (2, "both"), (3, "up"), (1, "both")):
        summed = (keep[mask] + beyond_two[1 + mask].astype(F32)).astype(BF16)[None]
        pieces = [summed, both] if direction == "up" else [both, summed]
        part = swap_over(mask, jnp.concatenate(pieces), direction)
        near_parts.append(part)
        slot = (part[1:3] if direction == "up" else part[0:2])[:, None]
        if direction == "up":
            slot = slot + gathered[:, mask : mask + 1]
        gathered = lax.dynamic_update_slice_in_dim(gathered, slot, mask, 1)

    half = gathered
    gathered = half.reshape(ranks, seqs, LANES)
    beyond = 1 - lax.bitwise_xor(lax.shift_right_logical(rank, 2), mine)
    leaving = lax.dynamic_index_in_dim(half, beyond, 0, keepdims=False)
    far = lax.ppermute(jnp.concatenate([leaving, left[None]]), "seq", swap)

    gradient = pl.pallas_call(
        functools.partial(small_grad_kernel, (2, 2, 0, 2)),
        in_specs=[vmem] * 5 + [[vmem] * 4] + [vmem] * 4,
        out_specs=vmem,
        out_shape=like(homolog_matrix.shape, BF16),
        compiler_params=limit,
        name="gradient",
    )(gathered, outer_near, outer_far, keep, beyond_two, near_parts, normed, inv_std, gain, spread_w)

    pair_delta = pl.pallas_call(
        functools.partial(small_pair_kernel, scale),
        in_specs=[vmem] * 5,
        out_specs=vmem,
        out_shape=like(coupling_cotangent.shape, BF16),
        scratch_shapes=[pltpu.VMEM((ranks // 2 * LANES, LANES), F32)],
        compiler_params=limit,
        name="pair",
    )(gathered, far, left, sorted_w, pair_offset)
    return (pair_delta, gradient)


def body(*arrays):
    if lax.axis_size("res") == 8:
        return small_slice(*arrays)
    return wide_slice(*arrays)


def solution(mesh):
    return jax.shard_map(
        body,
        mesh=mesh,
        in_specs=(
            P(("grp", "seq"), "res", None),
            P(),
            P(),
            P(),
            P(),
            P(),
            P(),
            P(),
            P(),
            P(("grp", "res"), "seq", None),
        ),
        out_specs=(P(("grp", "res"), "seq", None), P(("grp", "seq"), "res", None)),
        check_vma=False,
    )
```

```python
import functools

import jax
import jax.numpy as jnp
from jax import lax
from jax.experimental import pallas as pl
from jax.experimental.pallas import tpu as pltpu
from jax.sharding import PartitionSpec as P

LANES = 128
BF16 = jnp.bfloat16
F32 = jnp.float32
NT = (((1,), (1,)), ((), ()))
TN = (((0,), (0,)), ((), ()))


def lane_block(shape, width):
    return lax.broadcasted_iota(jnp.int32, shape, 1) // width


def pick(blocks, pieces):
    result = pieces[0]
    for place in range(1, len(pieces)):
        result = jnp.where(blocks == place, pieces[place], result)
    return result


def split_three(value):
    top = value.astype(BF16)
    rest = value - top.astype(F32)
    middle = rest.astype(BF16)
    low = (rest - middle.astype(F32)).astype(BF16)
    return top, middle, low


def normalise(rows):
    centred = rows - jnp.mean(rows, axis=-1, keepdims=True)
    inv_std = lax.rsqrt(jnp.mean(centred * centred, axis=-1, keepdims=True) + 1e-05)
    return centred * inv_std, inv_std


def residue_rows(x_ref):
    return jnp.concatenate(
        [x_ref[:, place, :].astype(F32) for place in range(x_ref.shape[1])], axis=0
    )


def project_kernel(
    x_ref, gain_ref, offset_ref, left_w_ref, left_b_ref, right_w_ref, right_b_ref, w_ref,
    left_ref, right_ref, sorted_w_ref, wide_ref,
):
    seqs, residues, _ = x_ref.shape
    depth = left_w_ref.shape[0]
    normed, _ = normalise(residue_rows(x_ref))
    ln_out = (normed * gain_ref[...] + offset_ref[...]).astype(BF16)
    blocks = lane_block((seqs, LANES), depth)
    for weight_ref, bias_ref, out_ref in (
        (left_w_ref, left_b_ref, left_ref),
        (right_w_ref, right_b_ref, right_ref),
    ):
        weight = jnp.concatenate([weight_ref[...]] * residues, axis=0)
        bias = jnp.concatenate([bias_ref[...]] * residues, axis=1)
        wide = lax.dot_general(ln_out, weight, NT, preferred_element_type=F32)
        own = pick(blocks, [wide[p * seqs : (p + 1) * seqs] for p in range(residues)])
        out_ref[...] = (own + bias).astype(BF16)
    wide_ref[...] = w_ref[...].astype(F32)
    for d in range(depth):
        sorted_w_ref[d * depth : (d + 1) * depth, :] = wide_ref[
            pl.ds(d, depth, stride=depth), :
        ].astype(BF16)


def cot_kernel(scale, own_ref, other_ref, sorted_w_ref, left_ref, right_ref,
               send_ref, outer_ref, turn_ref):
    residues, columns, _ = own_ref.shape
    depth = sorted_w_ref.shape[0] // (LANES // residues)
    depth = LANES // residues
    first = lax.axis_index("seq") == 0
    own = own_ref[...].reshape(residues * columns, LANES)
    other = other_ref[...].reshape(residues * columns, LANES)
    low = jnp.where(first, own, other)
    high = jnp.where(first, other, own)
    both = jnp.concatenate([low, high], axis=0)
    flat = lax.dot_general(both, sorted_w_ref[...], NT, preferred_element_type=F32) * scale
    blocks = lane_block((columns, LANES), depth)
    for half in range(2):
        for tile in range(depth * depth // LANES):
            block = flat[
                half * residues * columns : (half + 1) * residues * columns,
                tile * LANES : (tile + 1) * LANES,
            ]
            turned = [block] + [pltpu.roll(block, depth * t, 1) for t in range(1, residues)]
            for e in range(residues):
                piece = pick(
                    blocks,
                    [
                        turned[(i - e) % residues][i * columns : (i + 1) * columns]
                        for i in range(residues)
                    ],
                )
                turn_ref[pl.ds(half * columns * depth + tile * residues + e, columns, stride=depth), :] = piece
    outer = turn_ref[...].astype(BF16)
    half_rows = columns * depth
    partial = lax.dot_general(left_ref[...], outer, NT, preferred_element_type=F32).astype(BF16)
    seqs = left_ref.shape[0]
    ranks = columns // residues
    for half in range(2):
        outer_ref[half] = outer[half * half_rows : (half + 1) * half_rows]
        for rank in range(ranks):
            at = (half * ranks + rank) * LANES
            send_ref[half, rank, 0:seqs, :] = right_ref[...]
            send_ref[half, rank, seqs : 2 * seqs, :] = partial[:, at : at + LANES]


def grad_kernel(steps, got_ref, outer_ref, x_ref, gain_ref, left_w_ref, right_w_ref,
                grad_ref, left_cot_ref, right_cot_ref):
    step = pl.program_id(0)
    _, ranks, twice, _ = got_ref.shape
    seqs = twice // 2
    residues = x_ref.shape[1]
    depth = LANES // residues

    @pl.when(step == 0)
    def _():
        left_cot_ref[...] = jnp.zeros_like(left_cot_ref)
        right_cot_ref[...] = jnp.zeros_like(right_cot_ref)

    places = [(half, rank) for half in range(2) for rank in range(ranks)]
    right_all = jnp.concatenate([got_ref[h, r, 0:seqs, :] for h, r in places], axis=1)
    outer = jnp.concatenate([outer_ref[0], outer_ref[1]], axis=0)
    left_cot_ref[...] += jnp.dot(right_all, outer, preferred_element_type=F32)
    total = got_ref[0, 0, seqs:twice, :].astype(F32)
    for h, r in places[1:]:
        total = total + got_ref[h, r, seqs:twice, :].astype(F32)
    right_cot_ref[...] += total

    @pl.when(step == steps - 1)
    def _():
        blocks = lane_block((seqs, LANES), depth)
        left_cot, right_cot = left_cot_ref[...], right_cot_ref[...]
        spread = jnp.concatenate(
            [
                jnp.concatenate(
                    [
                        jnp.where(blocks == place, left_cot, 0.0),
                        jnp.where(blocks == place, right_cot, 0.0),
                    ],
                    axis=1,
                )
                for place in range(residues)
            ],
            axis=0,
        )
        weight = jnp.concatenate(
            [left_w_ref[...]] * residues + [right_w_ref[...]] * residues, axis=0
        )
        rows = residues * seqs
        parts = jnp.concatenate(split_three(spread), axis=0)
        ln_cot = jnp.dot(parts, weight, preferred_element_type=F32)
        ln_cot = ln_cot[0:rows] + (ln_cot[rows : 2 * rows] + ln_cot[2 * rows : 3 * rows])
        gained = ln_cot * gain_ref[...]
        normed, inv_std = normalise(residue_rows(x_ref))
        grad = inv_std * (
            gained
            - jnp.mean(gained, axis=-1, keepdims=True)
            - normed * jnp.mean(gained * normed, axis=-1, keepdims=True)
        )
        for place in range(residues):
            grad_ref[:, place, :] = grad[place * seqs : (place + 1) * seqs].astype(BF16)


def pair_kernel(scale, got_ref, far_ref, left_ref, far_left_ref, sorted_w_ref, offset_ref,
                pair_ref, turn_ref):
    residues, columns, _ = pair_ref.shape
    depth = LANES // residues
    ranks = columns // residues
    mine = lax.axis_index("seq")
    near = jnp.concatenate([got_ref[mine, r] for r in range(ranks)], axis=1)
    far = jnp.concatenate([far_ref[r] for r in range(ranks)], axis=1)
    right = jnp.concatenate([near, far], axis=0)
    left = jnp.concatenate([left_ref[...], far_left_ref[...]], axis=0)
    turn_ref[...] = lax.dot_general(right, left, TN, preferred_element_type=F32) * scale
    blocks = lane_block((columns, LANES), depth)
    tiles = []
    for tile in range(depth * depth // LANES):
        pieces = [
            turn_ref[pl.ds(tile * residues + e, columns, stride=depth), :]
            for e in range(residues)
        ]
        rows = jnp.concatenate(pieces, axis=0)
        turned = [rows] + [pltpu.roll(rows, depth * t, 1) for t in range(1, residues)]
        tiles.append(
            jnp.concatenate(
                [
                    pick(
                        blocks,
                        [
                            turned[(e - i) % residues][e * columns : (e + 1) * columns]
                            for e in range(residues)
                        ],
                    )
                    for i in range(residues)
                ],
                axis=0,
            )
        )
    flat = jnp.concatenate(tiles, axis=1)
    rows = residues * columns
    parts = jnp.concatenate(split_three(flat), axis=0)
    pair = jnp.dot(parts, sorted_w_ref[...], preferred_element_type=F32)
    pair = pair[0:rows] + (pair[rows : 2 * rows] + pair[2 * rows : 3 * rows])
    pair_ref[...] = (pair + offset_ref[...]).astype(BF16).reshape(pair_ref.shape)


def wide_slice(
    homolog_matrix,
    standardizer_scaling,
    standardizer_offset,
    left_projection_matrix,
    left_offset_vector,
    right_projection_matrix,
    right_offset_vector,
    coupling_matrix,
    coupling_offset,
    coupling_cotangent,
):
    seqs, residues, features = homolog_matrix.shape
    depth = left_projection_matrix.shape[1]
    ranks = lax.axis_size("res")
    scale = 1.0 / (seqs * lax.axis_size("seq"))
    half_ranks = ranks // 2
    half_columns = half_ranks * residues
    step_ranks = 4
    columns = step_ranks * residues
    steps = half_ranks // step_ranks
    mine = lax.axis_index("seq")
    swap = [(0, 1), (1, 0)]

    other_cot = lax.ppermute(coupling_cotangent, "seq", swap)
    gain = standardizer_scaling.reshape(1, -1)
    left_w = left_projection_matrix.T
    right_w = right_projection_matrix.T

    left, right, sorted_w = pl.pallas_call(
        project_kernel,
        out_shape=(
            jax.ShapeDtypeStruct((seqs, LANES), BF16),
            jax.ShapeDtypeStruct((seqs, LANES), BF16),
            jax.ShapeDtypeStruct(coupling_matrix.shape, BF16),
        ),
        scratch_shapes=[pltpu.VMEM(coupling_matrix.shape, F32)],
        name="project",
    )(
        homolog_matrix,
        gain,
        standardizer_offset.reshape(1, -1),
        left_w,
        left_offset_vector.reshape(1, -1),
        right_w,
        right_offset_vector.reshape(1, -1),
        coupling_matrix,
    )

    whole = lambda shape: pl.BlockSpec(shape, lambda g: (0,) * len(shape))
    cot_block = pl.BlockSpec((residues, columns, LANES), lambda g: (0, g, 0))
    outer_block = pl.BlockSpec((2, columns * depth, LANES), lambda g: (0, g, 0))
    send_block = pl.BlockSpec((2, step_ranks, 2 * seqs, LANES), lambda g: (0, g, 0, 0))
    send, outer = pl.pallas_call(
        functools.partial(cot_kernel, scale),
        grid=(steps,),
        in_specs=[
            cot_block,
            cot_block,
            whole(sorted_w.shape),
            whole(left.shape),
            whole(right.shape),
        ],
        out_specs=(send_block, outer_block),
        out_shape=(
            jax.ShapeDtypeStruct((2, half_ranks, 2 * seqs, LANES), BF16),
            jax.ShapeDtypeStruct((2, half_columns * depth, LANES), BF16),
        ),
        scratch_shapes=[pltpu.VMEM((2 * columns * depth, LANES), F32)],
        name="cotangent",
    )(coupling_cotangent, other_cot, sorted_w, left, right)

    got = lax.all_to_all(
        send.reshape(ranks, 2 * seqs, LANES), "res", split_axis=0, concat_axis=0, tiled=True
    ).reshape(send.shape)

    leaving = lax.dynamic_index_in_dim(got, 1 - mine, 0, keepdims=False)[:, 0:seqs, :]
    far = lax.ppermute(jnp.concatenate([leaving, left[None]], axis=0), "seq", swap)

    gradient = pl.pallas_call(
        functools.partial(grad_kernel, steps),
        grid=(steps,),
        in_specs=[
            send_block,
            outer_block,
            whole(homolog_matrix.shape),
            whole(gain.shape),
            whole(left_w.shape),
            whole(right_w.shape),
        ],
        out_specs=whole(homolog_matrix.shape),
        out_shape=jax.ShapeDtypeStruct(homolog_matrix.shape, BF16),
        scratch_shapes=[pltpu.VMEM((seqs, LANES), F32)] * 2,
        name="gradient",
    )(got, outer, homolog_matrix, gain, left_w, right_w)

    pair_delta = pl.pallas_call(
        functools.partial(pair_kernel, scale),
        grid=(steps,),
        in_specs=[
            pl.BlockSpec((2, step_ranks, seqs, LANES), lambda g: (0, g, 0, 0)),
            pl.BlockSpec((step_ranks, seqs, LANES), lambda g: (g, 0, 0)),
            whole(left.shape),
            pl.BlockSpec((None, seqs, LANES), lambda g: (half_ranks, 0, 0)),
            whole(sorted_w.shape),
            whole((1, LANES)),
        ],
        out_specs=cot_block,
        out_shape=jax.ShapeDtypeStruct(coupling_cotangent.shape, BF16),
        scratch_shapes=[pltpu.VMEM((columns * depth, LANES), F32)],
        name="pair",
    )(got, far, left, far, sorted_w, coupling_offset.reshape(1, -1))
    return (pair_delta, gradient)


def fetch(source, target, semaphore):
    copy = pltpu.make_async_copy(source, target, semaphore)
    copy.start()
    return copy


def start_copies(pairs, semaphores):
    copies = [
        pltpu.make_async_copy(source, target, semaphores.at[place])
        for place, (source, target) in enumerate(pairs)
    ]
    for copy in copies:
        copy.start()
    return copies


def small_project_kernel(
    x_hbm, gain_hbm, offset_hbm, left_w_hbm, left_b_hbm, right_w_hbm, right_b_hbm, pair_offset_hbm,
    both_ref, normed_ref, inv_std_ref, spread_w_ref, gain_ref, pair_offset_ref,
    x_ref, offset_ref, left_w_ref, left_b_ref, right_w_ref, right_b_ref, semaphores,
):
    copies = start_copies(
        (
            (x_hbm, x_ref),
            (gain_hbm, gain_ref),
            (offset_hbm, offset_ref),
            (left_w_hbm, left_w_ref),
            (left_b_hbm, left_b_ref),
            (right_w_hbm, right_w_ref),
            (right_b_hbm, right_b_ref),
            (pair_offset_hbm, pair_offset_ref),
        ),
        semaphores,
    )
    seqs, residues, _ = x_ref.shape
    depth = left_w_ref.shape[0]
    copies[0].wait()
    normed, inv_std = normalise(residue_rows(x_ref))
    for copy in copies[1:]:
        copy.wait()
    ln_out = (normed * gain_ref[...] + offset_ref[...]).astype(BF16)
    blocks = lane_block((seqs, LANES), depth)
    spread = []
    for place, (weight_ref, bias_ref) in enumerate(
        ((left_w_ref, left_b_ref), (right_w_ref, right_b_ref))
    ):
        weight = jnp.concatenate([weight_ref[...]] * residues, axis=0)
        spread.append(weight)
        bias = jnp.concatenate([bias_ref[...]] * residues, axis=1)
        wide = lax.dot_general(ln_out, weight, NT, preferred_element_type=F32)
        own = pick(blocks, [wide[p * seqs : (p + 1) * seqs] for p in range(residues)])
        both_ref[place] = (own + bias).astype(BF16)
    normed_ref[...] = normed
    inv_std_ref[...] = jnp.broadcast_to(inv_std, inv_std_ref.shape)
    spread_w_ref[...] = jnp.concatenate(spread, axis=0)


def outer_rows(scale, cot, residues, sorted_w_ref, turn_ref):
    columns = cot.shape[0] // residues
    depth = LANES // residues
    flat = lax.dot_general(cot, sorted_w_ref[...], NT, preferred_element_type=F32) * scale
    blocks = lane_block((columns, LANES), depth)
    for tile in range(depth * depth // LANES):
        block = flat[:, tile * LANES : (tile + 1) * LANES]
        turned = [block] + [pltpu.roll(block, depth * t, 1) for t in range(1, residues)]
        for e in range(residues):
            turn_ref[pl.ds(tile * residues + e, columns, stride=depth), :] = pick(
                blocks,
                [
                    turned[(i - e) % residues][i * columns : (i + 1) * columns]
                    for i in range(residues)
                ],
            )
    return turn_ref[...].astype(BF16)


def small_own_kernel(scale, own_ref, other_ref, w_ref, both_ref,
                     keep_ref, outer_near_ref, outer_far_ref, sorted_w_ref, turn_refs, wide_ref):
    residues, columns, _ = own_ref.shape
    depth = LANES // residues
    wide_ref[...] = w_ref[...].astype(F32)
    for d in range(depth):
        sorted_w_ref[d * depth : (d + 1) * depth, :] = wide_ref[
            pl.ds(d, depth, stride=depth), :
        ].astype(BF16)
    rank = lax.axis_index("res")
    own_is_near = lax.axis_index("seq") == lax.shift_right_logical(rank, 2)
    own = own_ref[...].reshape(residues * columns, LANES)
    other = other_ref[...].reshape(residues * columns, LANES)
    near = outer_rows(
        scale, jnp.where(own_is_near, own, other), residues, sorted_w_ref, turn_refs[0]
    )
    outer_near_ref[...] = near
    partial = lax.dot_general(both_ref[0], near, NT, preferred_element_type=F32)
    for place in range(columns // residues):
        keep_ref[lax.bitwise_xor(rank & 3, place)] = partial[:, place * LANES : (place + 1) * LANES]
    outer_far_ref[...] = outer_rows(
        scale, jnp.where(own_is_near, other, own), residues, sorted_w_ref, turn_refs[1]
    )


def small_partner_kernel(scale, residues, got_ref, sorted_w_ref, keep_ref, both_ref,
                         leaving_ref, keep_out_ref, turn_ref):
    rank = lax.axis_index("res")
    seqs = got_ref.shape[1]
    cot = got_ref[2:4].reshape(2 * seqs, LANES)
    outer = outer_rows(scale, cot, residues, sorted_w_ref, turn_ref)
    partial = lax.dot_general(got_ref[0], outer, NT, preferred_element_type=F32)
    for place in range(leaving_ref.shape[0]):
        leaving_ref[place, 0] = both_ref[1]
        leaving_ref[place, 1] = got_ref[1]
    for place in range(leaving_ref.shape[0]):
        distance = lax.bitwise_xor(rank & 3, place)
        total = keep_ref[distance] + partial[:, place * LANES : (place + 1) * LANES]
        leaving_ref[distance, 2] = total.astype(BF16)
        keep_out_ref[distance] = total


def small_grad_kernel(right_ref, outer_near_ref, outer_far_ref, keep_ref, near_refs, normed_ref, inv_std_ref,
                      gain_ref, spread_w_ref, grad_ref):
    ranks, seqs, _ = right_ref.shape
    residues = grad_ref.shape[1]
    depth = LANES // residues
    rank = lax.axis_index("res")
    places = [lax.bitwise_xor(rank & 3, place) for place in range(ranks // 2)]
    right_all = jnp.concatenate(
        [right_ref[place] for place in places] + [right_ref[4 + place] for place in places], axis=1
    )
    outer = jnp.concatenate([outer_near_ref[...], outer_far_ref[...]], axis=0)
    left_cot = jnp.dot(right_all, outer, preferred_element_type=F32)
    right_cot = keep_ref[0]
    for near_ref in near_refs:
        right_cot = right_cot + near_ref[2].astype(F32)
    blocks = lane_block((seqs, LANES), depth)
    spread = jnp.concatenate(
        [
            jnp.concatenate(
                [jnp.where(blocks == place, cot, 0.0) for cot in (left_cot, right_cot)], axis=1
            )
            for place in range(residues)
        ],
        axis=0,
    )
    rows = residues * seqs
    parts = jnp.concatenate(split_three(spread), axis=0)
    ln_cot = jnp.dot(parts, spread_w_ref[...], preferred_element_type=F32)
    ln_cot = ln_cot[0:rows] + (ln_cot[rows : 2 * rows] + ln_cot[2 * rows : 3 * rows])
    gained = ln_cot * gain_ref[...]
    normed = normed_ref[...]
    grad = inv_std_ref[:, 0:1] * (
        gained
        - jnp.mean(gained, axis=-1, keepdims=True)
        - normed * jnp.mean(gained * normed, axis=-1, keepdims=True)
    )
    for place in range(residues):
        grad_ref[:, place, :] = grad[place * seqs : (place + 1) * seqs].astype(BF16)


def small_pair_kernel(scale, right_ref, far_ref, left_ref, sorted_w_ref, offset_ref,
                     pair_ref, turn_ref):
    residues, columns, _ = pair_ref.shape
    depth = LANES // residues
    ranks = columns // residues
    rank = lax.axis_index("res")
    base = lax.axis_index("seq") * ranks
    near, far = [], []
    for place in range(ranks):
        distance = lax.bitwise_xor(rank, base + place)
        near.append(right_ref[distance])
        far.append(far_ref[distance & (ranks - 1)])
    right = jnp.concatenate(
        [jnp.concatenate(near, axis=1), jnp.concatenate(far, axis=1)], axis=0
    )
    left = jnp.concatenate([left_ref[...], far_ref[ranks]], axis=0)
    turn_ref[...] = lax.dot_general(right, left, TN, preferred_element_type=F32) * scale
    blocks = lane_block((columns, LANES), depth)
    tiles = []
    for tile in range(depth * depth // LANES):
        pieces = [
            turn_ref[pl.ds(tile * residues + e, columns, stride=depth), :]
            for e in range(residues)
        ]
        rows = jnp.concatenate(pieces, axis=0)
        turned = [rows] + [pltpu.roll(rows, depth * t, 1) for t in range(1, residues)]
        tiles.append(
            jnp.concatenate(
                [
                    pick(
                        blocks,
                        [
                            turned[(e - i) % residues][e * columns : (e + 1) * columns]
                            for e in range(residues)
                        ],
                    )
                    for i in range(residues)
                ],
                axis=0,
            )
        )
    flat = jnp.concatenate(tiles, axis=1)
    rows = residues * columns
    parts = jnp.concatenate(split_three(flat), axis=0)
    pair = jnp.dot(parts, sorted_w_ref[...], preferred_element_type=F32)
    pair = pair[0:rows] + (pair[rows : 2 * rows] + pair[2 * rows : 3 * rows])
    pair_ref[...] = (pair + offset_ref[...]).astype(BF16).reshape(pair_ref.shape)


def small_slice(
    homolog_matrix,
    standardizer_scaling,
    standardizer_offset,
    left_projection_matrix,
    left_offset_vector,
    right_projection_matrix,
    right_offset_vector,
    coupling_matrix,
    coupling_offset,
    coupling_cotangent,
):
    seqs, residues, features = homolog_matrix.shape
    depth = left_projection_matrix.shape[1]
    ranks = lax.axis_size("res")
    rows = seqs * residues
    scale = 1.0 / (seqs * lax.axis_size("seq"))
    rank = lax.axis_index("res")
    mine = lax.axis_index("seq")
    swap = [(0, 1), (1, 0)]
    limit = pltpu.CompilerParams(vmem_limit_bytes=8 * 1024 * 1024)
    vmem = pl.BlockSpec(memory_space=pltpu.VMEM)
    like = jax.ShapeDtypeStruct

    other_cot = lax.ppermute(coupling_cotangent, "seq", swap)
    hbm = pl.BlockSpec(memory_space=pltpu.HBM)
    pin = lambda array: pltpu.with_memory_space_constraint(array, pltpu.HBM)
    both, normed, inv_std, spread_w, gain, pair_offset = pl.pallas_call(
        small_project_kernel,
        in_specs=[hbm] * 8,
        out_specs=[vmem] * 6,
        out_shape=(
            like((2, seqs, LANES), BF16),
            like((rows, features), F32),
            like((rows, LANES), F32),
            like((2 * LANES, features), BF16),
            like((1, features), F32),
            like((1, LANES), F32),
        ),
        scratch_shapes=[
            pltpu.VMEM(homolog_matrix.shape, BF16),
            pltpu.VMEM((1, features), F32),
            pltpu.VMEM((depth, features), BF16),
            pltpu.VMEM((1, depth), F32),
            pltpu.VMEM((depth, features), BF16),
            pltpu.VMEM((1, depth), F32),
            pltpu.SemaphoreType.DMA((8,)),
        ],
        compiler_params=limit,
        name="project",
    )(
        *[
            pin(array)
            for array in (
                homolog_matrix,
                standardizer_scaling.reshape(1, -1),
                standardizer_offset.reshape(1, -1),
                left_projection_matrix.T,
                left_offset_vector.reshape(1, -1),
                right_projection_matrix.T,
                right_offset_vector.reshape(1, -1),
                coupling_offset.reshape(1, -1),
            )
        ]
    )

    def swap_over(mask, value):
        return lax.ppermute(value, "res", [(source, source ^ mask) for source in range(ranks)])

    own_is_near = mine == lax.shift_right_logical(rank, 2)
    far_cot = jnp.where(own_is_near, other_cot, coupling_cotangent).reshape(2, seqs, LANES)
    beyond_two = swap_over(4, jnp.concatenate([both, far_cot]))

    half_rows = ranks // 2 * LANES
    turn = pltpu.VMEM((half_rows, LANES), F32)
    keep, outer_near, outer_far, sorted_w = pl.pallas_call(
        functools.partial(small_own_kernel, scale),
        in_specs=[vmem] * 4,
        out_specs=[vmem] * 4,
        out_shape=(
            like((ranks // 2, seqs, LANES), F32),
            like((half_rows, LANES), BF16),
            like((half_rows, LANES), BF16),
            like(coupling_matrix.shape, BF16),
        ),
        scratch_shapes=[[turn, turn], pltpu.VMEM(coupling_matrix.shape, F32)],
        compiler_params=limit,
        name="own_pieces",
    )(coupling_cotangent, other_cot, coupling_matrix, both)

    leaving_parts, keep = pl.pallas_call(
        functools.partial(small_partner_kernel, scale, residues),
        in_specs=[vmem] * 4,
        out_specs=[vmem] * 2,
        out_shape=(
            like((ranks // 2, 3, seqs, LANES), BF16),
            like((ranks // 2, seqs, LANES), F32),
        ),
        scratch_shapes=[turn],
        compiler_params=limit,
        name="partner_pieces",
    )(beyond_two, sorted_w, keep, both)

    left = both[0]
    gathered = jnp.concatenate(
        [
            both[1:2],
            jnp.zeros((3, seqs, LANES), BF16),
            beyond_two[1:2],
            jnp.zeros((3, seqs, LANES), BF16),
        ]
    )
    near_parts = []
    for mask in (3, 2, 1):
        part = swap_over(mask, leaving_parts[mask])
        near_parts.append(part)
        gathered = lax.dynamic_update_slice_in_dim(gathered, part[0:1], mask, 0)
        gathered = lax.dynamic_update_slice_in_dim(gathered, part[1:2], 4 + mask, 0)

    half = gathered.reshape(2, ranks // 2, seqs, LANES)
    beyond = 1 - lax.bitwise_xor(lax.shift_right_logical(rank, 2), mine)
    leaving = lax.dynamic_index_in_dim(half, beyond, 0, keepdims=False)
    far = lax.ppermute(jnp.concatenate([leaving, left[None]]), "seq", swap)

    gradient = pl.pallas_call(
        small_grad_kernel,
        in_specs=[vmem] * 4 + [[vmem] * 3] + [vmem] * 4,
        out_specs=vmem,
        out_shape=like(homolog_matrix.shape, BF16),
        compiler_params=limit,
        name="gradient",
    )(gathered, outer_near, outer_far, keep, near_parts, normed, inv_std, gain, spread_w)

    pair_delta = pl.pallas_call(
        functools.partial(small_pair_kernel, scale),
        in_specs=[vmem] * 5,
        out_specs=vmem,
        out_shape=like(coupling_cotangent.shape, BF16),
        scratch_shapes=[pltpu.VMEM((ranks // 2 * LANES, LANES), F32)],
        compiler_params=limit,
        name="pair",
    )(gathered, far, left, sorted_w, pair_offset)
    return (pair_delta, gradient)


def body(*arrays):
    if lax.axis_size("res") == 8:
        return small_slice(*arrays)
    return wide_slice(*arrays)


def solution(mesh):
    return jax.shard_map(
        body,
        mesh=mesh,
        in_specs=(
            P(("grp", "seq"), "res", None),
            P(),
            P(),
            P(),
            P(),
            P(),
            P(),
            P(),
            P(),
            P(("grp", "res"), "seq", None),
        ),
        out_specs=(P(("grp", "res"), "seq", None), P(("grp", "seq"), "res", None)),
        check_vma=False,
    )
```

```python
import functools

import jax
import jax.numpy as jnp
from jax import lax
from jax.experimental import pallas as pl
from jax.experimental.pallas import tpu as pltpu
from jax.sharding import PartitionSpec as P

LANES = 128
BF16 = jnp.bfloat16
F32 = jnp.float32
NT = (((1,), (1,)), ((), ()))
TN = (((0,), (0,)), ((), ()))


def lane_block(shape, width):
    return lax.broadcasted_iota(jnp.int32, shape, 1) // width


def pick(blocks, pieces):
    result = pieces[0]
    for place in range(1, len(pieces)):
        result = jnp.where(blocks == place, pieces[place], result)
    return result


def split_three(value):
    top = value.astype(BF16)
    rest = value - top.astype(F32)
    middle = rest.astype(BF16)
    low = (rest - middle.astype(F32)).astype(BF16)
    return top, middle, low


def normalise(rows):
    centred = rows - jnp.mean(rows, axis=-1, keepdims=True)
    inv_std = lax.rsqrt(jnp.mean(centred * centred, axis=-1, keepdims=True) + 1e-05)
    return centred * inv_std, inv_std


def residue_rows(x_ref):
    return jnp.concatenate(
        [x_ref[:, place, :].astype(F32) for place in range(x_ref.shape[1])], axis=0
    )


def project_kernel(
    x_ref, gain_ref, offset_ref, left_w_ref, left_b_ref, right_w_ref, right_b_ref, w_ref,
    left_ref, right_ref, sorted_w_ref, wide_ref,
):
    seqs, residues, _ = x_ref.shape
    depth = left_w_ref.shape[0]
    normed, _ = normalise(residue_rows(x_ref))
    ln_out = (normed * gain_ref[...] + offset_ref[...]).astype(BF16)
    blocks = lane_block((seqs, LANES), depth)
    for weight_ref, bias_ref, out_ref in (
        (left_w_ref, left_b_ref, left_ref),
        (right_w_ref, right_b_ref, right_ref),
    ):
        weight = jnp.concatenate([weight_ref[...]] * residues, axis=0)
        bias = jnp.concatenate([bias_ref[...]] * residues, axis=1)
        wide = lax.dot_general(ln_out, weight, NT, preferred_element_type=F32)
        own = pick(blocks, [wide[p * seqs : (p + 1) * seqs] for p in range(residues)])
        out_ref[...] = (own + bias).astype(BF16)
    wide_ref[...] = w_ref[...].astype(F32)
    for d in range(depth):
        sorted_w_ref[d * depth : (d + 1) * depth, :] = wide_ref[
            pl.ds(d, depth, stride=depth), :
        ].astype(BF16)


def cot_kernel(scale, own_ref, other_ref, sorted_w_ref, left_ref, right_ref,
               send_ref, outer_ref, turn_ref):
    residues, columns, _ = own_ref.shape
    depth = sorted_w_ref.shape[0] // (LANES // residues)
    depth = LANES // residues
    first = lax.axis_index("seq") == 0
    own = own_ref[...].reshape(residues * columns, LANES)
    other = other_ref[...].reshape(residues * columns, LANES)
    low = jnp.where(first, own, other)
    high = jnp.where(first, other, own)
    both = jnp.concatenate([low, high], axis=0)
    flat = lax.dot_general(both, sorted_w_ref[...], NT, preferred_element_type=F32) * scale
    blocks = lane_block((columns, LANES), depth)
    for half in range(2):
        for tile in range(depth * depth // LANES):
            block = flat[
                half * residues * columns : (half + 1) * residues * columns,
                tile * LANES : (tile + 1) * LANES,
            ]
            turned = [block] + [pltpu.roll(block, depth * t, 1) for t in range(1, residues)]
            for e in range(residues):
                piece = pick(
                    blocks,
                    [
                        turned[(i - e) % residues][i * columns : (i + 1) * columns]
                        for i in range(residues)
                    ],
                )
                turn_ref[pl.ds(half * columns * depth + tile * residues + e, columns, stride=depth), :] = piece
    outer = turn_ref[...].astype(BF16)
    half_rows = columns * depth
    partial = lax.dot_general(left_ref[...], outer, NT, preferred_element_type=F32).astype(BF16)
    seqs = left_ref.shape[0]
    ranks = columns // residues
    for half in range(2):
        outer_ref[half] = outer[half * half_rows : (half + 1) * half_rows]
        for rank in range(ranks):
            at = (half * ranks + rank) * LANES
            send_ref[half, rank, 0:seqs, :] = right_ref[...]
            send_ref[half, rank, seqs : 2 * seqs, :] = partial[:, at : at + LANES]


def grad_kernel(steps, got_ref, outer_ref, x_ref, gain_ref, left_w_ref, right_w_ref,
                grad_ref, left_cot_ref, right_cot_ref):
    step = pl.program_id(0)
    _, ranks, twice, _ = got_ref.shape
    seqs = twice // 2
    residues = x_ref.shape[1]
    depth = LANES // residues

    @pl.when(step == 0)
    def _():
        left_cot_ref[...] = jnp.zeros_like(left_cot_ref)
        right_cot_ref[...] = jnp.zeros_like(right_cot_ref)

    places = [(half, rank) for half in range(2) for rank in range(ranks)]
    right_all = jnp.concatenate([got_ref[h, r, 0:seqs, :] for h, r in places], axis=1)
    outer = jnp.concatenate([outer_ref[0], outer_ref[1]], axis=0)
    left_cot_ref[...] += jnp.dot(right_all, outer, preferred_element_type=F32)
    total = got_ref[0, 0, seqs:twice, :].astype(F32)
    for h, r in places[1:]:
        total = total + got_ref[h, r, seqs:twice, :].astype(F32)
    right_cot_ref[...] += total

    @pl.when(step == steps - 1)
    def _():
        blocks = lane_block((seqs, LANES), depth)
        left_cot, right_cot = left_cot_ref[...], right_cot_ref[...]
        spread = jnp.concatenate(
            [
                jnp.concatenate(
                    [
                        jnp.where(blocks == place, left_cot, 0.0),
                        jnp.where(blocks == place, right_cot, 0.0),
                    ],
                    axis=1,
                )
                for place in range(residues)
            ],
            axis=0,
        )
        weight = jnp.concatenate(
            [left_w_ref[...]] * residues + [right_w_ref[...]] * residues, axis=0
        )
        rows = residues * seqs
        parts = jnp.concatenate(split_three(spread), axis=0)
        ln_cot = jnp.dot(parts, weight, preferred_element_type=F32)
        ln_cot = ln_cot[0:rows] + (ln_cot[rows : 2 * rows] + ln_cot[2 * rows : 3 * rows])
        gained = ln_cot * gain_ref[...]
        normed, inv_std = normalise(residue_rows(x_ref))
        grad = inv_std * (
            gained
            - jnp.mean(gained, axis=-1, keepdims=True)
            - normed * jnp.mean(gained * normed, axis=-1, keepdims=True)
        )
        for place in range(residues):
            grad_ref[:, place, :] = grad[place * seqs : (place + 1) * seqs].astype(BF16)


def pair_kernel(scale, got_ref, far_ref, left_ref, far_left_ref, sorted_w_ref, offset_ref,
                pair_ref, turn_ref):
    residues, columns, _ = pair_ref.shape
    depth = LANES // residues
    ranks = columns // residues
    mine = lax.axis_index("seq")
    near = jnp.concatenate([got_ref[mine, r] for r in range(ranks)], axis=1)
    far = jnp.concatenate([far_ref[r] for r in range(ranks)], axis=1)
    right = jnp.concatenate([near, far], axis=0)
    left = jnp.concatenate([left_ref[...], far_left_ref[...]], axis=0)
    turn_ref[...] = lax.dot_general(right, left, TN, preferred_element_type=F32) * scale
    blocks = lane_block((columns, LANES), depth)
    tiles = []
    for tile in range(depth * depth // LANES):
        pieces = [
            turn_ref[pl.ds(tile * residues + e, columns, stride=depth), :]
            for e in range(residues)
        ]
        rows = jnp.concatenate(pieces, axis=0)
        turned = [rows] + [pltpu.roll(rows, depth * t, 1) for t in range(1, residues)]
        tiles.append(
            jnp.concatenate(
                [
                    pick(
                        blocks,
                        [
                            turned[(e - i) % residues][e * columns : (e + 1) * columns]
                            for e in range(residues)
                        ],
                    )
                    for i in range(residues)
                ],
                axis=0,
            )
        )
    flat = jnp.concatenate(tiles, axis=1)
    rows = residues * columns
    parts = jnp.concatenate(split_three(flat), axis=0)
    pair = jnp.dot(parts, sorted_w_ref[...], preferred_element_type=F32)
    pair = pair[0:rows] + (pair[rows : 2 * rows] + pair[2 * rows : 3 * rows])
    pair_ref[...] = (pair + offset_ref[...]).astype(BF16).reshape(pair_ref.shape)


def wide_slice(
    homolog_matrix,
    standardizer_scaling,
    standardizer_offset,
    left_projection_matrix,
    left_offset_vector,
    right_projection_matrix,
    right_offset_vector,
    coupling_matrix,
    coupling_offset,
    coupling_cotangent,
):
    seqs, residues, features = homolog_matrix.shape
    depth = left_projection_matrix.shape[1]
    ranks = lax.axis_size("res")
    scale = 1.0 / (seqs * lax.axis_size("seq"))
    half_ranks = ranks // 2
    half_columns = half_ranks * residues
    step_ranks = 4
    columns = step_ranks * residues
    steps = half_ranks // step_ranks
    mine = lax.axis_index("seq")
    swap = [(0, 1), (1, 0)]

    other_cot = lax.ppermute(coupling_cotangent, "seq", swap)
    gain = standardizer_scaling.reshape(1, -1)
    left_w = left_projection_matrix.T
    right_w = right_projection_matrix.T

    left, right, sorted_w = pl.pallas_call(
        project_kernel,
        out_shape=(
            jax.ShapeDtypeStruct((seqs, LANES), BF16),
            jax.ShapeDtypeStruct((seqs, LANES), BF16),
            jax.ShapeDtypeStruct(coupling_matrix.shape, BF16),
        ),
        scratch_shapes=[pltpu.VMEM(coupling_matrix.shape, F32)],
        name="project",
    )(
        homolog_matrix,
        gain,
        standardizer_offset.reshape(1, -1),
        left_w,
        left_offset_vector.reshape(1, -1),
        right_w,
        right_offset_vector.reshape(1, -1),
        coupling_matrix,
    )

    whole = lambda shape: pl.BlockSpec(shape, lambda g: (0,) * len(shape))
    cot_block = pl.BlockSpec((residues, columns, LANES), lambda g: (0, g, 0))
    outer_block = pl.BlockSpec((2, columns * depth, LANES), lambda g: (0, g, 0))
    send_block = pl.BlockSpec((2, step_ranks, 2 * seqs, LANES), lambda g: (0, g, 0, 0))
    send, outer = pl.pallas_call(
        functools.partial(cot_kernel, scale),
        grid=(steps,),
        in_specs=[
            cot_block,
            cot_block,
            whole(sorted_w.shape),
            whole(left.shape),
            whole(right.shape),
        ],
        out_specs=(send_block, outer_block),
        out_shape=(
            jax.ShapeDtypeStruct((2, half_ranks, 2 * seqs, LANES), BF16),
            jax.ShapeDtypeStruct((2, half_columns * depth, LANES), BF16),
        ),
        scratch_shapes=[pltpu.VMEM((2 * columns * depth, LANES), F32)],
        name="cotangent",
    )(coupling_cotangent, other_cot, sorted_w, left, right)

    got = lax.all_to_all(
        send.reshape(ranks, 2 * seqs, LANES), "res", split_axis=0, concat_axis=0, tiled=True
    ).reshape(send.shape)

    leaving = lax.dynamic_index_in_dim(got, 1 - mine, 0, keepdims=False)[:, 0:seqs, :]
    far = lax.ppermute(jnp.concatenate([leaving, left[None]], axis=0), "seq", swap)

    gradient = pl.pallas_call(
        functools.partial(grad_kernel, steps),
        grid=(steps,),
        in_specs=[
            send_block,
            outer_block,
            whole(homolog_matrix.shape),
            whole(gain.shape),
            whole(left_w.shape),
            whole(right_w.shape),
        ],
        out_specs=whole(homolog_matrix.shape),
        out_shape=jax.ShapeDtypeStruct(homolog_matrix.shape, BF16),
        scratch_shapes=[pltpu.VMEM((seqs, LANES), F32)] * 2,
        name="gradient",
    )(got, outer, homolog_matrix, gain, left_w, right_w)

    pair_delta = pl.pallas_call(
        functools.partial(pair_kernel, scale),
        grid=(steps,),
        in_specs=[
            pl.BlockSpec((2, step_ranks, seqs, LANES), lambda g: (0, g, 0, 0)),
            pl.BlockSpec((step_ranks, seqs, LANES), lambda g: (g, 0, 0)),
            whole(left.shape),
            pl.BlockSpec((None, seqs, LANES), lambda g: (half_ranks, 0, 0)),
            whole(sorted_w.shape),
            whole((1, LANES)),
        ],
        out_specs=cot_block,
        out_shape=jax.ShapeDtypeStruct(coupling_cotangent.shape, BF16),
        scratch_shapes=[pltpu.VMEM((columns * depth, LANES), F32)],
        name="pair",
    )(got, far, left, far, sorted_w, coupling_offset.reshape(1, -1))
    return (pair_delta, gradient)


def fetch(source, target, semaphore):
    copy = pltpu.make_async_copy(source, target, semaphore)
    copy.start()
    return copy


def start_copies(pairs, semaphores):
    copies = [
        pltpu.make_async_copy(source, target, semaphores.at[place])
        for place, (source, target) in enumerate(pairs)
    ]
    for copy in copies:
        copy.start()
    return copies


def small_project_kernel(
    x_hbm, gain_hbm, offset_hbm, left_w_hbm, left_b_hbm, right_w_hbm, right_b_hbm, pair_offset_hbm,
    cot_hbm, both_ref, normed_ref, inv_std_ref, spread_w_ref, gain_ref, pair_offset_ref, cot_ref,
    x_ref, offset_ref, left_w_ref, left_b_ref, right_w_ref, right_b_ref, semaphores,
):
    copies = start_copies(
        (
            (x_hbm, x_ref),
            (gain_hbm, gain_ref),
            (offset_hbm, offset_ref),
            (left_w_hbm, left_w_ref),
            (left_b_hbm, left_b_ref),
            (right_w_hbm, right_w_ref),
            (right_b_hbm, right_b_ref),
            (pair_offset_hbm, pair_offset_ref),
            (cot_hbm, cot_ref),
        ),
        semaphores,
    )
    seqs, residues, _ = x_ref.shape
    depth = left_w_ref.shape[0]
    copies[0].wait()
    normed, inv_std = normalise(residue_rows(x_ref))
    for copy in copies[1:]:
        copy.wait()
    ln_out = (normed * gain_ref[...] + offset_ref[...]).astype(BF16)
    blocks = lane_block((seqs, LANES), depth)
    spread = []
    for place, (weight_ref, bias_ref) in enumerate(
        ((left_w_ref, left_b_ref), (right_w_ref, right_b_ref))
    ):
        weight = jnp.concatenate([weight_ref[...]] * residues, axis=0)
        spread.append(weight)
        bias = jnp.concatenate([bias_ref[...]] * residues, axis=1)
        wide = lax.dot_general(ln_out, weight, NT, preferred_element_type=F32)
        own = pick(blocks, [wide[p * seqs : (p + 1) * seqs] for p in range(residues)])
        both_ref[place] = (own + bias).astype(BF16)
    normed_ref[...] = normed
    inv_std_ref[...] = jnp.broadcast_to(inv_std, inv_std_ref.shape)
    spread_w_ref[...] = jnp.concatenate(spread, axis=0)


def outer_rows(scale, cot, residues, sorted_w_ref, turn_ref):
    columns = cot.shape[0] // residues
    depth = LANES // residues
    flat = lax.dot_general(cot, sorted_w_ref[...], NT, preferred_element_type=F32) * scale
    blocks = lane_block((columns, LANES), depth)
    for tile in range(depth * depth // LANES):
        block = flat[:, tile * LANES : (tile + 1) * LANES]
        turned = [block] + [pltpu.roll(block, depth * t, 1) for t in range(1, residues)]
        for e in range(residues):
            turn_ref[pl.ds(tile * residues + e, columns, stride=depth), :] = pick(
                blocks,
                [
                    turned[(i - e) % residues][i * columns : (i + 1) * columns]
                    for i in range(residues)
                ],
            )
    return turn_ref[...].astype(BF16)


def small_own_kernel(scale, own_ref, other_ref, w_ref, both_ref,
                     keep_ref, outer_near_ref, outer_far_ref, sorted_w_ref, turn_refs, wide_ref):
    residues, columns, _ = own_ref.shape
    depth = LANES // residues
    wide_ref[...] = w_ref[...].astype(F32)
    for d in range(depth):
        sorted_w_ref[d * depth : (d + 1) * depth, :] = wide_ref[
            pl.ds(d, depth, stride=depth), :
        ].astype(BF16)
    rank = lax.axis_index("res")
    own_is_near = lax.axis_index("seq") == lax.shift_right_logical(rank, 2)
    own = own_ref[...].reshape(residues * columns, LANES)
    other = other_ref[...].reshape(residues * columns, LANES)
    near = outer_rows(
        scale, jnp.where(own_is_near, own, other), residues, sorted_w_ref, turn_refs[0]
    )
    outer_near_ref[...] = near
    partial = lax.dot_general(both_ref[0], near, NT, preferred_element_type=F32)
    for place in range(columns // residues):
        keep_ref[lax.bitwise_xor(rank & 3, place)] = partial[:, place * LANES : (place + 1) * LANES]
    outer_far_ref[...] = outer_rows(
        scale, jnp.where(own_is_near, other, own), residues, sorted_w_ref, turn_refs[1]
    )


def small_partner_kernel(scale, residues, got_ref, sorted_w_ref, keep_ref, both_ref,
                         leaving_ref, keep_out_ref, right_ref, turn_ref):
    rank = lax.axis_index("res")
    seqs = got_ref.shape[1]
    cot = got_ref[2:4].reshape(2 * seqs, LANES)
    outer = outer_rows(scale, cot, residues, sorted_w_ref, turn_ref)
    partial = lax.dot_general(got_ref[0], outer, NT, preferred_element_type=F32)
    right_ref[0] = both_ref[1]
    right_ref[1] = got_ref[1]
    for place in range(leaving_ref.shape[0]):
        leaving_ref[place, 0] = both_ref[1]
        leaving_ref[place, 1] = got_ref[1]
    for place in range(leaving_ref.shape[0]):
        distance = lax.bitwise_xor(rank & 3, place)
        total = keep_ref[distance] + partial[:, place * LANES : (place + 1) * LANES]
        leaving_ref[distance, 2] = total.astype(BF16)
        keep_out_ref[distance] = total


def small_grad_kernel(right_ref, outer_near_ref, outer_far_ref, keep_ref, near_refs, normed_ref, inv_std_ref,
                      gain_ref, spread_w_ref, grad_ref):
    ranks, seqs, _ = right_ref.shape
    residues = grad_ref.shape[1]
    depth = LANES // residues
    rank = lax.axis_index("res")
    places = [lax.bitwise_xor(rank & 3, place) for place in range(ranks // 2)]
    right_all = jnp.concatenate(
        [right_ref[place] for place in places] + [right_ref[4 + place] for place in places], axis=1
    )
    outer = jnp.concatenate([outer_near_ref[...], outer_far_ref[...]], axis=0)
    left_cot = jnp.dot(right_all, outer, preferred_element_type=F32)
    right_cot = keep_ref[0]
    for near_ref in near_refs:
        right_cot = right_cot + near_ref[2].astype(F32)
    blocks = lane_block((seqs, LANES), depth)
    spread = jnp.concatenate(
        [
            jnp.concatenate(
                [jnp.where(blocks == place, cot, 0.0) for cot in (left_cot, right_cot)], axis=1
            )
            for place in range(residues)
        ],
        axis=0,
    )
    rows = residues * seqs
    parts = jnp.concatenate(split_three(spread), axis=0)
    ln_cot = jnp.dot(parts, spread_w_ref[...], preferred_element_type=F32)
    ln_cot = ln_cot[0:rows] + (ln_cot[rows : 2 * rows] + ln_cot[2 * rows : 3 * rows])
    gained = ln_cot * gain_ref[...]
    normed = normed_ref[...]
    grad = inv_std_ref[:, 0:1] * (
        gained
        - jnp.mean(gained, axis=-1, keepdims=True)
        - normed * jnp.mean(gained * normed, axis=-1, keepdims=True)
    )
    for place in range(residues):
        grad_ref[:, place, :] = grad[place * seqs : (place + 1) * seqs].astype(BF16)


def small_pair_kernel(scale, right_ref, far_ref, left_ref, sorted_w_ref, offset_ref,
                     pair_ref, turn_ref):
    residues, columns, _ = pair_ref.shape
    depth = LANES // residues
    ranks = columns // residues
    rank = lax.axis_index("res")
    base = lax.axis_index("seq") * ranks
    near, far = [], []
    for place in range(ranks):
        distance = lax.bitwise_xor(rank, base + place)
        near.append(right_ref[distance])
        far.append(far_ref[distance & (ranks - 1)])
    right = jnp.concatenate(
        [jnp.concatenate(near, axis=1), jnp.concatenate(far, axis=1)], axis=0
    )
    left = jnp.concatenate([left_ref[...], far_ref[ranks]], axis=0)
    turn_ref[...] = lax.dot_general(right, left, TN, preferred_element_type=F32) * scale
    blocks = lane_block((columns, LANES), depth)
    tiles = []
    for tile in range(depth * depth // LANES):
        pieces = [
            turn_ref[pl.ds(tile * residues + e, columns, stride=depth), :]
            for e in range(residues)
        ]
        rows = jnp.concatenate(pieces, axis=0)
        turned = [rows] + [pltpu.roll(rows, depth * t, 1) for t in range(1, residues)]
        tiles.append(
            jnp.concatenate(
                [
                    pick(
                        blocks,
                        [
                            turned[(e - i) % residues][e * columns : (e + 1) * columns]
                            for e in range(residues)
                        ],
                    )
                    for i in range(residues)
                ],
                axis=0,
            )
        )
    flat = jnp.concatenate(tiles, axis=1)
    rows = residues * columns
    parts = jnp.concatenate(split_three(flat), axis=0)
    pair = jnp.dot(parts, sorted_w_ref[...], preferred_element_type=F32)
    pair = pair[0:rows] + (pair[rows : 2 * rows] + pair[2 * rows : 3 * rows])
    pair_ref[...] = (pair + offset_ref[...]).astype(BF16).reshape(pair_ref.shape)


def small_slice(
    homolog_matrix,
    standardizer_scaling,
    standardizer_offset,
    left_projection_matrix,
    left_offset_vector,
    right_projection_matrix,
    right_offset_vector,
    coupling_matrix,
    coupling_offset,
    coupling_cotangent,
):
    seqs, residues, features = homolog_matrix.shape
    depth = left_projection_matrix.shape[1]
    ranks = lax.axis_size("res")
    rows = seqs * residues
    scale = 1.0 / (seqs * lax.axis_size("seq"))
    rank = lax.axis_index("res")
    mine = lax.axis_index("seq")
    swap = [(0, 1), (1, 0)]
    limit = pltpu.CompilerParams(vmem_limit_bytes=8 * 1024 * 1024)
    vmem = pl.BlockSpec(memory_space=pltpu.VMEM)
    like = jax.ShapeDtypeStruct

    other_cot = lax.ppermute(coupling_cotangent, "seq", swap)
    hbm = pl.BlockSpec(memory_space=pltpu.HBM)
    pin = lambda array: pltpu.with_memory_space_constraint(array, pltpu.HBM)
    both, normed, inv_std, spread_w, gain, pair_offset, own_cot = pl.pallas_call(
        small_project_kernel,
        in_specs=[hbm] * 9,
        out_specs=[vmem] * 7,
        out_shape=(
            like((2, seqs, LANES), BF16),
            like((rows, features), F32),
            like((rows, LANES), F32),
            like((2 * LANES, features), BF16),
            like((1, features), F32),
            like((1, LANES), F32),
            like(coupling_cotangent.shape, BF16),
        ),
        scratch_shapes=[
            pltpu.VMEM(homolog_matrix.shape, BF16),
            pltpu.VMEM((1, features), F32),
            pltpu.VMEM((depth, features), BF16),
            pltpu.VMEM((1, depth), F32),
            pltpu.VMEM((depth, features), BF16),
            pltpu.VMEM((1, depth), F32),
            pltpu.SemaphoreType.DMA((9,)),
        ],
        compiler_params=limit,
        name="project",
    )(
        *[
            pin(array)
            for array in (
                homolog_matrix,
                standardizer_scaling.reshape(1, -1),
                standardizer_offset.reshape(1, -1),
                left_projection_matrix.T,
                left_offset_vector.reshape(1, -1),
                right_projection_matrix.T,
                right_offset_vector.reshape(1, -1),
                coupling_offset.reshape(1, -1),
                coupling_cotangent,
            )
        ]
    )

    def swap_over(mask, value):
        return lax.ppermute(value, "res", [(source, source ^ mask) for source in range(ranks)])

    own_is_near = mine == lax.shift_right_logical(rank, 2)
    far_cot = jnp.where(own_is_near, other_cot, own_cot).reshape(2, seqs, LANES)
    beyond_two = swap_over(4, jnp.concatenate([both, far_cot]))

    half_rows = ranks // 2 * LANES
    turn = pltpu.VMEM((half_rows, LANES), F32)
    keep, outer_near, outer_far, sorted_w = pl.pallas_call(
        functools.partial(small_own_kernel, scale),
        in_specs=[vmem] * 4,
        out_specs=[vmem] * 4,
        out_shape=(
            like((ranks // 2, seqs, LANES), F32),
            like((half_rows, LANES), BF16),
            like((half_rows, LANES), BF16),
            like(coupling_matrix.shape, BF16),
        ),
        scratch_shapes=[[turn, turn], pltpu.VMEM(coupling_matrix.shape, F32)],
        compiler_params=limit,
        name="own_pieces",
    )(own_cot, other_cot, coupling_matrix, both)

    leaving_parts, keep, right = pl.pallas_call(
        functools.partial(small_partner_kernel, scale, residues),
        in_specs=[vmem] * 4,
        out_specs=[vmem] * 3,
        out_shape=(
            like((ranks // 2, 3, seqs, LANES), BF16),
            like((ranks // 2, seqs, LANES), F32),
            like((2, seqs, LANES), BF16),
        ),
        scratch_shapes=[turn],
        compiler_params=limit,
        name="partner_pieces",
    )(beyond_two, sorted_w, keep, both)

    left = both[0]
    gathered = jnp.concatenate(
        [
            right[0:1],
            jnp.zeros((3, seqs, LANES), BF16),
            right[1:2],
            jnp.zeros((3, seqs, LANES), BF16),
        ]
    )
    near_parts = []
    for mask in (3, 2, 1):
        part = swap_over(mask, leaving_parts[mask])
        near_parts.append(part)
        gathered = lax.dynamic_update_slice_in_dim(gathered, part[0:1], mask, 0)
        gathered = lax.dynamic_update_slice_in_dim(gathered, part[1:2], 4 + mask, 0)

    half = gathered.reshape(2, ranks // 2, seqs, LANES)
    beyond = 1 - lax.bitwise_xor(lax.shift_right_logical(rank, 2), mine)
    leaving = lax.dynamic_index_in_dim(half, beyond, 0, keepdims=False)
    far = lax.ppermute(jnp.concatenate([leaving, left[None]]), "seq", swap)

    gradient = pl.pallas_call(
        small_grad_kernel,
        in_specs=[vmem] * 4 + [[vmem] * 3] + [vmem] * 4,
        out_specs=vmem,
        out_shape=like(homolog_matrix.shape, BF16),
        compiler_params=limit,
        name="gradient",
    )(gathered, outer_near, outer_far, keep, near_parts, normed, inv_std, gain, spread_w)

    pair_delta = pl.pallas_call(
        functools.partial(small_pair_kernel, scale),
        in_specs=[vmem] * 5,
        out_specs=vmem,
        out_shape=like(coupling_cotangent.shape, BF16),
        scratch_shapes=[pltpu.VMEM((ranks // 2 * LANES, LANES), F32)],
        compiler_params=limit,
        name="pair",
    )(gathered, far, left, sorted_w, pair_offset)
    return (pair_delta, gradient)


def body(*arrays):
    if lax.axis_size("res") == 8:
        return small_slice(*arrays)
    return wide_slice(*arrays)


def solution(mesh):
    return jax.shard_map(
        body,
        mesh=mesh,
        in_specs=(
            P(("grp", "seq"), "res", None),
            P(),
            P(),
            P(),
            P(),
            P(),
            P(),
            P(),
            P(),
            P(("grp", "res"), "seq", None),
        ),
        out_specs=(P(("grp", "res"), "seq", None), P(("grp", "seq"), "res", None)),
        check_vma=False,
    )
```

```python
import functools

import jax
import jax.numpy as jnp
from jax import lax
from jax.experimental import pallas as pl
from jax.experimental.pallas import tpu as pltpu
from jax.sharding import PartitionSpec as P

LANES = 128
BF16 = jnp.bfloat16
F32 = jnp.float32
NT = (((1,), (1,)), ((), ()))
TN = (((0,), (0,)), ((), ()))


def lane_block(shape, width):
    return lax.broadcasted_iota(jnp.int32, shape, 1) // width


def pick(blocks, pieces):
    result = pieces[0]
    for place in range(1, len(pieces)):
        result = jnp.where(blocks == place, pieces[place], result)
    return result


def split_three(value):
    top = value.astype(BF16)
    rest = value - top.astype(F32)
    middle = rest.astype(BF16)
    low = (rest - middle.astype(F32)).astype(BF16)
    return top, middle, low


def split_two(value):
    top = value.astype(BF16)
    return top, (value - top.astype(F32)).astype(BF16)


def normalise(rows):
    centred = rows - jnp.mean(rows, axis=-1, keepdims=True)
    inv_std = lax.rsqrt(jnp.mean(centred * centred, axis=-1, keepdims=True) + 1e-05)
    return centred * inv_std, inv_std


def residue_rows(x_ref):
    return jnp.concatenate(
        [x_ref[:, place, :].astype(F32) for place in range(x_ref.shape[1])], axis=0
    )


def project_kernel(
    x_ref, gain_ref, offset_ref, left_w_ref, left_b_ref, right_w_ref, right_b_ref, w_ref,
    left_ref, right_ref, sorted_w_ref, wide_ref,
):
    seqs, residues, _ = x_ref.shape
    depth = left_w_ref.shape[0]
    normed, _ = normalise(residue_rows(x_ref))
    ln_out = (normed * gain_ref[...] + offset_ref[...]).astype(BF16)
    blocks = lane_block((seqs, LANES), depth)
    for weight_ref, bias_ref, out_ref in (
        (left_w_ref, left_b_ref, left_ref),
        (right_w_ref, right_b_ref, right_ref),
    ):
        weight = jnp.concatenate([weight_ref[...]] * residues, axis=0)
        bias = jnp.concatenate([bias_ref[...]] * residues, axis=1)
        wide = lax.dot_general(ln_out, weight, NT, preferred_element_type=F32)
        own = pick(blocks, [wide[p * seqs : (p + 1) * seqs] for p in range(residues)])
        out_ref[...] = (own + bias).astype(BF16)
    wide_ref[...] = w_ref[...].astype(F32)
    for d in range(depth):
        sorted_w_ref[d * depth : (d + 1) * depth, :] = wide_ref[
            pl.ds(d, depth, stride=depth), :
        ].astype(BF16)


def cot_kernel(scale, own_ref, other_ref, sorted_w_ref, left_ref, right_ref,
               send_ref, outer_ref, turn_ref):
    residues, columns, _ = own_ref.shape
    depth = sorted_w_ref.shape[0] // (LANES // residues)
    depth = LANES // residues
    first = lax.axis_index("seq") == 0
    own = own_ref[...].reshape(residues * columns, LANES)
    other = other_ref[...].reshape(residues * columns, LANES)
    low = jnp.where(first, own, other)
    high = jnp.where(first, other, own)
    both = jnp.concatenate([low, high], axis=0)
    flat = lax.dot_general(both, sorted_w_ref[...], NT, preferred_element_type=F32) * scale
    blocks = lane_block((columns, LANES), depth)
    for half in range(2):
        for tile in range(depth * depth // LANES):
            block = flat[
                half * residues * columns : (half + 1) * residues * columns,
                tile * LANES : (tile + 1) * LANES,
            ]
            turned = [block] + [pltpu.roll(block, depth * t, 1) for t in range(1, residues)]
            for e in range(residues):
                piece = pick(
                    blocks,
                    [
                        turned[(i - e) % residues][i * columns : (i + 1) * columns]
                        for i in range(residues)
                    ],
                )
                turn_ref[pl.ds(half * columns * depth + tile * residues + e, columns, stride=depth), :] = piece
    outer = turn_ref[...].astype(BF16)
    half_rows = columns * depth
    partial = lax.dot_general(left_ref[...], outer, NT, preferred_element_type=F32).astype(BF16)
    seqs = left_ref.shape[0]
    ranks = columns // residues
    for half in range(2):
        outer_ref[half] = outer[half * half_rows : (half + 1) * half_rows]
        for rank in range(ranks):
            at = (half * ranks + rank) * LANES
            send_ref[half, rank, 0:seqs, :] = right_ref[...]
            send_ref[half, rank, seqs : 2 * seqs, :] = partial[:, at : at + LANES]


def grad_kernel(steps, got_ref, outer_ref, x_ref, gain_ref, left_w_ref, right_w_ref,
                grad_ref, left_cot_ref, right_cot_ref):
    step = pl.program_id(0)
    _, ranks, twice, _ = got_ref.shape
    seqs = twice // 2
    residues = x_ref.shape[1]
    depth = LANES // residues

    @pl.when(step == 0)
    def _():
        left_cot_ref[...] = jnp.zeros_like(left_cot_ref)
        right_cot_ref[...] = jnp.zeros_like(right_cot_ref)

    places = [(half, rank) for half in range(2) for rank in range(ranks)]
    right_all = jnp.concatenate([got_ref[h, r, 0:seqs, :] for h, r in places], axis=1)
    outer = jnp.concatenate([outer_ref[0], outer_ref[1]], axis=0)
    left_cot_ref[...] += jnp.dot(right_all, outer, preferred_element_type=F32)
    total = got_ref[0, 0, seqs:twice, :].astype(F32)
    for h, r in places[1:]:
        total = total + got_ref[h, r, seqs:twice, :].astype(F32)
    right_cot_ref[...] += total

    @pl.when(step == steps - 1)
    def _():
        blocks = lane_block((seqs, LANES), depth)
        left_cot, right_cot = left_cot_ref[...], right_cot_ref[...]
        spread = jnp.concatenate(
            [
                jnp.concatenate(
                    [
                        jnp.where(blocks == place, left_cot, 0.0),
                        jnp.where(blocks == place, right_cot, 0.0),
                    ],
                    axis=1,
                )
                for place in range(residues)
            ],
            axis=0,
        )
        weight = jnp.concatenate(
            [left_w_ref[...]] * residues + [right_w_ref[...]] * residues, axis=0
        )
        rows = residues * seqs
        parts = jnp.concatenate(split_three(spread), axis=0)
        ln_cot = jnp.dot(parts, weight, preferred_element_type=F32)
        ln_cot = ln_cot[0:rows] + (ln_cot[rows : 2 * rows] + ln_cot[2 * rows : 3 * rows])
        gained = ln_cot * gain_ref[...]
        normed, inv_std = normalise(residue_rows(x_ref))
        grad = inv_std * (
            gained
            - jnp.mean(gained, axis=-1, keepdims=True)
            - normed * jnp.mean(gained * normed, axis=-1, keepdims=True)
        )
        for place in range(residues):
            grad_ref[:, place, :] = grad[place * seqs : (place + 1) * seqs].astype(BF16)


def pair_kernel(scale, got_ref, far_ref, left_ref, far_left_ref, sorted_w_ref, offset_ref,
                pair_ref, turn_ref):
    residues, columns, _ = pair_ref.shape
    depth = LANES // residues
    ranks = columns // residues
    mine = lax.axis_index("seq")
    near = jnp.concatenate([got_ref[mine, r] for r in range(ranks)], axis=1)
    far = jnp.concatenate([far_ref[r] for r in range(ranks)], axis=1)
    right = jnp.concatenate([near, far], axis=0)
    left = jnp.concatenate([left_ref[...], far_left_ref[...]], axis=0)
    turn_ref[...] = lax.dot_general(right, left, TN, preferred_element_type=F32) * scale
    blocks = lane_block((columns, LANES), depth)
    tiles = []
    for tile in range(depth * depth // LANES):
        pieces = [
            turn_ref[pl.ds(tile * residues + e, columns, stride=depth), :]
            for e in range(residues)
        ]
        rows = jnp.concatenate(pieces, axis=0)
        turned = [rows] + [pltpu.roll(rows, depth * t, 1) for t in range(1, residues)]
        tiles.append(
            jnp.concatenate(
                [
                    pick(
                        blocks,
                        [
                            turned[(e - i) % residues][e * columns : (e + 1) * columns]
                            for e in range(residues)
                        ],
                    )
                    for i in range(residues)
                ],
                axis=0,
            )
        )
    flat = jnp.concatenate(tiles, axis=1)
    rows = residues * columns
    parts = jnp.concatenate(split_three(flat), axis=0)
    pair = jnp.dot(parts, sorted_w_ref[...], preferred_element_type=F32)
    pair = pair[0:rows] + (pair[rows : 2 * rows] + pair[2 * rows : 3 * rows])
    pair_ref[...] = (pair + offset_ref[...]).astype(BF16).reshape(pair_ref.shape)


def wide_slice(
    homolog_matrix,
    standardizer_scaling,
    standardizer_offset,
    left_projection_matrix,
    left_offset_vector,
    right_projection_matrix,
    right_offset_vector,
    coupling_matrix,
    coupling_offset,
    coupling_cotangent,
):
    seqs, residues, features = homolog_matrix.shape
    depth = left_projection_matrix.shape[1]
    ranks = lax.axis_size("res")
    scale = 1.0 / (seqs * lax.axis_size("seq"))
    half_ranks = ranks // 2
    half_columns = half_ranks * residues
    step_ranks = 4
    columns = step_ranks * residues
    steps = half_ranks // step_ranks
    mine = lax.axis_index("seq")
    swap = [(0, 1), (1, 0)]

    other_cot = lax.ppermute(coupling_cotangent, "seq", swap)
    gain = standardizer_scaling.reshape(1, -1)
    left_w = left_projection_matrix.T
    right_w = right_projection_matrix.T

    left, right, sorted_w = pl.pallas_call(
        project_kernel,
        out_shape=(
            jax.ShapeDtypeStruct((seqs, LANES), BF16),
            jax.ShapeDtypeStruct((seqs, LANES), BF16),
            jax.ShapeDtypeStruct(coupling_matrix.shape, BF16),
        ),
        scratch_shapes=[pltpu.VMEM(coupling_matrix.shape, F32)],
        name="project",
    )(
        homolog_matrix,
        gain,
        standardizer_offset.reshape(1, -1),
        left_w,
        left_offset_vector.reshape(1, -1),
        right_w,
        right_offset_vector.reshape(1, -1),
        coupling_matrix,
    )

    whole = lambda shape: pl.BlockSpec(shape, lambda g: (0,) * len(shape))
    cot_block = pl.BlockSpec((residues, columns, LANES), lambda g: (0, g, 0))
    outer_block = pl.BlockSpec((2, columns * depth, LANES), lambda g: (0, g, 0))
    send_block = pl.BlockSpec((2, step_ranks, 2 * seqs, LANES), lambda g: (0, g, 0, 0))
    send, outer = pl.pallas_call(
        functools.partial(cot_kernel, scale),
        grid=(steps,),
        in_specs=[
            cot_block,
            cot_block,
            whole(sorted_w.shape),
            whole(left.shape),
            whole(right.shape),
        ],
        out_specs=(send_block, outer_block),
        out_shape=(
            jax.ShapeDtypeStruct((2, half_ranks, 2 * seqs, LANES), BF16),
            jax.ShapeDtypeStruct((2, half_columns * depth, LANES), BF16),
        ),
        scratch_shapes=[pltpu.VMEM((2 * columns * depth, LANES), F32)],
        name="cotangent",
    )(coupling_cotangent, other_cot, sorted_w, left, right)

    got = lax.all_to_all(
        send.reshape(ranks, 2 * seqs, LANES), "res", split_axis=0, concat_axis=0, tiled=True
    ).reshape(send.shape)

    leaving = lax.dynamic_index_in_dim(got, 1 - mine, 0, keepdims=False)[:, 0:seqs, :]
    far = lax.ppermute(jnp.concatenate([leaving, left[None]], axis=0), "seq", swap)

    gradient = pl.pallas_call(
        functools.partial(grad_kernel, steps),
        grid=(steps,),
        in_specs=[
            send_block,
            outer_block,
            whole(homolog_matrix.shape),
            whole(gain.shape),
            whole(left_w.shape),
            whole(right_w.shape),
        ],
        out_specs=whole(homolog_matrix.shape),
        out_shape=jax.ShapeDtypeStruct(homolog_matrix.shape, BF16),
        scratch_shapes=[pltpu.VMEM((seqs, LANES), F32)] * 2,
        name="gradient",
    )(got, outer, homolog_matrix, gain, left_w, right_w)

    pair_delta = pl.pallas_call(
        functools.partial(pair_kernel, scale),
        grid=(steps,),
        in_specs=[
            pl.BlockSpec((2, step_ranks, seqs, LANES), lambda g: (0, g, 0, 0)),
            pl.BlockSpec((step_ranks, seqs, LANES), lambda g: (g, 0, 0)),
            whole(left.shape),
            pl.BlockSpec((None, seqs, LANES), lambda g: (half_ranks, 0, 0)),
            whole(sorted_w.shape),
            whole((1, LANES)),
        ],
        out_specs=cot_block,
        out_shape=jax.ShapeDtypeStruct(coupling_cotangent.shape, BF16),
        scratch_shapes=[pltpu.VMEM((columns * depth, LANES), F32)],
        name="pair",
    )(got, far, left, far, sorted_w, coupling_offset.reshape(1, -1))
    return (pair_delta, gradient)


def fetch(source, target, semaphore):
    copy = pltpu.make_async_copy(source, target, semaphore)
    copy.start()
    return copy


def start_copies(pairs, semaphores):
    copies = [
        pltpu.make_async_copy(source, target, semaphores.at[place])
        for place, (source, target) in enumerate(pairs)
    ]
    for copy in copies:
        copy.start()
    return copies


def small_project_kernel(
    x_hbm, gain_hbm, offset_hbm, left_w_hbm, left_b_hbm, right_w_hbm, right_b_hbm, pair_offset_hbm,
    cot_hbm, both_ref, normed_ref, inv_std_ref, spread_w_ref, gain_ref, pair_offset_ref, cot_ref,
    x_ref, offset_ref, left_w_ref, left_b_ref, right_w_ref, right_b_ref, semaphores,
):
    seqs, residues, _ = x_ref.shape
    depth = left_w_ref.shape[0]
    parts = 4
    part = seqs // parts
    copies = start_copies(
        tuple(
            (x_hbm.at[pl.ds(place * part, part)], x_ref.at[pl.ds(place * part, part)])
            for place in range(parts)
        )
        + (
            (left_w_hbm, left_w_ref),
            (right_w_hbm, right_w_ref),
            (gain_hbm, gain_ref),
            (offset_hbm, offset_ref),
            (left_b_hbm, left_b_ref),
            (right_b_hbm, right_b_ref),
            (cot_hbm, cot_ref),
            (pair_offset_hbm, pair_offset_ref),
        ),
        semaphores,
    )
    for copy in copies[:parts]:
        copy.wait()
    normed, inv_std = normalise(residue_rows(x_ref))
    for copy in copies[parts:]:
        copy.wait()
    ln_out = (normed * gain_ref[...] + offset_ref[...]).astype(BF16)
    blocks = lane_block((seqs, LANES), depth)
    weight = jnp.concatenate(
        [left_w_ref[...]] * residues + [right_w_ref[...]] * residues, axis=0
    )
    wide = lax.dot_general(ln_out, weight, NT, preferred_element_type=F32)
    for place, bias_ref in enumerate((left_b_ref, right_b_ref)):
        bias = jnp.concatenate([bias_ref[...]] * residues, axis=1)
        lanes = wide[:, place * LANES : (place + 1) * LANES]
        own = pick(blocks, [lanes[p * seqs : (p + 1) * seqs] for p in range(residues)])
        both_ref[place] = (own + bias).astype(BF16)
    normed_ref[...] = normed
    inv_std_ref[...] = jnp.broadcast_to(inv_std, inv_std_ref.shape)
    spread_w_ref[...] = weight


def outer_rows(scale, cot, residues, sorted_wt_ref, turn_ref):
    columns = cot.shape[0] // residues
    depth = LANES // residues
    flat = jnp.dot(cot, sorted_wt_ref[...], preferred_element_type=F32) * scale
    blocks = lane_block((columns, LANES), depth)
    for tile in range(depth * depth // LANES):
        block = flat[:, tile * LANES : (tile + 1) * LANES]
        turned = [block] + [pltpu.roll(block, depth * t, 1) for t in range(1, residues)]
        for e in range(residues):
            turn_ref[pl.ds(tile * residues + e, columns, stride=depth), :] = pick(
                blocks,
                [
                    turned[(i - e) % residues][i * columns : (i + 1) * columns]
                    for i in range(residues)
                ],
            )
    return turn_ref[...].astype(BF16)


def small_own_kernel(scale, own_ref, other_ref, w_ref, both_ref,
                     keep_ref, outer_near_ref, outer_far_ref, sorted_w_ref, sorted_wt_ref, turn_refs, wide_ref):
    residues, columns, _ = own_ref.shape
    depth = LANES // residues
    wide_ref[...] = w_ref[...].astype(F32)
    for d in range(depth):
        sorted_w_ref[d * depth : (d + 1) * depth, :] = wide_ref[
            pl.ds(d, depth, stride=depth), :
        ].astype(BF16)
    sorted_wt_ref[...] = sorted_w_ref[...].T
    rank = lax.axis_index("res")
    own_is_near = lax.axis_index("seq") == lax.shift_right_logical(rank, 2)
    own = own_ref[...].reshape(residues * columns, LANES)
    other = other_ref[...].reshape(residues * columns, LANES)
    near = outer_rows(
        scale, jnp.where(own_is_near, own, other), residues, sorted_wt_ref, turn_refs[0]
    )
    outer_near_ref[...] = near
    partial = lax.dot_general(both_ref[0], near, NT, preferred_element_type=F32)
    for place in range(columns // residues):
        keep_ref[lax.bitwise_xor(rank & 3, place)] = partial[:, place * LANES : (place + 1) * LANES]
    outer_far_ref[...] = outer_rows(
        scale, jnp.where(own_is_near, other, own), residues, sorted_wt_ref, turn_refs[1]
    )


def small_partner_kernel(scale, residues, got_ref, sorted_wt_ref, keep_ref, both_ref,
                         leaving_ref, keep_out_ref, right_ref, turn_ref):
    rank = lax.axis_index("res")
    seqs = got_ref.shape[1]
    cot = got_ref[2:4].reshape(2 * seqs, LANES)
    outer = outer_rows(scale, cot, residues, sorted_wt_ref, turn_ref)
    partial = lax.dot_general(got_ref[0], outer, NT, preferred_element_type=F32)
    right_ref[0] = both_ref[1]
    right_ref[1] = got_ref[1]
    for place in range(leaving_ref.shape[0]):
        leaving_ref[place, 0] = both_ref[1]
        leaving_ref[place, 1] = got_ref[1]
    for place in range(leaving_ref.shape[0]):
        distance = lax.bitwise_xor(rank & 3, place)
        total = keep_ref[distance] + partial[:, place * LANES : (place + 1) * LANES]
        leaving_ref[distance, 2] = total.astype(BF16)
        keep_out_ref[distance] = total


def small_grad_kernel(right_ref, outer_near_ref, outer_far_ref, keep_ref, near_refs, normed_ref, inv_std_ref,
                      gain_ref, spread_w_ref, grad_ref):
    ranks, seqs, _ = right_ref.shape
    residues = grad_ref.shape[1]
    depth = LANES // residues
    rank = lax.axis_index("res")
    places = [lax.bitwise_xor(rank & 3, place) for place in range(ranks // 2)]
    right_all = jnp.concatenate(
        [right_ref[place] for place in places] + [right_ref[4 + place] for place in places], axis=1
    )
    outer = jnp.concatenate([outer_near_ref[...], outer_far_ref[...]], axis=0)
    left_cot = jnp.dot(right_all, outer, preferred_element_type=F32)
    right_cot = keep_ref[0]
    for near_ref in near_refs:
        right_cot = right_cot + near_ref[2].astype(F32)
    blocks = lane_block((seqs, LANES), depth)
    spread = jnp.concatenate(
        [
            jnp.concatenate(
                [jnp.where(blocks == place, cot, 0.0) for cot in (left_cot, right_cot)], axis=1
            )
            for place in range(residues)
        ],
        axis=0,
    )
    rows = residues * seqs
    parts = jnp.concatenate(split_two(spread), axis=0)
    ln_cot = jnp.dot(parts, spread_w_ref[...], preferred_element_type=F32)
    ln_cot = ln_cot[0:rows] + ln_cot[rows : 2 * rows]
    gained = ln_cot * gain_ref[...]
    normed = normed_ref[...]
    grad = inv_std_ref[:, 0:1] * (
        gained
        - jnp.mean(gained, axis=-1, keepdims=True)
        - normed * jnp.mean(gained * normed, axis=-1, keepdims=True)
    )
    for place in range(residues):
        grad_ref[:, place, :] = grad[place * seqs : (place + 1) * seqs].astype(BF16)


def small_pair_kernel(scale, right_ref, far_ref, left_ref, sorted_w_ref, offset_ref,
                     pair_ref, turn_ref):
    residues, columns, _ = pair_ref.shape
    depth = LANES // residues
    ranks = columns // residues
    rank = lax.axis_index("res")
    base = lax.axis_index("seq") * ranks
    near, far = [], []
    for place in range(ranks):
        distance = lax.bitwise_xor(rank, base + place)
        near.append(right_ref[distance])
        far.append(far_ref[distance & (ranks - 1)])
    right = jnp.concatenate(
        [jnp.concatenate(near, axis=1), jnp.concatenate(far, axis=1)], axis=0
    )
    left = jnp.concatenate([left_ref[...], far_ref[ranks]], axis=0)
    turn_ref[...] = lax.dot_general(right, left, TN, preferred_element_type=F32) * scale
    blocks = lane_block((columns, LANES), depth)
    tiles = []
    for tile in range(depth * depth // LANES):
        pieces = [
            turn_ref[pl.ds(tile * residues + e, columns, stride=depth), :]
            for e in range(residues)
        ]
        rows = jnp.concatenate(pieces, axis=0)
        turned = [rows] + [pltpu.roll(rows, depth * t, 1) for t in range(1, residues)]
        tiles.append(
            jnp.concatenate(
                [
                    pick(
                        blocks,
                        [
                            turned[(e - i) % residues][e * columns : (e + 1) * columns]
                            for e in range(residues)
                        ],
                    )
                    for i in range(residues)
                ],
                axis=0,
            )
        )
    flat = jnp.concatenate(tiles, axis=1)
    rows = residues * columns
    parts = jnp.concatenate(split_two(flat), axis=0)
    pair = jnp.dot(parts, sorted_w_ref[...], preferred_element_type=F32)
    pair = pair[0:rows] + pair[rows : 2 * rows]
    pair_ref[...] = (pair + offset_ref[...]).astype(BF16).reshape(pair_ref.shape)


def small_slice(
    homolog_matrix,
    standardizer_scaling,
    standardizer_offset,
    left_projection_matrix,
    left_offset_vector,
    right_projection_matrix,
    right_offset_vector,
    coupling_matrix,
    coupling_offset,
    coupling_cotangent,
):
    seqs, residues, features = homolog_matrix.shape
    depth = left_projection_matrix.shape[1]
    ranks = lax.axis_size("res")
    rows = seqs * residues
    scale = 1.0 / (seqs * lax.axis_size("seq"))
    rank = lax.axis_index("res")
    mine = lax.axis_index("seq")
    swap = [(0, 1), (1, 0)]
    limit = pltpu.CompilerParams(vmem_limit_bytes=8 * 1024 * 1024)
    vmem = pl.BlockSpec(memory_space=pltpu.VMEM)
    like = jax.ShapeDtypeStruct

    other_cot = lax.ppermute(coupling_cotangent, "seq", swap)
    hbm = pl.BlockSpec(memory_space=pltpu.HBM)
    pin = lambda array: pltpu.with_memory_space_constraint(array, pltpu.HBM)
    both, normed, inv_std, spread_w, gain, pair_offset, own_cot = pl.pallas_call(
        small_project_kernel,
        in_specs=[hbm] * 9,
        out_specs=[vmem] * 7,
        out_shape=(
            like((2, seqs, LANES), BF16),
            like((rows, features), F32),
            like((rows, LANES), F32),
            like((2 * LANES, features), BF16),
            like((1, features), F32),
            like((1, LANES), F32),
            like(coupling_cotangent.shape, BF16),
        ),
        scratch_shapes=[
            pltpu.VMEM(homolog_matrix.shape, BF16),
            pltpu.VMEM((1, features), F32),
            pltpu.VMEM((depth, features), BF16),
            pltpu.VMEM((1, depth), F32),
            pltpu.VMEM((depth, features), BF16),
            pltpu.VMEM((1, depth), F32),
            pltpu.SemaphoreType.DMA((12,)),
        ],
        compiler_params=limit,
        name="project",
    )(
        *[
            pin(array)
            for array in (
                homolog_matrix,
                standardizer_scaling.reshape(1, -1),
                standardizer_offset.reshape(1, -1),
                left_projection_matrix.T,
                left_offset_vector.reshape(1, -1),
                right_projection_matrix.T,
                right_offset_vector.reshape(1, -1),
                coupling_offset.reshape(1, -1),
                coupling_cotangent,
            )
        ]
    )

    def swap_over(mask, value):
        return lax.ppermute(value, "res", [(source, source ^ mask) for source in range(ranks)])

    own_is_near = mine == lax.shift_right_logical(rank, 2)
    far_cot = jnp.where(own_is_near, other_cot, own_cot).reshape(2, seqs, LANES)
    beyond_two = swap_over(4, jnp.concatenate([both, far_cot]))

    half_rows = ranks // 2 * LANES
    turn = pltpu.VMEM((half_rows, LANES), F32)
    keep, outer_near, outer_far, sorted_w, sorted_wt = pl.pallas_call(
        functools.partial(small_own_kernel, scale),
        in_specs=[vmem] * 4,
        out_specs=[vmem] * 5,
        out_shape=(
            like((ranks // 2, seqs, LANES), F32),
            like((half_rows, LANES), BF16),
            like((half_rows, LANES), BF16),
            like(coupling_matrix.shape, BF16),
            like(coupling_matrix.shape[::-1], BF16),
        ),
        scratch_shapes=[[turn, turn], pltpu.VMEM(coupling_matrix.shape, F32)],
        compiler_params=limit,
        name="own_pieces",
    )(own_cot, other_cot, coupling_matrix, both)

    leaving_parts, keep, right = pl.pallas_call(
        functools.partial(small_partner_kernel, scale, residues),
        in_specs=[vmem] * 4,
        out_specs=[vmem] * 3,
        out_shape=(
            like((ranks // 2, 3, seqs, LANES), BF16),
            like((ranks // 2, seqs, LANES), F32),
            like((2, seqs, LANES), BF16),
        ),
        scratch_shapes=[turn],
        compiler_params=limit,
        name="partner_pieces",
    )(beyond_two, sorted_wt, keep, both)

    left = both[0]
    gathered = jnp.concatenate(
        [
            right[0:1],
            jnp.zeros((3, seqs, LANES), BF16),
            right[1:2],
            jnp.zeros((3, seqs, LANES), BF16),
        ]
    )
    near_parts = []
    for mask in (3, 2, 1):
        part = swap_over(mask, leaving_parts[mask])
        near_parts.append(part)
        gathered = lax.dynamic_update_slice_in_dim(gathered, part[0:1], mask, 0)
        gathered = lax.dynamic_update_slice_in_dim(gathered, part[1:2], 4 + mask, 0)

    half = gathered.reshape(2, ranks // 2, seqs, LANES)
    beyond = 1 - lax.bitwise_xor(lax.shift_right_logical(rank, 2), mine)
    leaving = lax.dynamic_index_in_dim(half, beyond, 0, keepdims=False)
    far = lax.ppermute(jnp.concatenate([leaving, left[None]]), "seq", swap)

    gradient = pl.pallas_call(
        small_grad_kernel,
        in_specs=[vmem] * 4 + [[vmem] * 3] + [vmem] * 4,
        out_specs=vmem,
        out_shape=like(homolog_matrix.shape, BF16),
        compiler_params=limit,
        name="gradient",
    )(gathered, outer_near, outer_far, keep, near_parts, normed, inv_std, gain, spread_w)

    pair_delta = pl.pallas_call(
        functools.partial(small_pair_kernel, scale),
        in_specs=[vmem] * 5,
        out_specs=vmem,
        out_shape=like(coupling_cotangent.shape, BF16),
        scratch_shapes=[pltpu.VMEM((ranks // 2 * LANES, LANES), F32)],
        compiler_params=limit,
        name="pair",
    )(gathered, far, left, sorted_w, pair_offset)
    return (pair_delta, gradient)


def body(*arrays):
    if lax.axis_size("res") == 8:
        return small_slice(*arrays)
    return wide_slice(*arrays)


def solution(mesh):
    return jax.shard_map(
        body,
        mesh=mesh,
        in_specs=(
            P(("grp", "seq"), "res", None),
            P(),
            P(),
            P(),
            P(),
            P(),
            P(),
            P(),
            P(),
            P(("grp", "res"), "seq", None),
        ),
        out_specs=(P(("grp", "res"), "seq", None), P(("grp", "seq"), "res", None)),
        check_vma=False,
    )
```

```python
import functools

import jax
import jax.numpy as jnp
from jax import lax
from jax.experimental import pallas as pl
from jax.experimental.pallas import tpu as pltpu
from jax.sharding import PartitionSpec as P

LANES = 128
BF16 = jnp.bfloat16
F32 = jnp.float32
NT = (((1,), (1,)), ((), ()))
TN = (((0,), (0,)), ((), ()))


def lane_block(shape, width):
    return lax.broadcasted_iota(jnp.int32, shape, 1) // width


def pick(blocks, pieces):
    result = pieces[0]
    for place in range(1, len(pieces)):
        result = jnp.where(blocks == place, pieces[place], result)
    return result


def split_three(value):
    top = value.astype(BF16)
    rest = value - top.astype(F32)
    middle = rest.astype(BF16)
    low = (rest - middle.astype(F32)).astype(BF16)
    return top, middle, low


def split_two(value):
    top = value.astype(BF16)
    return top, (value - top.astype(F32)).astype(BF16)


def normalise(rows):
    centred = rows - jnp.mean(rows, axis=-1, keepdims=True)
    inv_std = lax.rsqrt(jnp.mean(centred * centred, axis=-1, keepdims=True) + 1e-05)
    return centred * inv_std, inv_std


def residue_rows(x_ref):
    return jnp.concatenate(
        [x_ref[:, place, :].astype(F32) for place in range(x_ref.shape[1])], axis=0
    )


def project_kernel(
    x_ref, gain_ref, offset_ref, left_w_ref, left_b_ref, right_w_ref, right_b_ref, w_ref,
    left_ref, right_ref, sorted_w_ref, wide_ref,
):
    seqs, residues, _ = x_ref.shape
    depth = left_w_ref.shape[0]
    normed, _ = normalise(residue_rows(x_ref))
    ln_out = (normed * gain_ref[...] + offset_ref[...]).astype(BF16)
    blocks = lane_block((seqs, LANES), depth)
    for weight_ref, bias_ref, out_ref in (
        (left_w_ref, left_b_ref, left_ref),
        (right_w_ref, right_b_ref, right_ref),
    ):
        weight = jnp.concatenate([weight_ref[...]] * residues, axis=0)
        bias = jnp.concatenate([bias_ref[...]] * residues, axis=1)
        wide = lax.dot_general(ln_out, weight, NT, preferred_element_type=F32)
        own = pick(blocks, [wide[p * seqs : (p + 1) * seqs] for p in range(residues)])
        out_ref[...] = (own + bias).astype(BF16)
    wide_ref[...] = w_ref[...].astype(F32)
    for d in range(depth):
        sorted_w_ref[d * depth : (d + 1) * depth, :] = wide_ref[
            pl.ds(d, depth, stride=depth), :
        ].astype(BF16)


def cot_kernel(scale, own_ref, other_ref, sorted_w_ref, left_ref, right_ref,
               send_ref, outer_ref, turn_ref):
    residues, columns, _ = own_ref.shape
    depth = sorted_w_ref.shape[0] // (LANES // residues)
    depth = LANES // residues
    first = lax.axis_index("seq") == 0
    own = own_ref[...].reshape(residues * columns, LANES)
    other = other_ref[...].reshape(residues * columns, LANES)
    low = jnp.where(first, own, other)
    high = jnp.where(first, other, own)
    both = jnp.concatenate([low, high], axis=0)
    flat = lax.dot_general(both, sorted_w_ref[...], NT, preferred_element_type=F32) * scale
    blocks = lane_block((columns, LANES), depth)
    for half in range(2):
        for tile in range(depth * depth // LANES):
            block = flat[
                half * residues * columns : (half + 1) * residues * columns,
                tile * LANES : (tile + 1) * LANES,
            ]
            turned = [block] + [pltpu.roll(block, depth * t, 1) for t in range(1, residues)]
            for e in range(residues):
                piece = pick(
                    blocks,
                    [
                        turned[(i - e) % residues][i * columns : (i + 1) * columns]
                        for i in range(residues)
                    ],
                )
                turn_ref[pl.ds(half * columns * depth + tile * residues + e, columns, stride=depth), :] = piece
    outer = turn_ref[...].astype(BF16)
    half_rows = columns * depth
    partial = lax.dot_general(left_ref[...], outer, NT, preferred_element_type=F32).astype(BF16)
    seqs = left_ref.shape[0]
    ranks = columns // residues
    for half in range(2):
        outer_ref[half] = outer[half * half_rows : (half + 1) * half_rows]
        for rank in range(ranks):
            at = (half * ranks + rank) * LANES
            send_ref[half, rank, 0:seqs, :] = right_ref[...]
            send_ref[half, rank, seqs : 2 * seqs, :] = partial[:, at : at + LANES]


def grad_kernel(steps, got_ref, outer_ref, x_ref, gain_ref, left_w_ref, right_w_ref,
                grad_ref, left_cot_ref, right_cot_ref):
    step = pl.program_id(0)
    _, ranks, twice, _ = got_ref.shape
    seqs = twice // 2
    residues = x_ref.shape[1]
    depth = LANES // residues

    @pl.when(step == 0)
    def _():
        left_cot_ref[...] = jnp.zeros_like(left_cot_ref)
        right_cot_ref[...] = jnp.zeros_like(right_cot_ref)

    places = [(half, rank) for half in range(2) for rank in range(ranks)]
    right_all = jnp.concatenate([got_ref[h, r, 0:seqs, :] for h, r in places], axis=1)
    outer = jnp.concatenate([outer_ref[0], outer_ref[1]], axis=0)
    left_cot_ref[...] += jnp.dot(right_all, outer, preferred_element_type=F32)
    total = got_ref[0, 0, seqs:twice, :].astype(F32)
    for h, r in places[1:]:
        total = total + got_ref[h, r, seqs:twice, :].astype(F32)
    right_cot_ref[...] += total

    @pl.when(step == steps - 1)
    def _():
        blocks = lane_block((seqs, LANES), depth)
        left_cot, right_cot = left_cot_ref[...], right_cot_ref[...]
        spread = jnp.concatenate(
            [
                jnp.concatenate(
                    [
                        jnp.where(blocks == place, left_cot, 0.0),
                        jnp.where(blocks == place, right_cot, 0.0),
                    ],
                    axis=1,
                )
                for place in range(residues)
            ],
            axis=0,
        )
        weight = jnp.concatenate(
            [left_w_ref[...]] * residues + [right_w_ref[...]] * residues, axis=0
        )
        rows = residues * seqs
        parts = jnp.concatenate(split_three(spread), axis=0)
        ln_cot = jnp.dot(parts, weight, preferred_element_type=F32)
        ln_cot = ln_cot[0:rows] + (ln_cot[rows : 2 * rows] + ln_cot[2 * rows : 3 * rows])
        gained = ln_cot * gain_ref[...]
        normed, inv_std = normalise(residue_rows(x_ref))
        grad = inv_std * (
            gained
            - jnp.mean(gained, axis=-1, keepdims=True)
            - normed * jnp.mean(gained * normed, axis=-1, keepdims=True)
        )
        for place in range(residues):
            grad_ref[:, place, :] = grad[place * seqs : (place + 1) * seqs].astype(BF16)


def pair_kernel(scale, got_ref, far_ref, left_ref, far_left_ref, sorted_w_ref, offset_ref,
                pair_ref, turn_ref):
    residues, columns, _ = pair_ref.shape
    depth = LANES // residues
    ranks = columns // residues
    mine = lax.axis_index("seq")
    near = jnp.concatenate([got_ref[mine, r] for r in range(ranks)], axis=1)
    far = jnp.concatenate([far_ref[r] for r in range(ranks)], axis=1)
    right = jnp.concatenate([near, far], axis=0)
    left = jnp.concatenate([left_ref[...], far_left_ref[...]], axis=0)
    turn_ref[...] = lax.dot_general(right, left, TN, preferred_element_type=F32) * scale
    blocks = lane_block((columns, LANES), depth)
    tiles = []
    for tile in range(depth * depth // LANES):
        pieces = [
            turn_ref[pl.ds(tile * residues + e, columns, stride=depth), :]
            for e in range(residues)
        ]
        rows = jnp.concatenate(pieces, axis=0)
        turned = [rows] + [pltpu.roll(rows, depth * t, 1) for t in range(1, residues)]
        tiles.append(
            jnp.concatenate(
                [
                    pick(
                        blocks,
                        [
                            turned[(e - i) % residues][e * columns : (e + 1) * columns]
                            for e in range(residues)
                        ],
                    )
                    for i in range(residues)
                ],
                axis=0,
            )
        )
    flat = jnp.concatenate(tiles, axis=1)
    rows = residues * columns
    parts = jnp.concatenate(split_three(flat), axis=0)
    pair = jnp.dot(parts, sorted_w_ref[...], preferred_element_type=F32)
    pair = pair[0:rows] + (pair[rows : 2 * rows] + pair[2 * rows : 3 * rows])
    pair_ref[...] = (pair + offset_ref[...]).astype(BF16).reshape(pair_ref.shape)


def wide_slice(
    homolog_matrix,
    standardizer_scaling,
    standardizer_offset,
    left_projection_matrix,
    left_offset_vector,
    right_projection_matrix,
    right_offset_vector,
    coupling_matrix,
    coupling_offset,
    coupling_cotangent,
):
    seqs, residues, features = homolog_matrix.shape
    depth = left_projection_matrix.shape[1]
    ranks = lax.axis_size("res")
    scale = 1.0 / (seqs * lax.axis_size("seq"))
    half_ranks = ranks // 2
    half_columns = half_ranks * residues
    step_ranks = 4
    columns = step_ranks * residues
    steps = half_ranks // step_ranks
    mine = lax.axis_index("seq")
    swap = [(0, 1), (1, 0)]

    other_cot = lax.ppermute(coupling_cotangent, "seq", swap)
    gain = standardizer_scaling.reshape(1, -1)
    left_w = left_projection_matrix.T
    right_w = right_projection_matrix.T

    left, right, sorted_w = pl.pallas_call(
        project_kernel,
        out_shape=(
            jax.ShapeDtypeStruct((seqs, LANES), BF16),
            jax.ShapeDtypeStruct((seqs, LANES), BF16),
            jax.ShapeDtypeStruct(coupling_matrix.shape, BF16),
        ),
        scratch_shapes=[pltpu.VMEM(coupling_matrix.shape, F32)],
        name="project",
    )(
        homolog_matrix,
        gain,
        standardizer_offset.reshape(1, -1),
        left_w,
        left_offset_vector.reshape(1, -1),
        right_w,
        right_offset_vector.reshape(1, -1),
        coupling_matrix,
    )

    whole = lambda shape: pl.BlockSpec(shape, lambda g: (0,) * len(shape))
    cot_block = pl.BlockSpec((residues, columns, LANES), lambda g: (0, g, 0))
    outer_block = pl.BlockSpec((2, columns * depth, LANES), lambda g: (0, g, 0))
    send_block = pl.BlockSpec((2, step_ranks, 2 * seqs, LANES), lambda g: (0, g, 0, 0))
    send, outer = pl.pallas_call(
        functools.partial(cot_kernel, scale),
        grid=(steps,),
        in_specs=[
            cot_block,
            cot_block,
            whole(sorted_w.shape),
            whole(left.shape),
            whole(right.shape),
        ],
        out_specs=(send_block, outer_block),
        out_shape=(
            jax.ShapeDtypeStruct((2, half_ranks, 2 * seqs, LANES), BF16),
            jax.ShapeDtypeStruct((2, half_columns * depth, LANES), BF16),
        ),
        scratch_shapes=[pltpu.VMEM((2 * columns * depth, LANES), F32)],
        name="cotangent",
    )(coupling_cotangent, other_cot, sorted_w, left, right)

    got = lax.all_to_all(
        send.reshape(ranks, 2 * seqs, LANES), "res", split_axis=0, concat_axis=0, tiled=True
    ).reshape(send.shape)

    leaving = lax.dynamic_index_in_dim(got, 1 - mine, 0, keepdims=False)[:, 0:seqs, :]
    far = lax.ppermute(jnp.concatenate([leaving, left[None]], axis=0), "seq", swap)

    gradient = pl.pallas_call(
        functools.partial(grad_kernel, steps),
        grid=(steps,),
        in_specs=[
            send_block,
            outer_block,
            whole(homolog_matrix.shape),
            whole(gain.shape),
            whole(left_w.shape),
            whole(right_w.shape),
        ],
        out_specs=whole(homolog_matrix.shape),
        out_shape=jax.ShapeDtypeStruct(homolog_matrix.shape, BF16),
        scratch_shapes=[pltpu.VMEM((seqs, LANES), F32)] * 2,
        name="gradient",
    )(got, outer, homolog_matrix, gain, left_w, right_w)

    pair_delta = pl.pallas_call(
        functools.partial(pair_kernel, scale),
        grid=(steps,),
        in_specs=[
            pl.BlockSpec((2, step_ranks, seqs, LANES), lambda g: (0, g, 0, 0)),
            pl.BlockSpec((step_ranks, seqs, LANES), lambda g: (g, 0, 0)),
            whole(left.shape),
            pl.BlockSpec((None, seqs, LANES), lambda g: (half_ranks, 0, 0)),
            whole(sorted_w.shape),
            whole((1, LANES)),
        ],
        out_specs=cot_block,
        out_shape=jax.ShapeDtypeStruct(coupling_cotangent.shape, BF16),
        scratch_shapes=[pltpu.VMEM((columns * depth, LANES), F32)],
        name="pair",
    )(got, far, left, far, sorted_w, coupling_offset.reshape(1, -1))
    return (pair_delta, gradient)


def fetch(source, target, semaphore):
    copy = pltpu.make_async_copy(source, target, semaphore)
    copy.start()
    return copy


def start_copies(pairs, semaphores):
    copies = [
        pltpu.make_async_copy(source, target, semaphores.at[place])
        for place, (source, target) in enumerate(pairs)
    ]
    for copy in copies:
        copy.start()
    return copies


def small_project_kernel(
    x_hbm, gain_hbm, offset_hbm, left_w_hbm, left_b_hbm, right_w_hbm, right_b_hbm, pair_offset_hbm,
    cot_hbm, both_ref, normed_ref, inv_std_ref, spread_w_ref, gain_ref, pair_offset_ref, cot_ref,
    x_ref, offset_ref, left_w_ref, left_b_ref, right_w_ref, right_b_ref, semaphores,
):
    seqs, residues, _ = x_ref.shape
    depth = left_w_ref.shape[0]
    parts = 4
    part = seqs // parts
    copies = start_copies(
        tuple(
            (x_hbm.at[pl.ds(place * part, part)], x_ref.at[pl.ds(place * part, part)])
            for place in range(parts)
        )
        + (
            (left_w_hbm, left_w_ref),
            (right_w_hbm, right_w_ref),
            (gain_hbm, gain_ref),
            (offset_hbm, offset_ref),
            (left_b_hbm, left_b_ref),
            (right_b_hbm, right_b_ref),
            (cot_hbm, cot_ref),
            (pair_offset_hbm, pair_offset_ref),
        ),
        semaphores,
    )
    for copy in copies[:parts]:
        copy.wait()
    normed, inv_std = normalise(residue_rows(x_ref))
    for copy in copies[parts:]:
        copy.wait()
    ln_out = (normed * gain_ref[...] + offset_ref[...]).astype(BF16)
    blocks = lane_block((seqs, LANES), depth)
    weight = jnp.concatenate(
        [left_w_ref[...]] * residues + [right_w_ref[...]] * residues, axis=0
    )
    wide = lax.dot_general(ln_out, weight, NT, preferred_element_type=F32)
    for place, bias_ref in enumerate((left_b_ref, right_b_ref)):
        bias = jnp.concatenate([bias_ref[...]] * residues, axis=1)
        lanes = wide[:, place * LANES : (place + 1) * LANES]
        own = pick(blocks, [lanes[p * seqs : (p + 1) * seqs] for p in range(residues)])
        both_ref[place] = (own + bias).astype(BF16)
    normed_ref[...] = normed
    inv_std_ref[...] = jnp.broadcast_to(inv_std, inv_std_ref.shape)
    spread_w_ref[...] = weight


def outer_rows(scale, cot, residues, sorted_wt_ref, turn_ref):
    columns = cot.shape[0] // residues
    depth = LANES // residues
    flat = jnp.dot(cot, sorted_wt_ref[...], preferred_element_type=F32) * scale
    blocks = lane_block((columns, LANES), depth)
    for tile in range(depth * depth // LANES):
        block = flat[:, tile * LANES : (tile + 1) * LANES]
        turned = [block] + [pltpu.roll(block, depth * t, 1) for t in range(1, residues)]
        for e in range(residues):
            turn_ref[pl.ds(tile * residues + e, columns, stride=depth), :] = pick(
                blocks,
                [
                    turned[(i - e) % residues][i * columns : (i + 1) * columns]
                    for i in range(residues)
                ],
            )
    return turn_ref[...].astype(BF16)


def small_own_kernel(scale, own_ref, other_ref, w_ref, both_ref,
                     keep_ref, outer_near_ref, outer_far_ref, sorted_w_ref, sorted_wt_ref, turn_refs, wide_ref):
    residues, columns, _ = own_ref.shape
    depth = LANES // residues
    wide_ref[...] = w_ref[...].astype(F32)
    for d in range(depth):
        sorted_w_ref[d * depth : (d + 1) * depth, :] = wide_ref[
            pl.ds(d, depth, stride=depth), :
        ].astype(BF16)
    sorted_wt_ref[...] = sorted_w_ref[...].T
    rank = lax.axis_index("res")
    own_is_near = lax.axis_index("seq") == lax.shift_right_logical(rank, 2)
    own = own_ref[...].reshape(residues * columns, LANES)
    other = other_ref[...].reshape(residues * columns, LANES)
    near = outer_rows(
        scale, jnp.where(own_is_near, own, other), residues, sorted_wt_ref, turn_refs[0]
    )
    outer_near_ref[...] = near
    partial = lax.dot_general(both_ref[0], near, NT, preferred_element_type=F32)
    for place in range(columns // residues):
        keep_ref[lax.bitwise_xor(rank & 3, place)] = partial[:, place * LANES : (place + 1) * LANES]
    outer_far_ref[...] = outer_rows(
        scale, jnp.where(own_is_near, other, own), residues, sorted_wt_ref, turn_refs[1]
    )


def small_partner_kernel(scale, residues, got_ref, sorted_wt_ref, keep_ref, both_ref,
                         leaving_ref, keep_out_ref, right_ref, swap_ref, turn_ref):
    rank = lax.axis_index("res")
    seqs = got_ref.shape[1]
    cot = got_ref[2:4].reshape(2 * seqs, LANES)
    outer = outer_rows(scale, cot, residues, sorted_wt_ref, turn_ref)
    partial = lax.dot_general(got_ref[0], outer, NT, preferred_element_type=F32)
    right_ref[0] = both_ref[1]
    right_ref[1] = got_ref[1]
    own_is_near = lax.axis_index("seq") == lax.shift_right_logical(rank, 2)
    swap_ref[0] = jnp.where(own_is_near, got_ref[1], both_ref[1])
    swap_ref[1] = both_ref[0]
    for place in range(leaving_ref.shape[0]):
        leaving_ref[place, 0] = both_ref[1]
        leaving_ref[place, 1] = got_ref[1]
    for place in range(leaving_ref.shape[0]):
        distance = lax.bitwise_xor(rank & 3, place)
        total = keep_ref[distance] + partial[:, place * LANES : (place + 1) * LANES]
        leaving_ref[distance, 2] = total.astype(BF16)
        keep_out_ref[distance] = total


def small_finish_kernel(
    scale, right_ref, part_refs, swapped_ref, swapped_late_ref, both_ref, outer_near_ref, outer_far_ref,
    keep_ref, normed_ref, inv_std_ref, gain_ref, spread_w_ref, sorted_w_ref, offset_ref,
    grad_hbm, pair_hbm, grad_ref, pair_ref, near_ref, beyond_ref, turn_ref, semaphores,
):
    seqs, residues, _ = grad_ref.shape
    columns = pair_ref.shape[1]
    depth = LANES // residues
    ranks = columns // residues
    rank = lax.axis_index("res")
    mine = lax.axis_index("seq")
    here = rank & 3

    blocks_of = [right_ref] + list(part_refs)
    right_all = jnp.concatenate(
        [ref[0] for ref in blocks_of] + [ref[1] for ref in blocks_of], axis=1
    )
    spots = [
        pl.ds(pl.multiple_of(lax.bitwise_xor(here, mask) * LANES, LANES), LANES)
        for mask in range(ranks)
    ]
    outer = jnp.concatenate(
        [outer_near_ref[spot, :] for spot in spots] + [outer_far_ref[spot, :] for spot in spots],
        axis=0,
    )
    left_cot = jnp.dot(right_all, outer, preferred_element_type=F32)
    right_cot = keep_ref[0]
    for part_ref in part_refs:
        right_cot = right_cot + part_ref[2].astype(F32)
    blocks = lane_block((seqs, LANES), depth)
    spread = jnp.concatenate(
        [
            jnp.concatenate(
                [jnp.where(blocks == place, cot, 0.0) for cot in (left_cot, right_cot)], axis=1
            )
            for place in range(residues)
        ],
        axis=0,
    )
    rows = residues * seqs
    parts = jnp.concatenate(split_two(spread), axis=0)
    ln_cot = jnp.dot(parts, spread_w_ref[...], preferred_element_type=F32)
    ln_cot = ln_cot[0:rows] + ln_cot[rows : 2 * rows]
    gained = ln_cot * gain_ref[...]
    normed = normed_ref[...]
    grad = inv_std_ref[:, 0:1] * (
        gained
        - jnp.mean(gained, axis=-1, keepdims=True)
        - normed * jnp.mean(gained * normed, axis=-1, keepdims=True)
    )
    for place in range(residues):
        grad_ref[:, place, :] = grad[place * seqs : (place + 1) * seqs].astype(BF16)
    grad_copy = pltpu.make_async_copy(grad_ref, grad_hbm, semaphores.at[0])
    grad_copy.start()

    half = jnp.where(mine == lax.shift_right_logical(rank, 2), 0, 1)
    for mask, ref in enumerate(blocks_of):
        near_ref[mask] = ref[half]
    beyond_ref[0] = swapped_ref[0]
    beyond_ref[1] = part_refs[0][3]
    beyond_ref[2] = part_refs[1][3]
    beyond_ref[3] = swapped_late_ref[...]
    masks = [lax.bitwise_xor(here, place) for place in range(ranks)]
    right = jnp.concatenate(
        [
            jnp.concatenate([ref[mask] for mask in masks], axis=1)
            for ref in (near_ref, beyond_ref)
        ],
        axis=0,
    )
    left = jnp.concatenate([both_ref[0], swapped_ref[1]], axis=0)
    turn_ref[...] = lax.dot_general(right, left, TN, preferred_element_type=F32) * scale
    blocks = lane_block((columns, LANES), depth)
    tiles = []
    for tile in range(depth * depth // LANES):
        pieces = [
            turn_ref[pl.ds(tile * residues + e, columns, stride=depth), :]
            for e in range(residues)
        ]
        lines = jnp.concatenate(pieces, axis=0)
        turned = [lines] + [pltpu.roll(lines, depth * t, 1) for t in range(1, residues)]
        tiles.append(
            jnp.concatenate(
                [
                    pick(
                        blocks,
                        [
                            turned[(e - i) % residues][e * columns : (e + 1) * columns]
                            for e in range(residues)
                        ],
                    )
                    for i in range(residues)
                ],
                axis=0,
            )
        )
    flat = jnp.concatenate(tiles, axis=1)
    rows = residues * columns
    parts = jnp.concatenate(split_two(flat), axis=0)
    pair = jnp.dot(parts, sorted_w_ref[...], preferred_element_type=F32)
    pair = pair[0:rows] + pair[rows : 2 * rows]
    pair_ref[...] = (pair + offset_ref[...]).astype(BF16).reshape(pair_ref.shape)
    pair_copy = pltpu.make_async_copy(pair_ref, pair_hbm, semaphores.at[1])
    pair_copy.start()
    grad_copy.wait()
    pair_copy.wait()


def small_slice(
    homolog_matrix,
    standardizer_scaling,
    standardizer_offset,
    left_projection_matrix,
    left_offset_vector,
    right_projection_matrix,
    right_offset_vector,
    coupling_matrix,
    coupling_offset,
    coupling_cotangent,
):
    seqs, residues, features = homolog_matrix.shape
    depth = left_projection_matrix.shape[1]
    ranks = lax.axis_size("res")
    rows = seqs * residues
    scale = 1.0 / (seqs * lax.axis_size("seq"))
    rank = lax.axis_index("res")
    mine = lax.axis_index("seq")
    swap = [(0, 1), (1, 0)]
    limit = pltpu.CompilerParams(vmem_limit_bytes=8 * 1024 * 1024)
    vmem = pl.BlockSpec(memory_space=pltpu.VMEM)
    like = jax.ShapeDtypeStruct

    other_cot = lax.ppermute(coupling_cotangent, "seq", swap)
    hbm = pl.BlockSpec(memory_space=pltpu.HBM)
    pin = lambda array: pltpu.with_memory_space_constraint(array, pltpu.HBM)
    both, normed, inv_std, spread_w, gain, pair_offset, own_cot = pl.pallas_call(
        small_project_kernel,
        in_specs=[hbm] * 9,
        out_specs=[vmem] * 7,
        out_shape=(
            like((2, seqs, LANES), BF16),
            like((rows, features), F32),
            like((rows, LANES), F32),
            like((2 * LANES, features), BF16),
            like((1, features), F32),
            like((1, LANES), F32),
            like(coupling_cotangent.shape, BF16),
        ),
        scratch_shapes=[
            pltpu.VMEM(homolog_matrix.shape, BF16),
            pltpu.VMEM((1, features), F32),
            pltpu.VMEM((depth, features), BF16),
            pltpu.VMEM((1, depth), F32),
            pltpu.VMEM((depth, features), BF16),
            pltpu.VMEM((1, depth), F32),
            pltpu.SemaphoreType.DMA((12,)),
        ],
        compiler_params=limit,
        name="project",
    )(
        *[
            pin(array)
            for array in (
                homolog_matrix,
                standardizer_scaling.reshape(1, -1),
                standardizer_offset.reshape(1, -1),
                left_projection_matrix.T,
                left_offset_vector.reshape(1, -1),
                right_projection_matrix.T,
                right_offset_vector.reshape(1, -1),
                coupling_offset.reshape(1, -1),
                coupling_cotangent,
            )
        ]
    )

    def swap_over(mask, value):
        return lax.ppermute(value, "res", [(source, source ^ mask) for source in range(ranks)])

    own_is_near = mine == lax.shift_right_logical(rank, 2)
    far_cot = jnp.where(own_is_near, other_cot, own_cot).reshape(2, seqs, LANES)
    beyond_two = swap_over(4, jnp.concatenate([both, far_cot]))

    half_rows = ranks // 2 * LANES
    turn = pltpu.VMEM((half_rows, LANES), F32)
    keep, outer_near, outer_far, sorted_w, sorted_wt = pl.pallas_call(
        functools.partial(small_own_kernel, scale),
        in_specs=[vmem] * 4,
        out_specs=[vmem] * 5,
        out_shape=(
            like((ranks // 2, seqs, LANES), F32),
            like((half_rows, LANES), BF16),
            like((half_rows, LANES), BF16),
            like(coupling_matrix.shape, BF16),
            like(coupling_matrix.shape[::-1], BF16),
        ),
        scratch_shapes=[[turn, turn], pltpu.VMEM(coupling_matrix.shape, F32)],
        compiler_params=limit,
        name="own_pieces",
    )(own_cot, other_cot, coupling_matrix, both)

    leaving_parts, keep, right, leaving = pl.pallas_call(
        functools.partial(small_partner_kernel, scale, residues),
        in_specs=[vmem] * 4,
        out_specs=[vmem] * 4,
        out_shape=(
            like((ranks // 2, 3, seqs, LANES), BF16),
            like((ranks // 2, seqs, LANES), F32),
            like((2, seqs, LANES), BF16),
            like((2, seqs, LANES), BF16),
        ),
        scratch_shapes=[turn],
        compiler_params=limit,
        name="partner_pieces",
    )(beyond_two, sorted_wt, keep, both)

    swapped = lax.ppermute(leaving, "seq", swap)
    diagonal = swap_over(3, leaving_parts[3])
    across, beside = [
        swap_over(mask, jnp.concatenate([leaving_parts[mask], swapped[0:1]])) for mask in (2, 1)
    ]
    swapped_late = lax.ppermute(
        jnp.where(own_is_near, diagonal[1], diagonal[0]), "seq", swap
    )

    pair_delta, gradient = pl.pallas_call(
        functools.partial(small_finish_kernel, scale),
        in_specs=[vmem, [vmem] * 3] + [vmem] * 12,
        out_specs=[pl.BlockSpec(memory_space=pl.ANY)] * 2,
        out_shape=(
            like(homolog_matrix.shape, BF16),
            like(coupling_cotangent.shape, BF16),
        ),
        scratch_shapes=[
            pltpu.VMEM(homolog_matrix.shape, BF16),
            pltpu.VMEM(coupling_cotangent.shape, BF16),
            pltpu.VMEM((ranks // 2, seqs, LANES), BF16),
            pltpu.VMEM((ranks // 2, seqs, LANES), BF16),
            pltpu.VMEM((ranks // 2 * LANES, LANES), F32),
            pltpu.SemaphoreType.DMA((2,)),
        ],
        compiler_params=limit,
        name="finish",
    )(
        right,
        [beside, across, diagonal],
        swapped,
        swapped_late,
        both,
        outer_near,
        outer_far,
        keep,
        normed,
        inv_std,
        gain,
        spread_w,
        sorted_w,
        pair_offset,
    )[::-1]
    return (pair_delta, gradient)


def body(*arrays):
    if lax.axis_size("res") == 8:
        return small_slice(*arrays)
    return wide_slice(*arrays)


def solution(mesh):
    return jax.shard_map(
        body,
        mesh=mesh,
        in_specs=(
            P(("grp", "seq"), "res", None),
            P(),
            P(),
            P(),
            P(),
            P(),
            P(),
            P(),
            P(),
            P(("grp", "res"), "seq", None),
        ),
        out_specs=(P(("grp", "res"), "seq", None), P(("grp", "seq"), "res", None)),
        check_vma=False,
    )
```

```python
import functools

import jax
import jax.numpy as jnp
from jax import lax
from jax.experimental import pallas as pl
from jax.experimental.pallas import tpu as pltpu
from jax.sharding import PartitionSpec as P

LANES = 128
BF16 = jnp.bfloat16
F32 = jnp.float32
NT = (((1,), (1,)), ((), ()))
TN = (((0,), (0,)), ((), ()))


def lane_block(shape, width):
    return lax.broadcasted_iota(jnp.int32, shape, 1) // width


def pick(blocks, pieces):
    result = pieces[0]
    for place in range(1, len(pieces)):
        result = jnp.where(blocks == place, pieces[place], result)
    return result


def split_three(value):
    top = value.astype(BF16)
    rest = value - top.astype(F32)
    middle = rest.astype(BF16)
    low = (rest - middle.astype(F32)).astype(BF16)
    return top, middle, low


def split_two(value):
    top = value.astype(BF16)
    return top, (value - top.astype(F32)).astype(BF16)


def normalise(rows):
    centred = rows - jnp.mean(rows, axis=-1, keepdims=True)
    inv_std = lax.rsqrt(jnp.mean(centred * centred, axis=-1, keepdims=True) + 1e-05)
    return centred * inv_std, inv_std


def residue_rows(x_ref):
    return jnp.concatenate(
        [x_ref[:, place, :].astype(F32) for place in range(x_ref.shape[1])], axis=0
    )


def project_kernel(
    x_ref, gain_ref, offset_ref, left_w_ref, left_b_ref, right_w_ref, right_b_ref, w_ref,
    left_ref, right_ref, sorted_w_ref, wide_ref,
):
    seqs, residues, _ = x_ref.shape
    depth = left_w_ref.shape[0]
    normed, _ = normalise(residue_rows(x_ref))
    ln_out = (normed * gain_ref[...] + offset_ref[...]).astype(BF16)
    blocks = lane_block((seqs, LANES), depth)
    for weight_ref, bias_ref, out_ref in (
        (left_w_ref, left_b_ref, left_ref),
        (right_w_ref, right_b_ref, right_ref),
    ):
        weight = jnp.concatenate([weight_ref[...]] * residues, axis=0)
        bias = jnp.concatenate([bias_ref[...]] * residues, axis=1)
        wide = lax.dot_general(ln_out, weight, NT, preferred_element_type=F32)
        own = pick(blocks, [wide[p * seqs : (p + 1) * seqs] for p in range(residues)])
        out_ref[...] = (own + bias).astype(BF16)
    wide_ref[...] = w_ref[...].astype(F32)
    for d in range(depth):
        sorted_w_ref[d * depth : (d + 1) * depth, :] = wide_ref[
            pl.ds(d, depth, stride=depth), :
        ].astype(BF16)


def cot_kernel(scale, own_ref, other_ref, sorted_w_ref, left_ref, right_ref,
               send_ref, outer_ref, turn_ref):
    residues, columns, _ = own_ref.shape
    depth = sorted_w_ref.shape[0] // (LANES // residues)
    depth = LANES // residues
    first = lax.axis_index("seq") == 0
    own = own_ref[...].reshape(residues * columns, LANES)
    other = other_ref[...].reshape(residues * columns, LANES)
    low = jnp.where(first, own, other)
    high = jnp.where(first, other, own)
    both = jnp.concatenate([low, high], axis=0)
    flat = lax.dot_general(both, sorted_w_ref[...], NT, preferred_element_type=F32) * scale
    blocks = lane_block((columns, LANES), depth)
    for half in range(2):
        for tile in range(depth * depth // LANES):
            block = flat[
                half * residues * columns : (half + 1) * residues * columns,
                tile * LANES : (tile + 1) * LANES,
            ]
            turned = [block] + [pltpu.roll(block, depth * t, 1) for t in range(1, residues)]
            for e in range(residues):
                piece = pick(
                    blocks,
                    [
                        turned[(i - e) % residues][i * columns : (i + 1) * columns]
                        for i in range(residues)
                    ],
                )
                turn_ref[pl.ds(half * columns * depth + tile * residues + e, columns, stride=depth), :] = piece
    outer = turn_ref[...].astype(BF16)
    half_rows = columns * depth
    partial = lax.dot_general(left_ref[...], outer, NT, preferred_element_type=F32).astype(BF16)
    seqs = left_ref.shape[0]
    ranks = columns // residues
    for half in range(2):
        outer_ref[half] = outer[half * half_rows : (half + 1) * half_rows]
        for rank in range(ranks):
            at = (half * ranks + rank) * LANES
            send_ref[half, rank, 0:seqs, :] = right_ref[...]
            send_ref[half, rank, seqs : 2 * seqs, :] = partial[:, at : at + LANES]


def grad_kernel(steps, got_ref, outer_ref, x_ref, gain_ref, left_w_ref, right_w_ref,
                grad_ref, left_cot_ref, right_cot_ref):
    step = pl.program_id(0)
    _, ranks, twice, _ = got_ref.shape
    seqs = twice // 2
    residues = x_ref.shape[1]
    depth = LANES // residues

    @pl.when(step == 0)
    def _():
        left_cot_ref[...] = jnp.zeros_like(left_cot_ref)
        right_cot_ref[...] = jnp.zeros_like(right_cot_ref)

    places = [(half, rank) for half in range(2) for rank in range(ranks)]
    right_all = jnp.concatenate([got_ref[h, r, 0:seqs, :] for h, r in places], axis=1)
    outer = jnp.concatenate([outer_ref[0], outer_ref[1]], axis=0)
    left_cot_ref[...] += jnp.dot(right_all, outer, preferred_element_type=F32)
    total = got_ref[0, 0, seqs:twice, :].astype(F32)
    for h, r in places[1:]:
        total = total + got_ref[h, r, seqs:twice, :].astype(F32)
    right_cot_ref[...] += total

    @pl.when(step == steps - 1)
    def _():
        blocks = lane_block((seqs, LANES), depth)
        left_cot, right_cot = left_cot_ref[...], right_cot_ref[...]
        spread = jnp.concatenate(
            [
                jnp.concatenate(
                    [
                        jnp.where(blocks == place, left_cot, 0.0),
                        jnp.where(blocks == place, right_cot, 0.0),
                    ],
                    axis=1,
                )
                for place in range(residues)
            ],
            axis=0,
        )
        weight = jnp.concatenate(
            [left_w_ref[...]] * residues + [right_w_ref[...]] * residues, axis=0
        )
        rows = residues * seqs
        parts = jnp.concatenate(split_three(spread), axis=0)
        ln_cot = jnp.dot(parts, weight, preferred_element_type=F32)
        ln_cot = ln_cot[0:rows] + (ln_cot[rows : 2 * rows] + ln_cot[2 * rows : 3 * rows])
        gained = ln_cot * gain_ref[...]
        normed, inv_std = normalise(residue_rows(x_ref))
        grad = inv_std * (
            gained
            - jnp.mean(gained, axis=-1, keepdims=True)
            - normed * jnp.mean(gained * normed, axis=-1, keepdims=True)
        )
        for place in range(residues):
            grad_ref[:, place, :] = grad[place * seqs : (place + 1) * seqs].astype(BF16)


def pair_kernel(scale, got_ref, far_ref, left_ref, far_left_ref, sorted_w_ref, offset_ref,
                pair_ref, turn_ref):
    residues, columns, _ = pair_ref.shape
    depth = LANES // residues
    ranks = columns // residues
    mine = lax.axis_index("seq")
    near = jnp.concatenate([got_ref[mine, r] for r in range(ranks)], axis=1)
    far = jnp.concatenate([far_ref[r] for r in range(ranks)], axis=1)
    right = jnp.concatenate([near, far], axis=0)
    left = jnp.concatenate([left_ref[...], far_left_ref[...]], axis=0)
    turn_ref[...] = lax.dot_general(right, left, TN, preferred_element_type=F32) * scale
    blocks = lane_block((columns, LANES), depth)
    tiles = []
    for tile in range(depth * depth // LANES):
        pieces = [
            turn_ref[pl.ds(tile * residues + e, columns, stride=depth), :]
            for e in range(residues)
        ]
        rows = jnp.concatenate(pieces, axis=0)
        turned = [rows] + [pltpu.roll(rows, depth * t, 1) for t in range(1, residues)]
        tiles.append(
            jnp.concatenate(
                [
                    pick(
                        blocks,
                        [
                            turned[(e - i) % residues][e * columns : (e + 1) * columns]
                            for e in range(residues)
                        ],
                    )
                    for i in range(residues)
                ],
                axis=0,
            )
        )
    flat = jnp.concatenate(tiles, axis=1)
    rows = residues * columns
    parts = jnp.concatenate(split_three(flat), axis=0)
    pair = jnp.dot(parts, sorted_w_ref[...], preferred_element_type=F32)
    pair = pair[0:rows] + (pair[rows : 2 * rows] + pair[2 * rows : 3 * rows])
    pair_ref[...] = (pair + offset_ref[...]).astype(BF16).reshape(pair_ref.shape)


def wide_slice(
    homolog_matrix,
    standardizer_scaling,
    standardizer_offset,
    left_projection_matrix,
    left_offset_vector,
    right_projection_matrix,
    right_offset_vector,
    coupling_matrix,
    coupling_offset,
    coupling_cotangent,
):
    seqs, residues, features = homolog_matrix.shape
    depth = left_projection_matrix.shape[1]
    ranks = lax.axis_size("res")
    scale = 1.0 / (seqs * lax.axis_size("seq"))
    half_ranks = ranks // 2
    half_columns = half_ranks * residues
    step_ranks = 4
    columns = step_ranks * residues
    steps = half_ranks // step_ranks
    mine = lax.axis_index("seq")
    swap = [(0, 1), (1, 0)]

    other_cot = lax.ppermute(coupling_cotangent, "seq", swap)
    gain = standardizer_scaling.reshape(1, -1)
    left_w = left_projection_matrix.T
    right_w = right_projection_matrix.T

    left, right, sorted_w = pl.pallas_call(
        project_kernel,
        out_shape=(
            jax.ShapeDtypeStruct((seqs, LANES), BF16),
            jax.ShapeDtypeStruct((seqs, LANES), BF16),
            jax.ShapeDtypeStruct(coupling_matrix.shape, BF16),
        ),
        scratch_shapes=[pltpu.VMEM(coupling_matrix.shape, F32)],
        name="project",
    )(
        homolog_matrix,
        gain,
        standardizer_offset.reshape(1, -1),
        left_w,
        left_offset_vector.reshape(1, -1),
        right_w,
        right_offset_vector.reshape(1, -1),
        coupling_matrix,
    )

    whole = lambda shape: pl.BlockSpec(shape, lambda g: (0,) * len(shape))
    cot_block = pl.BlockSpec((residues, columns, LANES), lambda g: (0, g, 0))
    outer_block = pl.BlockSpec((2, columns * depth, LANES), lambda g: (0, g, 0))
    send_block = pl.BlockSpec((2, step_ranks, 2 * seqs, LANES), lambda g: (0, g, 0, 0))
    send, outer = pl.pallas_call(
        functools.partial(cot_kernel, scale),
        grid=(steps,),
        in_specs=[
            cot_block,
            cot_block,
            whole(sorted_w.shape),
            whole(left.shape),
            whole(right.shape),
        ],
        out_specs=(send_block, outer_block),
        out_shape=(
            jax.ShapeDtypeStruct((2, half_ranks, 2 * seqs, LANES), BF16),
            jax.ShapeDtypeStruct((2, half_columns * depth, LANES), BF16),
        ),
        scratch_shapes=[pltpu.VMEM((2 * columns * depth, LANES), F32)],
        name="cotangent",
    )(coupling_cotangent, other_cot, sorted_w, left, right)

    got = lax.all_to_all(
        send.reshape(ranks, 2 * seqs, LANES), "res", split_axis=0, concat_axis=0, tiled=True
    ).reshape(send.shape)

    leaving = lax.dynamic_index_in_dim(got, 1 - mine, 0, keepdims=False)[:, 0:seqs, :]
    far = lax.ppermute(jnp.concatenate([leaving, left[None]], axis=0), "seq", swap)

    gradient = pl.pallas_call(
        functools.partial(grad_kernel, steps),
        grid=(steps,),
        in_specs=[
            send_block,
            outer_block,
            whole(homolog_matrix.shape),
            whole(gain.shape),
            whole(left_w.shape),
            whole(right_w.shape),
        ],
        out_specs=whole(homolog_matrix.shape),
        out_shape=jax.ShapeDtypeStruct(homolog_matrix.shape, BF16),
        scratch_shapes=[pltpu.VMEM((seqs, LANES), F32)] * 2,
        name="gradient",
    )(got, outer, homolog_matrix, gain, left_w, right_w)

    pair_delta = pl.pallas_call(
        functools.partial(pair_kernel, scale),
        grid=(steps,),
        in_specs=[
            pl.BlockSpec((2, step_ranks, seqs, LANES), lambda g: (0, g, 0, 0)),
            pl.BlockSpec((step_ranks, seqs, LANES), lambda g: (g, 0, 0)),
            whole(left.shape),
            pl.BlockSpec((None, seqs, LANES), lambda g: (half_ranks, 0, 0)),
            whole(sorted_w.shape),
            whole((1, LANES)),
        ],
        out_specs=cot_block,
        out_shape=jax.ShapeDtypeStruct(coupling_cotangent.shape, BF16),
        scratch_shapes=[pltpu.VMEM((columns * depth, LANES), F32)],
        name="pair",
    )(got, far, left, far, sorted_w, coupling_offset.reshape(1, -1))
    return (pair_delta, gradient)


def fetch(source, target, semaphore):
    copy = pltpu.make_async_copy(source, target, semaphore)
    copy.start()
    return copy


def start_copies(pairs, semaphores):
    copies = [
        pltpu.make_async_copy(source, target, semaphores.at[place])
        for place, (source, target) in enumerate(pairs)
    ]
    for copy in copies:
        copy.start()
    return copies


def small_project_kernel(
    x_hbm, gain_hbm, offset_hbm, left_w_hbm, left_b_hbm, right_w_hbm, right_b_hbm, pair_offset_hbm,
    cot_hbm, both_ref, normed_ref, inv_std_ref, spread_w_ref, gain_ref, pair_offset_ref, cot_ref,
    x_ref, offset_ref, left_w_ref, left_b_ref, right_w_ref, right_b_ref, semaphores,
):
    seqs, residues, _ = x_ref.shape
    depth = left_w_ref.shape[0]
    parts = 4
    part = seqs // parts
    copies = start_copies(
        tuple(
            (x_hbm.at[pl.ds(place * part, part)], x_ref.at[pl.ds(place * part, part)])
            for place in range(parts)
        )
        + (
            (left_w_hbm, left_w_ref),
            (right_w_hbm, right_w_ref),
            (gain_hbm, gain_ref),
            (offset_hbm, offset_ref),
            (left_b_hbm, left_b_ref),
            (right_b_hbm, right_b_ref),
            (cot_hbm, cot_ref),
            (pair_offset_hbm, pair_offset_ref),
        ),
        semaphores,
    )
    for copy in copies[:parts]:
        copy.wait()
    normed, inv_std = normalise(residue_rows(x_ref))
    for copy in copies[parts:]:
        copy.wait()
    ln_out = (normed * gain_ref[...] + offset_ref[...]).astype(BF16)
    blocks = lane_block((seqs, LANES), depth)
    weight = jnp.concatenate(
        [left_w_ref[...]] * residues + [right_w_ref[...]] * residues, axis=0
    )
    wide = lax.dot_general(ln_out, weight, NT, preferred_element_type=F32)
    for place, bias_ref in enumerate((left_b_ref, right_b_ref)):
        bias = jnp.concatenate([bias_ref[...]] * residues, axis=1)
        lanes = wide[:, place * LANES : (place + 1) * LANES]
        own = pick(blocks, [lanes[p * seqs : (p + 1) * seqs] for p in range(residues)])
        both_ref[place] = (own + bias).astype(BF16)
    normed_ref[...] = normed
    inv_std_ref[...] = jnp.broadcast_to(inv_std, inv_std_ref.shape)
    spread_w_ref[...] = weight


def outer_rows(scale, cot, residues, sorted_wt_ref, turn_ref):
    columns = cot.shape[0] // residues
    depth = LANES // residues
    flat = jnp.dot(cot, sorted_wt_ref[...], preferred_element_type=F32) * scale
    blocks = lane_block((columns, LANES), depth)
    for tile in range(depth * depth // LANES):
        block = flat[:, tile * LANES : (tile + 1) * LANES]
        turned = [block] + [pltpu.roll(block, depth * t, 1) for t in range(1, residues)]
        for e in range(residues):
            turn_ref[pl.ds(tile * residues + e, columns, stride=depth), :] = pick(
                blocks,
                [
                    turned[(i - e) % residues][i * columns : (i + 1) * columns]
                    for i in range(residues)
                ],
            )
    return turn_ref[...].astype(BF16)


def small_own_kernel(scale, own_ref, other_ref, w_ref, both_ref,
                     keep_ref, outer_near_ref, outer_far_ref, sorted_w_ref, sorted_wt_ref, turn_refs, wide_ref):
    residues, columns, _ = own_ref.shape
    depth = LANES // residues
    wide_ref[...] = w_ref[...].astype(F32)
    for d in range(depth):
        sorted_w_ref[d * depth : (d + 1) * depth, :] = wide_ref[
            pl.ds(d, depth, stride=depth), :
        ].astype(BF16)
    sorted_wt_ref[...] = sorted_w_ref[...].T
    rank = lax.axis_index("res")
    own_is_near = lax.axis_index("seq") == lax.shift_right_logical(rank, 2)
    own = own_ref[...].reshape(residues * columns, LANES)
    other = other_ref[...].reshape(residues * columns, LANES)
    near = outer_rows(
        scale, jnp.where(own_is_near, own, other), residues, sorted_wt_ref, turn_refs[0]
    )
    outer_near_ref[...] = near
    partial = lax.dot_general(both_ref[0], near, NT, preferred_element_type=F32)
    for place in range(columns // residues):
        keep_ref[lax.bitwise_xor(rank & 3, place)] = partial[:, place * LANES : (place + 1) * LANES]
    outer_far_ref[...] = outer_rows(
        scale, jnp.where(own_is_near, other, own), residues, sorted_wt_ref, turn_refs[1]
    )


def small_partner_kernel(scale, residues, got_ref, sorted_wt_ref, keep_ref, both_ref,
                         leaving_ref, keep_out_ref, right_ref, swap_ref, turn_ref):
    rank = lax.axis_index("res")
    seqs = got_ref.shape[1]
    cot = got_ref[2:4].reshape(2 * seqs, LANES)
    outer = outer_rows(scale, cot, residues, sorted_wt_ref, turn_ref)
    partial = lax.dot_general(got_ref[0], outer, NT, preferred_element_type=F32)
    right_ref[0] = both_ref[1]
    right_ref[1] = got_ref[1]
    own_is_near = lax.axis_index("seq") == lax.shift_right_logical(rank, 2)
    swap_ref[0] = jnp.where(own_is_near, got_ref[1], both_ref[1])
    swap_ref[1] = both_ref[0]
    for place in range(leaving_ref.shape[0]):
        leaving_ref[place, 0] = both_ref[1]
        leaving_ref[place, 1] = got_ref[1]
    for place in range(leaving_ref.shape[0]):
        distance = lax.bitwise_xor(rank & 3, place)
        total = keep_ref[distance] + partial[:, place * LANES : (place + 1) * LANES]
        leaving_ref[distance, 2] = total.astype(BF16)
        keep_out_ref[distance] = total


def small_finish_kernel(
    scale, right_ref, part_refs, swapped_ref, swapped_late_ref, both_ref, outer_near_ref, outer_far_ref,
    keep_ref, normed_ref, inv_std_ref, gain_ref, spread_w_ref, sorted_w_ref, offset_ref,
    grad_hbm, pair_hbm, grad_ref, pair_ref, near_ref, beyond_ref, turn_ref, semaphores,
):
    seqs, residues, _ = grad_ref.shape
    columns = pair_ref.shape[1]
    depth = LANES // residues
    ranks = columns // residues
    rank = lax.axis_index("res")
    mine = lax.axis_index("seq")
    here = rank & 3

    blocks_of = [right_ref] + list(part_refs)
    right_all = jnp.concatenate(
        [ref[0] for ref in blocks_of] + [ref[1] for ref in blocks_of], axis=1
    )
    spots = [
        pl.ds(pl.multiple_of(lax.bitwise_xor(here, mask) * LANES, LANES), LANES)
        for mask in range(ranks)
    ]
    outer = jnp.concatenate(
        [outer_near_ref[spot, :] for spot in spots] + [outer_far_ref[spot, :] for spot in spots],
        axis=0,
    )
    left_cot = jnp.dot(right_all, outer, preferred_element_type=F32)
    right_cot = keep_ref[0]
    for part_ref in part_refs:
        right_cot = right_cot + part_ref[2].astype(F32)
    blocks = lane_block((seqs, LANES), depth)
    spread = jnp.concatenate(
        [
            jnp.concatenate(
                [jnp.where(blocks == place, cot, 0.0) for cot in (left_cot, right_cot)], axis=1
            )
            for place in range(residues)
        ],
        axis=0,
    )
    rows = residues * seqs
    parts = jnp.concatenate(split_two(spread), axis=0)
    ln_cot = jnp.dot(parts, spread_w_ref[...], preferred_element_type=F32)
    ln_cot = ln_cot[0:rows] + ln_cot[rows : 2 * rows]
    gained = ln_cot * gain_ref[...]
    normed = normed_ref[...]
    grad = inv_std_ref[:, 0:1] * (
        gained
        - jnp.mean(gained, axis=-1, keepdims=True)
        - normed * jnp.mean(gained * normed, axis=-1, keepdims=True)
    )
    for place in range(residues):
        grad_ref[:, place, :] = grad[place * seqs : (place + 1) * seqs].astype(BF16)

    half = jnp.where(mine == lax.shift_right_logical(rank, 2), 0, 1)
    for mask, ref in enumerate(blocks_of):
        near_ref[mask] = ref[half]
    beyond_ref[0] = swapped_ref[0]
    beyond_ref[1] = part_refs[0][3]
    beyond_ref[2] = part_refs[1][3]
    beyond_ref[3] = swapped_late_ref[...]
    masks = [lax.bitwise_xor(here, place) for place in range(ranks)]
    right = jnp.concatenate(
        [
            jnp.concatenate([ref[mask] for mask in masks], axis=1)
            for ref in (near_ref, beyond_ref)
        ],
        axis=0,
    )
    left = jnp.concatenate([both_ref[0], swapped_ref[1]], axis=0)
    turn_ref[...] = lax.dot_general(right, left, TN, preferred_element_type=F32) * scale
    blocks = lane_block((columns, LANES), depth)
    tiles = []
    for tile in range(depth * depth // LANES):
        pieces = [
            turn_ref[pl.ds(tile * residues + e, columns, stride=depth), :]
            for e in range(residues)
        ]
        lines = jnp.concatenate(pieces, axis=0)
        turned = [lines] + [pltpu.roll(lines, depth * t, 1) for t in range(1, residues)]
        tiles.append(
            jnp.concatenate(
                [
                    pick(
                        blocks,
                        [
                            turned[(e - i) % residues][e * columns : (e + 1) * columns]
                            for e in range(residues)
                        ],
                    )
                    for i in range(residues)
                ],
                axis=0,
            )
        )
    flat = jnp.concatenate(tiles, axis=1)
    rows = residues * columns
    parts = jnp.concatenate(split_two(flat), axis=0)
    pair = jnp.dot(parts, sorted_w_ref[...], preferred_element_type=F32)
    pair = pair[0:rows] + pair[rows : 2 * rows]
    pair_ref[...] = (pair + offset_ref[...]).astype(BF16).reshape(pair_ref.shape)
    copies = start_copies(((grad_ref, grad_hbm), (pair_ref, pair_hbm)), semaphores)
    for copy in copies:
        copy.wait()


def small_slice(
    homolog_matrix,
    standardizer_scaling,
    standardizer_offset,
    left_projection_matrix,
    left_offset_vector,
    right_projection_matrix,
    right_offset_vector,
    coupling_matrix,
    coupling_offset,
    coupling_cotangent,
):
    seqs, residues, features = homolog_matrix.shape
    depth = left_projection_matrix.shape[1]
    ranks = lax.axis_size("res")
    rows = seqs * residues
    scale = 1.0 / (seqs * lax.axis_size("seq"))
    rank = lax.axis_index("res")
    mine = lax.axis_index("seq")
    swap = [(0, 1), (1, 0)]
    limit = pltpu.CompilerParams(vmem_limit_bytes=8 * 1024 * 1024)
    vmem = pl.BlockSpec(memory_space=pltpu.VMEM)
    like = jax.ShapeDtypeStruct

    other_cot = lax.ppermute(coupling_cotangent, "seq", swap)
    hbm = pl.BlockSpec(memory_space=pltpu.HBM)
    pin = lambda array: pltpu.with_memory_space_constraint(array, pltpu.HBM)
    both, normed, inv_std, spread_w, gain, pair_offset, own_cot = pl.pallas_call(
        small_project_kernel,
        in_specs=[hbm] * 9,
        out_specs=[vmem] * 7,
        out_shape=(
            like((2, seqs, LANES), BF16),
            like((rows, features), F32),
            like((rows, LANES), F32),
            like((2 * LANES, features), BF16),
            like((1, features), F32),
            like((1, LANES), F32),
            like(coupling_cotangent.shape, BF16),
        ),
        scratch_shapes=[
            pltpu.VMEM(homolog_matrix.shape, BF16),
            pltpu.VMEM((1, features), F32),
            pltpu.VMEM((depth, features), BF16),
            pltpu.VMEM((1, depth), F32),
            pltpu.VMEM((depth, features), BF16),
            pltpu.VMEM((1, depth), F32),
            pltpu.SemaphoreType.DMA((12,)),
        ],
        compiler_params=limit,
        name="project",
    )(
        *[
            pin(array)
            for array in (
                homolog_matrix,
                standardizer_scaling.reshape(1, -1),
                standardizer_offset.reshape(1, -1),
                left_projection_matrix.T,
                left_offset_vector.reshape(1, -1),
                right_projection_matrix.T,
                right_offset_vector.reshape(1, -1),
                coupling_offset.reshape(1, -1),
                coupling_cotangent,
            )
        ]
    )

    def swap_over(mask, value):
        return lax.ppermute(value, "res", [(source, source ^ mask) for source in range(ranks)])

    own_is_near = mine == lax.shift_right_logical(rank, 2)
    far_cot = jnp.where(own_is_near, other_cot, own_cot).reshape(2, seqs, LANES)
    beyond_two = swap_over(4, jnp.concatenate([both, far_cot]))

    half_rows = ranks // 2 * LANES
    turn = pltpu.VMEM((half_rows, LANES), F32)
    keep, outer_near, outer_far, sorted_w, sorted_wt = pl.pallas_call(
        functools.partial(small_own_kernel, scale),
        in_specs=[vmem] * 4,
        out_specs=[vmem] * 5,
        out_shape=(
            like((ranks // 2, seqs, LANES), F32),
            like((half_rows, LANES), BF16),
            like((half_rows, LANES), BF16),
            like(coupling_matrix.shape, BF16),
            like(coupling_matrix.shape[::-1], BF16),
        ),
        scratch_shapes=[[turn, turn], pltpu.VMEM(coupling_matrix.shape, F32)],
        compiler_params=limit,
        name="own_pieces",
    )(own_cot, other_cot, coupling_matrix, both)

    leaving_parts, keep, right, leaving = pl.pallas_call(
        functools.partial(small_partner_kernel, scale, residues),
        in_specs=[vmem] * 4,
        out_specs=[vmem] * 4,
        out_shape=(
            like((ranks // 2, 3, seqs, LANES), BF16),
            like((ranks // 2, seqs, LANES), F32),
            like((2, seqs, LANES), BF16),
            like((2, seqs, LANES), BF16),
        ),
        scratch_shapes=[turn],
        compiler_params=limit,
        name="partner_pieces",
    )(beyond_two, sorted_wt, keep, both)

    swapped = lax.ppermute(leaving, "seq", swap)
    diagonal = swap_over(3, leaving_parts[3])
    across, beside = [
        swap_over(mask, jnp.concatenate([leaving_parts[mask], swapped[0:1]])) for mask in (2, 1)
    ]
    swapped_late = lax.ppermute(
        jnp.where(own_is_near, diagonal[1], diagonal[0]), "seq", swap
    )

    pair_delta, gradient = pl.pallas_call(
        functools.partial(small_finish_kernel, scale),
        in_specs=[vmem, [vmem] * 3] + [vmem] * 12,
        out_specs=[pl.BlockSpec(memory_space=pl.ANY)] * 2,
        out_shape=(
            like(homolog_matrix.shape, BF16),
            like(coupling_cotangent.shape, BF16),
        ),
        scratch_shapes=[
            pltpu.VMEM(homolog_matrix.shape, BF16),
            pltpu.VMEM(coupling_cotangent.shape, BF16),
            pltpu.VMEM((ranks // 2, seqs, LANES), BF16),
            pltpu.VMEM((ranks // 2, seqs, LANES), BF16),
            pltpu.VMEM((ranks // 2 * LANES, LANES), F32),
            pltpu.SemaphoreType.DMA((2,)),
        ],
        compiler_params=limit,
        name="finish",
    )(
        right,
        [beside, across, diagonal],
        swapped,
        swapped_late,
        both,
        outer_near,
        outer_far,
        keep,
        normed,
        inv_std,
        gain,
        spread_w,
        sorted_w,
        pair_offset,
    )[::-1]
    return (pair_delta, gradient)


def body(*arrays):
    if lax.axis_size("res") == 8:
        return small_slice(*arrays)
    return wide_slice(*arrays)


def solution(mesh):
    return jax.shard_map(
        body,
        mesh=mesh,
        in_specs=(
            P(("grp", "seq"), "res", None),
            P(),
            P(),
            P(),
            P(),
            P(),
            P(),
            P(),
            P(),
            P(("grp", "res"), "seq", None),
        ),
        out_specs=(P(("grp", "res"), "seq", None), P(("grp", "seq"), "res", None)),
        check_vma=False,
    )
```

```python
import functools

import jax
import jax.numpy as jnp
from jax import lax
from jax.experimental import pallas as pl
from jax.experimental.pallas import tpu as pltpu
from jax.sharding import PartitionSpec as P

LANES = 128
BF16 = jnp.bfloat16
F32 = jnp.float32
NT = (((1,), (1,)), ((), ()))
TN = (((0,), (0,)), ((), ()))


def lane_block(shape, width):
    return lax.broadcasted_iota(jnp.int32, shape, 1) // width


def pick(blocks, pieces):
    result = pieces[0]
    for place in range(1, len(pieces)):
        result = jnp.where(blocks == place, pieces[place], result)
    return result


def split_three(value):
    top = value.astype(BF16)
    rest = value - top.astype(F32)
    middle = rest.astype(BF16)
    low = (rest - middle.astype(F32)).astype(BF16)
    return top, middle, low


def split_two(value):
    top = value.astype(BF16)
    return top, (value - top.astype(F32)).astype(BF16)


def normalise(rows):
    centred = rows - jnp.mean(rows, axis=-1, keepdims=True)
    inv_std = lax.rsqrt(jnp.mean(centred * centred, axis=-1, keepdims=True) + 1e-05)
    return centred * inv_std, inv_std


def residue_rows(x_ref):
    return jnp.concatenate(
        [x_ref[:, place, :].astype(F32) for place in range(x_ref.shape[1])], axis=0
    )


def project_kernel(
    x_ref, gain_ref, offset_ref, left_w_ref, left_b_ref, right_w_ref, right_b_ref, w_ref,
    left_ref, right_ref, sorted_w_ref, wide_ref,
):
    seqs, residues, _ = x_ref.shape
    depth = left_w_ref.shape[0]
    normed, _ = normalise(residue_rows(x_ref))
    ln_out = (normed * gain_ref[...] + offset_ref[...]).astype(BF16)
    blocks = lane_block((seqs, LANES), depth)
    for weight_ref, bias_ref, out_ref in (
        (left_w_ref, left_b_ref, left_ref),
        (right_w_ref, right_b_ref, right_ref),
    ):
        weight = jnp.concatenate([weight_ref[...]] * residues, axis=0)
        bias = jnp.concatenate([bias_ref[...]] * residues, axis=1)
        wide = lax.dot_general(ln_out, weight, NT, preferred_element_type=F32)
        own = pick(blocks, [wide[p * seqs : (p + 1) * seqs] for p in range(residues)])
        out_ref[...] = (own + bias).astype(BF16)
    wide_ref[...] = w_ref[...].astype(F32)
    for d in range(depth):
        sorted_w_ref[d * depth : (d + 1) * depth, :] = wide_ref[
            pl.ds(d, depth, stride=depth), :
        ].astype(BF16)


def cot_kernel(scale, own_ref, other_ref, sorted_w_ref, left_ref, right_ref,
               send_ref, outer_ref, turn_ref):
    residues, columns, _ = own_ref.shape
    depth = sorted_w_ref.shape[0] // (LANES // residues)
    depth = LANES // residues
    first = lax.axis_index("seq") == 0
    own = own_ref[...].reshape(residues * columns, LANES)
    other = other_ref[...].reshape(residues * columns, LANES)
    low = jnp.where(first, own, other)
    high = jnp.where(first, other, own)
    both = jnp.concatenate([low, high], axis=0)
    flat = lax.dot_general(both, sorted_w_ref[...], NT, preferred_element_type=F32) * scale
    blocks = lane_block((columns, LANES), depth)
    for half in range(2):
        for tile in range(depth * depth // LANES):
            block = flat[
                half * residues * columns : (half + 1) * residues * columns,
                tile * LANES : (tile + 1) * LANES,
            ]
            turned = [block] + [pltpu.roll(block, depth * t, 1) for t in range(1, residues)]
            for e in range(residues):
                piece = pick(
                    blocks,
                    [
                        turned[(i - e) % residues][i * columns : (i + 1) * columns]
                        for i in range(residues)
                    ],
                )
                turn_ref[pl.ds(half * columns * depth + tile * residues + e, columns, stride=depth), :] = piece
    outer = turn_ref[...].astype(BF16)
    half_rows = columns * depth
    partial = lax.dot_general(left_ref[...], outer, NT, preferred_element_type=F32).astype(BF16)
    seqs = left_ref.shape[0]
    ranks = columns // residues
    for half in range(2):
        outer_ref[half] = outer[half * half_rows : (half + 1) * half_rows]
        for rank in range(ranks):
            at = (half * ranks + rank) * LANES
            send_ref[half, rank, 0:seqs, :] = right_ref[...]
            send_ref[half, rank, seqs : 2 * seqs, :] = partial[:, at : at + LANES]


def grad_kernel(steps, got_ref, outer_ref, x_ref, gain_ref, left_w_ref, right_w_ref,
                grad_ref, left_cot_ref, right_cot_ref):
    step = pl.program_id(0)
    _, ranks, twice, _ = got_ref.shape
    seqs = twice // 2
    residues = x_ref.shape[1]
    depth = LANES // residues

    @pl.when(step == 0)
    def _():
        left_cot_ref[...] = jnp.zeros_like(left_cot_ref)
        right_cot_ref[...] = jnp.zeros_like(right_cot_ref)

    places = [(half, rank) for half in range(2) for rank in range(ranks)]
    right_all = jnp.concatenate([got_ref[h, r, 0:seqs, :] for h, r in places], axis=1)
    outer = jnp.concatenate([outer_ref[0], outer_ref[1]], axis=0)
    left_cot_ref[...] += jnp.dot(right_all, outer, preferred_element_type=F32)
    total = got_ref[0, 0, seqs:twice, :].astype(F32)
    for h, r in places[1:]:
        total = total + got_ref[h, r, seqs:twice, :].astype(F32)
    right_cot_ref[...] += total

    @pl.when(step == steps - 1)
    def _():
        blocks = lane_block((seqs, LANES), depth)
        left_cot, right_cot = left_cot_ref[...], right_cot_ref[...]
        spread = jnp.concatenate(
            [
                jnp.concatenate(
                    [
                        jnp.where(blocks == place, left_cot, 0.0),
                        jnp.where(blocks == place, right_cot, 0.0),
                    ],
                    axis=1,
                )
                for place in range(residues)
            ],
            axis=0,
        )
        weight = jnp.concatenate(
            [left_w_ref[...]] * residues + [right_w_ref[...]] * residues, axis=0
        )
        rows = residues * seqs
        parts = jnp.concatenate(split_three(spread), axis=0)
        ln_cot = jnp.dot(parts, weight, preferred_element_type=F32)
        ln_cot = ln_cot[0:rows] + (ln_cot[rows : 2 * rows] + ln_cot[2 * rows : 3 * rows])
        gained = ln_cot * gain_ref[...]
        normed, inv_std = normalise(residue_rows(x_ref))
        grad = inv_std * (
            gained
            - jnp.mean(gained, axis=-1, keepdims=True)
            - normed * jnp.mean(gained * normed, axis=-1, keepdims=True)
        )
        for place in range(residues):
            grad_ref[:, place, :] = grad[place * seqs : (place + 1) * seqs].astype(BF16)


def pair_kernel(scale, got_ref, far_ref, left_ref, far_left_ref, sorted_w_ref, offset_ref,
                pair_ref, turn_ref):
    residues, columns, _ = pair_ref.shape
    depth = LANES // residues
    ranks = columns // residues
    mine = lax.axis_index("seq")
    near = jnp.concatenate([got_ref[mine, r] for r in range(ranks)], axis=1)
    far = jnp.concatenate([far_ref[r] for r in range(ranks)], axis=1)
    right = jnp.concatenate([near, far], axis=0)
    left = jnp.concatenate([left_ref[...], far_left_ref[...]], axis=0)
    turn_ref[...] = lax.dot_general(right, left, TN, preferred_element_type=F32) * scale
    blocks = lane_block((columns, LANES), depth)
    tiles = []
    for tile in range(depth * depth // LANES):
        pieces = [
            turn_ref[pl.ds(tile * residues + e, columns, stride=depth), :]
            for e in range(residues)
        ]
        rows = jnp.concatenate(pieces, axis=0)
        turned = [rows] + [pltpu.roll(rows, depth * t, 1) for t in range(1, residues)]
        tiles.append(
            jnp.concatenate(
                [
                    pick(
                        blocks,
                        [
                            turned[(e - i) % residues][e * columns : (e + 1) * columns]
                            for e in range(residues)
                        ],
                    )
                    for i in range(residues)
                ],
                axis=0,
            )
        )
    flat = jnp.concatenate(tiles, axis=1)
    rows = residues * columns
    parts = jnp.concatenate(split_three(flat), axis=0)
    pair = jnp.dot(parts, sorted_w_ref[...], preferred_element_type=F32)
    pair = pair[0:rows] + (pair[rows : 2 * rows] + pair[2 * rows : 3 * rows])
    pair_ref[...] = (pair + offset_ref[...]).astype(BF16).reshape(pair_ref.shape)


def wide_slice(
    homolog_matrix,
    standardizer_scaling,
    standardizer_offset,
    left_projection_matrix,
    left_offset_vector,
    right_projection_matrix,
    right_offset_vector,
    coupling_matrix,
    coupling_offset,
    coupling_cotangent,
):
    seqs, residues, features = homolog_matrix.shape
    depth = left_projection_matrix.shape[1]
    ranks = lax.axis_size("res")
    scale = 1.0 / (seqs * lax.axis_size("seq"))
    half_ranks = ranks // 2
    half_columns = half_ranks * residues
    step_ranks = 4
    columns = step_ranks * residues
    steps = half_ranks // step_ranks
    mine = lax.axis_index("seq")
    swap = [(0, 1), (1, 0)]

    other_cot = lax.ppermute(coupling_cotangent, "seq", swap)
    gain = standardizer_scaling.reshape(1, -1)
    left_w = left_projection_matrix.T
    right_w = right_projection_matrix.T

    left, right, sorted_w = pl.pallas_call(
        project_kernel,
        out_shape=(
            jax.ShapeDtypeStruct((seqs, LANES), BF16),
            jax.ShapeDtypeStruct((seqs, LANES), BF16),
            jax.ShapeDtypeStruct(coupling_matrix.shape, BF16),
        ),
        scratch_shapes=[pltpu.VMEM(coupling_matrix.shape, F32)],
        name="project",
    )(
        homolog_matrix,
        gain,
        standardizer_offset.reshape(1, -1),
        left_w,
        left_offset_vector.reshape(1, -1),
        right_w,
        right_offset_vector.reshape(1, -1),
        coupling_matrix,
    )

    whole = lambda shape: pl.BlockSpec(shape, lambda g: (0,) * len(shape))
    cot_block = pl.BlockSpec((residues, columns, LANES), lambda g: (0, g, 0))
    outer_block = pl.BlockSpec((2, columns * depth, LANES), lambda g: (0, g, 0))
    send_block = pl.BlockSpec((2, step_ranks, 2 * seqs, LANES), lambda g: (0, g, 0, 0))
    send, outer = pl.pallas_call(
        functools.partial(cot_kernel, scale),
        grid=(steps,),
        in_specs=[
            cot_block,
            cot_block,
            whole(sorted_w.shape),
            whole(left.shape),
            whole(right.shape),
        ],
        out_specs=(send_block, outer_block),
        out_shape=(
            jax.ShapeDtypeStruct((2, half_ranks, 2 * seqs, LANES), BF16),
            jax.ShapeDtypeStruct((2, half_columns * depth, LANES), BF16),
        ),
        scratch_shapes=[pltpu.VMEM((2 * columns * depth, LANES), F32)],
        name="cotangent",
    )(coupling_cotangent, other_cot, sorted_w, left, right)

    got = lax.all_to_all(
        send.reshape(ranks, 2 * seqs, LANES), "res", split_axis=0, concat_axis=0, tiled=True
    ).reshape(send.shape)

    leaving = lax.dynamic_index_in_dim(got, 1 - mine, 0, keepdims=False)[:, 0:seqs, :]
    far = lax.ppermute(jnp.concatenate([leaving, left[None]], axis=0), "seq", swap)

    gradient = pl.pallas_call(
        functools.partial(grad_kernel, steps),
        grid=(steps,),
        in_specs=[
            send_block,
            outer_block,
            whole(homolog_matrix.shape),
            whole(gain.shape),
            whole(left_w.shape),
            whole(right_w.shape),
        ],
        out_specs=whole(homolog_matrix.shape),
        out_shape=jax.ShapeDtypeStruct(homolog_matrix.shape, BF16),
        scratch_shapes=[pltpu.VMEM((seqs, LANES), F32)] * 2,
        name="gradient",
    )(got, outer, homolog_matrix, gain, left_w, right_w)

    pair_delta = pl.pallas_call(
        functools.partial(pair_kernel, scale),
        grid=(steps,),
        in_specs=[
            pl.BlockSpec((2, step_ranks, seqs, LANES), lambda g: (0, g, 0, 0)),
            pl.BlockSpec((step_ranks, seqs, LANES), lambda g: (g, 0, 0)),
            whole(left.shape),
            pl.BlockSpec((None, seqs, LANES), lambda g: (half_ranks, 0, 0)),
            whole(sorted_w.shape),
            whole((1, LANES)),
        ],
        out_specs=cot_block,
        out_shape=jax.ShapeDtypeStruct(coupling_cotangent.shape, BF16),
        scratch_shapes=[pltpu.VMEM((columns * depth, LANES), F32)],
        name="pair",
    )(got, far, left, far, sorted_w, coupling_offset.reshape(1, -1))
    return (pair_delta, gradient)


def fetch(source, target, semaphore):
    copy = pltpu.make_async_copy(source, target, semaphore)
    copy.start()
    return copy


def start_copies(pairs, semaphores):
    copies = [
        pltpu.make_async_copy(source, target, semaphores.at[place])
        for place, (source, target) in enumerate(pairs)
    ]
    for copy in copies:
        copy.start()
    return copies


def small_project_kernel(
    x_hbm, gain_hbm, offset_hbm, left_w_hbm, left_b_hbm, right_w_hbm, right_b_hbm, pair_offset_hbm,
    cot_hbm, both_ref, normed_ref, inv_std_ref, spread_w_ref, gain_ref, pair_offset_ref, cot_ref,
    x_ref, offset_ref, left_w_ref, left_b_ref, right_w_ref, right_b_ref, semaphores,
):
    seqs, residues, _ = x_ref.shape
    depth = left_w_ref.shape[0]
    parts = 4
    part = seqs // parts
    copies = start_copies(
        tuple(
            (x_hbm.at[pl.ds(place * part, part)], x_ref.at[pl.ds(place * part, part)])
            for place in range(parts)
        )
        + (
            (left_w_hbm, left_w_ref),
            (right_w_hbm, right_w_ref),
            (gain_hbm, gain_ref),
            (offset_hbm, offset_ref),
            (left_b_hbm, left_b_ref),
            (right_b_hbm, right_b_ref),
            (cot_hbm, cot_ref),
            (pair_offset_hbm, pair_offset_ref),
        ),
        semaphores,
    )
    for copy in copies[:parts]:
        copy.wait()
    normed, inv_std = normalise(residue_rows(x_ref))
    for copy in copies[parts:]:
        copy.wait()
    ln_out = (normed * gain_ref[...] + offset_ref[...]).astype(BF16)
    blocks = lane_block((seqs, LANES), depth)
    weight = jnp.concatenate(
        [left_w_ref[...]] * residues + [right_w_ref[...]] * residues, axis=0
    )
    wide = lax.dot_general(ln_out, weight, NT, preferred_element_type=F32)
    for place, bias_ref in enumerate((left_b_ref, right_b_ref)):
        bias = jnp.concatenate([bias_ref[...]] * residues, axis=1)
        lanes = wide[:, place * LANES : (place + 1) * LANES]
        own = pick(blocks, [lanes[p * seqs : (p + 1) * seqs] for p in range(residues)])
        both_ref[place] = (own + bias).astype(BF16)
    normed_ref[...] = normed
    inv_std_ref[...] = jnp.broadcast_to(inv_std, inv_std_ref.shape)
    spread_w_ref[...] = weight


def outer_rows(scale, cot, residues, sorted_wt_ref, turn_ref):
    columns = cot.shape[0] // residues
    depth = LANES // residues
    flat = jnp.dot(cot, sorted_wt_ref[...], preferred_element_type=F32) * scale
    blocks = lane_block((columns, LANES), depth)
    for tile in range(depth * depth // LANES):
        block = flat[:, tile * LANES : (tile + 1) * LANES]
        turned = [block] + [pltpu.roll(block, depth * t, 1) for t in range(1, residues)]
        for e in range(residues):
            turn_ref[pl.ds(tile * residues + e, columns, stride=depth), :] = pick(
                blocks,
                [
                    turned[(i - e) % residues][i * columns : (i + 1) * columns]
                    for i in range(residues)
                ],
            )
    return turn_ref[...].astype(BF16)


def small_own_kernel(scale, own_ref, other_ref, w_ref, both_ref,
                     keep_ref, outer_near_ref, outer_far_ref, sorted_w_ref, sorted_wt_ref,
                     order_ref, repeat_ref, turn_refs, wide_ref):
    residues, columns, _ = own_ref.shape
    depth = LANES // residues
    wide_ref[...] = w_ref[...].astype(F32)
    for d in range(depth):
        sorted_w_ref[d * depth : (d + 1) * depth, :] = wide_ref[
            pl.ds(d, depth, stride=depth), :
        ].astype(BF16)
    sorted_wt_ref[...] = sorted_w_ref[...].T
    rank = lax.axis_index("res")
    own_is_near = lax.axis_index("seq") == lax.shift_right_logical(rank, 2)
    own = own_ref[...].reshape(residues * columns, LANES)
    other = other_ref[...].reshape(residues * columns, LANES)
    near = outer_rows(
        scale, jnp.where(own_is_near, own, other), residues, sorted_wt_ref, turn_refs[0]
    )
    outer_near_ref[...] = near
    partial = lax.dot_general(both_ref[0], near, NT, preferred_element_type=F32)
    for place in range(columns // residues):
        keep_ref[lax.bitwise_xor(rank & 3, place)] = partial[:, place * LANES : (place + 1) * LANES]
    outer_far_ref[...] = outer_rows(
        scale, jnp.where(own_is_near, other, own), residues, sorted_wt_ref, turn_refs[1]
    )
    order_ref[...] = one_hot(
        lambda row: (
            (2 * (row >> 6 & 1) + (row >> 2 & 1)) * LANES
            + (row & 3) * depth + (row >> 3 & 7) * residues + (row >> 7)
        ),
        order_ref.shape,
    )
    for place in range(residues):
        shape = (LANES, LANES)
        row = lax.broadcasted_iota(jnp.int32, shape, 0)
        lane = lax.broadcasted_iota(jnp.int32, shape, 1)
        repeat_ref[:, place * LANES : (place + 1) * LANES] = jnp.where(
            row == place * depth + lane % depth, 1.0, 0.0
        ).astype(BF16)


def one_hot(target, shape):
    part = (shape[0], LANES)
    wanted = target(lax.broadcasted_iota(jnp.int32, part, 0))
    lane = lax.broadcasted_iota(jnp.int32, part, 1)
    return jnp.concatenate(
        [
            jnp.where(wanted == lane + tile * LANES, 1.0, 0.0).astype(BF16)
            for tile in range(shape[1] // LANES)
        ],
        axis=1,
    )


def blocks_apart(left, repeat, residues):
    depth = LANES // residues
    wide = jnp.dot(left, repeat, preferred_element_type=F32)
    blocks = lane_block(wide.shape, depth) % residues
    return jnp.concatenate(
        [jnp.where(blocks == e, wide, 0.0).astype(BF16) for e in range(residues)], axis=0
    )


def small_partner_kernel(scale, residues, got_ref, sorted_wt_ref, keep_ref, both_ref, order_ref,
                         repeat_ref, leaving_ref, keep_out_ref, right_ref, swap_ref):
    rank = lax.axis_index("res")
    seqs = got_ref.shape[1]
    cot = got_ref[2:4].reshape(2 * seqs, LANES)
    columns = cot.shape[0] // residues
    tiles = sorted_wt_ref.shape[1] // LANES
    flat = jnp.dot(cot, sorted_wt_ref[...], preferred_element_type=F32) * scale
    outer = jnp.concatenate(
        [
            jnp.concatenate(
                [
                    flat[i * columns + start : i * columns + start + 8, tile * LANES : (tile + 1) * LANES]
                    for start in range(0, columns, 8)
                    for tile in range(tiles)
                ],
                axis=0,
            )
            for i in range(residues)
        ],
        axis=1,
    ).astype(BF16)
    apart = blocks_apart(got_ref[0], repeat_ref[...], residues)
    partial = lax.dot_general(apart, outer, NT, preferred_element_type=F32).astype(BF16)
    partial = jnp.concatenate(
        [partial[e * seqs : (e + 1) * seqs] for e in range(residues)], axis=1
    )
    partial = jnp.dot(partial, order_ref[...], preferred_element_type=F32)
    right_ref[0] = both_ref[1]
    right_ref[1] = got_ref[1]
    own_is_near = lax.axis_index("seq") == lax.shift_right_logical(rank, 2)
    swap_ref[0] = jnp.where(own_is_near, got_ref[1], both_ref[1])
    swap_ref[1] = both_ref[0]
    for place in range(leaving_ref.shape[0]):
        leaving_ref[place, 0] = both_ref[1]
        leaving_ref[place, 1] = got_ref[1]
    for place in range(leaving_ref.shape[0]):
        distance = lax.bitwise_xor(rank & 3, place)
        total = keep_ref[distance] + partial[:, place * LANES : (place + 1) * LANES]
        leaving_ref[distance, 2] = total.astype(BF16)
        keep_out_ref[distance] = total


def small_finish_kernel(
    scale, right_ref, part_refs, swapped_ref, swapped_late_ref, both_ref, outer_near_ref, outer_far_ref,
    keep_ref, normed_ref, inv_std_ref, gain_ref, spread_w_ref, sorted_w_ref, offset_ref,
    grad_hbm, pair_hbm, grad_ref, pair_ref, near_ref, beyond_ref, turn_ref, semaphores,
):
    seqs, residues, _ = grad_ref.shape
    columns = pair_ref.shape[1]
    depth = LANES // residues
    ranks = columns // residues
    rank = lax.axis_index("res")
    mine = lax.axis_index("seq")
    here = rank & 3

    blocks_of = [right_ref] + list(part_refs)
    right_all = jnp.concatenate(
        [ref[0] for ref in blocks_of] + [ref[1] for ref in blocks_of], axis=1
    )
    spots = [
        pl.ds(pl.multiple_of(lax.bitwise_xor(here, mask) * LANES, LANES), LANES)
        for mask in range(ranks)
    ]
    outer = jnp.concatenate(
        [outer_near_ref[spot, :] for spot in spots] + [outer_far_ref[spot, :] for spot in spots],
        axis=0,
    )
    left_cot = jnp.dot(right_all, outer, preferred_element_type=F32)
    right_cot = keep_ref[0]
    for part_ref in part_refs:
        right_cot = right_cot + part_ref[2].astype(F32)
    blocks = lane_block((seqs, LANES), depth)
    spread = jnp.concatenate(
        [
            jnp.concatenate(
                [jnp.where(blocks == place, cot, 0.0) for cot in (left_cot, right_cot)], axis=1
            )
            for place in range(residues)
        ],
        axis=0,
    )
    rows = residues * seqs
    parts = jnp.concatenate(split_two(spread), axis=0)
    ln_cot = jnp.dot(parts, spread_w_ref[...], preferred_element_type=F32)
    ln_cot = ln_cot[0:rows] + ln_cot[rows : 2 * rows]
    gained = ln_cot * gain_ref[...]
    normed = normed_ref[...]
    grad = inv_std_ref[:, 0:1] * (
        gained
        - jnp.mean(gained, axis=-1, keepdims=True)
        - normed * jnp.mean(gained * normed, axis=-1, keepdims=True)
    )
    for place in range(residues):
        grad_ref[:, place, :] = grad[place * seqs : (place + 1) * seqs].astype(BF16)
    grad_copy = pltpu.make_async_copy(grad_ref, grad_hbm, semaphores.at[0])
    grad_copy.start()

    half = jnp.where(mine == lax.shift_right_logical(rank, 2), 0, 1)
    for mask, ref in enumerate(blocks_of):
        near_ref[mask] = ref[half]
    beyond_ref[0] = swapped_ref[0]
    beyond_ref[1] = part_refs[0][3]
    beyond_ref[2] = part_refs[1][3]
    beyond_ref[3] = swapped_late_ref[...]
    masks = [lax.bitwise_xor(here, place) for place in range(ranks)]
    right = jnp.concatenate(
        [
            jnp.concatenate([ref[mask] for mask in masks], axis=1)
            for ref in (near_ref, beyond_ref)
        ],
        axis=0,
    )
    left = jnp.concatenate([both_ref[0], swapped_ref[1]], axis=0)
    turn_ref[...] = lax.dot_general(right, left, TN, preferred_element_type=F32) * scale
    blocks = lane_block((columns, LANES), depth)
    tiles = []
    for tile in range(depth * depth // LANES):
        pieces = [
            turn_ref[pl.ds(tile * residues + e, columns, stride=depth), :]
            for e in range(residues)
        ]
        lines = jnp.concatenate(pieces, axis=0)
        turned = [lines] + [pltpu.roll(lines, depth * t, 1) for t in range(1, residues)]
        tiles.append(
            jnp.concatenate(
                [
                    pick(
                        blocks,
                        [
                            turned[(e - i) % residues][e * columns : (e + 1) * columns]
                            for e in range(residues)
                        ],
                    )
                    for i in range(residues)
                ],
                axis=0,
            )
        )
    flat = jnp.concatenate(tiles, axis=1)
    rows = residues * columns
    parts = jnp.concatenate(split_two(flat), axis=0)
    pair = jnp.dot(parts, sorted_w_ref[...], preferred_element_type=F32)
    pair = pair[0:rows] + pair[rows : 2 * rows]
    pair_ref[...] = (pair + offset_ref[...]).astype(BF16).reshape(pair_ref.shape)
    pair_copy = pltpu.make_async_copy(pair_ref, pair_hbm, semaphores.at[1])
    pair_copy.start()
    grad_copy.wait()
    pair_copy.wait()


def small_slice(
    homolog_matrix,
    standardizer_scaling,
    standardizer_offset,
    left_projection_matrix,
    left_offset_vector,
    right_projection_matrix,
    right_offset_vector,
    coupling_matrix,
    coupling_offset,
    coupling_cotangent,
):
    seqs, residues, features = homolog_matrix.shape
    depth = left_projection_matrix.shape[1]
    ranks = lax.axis_size("res")
    rows = seqs * residues
    scale = 1.0 / (seqs * lax.axis_size("seq"))
    rank = lax.axis_index("res")
    mine = lax.axis_index("seq")
    swap = [(0, 1), (1, 0)]
    limit = pltpu.CompilerParams(vmem_limit_bytes=8 * 1024 * 1024)
    vmem = pl.BlockSpec(memory_space=pltpu.VMEM)
    like = jax.ShapeDtypeStruct

    other_cot = lax.ppermute(coupling_cotangent, "seq", swap)
    hbm = pl.BlockSpec(memory_space=pltpu.HBM)
    pin = lambda array: pltpu.with_memory_space_constraint(array, pltpu.HBM)
    both, normed, inv_std, spread_w, gain, pair_offset, own_cot = pl.pallas_call(
        small_project_kernel,
        in_specs=[hbm] * 9,
        out_specs=[vmem] * 7,
        out_shape=(
            like((2, seqs, LANES), BF16),
            like((rows, features), F32),
            like((rows, LANES), F32),
            like((2 * LANES, features), BF16),
            like((1, features), F32),
            like((1, LANES), F32),
            like(coupling_cotangent.shape, BF16),
        ),
        scratch_shapes=[
            pltpu.VMEM(homolog_matrix.shape, BF16),
            pltpu.VMEM((1, features), F32),
            pltpu.VMEM((depth, features), BF16),
            pltpu.VMEM((1, depth), F32),
            pltpu.VMEM((depth, features), BF16),
            pltpu.VMEM((1, depth), F32),
            pltpu.SemaphoreType.DMA((12,)),
        ],
        compiler_params=limit,
        name="project",
    )(
        *[
            pin(array)
            for array in (
                homolog_matrix,
                standardizer_scaling.reshape(1, -1),
                standardizer_offset.reshape(1, -1),
                left_projection_matrix.T,
                left_offset_vector.reshape(1, -1),
                right_projection_matrix.T,
                right_offset_vector.reshape(1, -1),
                coupling_offset.reshape(1, -1),
                coupling_cotangent,
            )
        ]
    )

    def swap_over(mask, value):
        return lax.ppermute(value, "res", [(source, source ^ mask) for source in range(ranks)])

    own_is_near = mine == lax.shift_right_logical(rank, 2)
    far_cot = jnp.where(own_is_near, other_cot, own_cot).reshape(2, seqs, LANES)
    beyond_two = swap_over(4, jnp.concatenate([both, far_cot]))

    half_rows = ranks // 2 * LANES
    turn = pltpu.VMEM((half_rows, LANES), F32)
    keep, outer_near, outer_far, sorted_w, sorted_wt, order, repeat = pl.pallas_call(
        functools.partial(small_own_kernel, scale),
        in_specs=[vmem] * 4,
        out_specs=[vmem] * 7,
        out_shape=(
            like((ranks // 2, seqs, LANES), F32),
            like((half_rows, LANES), BF16),
            like((half_rows, LANES), BF16),
            like(coupling_matrix.shape, BF16),
            like(coupling_matrix.shape[::-1], BF16),
            like((half_rows, half_rows), BF16),
            like((LANES, residues * LANES), BF16),
        ),
        scratch_shapes=[[turn, turn], pltpu.VMEM(coupling_matrix.shape, F32)],
        compiler_params=limit,
        name="own_pieces",
    )(own_cot, other_cot, coupling_matrix, both)

    leaving_parts, keep, right, leaving = pl.pallas_call(
        functools.partial(small_partner_kernel, scale, residues),
        in_specs=[vmem] * 6,
        out_specs=[vmem] * 4,
        out_shape=(
            like((ranks // 2, 3, seqs, LANES), BF16),
            like((ranks // 2, seqs, LANES), F32),
            like((2, seqs, LANES), BF16),
            like((2, seqs, LANES), BF16),
        ),
        compiler_params=limit,
        name="partner_pieces",
    )(beyond_two, sorted_wt, keep, both, order, repeat)

    swapped = lax.ppermute(leaving, "seq", swap)
    diagonal = swap_over(3, leaving_parts[3])
    across, beside = [
        swap_over(mask, jnp.concatenate([leaving_parts[mask], swapped[0:1]])) for mask in (2, 1)
    ]
    swapped_late = lax.ppermute(
        jnp.where(own_is_near, diagonal[1], diagonal[0]), "seq", swap
    )

    pair_delta, gradient = pl.pallas_call(
        functools.partial(small_finish_kernel, scale),
        in_specs=[vmem, [vmem] * 3] + [vmem] * 12,
        out_specs=[pl.BlockSpec(memory_space=pl.ANY)] * 2,
        out_shape=(
            like(homolog_matrix.shape, BF16),
            like(coupling_cotangent.shape, BF16),
        ),
        scratch_shapes=[
            pltpu.VMEM(homolog_matrix.shape, BF16),
            pltpu.VMEM(coupling_cotangent.shape, BF16),
            pltpu.VMEM((ranks // 2, seqs, LANES), BF16),
            pltpu.VMEM((ranks // 2, seqs, LANES), BF16),
            pltpu.VMEM((ranks // 2 * LANES, LANES), F32),
            pltpu.SemaphoreType.DMA((2,)),
        ],
        compiler_params=limit,
        name="finish",
    )(
        right,
        [beside, across, diagonal],
        swapped,
        swapped_late,
        both,
        outer_near,
        outer_far,
        keep,
        normed,
        inv_std,
        gain,
        spread_w,
        sorted_w,
        pair_offset,
    )[::-1]
    return (pair_delta, gradient)


def body(*arrays):
    if lax.axis_size("res") == 8:
        return small_slice(*arrays)
    return wide_slice(*arrays)


def solution(mesh):
    return jax.shard_map(
        body,
        mesh=mesh,
        in_specs=(
            P(("grp", "seq"), "res", None),
            P(),
            P(),
            P(),
            P(),
            P(),
            P(),
            P(),
            P(),
            P(("grp", "res"), "seq", None),
        ),
        out_specs=(P(("grp", "res"), "seq", None), P(("grp", "seq"), "res", None)),
        check_vma=False,
    )
```

```python
import functools

import jax
import jax.numpy as jnp
from jax import lax
from jax.experimental import pallas as pl
from jax.experimental.pallas import tpu as pltpu
from jax.sharding import PartitionSpec as P

LANES = 128
BF16 = jnp.bfloat16
F32 = jnp.float32
NT = (((1,), (1,)), ((), ()))
TN = (((0,), (0,)), ((), ()))


def lane_block(shape, width):
    return lax.broadcasted_iota(jnp.int32, shape, 1) // width


def pick(blocks, pieces):
    result = pieces[0]
    for place in range(1, len(pieces)):
        result = jnp.where(blocks == place, pieces[place], result)
    return result


def split_three(value):
    top = value.astype(BF16)
    rest = value - top.astype(F32)
    middle = rest.astype(BF16)
    low = (rest - middle.astype(F32)).astype(BF16)
    return top, middle, low


def split_two(value):
    top = value.astype(BF16)
    return top, (value - top.astype(F32)).astype(BF16)


def normalise(rows):
    centred = rows - jnp.mean(rows, axis=-1, keepdims=True)
    inv_std = lax.rsqrt(jnp.mean(centred * centred, axis=-1, keepdims=True) + 1e-05)
    return centred * inv_std, inv_std


def residue_rows(x_ref):
    return jnp.concatenate(
        [x_ref[:, place, :].astype(F32) for place in range(x_ref.shape[1])], axis=0
    )


def project_kernel(
    x_ref, gain_ref, offset_ref, left_w_ref, left_b_ref, right_w_ref, right_b_ref, w_ref,
    left_ref, right_ref, sorted_w_ref, wide_ref,
):
    seqs, residues, _ = x_ref.shape
    depth = left_w_ref.shape[0]
    normed, _ = normalise(residue_rows(x_ref))
    ln_out = (normed * gain_ref[...] + offset_ref[...]).astype(BF16)
    blocks = lane_block((seqs, LANES), depth)
    for weight_ref, bias_ref, out_ref in (
        (left_w_ref, left_b_ref, left_ref),
        (right_w_ref, right_b_ref, right_ref),
    ):
        weight = jnp.concatenate([weight_ref[...]] * residues, axis=0)
        bias = jnp.concatenate([bias_ref[...]] * residues, axis=1)
        wide = lax.dot_general(ln_out, weight, NT, preferred_element_type=F32)
        own = pick(blocks, [wide[p * seqs : (p + 1) * seqs] for p in range(residues)])
        out_ref[...] = (own + bias).astype(BF16)
    wide_ref[...] = w_ref[...].astype(F32)
    for d in range(depth):
        sorted_w_ref[d * depth : (d + 1) * depth, :] = wide_ref[
            pl.ds(d, depth, stride=depth), :
        ].astype(BF16)


def cot_kernel(scale, own_ref, other_ref, sorted_w_ref, left_ref, right_ref,
               send_ref, outer_ref, turn_ref):
    residues, columns, _ = own_ref.shape
    depth = sorted_w_ref.shape[0] // (LANES // residues)
    depth = LANES // residues
    first = lax.axis_index("seq") == 0
    own = own_ref[...].reshape(residues * columns, LANES)
    other = other_ref[...].reshape(residues * columns, LANES)
    low = jnp.where(first, own, other)
    high = jnp.where(first, other, own)
    both = jnp.concatenate([low, high], axis=0)
    flat = lax.dot_general(both, sorted_w_ref[...], NT, preferred_element_type=F32) * scale
    blocks = lane_block((columns, LANES), depth)
    for half in range(2):
        for tile in range(depth * depth // LANES):
            block = flat[
                half * residues * columns : (half + 1) * residues * columns,
                tile * LANES : (tile + 1) * LANES,
            ]
            turned = [block] + [pltpu.roll(block, depth * t, 1) for t in range(1, residues)]
            for e in range(residues):
                piece = pick(
                    blocks,
                    [
                        turned[(i - e) % residues][i * columns : (i + 1) * columns]
                        for i in range(residues)
                    ],
                )
                turn_ref[pl.ds(half * columns * depth + tile * residues + e, columns, stride=depth), :] = piece
    outer = turn_ref[...].astype(BF16)
    half_rows = columns * depth
    partial = lax.dot_general(left_ref[...], outer, NT, preferred_element_type=F32).astype(BF16)
    seqs = left_ref.shape[0]
    ranks = columns // residues
    for half in range(2):
        outer_ref[half] = outer[half * half_rows : (half + 1) * half_rows]
        for rank in range(ranks):
            at = (half * ranks + rank) * LANES
            send_ref[half, rank, 0:seqs, :] = right_ref[...]
            send_ref[half, rank, seqs : 2 * seqs, :] = partial[:, at : at + LANES]


def grad_kernel(steps, got_ref, outer_ref, x_ref, gain_ref, left_w_ref, right_w_ref,
                grad_ref, left_cot_ref, right_cot_ref):
    step = pl.program_id(0)
    _, ranks, twice, _ = got_ref.shape
    seqs = twice // 2
    residues = x_ref.shape[1]
    depth = LANES // residues

    @pl.when(step == 0)
    def _():
        left_cot_ref[...] = jnp.zeros_like(left_cot_ref)
        right_cot_ref[...] = jnp.zeros_like(right_cot_ref)

    places = [(half, rank) for half in range(2) for rank in range(ranks)]
    right_all = jnp.concatenate([got_ref[h, r, 0:seqs, :] for h, r in places], axis=1)
    outer = jnp.concatenate([outer_ref[0], outer_ref[1]], axis=0)
    left_cot_ref[...] += jnp.dot(right_all, outer, preferred_element_type=F32)
    total = got_ref[0, 0, seqs:twice, :].astype(F32)
    for h, r in places[1:]:
        total = total + got_ref[h, r, seqs:twice, :].astype(F32)
    right_cot_ref[...] += total

    @pl.when(step == steps - 1)
    def _():
        blocks = lane_block((seqs, LANES), depth)
        left_cot, right_cot = left_cot_ref[...], right_cot_ref[...]
        spread = jnp.concatenate(
            [
                jnp.concatenate(
                    [
                        jnp.where(blocks == place, left_cot, 0.0),
                        jnp.where(blocks == place, right_cot, 0.0),
                    ],
                    axis=1,
                )
                for place in range(residues)
            ],
            axis=0,
        )
        weight = jnp.concatenate(
            [left_w_ref[...]] * residues + [right_w_ref[...]] * residues, axis=0
        )
        rows = residues * seqs
        parts = jnp.concatenate(split_three(spread), axis=0)
        ln_cot = jnp.dot(parts, weight, preferred_element_type=F32)
        ln_cot = ln_cot[0:rows] + (ln_cot[rows : 2 * rows] + ln_cot[2 * rows : 3 * rows])
        gained = ln_cot * gain_ref[...]
        normed, inv_std = normalise(residue_rows(x_ref))
        grad = inv_std * (
            gained
            - jnp.mean(gained, axis=-1, keepdims=True)
            - normed * jnp.mean(gained * normed, axis=-1, keepdims=True)
        )
        for place in range(residues):
            grad_ref[:, place, :] = grad[place * seqs : (place + 1) * seqs].astype(BF16)


def pair_kernel(scale, got_ref, far_ref, left_ref, far_left_ref, sorted_w_ref, offset_ref,
                pair_ref, turn_ref):
    residues, columns, _ = pair_ref.shape
    depth = LANES // residues
    ranks = columns // residues
    mine = lax.axis_index("seq")
    near = jnp.concatenate([got_ref[mine, r] for r in range(ranks)], axis=1)
    far = jnp.concatenate([far_ref[r] for r in range(ranks)], axis=1)
    right = jnp.concatenate([near, far], axis=0)
    left = jnp.concatenate([left_ref[...], far_left_ref[...]], axis=0)
    turn_ref[...] = lax.dot_general(right, left, TN, preferred_element_type=F32) * scale
    blocks = lane_block((columns, LANES), depth)
    tiles = []
    for tile in range(depth * depth // LANES):
        pieces = [
            turn_ref[pl.ds(tile * residues + e, columns, stride=depth), :]
            for e in range(residues)
        ]
        rows = jnp.concatenate(pieces, axis=0)
        turned = [rows] + [pltpu.roll(rows, depth * t, 1) for t in range(1, residues)]
        tiles.append(
            jnp.concatenate(
                [
                    pick(
                        blocks,
                        [
                            turned[(e - i) % residues][e * columns : (e + 1) * columns]
                            for e in range(residues)
                        ],
                    )
                    for i in range(residues)
                ],
                axis=0,
            )
        )
    flat = jnp.concatenate(tiles, axis=1)
    rows = residues * columns
    parts = jnp.concatenate(split_three(flat), axis=0)
    pair = jnp.dot(parts, sorted_w_ref[...], preferred_element_type=F32)
    pair = pair[0:rows] + (pair[rows : 2 * rows] + pair[2 * rows : 3 * rows])
    pair_ref[...] = (pair + offset_ref[...]).astype(BF16).reshape(pair_ref.shape)


def wide_slice(
    homolog_matrix,
    standardizer_scaling,
    standardizer_offset,
    left_projection_matrix,
    left_offset_vector,
    right_projection_matrix,
    right_offset_vector,
    coupling_matrix,
    coupling_offset,
    coupling_cotangent,
):
    seqs, residues, features = homolog_matrix.shape
    depth = left_projection_matrix.shape[1]
    ranks = lax.axis_size("res")
    scale = 1.0 / (seqs * lax.axis_size("seq"))
    half_ranks = ranks // 2
    half_columns = half_ranks * residues
    step_ranks = 4
    columns = step_ranks * residues
    steps = half_ranks // step_ranks
    mine = lax.axis_index("seq")
    swap = [(0, 1), (1, 0)]

    other_cot = lax.ppermute(coupling_cotangent, "seq", swap)
    gain = standardizer_scaling.reshape(1, -1)
    left_w = left_projection_matrix.T
    right_w = right_projection_matrix.T

    left, right, sorted_w = pl.pallas_call(
        project_kernel,
        out_shape=(
            jax.ShapeDtypeStruct((seqs, LANES), BF16),
            jax.ShapeDtypeStruct((seqs, LANES), BF16),
            jax.ShapeDtypeStruct(coupling_matrix.shape, BF16),
        ),
        scratch_shapes=[pltpu.VMEM(coupling_matrix.shape, F32)],
        name="project",
    )(
        homolog_matrix,
        gain,
        standardizer_offset.reshape(1, -1),
        left_w,
        left_offset_vector.reshape(1, -1),
        right_w,
        right_offset_vector.reshape(1, -1),
        coupling_matrix,
    )

    whole = lambda shape: pl.BlockSpec(shape, lambda g: (0,) * len(shape))
    cot_block = pl.BlockSpec((residues, columns, LANES), lambda g: (0, g, 0))
    outer_block = pl.BlockSpec((2, columns * depth, LANES), lambda g: (0, g, 0))
    send_block = pl.BlockSpec((2, step_ranks, 2 * seqs, LANES), lambda g: (0, g, 0, 0))
    send, outer = pl.pallas_call(
        functools.partial(cot_kernel, scale),
        grid=(steps,),
        in_specs=[
            cot_block,
            cot_block,
            whole(sorted_w.shape),
            whole(left.shape),
            whole(right.shape),
        ],
        out_specs=(send_block, outer_block),
        out_shape=(
            jax.ShapeDtypeStruct((2, half_ranks, 2 * seqs, LANES), BF16),
            jax.ShapeDtypeStruct((2, half_columns * depth, LANES), BF16),
        ),
        scratch_shapes=[pltpu.VMEM((2 * columns * depth, LANES), F32)],
        name="cotangent",
    )(coupling_cotangent, other_cot, sorted_w, left, right)

    got = lax.all_to_all(
        send.reshape(ranks, 2 * seqs, LANES), "res", split_axis=0, concat_axis=0, tiled=True
    ).reshape(send.shape)

    leaving = lax.dynamic_index_in_dim(got, 1 - mine, 0, keepdims=False)[:, 0:seqs, :]
    far = lax.ppermute(jnp.concatenate([leaving, left[None]], axis=0), "seq", swap)

    gradient = pl.pallas_call(
        functools.partial(grad_kernel, steps),
        grid=(steps,),
        in_specs=[
            send_block,
            outer_block,
            whole(homolog_matrix.shape),
            whole(gain.shape),
            whole(left_w.shape),
            whole(right_w.shape),
        ],
        out_specs=whole(homolog_matrix.shape),
        out_shape=jax.ShapeDtypeStruct(homolog_matrix.shape, BF16),
        scratch_shapes=[pltpu.VMEM((seqs, LANES), F32)] * 2,
        name="gradient",
    )(got, outer, homolog_matrix, gain, left_w, right_w)

    pair_delta = pl.pallas_call(
        functools.partial(pair_kernel, scale),
        grid=(steps,),
        in_specs=[
            pl.BlockSpec((2, step_ranks, seqs, LANES), lambda g: (0, g, 0, 0)),
            pl.BlockSpec((step_ranks, seqs, LANES), lambda g: (g, 0, 0)),
            whole(left.shape),
            pl.BlockSpec((None, seqs, LANES), lambda g: (half_ranks, 0, 0)),
            whole(sorted_w.shape),
            whole((1, LANES)),
        ],
        out_specs=cot_block,
        out_shape=jax.ShapeDtypeStruct(coupling_cotangent.shape, BF16),
        scratch_shapes=[pltpu.VMEM((columns * depth, LANES), F32)],
        name="pair",
    )(got, far, left, far, sorted_w, coupling_offset.reshape(1, -1))
    return (pair_delta, gradient)


def fetch(source, target, semaphore):
    copy = pltpu.make_async_copy(source, target, semaphore)
    copy.start()
    return copy


def start_copies(pairs, semaphores):
    copies = [
        pltpu.make_async_copy(source, target, semaphores.at[place])
        for place, (source, target) in enumerate(pairs)
    ]
    for copy in copies:
        copy.start()
    return copies


def small_project_kernel(
    x_hbm, gain_hbm, offset_hbm, left_w_hbm, left_b_hbm, right_w_hbm, right_b_hbm, pair_offset_hbm,
    cot_hbm, both_ref, normed_ref, inv_std_ref, spread_w_ref, gain_ref, pair_offset_ref, cot_ref,
    x_ref, offset_ref, left_w_ref, left_b_ref, right_w_ref, right_b_ref, semaphores,
):
    seqs, residues, _ = x_ref.shape
    depth = left_w_ref.shape[0]
    parts = 4
    part = seqs // parts
    copies = start_copies(
        tuple(
            (x_hbm.at[pl.ds(place * part, part)], x_ref.at[pl.ds(place * part, part)])
            for place in range(parts)
        )
        + (
            (left_w_hbm, left_w_ref),
            (right_w_hbm, right_w_ref),
            (gain_hbm, gain_ref),
            (offset_hbm, offset_ref),
            (left_b_hbm, left_b_ref),
            (right_b_hbm, right_b_ref),
            (cot_hbm, cot_ref),
            (pair_offset_hbm, pair_offset_ref),
        ),
        semaphores,
    )
    for copy in copies[:parts]:
        copy.wait()
    normed, inv_std = normalise(residue_rows(x_ref))
    for copy in copies[parts:]:
        copy.wait()
    ln_out = (normed * gain_ref[...] + offset_ref[...]).astype(BF16)
    blocks = lane_block((seqs, LANES), depth)
    weight = jnp.concatenate(
        [left_w_ref[...]] * residues + [right_w_ref[...]] * residues, axis=0
    )
    wide = lax.dot_general(ln_out, weight, NT, preferred_element_type=F32)
    for place, bias_ref in enumerate((left_b_ref, right_b_ref)):
        bias = jnp.concatenate([bias_ref[...]] * residues, axis=1)
        lanes = wide[:, place * LANES : (place + 1) * LANES]
        own = pick(blocks, [lanes[p * seqs : (p + 1) * seqs] for p in range(residues)])
        both_ref[place] = (own + bias).astype(BF16)
    normed_ref[...] = normed
    inv_std_ref[...] = jnp.broadcast_to(inv_std, inv_std_ref.shape)
    spread_w_ref[...] = weight


def outer_rows(scale, cot, residues, sorted_wt_ref, turn_ref):
    columns = cot.shape[0] // residues
    depth = LANES // residues
    flat = jnp.dot(cot, sorted_wt_ref[...], preferred_element_type=F32) * scale
    blocks = lane_block((columns, LANES), depth)
    for tile in range(depth * depth // LANES):
        block = flat[:, tile * LANES : (tile + 1) * LANES]
        turned = [block] + [pltpu.roll(block, depth * t, 1) for t in range(1, residues)]
        for e in range(residues):
            turn_ref[pl.ds(tile * residues + e, columns, stride=depth), :] = pick(
                blocks,
                [
                    turned[(i - e) % residues][i * columns : (i + 1) * columns]
                    for i in range(residues)
                ],
            )
    return turn_ref[...].astype(BF16)


def small_own_kernel(scale, own_ref, other_ref, w_ref, both_ref,
                     keep_ref, outer_near_ref, outer_far_ref, sorted_w_ref, sorted_wt_ref,
                     order_ref, repeat_ref, turn_refs, wide_ref):
    residues, columns, _ = own_ref.shape
    depth = LANES // residues
    wide_ref[...] = w_ref[...].astype(F32)
    for d in range(depth):
        sorted_w_ref[d * depth : (d + 1) * depth, :] = wide_ref[
            pl.ds(d, depth, stride=depth), :
        ].astype(BF16)
    sorted_wt_ref[...] = sorted_w_ref[...].T
    rank = lax.axis_index("res")
    own_is_near = lax.axis_index("seq") == lax.shift_right_logical(rank, 2)
    own = own_ref[...].reshape(residues * columns, LANES)
    other = other_ref[...].reshape(residues * columns, LANES)
    near = outer_rows(
        scale, jnp.where(own_is_near, own, other), residues, sorted_wt_ref, turn_refs[0]
    )
    outer_near_ref[...] = near
    partial = lax.dot_general(both_ref[0], near, NT, preferred_element_type=F32)
    for place in range(columns // residues):
        keep_ref[lax.bitwise_xor(rank & 3, place)] = partial[:, place * LANES : (place + 1) * LANES]
    outer_far_ref[...] = outer_rows(
        scale, jnp.where(own_is_near, other, own), residues, sorted_wt_ref, turn_refs[1]
    )
    order_ref[...] = one_hot(
        lambda row: (
            (2 * (row >> 6 & 1) + (row >> 2 & 1)) * LANES
            + (row & 3) * depth + (row >> 3 & 7) * residues + (row >> 7)
        ),
        order_ref.shape,
    )
    for place in range(residues):
        shape = (LANES, LANES)
        row = lax.broadcasted_iota(jnp.int32, shape, 0)
        lane = lax.broadcasted_iota(jnp.int32, shape, 1)
        repeat_ref[:, place * LANES : (place + 1) * LANES] = jnp.where(
            row == place * depth + lane % depth, 1.0, 0.0
        ).astype(BF16)


def one_hot(target, shape):
    part = (shape[0], LANES)
    wanted = target(lax.broadcasted_iota(jnp.int32, part, 0))
    lane = lax.broadcasted_iota(jnp.int32, part, 1)
    return jnp.concatenate(
        [
            jnp.where(wanted == lane + tile * LANES, 1.0, 0.0).astype(BF16)
            for tile in range(shape[1] // LANES)
        ],
        axis=1,
    )


def blocks_apart(left, repeat, residues):
    depth = LANES // residues
    wide = jnp.dot(left, repeat, preferred_element_type=F32)
    blocks = lane_block(wide.shape, depth) % residues
    return jnp.concatenate(
        [jnp.where(blocks == e, wide, 0.0).astype(BF16) for e in range(residues)], axis=0
    )


def small_partner_kernel(scale, residues, got_ref, sorted_wt_ref, keep_ref, both_ref, order_ref,
                         repeat_ref, leaving_ref, keep_out_ref, right_ref, swap_ref):
    rank = lax.axis_index("res")
    seqs = got_ref.shape[1]
    cot = got_ref[2:4].reshape(2 * seqs, LANES)
    columns = cot.shape[0] // residues
    tiles = sorted_wt_ref.shape[1] // LANES
    flat = jnp.dot(cot, sorted_wt_ref[...], preferred_element_type=F32) * scale
    outer = jnp.concatenate(
        [
            jnp.concatenate(
                [
                    flat[i * columns + start : i * columns + start + 8, tile * LANES : (tile + 1) * LANES]
                    for start in range(0, columns, 8)
                    for tile in range(tiles)
                ],
                axis=0,
            )
            for i in range(residues)
        ],
        axis=1,
    ).astype(BF16)
    apart = blocks_apart(got_ref[0], repeat_ref[...], residues)
    partial = lax.dot_general(apart, outer, NT, preferred_element_type=F32).astype(BF16)
    partial = jnp.concatenate(
        [partial[e * seqs : (e + 1) * seqs] for e in range(residues)], axis=1
    )
    partial = jnp.dot(partial, order_ref[...], preferred_element_type=F32)
    right_ref[0] = both_ref[1]
    right_ref[1] = got_ref[1]
    own_is_near = lax.axis_index("seq") == lax.shift_right_logical(rank, 2)
    swap_ref[0] = jnp.where(own_is_near, got_ref[1], both_ref[1])
    swap_ref[1] = both_ref[0]
    for place in range(leaving_ref.shape[0]):
        leaving_ref[place, 0] = both_ref[1]
        leaving_ref[place, 1] = got_ref[1]
    for place in range(leaving_ref.shape[0]):
        distance = lax.bitwise_xor(rank & 3, place)
        total = keep_ref[distance] + partial[:, place * LANES : (place + 1) * LANES]
        leaving_ref[distance, 2] = total.astype(BF16)
        keep_out_ref[distance] = total


def small_prepare_kernel(both_ref, swapped_ref, repeat_ref, keep_ref, part_ref,
                         apart_ref, order_ref, right_cot_ref):
    residues = apart_ref.shape[1] // LANES
    depth = LANES // residues
    left = jnp.concatenate([both_ref[0], swapped_ref[1]], axis=0)
    apart_ref[...] = blocks_apart(left, repeat_ref[...], residues)
    order_ref[...] = one_hot(
        lambda row: (
            (row & 3) * LANES + (row >> 2 & 7) * (4 * residues) + (row >> 7) * residues + (row >> 5 & 3)
        ),
        order_ref.shape,
    )
    right_cot_ref[...] = keep_ref[0] + part_ref[2].astype(F32)


def small_finish_kernel(
    scale, right_ref, part_refs, swapped_ref, swapped_late_ref, outer_near_ref, outer_far_ref,
    right_cot_ref, normed_ref, inv_std_ref, gain_ref, spread_w_ref, sorted_w_ref, offset_ref, apart_ref,
    order_ref, grad_hbm, pair_hbm, grad_ref, pair_ref, near_ref, beyond_ref, semaphores,
):
    seqs, residues, _ = grad_ref.shape
    columns = pair_ref.shape[1]
    depth = LANES // residues
    ranks = columns // residues
    rank = lax.axis_index("res")
    mine = lax.axis_index("seq")
    here = rank & 3

    blocks_of = [right_ref] + list(part_refs)
    right_all = jnp.concatenate(
        [ref[0] for ref in blocks_of] + [ref[1] for ref in blocks_of], axis=1
    )
    spots = [
        pl.ds(pl.multiple_of(lax.bitwise_xor(here, mask) * LANES, LANES), LANES)
        for mask in range(ranks)
    ]
    outer = jnp.concatenate(
        [outer_near_ref[spot, :] for spot in spots] + [outer_far_ref[spot, :] for spot in spots],
        axis=0,
    )
    left_cot = jnp.dot(right_all, outer, preferred_element_type=F32)
    right_cot = right_cot_ref[...]
    for part_ref in part_refs[:2]:
        right_cot = right_cot + part_ref[2].astype(F32)
    blocks = lane_block((seqs, LANES), depth)
    spread = jnp.concatenate(
        [
            jnp.concatenate(
                [jnp.where(blocks == place, cot, 0.0) for cot in (left_cot, right_cot)], axis=1
            )
            for place in range(residues)
        ],
        axis=0,
    )
    rows = residues * seqs
    parts = jnp.concatenate(split_two(spread), axis=0)
    ln_cot = jnp.dot(parts, spread_w_ref[...], preferred_element_type=F32)
    ln_cot = ln_cot[0:rows] + ln_cot[rows : 2 * rows]
    gained = ln_cot * gain_ref[...]
    normed = normed_ref[...]
    grad = inv_std_ref[:, 0:1] * (
        gained
        - jnp.mean(gained, axis=-1, keepdims=True)
        - normed * jnp.mean(gained * normed, axis=-1, keepdims=True)
    )
    for place in range(residues):
        grad_ref[:, place, :] = grad[place * seqs : (place + 1) * seqs].astype(BF16)
    grad_copy = pltpu.make_async_copy(grad_ref, grad_hbm, semaphores.at[0])
    grad_copy.start()

    half = jnp.where(mine == lax.shift_right_logical(rank, 2), 0, 1)
    for mask, ref in enumerate(blocks_of):
        near_ref[mask] = ref[half]
    beyond_ref[0] = swapped_ref[0]
    beyond_ref[1] = part_refs[0][3]
    beyond_ref[2] = part_refs[1][3]
    beyond_ref[3] = swapped_late_ref[...]
    masks = [lax.bitwise_xor(here, place) for place in range(ranks)]
    right = jnp.concatenate(
        [
            jnp.concatenate([ref[mask] for mask in masks], axis=1)
            for ref in (near_ref, beyond_ref)
        ],
        axis=0,
    )
    right = jnp.dot(right, order_ref[...], preferred_element_type=F32).astype(BF16)
    right = jnp.concatenate(
        [right[:, e * LANES : (e + 1) * LANES] for e in range(residues)], axis=0
    )
    flat = lax.dot_general(right, apart_ref[...], TN, preferred_element_type=F32) * scale
    flat = jnp.concatenate(
        [
            jnp.concatenate(
                [
                    flat[tile * columns : (tile + 1) * columns, i * LANES : (i + 1) * LANES]
                    for tile in range(depth * depth // LANES)
                ],
                axis=1,
            )
            for i in range(residues)
        ],
        axis=0,
    )
    rows = residues * columns
    parts = jnp.concatenate(split_two(flat), axis=0)
    pair = jnp.dot(parts, sorted_w_ref[...], preferred_element_type=F32)
    pair = pair[0:rows] + pair[rows : 2 * rows]
    pair_ref[...] = (pair + offset_ref[...]).astype(BF16).reshape(pair_ref.shape)
    pair_copy = pltpu.make_async_copy(pair_ref, pair_hbm, semaphores.at[1])
    pair_copy.start()
    grad_copy.wait()
    pair_copy.wait()


def small_slice(
    homolog_matrix,
    standardizer_scaling,
    standardizer_offset,
    left_projection_matrix,
    left_offset_vector,
    right_projection_matrix,
    right_offset_vector,
    coupling_matrix,
    coupling_offset,
    coupling_cotangent,
):
    seqs, residues, features = homolog_matrix.shape
    depth = left_projection_matrix.shape[1]
    ranks = lax.axis_size("res")
    rows = seqs * residues
    scale = 1.0 / (seqs * lax.axis_size("seq"))
    rank = lax.axis_index("res")
    mine = lax.axis_index("seq")
    swap = [(0, 1), (1, 0)]
    limit = pltpu.CompilerParams(vmem_limit_bytes=8 * 1024 * 1024)
    vmem = pl.BlockSpec(memory_space=pltpu.VMEM)
    like = jax.ShapeDtypeStruct

    other_cot = lax.ppermute(coupling_cotangent, "seq", swap)
    hbm = pl.BlockSpec(memory_space=pltpu.HBM)
    pin = lambda array: pltpu.with_memory_space_constraint(array, pltpu.HBM)
    both, normed, inv_std, spread_w, gain, pair_offset, own_cot = pl.pallas_call(
        small_project_kernel,
        in_specs=[hbm] * 9,
        out_specs=[vmem] * 7,
        out_shape=(
            like((2, seqs, LANES), BF16),
            like((rows, features), F32),
            like((rows, LANES), F32),
            like((2 * LANES, features), BF16),
            like((1, features), F32),
            like((1, LANES), F32),
            like(coupling_cotangent.shape, BF16),
        ),
        scratch_shapes=[
            pltpu.VMEM(homolog_matrix.shape, BF16),
            pltpu.VMEM((1, features), F32),
            pltpu.VMEM((depth, features), BF16),
            pltpu.VMEM((1, depth), F32),
            pltpu.VMEM((depth, features), BF16),
            pltpu.VMEM((1, depth), F32),
            pltpu.SemaphoreType.DMA((12,)),
        ],
        compiler_params=limit,
        name="project",
    )(
        *[
            pin(array)
            for array in (
                homolog_matrix,
                standardizer_scaling.reshape(1, -1),
                standardizer_offset.reshape(1, -1),
                left_projection_matrix.T,
                left_offset_vector.reshape(1, -1),
                right_projection_matrix.T,
                right_offset_vector.reshape(1, -1),
                coupling_offset.reshape(1, -1),
                coupling_cotangent,
            )
        ]
    )

    def swap_over(mask, value):
        return lax.ppermute(value, "res", [(source, source ^ mask) for source in range(ranks)])

    own_is_near = mine == lax.shift_right_logical(rank, 2)
    far_cot = jnp.where(own_is_near, other_cot, own_cot).reshape(2, seqs, LANES)
    beyond_two = swap_over(4, jnp.concatenate([both, far_cot]))

    half_rows = ranks // 2 * LANES
    turn = pltpu.VMEM((half_rows, LANES), F32)
    keep, outer_near, outer_far, sorted_w, sorted_wt, order, repeat = pl.pallas_call(
        functools.partial(small_own_kernel, scale),
        in_specs=[vmem] * 4,
        out_specs=[vmem] * 7,
        out_shape=(
            like((ranks // 2, seqs, LANES), F32),
            like((half_rows, LANES), BF16),
            like((half_rows, LANES), BF16),
            like(coupling_matrix.shape, BF16),
            like(coupling_matrix.shape[::-1], BF16),
            like((half_rows, half_rows), BF16),
            like((LANES, residues * LANES), BF16),
        ),
        scratch_shapes=[[turn, turn], pltpu.VMEM(coupling_matrix.shape, F32)],
        compiler_params=limit,
        name="own_pieces",
    )(own_cot, other_cot, coupling_matrix, both)

    leaving_parts, keep, right, leaving = pl.pallas_call(
        functools.partial(small_partner_kernel, scale, residues),
        in_specs=[vmem] * 6,
        out_specs=[vmem] * 4,
        out_shape=(
            like((ranks // 2, 3, seqs, LANES), BF16),
            like((ranks // 2, seqs, LANES), F32),
            like((2, seqs, LANES), BF16),
            like((2, seqs, LANES), BF16),
        ),
        compiler_params=limit,
        name="partner_pieces",
    )(beyond_two, sorted_wt, keep, both, order, repeat)

    swapped = lax.ppermute(leaving, "seq", swap)
    diagonal = swap_over(3, leaving_parts[3])
    across, beside = [
        swap_over(mask, jnp.concatenate([leaving_parts[mask], swapped[0:1]])) for mask in (2, 1)
    ]
    swapped_late = lax.ppermute(
        jnp.where(own_is_near, diagonal[1], diagonal[0]), "seq", swap
    )

    apart, column_order, right_cot = pl.pallas_call(
        small_prepare_kernel,
        in_specs=[vmem] * 5,
        out_specs=[vmem] * 3,
        out_shape=(
            like((2 * residues * seqs, residues * LANES), BF16),
            like((half_rows, half_rows), BF16),
            like((seqs, LANES), F32),
        ),
        compiler_params=limit,
        name="prepare",
    )(both, swapped, repeat, keep, diagonal)

    pair_delta, gradient = pl.pallas_call(
        functools.partial(small_finish_kernel, scale),
        in_specs=[vmem, [vmem] * 3] + [vmem] * 13,
        out_specs=[pl.BlockSpec(memory_space=pl.ANY)] * 2,
        out_shape=(
            like(homolog_matrix.shape, BF16),
            like(coupling_cotangent.shape, BF16),
        ),
        scratch_shapes=[
            pltpu.VMEM(homolog_matrix.shape, BF16),
            pltpu.VMEM(coupling_cotangent.shape, BF16),
            pltpu.VMEM((ranks // 2, seqs, LANES), BF16),
            pltpu.VMEM((ranks // 2, seqs, LANES), BF16),
            pltpu.SemaphoreType.DMA((2,)),
        ],
        compiler_params=limit,
        name="finish",
    )(
        right,
        [beside, across, diagonal],
        swapped,
        swapped_late,
        outer_near,
        outer_far,
        right_cot,
        normed,
        inv_std,
        gain,
        spread_w,
        sorted_w,
        pair_offset,
        apart,
        column_order,
    )[::-1]
    return (pair_delta, gradient)


def body(*arrays):
    if lax.axis_size("res") == 8:
        return small_slice(*arrays)
    return wide_slice(*arrays)


def solution(mesh):
    return jax.shard_map(
        body,
        mesh=mesh,
        in_specs=(
            P(("grp", "seq"), "res", None),
            P(),
            P(),
            P(),
            P(),
            P(),
            P(),
            P(),
            P(),
            P(("grp", "res"), "seq", None),
        ),
        out_specs=(P(("grp", "res"), "seq", None), P(("grp", "seq"), "res", None)),
        check_vma=False,
    )
```

```python
import functools

import jax
import jax.numpy as jnp
from jax import lax
from jax.experimental import pallas as pl
from jax.experimental.pallas import tpu as pltpu
from jax.sharding import PartitionSpec as P

LANES = 128
BF16 = jnp.bfloat16
F32 = jnp.float32
NT = (((1,), (1,)), ((), ()))
TN = (((0,), (0,)), ((), ()))


def lane_block(shape, width):
    return lax.broadcasted_iota(jnp.int32, shape, 1) // width


def pick(blocks, pieces):
    result = pieces[0]
    for place in range(1, len(pieces)):
        result = jnp.where(blocks == place, pieces[place], result)
    return result


def split_three(value):
    top = value.astype(BF16)
    rest = value - top.astype(F32)
    middle = rest.astype(BF16)
    low = (rest - middle.astype(F32)).astype(BF16)
    return top, middle, low


def split_two(value):
    top = value.astype(BF16)
    return top, (value - top.astype(F32)).astype(BF16)


def normalise(rows):
    centred = rows - jnp.mean(rows, axis=-1, keepdims=True)
    inv_std = lax.rsqrt(jnp.mean(centred * centred, axis=-1, keepdims=True) + 1e-05)
    return centred * inv_std, inv_std


def residue_rows(x_ref):
    return jnp.concatenate(
        [x_ref[:, place, :].astype(F32) for place in range(x_ref.shape[1])], axis=0
    )


def project_kernel(
    x_ref, gain_ref, offset_ref, left_w_ref, left_b_ref, right_w_ref, right_b_ref, w_ref,
    left_ref, right_ref, sorted_w_ref, wide_ref,
):
    seqs, residues, _ = x_ref.shape
    depth = left_w_ref.shape[0]
    normed, _ = normalise(residue_rows(x_ref))
    ln_out = (normed * gain_ref[...] + offset_ref[...]).astype(BF16)
    blocks = lane_block((seqs, LANES), depth)
    for weight_ref, bias_ref, out_ref in (
        (left_w_ref, left_b_ref, left_ref),
        (right_w_ref, right_b_ref, right_ref),
    ):
        weight = jnp.concatenate([weight_ref[...]] * residues, axis=0)
        bias = jnp.concatenate([bias_ref[...]] * residues, axis=1)
        wide = lax.dot_general(ln_out, weight, NT, preferred_element_type=F32)
        own = pick(blocks, [wide[p * seqs : (p + 1) * seqs] for p in range(residues)])
        out_ref[...] = (own + bias).astype(BF16)
    wide_ref[...] = w_ref[...].astype(F32)
    for d in range(depth):
        sorted_w_ref[d * depth : (d + 1) * depth, :] = wide_ref[
            pl.ds(d, depth, stride=depth), :
        ].astype(BF16)


def cot_kernel(scale, own_ref, other_ref, sorted_w_ref, left_ref, right_ref,
               send_ref, outer_ref, turn_ref):
    residues, columns, _ = own_ref.shape
    depth = sorted_w_ref.shape[0] // (LANES // residues)
    depth = LANES // residues
    first = lax.axis_index("seq") == 0
    own = own_ref[...].reshape(residues * columns, LANES)
    other = other_ref[...].reshape(residues * columns, LANES)
    low = jnp.where(first, own, other)
    high = jnp.where(first, other, own)
    both = jnp.concatenate([low, high], axis=0)
    flat = lax.dot_general(both, sorted_w_ref[...], NT, preferred_element_type=F32) * scale
    blocks = lane_block((columns, LANES), depth)
    for half in range(2):
        for tile in range(depth * depth // LANES):
            block = flat[
                half * residues * columns : (half + 1) * residues * columns,
                tile * LANES : (tile + 1) * LANES,
            ]
            turned = [block] + [pltpu.roll(block, depth * t, 1) for t in range(1, residues)]
            for e in range(residues):
                piece = pick(
                    blocks,
                    [
                        turned[(i - e) % residues][i * columns : (i + 1) * columns]
                        for i in range(residues)
                    ],
                )
                turn_ref[pl.ds(half * columns * depth + tile * residues + e, columns, stride=depth), :] = piece
    outer = turn_ref[...].astype(BF16)
    half_rows = columns * depth
    partial = lax.dot_general(left_ref[...], outer, NT, preferred_element_type=F32).astype(BF16)
    seqs = left_ref.shape[0]
    ranks = columns // residues
    for half in range(2):
        outer_ref[half] = outer[half * half_rows : (half + 1) * half_rows]
        for rank in range(ranks):
            at = (half * ranks + rank) * LANES
            send_ref[half, rank, 0:seqs, :] = right_ref[...]
            send_ref[half, rank, seqs : 2 * seqs, :] = partial[:, at : at + LANES]


def grad_kernel(steps, got_ref, outer_ref, x_ref, gain_ref, left_w_ref, right_w_ref,
                grad_ref, left_cot_ref, right_cot_ref):
    step = pl.program_id(0)
    _, ranks, twice, _ = got_ref.shape
    seqs = twice // 2
    residues = x_ref.shape[1]
    depth = LANES // residues

    @pl.when(step == 0)
    def _():
        left_cot_ref[...] = jnp.zeros_like(left_cot_ref)
        right_cot_ref[...] = jnp.zeros_like(right_cot_ref)

    places = [(half, rank) for half in range(2) for rank in range(ranks)]
    right_all = jnp.concatenate([got_ref[h, r, 0:seqs, :] for h, r in places], axis=1)
    outer = jnp.concatenate([outer_ref[0], outer_ref[1]], axis=0)
    left_cot_ref[...] += jnp.dot(right_all, outer, preferred_element_type=F32)
    total = got_ref[0, 0, seqs:twice, :].astype(F32)
    for h, r in places[1:]:
        total = total + got_ref[h, r, seqs:twice, :].astype(F32)
    right_cot_ref[...] += total

    @pl.when(step == steps - 1)
    def _():
        blocks = lane_block((seqs, LANES), depth)
        left_cot, right_cot = left_cot_ref[...], right_cot_ref[...]
        spread = jnp.concatenate(
            [
                jnp.concatenate(
                    [
                        jnp.where(blocks == place, left_cot, 0.0),
                        jnp.where(blocks == place, right_cot, 0.0),
                    ],
                    axis=1,
                )
                for place in range(residues)
            ],
            axis=0,
        )
        weight = jnp.concatenate(
            [left_w_ref[...]] * residues + [right_w_ref[...]] * residues, axis=0
        )
        rows = residues * seqs
        parts = jnp.concatenate(split_three(spread), axis=0)
        ln_cot = jnp.dot(parts, weight, preferred_element_type=F32)
        ln_cot = ln_cot[0:rows] + (ln_cot[rows : 2 * rows] + ln_cot[2 * rows : 3 * rows])
        gained = ln_cot * gain_ref[...]
        normed, inv_std = normalise(residue_rows(x_ref))
        grad = inv_std * (
            gained
            - jnp.mean(gained, axis=-1, keepdims=True)
            - normed * jnp.mean(gained * normed, axis=-1, keepdims=True)
        )
        for place in range(residues):
            grad_ref[:, place, :] = grad[place * seqs : (place + 1) * seqs].astype(BF16)


def pair_kernel(scale, got_ref, far_ref, left_ref, far_left_ref, sorted_w_ref, offset_ref,
                pair_ref, turn_ref):
    residues, columns, _ = pair_ref.shape
    depth = LANES // residues
    ranks = columns // residues
    mine = lax.axis_index("seq")
    near = jnp.concatenate([got_ref[mine, r] for r in range(ranks)], axis=1)
    far = jnp.concatenate([far_ref[r] for r in range(ranks)], axis=1)
    right = jnp.concatenate([near, far], axis=0)
    left = jnp.concatenate([left_ref[...], far_left_ref[...]], axis=0)
    turn_ref[...] = lax.dot_general(right, left, TN, preferred_element_type=F32) * scale
    blocks = lane_block((columns, LANES), depth)
    tiles = []
    for tile in range(depth * depth // LANES):
        pieces = [
            turn_ref[pl.ds(tile * residues + e, columns, stride=depth), :]
            for e in range(residues)
        ]
        rows = jnp.concatenate(pieces, axis=0)
        turned = [rows] + [pltpu.roll(rows, depth * t, 1) for t in range(1, residues)]
        tiles.append(
            jnp.concatenate(
                [
                    pick(
                        blocks,
                        [
                            turned[(e - i) % residues][e * columns : (e + 1) * columns]
                            for e in range(residues)
                        ],
                    )
                    for i in range(residues)
                ],
                axis=0,
            )
        )
    flat = jnp.concatenate(tiles, axis=1)
    rows = residues * columns
    parts = jnp.concatenate(split_three(flat), axis=0)
    pair = jnp.dot(parts, sorted_w_ref[...], preferred_element_type=F32)
    pair = pair[0:rows] + (pair[rows : 2 * rows] + pair[2 * rows : 3 * rows])
    pair_ref[...] = (pair + offset_ref[...]).astype(BF16).reshape(pair_ref.shape)


def wide_slice(
    homolog_matrix,
    standardizer_scaling,
    standardizer_offset,
    left_projection_matrix,
    left_offset_vector,
    right_projection_matrix,
    right_offset_vector,
    coupling_matrix,
    coupling_offset,
    coupling_cotangent,
):
    seqs, residues, features = homolog_matrix.shape
    depth = left_projection_matrix.shape[1]
    ranks = lax.axis_size("res")
    scale = 1.0 / (seqs * lax.axis_size("seq"))
    half_ranks = ranks // 2
    half_columns = half_ranks * residues
    step_ranks = 4
    columns = step_ranks * residues
    steps = half_ranks // step_ranks
    mine = lax.axis_index("seq")
    swap = [(0, 1), (1, 0)]

    other_cot = lax.ppermute(coupling_cotangent, "seq", swap)
    gain = standardizer_scaling.reshape(1, -1)
    left_w = left_projection_matrix.T
    right_w = right_projection_matrix.T

    left, right, sorted_w = pl.pallas_call(
        project_kernel,
        out_shape=(
            jax.ShapeDtypeStruct((seqs, LANES), BF16),
            jax.ShapeDtypeStruct((seqs, LANES), BF16),
            jax.ShapeDtypeStruct(coupling_matrix.shape, BF16),
        ),
        scratch_shapes=[pltpu.VMEM(coupling_matrix.shape, F32)],
        name="project",
    )(
        homolog_matrix,
        gain,
        standardizer_offset.reshape(1, -1),
        left_w,
        left_offset_vector.reshape(1, -1),
        right_w,
        right_offset_vector.reshape(1, -1),
        coupling_matrix,
    )

    whole = lambda shape: pl.BlockSpec(shape, lambda g: (0,) * len(shape))
    cot_block = pl.BlockSpec((residues, columns, LANES), lambda g: (0, g, 0))
    outer_block = pl.BlockSpec((2, columns * depth, LANES), lambda g: (0, g, 0))
    send_block = pl.BlockSpec((2, step_ranks, 2 * seqs, LANES), lambda g: (0, g, 0, 0))
    send, outer = pl.pallas_call(
        functools.partial(cot_kernel, scale),
        grid=(steps,),
        in_specs=[
            cot_block,
            cot_block,
            whole(sorted_w.shape),
            whole(left.shape),
            whole(right.shape),
        ],
        out_specs=(send_block, outer_block),
        out_shape=(
            jax.ShapeDtypeStruct((2, half_ranks, 2 * seqs, LANES), BF16),
            jax.ShapeDtypeStruct((2, half_columns * depth, LANES), BF16),
        ),
        scratch_shapes=[pltpu.VMEM((2 * columns * depth, LANES), F32)],
        name="cotangent",
    )(coupling_cotangent, other_cot, sorted_w, left, right)

    got = lax.all_to_all(
        send.reshape(ranks, 2 * seqs, LANES), "res", split_axis=0, concat_axis=0, tiled=True
    ).reshape(send.shape)

    leaving = lax.dynamic_index_in_dim(got, 1 - mine, 0, keepdims=False)[:, 0:seqs, :]
    far = lax.ppermute(jnp.concatenate([leaving, left[None]], axis=0), "seq", swap)

    gradient = pl.pallas_call(
        functools.partial(grad_kernel, steps),
        grid=(steps,),
        in_specs=[
            send_block,
            outer_block,
            whole(homolog_matrix.shape),
            whole(gain.shape),
            whole(left_w.shape),
            whole(right_w.shape),
        ],
        out_specs=whole(homolog_matrix.shape),
        out_shape=jax.ShapeDtypeStruct(homolog_matrix.shape, BF16),
        scratch_shapes=[pltpu.VMEM((seqs, LANES), F32)] * 2,
        name="gradient",
    )(got, outer, homolog_matrix, gain, left_w, right_w)

    pair_delta = pl.pallas_call(
        functools.partial(pair_kernel, scale),
        grid=(steps,),
        in_specs=[
            pl.BlockSpec((2, step_ranks, seqs, LANES), lambda g: (0, g, 0, 0)),
            pl.BlockSpec((step_ranks, seqs, LANES), lambda g: (g, 0, 0)),
            whole(left.shape),
            pl.BlockSpec((None, seqs, LANES), lambda g: (half_ranks, 0, 0)),
            whole(sorted_w.shape),
            whole((1, LANES)),
        ],
        out_specs=cot_block,
        out_shape=jax.ShapeDtypeStruct(coupling_cotangent.shape, BF16),
        scratch_shapes=[pltpu.VMEM((columns * depth, LANES), F32)],
        name="pair",
    )(got, far, left, far, sorted_w, coupling_offset.reshape(1, -1))
    return (pair_delta, gradient)


def fetch(source, target, semaphore):
    copy = pltpu.make_async_copy(source, target, semaphore)
    copy.start()
    return copy


def start_copies(pairs, semaphores):
    copies = [
        pltpu.make_async_copy(source, target, semaphores.at[place])
        for place, (source, target) in enumerate(pairs)
    ]
    for copy in copies:
        copy.start()
    return copies


def small_project_kernel(
    x_hbm, gain_hbm, offset_hbm, left_w_hbm, left_b_hbm, right_w_hbm, right_b_hbm, pair_offset_hbm,
    cot_hbm, both_ref, normed_ref, inv_std_ref, spread_w_ref, gain_ref, pair_offset_ref, cot_ref,
    x_ref, offset_ref, left_w_ref, left_b_ref, right_w_ref, right_b_ref, semaphores,
):
    seqs, residues, _ = x_ref.shape
    depth = left_w_ref.shape[0]
    parts = 4
    part = seqs // parts
    copies = start_copies(
        tuple(
            (x_hbm.at[pl.ds(place * part, part)], x_ref.at[pl.ds(place * part, part)])
            for place in range(parts)
        )
        + (
            (left_w_hbm, left_w_ref),
            (right_w_hbm, right_w_ref),
            (gain_hbm, gain_ref),
            (offset_hbm, offset_ref),
            (left_b_hbm, left_b_ref),
            (right_b_hbm, right_b_ref),
            (cot_hbm, cot_ref),
            (pair_offset_hbm, pair_offset_ref),
        ),
        semaphores,
    )
    for copy in copies[:parts]:
        copy.wait()
    normed, inv_std = normalise(residue_rows(x_ref))
    for copy in copies[parts:]:
        copy.wait()
    ln_out = (normed * gain_ref[...] + offset_ref[...]).astype(BF16)
    blocks = lane_block((seqs, LANES), depth)
    weight = jnp.concatenate(
        [left_w_ref[...]] * residues + [right_w_ref[...]] * residues, axis=0
    )
    wide = lax.dot_general(ln_out, weight, NT, preferred_element_type=F32)
    for place, bias_ref in enumerate((left_b_ref, right_b_ref)):
        bias = jnp.concatenate([bias_ref[...]] * residues, axis=1)
        lanes = wide[:, place * LANES : (place + 1) * LANES]
        own = pick(blocks, [lanes[p * seqs : (p + 1) * seqs] for p in range(residues)])
        both_ref[place] = (own + bias).astype(BF16)
    normed_ref[...] = normed
    inv_std_ref[...] = jnp.broadcast_to(inv_std, inv_std_ref.shape)
    spread_w_ref[...] = weight


def outer_rows(scale, cot, residues, sorted_wt_ref, turn_ref):
    columns = cot.shape[0] // residues
    depth = LANES // residues
    flat = jnp.dot(cot, sorted_wt_ref[...], preferred_element_type=F32) * scale
    blocks = lane_block((columns, LANES), depth)
    for tile in range(depth * depth // LANES):
        block = flat[:, tile * LANES : (tile + 1) * LANES]
        turned = [block] + [pltpu.roll(block, depth * t, 1) for t in range(1, residues)]
        for e in range(residues):
            turn_ref[pl.ds(tile * residues + e, columns, stride=depth), :] = pick(
                blocks,
                [
                    turned[(i - e) % residues][i * columns : (i + 1) * columns]
                    for i in range(residues)
                ],
            )
    return turn_ref[...].astype(BF16)


def small_own_kernel(scale, own_ref, other_ref, w_ref, both_ref,
                     keep_ref, outer_near_ref, outer_far_ref, sorted_w_ref, sorted_wt_ref,
                     order_ref, repeat_ref, turn_refs, wide_ref):
    residues, columns, _ = own_ref.shape
    depth = LANES // residues
    wide_ref[...] = w_ref[...].astype(F32)
    for d in range(depth):
        sorted_w_ref[d * depth : (d + 1) * depth, :] = wide_ref[
            pl.ds(d, depth, stride=depth), :
        ].astype(BF16)
    sorted_wt_ref[...] = sorted_w_ref[...].T
    rank = lax.axis_index("res")
    own_is_near = lax.axis_index("seq") == lax.shift_right_logical(rank, 2)
    own = own_ref[...].reshape(residues * columns, LANES)
    other = other_ref[...].reshape(residues * columns, LANES)
    near = outer_rows(
        scale, jnp.where(own_is_near, own, other), residues, sorted_wt_ref, turn_refs[0]
    )
    outer_near_ref[...] = near
    partial = lax.dot_general(both_ref[0], near, NT, preferred_element_type=F32)
    for place in range(columns // residues):
        keep_ref[lax.bitwise_xor(rank & 3, place)] = partial[:, place * LANES : (place + 1) * LANES]
    outer_far_ref[...] = outer_rows(
        scale, jnp.where(own_is_near, other, own), residues, sorted_wt_ref, turn_refs[1]
    )
    order_ref[...] = one_hot(
        lambda row: (
            (2 * (row >> 6 & 1) + (row >> 2 & 1)) * LANES
            + (row & 3) * depth + (row >> 3 & 7) * residues + (row >> 7)
        ),
        order_ref.shape,
    )
    for place in range(residues):
        shape = (LANES, LANES)
        row = lax.broadcasted_iota(jnp.int32, shape, 0)
        lane = lax.broadcasted_iota(jnp.int32, shape, 1)
        repeat_ref[:, place * LANES : (place + 1) * LANES] = jnp.where(
            row == place * depth + lane % depth, 1.0, 0.0
        ).astype(BF16)


def one_hot(target, shape):
    part = (shape[0], LANES)
    wanted = target(lax.broadcasted_iota(jnp.int32, part, 0))
    lane = lax.broadcasted_iota(jnp.int32, part, 1)
    return jnp.concatenate(
        [
            jnp.where(wanted == lane + tile * LANES, 1.0, 0.0).astype(BF16)
            for tile in range(shape[1] // LANES)
        ],
        axis=1,
    )


def blocks_apart(left, repeat, residues):
    depth = LANES // residues
    wide = jnp.dot(left, repeat, preferred_element_type=F32)
    blocks = lane_block(wide.shape, depth) % residues
    return jnp.concatenate(
        [jnp.where(blocks == e, wide, 0.0).astype(BF16) for e in range(residues)], axis=0
    )


def small_partner_kernel(scale, residues, got_ref, sorted_wt_ref, keep_ref, both_ref, order_ref,
                         repeat_ref, leaving_ref, keep_out_ref, right_ref, swap_ref):
    rank = lax.axis_index("res")
    seqs = got_ref.shape[1]
    cot = got_ref[2:4].reshape(2 * seqs, LANES)
    columns = cot.shape[0] // residues
    tiles = sorted_wt_ref.shape[1] // LANES
    flat = jnp.dot(cot, sorted_wt_ref[...], preferred_element_type=F32) * scale
    outer = jnp.concatenate(
        [
            jnp.concatenate(
                [
                    flat[i * columns + start : i * columns + start + 8, tile * LANES : (tile + 1) * LANES]
                    for start in range(0, columns, 8)
                    for tile in range(tiles)
                ],
                axis=0,
            )
            for i in range(residues)
        ],
        axis=1,
    ).astype(BF16)
    apart = blocks_apart(got_ref[0], repeat_ref[...], residues)
    partial = lax.dot_general(apart, outer, NT, preferred_element_type=F32).astype(BF16)
    partial = jnp.concatenate(
        [partial[e * seqs : (e + 1) * seqs] for e in range(residues)], axis=1
    )
    partial = jnp.dot(partial, order_ref[...], preferred_element_type=F32)
    right_ref[0] = both_ref[1]
    right_ref[1] = got_ref[1]
    own_is_near = lax.axis_index("seq") == lax.shift_right_logical(rank, 2)
    swap_ref[0] = jnp.where(own_is_near, got_ref[1], both_ref[1])
    swap_ref[1] = both_ref[0]
    for place in range(leaving_ref.shape[0]):
        leaving_ref[place, 0] = both_ref[1]
        leaving_ref[place, 1] = got_ref[1]
    for place in range(leaving_ref.shape[0]):
        distance = lax.bitwise_xor(rank & 3, place)
        total = keep_ref[distance] + partial[:, place * LANES : (place + 1) * LANES]
        leaving_ref[distance, 2] = total.astype(BF16)
        keep_out_ref[distance] = total


def pair_rows(scale, right, left, residues, sorted_w_ref, turn_ref):
    depth = LANES // residues
    columns = right.shape[1] // depth
    turn_ref[...] = lax.dot_general(right, left, TN, preferred_element_type=F32) * scale
    blocks = lane_block((columns, LANES), depth)
    tiles = []
    for tile in range(depth * depth // LANES):
        pieces = [
            turn_ref[pl.ds(tile * residues + e, columns, stride=depth), :]
            for e in range(residues)
        ]
        lines = jnp.concatenate(pieces, axis=0)
        turned = [lines] + [pltpu.roll(lines, depth * t, 1) for t in range(1, residues)]
        tiles.append(
            jnp.concatenate(
                [
                    pick(
                        blocks,
                        [
                            turned[(e - i) % residues][e * columns : (e + 1) * columns]
                            for e in range(residues)
                        ],
                    )
                    for i in range(residues)
                ],
                axis=0,
            )
        )
    flat = jnp.concatenate(tiles, axis=1)
    rows = residues * columns
    parts = jnp.concatenate(split_two(flat), axis=0)
    pair = jnp.dot(parts, sorted_w_ref[...], preferred_element_type=F32)
    return pair[0:rows] + pair[rows : 2 * rows]


def left_share(block_refs, masks, outer_near_ref, outer_far_ref):
    here = lax.axis_index("res") & 3
    spots = [
        pl.ds(pl.multiple_of(lax.bitwise_xor(here, mask) * LANES, LANES), LANES) for mask in masks
    ]
    right = jnp.concatenate([ref[0] for ref in block_refs] + [ref[1] for ref in block_refs], axis=1)
    outer = jnp.concatenate(
        [outer_near_ref[spot, :] for spot in spots] + [outer_far_ref[spot, :] for spot in spots],
        axis=0,
    )
    return jnp.dot(right, outer, preferred_element_type=F32)


def own_half():
    near = lax.axis_index("seq") == lax.shift_right_logical(lax.axis_index("res"), 2)
    return jnp.where(near, 0, 1)


def small_early_kernel(
    scale, right_ref, part_ref, swapped_ref, swapped_late_ref, both_ref, outer_near_ref, outer_far_ref,
    keep_ref, sorted_w_ref,
    pair_ref, left_cot_ref, right_cot_ref, turn_ref,
):
    residues = pair_ref.shape[1] // 4
    left_cot_ref[...] = left_share([right_ref, part_ref], (0, 3), outer_near_ref, outer_far_ref)
    right_cot_ref[...] = keep_ref[0] + part_ref[2].astype(F32)
    half = own_half()
    right = jnp.concatenate(
        [
            jnp.concatenate([right_ref[half], part_ref[half]], axis=1),
            jnp.concatenate([swapped_ref[0], swapped_late_ref[...]], axis=1),
        ],
        axis=0,
    )
    left = jnp.concatenate([both_ref[0], swapped_ref[1]], axis=0)
    pair = pair_rows(scale, right, left, residues, sorted_w_ref, turn_ref)
    store_pairs(pair, (0, 1), residues, pair_ref)


def store_pairs(pair, spots, residues, pair_ref):
    columns = pair.shape[0] // residues // len(spots)
    for i in range(residues):
        for place, spot in enumerate(spots):
            start = (i * len(spots) + place) * columns
            pair_ref[spot, i * columns : (i + 1) * columns, :] = pair[start : start + columns]


def small_finish_kernel(
    scale, part_refs, swapped_ref, both_ref, outer_near_ref, outer_far_ref, early_pair_ref,
    early_left_ref, early_right_ref, normed_ref, inv_std_ref, gain_ref, spread_w_ref, sorted_w_ref,
    offset_ref, grad_hbm, pair_hbm, grad_ref, pair_ref, pairs_ref, turn_ref, semaphores,
):
    seqs, residues, _ = grad_ref.shape
    columns = pair_ref.shape[1]
    depth = LANES // residues
    ranks = columns // residues

    left_cot = early_left_ref[...] + left_share(part_refs, (1, 2), outer_near_ref, outer_far_ref)
    right_cot = early_right_ref[...]
    for part_ref in part_refs:
        right_cot = right_cot + part_ref[2].astype(F32)
    blocks = lane_block((seqs, LANES), depth)
    spread = jnp.concatenate(
        [
            jnp.concatenate(
                [jnp.where(blocks == place, cot, 0.0) for cot in (left_cot, right_cot)], axis=1
            )
            for place in range(residues)
        ],
        axis=0,
    )
    rows = residues * seqs
    parts = jnp.concatenate(split_two(spread), axis=0)
    ln_cot = jnp.dot(parts, spread_w_ref[...], preferred_element_type=F32)
    ln_cot = ln_cot[0:rows] + ln_cot[rows : 2 * rows]
    gained = ln_cot * gain_ref[...]
    normed = normed_ref[...]
    grad = inv_std_ref[:, 0:1] * (
        gained
        - jnp.mean(gained, axis=-1, keepdims=True)
        - normed * jnp.mean(gained * normed, axis=-1, keepdims=True)
    )
    for place in range(residues):
        grad_ref[:, place, :] = grad[place * seqs : (place + 1) * seqs].astype(BF16)
    grad_copy = pltpu.make_async_copy(grad_ref, grad_hbm, semaphores.at[0])
    grad_copy.start()

    half = own_half()
    right = jnp.concatenate(
        [
            jnp.concatenate([ref[half] for ref in part_refs], axis=1),
            jnp.concatenate([ref[3] for ref in part_refs], axis=1),
        ],
        axis=0,
    )
    left = jnp.concatenate([both_ref[0], swapped_ref[1]], axis=0)
    pair = pair_rows(scale, right, left, residues, sorted_w_ref, turn_ref)
    pairs_ref[0] = early_pair_ref[0]
    pairs_ref[3] = early_pair_ref[1]
    store_pairs(pair, (1, 2), residues, pairs_ref)
    here = lax.axis_index("res") & 3
    placed = [pairs_ref[lax.bitwise_xor(here, place)] for place in range(ranks)]
    for i in range(residues):
        own = [block[i * residues : (i + 1) * residues] for block in placed]
        pair_ref[i] = (jnp.concatenate(own, axis=0) + offset_ref[...]).astype(BF16)
    pair_copy = pltpu.make_async_copy(pair_ref, pair_hbm, semaphores.at[1])
    pair_copy.start()
    grad_copy.wait()
    pair_copy.wait()


def small_slice(
    homolog_matrix,
    standardizer_scaling,
    standardizer_offset,
    left_projection_matrix,
    left_offset_vector,
    right_projection_matrix,
    right_offset_vector,
    coupling_matrix,
    coupling_offset,
    coupling_cotangent,
):
    seqs, residues, features = homolog_matrix.shape
    depth = left_projection_matrix.shape[1]
    ranks = lax.axis_size("res")
    rows = seqs * residues
    scale = 1.0 / (seqs * lax.axis_size("seq"))
    rank = lax.axis_index("res")
    mine = lax.axis_index("seq")
    swap = [(0, 1), (1, 0)]
    limit = pltpu.CompilerParams(vmem_limit_bytes=8 * 1024 * 1024)
    vmem = pl.BlockSpec(memory_space=pltpu.VMEM)
    like = jax.ShapeDtypeStruct

    other_cot = lax.ppermute(coupling_cotangent, "seq", swap)
    hbm = pl.BlockSpec(memory_space=pltpu.HBM)
    pin = lambda array: pltpu.with_memory_space_constraint(array, pltpu.HBM)
    both, normed, inv_std, spread_w, gain, pair_offset, own_cot = pl.pallas_call(
        small_project_kernel,
        in_specs=[hbm] * 9,
        out_specs=[vmem] * 7,
        out_shape=(
            like((2, seqs, LANES), BF16),
            like((rows, features), F32),
            like((rows, LANES), F32),
            like((2 * LANES, features), BF16),
            like((1, features), F32),
            like((1, LANES), F32),
            like(coupling_cotangent.shape, BF16),
        ),
        scratch_shapes=[
            pltpu.VMEM(homolog_matrix.shape, BF16),
            pltpu.VMEM((1, features), F32),
            pltpu.VMEM((depth, features), BF16),
            pltpu.VMEM((1, depth), F32),
            pltpu.VMEM((depth, features), BF16),
            pltpu.VMEM((1, depth), F32),
            pltpu.SemaphoreType.DMA((12,)),
        ],
        compiler_params=limit,
        name="project",
    )(
        *[
            pin(array)
            for array in (
                homolog_matrix,
                standardizer_scaling.reshape(1, -1),
                standardizer_offset.reshape(1, -1),
                left_projection_matrix.T,
                left_offset_vector.reshape(1, -1),
                right_projection_matrix.T,
                right_offset_vector.reshape(1, -1),
                coupling_offset.reshape(1, -1),
                coupling_cotangent,
            )
        ]
    )

    def swap_over(mask, value):
        return lax.ppermute(value, "res", [(source, source ^ mask) for source in range(ranks)])

    own_is_near = mine == lax.shift_right_logical(rank, 2)
    far_cot = jnp.where(own_is_near, other_cot, own_cot).reshape(2, seqs, LANES)
    beyond_two = swap_over(4, jnp.concatenate([both, far_cot]))

    half_rows = ranks // 2 * LANES
    turn = pltpu.VMEM((half_rows, LANES), F32)
    keep, outer_near, outer_far, sorted_w, sorted_wt, order, repeat = pl.pallas_call(
        functools.partial(small_own_kernel, scale),
        in_specs=[vmem] * 4,
        out_specs=[vmem] * 7,
        out_shape=(
            like((ranks // 2, seqs, LANES), F32),
            like((half_rows, LANES), BF16),
            like((half_rows, LANES), BF16),
            like(coupling_matrix.shape, BF16),
            like(coupling_matrix.shape[::-1], BF16),
            like((half_rows, half_rows), BF16),
            like((LANES, residues * LANES), BF16),
        ),
        scratch_shapes=[[turn, turn], pltpu.VMEM(coupling_matrix.shape, F32)],
        compiler_params=limit,
        name="own_pieces",
    )(own_cot, other_cot, coupling_matrix, both)

    leaving_parts, keep, right, leaving = pl.pallas_call(
        functools.partial(small_partner_kernel, scale, residues),
        in_specs=[vmem] * 6,
        out_specs=[vmem] * 4,
        out_shape=(
            like((ranks // 2, 3, seqs, LANES), BF16),
            like((ranks // 2, seqs, LANES), F32),
            like((2, seqs, LANES), BF16),
            like((2, seqs, LANES), BF16),
        ),
        compiler_params=limit,
        name="partner_pieces",
    )(beyond_two, sorted_wt, keep, both, order, repeat)

    swapped = lax.ppermute(leaving, "seq", swap)
    diagonal = swap_over(3, leaving_parts[3])
    across, beside = [
        swap_over(mask, jnp.concatenate([leaving_parts[mask], swapped[0:1]])) for mask in (2, 1)
    ]
    swapped_late = lax.ppermute(
        jnp.where(own_is_near, diagonal[1], diagonal[0]), "seq", swap
    )

    pair_turn = pltpu.VMEM((2 * LANES, LANES), F32)
    early_pair, early_left, early_right = pl.pallas_call(
        functools.partial(small_early_kernel, scale),
        in_specs=[vmem] * 9,
        out_specs=[vmem] * 3,
        out_shape=(
            like((2, residues * residues, LANES), F32),
            like((seqs, LANES), F32),
            like((seqs, LANES), F32),
        ),
        scratch_shapes=[pair_turn],
        compiler_params=limit,
        name="early",
    )(right, diagonal, swapped, swapped_late, both, outer_near, outer_far, keep, sorted_w)

    gradient, pair_delta = pl.pallas_call(
        functools.partial(small_finish_kernel, scale),
        in_specs=[[vmem] * 2] + [vmem] * 13,
        out_specs=[pl.BlockSpec(memory_space=pl.ANY)] * 2,
        out_shape=(
            like(homolog_matrix.shape, BF16),
            like(coupling_cotangent.shape, BF16),
        ),
        scratch_shapes=[
            pltpu.VMEM(homolog_matrix.shape, BF16),
            pltpu.VMEM(coupling_cotangent.shape, BF16),
            pltpu.VMEM((ranks // 2, residues * residues, LANES), F32),
            pair_turn,
            pltpu.SemaphoreType.DMA((2,)),
        ],
        compiler_params=limit,
        name="finish",
    )(
        [beside, across],
        swapped,
        both,
        outer_near,
        outer_far,
        early_pair,
        early_left,
        early_right,
        normed,
        inv_std,
        gain,
        spread_w,
        sorted_w,
        pair_offset,
    )
    return (pair_delta, gradient)


def body(*arrays):
    if lax.axis_size("res") == 8:
        return small_slice(*arrays)
    return wide_slice(*arrays)


def solution(mesh):
    return jax.shard_map(
        body,
        mesh=mesh,
        in_specs=(
            P(("grp", "seq"), "res", None),
            P(),
            P(),
            P(),
            P(),
            P(),
            P(),
            P(),
            P(),
            P(("grp", "res"), "seq", None),
        ),
        out_specs=(P(("grp", "res"), "seq", None), P(("grp", "seq"), "res", None)),
        check_vma=False,
    )
```

```python
import functools

import jax
import jax.numpy as jnp
from jax import lax
from jax.experimental import pallas as pl
from jax.experimental.pallas import tpu as pltpu
from jax.sharding import PartitionSpec as P

LANES = 128
BF16 = jnp.bfloat16
F32 = jnp.float32
NT = (((1,), (1,)), ((), ()))
TN = (((0,), (0,)), ((), ()))


def lane_block(shape, width):
    return lax.broadcasted_iota(jnp.int32, shape, 1) // width


def pick(blocks, pieces):
    result = pieces[0]
    for place in range(1, len(pieces)):
        result = jnp.where(blocks == place, pieces[place], result)
    return result


def split_three(value):
    top = value.astype(BF16)
    rest = value - top.astype(F32)
    middle = rest.astype(BF16)
    low = (rest - middle.astype(F32)).astype(BF16)
    return top, middle, low


def split_two(value):
    top = value.astype(BF16)
    return top, (value - top.astype(F32)).astype(BF16)


def normalise(rows):
    centred = rows - jnp.mean(rows, axis=-1, keepdims=True)
    inv_std = lax.rsqrt(jnp.mean(centred * centred, axis=-1, keepdims=True) + 1e-05)
    return centred * inv_std, inv_std


def residue_rows(x_ref):
    return jnp.concatenate(
        [x_ref[:, place, :].astype(F32) for place in range(x_ref.shape[1])], axis=0
    )


def project_kernel(
    x_ref, gain_ref, offset_ref, left_w_ref, left_b_ref, right_w_ref, right_b_ref, w_ref,
    left_ref, right_ref, sorted_w_ref, wide_ref,
):
    seqs, residues, _ = x_ref.shape
    depth = left_w_ref.shape[0]
    normed, _ = normalise(residue_rows(x_ref))
    ln_out = (normed * gain_ref[...] + offset_ref[...]).astype(BF16)
    blocks = lane_block((seqs, LANES), depth)
    for weight_ref, bias_ref, out_ref in (
        (left_w_ref, left_b_ref, left_ref),
        (right_w_ref, right_b_ref, right_ref),
    ):
        weight = jnp.concatenate([weight_ref[...]] * residues, axis=0)
        bias = jnp.concatenate([bias_ref[...]] * residues, axis=1)
        wide = lax.dot_general(ln_out, weight, NT, preferred_element_type=F32)
        own = pick(blocks, [wide[p * seqs : (p + 1) * seqs] for p in range(residues)])
        out_ref[...] = (own + bias).astype(BF16)
    wide_ref[...] = w_ref[...].astype(F32)
    for d in range(depth):
        sorted_w_ref[d * depth : (d + 1) * depth, :] = wide_ref[
            pl.ds(d, depth, stride=depth), :
        ].astype(BF16)


def cot_kernel(scale, own_ref, other_ref, sorted_w_ref, left_ref, right_ref,
               send_ref, outer_ref, turn_ref):
    residues, columns, _ = own_ref.shape
    depth = sorted_w_ref.shape[0] // (LANES // residues)
    depth = LANES // residues
    first = lax.axis_index("seq") == 0
    own = own_ref[...].reshape(residues * columns, LANES)
    other = other_ref[...].reshape(residues * columns, LANES)
    low = jnp.where(first, own, other)
    high = jnp.where(first, other, own)
    both = jnp.concatenate([low, high], axis=0)
    flat = lax.dot_general(both, sorted_w_ref[...], NT, preferred_element_type=F32) * scale
    blocks = lane_block((columns, LANES), depth)
    for half in range(2):
        for tile in range(depth * depth // LANES):
            block = flat[
                half * residues * columns : (half + 1) * residues * columns,
                tile * LANES : (tile + 1) * LANES,
            ]
            turned = [block] + [pltpu.roll(block, depth * t, 1) for t in range(1, residues)]
            for e in range(residues):
                piece = pick(
                    blocks,
                    [
                        turned[(i - e) % residues][i * columns : (i + 1) * columns]
                        for i in range(residues)
                    ],
                )
                turn_ref[pl.ds(half * columns * depth + tile * residues + e, columns, stride=depth), :] = piece
    outer = turn_ref[...].astype(BF16)
    half_rows = columns * depth
    partial = lax.dot_general(left_ref[...], outer, NT, preferred_element_type=F32).astype(BF16)
    seqs = left_ref.shape[0]
    ranks = columns // residues
    for half in range(2):
        outer_ref[half] = outer[half * half_rows : (half + 1) * half_rows]
        for rank in range(ranks):
            at = (half * ranks + rank) * LANES
            send_ref[half, rank, 0:seqs, :] = right_ref[...]
            send_ref[half, rank, seqs : 2 * seqs, :] = partial[:, at : at + LANES]


def grad_kernel(steps, got_ref, outer_ref, x_ref, gain_ref, left_w_ref, right_w_ref,
                grad_ref, left_cot_ref, right_cot_ref):
    step = pl.program_id(0)
    _, ranks, twice, _ = got_ref.shape
    seqs = twice // 2
    residues = x_ref.shape[1]
    depth = LANES // residues

    @pl.when(step == 0)
    def _():
        left_cot_ref[...] = jnp.zeros_like(left_cot_ref)
        right_cot_ref[...] = jnp.zeros_like(right_cot_ref)

    places = [(half, rank) for half in range(2) for rank in range(ranks)]
    right_all = jnp.concatenate([got_ref[h, r, 0:seqs, :] for h, r in places], axis=1)
    outer = jnp.concatenate([outer_ref[0], outer_ref[1]], axis=0)
    left_cot_ref[...] += jnp.dot(right_all, outer, preferred_element_type=F32)
    total = got_ref[0, 0, seqs:twice, :].astype(F32)
    for h, r in places[1:]:
        total = total + got_ref[h, r, seqs:twice, :].astype(F32)
    right_cot_ref[...] += total

    @pl.when(step == steps - 1)
    def _():
        blocks = lane_block((seqs, LANES), depth)
        left_cot, right_cot = left_cot_ref[...], right_cot_ref[...]
        spread = jnp.concatenate(
            [
                jnp.concatenate(
                    [
                        jnp.where(blocks == place, left_cot, 0.0),
                        jnp.where(blocks == place, right_cot, 0.0),
                    ],
                    axis=1,
                )
                for place in range(residues)
            ],
            axis=0,
        )
        weight = jnp.concatenate(
            [left_w_ref[...]] * residues + [right_w_ref[...]] * residues, axis=0
        )
        rows = residues * seqs
        parts = jnp.concatenate(split_three(spread), axis=0)
        ln_cot = jnp.dot(parts, weight, preferred_element_type=F32)
        ln_cot = ln_cot[0:rows] + (ln_cot[rows : 2 * rows] + ln_cot[2 * rows : 3 * rows])
        gained = ln_cot * gain_ref[...]
        normed, inv_std = normalise(residue_rows(x_ref))
        grad = inv_std * (
            gained
            - jnp.mean(gained, axis=-1, keepdims=True)
            - normed * jnp.mean(gained * normed, axis=-1, keepdims=True)
        )
        for place in range(residues):
            grad_ref[:, place, :] = grad[place * seqs : (place + 1) * seqs].astype(BF16)


def pair_kernel(scale, got_ref, far_ref, left_ref, far_left_ref, sorted_w_ref, offset_ref,
                pair_ref, turn_ref):
    residues, columns, _ = pair_ref.shape
    depth = LANES // residues
    ranks = columns // residues
    mine = lax.axis_index("seq")
    near = jnp.concatenate([got_ref[mine, r] for r in range(ranks)], axis=1)
    far = jnp.concatenate([far_ref[r] for r in range(ranks)], axis=1)
    right = jnp.concatenate([near, far], axis=0)
    left = jnp.concatenate([left_ref[...], far_left_ref[...]], axis=0)
    turn_ref[...] = lax.dot_general(right, left, TN, preferred_element_type=F32) * scale
    blocks = lane_block((columns, LANES), depth)
    tiles = []
    for tile in range(depth * depth // LANES):
        pieces = [
            turn_ref[pl.ds(tile * residues + e, columns, stride=depth), :]
            for e in range(residues)
        ]
        rows = jnp.concatenate(pieces, axis=0)
        turned = [rows] + [pltpu.roll(rows, depth * t, 1) for t in range(1, residues)]
        tiles.append(
            jnp.concatenate(
                [
                    pick(
                        blocks,
                        [
                            turned[(e - i) % residues][e * columns : (e + 1) * columns]
                            for e in range(residues)
                        ],
                    )
                    for i in range(residues)
                ],
                axis=0,
            )
        )
    flat = jnp.concatenate(tiles, axis=1)
    rows = residues * columns
    parts = jnp.concatenate(split_three(flat), axis=0)
    pair = jnp.dot(parts, sorted_w_ref[...], preferred_element_type=F32)
    pair = pair[0:rows] + (pair[rows : 2 * rows] + pair[2 * rows : 3 * rows])
    pair_ref[...] = (pair + offset_ref[...]).astype(BF16).reshape(pair_ref.shape)


def wide_slice(
    homolog_matrix,
    standardizer_scaling,
    standardizer_offset,
    left_projection_matrix,
    left_offset_vector,
    right_projection_matrix,
    right_offset_vector,
    coupling_matrix,
    coupling_offset,
    coupling_cotangent,
):
    seqs, residues, features = homolog_matrix.shape
    depth = left_projection_matrix.shape[1]
    ranks = lax.axis_size("res")
    scale = 1.0 / (seqs * lax.axis_size("seq"))
    half_ranks = ranks // 2
    half_columns = half_ranks * residues
    step_ranks = 4
    columns = step_ranks * residues
    steps = half_ranks // step_ranks
    mine = lax.axis_index("seq")
    swap = [(0, 1), (1, 0)]

    other_cot = lax.ppermute(coupling_cotangent, "seq", swap)
    gain = standardizer_scaling.reshape(1, -1)
    left_w = left_projection_matrix.T
    right_w = right_projection_matrix.T

    left, right, sorted_w = pl.pallas_call(
        project_kernel,
        out_shape=(
            jax.ShapeDtypeStruct((seqs, LANES), BF16),
            jax.ShapeDtypeStruct((seqs, LANES), BF16),
            jax.ShapeDtypeStruct(coupling_matrix.shape, BF16),
        ),
        scratch_shapes=[pltpu.VMEM(coupling_matrix.shape, F32)],
        name="project",
    )(
        homolog_matrix,
        gain,
        standardizer_offset.reshape(1, -1),
        left_w,
        left_offset_vector.reshape(1, -1),
        right_w,
        right_offset_vector.reshape(1, -1),
        coupling_matrix,
    )

    whole = lambda shape: pl.BlockSpec(shape, lambda g: (0,) * len(shape))
    cot_block = pl.BlockSpec((residues, columns, LANES), lambda g: (0, g, 0))
    outer_block = pl.BlockSpec((2, columns * depth, LANES), lambda g: (0, g, 0))
    send_block = pl.BlockSpec((2, step_ranks, 2 * seqs, LANES), lambda g: (0, g, 0, 0))
    send, outer = pl.pallas_call(
        functools.partial(cot_kernel, scale),
        grid=(steps,),
        in_specs=[
            cot_block,
            cot_block,
            whole(sorted_w.shape),
            whole(left.shape),
            whole(right.shape),
        ],
        out_specs=(send_block, outer_block),
        out_shape=(
            jax.ShapeDtypeStruct((2, half_ranks, 2 * seqs, LANES), BF16),
            jax.ShapeDtypeStruct((2, half_columns * depth, LANES), BF16),
        ),
        scratch_shapes=[pltpu.VMEM((2 * columns * depth, LANES), F32)],
        name="cotangent",
    )(coupling_cotangent, other_cot, sorted_w, left, right)

    got = lax.all_to_all(
        send.reshape(ranks, 2 * seqs, LANES), "res", split_axis=0, concat_axis=0, tiled=True
    ).reshape(send.shape)

    leaving = lax.dynamic_index_in_dim(got, 1 - mine, 0, keepdims=False)[:, 0:seqs, :]
    far = lax.ppermute(jnp.concatenate([leaving, left[None]], axis=0), "seq", swap)

    gradient = pl.pallas_call(
        functools.partial(grad_kernel, steps),
        grid=(steps,),
        in_specs=[
            send_block,
            outer_block,
            whole(homolog_matrix.shape),
            whole(gain.shape),
            whole(left_w.shape),
            whole(right_w.shape),
        ],
        out_specs=whole(homolog_matrix.shape),
        out_shape=jax.ShapeDtypeStruct(homolog_matrix.shape, BF16),
        scratch_shapes=[pltpu.VMEM((seqs, LANES), F32)] * 2,
        name="gradient",
    )(got, outer, homolog_matrix, gain, left_w, right_w)

    pair_delta = pl.pallas_call(
        functools.partial(pair_kernel, scale),
        grid=(steps,),
        in_specs=[
            pl.BlockSpec((2, step_ranks, seqs, LANES), lambda g: (0, g, 0, 0)),
            pl.BlockSpec((step_ranks, seqs, LANES), lambda g: (g, 0, 0)),
            whole(left.shape),
            pl.BlockSpec((None, seqs, LANES), lambda g: (half_ranks, 0, 0)),
            whole(sorted_w.shape),
            whole((1, LANES)),
        ],
        out_specs=cot_block,
        out_shape=jax.ShapeDtypeStruct(coupling_cotangent.shape, BF16),
        scratch_shapes=[pltpu.VMEM((columns * depth, LANES), F32)],
        name="pair",
    )(got, far, left, far, sorted_w, coupling_offset.reshape(1, -1))
    return (pair_delta, gradient)


def fetch(source, target, semaphore):
    copy = pltpu.make_async_copy(source, target, semaphore)
    copy.start()
    return copy


def start_copies(pairs, semaphores):
    copies = [
        pltpu.make_async_copy(source, target, semaphores.at[place])
        for place, (source, target) in enumerate(pairs)
    ]
    for copy in copies:
        copy.start()
    return copies


def small_project_kernel(
    x_hbm, gain_hbm, offset_hbm, left_w_hbm, left_b_hbm, right_w_hbm, right_b_hbm, pair_offset_hbm,
    cot_hbm, both_ref, normed_ref, inv_std_ref, spread_w_ref, gain_ref, pair_offset_ref, cot_ref,
    x_ref, offset_ref, left_w_ref, left_b_ref, right_w_ref, right_b_ref, semaphores,
):
    seqs, residues, _ = x_ref.shape
    depth = left_w_ref.shape[0]
    parts = 4
    part = seqs // parts
    copies = start_copies(
        tuple(
            (x_hbm.at[pl.ds(place * part, part)], x_ref.at[pl.ds(place * part, part)])
            for place in range(parts)
        )
        + (
            (left_w_hbm, left_w_ref),
            (right_w_hbm, right_w_ref),
            (gain_hbm, gain_ref),
            (offset_hbm, offset_ref),
            (left_b_hbm, left_b_ref),
            (right_b_hbm, right_b_ref),
            (cot_hbm, cot_ref),
            (pair_offset_hbm, pair_offset_ref),
        ),
        semaphores,
    )
    for copy in copies[:parts]:
        copy.wait()
    normed, inv_std = normalise(residue_rows(x_ref))
    for copy in copies[parts:]:
        copy.wait()
    ln_out = (normed * gain_ref[...] + offset_ref[...]).astype(BF16)
    blocks = lane_block((seqs, LANES), depth)
    weight = jnp.concatenate(
        [left_w_ref[...]] * residues + [right_w_ref[...]] * residues, axis=0
    )
    wide = lax.dot_general(ln_out, weight, NT, preferred_element_type=F32)
    for place, bias_ref in enumerate((left_b_ref, right_b_ref)):
        bias = jnp.concatenate([bias_ref[...]] * residues, axis=1)
        lanes = wide[:, place * LANES : (place + 1) * LANES]
        own = pick(blocks, [lanes[p * seqs : (p + 1) * seqs] for p in range(residues)])
        both_ref[place] = (own + bias).astype(BF16)
    normed_ref[...] = normed
    inv_std_ref[...] = jnp.broadcast_to(inv_std, inv_std_ref.shape)
    spread_w_ref[...] = weight


def outer_rows(scale, cot, residues, sorted_wt_ref, turn_ref):
    columns = cot.shape[0] // residues
    depth = LANES // residues
    flat = jnp.dot(cot, sorted_wt_ref[...], preferred_element_type=F32) * scale
    blocks = lane_block((columns, LANES), depth)
    for tile in range(depth * depth // LANES):
        block = flat[:, tile * LANES : (tile + 1) * LANES]
        turned = [block] + [pltpu.roll(block, depth * t, 1) for t in range(1, residues)]
        for e in range(residues):
            turn_ref[pl.ds(tile * residues + e, columns, stride=depth), :] = pick(
                blocks,
                [
                    turned[(i - e) % residues][i * columns : (i + 1) * columns]
                    for i in range(residues)
                ],
            )
    return turn_ref[...].astype(BF16)


def small_own_kernel(scale, own_ref, other_ref, w_ref, both_ref,
                     keep_ref, outer_near_ref, outer_far_ref, sorted_w_ref, sorted_wt_ref,
                     order_ref, repeat_ref, turn_refs, wide_ref):
    residues, columns, _ = own_ref.shape
    depth = LANES // residues
    wide_ref[...] = w_ref[...].astype(F32)
    for d in range(depth):
        sorted_w_ref[d * depth : (d + 1) * depth, :] = wide_ref[
            pl.ds(d, depth, stride=depth), :
        ].astype(BF16)
    sorted_wt_ref[...] = sorted_w_ref[...].T
    rank = lax.axis_index("res")
    own_is_near = lax.axis_index("seq") == lax.shift_right_logical(rank, 2)
    own = own_ref[...].reshape(residues * columns, LANES)
    other = other_ref[...].reshape(residues * columns, LANES)
    near = outer_rows(
        scale, jnp.where(own_is_near, own, other), residues, sorted_wt_ref, turn_refs[0]
    )
    outer_near_ref[...] = near
    partial = lax.dot_general(both_ref[0], near, NT, preferred_element_type=F32)
    for place in range(columns // residues):
        keep_ref[lax.bitwise_xor(rank & 3, place)] = partial[:, place * LANES : (place + 1) * LANES]
    outer_far_ref[...] = outer_rows(
        scale, jnp.where(own_is_near, other, own), residues, sorted_wt_ref, turn_refs[1]
    )
    order_ref[...] = one_hot(
        lambda row: (
            (2 * (row >> 6 & 1) + (row >> 2 & 1)) * LANES
            + (row & 3) * depth + (row >> 3 & 7) * residues + (row >> 7)
        ),
        order_ref.shape,
    )
    for place in range(residues):
        shape = (LANES, LANES)
        row = lax.broadcasted_iota(jnp.int32, shape, 0)
        lane = lax.broadcasted_iota(jnp.int32, shape, 1)
        repeat_ref[:, place * LANES : (place + 1) * LANES] = jnp.where(
            row == place * depth + lane % depth, 1.0, 0.0
        ).astype(BF16)


def one_hot(target, shape):
    part = (shape[0], LANES)
    wanted = target(lax.broadcasted_iota(jnp.int32, part, 0))
    lane = lax.broadcasted_iota(jnp.int32, part, 1)
    return jnp.concatenate(
        [
            jnp.where(wanted == lane + tile * LANES, 1.0, 0.0).astype(BF16)
            for tile in range(shape[1] // LANES)
        ],
        axis=1,
    )


def blocks_apart(left, repeat, residues):
    depth = LANES // residues
    wide = jnp.dot(left, repeat, preferred_element_type=F32)
    blocks = lane_block(wide.shape, depth) % residues
    return jnp.concatenate(
        [jnp.where(blocks == e, wide, 0.0).astype(BF16) for e in range(residues)], axis=0
    )


def small_partner_kernel(scale, residues, got_ref, sorted_wt_ref, keep_ref, both_ref, order_ref,
                         repeat_ref, leaving_ref, keep_out_ref, right_ref, swap_ref):
    rank = lax.axis_index("res")
    seqs = got_ref.shape[1]
    cot = got_ref[2:4].reshape(2 * seqs, LANES)
    columns = cot.shape[0] // residues
    tiles = sorted_wt_ref.shape[1] // LANES
    flat = jnp.dot(cot, sorted_wt_ref[...], preferred_element_type=F32) * scale
    outer = jnp.concatenate(
        [
            jnp.concatenate(
                [
                    flat[i * columns + start : i * columns + start + 8, tile * LANES : (tile + 1) * LANES]
                    for start in range(0, columns, 8)
                    for tile in range(tiles)
                ],
                axis=0,
            )
            for i in range(residues)
        ],
        axis=1,
    ).astype(BF16)
    apart = blocks_apart(got_ref[0], repeat_ref[...], residues)
    partial = lax.dot_general(apart, outer, NT, preferred_element_type=F32).astype(BF16)
    partial = jnp.concatenate(
        [partial[e * seqs : (e + 1) * seqs] for e in range(residues)], axis=1
    )
    partial = jnp.dot(partial, order_ref[...], preferred_element_type=F32)
    right_ref[0] = both_ref[1]
    right_ref[1] = got_ref[1]
    own_is_near = lax.axis_index("seq") == lax.shift_right_logical(rank, 2)
    swap_ref[0] = jnp.where(own_is_near, got_ref[1], both_ref[1])
    swap_ref[1] = both_ref[0]
    for place in range(leaving_ref.shape[0]):
        leaving_ref[place, 0] = both_ref[1]
        leaving_ref[place, 1] = got_ref[1]
    for place in range(leaving_ref.shape[0]):
        distance = lax.bitwise_xor(rank & 3, place)
        total = keep_ref[distance] + partial[:, place * LANES : (place + 1) * LANES]
        leaving_ref[distance, 2] = total.astype(BF16)
        keep_out_ref[distance] = total


def pair_rows(scale, right, left, residues, sorted_w_ref, turn_ref):
    depth = LANES // residues
    columns = right.shape[1] // depth
    turn_ref[...] = lax.dot_general(right, left, TN, preferred_element_type=F32) * scale
    blocks = lane_block((columns, LANES), depth)
    tiles = []
    for tile in range(depth * depth // LANES):
        pieces = [
            turn_ref[pl.ds(tile * residues + e, columns, stride=depth), :]
            for e in range(residues)
        ]
        lines = jnp.concatenate(pieces, axis=0)
        turned = [lines] + [pltpu.roll(lines, depth * t, 1) for t in range(1, residues)]
        tiles.append(
            jnp.concatenate(
                [
                    pick(
                        blocks,
                        [
                            turned[(e - i) % residues][e * columns : (e + 1) * columns]
                            for e in range(residues)
                        ],
                    )
                    for i in range(residues)
                ],
                axis=0,
            )
        )
    flat = jnp.concatenate(tiles, axis=1)
    rows = residues * columns
    parts = jnp.concatenate(split_two(flat), axis=0)
    pair = jnp.dot(parts, sorted_w_ref[...], preferred_element_type=F32)
    return pair[0:rows] + pair[rows : 2 * rows]


def left_share(block_refs, masks, outer_near_ref, outer_far_ref):
    here = lax.axis_index("res") & 3
    spots = [
        pl.ds(pl.multiple_of(lax.bitwise_xor(here, mask) * LANES, LANES), LANES) for mask in masks
    ]
    right = jnp.concatenate([ref[0] for ref in block_refs] + [ref[1] for ref in block_refs], axis=1)
    outer = jnp.concatenate(
        [outer_near_ref[spot, :] for spot in spots] + [outer_far_ref[spot, :] for spot in spots],
        axis=0,
    )
    return jnp.dot(right, outer, preferred_element_type=F32)


def own_half():
    near = lax.axis_index("seq") == lax.shift_right_logical(lax.axis_index("res"), 2)
    return jnp.where(near, 0, 1)


def small_early_kernel(
    scale, right_ref, part_ref, swapped_ref, swapped_late_ref, both_ref, outer_near_ref, outer_far_ref,
    keep_ref, sorted_w_ref,
    pair_ref, left_cot_ref, right_cot_ref, turn_ref,
):
    residues = pair_ref.shape[1] // 4
    left_cot_ref[...] = left_share([right_ref, part_ref], (0, 3), outer_near_ref, outer_far_ref)
    right_cot_ref[...] = keep_ref[0] + part_ref[2].astype(F32)
    half = own_half()
    right = jnp.concatenate(
        [
            jnp.concatenate([right_ref[half], part_ref[half]], axis=1),
            jnp.concatenate([swapped_ref[0], swapped_late_ref[...]], axis=1),
        ],
        axis=0,
    )
    left = jnp.concatenate([both_ref[0], swapped_ref[1]], axis=0)
    pair = pair_rows(scale, right, left, residues, sorted_w_ref, turn_ref)
    store_pairs(pair, (0, 1), residues, pair_ref)


def store_pairs(pair, spots, residues, pair_ref):
    columns = pair.shape[0] // residues // len(spots)
    for i in range(residues):
        for place, spot in enumerate(spots):
            start = (i * len(spots) + place) * columns
            pair_ref[spot, i * columns : (i + 1) * columns, :] = pair[start : start + columns]


def small_finish_kernel(
    scale, part_refs, swapped_ref, both_ref, outer_near_ref, outer_far_ref, early_pair_ref,
    early_left_ref, early_right_ref, normed_ref, inv_std_ref, gain_ref, spread_w_ref, sorted_w_ref,
    offset_ref, grad_hbm, pair_hbm, grad_ref, pair_ref, pairs_ref, turn_ref, semaphores,
):
    seqs, residues, _ = grad_ref.shape
    columns = pair_ref.shape[1]
    depth = LANES // residues
    ranks = columns // residues

    left_cot = early_left_ref[...] + left_share(part_refs, (1, 2), outer_near_ref, outer_far_ref)
    right_cot = early_right_ref[...]
    for part_ref in part_refs:
        right_cot = right_cot + part_ref[2].astype(F32)
    blocks = lane_block((seqs, LANES), depth)
    spread = jnp.concatenate(
        [
            jnp.concatenate(
                [jnp.where(blocks == place, cot, 0.0) for cot in (left_cot, right_cot)], axis=1
            )
            for place in range(residues)
        ],
        axis=0,
    )
    rows = residues * seqs
    parts = jnp.concatenate(split_two(spread), axis=0)
    ln_cot = jnp.dot(parts, spread_w_ref[...], preferred_element_type=F32)
    ln_cot = ln_cot[0:rows] + ln_cot[rows : 2 * rows]
    gained = ln_cot * gain_ref[...]
    normed = normed_ref[...]
    grad = inv_std_ref[:, 0:1] * (
        gained
        - jnp.mean(gained, axis=-1, keepdims=True)
        - normed * jnp.mean(gained * normed, axis=-1, keepdims=True)
    )
    for place in range(residues):
        grad_ref[:, place, :] = grad[place * seqs : (place + 1) * seqs].astype(BF16)
    parts = 4
    part = seqs // parts
    copies = start_copies(
        tuple(
            (grad_ref.at[pl.ds(place * part, part)], grad_hbm.at[pl.ds(place * part, part)])
            for place in range(parts)
        ),
        semaphores,
    )

    half = own_half()
    right = jnp.concatenate(
        [
            jnp.concatenate([ref[half] for ref in part_refs], axis=1),
            jnp.concatenate([ref[3] for ref in part_refs], axis=1),
        ],
        axis=0,
    )
    left = jnp.concatenate([both_ref[0], swapped_ref[1]], axis=0)
    pair = pair_rows(scale, right, left, residues, sorted_w_ref, turn_ref)
    pairs_ref[0] = early_pair_ref[0]
    pairs_ref[3] = early_pair_ref[1]
    store_pairs(pair, (1, 2), residues, pairs_ref)
    here = lax.axis_index("res") & 3
    placed = [pairs_ref[lax.bitwise_xor(here, place)] for place in range(ranks)]
    for i in range(residues):
        own = [block[i * residues : (i + 1) * residues] for block in placed]
        pair_ref[i] = (jnp.concatenate(own, axis=0) + offset_ref[...]).astype(BF16)
    pair_copy = pltpu.make_async_copy(pair_ref, pair_hbm, semaphores.at[parts])
    pair_copy.start()
    for copy in copies:
        copy.wait()
    pair_copy.wait()


def small_slice(
    homolog_matrix,
    standardizer_scaling,
    standardizer_offset,
    left_projection_matrix,
    left_offset_vector,
    right_projection_matrix,
    right_offset_vector,
    coupling_matrix,
    coupling_offset,
    coupling_cotangent,
):
    seqs, residues, features = homolog_matrix.shape
    depth = left_projection_matrix.shape[1]
    ranks = lax.axis_size("res")
    rows = seqs * residues
    scale = 1.0 / (seqs * lax.axis_size("seq"))
    rank = lax.axis_index("res")
    mine = lax.axis_index("seq")
    swap = [(0, 1), (1, 0)]
    limit = pltpu.CompilerParams(vmem_limit_bytes=8 * 1024 * 1024)
    vmem = pl.BlockSpec(memory_space=pltpu.VMEM)
    like = jax.ShapeDtypeStruct

    other_cot = lax.ppermute(coupling_cotangent, "seq", swap)
    hbm = pl.BlockSpec(memory_space=pltpu.HBM)
    pin = lambda array: pltpu.with_memory_space_constraint(array, pltpu.HBM)
    both, normed, inv_std, spread_w, gain, pair_offset, own_cot = pl.pallas_call(
        small_project_kernel,
        in_specs=[hbm] * 9,
        out_specs=[vmem] * 7,
        out_shape=(
            like((2, seqs, LANES), BF16),
            like((rows, features), F32),
            like((rows, LANES), F32),
            like((2 * LANES, features), BF16),
            like((1, features), F32),
            like((1, LANES), F32),
            like(coupling_cotangent.shape, BF16),
        ),
        scratch_shapes=[
            pltpu.VMEM(homolog_matrix.shape, BF16),
            pltpu.VMEM((1, features), F32),
            pltpu.VMEM((depth, features), BF16),
            pltpu.VMEM((1, depth), F32),
            pltpu.VMEM((depth, features), BF16),
            pltpu.VMEM((1, depth), F32),
            pltpu.SemaphoreType.DMA((12,)),
        ],
        compiler_params=limit,
        name="project",
    )(
        *[
            pin(array)
            for array in (
                homolog_matrix,
                standardizer_scaling.reshape(1, -1),
                standardizer_offset.reshape(1, -1),
                left_projection_matrix.T,
                left_offset_vector.reshape(1, -1),
                right_projection_matrix.T,
                right_offset_vector.reshape(1, -1),
                coupling_offset.reshape(1, -1),
                coupling_cotangent,
            )
        ]
    )

    def swap_over(mask, value):
        return lax.ppermute(value, "res", [(source, source ^ mask) for source in range(ranks)])

    own_is_near = mine == lax.shift_right_logical(rank, 2)
    far_cot = jnp.where(own_is_near, other_cot, own_cot).reshape(2, seqs, LANES)
    beyond_two = swap_over(4, jnp.concatenate([both, far_cot]))

    half_rows = ranks // 2 * LANES
    turn = pltpu.VMEM((half_rows, LANES), F32)
    keep, outer_near, outer_far, sorted_w, sorted_wt, order, repeat = pl.pallas_call(
        functools.partial(small_own_kernel, scale),
        in_specs=[vmem] * 4,
        out_specs=[vmem] * 7,
        out_shape=(
            like((ranks // 2, seqs, LANES), F32),
            like((half_rows, LANES), BF16),
            like((half_rows, LANES), BF16),
            like(coupling_matrix.shape, BF16),
            like(coupling_matrix.shape[::-1], BF16),
            like((half_rows, half_rows), BF16),
            like((LANES, residues * LANES), BF16),
        ),
        scratch_shapes=[[turn, turn], pltpu.VMEM(coupling_matrix.shape, F32)],
        compiler_params=limit,
        name="own_pieces",
    )(own_cot, other_cot, coupling_matrix, both)

    leaving_parts, keep, right, leaving = pl.pallas_call(
        functools.partial(small_partner_kernel, scale, residues),
        in_specs=[vmem] * 6,
        out_specs=[vmem] * 4,
        out_shape=(
            like((ranks // 2, 3, seqs, LANES), BF16),
            like((ranks // 2, seqs, LANES), F32),
            like((2, seqs, LANES), BF16),
            like((2, seqs, LANES), BF16),
        ),
        compiler_params=limit,
        name="partner_pieces",
    )(beyond_two, sorted_wt, keep, both, order, repeat)

    swapped = lax.ppermute(leaving, "seq", swap)
    diagonal = swap_over(3, leaving_parts[3])
    across, beside = [
        swap_over(mask, jnp.concatenate([leaving_parts[mask], swapped[0:1]])) for mask in (2, 1)
    ]
    swapped_late = lax.ppermute(
        jnp.where(own_is_near, diagonal[1], diagonal[0]), "seq", swap
    )

    pair_turn = pltpu.VMEM((2 * LANES, LANES), F32)
    early_pair, early_left, early_right = pl.pallas_call(
        functools.partial(small_early_kernel, scale),
        in_specs=[vmem] * 9,
        out_specs=[vmem] * 3,
        out_shape=(
            like((2, residues * residues, LANES), F32),
            like((seqs, LANES), F32),
            like((seqs, LANES), F32),
        ),
        scratch_shapes=[pair_turn],
        compiler_params=limit,
        name="early",
    )(right, diagonal, swapped, swapped_late, both, outer_near, outer_far, keep, sorted_w)

    gradient, pair_delta = pl.pallas_call(
        functools.partial(small_finish_kernel, scale),
        in_specs=[[vmem] * 2] + [vmem] * 13,
        out_specs=[pl.BlockSpec(memory_space=pl.ANY)] * 2,
        out_shape=(
            like(homolog_matrix.shape, BF16),
            like(coupling_cotangent.shape, BF16),
        ),
        scratch_shapes=[
            pltpu.VMEM(homolog_matrix.shape, BF16),
            pltpu.VMEM(coupling_cotangent.shape, BF16),
            pltpu.VMEM((ranks // 2, residues * residues, LANES), F32),
            pair_turn,
            pltpu.SemaphoreType.DMA((5,)),
        ],
        compiler_params=limit,
        name="finish",
    )(
        [beside, across],
        swapped,
        both,
        outer_near,
        outer_far,
        early_pair,
        early_left,
        early_right,
        normed,
        inv_std,
        gain,
        spread_w,
        sorted_w,
        pair_offset,
    )
    return (pair_delta, gradient)


def body(*arrays):
    if lax.axis_size("res") == 8:
        return small_slice(*arrays)
    return wide_slice(*arrays)


def solution(mesh):
    return jax.shard_map(
        body,
        mesh=mesh,
        in_specs=(
            P(("grp", "seq"), "res", None),
            P(),
            P(),
            P(),
            P(),
            P(),
            P(),
            P(),
            P(),
            P(("grp", "res"), "seq", None),
        ),
        out_specs=(P(("grp", "res"), "seq", None), P(("grp", "seq"), "res", None)),
        check_vma=False,
    )
```

```python
import functools

import jax
import jax.numpy as jnp
from jax import lax
from jax.experimental import pallas as pl
from jax.experimental.pallas import tpu as pltpu
from jax.sharding import PartitionSpec as P

LANES = 128
BF16 = jnp.bfloat16
F32 = jnp.float32
NT = (((1,), (1,)), ((), ()))
TN = (((0,), (0,)), ((), ()))


def lane_block(shape, width):
    return lax.broadcasted_iota(jnp.int32, shape, 1) // width


def pick(blocks, pieces):
    result = pieces[0]
    for place in range(1, len(pieces)):
        result = jnp.where(blocks == place, pieces[place], result)
    return result


def split_three(value):
    top = value.astype(BF16)
    rest = value - top.astype(F32)
    middle = rest.astype(BF16)
    low = (rest - middle.astype(F32)).astype(BF16)
    return top, middle, low


def split_two(value):
    top = value.astype(BF16)
    return top, (value - top.astype(F32)).astype(BF16)


def normalise(rows):
    centred = rows - jnp.mean(rows, axis=-1, keepdims=True)
    inv_std = lax.rsqrt(jnp.mean(centred * centred, axis=-1, keepdims=True) + 1e-05)
    return centred * inv_std, inv_std


def residue_rows(x_ref):
    return jnp.concatenate(
        [x_ref[:, place, :].astype(F32) for place in range(x_ref.shape[1])], axis=0
    )


def project_kernel(
    x_ref, gain_ref, offset_ref, left_w_ref, left_b_ref, right_w_ref, right_b_ref, w_ref,
    left_ref, right_ref, sorted_w_ref, wide_ref,
):
    seqs, residues, _ = x_ref.shape
    depth = left_w_ref.shape[0]
    normed, _ = normalise(residue_rows(x_ref))
    ln_out = (normed * gain_ref[...] + offset_ref[...]).astype(BF16)
    blocks = lane_block((seqs, LANES), depth)
    for weight_ref, bias_ref, out_ref in (
        (left_w_ref, left_b_ref, left_ref),
        (right_w_ref, right_b_ref, right_ref),
    ):
        weight = jnp.concatenate([weight_ref[...]] * residues, axis=0)
        bias = jnp.concatenate([bias_ref[...]] * residues, axis=1)
        wide = lax.dot_general(ln_out, weight, NT, preferred_element_type=F32)
        own = pick(blocks, [wide[p * seqs : (p + 1) * seqs] for p in range(residues)])
        out_ref[...] = (own + bias).astype(BF16)
    wide_ref[...] = w_ref[...].astype(F32)
    for d in range(depth):
        sorted_w_ref[d * depth : (d + 1) * depth, :] = wide_ref[
            pl.ds(d, depth, stride=depth), :
        ].astype(BF16)


def cot_kernel(scale, own_ref, other_ref, sorted_w_ref, left_ref, right_ref,
               send_ref, outer_ref, turn_ref):
    residues, columns, _ = own_ref.shape
    depth = sorted_w_ref.shape[0] // (LANES // residues)
    depth = LANES // residues
    first = lax.axis_index("seq") == 0
    own = own_ref[...].reshape(residues * columns, LANES)
    other = other_ref[...].reshape(residues * columns, LANES)
    low = jnp.where(first, own, other)
    high = jnp.where(first, other, own)
    both = jnp.concatenate([low, high], axis=0)
    flat = lax.dot_general(both, sorted_w_ref[...], NT, preferred_element_type=F32) * scale
    blocks = lane_block((columns, LANES), depth)
    for half in range(2):
        for tile in range(depth * depth // LANES):
            block = flat[
                half * residues * columns : (half + 1) * residues * columns,
                tile * LANES : (tile + 1) * LANES,
            ]
            turned = [block] + [pltpu.roll(block, depth * t, 1) for t in range(1, residues)]
            for e in range(residues):
                piece = pick(
                    blocks,
                    [
                        turned[(i - e) % residues][i * columns : (i + 1) * columns]
                        for i in range(residues)
                    ],
                )
                turn_ref[pl.ds(half * columns * depth + tile * residues + e, columns, stride=depth), :] = piece
    outer = turn_ref[...].astype(BF16)
    half_rows = columns * depth
    partial = lax.dot_general(left_ref[...], outer, NT, preferred_element_type=F32).astype(BF16)
    seqs = left_ref.shape[0]
    ranks = columns // residues
    for half in range(2):
        outer_ref[half] = outer[half * half_rows : (half + 1) * half_rows]
        for rank in range(ranks):
            at = (half * ranks + rank) * LANES
            send_ref[half, rank, 0:seqs, :] = right_ref[...]
            send_ref[half, rank, seqs : 2 * seqs, :] = partial[:, at : at + LANES]


def grad_kernel(steps, got_ref, outer_ref, x_ref, gain_ref, left_w_ref, right_w_ref,
                grad_ref, left_cot_ref, right_cot_ref):
    step = pl.program_id(0)
    _, ranks, twice, _ = got_ref.shape
    seqs = twice // 2
    residues = x_ref.shape[1]
    depth = LANES // residues

    @pl.when(step == 0)
    def _():
        left_cot_ref[...] = jnp.zeros_like(left_cot_ref)
        right_cot_ref[...] = jnp.zeros_like(right_cot_ref)

    places = [(half, rank) for half in range(2) for rank in range(ranks)]
    right_all = jnp.concatenate([got_ref[h, r, 0:seqs, :] for h, r in places], axis=1)
    outer = jnp.concatenate([outer_ref[0], outer_ref[1]], axis=0)
    left_cot_ref[...] += jnp.dot(right_all, outer, preferred_element_type=F32)
    total = got_ref[0, 0, seqs:twice, :].astype(F32)
    for h, r in places[1:]:
        total = total + got_ref[h, r, seqs:twice, :].astype(F32)
    right_cot_ref[...] += total

    @pl.when(step == steps - 1)
    def _():
        blocks = lane_block((seqs, LANES), depth)
        left_cot, right_cot = left_cot_ref[...], right_cot_ref[...]
        spread = jnp.concatenate(
            [
                jnp.concatenate(
                    [
                        jnp.where(blocks == place, left_cot, 0.0),
                        jnp.where(blocks == place, right_cot, 0.0),
                    ],
                    axis=1,
                )
                for place in range(residues)
            ],
            axis=0,
        )
        weight = jnp.concatenate(
            [left_w_ref[...]] * residues + [right_w_ref[...]] * residues, axis=0
        )
        rows = residues * seqs
        parts = jnp.concatenate(split_three(spread), axis=0)
        ln_cot = jnp.dot(parts, weight, preferred_element_type=F32)
        ln_cot = ln_cot[0:rows] + (ln_cot[rows : 2 * rows] + ln_cot[2 * rows : 3 * rows])
        gained = ln_cot * gain_ref[...]
        normed, inv_std = normalise(residue_rows(x_ref))
        grad = inv_std * (
            gained
            - jnp.mean(gained, axis=-1, keepdims=True)
            - normed * jnp.mean(gained * normed, axis=-1, keepdims=True)
        )
        for place in range(residues):
            grad_ref[:, place, :] = grad[place * seqs : (place + 1) * seqs].astype(BF16)


def pair_kernel(scale, got_ref, far_ref, left_ref, far_left_ref, sorted_w_ref, offset_ref,
                pair_ref, turn_ref):
    residues, columns, _ = pair_ref.shape
    depth = LANES // residues
    ranks = columns // residues
    mine = lax.axis_index("seq")
    near = jnp.concatenate([got_ref[mine, r] for r in range(ranks)], axis=1)
    far = jnp.concatenate([far_ref[r] for r in range(ranks)], axis=1)
    right = jnp.concatenate([near, far], axis=0)
    left = jnp.concatenate([left_ref[...], far_left_ref[...]], axis=0)
    turn_ref[...] = lax.dot_general(right, left, TN, preferred_element_type=F32) * scale
    blocks = lane_block((columns, LANES), depth)
    tiles = []
    for tile in range(depth * depth // LANES):
        pieces = [
            turn_ref[pl.ds(tile * residues + e, columns, stride=depth), :]
            for e in range(residues)
        ]
        rows = jnp.concatenate(pieces, axis=0)
        turned = [rows] + [pltpu.roll(rows, depth * t, 1) for t in range(1, residues)]
        tiles.append(
            jnp.concatenate(
                [
                    pick(
                        blocks,
                        [
                            turned[(e - i) % residues][e * columns : (e + 1) * columns]
                            for e in range(residues)
                        ],
                    )
                    for i in range(residues)
                ],
                axis=0,
            )
        )
    flat = jnp.concatenate(tiles, axis=1)
    rows = residues * columns
    parts = jnp.concatenate(split_three(flat), axis=0)
    pair = jnp.dot(parts, sorted_w_ref[...], preferred_element_type=F32)
    pair = pair[0:rows] + (pair[rows : 2 * rows] + pair[2 * rows : 3 * rows])
    pair_ref[...] = (pair + offset_ref[...]).astype(BF16).reshape(pair_ref.shape)


def wide_slice(
    homolog_matrix,
    standardizer_scaling,
    standardizer_offset,
    left_projection_matrix,
    left_offset_vector,
    right_projection_matrix,
    right_offset_vector,
    coupling_matrix,
    coupling_offset,
    coupling_cotangent,
):
    seqs, residues, features = homolog_matrix.shape
    depth = left_projection_matrix.shape[1]
    ranks = lax.axis_size("res")
    scale = 1.0 / (seqs * lax.axis_size("seq"))
    half_ranks = ranks // 2
    half_columns = half_ranks * residues
    step_ranks = 4
    columns = step_ranks * residues
    steps = half_ranks // step_ranks
    mine = lax.axis_index("seq")
    swap = [(0, 1), (1, 0)]

    other_cot = lax.ppermute(coupling_cotangent, "seq", swap)
    gain = standardizer_scaling.reshape(1, -1)
    left_w = left_projection_matrix.T
    right_w = right_projection_matrix.T

    left, right, sorted_w = pl.pallas_call(
        project_kernel,
        out_shape=(
            jax.ShapeDtypeStruct((seqs, LANES), BF16),
            jax.ShapeDtypeStruct((seqs, LANES), BF16),
            jax.ShapeDtypeStruct(coupling_matrix.shape, BF16),
        ),
        scratch_shapes=[pltpu.VMEM(coupling_matrix.shape, F32)],
        name="project",
    )(
        homolog_matrix,
        gain,
        standardizer_offset.reshape(1, -1),
        left_w,
        left_offset_vector.reshape(1, -1),
        right_w,
        right_offset_vector.reshape(1, -1),
        coupling_matrix,
    )

    whole = lambda shape: pl.BlockSpec(shape, lambda g: (0,) * len(shape))
    cot_block = pl.BlockSpec((residues, columns, LANES), lambda g: (0, g, 0))
    outer_block = pl.BlockSpec((2, columns * depth, LANES), lambda g: (0, g, 0))
    send_block = pl.BlockSpec((2, step_ranks, 2 * seqs, LANES), lambda g: (0, g, 0, 0))
    send, outer = pl.pallas_call(
        functools.partial(cot_kernel, scale),
        grid=(steps,),
        in_specs=[
            cot_block,
            cot_block,
            whole(sorted_w.shape),
            whole(left.shape),
            whole(right.shape),
        ],
        out_specs=(send_block, outer_block),
        out_shape=(
            jax.ShapeDtypeStruct((2, half_ranks, 2 * seqs, LANES), BF16),
            jax.ShapeDtypeStruct((2, half_columns * depth, LANES), BF16),
        ),
        scratch_shapes=[pltpu.VMEM((2 * columns * depth, LANES), F32)],
        name="cotangent",
    )(coupling_cotangent, other_cot, sorted_w, left, right)

    got = lax.all_to_all(
        send.reshape(ranks, 2 * seqs, LANES), "res", split_axis=0, concat_axis=0, tiled=True
    ).reshape(send.shape)

    leaving = lax.dynamic_index_in_dim(got, 1 - mine, 0, keepdims=False)[:, 0:seqs, :]
    far = lax.ppermute(jnp.concatenate([leaving, left[None]], axis=0), "seq", swap)

    gradient = pl.pallas_call(
        functools.partial(grad_kernel, steps),
        grid=(steps,),
        in_specs=[
            send_block,
            outer_block,
            whole(homolog_matrix.shape),
            whole(gain.shape),
            whole(left_w.shape),
            whole(right_w.shape),
        ],
        out_specs=whole(homolog_matrix.shape),
        out_shape=jax.ShapeDtypeStruct(homolog_matrix.shape, BF16),
        scratch_shapes=[pltpu.VMEM((seqs, LANES), F32)] * 2,
        name="gradient",
    )(got, outer, homolog_matrix, gain, left_w, right_w)

    pair_delta = pl.pallas_call(
        functools.partial(pair_kernel, scale),
        grid=(steps,),
        in_specs=[
            pl.BlockSpec((2, step_ranks, seqs, LANES), lambda g: (0, g, 0, 0)),
            pl.BlockSpec((step_ranks, seqs, LANES), lambda g: (g, 0, 0)),
            whole(left.shape),
            pl.BlockSpec((None, seqs, LANES), lambda g: (half_ranks, 0, 0)),
            whole(sorted_w.shape),
            whole((1, LANES)),
        ],
        out_specs=cot_block,
        out_shape=jax.ShapeDtypeStruct(coupling_cotangent.shape, BF16),
        scratch_shapes=[pltpu.VMEM((columns * depth, LANES), F32)],
        name="pair",
    )(got, far, left, far, sorted_w, coupling_offset.reshape(1, -1))
    return (pair_delta, gradient)


def fetch(source, target, semaphore):
    copy = pltpu.make_async_copy(source, target, semaphore)
    copy.start()
    return copy


def start_copies(pairs, semaphores):
    copies = [
        pltpu.make_async_copy(source, target, semaphores.at[place])
        for place, (source, target) in enumerate(pairs)
    ]
    for copy in copies:
        copy.start()
    return copies


def small_project_kernel(
    x_hbm, gain_hbm, offset_hbm, left_w_hbm, left_b_hbm, right_w_hbm, right_b_hbm, pair_offset_hbm,
    cot_hbm, both_ref, normed_ref, inv_std_ref, spread_w_ref, gain_ref, pair_offset_ref, cot_ref,
    x_ref, offset_ref, left_w_ref, left_b_ref, right_w_ref, right_b_ref, semaphores,
):
    seqs, residues, _ = x_ref.shape
    depth = left_w_ref.shape[0]
    parts = 4
    part = seqs // parts
    copies = start_copies(
        tuple(
            (x_hbm.at[pl.ds(place * part, part)], x_ref.at[pl.ds(place * part, part)])
            for place in range(parts)
        )
        + (
            (left_w_hbm, left_w_ref),
            (right_w_hbm, right_w_ref),
            (gain_hbm, gain_ref),
            (offset_hbm, offset_ref),
            (left_b_hbm, left_b_ref),
            (right_b_hbm, right_b_ref),
            (cot_hbm, cot_ref),
            (pair_offset_hbm, pair_offset_ref),
        ),
        semaphores,
    )
    for copy in copies[:parts]:
        copy.wait()
    normed, inv_std = normalise(residue_rows(x_ref))
    for copy in copies[parts:]:
        copy.wait()
    ln_out = (normed * gain_ref[...] + offset_ref[...]).astype(BF16)
    blocks = lane_block((seqs, LANES), depth)
    weight = jnp.concatenate(
        [left_w_ref[...]] * residues + [right_w_ref[...]] * residues, axis=0
    )
    wide = lax.dot_general(ln_out, weight, NT, preferred_element_type=F32)
    for place, bias_ref in enumerate((left_b_ref, right_b_ref)):
        bias = jnp.concatenate([bias_ref[...]] * residues, axis=1)
        lanes = wide[:, place * LANES : (place + 1) * LANES]
        own = pick(blocks, [lanes[p * seqs : (p + 1) * seqs] for p in range(residues)])
        both_ref[place] = (own + bias).astype(BF16)
    normed_ref[...] = normed
    inv_std_ref[...] = jnp.broadcast_to(inv_std, inv_std_ref.shape)
    spread_w_ref[...] = weight


def outer_rows(scale, cot, residues, sorted_wt_ref, turn_ref):
    columns = cot.shape[0] // residues
    depth = LANES // residues
    flat = jnp.dot(cot, sorted_wt_ref[...], preferred_element_type=F32) * scale
    blocks = lane_block((columns, LANES), depth)
    for tile in range(depth * depth // LANES):
        block = flat[:, tile * LANES : (tile + 1) * LANES]
        turned = [block] + [pltpu.roll(block, depth * t, 1) for t in range(1, residues)]
        for e in range(residues):
            turn_ref[pl.ds(tile * residues + e, columns, stride=depth), :] = pick(
                blocks,
                [
                    turned[(i - e) % residues][i * columns : (i + 1) * columns]
                    for i in range(residues)
                ],
            )
    return turn_ref[...].astype(BF16)


def small_own_kernel(scale, own_ref, other_ref, w_ref, both_ref,
                     keep_ref, outer_near_ref, outer_far_ref, sorted_w_ref, sorted_wt_ref,
                     order_ref, repeat_ref, turn_refs, wide_ref):
    residues, columns, _ = own_ref.shape
    depth = LANES // residues
    wide_ref[...] = w_ref[...].astype(F32)
    for d in range(depth):
        sorted_w_ref[d * depth : (d + 1) * depth, :] = wide_ref[
            pl.ds(d, depth, stride=depth), :
        ].astype(BF16)
    sorted_wt_ref[...] = sorted_w_ref[...].T
    rank = lax.axis_index("res")
    own_is_near = lax.axis_index("seq") == lax.shift_right_logical(rank, 2)
    own = own_ref[...].reshape(residues * columns, LANES)
    other = other_ref[...].reshape(residues * columns, LANES)
    near = outer_rows(
        scale, jnp.where(own_is_near, own, other), residues, sorted_wt_ref, turn_refs[0]
    )
    outer_near_ref[...] = near
    partial = lax.dot_general(both_ref[0], near, NT, preferred_element_type=F32)
    for place in range(columns // residues):
        keep_ref[lax.bitwise_xor(rank & 3, place)] = partial[:, place * LANES : (place + 1) * LANES]
    outer_far_ref[...] = outer_rows(
        scale, jnp.where(own_is_near, other, own), residues, sorted_wt_ref, turn_refs[1]
    )
    order_ref[...] = one_hot(
        lambda row: (
            (2 * (row >> 6 & 1) + (row >> 2 & 1)) * LANES
            + (row & 3) * depth + (row >> 3 & 7) * residues + (row >> 7)
        ),
        order_ref.shape,
    )
    for place in range(residues):
        shape = (LANES, LANES)
        row = lax.broadcasted_iota(jnp.int32, shape, 0)
        lane = lax.broadcasted_iota(jnp.int32, shape, 1)
        repeat_ref[:, place * LANES : (place + 1) * LANES] = jnp.where(
            row == place * depth + lane % depth, 1.0, 0.0
        ).astype(BF16)


def one_hot(target, shape):
    part = (shape[0], LANES)
    wanted = target(lax.broadcasted_iota(jnp.int32, part, 0))
    lane = lax.broadcasted_iota(jnp.int32, part, 1)
    return jnp.concatenate(
        [
            jnp.where(wanted == lane + tile * LANES, 1.0, 0.0).astype(BF16)
            for tile in range(shape[1] // LANES)
        ],
        axis=1,
    )


def blocks_apart(left, repeat, residues):
    depth = LANES // residues
    wide = jnp.dot(left, repeat, preferred_element_type=F32)
    blocks = lane_block(wide.shape, depth) % residues
    return jnp.concatenate(
        [jnp.where(blocks == e, wide, 0.0).astype(BF16) for e in range(residues)], axis=0
    )


def small_partner_kernel(scale, residues, got_ref, sorted_wt_ref, keep_ref, both_ref, order_ref,
                         repeat_ref, leaving_ref, keep_out_ref, right_ref, swap_ref):
    rank = lax.axis_index("res")
    seqs = got_ref.shape[1]
    cot = got_ref[2:4].reshape(2 * seqs, LANES)
    columns = cot.shape[0] // residues
    tiles = sorted_wt_ref.shape[1] // LANES
    flat = jnp.dot(cot, sorted_wt_ref[...], preferred_element_type=F32) * scale
    outer = jnp.concatenate(
        [
            jnp.concatenate(
                [
                    flat[i * columns + start : i * columns + start + 8, tile * LANES : (tile + 1) * LANES]
                    for start in range(0, columns, 8)
                    for tile in range(tiles)
                ],
                axis=0,
            )
            for i in range(residues)
        ],
        axis=1,
    ).astype(BF16)
    apart = blocks_apart(got_ref[0], repeat_ref[...], residues)
    partial = lax.dot_general(apart, outer, NT, preferred_element_type=F32).astype(BF16)
    partial = jnp.concatenate(
        [partial[e * seqs : (e + 1) * seqs] for e in range(residues)], axis=1
    )
    partial = jnp.dot(partial, order_ref[...], preferred_element_type=F32)
    right_ref[0] = both_ref[1]
    right_ref[1] = got_ref[1]
    own_is_near = lax.axis_index("seq") == lax.shift_right_logical(rank, 2)
    swap_ref[0] = jnp.where(own_is_near, got_ref[1], both_ref[1])
    swap_ref[1] = both_ref[0]
    for place in range(leaving_ref.shape[0]):
        leaving_ref[place, 0] = both_ref[1]
        leaving_ref[place, 1] = got_ref[1]
    for place in range(leaving_ref.shape[0]):
        distance = lax.bitwise_xor(rank & 3, place)
        total = keep_ref[distance] + partial[:, place * LANES : (place + 1) * LANES]
        leaving_ref[distance, 2] = total.astype(BF16)
        keep_out_ref[distance] = total


def pair_rows(scale, right, left, residues, sorted_w_ref, turn_ref):
    depth = LANES // residues
    columns = right.shape[1] // depth
    turn_ref[...] = lax.dot_general(right, left, TN, preferred_element_type=F32) * scale
    blocks = lane_block((columns, LANES), depth)
    tiles = []
    for tile in range(depth * depth // LANES):
        pieces = [
            turn_ref[pl.ds(tile * residues + e, columns, stride=depth), :]
            for e in range(residues)
        ]
        lines = jnp.concatenate(pieces, axis=0)
        turned = [lines] + [pltpu.roll(lines, depth * t, 1) for t in range(1, residues)]
        tiles.append(
            jnp.concatenate(
                [
                    pick(
                        blocks,
                        [
                            turned[(e - i) % residues][e * columns : (e + 1) * columns]
                            for e in range(residues)
                        ],
                    )
                    for i in range(residues)
                ],
                axis=0,
            )
        )
    flat = jnp.concatenate(tiles, axis=1)
    rows = residues * columns
    parts = jnp.concatenate(split_two(flat), axis=0)
    pair = jnp.dot(parts, sorted_w_ref[...], preferred_element_type=F32)
    return pair[0:rows] + pair[rows : 2 * rows]


def left_share(block_refs, masks, outer_near_ref, outer_far_ref):
    here = lax.axis_index("res") & 3
    spots = [
        pl.ds(pl.multiple_of(lax.bitwise_xor(here, mask) * LANES, LANES), LANES) for mask in masks
    ]
    right = jnp.concatenate([ref[0] for ref in block_refs] + [ref[1] for ref in block_refs], axis=1)
    outer = jnp.concatenate(
        [outer_near_ref[spot, :] for spot in spots] + [outer_far_ref[spot, :] for spot in spots],
        axis=0,
    )
    return jnp.dot(right, outer, preferred_element_type=F32)


def own_half():
    near = lax.axis_index("seq") == lax.shift_right_logical(lax.axis_index("res"), 2)
    return jnp.where(near, 0, 1)


def small_early_kernel(
    scale, right_ref, part_ref, swapped_ref, swapped_late_ref, both_ref, outer_near_ref, outer_far_ref,
    keep_ref, sorted_w_ref,
    pair_ref, left_cot_ref, right_cot_ref, turn_ref,
):
    residues = pair_ref.shape[1] // 4
    left_cot_ref[...] = left_share([right_ref, part_ref], (0, 3), outer_near_ref, outer_far_ref)
    right_cot_ref[...] = keep_ref[0] + part_ref[2].astype(F32)
    half = own_half()
    right = jnp.concatenate(
        [
            jnp.concatenate([right_ref[half], part_ref[half]], axis=1),
            jnp.concatenate([swapped_ref[0], swapped_late_ref[...]], axis=1),
        ],
        axis=0,
    )
    left = jnp.concatenate([both_ref[0], swapped_ref[1]], axis=0)
    pair = pair_rows(scale, right, left, residues, sorted_w_ref, turn_ref)
    store_pairs(pair, (0, 1), residues, pair_ref)


def store_pairs(pair, spots, residues, pair_ref):
    columns = pair.shape[0] // residues // len(spots)
    for i in range(residues):
        for place, spot in enumerate(spots):
            start = (i * len(spots) + place) * columns
            pair_ref[spot, i * columns : (i + 1) * columns, :] = pair[start : start + columns]


def small_finish_kernel(
    scale, part_refs, swapped_ref, both_ref, outer_near_ref, outer_far_ref, early_pair_ref,
    early_left_ref, early_right_ref, normed_ref, inv_std_ref, gain_ref, spread_w_ref, sorted_w_ref,
    offset_ref, grad_hbm, pair_hbm, grad_ref, pair_ref, pairs_ref, turn_ref, semaphores,
):
    seqs, residues, _ = grad_ref.shape
    columns = pair_ref.shape[1]
    depth = LANES // residues
    ranks = columns // residues

    left_cot = early_left_ref[...] + left_share(part_refs, (1, 2), outer_near_ref, outer_far_ref)
    right_cot = early_right_ref[...]
    for part_ref in part_refs:
        right_cot = right_cot + part_ref[2].astype(F32)
    blocks = lane_block((seqs, LANES), depth)
    spread = jnp.concatenate(
        [
            jnp.concatenate(
                [jnp.where(blocks == place, cot, 0.0) for cot in (left_cot, right_cot)], axis=1
            )
            for place in range(residues)
        ],
        axis=0,
    )
    rows = residues * seqs
    parts = jnp.concatenate(split_two(spread), axis=0)
    ln_cot = jnp.dot(parts, spread_w_ref[...], preferred_element_type=F32)
    ln_cot = ln_cot[0:rows] + ln_cot[rows : 2 * rows]
    gained = ln_cot * gain_ref[...]
    normed = normed_ref[...]
    grad = inv_std_ref[:, 0:1] * (
        gained
        - jnp.mean(gained, axis=-1, keepdims=True)
        - normed * jnp.mean(gained * normed, axis=-1, keepdims=True)
    )
    for place in range(residues):
        grad_ref[:, place, :] = grad[place * seqs : (place + 1) * seqs].astype(BF16)
    half = own_half()
    right = jnp.concatenate(
        [
            jnp.concatenate([ref[half] for ref in part_refs], axis=1),
            jnp.concatenate([ref[3] for ref in part_refs], axis=1),
        ],
        axis=0,
    )
    left = jnp.concatenate([both_ref[0], swapped_ref[1]], axis=0)
    pair = pair_rows(scale, right, left, residues, sorted_w_ref, turn_ref)
    pairs_ref[0] = early_pair_ref[0]
    pairs_ref[3] = early_pair_ref[1]
    store_pairs(pair, (1, 2), residues, pairs_ref)
    here = lax.axis_index("res") & 3
    placed = [pairs_ref[lax.bitwise_xor(here, place)] for place in range(ranks)]
    for i in range(residues):
        own = [block[i * residues : (i + 1) * residues] for block in placed]
        pair_ref[i] = (jnp.concatenate(own, axis=0) + offset_ref[...]).astype(BF16)
    parts = 4
    part = seqs // parts
    copies = start_copies(
        ((pair_ref, pair_hbm),)
        + tuple(
            (grad_ref.at[pl.ds(place * part, part)], grad_hbm.at[pl.ds(place * part, part)])
            for place in range(parts)
        ),
        semaphores,
    )
    for copy in copies:
        copy.wait()


def small_slice(
    homolog_matrix,
    standardizer_scaling,
    standardizer_offset,
    left_projection_matrix,
    left_offset_vector,
    right_projection_matrix,
    right_offset_vector,
    coupling_matrix,
    coupling_offset,
    coupling_cotangent,
):
    seqs, residues, features = homolog_matrix.shape
    depth = left_projection_matrix.shape[1]
    ranks = lax.axis_size("res")
    rows = seqs * residues
    scale = 1.0 / (seqs * lax.axis_size("seq"))
    rank = lax.axis_index("res")
    mine = lax.axis_index("seq")
    swap = [(0, 1), (1, 0)]
    limit = pltpu.CompilerParams(vmem_limit_bytes=8 * 1024 * 1024)
    vmem = pl.BlockSpec(memory_space=pltpu.VMEM)
    like = jax.ShapeDtypeStruct

    other_cot = lax.ppermute(coupling_cotangent, "seq", swap)
    hbm = pl.BlockSpec(memory_space=pltpu.HBM)
    pin = lambda array: pltpu.with_memory_space_constraint(array, pltpu.HBM)
    both, normed, inv_std, spread_w, gain, pair_offset, own_cot = pl.pallas_call(
        small_project_kernel,
        in_specs=[hbm] * 9,
        out_specs=[vmem] * 7,
        out_shape=(
            like((2, seqs, LANES), BF16),
            like((rows, features), F32),
            like((rows, LANES), F32),
            like((2 * LANES, features), BF16),
            like((1, features), F32),
            like((1, LANES), F32),
            like(coupling_cotangent.shape, BF16),
        ),
        scratch_shapes=[
            pltpu.VMEM(homolog_matrix.shape, BF16),
            pltpu.VMEM((1, features), F32),
            pltpu.VMEM((depth, features), BF16),
            pltpu.VMEM((1, depth), F32),
            pltpu.VMEM((depth, features), BF16),
            pltpu.VMEM((1, depth), F32),
            pltpu.SemaphoreType.DMA((12,)),
        ],
        compiler_params=limit,
        name="project",
    )(
        *[
            pin(array)
            for array in (
                homolog_matrix,
                standardizer_scaling.reshape(1, -1),
                standardizer_offset.reshape(1, -1),
                left_projection_matrix.T,
                left_offset_vector.reshape(1, -1),
                right_projection_matrix.T,
                right_offset_vector.reshape(1, -1),
                coupling_offset.reshape(1, -1),
                coupling_cotangent,
            )
        ]
    )

    def swap_over(mask, value):
        return lax.ppermute(value, "res", [(source, source ^ mask) for source in range(ranks)])

    own_is_near = mine == lax.shift_right_logical(rank, 2)
    far_cot = jnp.where(own_is_near, other_cot, own_cot).reshape(2, seqs, LANES)
    beyond_two = swap_over(4, jnp.concatenate([both, far_cot]))

    half_rows = ranks // 2 * LANES
    turn = pltpu.VMEM((half_rows, LANES), F32)
    keep, outer_near, outer_far, sorted_w, sorted_wt, order, repeat = pl.pallas_call(
        functools.partial(small_own_kernel, scale),
        in_specs=[vmem] * 4,
        out_specs=[vmem] * 7,
        out_shape=(
            like((ranks // 2, seqs, LANES), F32),
            like((half_rows, LANES), BF16),
            like((half_rows, LANES), BF16),
            like(coupling_matrix.shape, BF16),
            like(coupling_matrix.shape[::-1], BF16),
            like((half_rows, half_rows), BF16),
            like((LANES, residues * LANES), BF16),
        ),
        scratch_shapes=[[turn, turn], pltpu.VMEM(coupling_matrix.shape, F32)],
        compiler_params=limit,
        name="own_pieces",
    )(own_cot, other_cot, coupling_matrix, both)

    leaving_parts, keep, right, leaving = pl.pallas_call(
        functools.partial(small_partner_kernel, scale, residues),
        in_specs=[vmem] * 6,
        out_specs=[vmem] * 4,
        out_shape=(
            like((ranks // 2, 3, seqs, LANES), BF16),
            like((ranks // 2, seqs, LANES), F32),
            like((2, seqs, LANES), BF16),
            like((2, seqs, LANES), BF16),
        ),
        compiler_params=limit,
        name="partner_pieces",
    )(beyond_two, sorted_wt, keep, both, order, repeat)

    swapped = lax.ppermute(leaving, "seq", swap)
    diagonal = swap_over(3, leaving_parts[3])
    across, beside = [
        swap_over(mask, jnp.concatenate([leaving_parts[mask], swapped[0:1]])) for mask in (2, 1)
    ]
    swapped_late = lax.ppermute(
        jnp.where(own_is_near, diagonal[1], diagonal[0]), "seq", swap
    )

    pair_turn = pltpu.VMEM((2 * LANES, LANES), F32)
    early_pair, early_left, early_right = pl.pallas_call(
        functools.partial(small_early_kernel, scale),
        in_specs=[vmem] * 9,
        out_specs=[vmem] * 3,
        out_shape=(
            like((2, residues * residues, LANES), F32),
            like((seqs, LANES), F32),
            like((seqs, LANES), F32),
        ),
        scratch_shapes=[pair_turn],
        compiler_params=limit,
        name="early",
    )(right, diagonal, swapped, swapped_late, both, outer_near, outer_far, keep, sorted_w)

    gradient, pair_delta = pl.pallas_call(
        functools.partial(small_finish_kernel, scale),
        in_specs=[[vmem] * 2] + [vmem] * 13,
        out_specs=[pl.BlockSpec(memory_space=pl.ANY)] * 2,
        out_shape=(
            like(homolog_matrix.shape, BF16),
            like(coupling_cotangent.shape, BF16),
        ),
        scratch_shapes=[
            pltpu.VMEM(homolog_matrix.shape, BF16),
            pltpu.VMEM(coupling_cotangent.shape, BF16),
            pltpu.VMEM((ranks // 2, residues * residues, LANES), F32),
            pair_turn,
            pltpu.SemaphoreType.DMA((5,)),
        ],
        compiler_params=limit,
        name="finish",
    )(
        [beside, across],
        swapped,
        both,
        outer_near,
        outer_far,
        early_pair,
        early_left,
        early_right,
        normed,
        inv_std,
        gain,
        spread_w,
        sorted_w,
        pair_offset,
    )
    return (pair_delta, gradient)


def body(*arrays):
    if lax.axis_size("res") == 8:
        return small_slice(*arrays)
    return wide_slice(*arrays)


def solution(mesh):
    return jax.shard_map(
        body,
        mesh=mesh,
        in_specs=(
            P(("grp", "seq"), "res", None),
            P(),
            P(),
            P(),
            P(),
            P(),
            P(),
            P(),
            P(),
            P(("grp", "res"), "seq", None),
        ),
        out_specs=(P(("grp", "res"), "seq", None), P(("grp", "seq"), "res", None)),
        check_vma=False,
    )
```

```python
import functools

import jax
import jax.numpy as jnp
from jax import lax
from jax.experimental import pallas as pl
from jax.experimental.pallas import tpu as pltpu
from jax.sharding import PartitionSpec as P

LANES = 128
BF16 = jnp.bfloat16
F32 = jnp.float32
NT = (((1,), (1,)), ((), ()))
TN = (((0,), (0,)), ((), ()))


def lane_block(shape, width):
    return lax.broadcasted_iota(jnp.int32, shape, 1) // width


def pick(blocks, pieces):
    result = pieces[0]
    for place in range(1, len(pieces)):
        result = jnp.where(blocks == place, pieces[place], result)
    return result


def split_three(value):
    top = value.astype(BF16)
    rest = value - top.astype(F32)
    middle = rest.astype(BF16)
    low = (rest - middle.astype(F32)).astype(BF16)
    return top, middle, low


def exchange_blocks(pieces, width):
    first, second, third, fourth = pieces
    blocks = lane_block(first.shape, width)
    odd, high = blocks % 2 == 1, blocks >= 2
    roll = lambda value, count: pltpu.roll(value, count * width, 1)
    first, second = jnp.where(odd, roll(second, 1), first), jnp.where(odd, second, roll(first, 3))
    third, fourth = jnp.where(odd, roll(fourth, 1), third), jnp.where(odd, fourth, roll(third, 3))
    return [
        jnp.where(high, roll(third, 2), first),
        jnp.where(high, roll(fourth, 2), second),
        jnp.where(high, third, roll(first, 2)),
        jnp.where(high, fourth, roll(second, 2)),
    ]


def split_two(value):
    top = value.astype(BF16)
    return top, (value - top.astype(F32)).astype(BF16)


def normalise(rows):
    centred = rows - jnp.mean(rows, axis=-1, keepdims=True)
    inv_std = lax.rsqrt(jnp.mean(centred * centred, axis=-1, keepdims=True) + 1e-05)
    return centred * inv_std, inv_std


def residue_rows(x_ref):
    return jnp.concatenate(
        [x_ref[:, place, :].astype(F32) for place in range(x_ref.shape[1])], axis=0
    )


def project_kernel(
    x_ref, gain_ref, offset_ref, left_w_ref, left_b_ref, right_w_ref, right_b_ref, w_ref,
    left_ref, right_ref, sorted_w_ref, wide_ref,
):
    seqs, residues, _ = x_ref.shape
    depth = left_w_ref.shape[0]
    normed, _ = normalise(residue_rows(x_ref))
    ln_out = (normed * gain_ref[...] + offset_ref[...]).astype(BF16)
    blocks = lane_block((seqs, LANES), depth)
    for weight_ref, bias_ref, out_ref in (
        (left_w_ref, left_b_ref, left_ref),
        (right_w_ref, right_b_ref, right_ref),
    ):
        weight = jnp.concatenate([weight_ref[...]] * residues, axis=0)
        bias = jnp.concatenate([bias_ref[...]] * residues, axis=1)
        wide = lax.dot_general(ln_out, weight, NT, preferred_element_type=F32)
        own = pick(blocks, [wide[p * seqs : (p + 1) * seqs] for p in range(residues)])
        out_ref[...] = (own + bias).astype(BF16)
    wide_ref[...] = w_ref[...].astype(F32)
    for d in range(depth):
        sorted_w_ref[d * depth : (d + 1) * depth, :] = wide_ref[
            pl.ds(d, depth, stride=depth), :
        ].astype(BF16)


def cot_kernel(scale, own_ref, other_ref, sorted_w_ref, left_ref, right_ref,
               send_ref, outer_ref, turn_ref):
    residues, columns, _ = own_ref.shape
    depth = sorted_w_ref.shape[0] // (LANES // residues)
    depth = LANES // residues
    first = lax.axis_index("seq") == 0
    own = own_ref[...].reshape(residues * columns, LANES)
    other = other_ref[...].reshape(residues * columns, LANES)
    low = jnp.where(first, own, other)
    high = jnp.where(first, other, own)
    both = jnp.concatenate([low, high], axis=0)
    flat = lax.dot_general(both, sorted_w_ref[...], NT, preferred_element_type=F32) * scale
    blocks = lane_block((columns, LANES), depth)
    for half in range(2):
        for tile in range(depth * depth // LANES):
            block = flat[
                half * residues * columns : (half + 1) * residues * columns,
                tile * LANES : (tile + 1) * LANES,
            ]
            turned = [block] + [pltpu.roll(block, depth * t, 1) for t in range(1, residues)]
            for e in range(residues):
                piece = pick(
                    blocks,
                    [
                        turned[(i - e) % residues][i * columns : (i + 1) * columns]
                        for i in range(residues)
                    ],
                )
                turn_ref[pl.ds(half * columns * depth + tile * residues + e, columns, stride=depth), :] = piece
    outer = turn_ref[...].astype(BF16)
    half_rows = columns * depth
    partial = lax.dot_general(left_ref[...], outer, NT, preferred_element_type=F32).astype(BF16)
    seqs = left_ref.shape[0]
    ranks = columns // residues
    for half in range(2):
        outer_ref[half] = outer[half * half_rows : (half + 1) * half_rows]
        for rank in range(ranks):
            at = (half * ranks + rank) * LANES
            send_ref[half, rank, 0:seqs, :] = right_ref[...]
            send_ref[half, rank, seqs : 2 * seqs, :] = partial[:, at : at + LANES]


def grad_kernel(steps, got_ref, outer_ref, x_ref, gain_ref, left_w_ref, right_w_ref,
                grad_ref, left_cot_ref, right_cot_ref):
    step = pl.program_id(0)
    _, ranks, twice, _ = got_ref.shape
    seqs = twice // 2
    residues = x_ref.shape[1]
    depth = LANES // residues

    @pl.when(step == 0)
    def _():
        left_cot_ref[...] = jnp.zeros_like(left_cot_ref)
        right_cot_ref[...] = jnp.zeros_like(right_cot_ref)

    places = [(half, rank) for half in range(2) for rank in range(ranks)]
    right_all = jnp.concatenate([got_ref[h, r, 0:seqs, :] for h, r in places], axis=1)
    outer = jnp.concatenate([outer_ref[0], outer_ref[1]], axis=0)
    left_cot_ref[...] += jnp.dot(right_all, outer, preferred_element_type=F32)
    total = got_ref[0, 0, seqs:twice, :].astype(F32)
    for h, r in places[1:]:
        total = total + got_ref[h, r, seqs:twice, :].astype(F32)
    right_cot_ref[...] += total

    @pl.when(step == steps - 1)
    def _():
        blocks = lane_block((seqs, LANES), depth)
        left_cot, right_cot = left_cot_ref[...], right_cot_ref[...]
        spread = jnp.concatenate(
            [
                jnp.concatenate(
                    [
                        jnp.where(blocks == place, left_cot, 0.0),
                        jnp.where(blocks == place, right_cot, 0.0),
                    ],
                    axis=1,
                )
                for place in range(residues)
            ],
            axis=0,
        )
        weight = jnp.concatenate(
            [left_w_ref[...]] * residues + [right_w_ref[...]] * residues, axis=0
        )
        rows = residues * seqs
        parts = jnp.concatenate(split_three(spread), axis=0)
        ln_cot = jnp.dot(parts, weight, preferred_element_type=F32)
        ln_cot = ln_cot[0:rows] + (ln_cot[rows : 2 * rows] + ln_cot[2 * rows : 3 * rows])
        gained = ln_cot * gain_ref[...]
        normed, inv_std = normalise(residue_rows(x_ref))
        grad = inv_std * (
            gained
            - jnp.mean(gained, axis=-1, keepdims=True)
            - normed * jnp.mean(gained * normed, axis=-1, keepdims=True)
        )
        for place in range(residues):
            grad_ref[:, place, :] = grad[place * seqs : (place + 1) * seqs].astype(BF16)


def pair_kernel(scale, got_ref, far_ref, left_ref, far_left_ref, sorted_w_ref, offset_ref,
                pair_ref, turn_ref):
    residues, columns, _ = pair_ref.shape
    depth = LANES // residues
    ranks = columns // residues
    mine = lax.axis_index("seq")
    near = jnp.concatenate([got_ref[mine, r] for r in range(ranks)], axis=1)
    far = jnp.concatenate([far_ref[r] for r in range(ranks)], axis=1)
    right = jnp.concatenate([near, far], axis=0)
    left = jnp.concatenate([left_ref[...], far_left_ref[...]], axis=0)
    turn_ref[...] = lax.dot_general(right, left, TN, preferred_element_type=F32) * scale
    blocks = lane_block((columns, LANES), depth)
    tiles = []
    for tile in range(depth * depth // LANES):
        pieces = [
            turn_ref[pl.ds(tile * residues + e, columns, stride=depth), :]
            for e in range(residues)
        ]
        rows = jnp.concatenate(pieces, axis=0)
        turned = [rows] + [pltpu.roll(rows, depth * t, 1) for t in range(1, residues)]
        tiles.append(
            jnp.concatenate(
                [
                    pick(
                        blocks,
                        [
                            turned[(e - i) % residues][e * columns : (e + 1) * columns]
                            for e in range(residues)
                        ],
                    )
                    for i in range(residues)
                ],
                axis=0,
            )
        )
    flat = jnp.concatenate(tiles, axis=1)
    rows = residues * columns
    parts = jnp.concatenate(split_three(flat), axis=0)
    pair = jnp.dot(parts, sorted_w_ref[...], preferred_element_type=F32)
    pair = pair[0:rows] + (pair[rows : 2 * rows] + pair[2 * rows : 3 * rows])
    pair_ref[...] = (pair + offset_ref[...]).astype(BF16).reshape(pair_ref.shape)


def wide_slice(
    homolog_matrix,
    standardizer_scaling,
    standardizer_offset,
    left_projection_matrix,
    left_offset_vector,
    right_projection_matrix,
    right_offset_vector,
    coupling_matrix,
    coupling_offset,
    coupling_cotangent,
):
    seqs, residues, features = homolog_matrix.shape
    depth = left_projection_matrix.shape[1]
    ranks = lax.axis_size("res")
    scale = 1.0 / (seqs * lax.axis_size("seq"))
    half_ranks = ranks // 2
    half_columns = half_ranks * residues
    step_ranks = 4
    columns = step_ranks * residues
    steps = half_ranks // step_ranks
    mine = lax.axis_index("seq")
    swap = [(0, 1), (1, 0)]

    other_cot = lax.ppermute(coupling_cotangent, "seq", swap)
    gain = standardizer_scaling.reshape(1, -1)
    left_w = left_projection_matrix.T
    right_w = right_projection_matrix.T

    left, right, sorted_w = pl.pallas_call(
        project_kernel,
        out_shape=(
            jax.ShapeDtypeStruct((seqs, LANES), BF16),
            jax.ShapeDtypeStruct((seqs, LANES), BF16),
            jax.ShapeDtypeStruct(coupling_matrix.shape, BF16),
        ),
        scratch_shapes=[pltpu.VMEM(coupling_matrix.shape, F32)],
        name="project",
    )(
        homolog_matrix,
        gain,
        standardizer_offset.reshape(1, -1),
        left_w,
        left_offset_vector.reshape(1, -1),
        right_w,
        right_offset_vector.reshape(1, -1),
        coupling_matrix,
    )

    whole = lambda shape: pl.BlockSpec(shape, lambda g: (0,) * len(shape))
    cot_block = pl.BlockSpec((residues, columns, LANES), lambda g: (0, g, 0))
    outer_block = pl.BlockSpec((2, columns * depth, LANES), lambda g: (0, g, 0))
    send_block = pl.BlockSpec((2, step_ranks, 2 * seqs, LANES), lambda g: (0, g, 0, 0))
    send, outer = pl.pallas_call(
        functools.partial(cot_kernel, scale),
        grid=(steps,),
        in_specs=[
            cot_block,
            cot_block,
            whole(sorted_w.shape),
            whole(left.shape),
            whole(right.shape),
        ],
        out_specs=(send_block, outer_block),
        out_shape=(
            jax.ShapeDtypeStruct((2, half_ranks, 2 * seqs, LANES), BF16),
            jax.ShapeDtypeStruct((2, half_columns * depth, LANES), BF16),
        ),
        scratch_shapes=[pltpu.VMEM((2 * columns * depth, LANES), F32)],
        name="cotangent",
    )(coupling_cotangent, other_cot, sorted_w, left, right)

    got = lax.all_to_all(
        send.reshape(ranks, 2 * seqs, LANES), "res", split_axis=0, concat_axis=0, tiled=True
    ).reshape(send.shape)

    leaving = lax.dynamic_index_in_dim(got, 1 - mine, 0, keepdims=False)[:, 0:seqs, :]
    far = lax.ppermute(jnp.concatenate([leaving, left[None]], axis=0), "seq", swap)

    gradient = pl.pallas_call(
        functools.partial(grad_kernel, steps),
        grid=(steps,),
        in_specs=[
            send_block,
            outer_block,
            whole(homolog_matrix.shape),
            whole(gain.shape),
            whole(left_w.shape),
            whole(right_w.shape),
        ],
        out_specs=whole(homolog_matrix.shape),
        out_shape=jax.ShapeDtypeStruct(homolog_matrix.shape, BF16),
        scratch_shapes=[pltpu.VMEM((seqs, LANES), F32)] * 2,
        name="gradient",
    )(got, outer, homolog_matrix, gain, left_w, right_w)

    pair_delta = pl.pallas_call(
        functools.partial(pair_kernel, scale),
        grid=(steps,),
        in_specs=[
            pl.BlockSpec((2, step_ranks, seqs, LANES), lambda g: (0, g, 0, 0)),
            pl.BlockSpec((step_ranks, seqs, LANES), lambda g: (g, 0, 0)),
            whole(left.shape),
            pl.BlockSpec((None, seqs, LANES), lambda g: (half_ranks, 0, 0)),
            whole(sorted_w.shape),
            whole((1, LANES)),
        ],
        out_specs=cot_block,
        out_shape=jax.ShapeDtypeStruct(coupling_cotangent.shape, BF16),
        scratch_shapes=[pltpu.VMEM((columns * depth, LANES), F32)],
        name="pair",
    )(got, far, left, far, sorted_w, coupling_offset.reshape(1, -1))
    return (pair_delta, gradient)


def fetch(source, target, semaphore):
    copy = pltpu.make_async_copy(source, target, semaphore)
    copy.start()
    return copy


def start_copies(pairs, semaphores):
    copies = [
        pltpu.make_async_copy(source, target, semaphores.at[place])
        for place, (source, target) in enumerate(pairs)
    ]
    for copy in copies:
        copy.start()
    return copies


def small_project_kernel(
    x_hbm, gain_hbm, offset_hbm, left_w_hbm, left_b_hbm, right_w_hbm, right_b_hbm, pair_offset_hbm,
    cot_hbm, both_ref, normed_ref, inv_std_ref, spread_w_ref, gain_ref, pair_offset_ref, cot_ref,
    x_ref, offset_ref, left_w_ref, left_b_ref, right_w_ref, right_b_ref, wide_ref, semaphores,
):
    seqs, residues, _ = x_ref.shape
    depth = left_w_ref.shape[0]
    parts = 4
    part = seqs // parts
    copies = start_copies(
        tuple(
            (x_hbm.at[pl.ds(place * part, part)], x_ref.at[pl.ds(place * part, part)])
            for place in range(parts)
        )
        + (
            (left_w_hbm, left_w_ref),
            (right_w_hbm, right_w_ref),
            (gain_hbm, gain_ref),
            (offset_hbm, offset_ref),
            (left_b_hbm, left_b_ref),
            (right_b_hbm, right_b_ref),
            (cot_hbm, cot_ref),
            (pair_offset_hbm, pair_offset_ref),
        ),
        semaphores,
    )
    for copy in copies[:parts]:
        copy.wait()
    rows = x_ref[...].astype(F32).reshape(seqs * residues, x_ref.shape[2])
    normed, inv_std = normalise(rows)
    for copy in copies[parts:]:
        copy.wait()
    ln_out = (normed * gain_ref[...] + offset_ref[...]).astype(BF16)
    blocks = lane_block((seqs, LANES), depth)
    weight = jnp.concatenate(
        [left_w_ref[...]] * residues + [right_w_ref[...]] * residues, axis=0
    )
    wide = lax.dot_general(ln_out, weight, NT, preferred_element_type=F32)
    for place, bias_ref in enumerate((left_b_ref, right_b_ref)):
        bias = jnp.concatenate([bias_ref[...]] * residues, axis=1)
        wide_ref[place] = wide[:, place * LANES : (place + 1) * LANES]
        own = pick(
            blocks, [wide_ref[place, pl.ds(p, seqs, stride=residues), :] for p in range(residues)]
        )
        both_ref[place] = (own + bias).astype(BF16)
    normed_ref[...] = normed
    inv_std_ref[...] = jnp.broadcast_to(inv_std, inv_std_ref.shape)
    spread_w_ref[...] = weight


def outer_rows(scale, cot, residues, sorted_wt_ref, turn_ref):
    columns = cot.shape[0] // residues
    depth = LANES // residues
    flat = jnp.dot(cot, sorted_wt_ref[...], preferred_element_type=F32) * scale
    for tile in range(depth * depth // LANES):
        block = flat[:, tile * LANES : (tile + 1) * LANES]
        turned = exchange_blocks(
            [block[i * columns : (i + 1) * columns] for i in range(residues)], depth
        )
        for e in range(residues):
            turn_ref[pl.ds(tile * residues + e, columns, stride=depth), :] = turned[e]
    return turn_ref[...].astype(BF16)


def small_own_kernel(scale, own_ref, other_ref, w_ref, both_ref,
                     keep_ref, outer_near_ref, outer_far_ref, sorted_w_ref, sorted_wt_ref,
                     order_ref, repeat_ref, turn_refs, wide_ref):
    residues, columns, _ = own_ref.shape
    depth = LANES // residues
    wide_ref[...] = w_ref[...].astype(F32)
    for d in range(depth):
        sorted_w_ref[d * depth : (d + 1) * depth, :] = wide_ref[
            pl.ds(d, depth, stride=depth), :
        ].astype(BF16)
    sorted_wt_ref[...] = sorted_w_ref[...].T
    rank = lax.axis_index("res")
    own_is_near = lax.axis_index("seq") == lax.shift_right_logical(rank, 2)
    own = own_ref[...].reshape(residues * columns, LANES)
    other = other_ref[...].reshape(residues * columns, LANES)
    near = outer_rows(
        scale, jnp.where(own_is_near, own, other), residues, sorted_wt_ref, turn_refs[0]
    )
    outer_near_ref[...] = near
    partial = lax.dot_general(both_ref[0], near, NT, preferred_element_type=F32)
    for place in range(columns // residues):
        keep_ref[lax.bitwise_xor(rank & 3, place)] = partial[:, place * LANES : (place + 1) * LANES]
    outer_far_ref[...] = outer_rows(
        scale, jnp.where(own_is_near, other, own), residues, sorted_wt_ref, turn_refs[1]
    )
    order_ref[...] = one_hot(
        lambda row: (
            (2 * (row >> 6 & 1) + (row >> 2 & 1)) * LANES
            + (row & 3) * depth + (row >> 3 & 7) * residues + (row >> 7)
        ),
        order_ref.shape,
    )
    for place in range(residues):
        shape = (LANES, LANES)
        row = lax.broadcasted_iota(jnp.int32, shape, 0)
        lane = lax.broadcasted_iota(jnp.int32, shape, 1)
        repeat_ref[:, place * LANES : (place + 1) * LANES] = jnp.where(
            row == place * depth + lane % depth, 1.0, 0.0
        ).astype(BF16)


def one_hot(target, shape):
    part = (shape[0], LANES)
    wanted = target(lax.broadcasted_iota(jnp.int32, part, 0))
    lane = lax.broadcasted_iota(jnp.int32, part, 1)
    return jnp.concatenate(
        [
            jnp.where(wanted == lane + tile * LANES, 1.0, 0.0).astype(BF16)
            for tile in range(shape[1] // LANES)
        ],
        axis=1,
    )


def blocks_apart(left, repeat, residues):
    depth = LANES // residues
    wide = jnp.dot(left, repeat, preferred_element_type=F32)
    blocks = lane_block(wide.shape, depth) % residues
    return jnp.concatenate(
        [jnp.where(blocks == e, wide, 0.0).astype(BF16) for e in range(residues)], axis=0
    )


def small_partner_kernel(scale, residues, got_ref, sorted_wt_ref, keep_ref, both_ref, order_ref,
                         repeat_ref, leaving_ref, keep_out_ref, right_ref, swap_ref):
    rank = lax.axis_index("res")
    seqs = got_ref.shape[1]
    cot = got_ref[2:4].reshape(2 * seqs, LANES)
    columns = cot.shape[0] // residues
    tiles = sorted_wt_ref.shape[1] // LANES
    flat = jnp.dot(cot, sorted_wt_ref[...], preferred_element_type=F32) * scale
    outer = jnp.concatenate(
        [
            jnp.concatenate(
                [
                    flat[i * columns + start : i * columns + start + 8, tile * LANES : (tile + 1) * LANES]
                    for start in range(0, columns, 8)
                    for tile in range(tiles)
                ],
                axis=0,
            )
            for i in range(residues)
        ],
        axis=1,
    ).astype(BF16)
    apart = blocks_apart(got_ref[0], repeat_ref[...], residues)
    partial = lax.dot_general(apart, outer, NT, preferred_element_type=F32).astype(BF16)
    partial = jnp.concatenate(
        [partial[e * seqs : (e + 1) * seqs] for e in range(residues)], axis=1
    )
    partial = jnp.dot(partial, order_ref[...], preferred_element_type=F32)
    right_ref[0] = both_ref[1]
    right_ref[1] = got_ref[1]
    own_is_near = lax.axis_index("seq") == lax.shift_right_logical(rank, 2)
    swap_ref[0] = jnp.where(own_is_near, got_ref[1], both_ref[1])
    swap_ref[1] = both_ref[0]
    for place in range(leaving_ref.shape[0]):
        leaving_ref[place, 0] = both_ref[1]
        leaving_ref[place, 1] = got_ref[1]
    for place in range(leaving_ref.shape[0]):
        distance = lax.bitwise_xor(rank & 3, place)
        total = keep_ref[distance] + partial[:, place * LANES : (place + 1) * LANES]
        leaving_ref[distance, 2] = total.astype(BF16)
        keep_out_ref[distance] = total


def small_finish_kernel(
    scale, right_ref, part_refs, swapped_ref, swapped_late_ref, both_ref, outer_near_ref, outer_far_ref,
    keep_ref, normed_ref, inv_std_ref, gain_ref, spread_w_ref, sorted_w_ref, offset_ref,
    grad_hbm, pair_hbm, grad_ref, pair_ref, near_ref, beyond_ref, turn_ref, lines_ref, semaphores,
):
    seqs, residues, _ = grad_ref.shape
    columns = pair_ref.shape[1]
    depth = LANES // residues
    ranks = columns // residues
    rank = lax.axis_index("res")
    mine = lax.axis_index("seq")
    here = rank & 3

    blocks_of = [right_ref] + list(part_refs)
    right_all = jnp.concatenate(
        [ref[0] for ref in blocks_of] + [ref[1] for ref in blocks_of], axis=1
    )
    spots = [
        pl.ds(pl.multiple_of(lax.bitwise_xor(here, mask) * LANES, LANES), LANES)
        for mask in range(ranks)
    ]
    outer = jnp.concatenate(
        [outer_near_ref[spot, :] for spot in spots] + [outer_far_ref[spot, :] for spot in spots],
        axis=0,
    )
    left_cot = jnp.dot(right_all, outer, preferred_element_type=F32)
    right_cot = keep_ref[0]
    for part_ref in part_refs:
        right_cot = right_cot + part_ref[2].astype(F32)
    blocks = lane_block((seqs, LANES), depth)
    spread = jnp.concatenate(
        [
            jnp.concatenate(
                [jnp.where(blocks == place, cot, 0.0) for cot in (left_cot, right_cot)], axis=1
            )
            for place in range(residues)
        ],
        axis=0,
    )
    rows = residues * seqs
    parts = jnp.concatenate(split_two(spread), axis=0)
    ln_cot = jnp.dot(parts, spread_w_ref[...], preferred_element_type=F32)
    ln_cot = ln_cot[0:rows] + ln_cot[rows : 2 * rows]
    tiles = range(lines_ref.shape[0])
    for place in range(residues):
        for tile in tiles:
            lines_ref[tile, pl.ds(place, seqs, stride=residues), :] = ln_cot[
                place * seqs : (place + 1) * seqs, tile * LANES : (tile + 1) * LANES
            ]
    gained = jnp.concatenate([lines_ref[tile] for tile in tiles], axis=1) * gain_ref[...]
    normed = normed_ref[...]
    grad = inv_std_ref[:, 0:1] * (
        gained
        - jnp.mean(gained, axis=-1, keepdims=True)
        - normed * jnp.mean(gained * normed, axis=-1, keepdims=True)
    )
    grad_ref[...] = grad.reshape(grad_ref.shape).astype(BF16)
    grad_copy = pltpu.make_async_copy(grad_ref, grad_hbm, semaphores.at[0])
    grad_copy.start()

    half = jnp.where(mine == lax.shift_right_logical(rank, 2), 0, 1)
    for mask, ref in enumerate(blocks_of):
        near_ref[mask] = ref[half]
    beyond_ref[0] = swapped_ref[0]
    beyond_ref[1] = part_refs[0][3]
    beyond_ref[2] = part_refs[1][3]
    beyond_ref[3] = swapped_late_ref[...]
    masks = [lax.bitwise_xor(here, place) for place in range(ranks)]
    right = jnp.concatenate(
        [
            jnp.concatenate([ref[mask] for mask in masks], axis=1)
            for ref in (near_ref, beyond_ref)
        ],
        axis=0,
    )
    left = jnp.concatenate([both_ref[0], swapped_ref[1]], axis=0)
    turn_ref[...] = lax.dot_general(right, left, TN, preferred_element_type=F32) * scale
    tiles = []
    for tile in range(depth * depth // LANES):
        turned = exchange_blocks(
            [
                turn_ref[pl.ds(tile * residues + e, columns, stride=depth), :]
                for e in range(residues)
            ],
            depth,
        )
        tiles.append(jnp.concatenate(turned, axis=0))
    flat = jnp.concatenate(tiles, axis=1)
    rows = residues * columns
    parts = jnp.concatenate(split_two(flat), axis=0)
    pair = jnp.dot(parts, sorted_w_ref[...], preferred_element_type=F32)
    pair = pair[0:rows] + pair[rows : 2 * rows]
    pair_ref[...] = (pair + offset_ref[...]).astype(BF16).reshape(pair_ref.shape)
    pair_copy = pltpu.make_async_copy(pair_ref, pair_hbm, semaphores.at[1])
    pair_copy.start()
    grad_copy.wait()
    pair_copy.wait()


def small_slice(
    homolog_matrix,
    standardizer_scaling,
    standardizer_offset,
    left_projection_matrix,
    left_offset_vector,
    right_projection_matrix,
    right_offset_vector,
    coupling_matrix,
    coupling_offset,
    coupling_cotangent,
):
    seqs, residues, features = homolog_matrix.shape
    depth = left_projection_matrix.shape[1]
    ranks = lax.axis_size("res")
    rows = seqs * residues
    scale = 1.0 / (seqs * lax.axis_size("seq"))
    rank = lax.axis_index("res")
    mine = lax.axis_index("seq")
    swap = [(0, 1), (1, 0)]
    limit = pltpu.CompilerParams(vmem_limit_bytes=8 * 1024 * 1024)
    vmem = pl.BlockSpec(memory_space=pltpu.VMEM)
    like = jax.ShapeDtypeStruct

    other_cot = lax.ppermute(coupling_cotangent, "seq", swap)
    hbm = pl.BlockSpec(memory_space=pltpu.HBM)
    pin = lambda array: pltpu.with_memory_space_constraint(array, pltpu.HBM)
    both, normed, inv_std, spread_w, gain, pair_offset, own_cot = pl.pallas_call(
        small_project_kernel,
        in_specs=[hbm] * 9,
        out_specs=[vmem] * 7,
        out_shape=(
            like((2, seqs, LANES), BF16),
            like((rows, features), F32),
            like((rows, LANES), F32),
            like((2 * LANES, features), BF16),
            like((1, features), F32),
            like((1, LANES), F32),
            like(coupling_cotangent.shape, BF16),
        ),
        scratch_shapes=[
            pltpu.VMEM(homolog_matrix.shape, BF16),
            pltpu.VMEM((1, features), F32),
            pltpu.VMEM((depth, features), BF16),
            pltpu.VMEM((1, depth), F32),
            pltpu.VMEM((depth, features), BF16),
            pltpu.VMEM((1, depth), F32),
            pltpu.VMEM((2, rows, LANES), F32),
            pltpu.SemaphoreType.DMA((12,)),
        ],
        compiler_params=limit,
        name="project",
    )(
        *[
            pin(array)
            for array in (
                homolog_matrix,
                standardizer_scaling.reshape(1, -1),
                standardizer_offset.reshape(1, -1),
                left_projection_matrix.T,
                left_offset_vector.reshape(1, -1),
                right_projection_matrix.T,
                right_offset_vector.reshape(1, -1),
                coupling_offset.reshape(1, -1),
                coupling_cotangent,
            )
        ]
    )

    def swap_over(mask, value):
        return lax.ppermute(value, "res", [(source, source ^ mask) for source in range(ranks)])

    own_is_near = mine == lax.shift_right_logical(rank, 2)
    far_cot = jnp.where(own_is_near, other_cot, own_cot).reshape(2, seqs, LANES)
    beyond_two = swap_over(4, jnp.concatenate([both, far_cot]))

    half_rows = ranks // 2 * LANES
    turn = pltpu.VMEM((half_rows, LANES), F32)
    keep, outer_near, outer_far, sorted_w, sorted_wt, order, repeat = pl.pallas_call(
        functools.partial(small_own_kernel, scale),
        in_specs=[vmem] * 4,
        out_specs=[vmem] * 7,
        out_shape=(
            like((ranks // 2, seqs, LANES), F32),
            like((half_rows, LANES), BF16),
            like((half_rows, LANES), BF16),
            like(coupling_matrix.shape, BF16),
            like(coupling_matrix.shape[::-1], BF16),
            like((half_rows, half_rows), BF16),
            like((LANES, residues * LANES), BF16),
        ),
        scratch_shapes=[[turn, turn], pltpu.VMEM(coupling_matrix.shape, F32)],
        compiler_params=limit,
        name="own_pieces",
    )(own_cot, other_cot, coupling_matrix, both)

    leaving_parts, keep, right, leaving = pl.pallas_call(
        functools.partial(small_partner_kernel, scale, residues),
        in_specs=[vmem] * 6,
        out_specs=[vmem] * 4,
        out_shape=(
            like((ranks // 2, 3, seqs, LANES), BF16),
            like((ranks // 2, seqs, LANES), F32),
            like((2, seqs, LANES), BF16),
            like((2, seqs, LANES), BF16),
        ),
        compiler_params=limit,
        name="partner_pieces",
    )(beyond_two, sorted_wt, keep, both, order, repeat)

    swapped = lax.ppermute(leaving, "seq", swap)
    diagonal = swap_over(3, leaving_parts[3])
    across, beside = [
        swap_over(mask, jnp.concatenate([leaving_parts[mask], swapped[0:1]])) for mask in (2, 1)
    ]
    swapped_late = lax.ppermute(
        jnp.where(own_is_near, diagonal[1], diagonal[0]), "seq", swap
    )

    pair_delta, gradient = pl.pallas_call(
        functools.partial(small_finish_kernel, scale),
        in_specs=[vmem, [vmem] * 3] + [vmem] * 12,
        out_specs=[pl.BlockSpec(memory_space=pl.ANY)] * 2,
        out_shape=(
            like(homolog_matrix.shape, BF16),
            like(coupling_cotangent.shape, BF16),
        ),
        scratch_shapes=[
            pltpu.VMEM(homolog_matrix.shape, BF16),
            pltpu.VMEM(coupling_cotangent.shape, BF16),
            pltpu.VMEM((ranks // 2, seqs, LANES), BF16),
            pltpu.VMEM((ranks // 2, seqs, LANES), BF16),
            pltpu.VMEM((ranks // 2 * LANES, LANES), F32),
            pltpu.VMEM((features // LANES, rows, LANES), F32),
            pltpu.SemaphoreType.DMA((2,)),
        ],
        compiler_params=limit,
        name="finish",
    )(
        right,
        [beside, across, diagonal],
        swapped,
        swapped_late,
        both,
        outer_near,
        outer_far,
        keep,
        normed,
        inv_std,
        gain,
        spread_w,
        sorted_w,
        pair_offset,
    )[::-1]
    return (pair_delta, gradient)


def body(*arrays):
    if lax.axis_size("res") == 8:
        return small_slice(*arrays)
    return wide_slice(*arrays)


def solution(mesh):
    return jax.shard_map(
        body,
        mesh=mesh,
        in_specs=(
            P(("grp", "seq"), "res", None),
            P(),
            P(),
            P(),
            P(),
            P(),
            P(),
            P(),
            P(),
            P(("grp", "res"), "seq", None),
        ),
        out_specs=(P(("grp", "res"), "seq", None), P(("grp", "seq"), "res", None)),
        check_vma=False,
    )
```

```python
import functools

import jax
import jax.numpy as jnp
from jax import lax
from jax.experimental import pallas as pl
from jax.experimental.pallas import tpu as pltpu
from jax.sharding import PartitionSpec as P

LANES = 128
BF16 = jnp.bfloat16
F32 = jnp.float32
NT = (((1,), (1,)), ((), ()))
TN = (((0,), (0,)), ((), ()))


def lane_block(shape, width):
    return lax.broadcasted_iota(jnp.int32, shape, 1) // width


def pick(blocks, pieces):
    result = pieces[0]
    for place in range(1, len(pieces)):
        result = jnp.where(blocks == place, pieces[place], result)
    return result


def split_three(value):
    top = value.astype(BF16)
    rest = value - top.astype(F32)
    middle = rest.astype(BF16)
    low = (rest - middle.astype(F32)).astype(BF16)
    return top, middle, low


def exchange_blocks(pieces, width):
    first, second, third, fourth = pieces
    blocks = lane_block(first.shape, width)
    odd, high = blocks % 2 == 1, blocks >= 2
    roll = lambda value, count: pltpu.roll(value, count * width, 1)
    first, second = jnp.where(odd, roll(second, 1), first), jnp.where(odd, second, roll(first, 3))
    third, fourth = jnp.where(odd, roll(fourth, 1), third), jnp.where(odd, fourth, roll(third, 3))
    return [
        jnp.where(high, roll(third, 2), first),
        jnp.where(high, roll(fourth, 2), second),
        jnp.where(high, third, roll(first, 2)),
        jnp.where(high, fourth, roll(second, 2)),
    ]


def split_two(value):
    top = value.astype(BF16)
    return top, (value - top.astype(F32)).astype(BF16)


def normalise(rows):
    centred = rows - jnp.mean(rows, axis=-1, keepdims=True)
    inv_std = lax.rsqrt(jnp.mean(centred * centred, axis=-1, keepdims=True) + 1e-05)
    return centred * inv_std, inv_std


def residue_rows(x_ref):
    return jnp.concatenate(
        [x_ref[:, place, :].astype(F32) for place in range(x_ref.shape[1])], axis=0
    )


def project_kernel(
    x_ref, gain_ref, offset_ref, left_w_ref, left_b_ref, right_w_ref, right_b_ref, w_ref,
    left_ref, right_ref, sorted_w_ref, wide_ref,
):
    seqs, residues, _ = x_ref.shape
    depth = left_w_ref.shape[0]
    normed, _ = normalise(residue_rows(x_ref))
    ln_out = (normed * gain_ref[...] + offset_ref[...]).astype(BF16)
    blocks = lane_block((seqs, LANES), depth)
    for weight_ref, bias_ref, out_ref in (
        (left_w_ref, left_b_ref, left_ref),
        (right_w_ref, right_b_ref, right_ref),
    ):
        weight = jnp.concatenate([weight_ref[...]] * residues, axis=0)
        bias = jnp.concatenate([bias_ref[...]] * residues, axis=1)
        wide = lax.dot_general(ln_out, weight, NT, preferred_element_type=F32)
        own = pick(blocks, [wide[p * seqs : (p + 1) * seqs] for p in range(residues)])
        out_ref[...] = (own + bias).astype(BF16)
    wide_ref[...] = w_ref[...].astype(F32)
    for d in range(depth):
        sorted_w_ref[d * depth : (d + 1) * depth, :] = wide_ref[
            pl.ds(d, depth, stride=depth), :
        ].astype(BF16)


def cot_kernel(scale, own_ref, other_ref, sorted_w_ref, left_ref, right_ref,
               send_ref, outer_ref, turn_ref):
    residues, columns, _ = own_ref.shape
    depth = sorted_w_ref.shape[0] // (LANES // residues)
    depth = LANES // residues
    first = lax.axis_index("seq") == 0
    own = own_ref[...].reshape(residues * columns, LANES)
    other = other_ref[...].reshape(residues * columns, LANES)
    low = jnp.where(first, own, other)
    high = jnp.where(first, other, own)
    both = jnp.concatenate([low, high], axis=0)
    flat = lax.dot_general(both, sorted_w_ref[...], NT, preferred_element_type=F32) * scale
    blocks = lane_block((columns, LANES), depth)
    for half in range(2):
        for tile in range(depth * depth // LANES):
            block = flat[
                half * residues * columns : (half + 1) * residues * columns,
                tile * LANES : (tile + 1) * LANES,
            ]
            turned = [block] + [pltpu.roll(block, depth * t, 1) for t in range(1, residues)]
            for e in range(residues):
                piece = pick(
                    blocks,
                    [
                        turned[(i - e) % residues][i * columns : (i + 1) * columns]
                        for i in range(residues)
                    ],
                )
                turn_ref[pl.ds(half * columns * depth + tile * residues + e, columns, stride=depth), :] = piece
    outer = turn_ref[...].astype(BF16)
    half_rows = columns * depth
    partial = lax.dot_general(left_ref[...], outer, NT, preferred_element_type=F32).astype(BF16)
    seqs = left_ref.shape[0]
    ranks = columns // residues
    for half in range(2):
        outer_ref[half] = outer[half * half_rows : (half + 1) * half_rows]
        for rank in range(ranks):
            at = (half * ranks + rank) * LANES
            send_ref[half, rank, 0:seqs, :] = right_ref[...]
            send_ref[half, rank, seqs : 2 * seqs, :] = partial[:, at : at + LANES]


def grad_kernel(steps, got_ref, outer_ref, x_ref, gain_ref, left_w_ref, right_w_ref,
                grad_ref, left_cot_ref, right_cot_ref):
    step = pl.program_id(0)
    _, ranks, twice, _ = got_ref.shape
    seqs = twice // 2
    residues = x_ref.shape[1]
    depth = LANES // residues

    @pl.when(step == 0)
    def _():
        left_cot_ref[...] = jnp.zeros_like(left_cot_ref)
        right_cot_ref[...] = jnp.zeros_like(right_cot_ref)

    places = [(half, rank) for half in range(2) for rank in range(ranks)]
    right_all = jnp.concatenate([got_ref[h, r, 0:seqs, :] for h, r in places], axis=1)
    outer = jnp.concatenate([outer_ref[0], outer_ref[1]], axis=0)
    left_cot_ref[...] += jnp.dot(right_all, outer, preferred_element_type=F32)
    total = got_ref[0, 0, seqs:twice, :].astype(F32)
    for h, r in places[1:]:
        total = total + got_ref[h, r, seqs:twice, :].astype(F32)
    right_cot_ref[...] += total

    @pl.when(step == steps - 1)
    def _():
        blocks = lane_block((seqs, LANES), depth)
        left_cot, right_cot = left_cot_ref[...], right_cot_ref[...]
        spread = jnp.concatenate(
            [
                jnp.concatenate(
                    [
                        jnp.where(blocks == place, left_cot, 0.0),
                        jnp.where(blocks == place, right_cot, 0.0),
                    ],
                    axis=1,
                )
                for place in range(residues)
            ],
            axis=0,
        )
        weight = jnp.concatenate(
            [left_w_ref[...]] * residues + [right_w_ref[...]] * residues, axis=0
        )
        rows = residues * seqs
        parts = jnp.concatenate(split_three(spread), axis=0)
        ln_cot = jnp.dot(parts, weight, preferred_element_type=F32)
        ln_cot = ln_cot[0:rows] + (ln_cot[rows : 2 * rows] + ln_cot[2 * rows : 3 * rows])
        gained = ln_cot * gain_ref[...]
        normed, inv_std = normalise(residue_rows(x_ref))
        grad = inv_std * (
            gained
            - jnp.mean(gained, axis=-1, keepdims=True)
            - normed * jnp.mean(gained * normed, axis=-1, keepdims=True)
        )
        for place in range(residues):
            grad_ref[:, place, :] = grad[place * seqs : (place + 1) * seqs].astype(BF16)


def pair_kernel(scale, got_ref, far_ref, left_ref, far_left_ref, sorted_w_ref, offset_ref,
                pair_ref, turn_ref):
    residues, columns, _ = pair_ref.shape
    depth = LANES // residues
    ranks = columns // residues
    mine = lax.axis_index("seq")
    near = jnp.concatenate([got_ref[mine, r] for r in range(ranks)], axis=1)
    far = jnp.concatenate([far_ref[r] for r in range(ranks)], axis=1)
    right = jnp.concatenate([near, far], axis=0)
    left = jnp.concatenate([left_ref[...], far_left_ref[...]], axis=0)
    turn_ref[...] = lax.dot_general(right, left, TN, preferred_element_type=F32) * scale
    blocks = lane_block((columns, LANES), depth)
    tiles = []
    for tile in range(depth * depth // LANES):
        pieces = [
            turn_ref[pl.ds(tile * residues + e, columns, stride=depth), :]
            for e in range(residues)
        ]
        rows = jnp.concatenate(pieces, axis=0)
        turned = [rows] + [pltpu.roll(rows, depth * t, 1) for t in range(1, residues)]
        tiles.append(
            jnp.concatenate(
                [
                    pick(
                        blocks,
                        [
                            turned[(e - i) % residues][e * columns : (e + 1) * columns]
                            for e in range(residues)
                        ],
                    )
                    for i in range(residues)
                ],
                axis=0,
            )
        )
    flat = jnp.concatenate(tiles, axis=1)
    rows = residues * columns
    parts = jnp.concatenate(split_three(flat), axis=0)
    pair = jnp.dot(parts, sorted_w_ref[...], preferred_element_type=F32)
    pair = pair[0:rows] + (pair[rows : 2 * rows] + pair[2 * rows : 3 * rows])
    pair_ref[...] = (pair + offset_ref[...]).astype(BF16).reshape(pair_ref.shape)


def wide_slice(
    homolog_matrix,
    standardizer_scaling,
    standardizer_offset,
    left_projection_matrix,
    left_offset_vector,
    right_projection_matrix,
    right_offset_vector,
    coupling_matrix,
    coupling_offset,
    coupling_cotangent,
):
    seqs, residues, features = homolog_matrix.shape
    depth = left_projection_matrix.shape[1]
    ranks = lax.axis_size("res")
    scale = 1.0 / (seqs * lax.axis_size("seq"))
    half_ranks = ranks // 2
    half_columns = half_ranks * residues
    step_ranks = 4
    columns = step_ranks * residues
    steps = half_ranks // step_ranks
    mine = lax.axis_index("seq")
    swap = [(0, 1), (1, 0)]

    other_cot = lax.ppermute(coupling_cotangent, "seq", swap)
    gain = standardizer_scaling.reshape(1, -1)
    left_w = left_projection_matrix.T
    right_w = right_projection_matrix.T

    left, right, sorted_w = pl.pallas_call(
        project_kernel,
        out_shape=(
            jax.ShapeDtypeStruct((seqs, LANES), BF16),
            jax.ShapeDtypeStruct((seqs, LANES), BF16),
            jax.ShapeDtypeStruct(coupling_matrix.shape, BF16),
        ),
        scratch_shapes=[pltpu.VMEM(coupling_matrix.shape, F32)],
        name="project",
    )(
        homolog_matrix,
        gain,
        standardizer_offset.reshape(1, -1),
        left_w,
        left_offset_vector.reshape(1, -1),
        right_w,
        right_offset_vector.reshape(1, -1),
        coupling_matrix,
    )

    whole = lambda shape: pl.BlockSpec(shape, lambda g: (0,) * len(shape))
    cot_block = pl.BlockSpec((residues, columns, LANES), lambda g: (0, g, 0))
    outer_block = pl.BlockSpec((2, columns * depth, LANES), lambda g: (0, g, 0))
    send_block = pl.BlockSpec((2, step_ranks, 2 * seqs, LANES), lambda g: (0, g, 0, 0))
    send, outer = pl.pallas_call(
        functools.partial(cot_kernel, scale),
        grid=(steps,),
        in_specs=[
            cot_block,
            cot_block,
            whole(sorted_w.shape),
            whole(left.shape),
            whole(right.shape),
        ],
        out_specs=(send_block, outer_block),
        out_shape=(
            jax.ShapeDtypeStruct((2, half_ranks, 2 * seqs, LANES), BF16),
            jax.ShapeDtypeStruct((2, half_columns * depth, LANES), BF16),
        ),
        scratch_shapes=[pltpu.VMEM((2 * columns * depth, LANES), F32)],
        name="cotangent",
    )(coupling_cotangent, other_cot, sorted_w, left, right)

    got = lax.all_to_all(
        send.reshape(ranks, 2 * seqs, LANES), "res", split_axis=0, concat_axis=0, tiled=True
    ).reshape(send.shape)

    leaving = lax.dynamic_index_in_dim(got, 1 - mine, 0, keepdims=False)[:, 0:seqs, :]
    far = lax.ppermute(jnp.concatenate([leaving, left[None]], axis=0), "seq", swap)

    gradient = pl.pallas_call(
        functools.partial(grad_kernel, steps),
        grid=(steps,),
        in_specs=[
            send_block,
            outer_block,
            whole(homolog_matrix.shape),
            whole(gain.shape),
            whole(left_w.shape),
            whole(right_w.shape),
        ],
        out_specs=whole(homolog_matrix.shape),
        out_shape=jax.ShapeDtypeStruct(homolog_matrix.shape, BF16),
        scratch_shapes=[pltpu.VMEM((seqs, LANES), F32)] * 2,
        name="gradient",
    )(got, outer, homolog_matrix, gain, left_w, right_w)

    pair_delta = pl.pallas_call(
        functools.partial(pair_kernel, scale),
        grid=(steps,),
        in_specs=[
            pl.BlockSpec((2, step_ranks, seqs, LANES), lambda g: (0, g, 0, 0)),
            pl.BlockSpec((step_ranks, seqs, LANES), lambda g: (g, 0, 0)),
            whole(left.shape),
            pl.BlockSpec((None, seqs, LANES), lambda g: (half_ranks, 0, 0)),
            whole(sorted_w.shape),
            whole((1, LANES)),
        ],
        out_specs=cot_block,
        out_shape=jax.ShapeDtypeStruct(coupling_cotangent.shape, BF16),
        scratch_shapes=[pltpu.VMEM((columns * depth, LANES), F32)],
        name="pair",
    )(got, far, left, far, sorted_w, coupling_offset.reshape(1, -1))
    return (pair_delta, gradient)


def fetch(source, target, semaphore):
    copy = pltpu.make_async_copy(source, target, semaphore)
    copy.start()
    return copy


def start_copies(pairs, semaphores):
    copies = [
        pltpu.make_async_copy(source, target, semaphores.at[place])
        for place, (source, target) in enumerate(pairs)
    ]
    for copy in copies:
        copy.start()
    return copies


def small_project_kernel(
    x_hbm, gain_hbm, offset_hbm, left_w_hbm, left_b_hbm, right_w_hbm, right_b_hbm, pair_offset_hbm,
    cot_hbm, both_ref, normed_ref, inv_std_ref, spread_w_ref, gain_ref, pair_offset_ref, cot_ref,
    x_ref, offset_ref, left_w_ref, left_b_ref, right_w_ref, right_b_ref, wide_ref, semaphores,
):
    seqs, residues, _ = x_ref.shape
    depth = left_w_ref.shape[0]
    parts = 4
    part = seqs // parts
    copies = start_copies(
        tuple(
            (x_hbm.at[pl.ds(place * part, part)], x_ref.at[pl.ds(place * part, part)])
            for place in range(parts)
        )
        + (
            (left_w_hbm, left_w_ref),
            (right_w_hbm, right_w_ref),
            (gain_hbm, gain_ref),
            (offset_hbm, offset_ref),
            (left_b_hbm, left_b_ref),
            (right_b_hbm, right_b_ref),
            (cot_hbm, cot_ref),
            (pair_offset_hbm, pair_offset_ref),
        ),
        semaphores,
    )
    for copy in copies[:parts]:
        copy.wait()
    rows = x_ref[...].astype(F32).reshape(seqs * residues, x_ref.shape[2])
    normed, inv_std = normalise(rows)
    for copy in copies[parts:]:
        copy.wait()
    ln_out = (normed * gain_ref[...] + offset_ref[...]).astype(BF16)
    blocks = lane_block((seqs, LANES), depth)
    weight = jnp.concatenate(
        [left_w_ref[...]] * residues + [right_w_ref[...]] * residues, axis=0
    )
    wide = lax.dot_general(ln_out, weight, NT, preferred_element_type=F32)
    for place, bias_ref in enumerate((left_b_ref, right_b_ref)):
        bias = jnp.concatenate([bias_ref[...]] * residues, axis=1)
        wide_ref[place, 0 : seqs * residues, :] = wide[:, place * LANES : (place + 1) * LANES]
        own = pick(
            blocks, [wide_ref[place, pl.ds(p, seqs, stride=residues), :] for p in range(residues)]
        )
        both_ref[place] = (own + bias).astype(BF16)
    normed_ref[...] = normed
    inv_std_ref[...] = jnp.broadcast_to(inv_std, inv_std_ref.shape)
    spread_w_ref[...] = weight


def outer_flat(scale, cot, sorted_wt_ref):
    return jnp.dot(cot, sorted_wt_ref[...], preferred_element_type=F32) * scale


def outer_rows(flat, residues, turn_ref):
    columns = flat.shape[0] // residues
    depth = LANES // residues
    for tile in range(depth * depth // LANES):
        block = flat[:, tile * LANES : (tile + 1) * LANES]
        turned = exchange_blocks(
            [block[i * columns : (i + 1) * columns] for i in range(residues)], depth
        )
        for e in range(residues):
            turn_ref[pl.ds(tile * residues + e, columns, stride=depth), :] = turned[e]
    return turn_ref[0 : columns * depth, :].astype(BF16)


def outer_tiles(flat, residues):
    columns = flat.shape[0] // residues
    return jnp.concatenate(
        [
            jnp.concatenate(
                [
                    flat[i * columns + start : i * columns + start + 8, tile : tile + LANES]
                    for start in range(0, columns, 8)
                    for tile in range(0, flat.shape[1], LANES)
                ],
                axis=0,
            )
            for i in range(residues)
        ],
        axis=1,
    ).astype(BF16)


def blocks_apart(left, repeat, residues):
    depth = LANES // residues
    wide = jnp.dot(left, repeat, preferred_element_type=F32)
    blocks = lane_block(wide.shape, depth) % residues
    return jnp.concatenate(
        [jnp.where(blocks == e, wide, 0.0).astype(BF16) for e in range(residues)], axis=0
    )


def column_pieces(left, outer, repeat, residues):
    seqs = left.shape[0]
    partial = lax.dot_general(
        blocks_apart(left, repeat, residues), outer, NT, preferred_element_type=F32
    )
    rows = [partial[e * seqs : (e + 1) * seqs] for e in range(residues)]
    turned = [pltpu.roll(row, LANES // 2, 1) for row in rows]
    low = lane_block(rows[0].shape, LANES // 2) == 0
    return [
        [jnp.where(low, rows[e], turned[e + 1]) for e in (0, 2)],
        [jnp.where(low, turned[e], rows[e + 1]) for e in (0, 2)],
    ]


def small_own_kernel(scale, own_ref, other_ref, w_ref, both_ref, spread_w_ref,
                     keep_ref, outer_near_ref, outer_far_ref, sorted_w_ref, sorted_wt_ref,
                     repeat_ref, columns_w_ref, turn_refs, wide_ref):
    residues, columns, _ = own_ref.shape
    depth = LANES // residues
    wide_ref[0 : w_ref.shape[0], :] = w_ref[...].astype(F32)
    for d in range(depth):
        sorted_w_ref[d * depth : (d + 1) * depth, :] = wide_ref[
            pl.ds(d, depth, stride=depth), :
        ].astype(BF16)
    sorted_wt_ref[...] = sorted_w_ref[...].T
    shape = (LANES, LANES)
    row = lax.broadcasted_iota(jnp.int32, shape, 0)
    lane = lax.broadcasted_iota(jnp.int32, shape, 1)
    for place in range(residues):
        repeat_ref[:, place * LANES : (place + 1) * LANES] = jnp.where(
            row == place * depth + lane % depth, 1.0, 0.0
        ).astype(BF16)
    shape = (columns_w_ref.shape[0], depth)
    row = lax.broadcasted_iota(jnp.int32, shape, 0)
    lane = lax.broadcasted_iota(jnp.int32, shape, 1)
    chosen = jnp.where(lane == (row >> 3 & 7) * residues + (row >> 6), 1.0, 0.0).astype(BF16)
    columns_w_ref[...] = jnp.dot(
        chosen, spread_w_ref[LANES : LANES + depth, :], preferred_element_type=F32
    ).astype(BF16)

    rank = lax.axis_index("res")
    own_is_near = lax.axis_index("seq") == lax.shift_right_logical(rank, 2)
    own = own_ref[...].reshape(residues * columns, LANES)
    other = other_ref[...].reshape(residues * columns, LANES)
    flat = outer_flat(scale, jnp.where(own_is_near, own, other), sorted_wt_ref)
    pieces = column_pieces(both_ref[0], outer_tiles(flat, residues), repeat_ref[...], residues)
    for block in range(2):
        for tile in range(2):
            keep_ref[block, tile] = pieces[block][tile]
    outer_near_ref[...] = outer_rows(flat, residues, turn_refs[0])
    flat = outer_flat(scale, jnp.where(own_is_near, other, own), sorted_wt_ref)
    outer_far_ref[...] = outer_rows(flat, residues, turn_refs[1])


def small_partner_kernel(scale, residues, got_ref, sorted_wt_ref, keep_ref, both_ref, repeat_ref,
                         leaving_ref, keep_out_ref, right_ref, swap_ref):
    rank = lax.axis_index("res")
    seqs = got_ref.shape[1]
    cot = got_ref[2:4].reshape(2 * seqs, LANES)
    outer = outer_tiles(outer_flat(scale, cot, sorted_wt_ref), residues)
    pieces = column_pieces(got_ref[0], outer, repeat_ref[...], residues)
    right_ref[0] = both_ref[1]
    right_ref[1] = got_ref[1]
    own_is_near = lax.axis_index("seq") == lax.shift_right_logical(rank, 2)
    swap_ref[0] = jnp.where(own_is_near, got_ref[1], both_ref[1])
    swap_ref[1] = both_ref[0]
    first = lax.shift_right_logical(rank & 3, 1)
    for block in range(2):
        distance = 2 * lax.bitwise_xor(first, block)
        for tile in range(2):
            total = keep_ref[block, tile] + pieces[block][tile]
            keep_out_ref[distance, tile] = total
            total = total.astype(BF16)
            leaving_ref[distance, 2 + tile] = total
            leaving_ref[distance + 1, 2 + tile] = total
    for place in range(leaving_ref.shape[0]):
        leaving_ref[place, 0] = both_ref[1]
        leaving_ref[place, 1] = got_ref[1]


def small_finish_kernel(
    scale, right_ref, part_refs, swapped_ref, swapped_late_ref, both_ref, outer_near_ref, outer_far_ref,
    keep_ref, normed_ref, inv_std_ref, gain_ref, spread_w_ref, columns_w_ref, sorted_w_ref, offset_ref,
    grad_hbm, pair_hbm, grad_ref, pair_ref, near_ref, beyond_ref, turn_ref, lines_ref, semaphores,
):
    seqs, residues, _ = grad_ref.shape
    columns = pair_ref.shape[1]
    depth = LANES // residues
    ranks = columns // residues
    rank = lax.axis_index("res")
    mine = lax.axis_index("seq")
    here = rank & 3

    blocks_of = [right_ref] + list(part_refs)
    right_all = jnp.concatenate(
        [ref[0] for ref in blocks_of] + [ref[1] for ref in blocks_of], axis=1
    )
    spots = [
        pl.ds(pl.multiple_of(lax.bitwise_xor(here, mask) * LANES, LANES), LANES)
        for mask in range(ranks)
    ]
    outer = jnp.concatenate(
        [outer_near_ref[spot, :] for spot in spots] + [outer_far_ref[spot, :] for spot in spots],
        axis=0,
    )
    left_cot = jnp.dot(right_all, outer, preferred_element_type=F32)
    right_cot = []
    for tile in range(2):
        total = keep_ref[0, tile]
        for part_ref in part_refs:
            total = total + part_ref[2 + tile].astype(F32)
        right_cot.append(total)
    blocks = lane_block((seqs, LANES), depth)
    column = lane_block((seqs, LANES), 1) % 8 - residues * (rank & 1)
    spread = jnp.concatenate(
        [
            jnp.concatenate(
                [jnp.where(blocks == place, left_cot, 0.0)]
                + [jnp.where(column == place, cot, 0.0) for cot in right_cot],
                axis=1,
            )
            for place in range(residues)
        ],
        axis=0,
    )
    rows = residues * seqs
    parts = jnp.concatenate(split_two(spread), axis=0)
    weight = jnp.concatenate([spread_w_ref[0:LANES, :], columns_w_ref[...]], axis=0)
    ln_cot = jnp.dot(parts, weight, preferred_element_type=F32)
    ln_cot = ln_cot[0:rows] + ln_cot[rows : 2 * rows]
    tiles = range(lines_ref.shape[0])
    for place in range(residues):
        for tile in tiles:
            lines_ref[tile, pl.ds(place, seqs, stride=residues), :] = ln_cot[
                place * seqs : (place + 1) * seqs, tile * LANES : (tile + 1) * LANES
            ]
    gained = jnp.concatenate([lines_ref[tile, 0:rows, :] for tile in tiles], axis=1) * gain_ref[...]
    normed = normed_ref[...]
    grad = inv_std_ref[:, 0:1] * (
        gained
        - jnp.mean(gained, axis=-1, keepdims=True)
        - normed * jnp.mean(gained * normed, axis=-1, keepdims=True)
    )
    grad_ref[...] = grad.reshape(grad_ref.shape).astype(BF16)
    grad_copy = pltpu.make_async_copy(grad_ref, grad_hbm, semaphores.at[0])
    grad_copy.start()

    half = jnp.where(mine == lax.shift_right_logical(rank, 2), 0, 1)
    for mask, ref in enumerate(blocks_of):
        near_ref[mask] = ref[half]
    beyond_ref[0] = swapped_ref[0]
    beyond_ref[1] = part_refs[0][4]
    beyond_ref[2] = part_refs[1][4]
    beyond_ref[3] = swapped_late_ref[...]
    masks = [lax.bitwise_xor(here, place) for place in range(ranks)]
    right = jnp.concatenate(
        [
            jnp.concatenate([ref[mask] for mask in masks], axis=1)
            for ref in (near_ref, beyond_ref)
        ],
        axis=0,
    )
    left = jnp.concatenate([both_ref[0], swapped_ref[1]], axis=0)
    turn_ref[0 : columns * depth, :] = lax.dot_general(right, left, TN, preferred_element_type=F32) * scale
    tiles = []
    for tile in range(depth * depth // LANES):
        turned = exchange_blocks(
            [
                turn_ref[pl.ds(tile * residues + e, columns, stride=depth), :]
                for e in range(residues)
            ],
            depth,
        )
        tiles.append(jnp.concatenate(turned, axis=0))
    flat = jnp.concatenate(tiles, axis=1)
    rows = residues * columns
    parts = jnp.concatenate(split_two(flat), axis=0)
    pair = jnp.dot(parts, sorted_w_ref[...], preferred_element_type=F32)
    pair = pair[0:rows] + pair[rows : 2 * rows]
    pair_ref[...] = (pair + offset_ref[...]).astype(BF16).reshape(pair_ref.shape)
    pair_copy = pltpu.make_async_copy(pair_ref, pair_hbm, semaphores.at[1])
    pair_copy.start()
    grad_copy.wait()
    pair_copy.wait()


def small_slice(
    homolog_matrix,
    standardizer_scaling,
    standardizer_offset,
    left_projection_matrix,
    left_offset_vector,
    right_projection_matrix,
    right_offset_vector,
    coupling_matrix,
    coupling_offset,
    coupling_cotangent,
):
    seqs, residues, features = homolog_matrix.shape
    depth = left_projection_matrix.shape[1]
    ranks = lax.axis_size("res")
    rows = seqs * residues
    scale = 1.0 / (seqs * lax.axis_size("seq"))
    rank = lax.axis_index("res")
    mine = lax.axis_index("seq")
    swap = [(0, 1), (1, 0)]
    limit = pltpu.CompilerParams(vmem_limit_bytes=8 * 1024 * 1024)
    vmem = pl.BlockSpec(memory_space=pltpu.VMEM)
    like = jax.ShapeDtypeStruct

    other_cot = lax.ppermute(coupling_cotangent, "seq", swap)
    hbm = pl.BlockSpec(memory_space=pltpu.HBM)
    pin = lambda array: pltpu.with_memory_space_constraint(array, pltpu.HBM)
    both, normed, inv_std, spread_w, gain, pair_offset, own_cot = pl.pallas_call(
        small_project_kernel,
        in_specs=[hbm] * 9,
        out_specs=[vmem] * 7,
        out_shape=(
            like((2, seqs, LANES), BF16),
            like((rows, features), F32),
            like((rows, LANES), F32),
            like((2 * LANES, features), BF16),
            like((1, features), F32),
            like((1, LANES), F32),
            like(coupling_cotangent.shape, BF16),
        ),
        scratch_shapes=[
            pltpu.VMEM(homolog_matrix.shape, BF16),
            pltpu.VMEM((1, features), F32),
            pltpu.VMEM((depth, features), BF16),
            pltpu.VMEM((1, depth), F32),
            pltpu.VMEM((depth, features), BF16),
            pltpu.VMEM((1, depth), F32),
            pltpu.VMEM((2, rows + 8, LANES), F32),
            pltpu.SemaphoreType.DMA((12,)),
        ],
        compiler_params=limit,
        name="project",
    )(
        *[
            pin(array)
            for array in (
                homolog_matrix,
                standardizer_scaling.reshape(1, -1),
                standardizer_offset.reshape(1, -1),
                left_projection_matrix.T,
                left_offset_vector.reshape(1, -1),
                right_projection_matrix.T,
                right_offset_vector.reshape(1, -1),
                coupling_offset.reshape(1, -1),
                coupling_cotangent,
            )
        ]
    )

    def swap_over(mask, value):
        return lax.ppermute(value, "res", [(source, source ^ mask) for source in range(ranks)])

    own_is_near = mine == lax.shift_right_logical(rank, 2)
    far_cot = jnp.where(own_is_near, other_cot, own_cot).reshape(2, seqs, LANES)
    beyond_two = swap_over(4, jnp.concatenate([both, far_cot]))

    half_rows = ranks // 2 * LANES
    turn = pltpu.VMEM((half_rows + depth, LANES), F32)
    keep, outer_near, outer_far, sorted_w, sorted_wt, repeat, columns_w = pl.pallas_call(
        functools.partial(small_own_kernel, scale),
        in_specs=[vmem] * 5,
        out_specs=[vmem] * 7,
        out_shape=(
            like((2, 2, seqs, LANES), F32),
            like((half_rows, LANES), BF16),
            like((half_rows, LANES), BF16),
            like(coupling_matrix.shape, BF16),
            like(coupling_matrix.shape[::-1], BF16),
            like((LANES, residues * LANES), BF16),
            like((2 * LANES, features), BF16),
        ),
        scratch_shapes=[
            [turn, turn],
            pltpu.VMEM((coupling_matrix.shape[0] + depth, LANES), F32),
        ],
        compiler_params=limit,
        name="own_pieces",
    )(own_cot, other_cot, coupling_matrix, both, spread_w)

    leaving_parts, keep, right, leaving = pl.pallas_call(
        functools.partial(small_partner_kernel, scale, residues),
        in_specs=[vmem] * 5,
        out_specs=[vmem] * 4,
        out_shape=(
            like((ranks // 2, 4, seqs, LANES), BF16),
            like((ranks // 2, 2, seqs, LANES), F32),
            like((2, seqs, LANES), BF16),
            like((2, seqs, LANES), BF16),
        ),
        compiler_params=limit,
        name="partner_pieces",
    )(beyond_two, sorted_wt, keep, both, repeat)

    swapped = lax.ppermute(leaving, "seq", swap)
    diagonal = swap_over(3, leaving_parts[3])
    across, beside = [
        swap_over(mask, jnp.concatenate([leaving_parts[mask], swapped[0:1]])) for mask in (2, 1)
    ]
    swapped_late = lax.ppermute(
        jnp.where(own_is_near, diagonal[1], diagonal[0]), "seq", swap
    )

    pair_delta, gradient = pl.pallas_call(
        functools.partial(small_finish_kernel, scale),
        in_specs=[vmem, [vmem] * 3] + [vmem] * 13,
        out_specs=[pl.BlockSpec(memory_space=pl.ANY)] * 2,
        out_shape=(
            like(homolog_matrix.shape, BF16),
            like(coupling_cotangent.shape, BF16),
        ),
        scratch_shapes=[
            pltpu.VMEM(homolog_matrix.shape, BF16),
            pltpu.VMEM(coupling_cotangent.shape, BF16),
            pltpu.VMEM((ranks // 2, seqs, LANES), BF16),
            pltpu.VMEM((ranks // 2, seqs, LANES), BF16),
            turn,
            pltpu.VMEM((features // LANES, rows + 8, LANES), F32),
            pltpu.SemaphoreType.DMA((2,)),
        ],
        compiler_params=limit,
        name="finish",
    )(
        right,
        [beside, across, diagonal],
        swapped,
        swapped_late,
        both,
        outer_near,
        outer_far,
        keep,
        normed,
        inv_std,
        gain,
        spread_w,
        columns_w,
        sorted_w,
        pair_offset,
    )[::-1]
    return (pair_delta, gradient)


def body(*arrays):
    if lax.axis_size("res") == 8:
        return small_slice(*arrays)
    return wide_slice(*arrays)


def solution(mesh):
    return jax.shard_map(
        body,
        mesh=mesh,
        in_specs=(
            P(("grp", "seq"), "res", None),
            P(),
            P(),
            P(),
            P(),
            P(),
            P(),
            P(),
            P(),
            P(("grp", "res"), "seq", None),
        ),
        out_specs=(P(("grp", "res"), "seq", None), P(("grp", "seq"), "res", None)),
        check_vma=False,
    )
```

```python
import functools

import jax
import jax.numpy as jnp
from jax import lax
from jax.experimental import pallas as pl
from jax.experimental.pallas import tpu as pltpu
from jax.sharding import PartitionSpec as P

LANES = 128
BF16 = jnp.bfloat16
F32 = jnp.float32
NT = (((1,), (1,)), ((), ()))
TN = (((0,), (0,)), ((), ()))


def lane_block(shape, width):
    return lax.broadcasted_iota(jnp.int32, shape, 1) // width


def pick(blocks, pieces):
    result = pieces[0]
    for place in range(1, len(pieces)):
        result = jnp.where(blocks == place, pieces[place], result)
    return result


def split_three(value):
    top = value.astype(BF16)
    rest = value - top.astype(F32)
    middle = rest.astype(BF16)
    low = (rest - middle.astype(F32)).astype(BF16)
    return top, middle, low


def exchange_blocks(pieces, width):
    first, second, third, fourth = pieces
    blocks = lane_block(first.shape, width)
    odd, high = blocks % 2 == 1, blocks >= 2
    roll = lambda value, count: pltpu.roll(value, count * width, 1)
    first, second = jnp.where(odd, roll(second, 1), first), jnp.where(odd, second, roll(first, 3))
    third, fourth = jnp.where(odd, roll(fourth, 1), third), jnp.where(odd, fourth, roll(third, 3))
    return [
        jnp.where(high, roll(third, 2), first),
        jnp.where(high, roll(fourth, 2), second),
        jnp.where(high, third, roll(first, 2)),
        jnp.where(high, fourth, roll(second, 2)),
    ]


def split_two(value):
    top = value.astype(BF16)
    return top, (value - top.astype(F32)).astype(BF16)


def normalise(rows):
    centred = rows - jnp.mean(rows, axis=-1, keepdims=True)
    inv_std = lax.rsqrt(jnp.mean(centred * centred, axis=-1, keepdims=True) + 1e-05)
    return centred * inv_std, inv_std


def residue_rows(x_ref):
    return jnp.concatenate(
        [x_ref[:, place, :].astype(F32) for place in range(x_ref.shape[1])], axis=0
    )


def project_kernel(
    x_ref, gain_ref, offset_ref, left_w_ref, left_b_ref, right_w_ref, right_b_ref, w_ref,
    left_ref, right_ref, sorted_w_ref, wide_ref,
):
    seqs, residues, _ = x_ref.shape
    depth = left_w_ref.shape[0]
    normed, _ = normalise(residue_rows(x_ref))
    ln_out = (normed * gain_ref[...] + offset_ref[...]).astype(BF16)
    blocks = lane_block((seqs, LANES), depth)
    for weight_ref, bias_ref, out_ref in (
        (left_w_ref, left_b_ref, left_ref),
        (right_w_ref, right_b_ref, right_ref),
    ):
        weight = jnp.concatenate([weight_ref[...]] * residues, axis=0)
        bias = jnp.concatenate([bias_ref[...]] * residues, axis=1)
        wide = lax.dot_general(ln_out, weight, NT, preferred_element_type=F32)
        own = pick(blocks, [wide[p * seqs : (p + 1) * seqs] for p in range(residues)])
        out_ref[...] = (own + bias).astype(BF16)
    wide_ref[...] = w_ref[...].astype(F32)
    for d in range(depth):
        sorted_w_ref[d * depth : (d + 1) * depth, :] = wide_ref[
            pl.ds(d, depth, stride=depth), :
        ].astype(BF16)


def cot_kernel(scale, own_ref, other_ref, sorted_w_ref, left_ref, right_ref,
               send_ref, outer_ref, turn_ref):
    residues, columns, _ = own_ref.shape
    depth = sorted_w_ref.shape[0] // (LANES // residues)
    depth = LANES // residues
    first = lax.axis_index("seq") == 0
    own = own_ref[...].reshape(residues * columns, LANES)
    other = other_ref[...].reshape(residues * columns, LANES)
    low = jnp.where(first, own, other)
    high = jnp.where(first, other, own)
    both = jnp.concatenate([low, high], axis=0)
    flat = lax.dot_general(both, sorted_w_ref[...], NT, preferred_element_type=F32) * scale
    blocks = lane_block((columns, LANES), depth)
    for half in range(2):
        for tile in range(depth * depth // LANES):
            block = flat[
                half * residues * columns : (half + 1) * residues * columns,
                tile * LANES : (tile + 1) * LANES,
            ]
            turned = [block] + [pltpu.roll(block, depth * t, 1) for t in range(1, residues)]
            for e in range(residues):
                piece = pick(
                    blocks,
                    [
                        turned[(i - e) % residues][i * columns : (i + 1) * columns]
                        for i in range(residues)
                    ],
                )
                turn_ref[pl.ds(half * columns * depth + tile * residues + e, columns, stride=depth), :] = piece
    outer = turn_ref[...].astype(BF16)
    half_rows = columns * depth
    partial = lax.dot_general(left_ref[...], outer, NT, preferred_element_type=F32).astype(BF16)
    seqs = left_ref.shape[0]
    ranks = columns // residues
    for half in range(2):
        outer_ref[half] = outer[half * half_rows : (half + 1) * half_rows]
        for rank in range(ranks):
            at = (half * ranks + rank) * LANES
            send_ref[half, rank, 0:seqs, :] = right_ref[...]
            send_ref[half, rank, seqs : 2 * seqs, :] = partial[:, at : at + LANES]


def grad_kernel(steps, got_ref, outer_ref, x_ref, gain_ref, left_w_ref, right_w_ref,
                grad_ref, left_cot_ref, right_cot_ref):
    step = pl.program_id(0)
    _, ranks, twice, _ = got_ref.shape
    seqs = twice // 2
    residues = x_ref.shape[1]
    depth = LANES // residues

    @pl.when(step == 0)
    def _():
        left_cot_ref[...] = jnp.zeros_like(left_cot_ref)
        right_cot_ref[...] = jnp.zeros_like(right_cot_ref)

    places = [(half, rank) for half in range(2) for rank in range(ranks)]
    right_all = jnp.concatenate([got_ref[h, r, 0:seqs, :] for h, r in places], axis=1)
    outer = jnp.concatenate([outer_ref[0], outer_ref[1]], axis=0)
    left_cot_ref[...] += jnp.dot(right_all, outer, preferred_element_type=F32)
    total = got_ref[0, 0, seqs:twice, :].astype(F32)
    for h, r in places[1:]:
        total = total + got_ref[h, r, seqs:twice, :].astype(F32)
    right_cot_ref[...] += total

    @pl.when(step == steps - 1)
    def _():
        blocks = lane_block((seqs, LANES), depth)
        left_cot, right_cot = left_cot_ref[...], right_cot_ref[...]
        spread = jnp.concatenate(
            [
                jnp.concatenate(
                    [
                        jnp.where(blocks == place, left_cot, 0.0),
                        jnp.where(blocks == place, right_cot, 0.0),
                    ],
                    axis=1,
                )
                for place in range(residues)
            ],
            axis=0,
        )
        weight = jnp.concatenate(
            [left_w_ref[...]] * residues + [right_w_ref[...]] * residues, axis=0
        )
        rows = residues * seqs
        parts = jnp.concatenate(split_three(spread), axis=0)
        ln_cot = jnp.dot(parts, weight, preferred_element_type=F32)
        ln_cot = ln_cot[0:rows] + (ln_cot[rows : 2 * rows] + ln_cot[2 * rows : 3 * rows])
        gained = ln_cot * gain_ref[...]
        normed, inv_std = normalise(residue_rows(x_ref))
        grad = inv_std * (
            gained
            - jnp.mean(gained, axis=-1, keepdims=True)
            - normed * jnp.mean(gained * normed, axis=-1, keepdims=True)
        )
        for place in range(residues):
            grad_ref[:, place, :] = grad[place * seqs : (place + 1) * seqs].astype(BF16)


def pair_kernel(scale, got_ref, far_ref, left_ref, far_left_ref, sorted_w_ref, offset_ref,
                pair_ref, turn_ref):
    residues, columns, _ = pair_ref.shape
    depth = LANES // residues
    ranks = columns // residues
    mine = lax.axis_index("seq")
    near = jnp.concatenate([got_ref[mine, r] for r in range(ranks)], axis=1)
    far = jnp.concatenate([far_ref[r] for r in range(ranks)], axis=1)
    right = jnp.concatenate([near, far], axis=0)
    left = jnp.concatenate([left_ref[...], far_left_ref[...]], axis=0)
    turn_ref[...] = lax.dot_general(right, left, TN, preferred_element_type=F32) * scale
    blocks = lane_block((columns, LANES), depth)
    tiles = []
    for tile in range(depth * depth // LANES):
        pieces = [
            turn_ref[pl.ds(tile * residues + e, columns, stride=depth), :]
            for e in range(residues)
        ]
        rows = jnp.concatenate(pieces, axis=0)
        turned = [rows] + [pltpu.roll(rows, depth * t, 1) for t in range(1, residues)]
        tiles.append(
            jnp.concatenate(
                [
                    pick(
                        blocks,
                        [
                            turned[(e - i) % residues][e * columns : (e + 1) * columns]
                            for e in range(residues)
                        ],
                    )
                    for i in range(residues)
                ],
                axis=0,
            )
        )
    flat = jnp.concatenate(tiles, axis=1)
    rows = residues * columns
    parts = jnp.concatenate(split_three(flat), axis=0)
    pair = jnp.dot(parts, sorted_w_ref[...], preferred_element_type=F32)
    pair = pair[0:rows] + (pair[rows : 2 * rows] + pair[2 * rows : 3 * rows])
    pair_ref[...] = (pair + offset_ref[...]).astype(BF16).reshape(pair_ref.shape)


def wide_slice(
    homolog_matrix,
    standardizer_scaling,
    standardizer_offset,
    left_projection_matrix,
    left_offset_vector,
    right_projection_matrix,
    right_offset_vector,
    coupling_matrix,
    coupling_offset,
    coupling_cotangent,
):
    seqs, residues, features = homolog_matrix.shape
    depth = left_projection_matrix.shape[1]
    ranks = lax.axis_size("res")
    scale = 1.0 / (seqs * lax.axis_size("seq"))
    half_ranks = ranks // 2
    half_columns = half_ranks * residues
    step_ranks = 4
    columns = step_ranks * residues
    steps = half_ranks // step_ranks
    mine = lax.axis_index("seq")
    swap = [(0, 1), (1, 0)]

    other_cot = lax.ppermute(coupling_cotangent, "seq", swap)
    gain = standardizer_scaling.reshape(1, -1)
    left_w = left_projection_matrix.T
    right_w = right_projection_matrix.T

    left, right, sorted_w = pl.pallas_call(
        project_kernel,
        out_shape=(
            jax.ShapeDtypeStruct((seqs, LANES), BF16),
            jax.ShapeDtypeStruct((seqs, LANES), BF16),
            jax.ShapeDtypeStruct(coupling_matrix.shape, BF16),
        ),
        scratch_shapes=[pltpu.VMEM(coupling_matrix.shape, F32)],
        name="project",
    )(
        homolog_matrix,
        gain,
        standardizer_offset.reshape(1, -1),
        left_w,
        left_offset_vector.reshape(1, -1),
        right_w,
        right_offset_vector.reshape(1, -1),
        coupling_matrix,
    )

    whole = lambda shape: pl.BlockSpec(shape, lambda g: (0,) * len(shape))
    cot_block = pl.BlockSpec((residues, columns, LANES), lambda g: (0, g, 0))
    outer_block = pl.BlockSpec((2, columns * depth, LANES), lambda g: (0, g, 0))
    send_block = pl.BlockSpec((2, step_ranks, 2 * seqs, LANES), lambda g: (0, g, 0, 0))
    send, outer = pl.pallas_call(
        functools.partial(cot_kernel, scale),
        grid=(steps,),
        in_specs=[
            cot_block,
            cot_block,
            whole(sorted_w.shape),
            whole(left.shape),
            whole(right.shape),
        ],
        out_specs=(send_block, outer_block),
        out_shape=(
            jax.ShapeDtypeStruct((2, half_ranks, 2 * seqs, LANES), BF16),
            jax.ShapeDtypeStruct((2, half_columns * depth, LANES), BF16),
        ),
        scratch_shapes=[pltpu.VMEM((2 * columns * depth, LANES), F32)],
        name="cotangent",
    )(coupling_cotangent, other_cot, sorted_w, left, right)

    got = lax.all_to_all(
        send.reshape(ranks, 2 * seqs, LANES), "res", split_axis=0, concat_axis=0, tiled=True
    ).reshape(send.shape)

    leaving = lax.dynamic_index_in_dim(got, 1 - mine, 0, keepdims=False)[:, 0:seqs, :]
    far = lax.ppermute(jnp.concatenate([leaving, left[None]], axis=0), "seq", swap)

    gradient = pl.pallas_call(
        functools.partial(grad_kernel, steps),
        grid=(steps,),
        in_specs=[
            send_block,
            outer_block,
            whole(homolog_matrix.shape),
            whole(gain.shape),
            whole(left_w.shape),
            whole(right_w.shape),
        ],
        out_specs=whole(homolog_matrix.shape),
        out_shape=jax.ShapeDtypeStruct(homolog_matrix.shape, BF16),
        scratch_shapes=[pltpu.VMEM((seqs, LANES), F32)] * 2,
        name="gradient",
    )(got, outer, homolog_matrix, gain, left_w, right_w)

    pair_delta = pl.pallas_call(
        functools.partial(pair_kernel, scale),
        grid=(steps,),
        in_specs=[
            pl.BlockSpec((2, step_ranks, seqs, LANES), lambda g: (0, g, 0, 0)),
            pl.BlockSpec((step_ranks, seqs, LANES), lambda g: (g, 0, 0)),
            whole(left.shape),
            pl.BlockSpec((None, seqs, LANES), lambda g: (half_ranks, 0, 0)),
            whole(sorted_w.shape),
            whole((1, LANES)),
        ],
        out_specs=cot_block,
        out_shape=jax.ShapeDtypeStruct(coupling_cotangent.shape, BF16),
        scratch_shapes=[pltpu.VMEM((columns * depth, LANES), F32)],
        name="pair",
    )(got, far, left, far, sorted_w, coupling_offset.reshape(1, -1))
    return (pair_delta, gradient)


def fetch(source, target, semaphore):
    copy = pltpu.make_async_copy(source, target, semaphore)
    copy.start()
    return copy


def start_copies(pairs, semaphores):
    copies = [
        pltpu.make_async_copy(source, target, semaphores.at[place])
        for place, (source, target) in enumerate(pairs)
    ]
    for copy in copies:
        copy.start()
    return copies


def small_project_kernel(
    x_hbm, gain_hbm, offset_hbm, left_w_hbm, left_b_hbm, right_w_hbm, right_b_hbm, pair_offset_hbm,
    cot_hbm, both_ref, normed_ref, inv_std_ref, spread_w_ref, gain_ref, pair_offset_ref, cot_ref,
    x_ref, offset_ref, left_w_ref, left_b_ref, right_w_ref, right_b_ref, wide_ref, semaphores,
):
    seqs, residues, _ = x_ref.shape
    depth = left_w_ref.shape[0]
    parts = 4
    part = seqs // parts
    copies = start_copies(
        tuple(
            (x_hbm.at[pl.ds(place * part, part)], x_ref.at[pl.ds(place * part, part)])
            for place in range(parts)
        )
        + (
            (left_w_hbm, left_w_ref),
            (right_w_hbm, right_w_ref),
            (gain_hbm, gain_ref),
            (offset_hbm, offset_ref),
            (left_b_hbm, left_b_ref),
            (right_b_hbm, right_b_ref),
            (cot_hbm, cot_ref),
            (pair_offset_hbm, pair_offset_ref),
        ),
        semaphores,
    )
    for copy in copies[:parts]:
        copy.wait()
    rows = x_ref[...].astype(F32).reshape(seqs * residues, x_ref.shape[2])
    normed, inv_std = normalise(rows)
    for copy in copies[parts:]:
        copy.wait()
    ln_out = (normed * gain_ref[...] + offset_ref[...]).astype(BF16)
    blocks = lane_block((seqs, LANES), depth)
    weight = jnp.concatenate(
        [left_w_ref[...]] * residues + [right_w_ref[...]] * residues, axis=0
    )
    wide = lax.dot_general(ln_out, weight, NT, preferred_element_type=F32)
    for place, bias_ref in enumerate((left_b_ref, right_b_ref)):
        bias = jnp.concatenate([bias_ref[...]] * residues, axis=1)
        wide_ref[place, 0 : seqs * residues, :] = wide[:, place * LANES : (place + 1) * LANES]
        own = pick(
            blocks, [wide_ref[place, pl.ds(p, seqs, stride=residues), :] for p in range(residues)]
        )
        both_ref[place] = (own + bias).astype(BF16)
    normed_ref[...] = normed
    inv_std_ref[...] = jnp.broadcast_to(inv_std, inv_std_ref.shape)
    spread_w_ref[...] = weight


def outer_flat(scale, cot, sorted_wt_ref):
    return jnp.dot(cot, sorted_wt_ref[...], preferred_element_type=F32) * scale


def outer_rows(flat, residues, turn_ref):
    columns = flat.shape[0] // residues
    depth = LANES // residues
    for tile in range(depth * depth // LANES):
        block = flat[:, tile * LANES : (tile + 1) * LANES]
        turned = exchange_blocks(
            [block[i * columns : (i + 1) * columns] for i in range(residues)], depth
        )
        for e in range(residues):
            turn_ref[pl.ds(tile * residues + e, columns, stride=depth), :] = turned[e]
    return turn_ref[0 : columns * depth, :].astype(BF16)


def outer_tiles(flat, residues):
    columns = flat.shape[0] // residues
    return jnp.concatenate(
        [
            jnp.concatenate(
                [
                    flat[i * columns + start : i * columns + start + 8, tile : tile + LANES]
                    for start in range(0, columns, 8)
                    for tile in range(0, flat.shape[1], LANES)
                ],
                axis=0,
            )
            for i in range(residues)
        ],
        axis=1,
    ).astype(BF16)


def blocks_apart(left, repeat, residues):
    depth = LANES // residues
    wide = jnp.dot(left, repeat, preferred_element_type=F32)
    blocks = lane_block(wide.shape, depth) % residues
    return jnp.concatenate(
        [jnp.where(blocks == e, wide, 0.0).astype(BF16) for e in range(residues)], axis=0
    )


def column_pieces(left, outer, repeat, residues):
    seqs = left.shape[0]
    partial = lax.dot_general(
        blocks_apart(left, repeat, residues), outer, NT, preferred_element_type=F32
    )
    rows = [partial[e * seqs : (e + 1) * seqs] for e in range(residues)]
    turned = [pltpu.roll(row, LANES // 2, 1) for row in rows]
    low = lane_block(rows[0].shape, LANES // 2) == 0
    first = lane_block(rows[0].shape, residues) % 2 == 0
    pieces = []
    for block in (
        [jnp.where(low, rows[e], turned[e + 1]) for e in (0, 2)],
        [jnp.where(low, turned[e], rows[e + 1]) for e in (0, 2)],
    ):
        pieces.append(jnp.where(first, block[0], pltpu.roll(block[1], residues, 1)))
        pieces.append(jnp.where(first, pltpu.roll(block[0], LANES - residues, 1), block[1]))
    return pieces


def small_own_kernel(scale, own_ref, other_ref, w_ref, both_ref, spread_w_ref,
                     keep_ref, outer_near_ref, outer_far_ref, sorted_w_ref, sorted_wt_ref,
                     repeat_ref, columns_w_ref, turn_refs, wide_ref):
    residues, columns, _ = own_ref.shape
    depth = LANES // residues
    wide_ref[0 : w_ref.shape[0], :] = w_ref[...].astype(F32)
    for d in range(depth):
        sorted_w_ref[d * depth : (d + 1) * depth, :] = wide_ref[
            pl.ds(d, depth, stride=depth), :
        ].astype(BF16)
    sorted_wt_ref[...] = sorted_w_ref[...].T
    shape = (LANES, LANES)
    row = lax.broadcasted_iota(jnp.int32, shape, 0)
    lane = lax.broadcasted_iota(jnp.int32, shape, 1)
    for place in range(residues):
        repeat_ref[:, place * LANES : (place + 1) * LANES] = jnp.where(
            row == place * depth + lane % depth, 1.0, 0.0
        ).astype(BF16)
    shape = (columns_w_ref.shape[0], depth)
    row = lax.broadcasted_iota(jnp.int32, shape, 0)
    lane = lax.broadcasted_iota(jnp.int32, shape, 1)
    place = (row >> 3 & 7) * residues + 2 * (row >> 2 & 1) + (row >> 6)
    chosen = jnp.where(lane == place, 1.0, 0.0).astype(BF16)
    columns_w_ref[...] = jnp.dot(
        chosen, spread_w_ref[LANES : LANES + depth, :], preferred_element_type=F32
    ).astype(BF16)

    rank = lax.axis_index("res")
    own_is_near = lax.axis_index("seq") == lax.shift_right_logical(rank, 2)
    own = own_ref[...].reshape(residues * columns, LANES)
    other = other_ref[...].reshape(residues * columns, LANES)
    flat = outer_flat(scale, jnp.where(own_is_near, own, other), sorted_wt_ref)
    pieces = column_pieces(both_ref[0], outer_tiles(flat, residues), repeat_ref[...], residues)
    for place, piece in enumerate(pieces):
        keep_ref[place] = piece
    outer_near_ref[...] = outer_rows(flat, residues, turn_refs[0])
    flat = outer_flat(scale, jnp.where(own_is_near, other, own), sorted_wt_ref)
    outer_far_ref[...] = outer_rows(flat, residues, turn_refs[1])


def small_partner_kernel(scale, residues, got_ref, sorted_wt_ref, keep_ref, both_ref, repeat_ref,
                         leaving_ref, keep_out_ref, right_ref, swap_ref):
    rank = lax.axis_index("res")
    seqs = got_ref.shape[1]
    cot = got_ref[2:4].reshape(2 * seqs, LANES)
    outer = outer_tiles(outer_flat(scale, cot, sorted_wt_ref), residues)
    pieces = column_pieces(got_ref[0], outer, repeat_ref[...], residues)
    right_ref[0] = both_ref[1]
    right_ref[1] = got_ref[1]
    own_is_near = lax.axis_index("seq") == lax.shift_right_logical(rank, 2)
    swap_ref[0] = jnp.where(own_is_near, got_ref[1], both_ref[1])
    swap_ref[1] = both_ref[0]
    for place, piece in enumerate(pieces):
        distance = lax.bitwise_xor(rank & 3, place)
        total = keep_ref[place] + piece
        keep_out_ref[distance] = total
        leaving_ref[distance, 2] = total.astype(BF16)
    for place in range(leaving_ref.shape[0]):
        leaving_ref[place, 0] = both_ref[1]
        leaving_ref[place, 1] = got_ref[1]


def small_finish_kernel(
    scale, right_ref, part_refs, swapped_ref, swapped_late_ref, both_ref, outer_near_ref, outer_far_ref,
    keep_ref, normed_ref, inv_std_ref, gain_ref, spread_w_ref, columns_w_ref, sorted_w_ref, offset_ref,
    grad_hbm, pair_hbm, grad_ref, pair_ref, near_ref, beyond_ref, turn_ref, lines_ref, semaphores,
):
    seqs, residues, _ = grad_ref.shape
    columns = pair_ref.shape[1]
    depth = LANES // residues
    ranks = columns // residues
    rank = lax.axis_index("res")
    mine = lax.axis_index("seq")
    here = rank & 3

    blocks_of = [right_ref] + list(part_refs)
    right_all = jnp.concatenate(
        [ref[0] for ref in blocks_of] + [ref[1] for ref in blocks_of], axis=1
    )
    spots = [
        pl.ds(pl.multiple_of(lax.bitwise_xor(here, mask) * LANES, LANES), LANES)
        for mask in range(ranks)
    ]
    outer = jnp.concatenate(
        [outer_near_ref[spot, :] for spot in spots] + [outer_far_ref[spot, :] for spot in spots],
        axis=0,
    )
    left_cot = jnp.dot(right_all, outer, preferred_element_type=F32)
    right_cot = keep_ref[0]
    for part_ref in part_refs:
        right_cot = right_cot + part_ref[2].astype(F32)
    blocks = lane_block((seqs, LANES), depth)
    column = lane_block((seqs, LANES), 1) % residues
    spread = jnp.concatenate(
        [
            jnp.concatenate(
                [
                    jnp.where(blocks == place, left_cot, 0.0),
                    jnp.where(column == place, right_cot, 0.0),
                ],
                axis=1,
            )
            for place in range(residues)
        ],
        axis=0,
    )
    rows = residues * seqs
    parts = jnp.concatenate(split_two(spread), axis=0)
    weight = jnp.concatenate([spread_w_ref[0:LANES, :], columns_w_ref[...]], axis=0)
    ln_cot = jnp.dot(parts, weight, preferred_element_type=F32)
    ln_cot = ln_cot[0:rows] + ln_cot[rows : 2 * rows]
    tiles = range(lines_ref.shape[0])
    for place in range(residues):
        for tile in tiles:
            lines_ref[tile, pl.ds(place, seqs, stride=residues), :] = ln_cot[
                place * seqs : (place + 1) * seqs, tile * LANES : (tile + 1) * LANES
            ]
    gained = jnp.concatenate([lines_ref[tile, 0:rows, :] for tile in tiles], axis=1) * gain_ref[...]
    normed = normed_ref[...]
    grad = inv_std_ref[:, 0:1] * (
        gained
        - jnp.mean(gained, axis=-1, keepdims=True)
        - normed * jnp.mean(gained * normed, axis=-1, keepdims=True)
    )
    grad_ref[...] = grad.reshape(grad_ref.shape).astype(BF16)
    grad_copy = pltpu.make_async_copy(grad_ref, grad_hbm, semaphores.at[0])
    grad_copy.start()

    half = jnp.where(mine == lax.shift_right_logical(rank, 2), 0, 1)
    for mask, ref in enumerate(blocks_of):
        near_ref[mask] = ref[half]
    beyond_ref[0] = swapped_ref[0]
    beyond_ref[1] = part_refs[0][3]
    beyond_ref[2] = part_refs[1][3]
    beyond_ref[3] = swapped_late_ref[...]
    masks = [lax.bitwise_xor(here, place) for place in range(ranks)]
    right = jnp.concatenate(
        [
            jnp.concatenate([ref[mask] for mask in masks], axis=1)
            for ref in (near_ref, beyond_ref)
        ],
        axis=0,
    )
    left = jnp.concatenate([both_ref[0], swapped_ref[1]], axis=0)
    turn_ref[0 : columns * depth, :] = lax.dot_general(right, left, TN, preferred_element_type=F32) * scale
    tiles = []
    for tile in range(depth * depth // LANES):
        turned = exchange_blocks(
            [
                turn_ref[pl.ds(tile * residues + e, columns, stride=depth), :]
                for e in range(residues)
            ],
            depth,
        )
        tiles.append(jnp.concatenate(turned, axis=0))
    flat = jnp.concatenate(tiles, axis=1)
    rows = residues * columns
    parts = jnp.concatenate(split_two(flat), axis=0)
    pair = jnp.dot(parts, sorted_w_ref[...], preferred_element_type=F32)
    pair = pair[0:rows] + pair[rows : 2 * rows]
    pair_ref[...] = (pair + offset_ref[...]).astype(BF16).reshape(pair_ref.shape)
    pair_copy = pltpu.make_async_copy(pair_ref, pair_hbm, semaphores.at[1])
    pair_copy.start()
    grad_copy.wait()
    pair_copy.wait()


def small_slice(
    homolog_matrix,
    standardizer_scaling,
    standardizer_offset,
    left_projection_matrix,
    left_offset_vector,
    right_projection_matrix,
    right_offset_vector,
    coupling_matrix,
    coupling_offset,
    coupling_cotangent,
):
    seqs, residues, features = homolog_matrix.shape
    depth = left_projection_matrix.shape[1]
    ranks = lax.axis_size("res")
    rows = seqs * residues
    scale = 1.0 / (seqs * lax.axis_size("seq"))
    rank = lax.axis_index("res")
    mine = lax.axis_index("seq")
    swap = [(0, 1), (1, 0)]
    limit = pltpu.CompilerParams(vmem_limit_bytes=8 * 1024 * 1024)
    vmem = pl.BlockSpec(memory_space=pltpu.VMEM)
    like = jax.ShapeDtypeStruct

    other_cot = lax.ppermute(coupling_cotangent, "seq", swap)
    hbm = pl.BlockSpec(memory_space=pltpu.HBM)
    pin = lambda array: pltpu.with_memory_space_constraint(array, pltpu.HBM)
    both, normed, inv_std, spread_w, gain, pair_offset, own_cot = pl.pallas_call(
        small_project_kernel,
        in_specs=[hbm] * 9,
        out_specs=[vmem] * 7,
        out_shape=(
            like((2, seqs, LANES), BF16),
            like((rows, features), F32),
            like((rows, LANES), F32),
            like((2 * LANES, features), BF16),
            like((1, features), F32),
            like((1, LANES), F32),
            like(coupling_cotangent.shape, BF16),
        ),
        scratch_shapes=[
            pltpu.VMEM(homolog_matrix.shape, BF16),
            pltpu.VMEM((1, features), F32),
            pltpu.VMEM((depth, features), BF16),
            pltpu.VMEM((1, depth), F32),
            pltpu.VMEM((depth, features), BF16),
            pltpu.VMEM((1, depth), F32),
            pltpu.VMEM((2, rows + 8, LANES), F32),
            pltpu.SemaphoreType.DMA((12,)),
        ],
        compiler_params=limit,
        name="project",
    )(
        *[
            pin(array)
            for array in (
                homolog_matrix,
                standardizer_scaling.reshape(1, -1),
                standardizer_offset.reshape(1, -1),
                left_projection_matrix.T,
                left_offset_vector.reshape(1, -1),
                right_projection_matrix.T,
                right_offset_vector.reshape(1, -1),
                coupling_offset.reshape(1, -1),
                coupling_cotangent,
            )
        ]
    )

    def swap_over(mask, value):
        return lax.ppermute(value, "res", [(source, source ^ mask) for source in range(ranks)])

    own_is_near = mine == lax.shift_right_logical(rank, 2)
    far_cot = jnp.where(own_is_near, other_cot, own_cot).reshape(2, seqs, LANES)
    beyond_two = swap_over(4, jnp.concatenate([both, far_cot]))

    half_rows = ranks // 2 * LANES
    turn = pltpu.VMEM((half_rows + depth, LANES), F32)
    keep, outer_near, outer_far, sorted_w, sorted_wt, repeat, columns_w = pl.pallas_call(
        functools.partial(small_own_kernel, scale),
        in_specs=[vmem] * 5,
        out_specs=[vmem] * 7,
        out_shape=(
            like((ranks // 2, seqs, LANES), F32),
            like((half_rows, LANES), BF16),
            like((half_rows, LANES), BF16),
            like(coupling_matrix.shape, BF16),
            like(coupling_matrix.shape[::-1], BF16),
            like((LANES, residues * LANES), BF16),
            like((LANES, features), BF16),
        ),
        scratch_shapes=[
            [turn, turn],
            pltpu.VMEM((coupling_matrix.shape[0] + depth, LANES), F32),
        ],
        compiler_params=limit,
        name="own_pieces",
    )(own_cot, other_cot, coupling_matrix, both, spread_w)

    leaving_parts, keep, right, leaving = pl.pallas_call(
        functools.partial(small_partner_kernel, scale, residues),
        in_specs=[vmem] * 5,
        out_specs=[vmem] * 4,
        out_shape=(
            like((ranks // 2, 3, seqs, LANES), BF16),
            like((ranks // 2, seqs, LANES), F32),
            like((2, seqs, LANES), BF16),
            like((2, seqs, LANES), BF16),
        ),
        compiler_params=limit,
        name="partner_pieces",
    )(beyond_two, sorted_wt, keep, both, repeat)

    swapped = lax.ppermute(leaving, "seq", swap)
    diagonal = swap_over(3, leaving_parts[3])
    across, beside = [
        swap_over(mask, jnp.concatenate([leaving_parts[mask], swapped[0:1]])) for mask in (2, 1)
    ]
    swapped_late = lax.ppermute(
        jnp.where(own_is_near, diagonal[1], diagonal[0]), "seq", swap
    )

    pair_delta, gradient = pl.pallas_call(
        functools.partial(small_finish_kernel, scale),
        in_specs=[vmem, [vmem] * 3] + [vmem] * 13,
        out_specs=[pl.BlockSpec(memory_space=pl.ANY)] * 2,
        out_shape=(
            like(homolog_matrix.shape, BF16),
            like(coupling_cotangent.shape, BF16),
        ),
        scratch_shapes=[
            pltpu.VMEM(homolog_matrix.shape, BF16),
            pltpu.VMEM(coupling_cotangent.shape, BF16),
            pltpu.VMEM((ranks // 2, seqs, LANES), BF16),
            pltpu.VMEM((ranks // 2, seqs, LANES), BF16),
            turn,
            pltpu.VMEM((features // LANES, rows + 8, LANES), F32),
            pltpu.SemaphoreType.DMA((2,)),
        ],
        compiler_params=limit,
        name="finish",
    )(
        right,
        [beside, across, diagonal],
        swapped,
        swapped_late,
        both,
        outer_near,
        outer_far,
        keep,
        normed,
        inv_std,
        gain,
        spread_w,
        columns_w,
        sorted_w,
        pair_offset,
    )[::-1]
    return (pair_delta, gradient)


def body(*arrays):
    if lax.axis_size("res") == 8:
        return small_slice(*arrays)
    return wide_slice(*arrays)


def solution(mesh):
    return jax.shard_map(
        body,
        mesh=mesh,
        in_specs=(
            P(("grp", "seq"), "res", None),
            P(),
            P(),
            P(),
            P(),
            P(),
            P(),
            P(),
            P(),
            P(("grp", "res"), "seq", None),
        ),
        out_specs=(P(("grp", "res"), "seq", None), P(("grp", "seq"), "res", None)),
        check_vma=False,
    )
```

```python
import functools

import jax
import jax.numpy as jnp
from jax import lax
from jax.experimental import pallas as pl
from jax.experimental.pallas import tpu as pltpu
from jax.sharding import PartitionSpec as P

LANES = 128
BF16 = jnp.bfloat16
F32 = jnp.float32
NT = (((1,), (1,)), ((), ()))
TN = (((0,), (0,)), ((), ()))


def lane_block(shape, width):
    return lax.broadcasted_iota(jnp.int32, shape, 1) // width


def pick(blocks, pieces):
    result = pieces[0]
    for place in range(1, len(pieces)):
        result = jnp.where(blocks == place, pieces[place], result)
    return result


def split_three(value):
    top = value.astype(BF16)
    rest = value - top.astype(F32)
    middle = rest.astype(BF16)
    low = (rest - middle.astype(F32)).astype(BF16)
    return top, middle, low


def exchange_blocks(pieces, width):
    first, second, third, fourth = pieces
    blocks = lane_block(first.shape, width)
    odd, high = blocks % 2 == 1, blocks >= 2
    roll = lambda value, count: pltpu.roll(value, count * width, 1)
    first, second = jnp.where(odd, roll(second, 1), first), jnp.where(odd, second, roll(first, 3))
    third, fourth = jnp.where(odd, roll(fourth, 1), third), jnp.where(odd, fourth, roll(third, 3))
    return [
        jnp.where(high, roll(third, 2), first),
        jnp.where(high, roll(fourth, 2), second),
        jnp.where(high, third, roll(first, 2)),
        jnp.where(high, fourth, roll(second, 2)),
    ]


def split_two(value):
    top = value.astype(BF16)
    return top, (value - top.astype(F32)).astype(BF16)


def normalise(rows):
    centred = rows - jnp.mean(rows, axis=-1, keepdims=True)
    inv_std = lax.rsqrt(jnp.mean(centred * centred, axis=-1, keepdims=True) + 1e-05)
    return centred * inv_std, inv_std


def residue_rows(x_ref):
    return jnp.concatenate(
        [x_ref[:, place, :].astype(F32) for place in range(x_ref.shape[1])], axis=0
    )


def project_kernel(
    x_ref, gain_ref, offset_ref, left_w_ref, left_b_ref, right_w_ref, right_b_ref, w_ref,
    left_ref, right_ref, sorted_w_ref, wide_ref,
):
    seqs, residues, _ = x_ref.shape
    depth = left_w_ref.shape[0]
    normed, _ = normalise(residue_rows(x_ref))
    ln_out = (normed * gain_ref[...] + offset_ref[...]).astype(BF16)
    blocks = lane_block((seqs, LANES), depth)
    for weight_ref, bias_ref, out_ref in (
        (left_w_ref, left_b_ref, left_ref),
        (right_w_ref, right_b_ref, right_ref),
    ):
        weight = jnp.concatenate([weight_ref[...]] * residues, axis=0)
        bias = jnp.concatenate([bias_ref[...]] * residues, axis=1)
        wide = lax.dot_general(ln_out, weight, NT, preferred_element_type=F32)
        own = pick(blocks, [wide[p * seqs : (p + 1) * seqs] for p in range(residues)])
        out_ref[...] = (own + bias).astype(BF16)
    wide_ref[...] = w_ref[...].astype(F32)
    for d in range(depth):
        sorted_w_ref[d * depth : (d + 1) * depth, :] = wide_ref[
            pl.ds(d, depth, stride=depth), :
        ].astype(BF16)


def cot_kernel(scale, own_ref, other_ref, sorted_w_ref, left_ref, right_ref,
               send_ref, outer_ref, turn_ref):
    residues, columns, _ = own_ref.shape
    depth = sorted_w_ref.shape[0] // (LANES // residues)
    depth = LANES // residues
    first = lax.axis_index("seq") == 0
    own = own_ref[...].reshape(residues * columns, LANES)
    other = other_ref[...].reshape(residues * columns, LANES)
    low = jnp.where(first, own, other)
    high = jnp.where(first, other, own)
    both = jnp.concatenate([low, high], axis=0)
    flat = lax.dot_general(both, sorted_w_ref[...], NT, preferred_element_type=F32) * scale
    blocks = lane_block((columns, LANES), depth)
    for half in range(2):
        for tile in range(depth * depth // LANES):
            block = flat[
                half * residues * columns : (half + 1) * residues * columns,
                tile * LANES : (tile + 1) * LANES,
            ]
            turned = [block] + [pltpu.roll(block, depth * t, 1) for t in range(1, residues)]
            for e in range(residues):
                piece = pick(
                    blocks,
                    [
                        turned[(i - e) % residues][i * columns : (i + 1) * columns]
                        for i in range(residues)
                    ],
                )
                turn_ref[pl.ds(half * columns * depth + tile * residues + e, columns, stride=depth), :] = piece
    outer = turn_ref[...].astype(BF16)
    half_rows = columns * depth
    partial = lax.dot_general(left_ref[...], outer, NT, preferred_element_type=F32).astype(BF16)
    seqs = left_ref.shape[0]
    ranks = columns // residues
    for half in range(2):
        outer_ref[half] = outer[half * half_rows : (half + 1) * half_rows]
        for rank in range(ranks):
            at = (half * ranks + rank) * LANES
            send_ref[half, rank, 0:seqs, :] = right_ref[...]
            send_ref[half, rank, seqs : 2 * seqs, :] = partial[:, at : at + LANES]


def grad_kernel(steps, got_ref, outer_ref, x_ref, gain_ref, left_w_ref, right_w_ref,
                grad_ref, left_cot_ref, right_cot_ref):
    step = pl.program_id(0)
    _, ranks, twice, _ = got_ref.shape
    seqs = twice // 2
    residues = x_ref.shape[1]
    depth = LANES // residues

    @pl.when(step == 0)
    def _():
        left_cot_ref[...] = jnp.zeros_like(left_cot_ref)
        right_cot_ref[...] = jnp.zeros_like(right_cot_ref)

    places = [(half, rank) for half in range(2) for rank in range(ranks)]
    right_all = jnp.concatenate([got_ref[h, r, 0:seqs, :] for h, r in places], axis=1)
    outer = jnp.concatenate([outer_ref[0], outer_ref[1]], axis=0)
    left_cot_ref[...] += jnp.dot(right_all, outer, preferred_element_type=F32)
    total = got_ref[0, 0, seqs:twice, :].astype(F32)
    for h, r in places[1:]:
        total = total + got_ref[h, r, seqs:twice, :].astype(F32)
    right_cot_ref[...] += total

    @pl.when(step == steps - 1)
    def _():
        blocks = lane_block((seqs, LANES), depth)
        left_cot, right_cot = left_cot_ref[...], right_cot_ref[...]
        spread = jnp.concatenate(
            [
                jnp.concatenate(
                    [
                        jnp.where(blocks == place, left_cot, 0.0),
                        jnp.where(blocks == place, right_cot, 0.0),
                    ],
                    axis=1,
                )
                for place in range(residues)
            ],
            axis=0,
        )
        weight = jnp.concatenate(
            [left_w_ref[...]] * residues + [right_w_ref[...]] * residues, axis=0
        )
        rows = residues * seqs
        parts = jnp.concatenate(split_three(spread), axis=0)
        ln_cot = jnp.dot(parts, weight, preferred_element_type=F32)
        ln_cot = ln_cot[0:rows] + (ln_cot[rows : 2 * rows] + ln_cot[2 * rows : 3 * rows])
        gained = ln_cot * gain_ref[...]
        normed, inv_std = normalise(residue_rows(x_ref))
        grad = inv_std * (
            gained
            - jnp.mean(gained, axis=-1, keepdims=True)
            - normed * jnp.mean(gained * normed, axis=-1, keepdims=True)
        )
        for place in range(residues):
            grad_ref[:, place, :] = grad[place * seqs : (place + 1) * seqs].astype(BF16)


def pair_kernel(scale, got_ref, far_ref, left_ref, far_left_ref, sorted_w_ref, offset_ref,
                pair_ref, turn_ref):
    residues, columns, _ = pair_ref.shape
    depth = LANES // residues
    ranks = columns // residues
    mine = lax.axis_index("seq")
    near = jnp.concatenate([got_ref[mine, r] for r in range(ranks)], axis=1)
    far = jnp.concatenate([far_ref[r] for r in range(ranks)], axis=1)
    right = jnp.concatenate([near, far], axis=0)
    left = jnp.concatenate([left_ref[...], far_left_ref[...]], axis=0)
    turn_ref[...] = lax.dot_general(right, left, TN, preferred_element_type=F32) * scale
    blocks = lane_block((columns, LANES), depth)
    tiles = []
    for tile in range(depth * depth // LANES):
        pieces = [
            turn_ref[pl.ds(tile * residues + e, columns, stride=depth), :]
            for e in range(residues)
        ]
        rows = jnp.concatenate(pieces, axis=0)
        turned = [rows] + [pltpu.roll(rows, depth * t, 1) for t in range(1, residues)]
        tiles.append(
            jnp.concatenate(
                [
                    pick(
                        blocks,
                        [
                            turned[(e - i) % residues][e * columns : (e + 1) * columns]
                            for e in range(residues)
                        ],
                    )
                    for i in range(residues)
                ],
                axis=0,
            )
        )
    flat = jnp.concatenate(tiles, axis=1)
    rows = residues * columns
    parts = jnp.concatenate(split_three(flat), axis=0)
    pair = jnp.dot(parts, sorted_w_ref[...], preferred_element_type=F32)
    pair = pair[0:rows] + (pair[rows : 2 * rows] + pair[2 * rows : 3 * rows])
    pair_ref[...] = (pair + offset_ref[...]).astype(BF16).reshape(pair_ref.shape)


def wide_slice(
    homolog_matrix,
    standardizer_scaling,
    standardizer_offset,
    left_projection_matrix,
    left_offset_vector,
    right_projection_matrix,
    right_offset_vector,
    coupling_matrix,
    coupling_offset,
    coupling_cotangent,
):
    seqs, residues, features = homolog_matrix.shape
    depth = left_projection_matrix.shape[1]
    ranks = lax.axis_size("res")
    scale = 1.0 / (seqs * lax.axis_size("seq"))
    half_ranks = ranks // 2
    half_columns = half_ranks * residues
    step_ranks = 4
    columns = step_ranks * residues
    steps = half_ranks // step_ranks
    mine = lax.axis_index("seq")
    swap = [(0, 1), (1, 0)]

    other_cot = lax.ppermute(coupling_cotangent, "seq", swap)
    gain = standardizer_scaling.reshape(1, -1)
    left_w = left_projection_matrix.T
    right_w = right_projection_matrix.T

    left, right, sorted_w = pl.pallas_call(
        project_kernel,
        out_shape=(
            jax.ShapeDtypeStruct((seqs, LANES), BF16),
            jax.ShapeDtypeStruct((seqs, LANES), BF16),
            jax.ShapeDtypeStruct(coupling_matrix.shape, BF16),
        ),
        scratch_shapes=[pltpu.VMEM(coupling_matrix.shape, F32)],
        name="project",
    )(
        homolog_matrix,
        gain,
        standardizer_offset.reshape(1, -1),
        left_w,
        left_offset_vector.reshape(1, -1),
        right_w,
        right_offset_vector.reshape(1, -1),
        coupling_matrix,
    )

    whole = lambda shape: pl.BlockSpec(shape, lambda g: (0,) * len(shape))
    cot_block = pl.BlockSpec((residues, columns, LANES), lambda g: (0, g, 0))
    outer_block = pl.BlockSpec((2, columns * depth, LANES), lambda g: (0, g, 0))
    send_block = pl.BlockSpec((2, step_ranks, 2 * seqs, LANES), lambda g: (0, g, 0, 0))
    send, outer = pl.pallas_call(
        functools.partial(cot_kernel, scale),
        grid=(steps,),
        in_specs=[
            cot_block,
            cot_block,
            whole(sorted_w.shape),
            whole(left.shape),
            whole(right.shape),
        ],
        out_specs=(send_block, outer_block),
        out_shape=(
            jax.ShapeDtypeStruct((2, half_ranks, 2 * seqs, LANES), BF16),
            jax.ShapeDtypeStruct((2, half_columns * depth, LANES), BF16),
        ),
        scratch_shapes=[pltpu.VMEM((2 * columns * depth, LANES), F32)],
        name="cotangent",
    )(coupling_cotangent, other_cot, sorted_w, left, right)

    got = lax.all_to_all(
        send.reshape(ranks, 2 * seqs, LANES), "res", split_axis=0, concat_axis=0, tiled=True
    ).reshape(send.shape)

    leaving = lax.dynamic_index_in_dim(got, 1 - mine, 0, keepdims=False)[:, 0:seqs, :]
    far = lax.ppermute(jnp.concatenate([leaving, left[None]], axis=0), "seq", swap)

    gradient = pl.pallas_call(
        functools.partial(grad_kernel, steps),
        grid=(steps,),
        in_specs=[
            send_block,
            outer_block,
            whole(homolog_matrix.shape),
            whole(gain.shape),
            whole(left_w.shape),
            whole(right_w.shape),
        ],
        out_specs=whole(homolog_matrix.shape),
        out_shape=jax.ShapeDtypeStruct(homolog_matrix.shape, BF16),
        scratch_shapes=[pltpu.VMEM((seqs, LANES), F32)] * 2,
        name="gradient",
    )(got, outer, homolog_matrix, gain, left_w, right_w)

    pair_delta = pl.pallas_call(
        functools.partial(pair_kernel, scale),
        grid=(steps,),
        in_specs=[
            pl.BlockSpec((2, step_ranks, seqs, LANES), lambda g: (0, g, 0, 0)),
            pl.BlockSpec((step_ranks, seqs, LANES), lambda g: (g, 0, 0)),
            whole(left.shape),
            pl.BlockSpec((None, seqs, LANES), lambda g: (half_ranks, 0, 0)),
            whole(sorted_w.shape),
            whole((1, LANES)),
        ],
        out_specs=cot_block,
        out_shape=jax.ShapeDtypeStruct(coupling_cotangent.shape, BF16),
        scratch_shapes=[pltpu.VMEM((columns * depth, LANES), F32)],
        name="pair",
    )(got, far, left, far, sorted_w, coupling_offset.reshape(1, -1))
    return (pair_delta, gradient)


def fetch(source, target, semaphore):
    copy = pltpu.make_async_copy(source, target, semaphore)
    copy.start()
    return copy


def start_copies(pairs, semaphores):
    copies = [
        pltpu.make_async_copy(source, target, semaphores.at[place])
        for place, (source, target) in enumerate(pairs)
    ]
    for copy in copies:
        copy.start()
    return copies


def small_project_kernel(
    x_hbm, gain_hbm, offset_hbm, left_w_hbm, left_b_hbm, right_w_hbm, right_b_hbm, pair_offset_hbm,
    cot_hbm, both_ref, normed_ref, inv_std_ref, spread_w_ref, gain_ref, pair_offset_ref, cot_ref,
    x_ref, offset_ref, left_w_ref, left_b_ref, right_w_ref, right_b_ref, wide_ref, semaphores,
):
    seqs, residues, _ = x_ref.shape
    depth = left_w_ref.shape[0]
    parts = 4
    part = seqs // parts
    copies = start_copies(
        tuple(
            (x_hbm.at[pl.ds(place * part, part)], x_ref.at[pl.ds(place * part, part)])
            for place in range(parts)
        )
        + (
            (left_w_hbm, left_w_ref),
            (right_w_hbm, right_w_ref),
            (gain_hbm, gain_ref),
            (offset_hbm, offset_ref),
            (left_b_hbm, left_b_ref),
            (right_b_hbm, right_b_ref),
            (cot_hbm, cot_ref),
            (pair_offset_hbm, pair_offset_ref),
        ),
        semaphores,
    )
    for copy in copies[:parts]:
        copy.wait()
    rows = x_ref[...].astype(F32).reshape(seqs * residues, x_ref.shape[2])
    normed, inv_std = normalise(rows)
    for copy in copies[parts:]:
        copy.wait()
    ln_out = (normed * gain_ref[...] + offset_ref[...]).astype(BF16)
    blocks = lane_block((seqs, LANES), depth)
    weight = jnp.concatenate(
        [left_w_ref[...]] * residues + [right_w_ref[...]] * residues, axis=0
    )
    wide = lax.dot_general(ln_out, weight, NT, preferred_element_type=F32)
    for place, bias_ref in enumerate((left_b_ref, right_b_ref)):
        bias = jnp.concatenate([bias_ref[...]] * residues, axis=1)
        wide_ref[place, 0 : seqs * residues, :] = wide[:, place * LANES : (place + 1) * LANES]
        own = pick(
            blocks, [wide_ref[place, pl.ds(p, seqs, stride=residues), :] for p in range(residues)]
        )
        both_ref[place] = (own + bias).astype(BF16)
    normed_ref[...] = normed
    inv_std_ref[...] = jnp.broadcast_to(inv_std, inv_std_ref.shape)
    spread_w_ref[...] = weight


def outer_flat(scale, cot, sorted_wt_ref):
    return jnp.dot(cot, sorted_wt_ref[...], preferred_element_type=F32) * scale


def outer_rows(flat, residues, turn_ref):
    columns = flat.shape[0] // residues
    depth = LANES // residues
    for tile in range(depth * depth // LANES):
        block = flat[:, tile * LANES : (tile + 1) * LANES]
        turned = exchange_blocks(
            [block[i * columns : (i + 1) * columns] for i in range(residues)], depth
        )
        for e in range(residues):
            turn_ref[pl.ds(tile * residues + e, columns, stride=depth), :] = turned[e]
    return turn_ref[0 : columns * depth, :].astype(BF16)


def outer_tiles(flat, residues):
    columns = flat.shape[0] // residues
    return jnp.concatenate(
        [
            jnp.concatenate(
                [
                    flat[i * columns + start : i * columns + start + 8, tile : tile + LANES]
                    for start in range(0, columns, 8)
                    for tile in range(0, flat.shape[1], LANES)
                ],
                axis=0,
            )
            for i in range(residues)
        ],
        axis=1,
    ).astype(BF16)


def blocks_apart(left, repeat, residues):
    depth = LANES // residues
    wide = jnp.dot(left, repeat, preferred_element_type=F32)
    blocks = lane_block(wide.shape, depth) % residues
    return jnp.concatenate(
        [jnp.where(blocks == e, wide, 0.0).astype(BF16) for e in range(residues)], axis=0
    )


def column_pieces(left, outer, repeat, residues):
    seqs = left.shape[0]
    partial = lax.dot_general(
        blocks_apart(left, repeat, residues), outer, NT, preferred_element_type=F32
    )
    rows = [partial[e * seqs : (e + 1) * seqs] for e in range(residues)]
    turned = [pltpu.roll(row, LANES // 2, 1) for row in rows]
    low = lane_block(rows[0].shape, LANES // 2) == 0
    first = lane_block(rows[0].shape, residues) % 2 == 0
    pieces = []
    for block in (
        [jnp.where(low, rows[e], turned[e + 1]) for e in (0, 2)],
        [jnp.where(low, turned[e], rows[e + 1]) for e in (0, 2)],
    ):
        pieces.append(jnp.where(first, block[0], pltpu.roll(block[1], residues, 1)))
        pieces.append(jnp.where(first, pltpu.roll(block[0], LANES - residues, 1), block[1]))
    return pieces


def small_own_kernel(scale, own_ref, other_ref, w_ref, both_ref, spread_w_ref,
                     keep_ref, outer_near_ref, outer_far_ref, sorted_w_ref, sorted_wt_ref,
                     repeat_ref, columns_w_ref, turn_refs, wide_ref):
    residues, columns, _ = own_ref.shape
    depth = LANES // residues
    wide_ref[0 : w_ref.shape[0], :] = w_ref[...].astype(F32)
    for d in range(depth):
        sorted_w_ref[d * depth : (d + 1) * depth, :] = wide_ref[
            pl.ds(d, depth, stride=depth), :
        ].astype(BF16)
    sorted_wt_ref[...] = sorted_w_ref[...].T
    shape = (LANES, LANES)
    row = lax.broadcasted_iota(jnp.int32, shape, 0)
    lane = lax.broadcasted_iota(jnp.int32, shape, 1)
    for place in range(residues):
        repeat_ref[:, place * LANES : (place + 1) * LANES] = jnp.where(
            row == place * depth + lane % depth, 1.0, 0.0
        ).astype(BF16)
    shape = (columns_w_ref.shape[0], depth)
    row = lax.broadcasted_iota(jnp.int32, shape, 0)
    lane = lax.broadcasted_iota(jnp.int32, shape, 1)
    place = (row >> 3 & 7) * residues + 2 * (row >> 2 & 1) + (row >> 6)
    chosen = jnp.where(lane == place, 1.0, 0.0).astype(BF16)
    columns_w_ref[...] = jnp.dot(
        chosen, spread_w_ref[LANES : LANES + depth, :], preferred_element_type=F32
    ).astype(BF16)

    rank = lax.axis_index("res")
    own_is_near = lax.axis_index("seq") == lax.shift_right_logical(rank, 2)
    own = own_ref[...].reshape(residues * columns, LANES)
    other = other_ref[...].reshape(residues * columns, LANES)
    flat = outer_flat(scale, jnp.where(own_is_near, own, other), sorted_wt_ref)
    pieces = column_pieces(both_ref[0], outer_tiles(flat, residues), repeat_ref[...], residues)
    for place, piece in enumerate(pieces):
        keep_ref[place] = piece
    outer_near_ref[...] = outer_rows(flat, residues, turn_refs[0])
    flat = outer_flat(scale, jnp.where(own_is_near, other, own), sorted_wt_ref)
    outer_far_ref[...] = outer_rows(flat, residues, turn_refs[1])


def small_partner_kernel(scale, residues, got_ref, sorted_wt_ref, keep_ref, both_ref, repeat_ref,
                         leaving_ref, keep_out_ref, right_ref, swap_ref):
    rank = lax.axis_index("res")
    seqs = got_ref.shape[1]
    cot = got_ref[2:4].reshape(2 * seqs, LANES)
    outer = outer_tiles(outer_flat(scale, cot, sorted_wt_ref), residues)
    pieces = column_pieces(got_ref[0], outer, repeat_ref[...], residues)
    right_ref[0] = both_ref[1]
    right_ref[1] = got_ref[1]
    own_is_near = lax.axis_index("seq") == lax.shift_right_logical(rank, 2)
    swap_ref[0] = jnp.where(own_is_near, got_ref[1], both_ref[1])
    swap_ref[1] = both_ref[0]
    for place, piece in enumerate(pieces):
        distance = lax.bitwise_xor(rank & 3, place)
        total = keep_ref[place] + piece
        keep_out_ref[distance] = total
        leaving_ref[distance, 2] = total.astype(BF16)
    for place in range(leaving_ref.shape[0]):
        leaving_ref[place, 0] = both_ref[1]
        leaving_ref[place, 1] = got_ref[1]


def pair_rows(scale, right, left, residues, sorted_w_ref, turn_ref):
    depth = LANES // residues
    columns = right.shape[1] // depth
    turn_ref[0 : columns * depth, :] = (
        lax.dot_general(right, left, TN, preferred_element_type=F32) * scale
    )
    tiles = []
    for tile in range(depth * depth // LANES):
        turned = exchange_blocks(
            [
                turn_ref[pl.ds(tile * residues + e, columns, stride=depth), :]
                for e in range(residues)
            ],
            depth,
        )
        tiles.append(jnp.concatenate(turned, axis=0))
    flat = jnp.concatenate(tiles, axis=1)
    rows = residues * columns
    parts = jnp.concatenate(split_two(flat), axis=0)
    pair = jnp.dot(parts, sorted_w_ref[...], preferred_element_type=F32)
    return pair[0:rows] + pair[rows : 2 * rows]


def store_pairs(pair, spots, residues, pair_ref):
    columns = pair.shape[0] // residues // len(spots)
    for i in range(residues):
        for place, spot in enumerate(spots):
            start = (i * len(spots) + place) * columns
            pair_ref[spot, i * columns : (i + 1) * columns, :] = pair[start : start + columns]


def left_share(block_refs, masks, outer_near_ref, outer_far_ref):
    here = lax.axis_index("res") & 3
    spots = [
        pl.ds(pl.multiple_of(lax.bitwise_xor(here, mask) * LANES, LANES), LANES) for mask in masks
    ]
    right = jnp.concatenate([ref[0] for ref in block_refs] + [ref[1] for ref in block_refs], axis=1)
    outer = jnp.concatenate(
        [outer_near_ref[spot, :] for spot in spots] + [outer_far_ref[spot, :] for spot in spots],
        axis=0,
    )
    return jnp.dot(right, outer, preferred_element_type=F32)


def own_half():
    near = lax.axis_index("seq") == lax.shift_right_logical(lax.axis_index("res"), 2)
    return jnp.where(near, 0, 1)


def small_early_kernel(
    scale, right_ref, part_ref, swapped_ref, swapped_late_ref, both_ref, outer_near_ref, outer_far_ref,
    keep_ref, sorted_w_ref,
    pair_ref, left_cot_ref, right_cot_ref, turn_ref,
):
    residues = pair_ref.shape[1] // 4
    left_cot_ref[...] = left_share([right_ref, part_ref], (0, 3), outer_near_ref, outer_far_ref)
    right_cot_ref[...] = keep_ref[0] + part_ref[2].astype(F32)
    half = own_half()
    right = jnp.concatenate(
        [
            jnp.concatenate([right_ref[half], part_ref[half]], axis=1),
            jnp.concatenate([swapped_ref[0], swapped_late_ref[...]], axis=1),
        ],
        axis=0,
    )
    left = jnp.concatenate([both_ref[0], swapped_ref[1]], axis=0)
    pair = pair_rows(scale, right, left, residues, sorted_w_ref, turn_ref)
    store_pairs(pair, (0, 1), residues, pair_ref)


def small_finish_kernel(
    scale, part_refs, swapped_ref, both_ref, outer_near_ref, outer_far_ref, early_pair_ref,
    early_left_ref, early_right_ref, normed_ref, inv_std_ref, gain_ref, spread_w_ref, columns_w_ref,
    sorted_w_ref, offset_ref, grad_hbm, pair_hbm, grad_ref, pair_ref, pairs_ref, turn_ref, lines_ref,
    semaphores,
):
    seqs, residues, _ = grad_ref.shape
    columns = pair_ref.shape[1]
    depth = LANES // residues
    ranks = columns // residues

    left_cot = early_left_ref[...] + left_share(part_refs, (1, 2), outer_near_ref, outer_far_ref)
    right_cot = early_right_ref[...]
    for part_ref in part_refs:
        right_cot = right_cot + part_ref[2].astype(F32)
    blocks = lane_block((seqs, LANES), depth)
    column = lane_block((seqs, LANES), 1) % residues
    spread = jnp.concatenate(
        [
            jnp.concatenate(
                [
                    jnp.where(blocks == place, left_cot, 0.0),
                    jnp.where(column == place, right_cot, 0.0),
                ],
                axis=1,
            )
            for place in range(residues)
        ],
        axis=0,
    )
    rows = residues * seqs
    parts = jnp.concatenate(split_two(spread), axis=0)
    weight = jnp.concatenate([spread_w_ref[0:LANES, :], columns_w_ref[...]], axis=0)
    ln_cot = jnp.dot(parts, weight, preferred_element_type=F32)
    ln_cot = ln_cot[0:rows] + ln_cot[rows : 2 * rows]
    tiles = range(lines_ref.shape[0])
    for place in range(residues):
        for tile in tiles:
            lines_ref[tile, pl.ds(place, seqs, stride=residues), :] = ln_cot[
                place * seqs : (place + 1) * seqs, tile * LANES : (tile + 1) * LANES
            ]
    copies = []
    for half in range(2):
        some = pl.ds(half * rows // 2, rows // 2)
        gained = jnp.concatenate([lines_ref[tile, some, :] for tile in tiles], axis=1) * gain_ref[...]
        normed = normed_ref[some, :]
        grad = inv_std_ref[some, 0:1] * (
            gained
            - jnp.mean(gained, axis=-1, keepdims=True)
            - normed * jnp.mean(gained * normed, axis=-1, keepdims=True)
        )
        some = pl.ds(half * seqs // 2, seqs // 2)
        grad_ref[some] = grad.reshape(seqs // 2, residues, grad.shape[1]).astype(BF16)
        copy = pltpu.make_async_copy(grad_ref.at[some], grad_hbm.at[some], semaphores.at[half])
        copy.start()
        copies.append(copy)

    half = own_half()
    right = jnp.concatenate(
        [
            jnp.concatenate([ref[half] for ref in part_refs], axis=1),
            jnp.concatenate([ref[3] for ref in part_refs], axis=1),
        ],
        axis=0,
    )
    left = jnp.concatenate([both_ref[0], swapped_ref[1]], axis=0)
    pair = pair_rows(scale, right, left, residues, sorted_w_ref, turn_ref)
    pairs_ref[0] = early_pair_ref[0]
    pairs_ref[3] = early_pair_ref[1]
    store_pairs(pair, (1, 2), residues, pairs_ref)
    here = lax.axis_index("res") & 3
    placed = [pairs_ref[lax.bitwise_xor(here, place)] for place in range(ranks)]
    for i in range(residues):
        own = [block[i * residues : (i + 1) * residues] for block in placed]
        pair_ref[i] = (jnp.concatenate(own, axis=0) + offset_ref[...]).astype(BF16)
    copy = pltpu.make_async_copy(pair_ref, pair_hbm, semaphores.at[2])
    copy.start()
    for copy in copies + [copy]:
        copy.wait()


def small_slice(
    homolog_matrix,
    standardizer_scaling,
    standardizer_offset,
    left_projection_matrix,
    left_offset_vector,
    right_projection_matrix,
    right_offset_vector,
    coupling_matrix,
    coupling_offset,
    coupling_cotangent,
):
    seqs, residues, features = homolog_matrix.shape
    depth = left_projection_matrix.shape[1]
    ranks = lax.axis_size("res")
    rows = seqs * residues
    scale = 1.0 / (seqs * lax.axis_size("seq"))
    rank = lax.axis_index("res")
    mine = lax.axis_index("seq")
    swap = [(0, 1), (1, 0)]
    limit = pltpu.CompilerParams(vmem_limit_bytes=8 * 1024 * 1024)
    vmem = pl.BlockSpec(memory_space=pltpu.VMEM)
    like = jax.ShapeDtypeStruct

    other_cot = lax.ppermute(coupling_cotangent, "seq", swap)
    hbm = pl.BlockSpec(memory_space=pltpu.HBM)
    pin = lambda array: pltpu.with_memory_space_constraint(array, pltpu.HBM)
    both, normed, inv_std, spread_w, gain, pair_offset, own_cot = pl.pallas_call(
        small_project_kernel,
        in_specs=[hbm] * 9,
        out_specs=[vmem] * 7,
        out_shape=(
            like((2, seqs, LANES), BF16),
            like((rows, features), F32),
            like((rows, LANES), F32),
            like((2 * LANES, features), BF16),
            like((1, features), F32),
            like((1, LANES), F32),
            like(coupling_cotangent.shape, BF16),
        ),
        scratch_shapes=[
            pltpu.VMEM(homolog_matrix.shape, BF16),
            pltpu.VMEM((1, features), F32),
            pltpu.VMEM((depth, features), BF16),
            pltpu.VMEM((1, depth), F32),
            pltpu.VMEM((depth, features), BF16),
            pltpu.VMEM((1, depth), F32),
            pltpu.VMEM((2, rows + 8, LANES), F32),
            pltpu.SemaphoreType.DMA((12,)),
        ],
        compiler_params=limit,
        name="project",
    )(
        *[
            pin(array)
            for array in (
                homolog_matrix,
                standardizer_scaling.reshape(1, -1),
                standardizer_offset.reshape(1, -1),
                left_projection_matrix.T,
                left_offset_vector.reshape(1, -1),
                right_projection_matrix.T,
                right_offset_vector.reshape(1, -1),
                coupling_offset.reshape(1, -1),
                coupling_cotangent,
            )
        ]
    )

    def swap_over(mask, value):
        return lax.ppermute(value, "res", [(source, source ^ mask) for source in range(ranks)])

    own_is_near = mine == lax.shift_right_logical(rank, 2)
    far_cot = jnp.where(own_is_near, other_cot, own_cot).reshape(2, seqs, LANES)
    beyond_two = swap_over(4, jnp.concatenate([both, far_cot]))

    half_rows = ranks // 2 * LANES
    turn = pltpu.VMEM((half_rows + depth, LANES), F32)
    keep, outer_near, outer_far, sorted_w, sorted_wt, repeat, columns_w = pl.pallas_call(
        functools.partial(small_own_kernel, scale),
        in_specs=[vmem] * 5,
        out_specs=[vmem] * 7,
        out_shape=(
            like((ranks // 2, seqs, LANES), F32),
            like((half_rows, LANES), BF16),
            like((half_rows, LANES), BF16),
            like(coupling_matrix.shape, BF16),
            like(coupling_matrix.shape[::-1], BF16),
            like((LANES, residues * LANES), BF16),
            like((LANES, features), BF16),
        ),
        scratch_shapes=[
            [turn, turn],
            pltpu.VMEM((coupling_matrix.shape[0] + depth, LANES), F32),
        ],
        compiler_params=limit,
        name="own_pieces",
    )(own_cot, other_cot, coupling_matrix, both, spread_w)

    leaving_parts, keep, right, leaving = pl.pallas_call(
        functools.partial(small_partner_kernel, scale, residues),
        in_specs=[vmem] * 5,
        out_specs=[vmem] * 4,
        out_shape=(
            like((ranks // 2, 3, seqs, LANES), BF16),
            like((ranks // 2, seqs, LANES), F32),
            like((2, seqs, LANES), BF16),
            like((2, seqs, LANES), BF16),
        ),
        compiler_params=limit,
        name="partner_pieces",
    )(beyond_two, sorted_wt, keep, both, repeat)

    swapped = lax.ppermute(leaving, "seq", swap)
    diagonal = swap_over(3, leaving_parts[3])
    across, beside = [
        swap_over(mask, jnp.concatenate([leaving_parts[mask], swapped[0:1]])) for mask in (2, 1)
    ]
    swapped_late = lax.ppermute(
        jnp.where(own_is_near, diagonal[1], diagonal[0]), "seq", swap
    )

    pair_turn = pltpu.VMEM((2 * LANES + depth, LANES), F32)
    early_pair, early_left, early_right = pl.pallas_call(
        functools.partial(small_early_kernel, scale),
        in_specs=[vmem] * 9,
        out_specs=[vmem] * 3,
        out_shape=(
            like((2, residues * residues, LANES), F32),
            like((seqs, LANES), F32),
            like((seqs, LANES), F32),
        ),
        scratch_shapes=[pair_turn],
        compiler_params=limit,
        name="early",
    )(right, diagonal, swapped, swapped_late, both, outer_near, outer_far, keep, sorted_w)

    gradient, pair_delta = pl.pallas_call(
        functools.partial(small_finish_kernel, scale),
        in_specs=[[vmem] * 2] + [vmem] * 14,
        out_specs=[pl.BlockSpec(memory_space=pl.ANY)] * 2,
        out_shape=(
            like(homolog_matrix.shape, BF16),
            like(coupling_cotangent.shape, BF16),
        ),
        scratch_shapes=[
            pltpu.VMEM(homolog_matrix.shape, BF16),
            pltpu.VMEM(coupling_cotangent.shape, BF16),
            pltpu.VMEM((ranks // 2, residues * residues, LANES), F32),
            pair_turn,
            pltpu.VMEM((features // LANES, rows + 8, LANES), F32),
            pltpu.SemaphoreType.DMA((3,)),
        ],
        compiler_params=limit,
        name="finish",
    )(
        [beside, across],
        swapped,
        both,
        outer_near,
        outer_far,
        early_pair,
        early_left,
        early_right,
        normed,
        inv_std,
        gain,
        spread_w,
        columns_w,
        sorted_w,
        pair_offset,
    )
    return (pair_delta, gradient)


def body(*arrays):
    if lax.axis_size("res") == 8:
        return small_slice(*arrays)
    return wide_slice(*arrays)


def solution(mesh):
    return jax.shard_map(
        body,
        mesh=mesh,
        in_specs=(
            P(("grp", "seq"), "res", None),
            P(),
            P(),
            P(),
            P(),
            P(),
            P(),
            P(),
            P(),
            P(("grp", "res"), "seq", None),
        ),
        out_specs=(P(("grp", "res"), "seq", None), P(("grp", "seq"), "res", None)),
        check_vma=False,
    )
```

```python
import functools

import jax
import jax.numpy as jnp
from jax import lax
from jax.experimental import pallas as pl
from jax.experimental.pallas import tpu as pltpu
from jax.sharding import PartitionSpec as P

LANES = 128
BF16 = jnp.bfloat16
F32 = jnp.float32
NT = (((1,), (1,)), ((), ()))
TN = (((0,), (0,)), ((), ()))


def lane_block(shape, width):
    return lax.broadcasted_iota(jnp.int32, shape, 1) // width


def pick(blocks, pieces):
    result = pieces[0]
    for place in range(1, len(pieces)):
        result = jnp.where(blocks == place, pieces[place], result)
    return result


def split_three(value):
    top = value.astype(BF16)
    rest = value - top.astype(F32)
    middle = rest.astype(BF16)
    low = (rest - middle.astype(F32)).astype(BF16)
    return top, middle, low


def exchange_blocks(pieces, width):
    first, second, third, fourth = pieces
    blocks = lane_block(first.shape, width)
    odd, high = blocks % 2 == 1, blocks >= 2
    roll = lambda value, count: pltpu.roll(value, count * width, 1)
    first, second = jnp.where(odd, roll(second, 1), first), jnp.where(odd, second, roll(first, 3))
    third, fourth = jnp.where(odd, roll(fourth, 1), third), jnp.where(odd, fourth, roll(third, 3))
    return [
        jnp.where(high, roll(third, 2), first),
        jnp.where(high, roll(fourth, 2), second),
        jnp.where(high, third, roll(first, 2)),
        jnp.where(high, fourth, roll(second, 2)),
    ]


def split_two(value):
    top = value.astype(BF16)
    return top, (value - top.astype(F32)).astype(BF16)


def normalise(rows):
    centred = rows - jnp.mean(rows, axis=-1, keepdims=True)
    inv_std = lax.rsqrt(jnp.mean(centred * centred, axis=-1, keepdims=True) + 1e-05)
    return centred * inv_std, inv_std


def residue_rows(x_ref):
    return jnp.concatenate(
        [x_ref[:, place, :].astype(F32) for place in range(x_ref.shape[1])], axis=0
    )


def project_kernel(
    x_ref, gain_ref, offset_ref, left_w_ref, left_b_ref, right_w_ref, right_b_ref, w_ref,
    left_ref, right_ref, sorted_w_ref, wide_ref,
):
    seqs, residues, _ = x_ref.shape
    depth = left_w_ref.shape[0]
    normed, _ = normalise(residue_rows(x_ref))
    ln_out = (normed * gain_ref[...] + offset_ref[...]).astype(BF16)
    blocks = lane_block((seqs, LANES), depth)
    for weight_ref, bias_ref, out_ref in (
        (left_w_ref, left_b_ref, left_ref),
        (right_w_ref, right_b_ref, right_ref),
    ):
        weight = jnp.concatenate([weight_ref[...]] * residues, axis=0)
        bias = jnp.concatenate([bias_ref[...]] * residues, axis=1)
        wide = lax.dot_general(ln_out, weight, NT, preferred_element_type=F32)
        own = pick(blocks, [wide[p * seqs : (p + 1) * seqs] for p in range(residues)])
        out_ref[...] = (own + bias).astype(BF16)
    wide_ref[...] = w_ref[...].astype(F32)
    for d in range(depth):
        sorted_w_ref[d * depth : (d + 1) * depth, :] = wide_ref[
            pl.ds(d, depth, stride=depth), :
        ].astype(BF16)


def cot_kernel(scale, own_ref, other_ref, sorted_w_ref, left_ref, right_ref,
               send_ref, outer_ref, turn_ref):
    residues, columns, _ = own_ref.shape
    depth = sorted_w_ref.shape[0] // (LANES // residues)
    depth = LANES // residues
    first = lax.axis_index("seq") == 0
    own = own_ref[...].reshape(residues * columns, LANES)
    other = other_ref[...].reshape(residues * columns, LANES)
    low = jnp.where(first, own, other)
    high = jnp.where(first, other, own)
    both = jnp.concatenate([low, high], axis=0)
    flat = lax.dot_general(both, sorted_w_ref[...], NT, preferred_element_type=F32) * scale
    blocks = lane_block((columns, LANES), depth)
    for half in range(2):
        for tile in range(depth * depth // LANES):
            block = flat[
                half * residues * columns : (half + 1) * residues * columns,
                tile * LANES : (tile + 1) * LANES,
            ]
            turned = [block] + [pltpu.roll(block, depth * t, 1) for t in range(1, residues)]
            for e in range(residues):
                piece = pick(
                    blocks,
                    [
                        turned[(i - e) % residues][i * columns : (i + 1) * columns]
                        for i in range(residues)
                    ],
                )
                turn_ref[pl.ds(half * columns * depth + tile * residues + e, columns, stride=depth), :] = piece
    outer = turn_ref[...].astype(BF16)
    half_rows = columns * depth
    partial = lax.dot_general(left_ref[...], outer, NT, preferred_element_type=F32).astype(BF16)
    seqs = left_ref.shape[0]
    ranks = columns // residues
    for half in range(2):
        outer_ref[half] = outer[half * half_rows : (half + 1) * half_rows]
        for rank in range(ranks):
            at = (half * ranks + rank) * LANES
            send_ref[half, rank, 0:seqs, :] = right_ref[...]
            send_ref[half, rank, seqs : 2 * seqs, :] = partial[:, at : at + LANES]


def grad_kernel(steps, got_ref, outer_ref, x_ref, gain_ref, left_w_ref, right_w_ref,
                grad_ref, left_cot_ref, right_cot_ref):
    step = pl.program_id(0)
    _, ranks, twice, _ = got_ref.shape
    seqs = twice // 2
    residues = x_ref.shape[1]
    depth = LANES // residues

    @pl.when(step == 0)
    def _():
        left_cot_ref[...] = jnp.zeros_like(left_cot_ref)
        right_cot_ref[...] = jnp.zeros_like(right_cot_ref)

    places = [(half, rank) for half in range(2) for rank in range(ranks)]
    right_all = jnp.concatenate([got_ref[h, r, 0:seqs, :] for h, r in places], axis=1)
    outer = jnp.concatenate([outer_ref[0], outer_ref[1]], axis=0)
    left_cot_ref[...] += jnp.dot(right_all, outer, preferred_element_type=F32)
    total = got_ref[0, 0, seqs:twice, :].astype(F32)
    for h, r in places[1:]:
        total = total + got_ref[h, r, seqs:twice, :].astype(F32)
    right_cot_ref[...] += total

    @pl.when(step == steps - 1)
    def _():
        blocks = lane_block((seqs, LANES), depth)
        left_cot, right_cot = left_cot_ref[...], right_cot_ref[...]
        spread = jnp.concatenate(
            [
                jnp.concatenate(
                    [
                        jnp.where(blocks == place, left_cot, 0.0),
                        jnp.where(blocks == place, right_cot, 0.0),
                    ],
                    axis=1,
                )
                for place in range(residues)
            ],
            axis=0,
        )
        weight = jnp.concatenate(
            [left_w_ref[...]] * residues + [right_w_ref[...]] * residues, axis=0
        )
        rows = residues * seqs
        parts = jnp.concatenate(split_three(spread), axis=0)
        ln_cot = jnp.dot(parts, weight, preferred_element_type=F32)
        ln_cot = ln_cot[0:rows] + (ln_cot[rows : 2 * rows] + ln_cot[2 * rows : 3 * rows])
        gained = ln_cot * gain_ref[...]
        normed, inv_std = normalise(residue_rows(x_ref))
        grad = inv_std * (
            gained
            - jnp.mean(gained, axis=-1, keepdims=True)
            - normed * jnp.mean(gained * normed, axis=-1, keepdims=True)
        )
        for place in range(residues):
            grad_ref[:, place, :] = grad[place * seqs : (place + 1) * seqs].astype(BF16)


def pair_kernel(scale, got_ref, far_ref, left_ref, far_left_ref, sorted_w_ref, offset_ref,
                pair_ref, turn_ref):
    residues, columns, _ = pair_ref.shape
    depth = LANES // residues
    ranks = columns // residues
    mine = lax.axis_index("seq")
    near = jnp.concatenate([got_ref[mine, r] for r in range(ranks)], axis=1)
    far = jnp.concatenate([far_ref[r] for r in range(ranks)], axis=1)
    right = jnp.concatenate([near, far], axis=0)
    left = jnp.concatenate([left_ref[...], far_left_ref[...]], axis=0)
    turn_ref[...] = lax.dot_general(right, left, TN, preferred_element_type=F32) * scale
    blocks = lane_block((columns, LANES), depth)
    tiles = []
    for tile in range(depth * depth // LANES):
        pieces = [
            turn_ref[pl.ds(tile * residues + e, columns, stride=depth), :]
            for e in range(residues)
        ]
        rows = jnp.concatenate(pieces, axis=0)
        turned = [rows] + [pltpu.roll(rows, depth * t, 1) for t in range(1, residues)]
        tiles.append(
            jnp.concatenate(
                [
                    pick(
                        blocks,
                        [
                            turned[(e - i) % residues][e * columns : (e + 1) * columns]
                            for e in range(residues)
                        ],
                    )
                    for i in range(residues)
                ],
                axis=0,
            )
        )
    flat = jnp.concatenate(tiles, axis=1)
    rows = residues * columns
    parts = jnp.concatenate(split_three(flat), axis=0)
    pair = jnp.dot(parts, sorted_w_ref[...], preferred_element_type=F32)
    pair = pair[0:rows] + (pair[rows : 2 * rows] + pair[2 * rows : 3 * rows])
    pair_ref[...] = (pair + offset_ref[...]).astype(BF16).reshape(pair_ref.shape)


def wide_slice(
    homolog_matrix,
    standardizer_scaling,
    standardizer_offset,
    left_projection_matrix,
    left_offset_vector,
    right_projection_matrix,
    right_offset_vector,
    coupling_matrix,
    coupling_offset,
    coupling_cotangent,
):
    seqs, residues, features = homolog_matrix.shape
    depth = left_projection_matrix.shape[1]
    ranks = lax.axis_size("res")
    scale = 1.0 / (seqs * lax.axis_size("seq"))
    half_ranks = ranks // 2
    half_columns = half_ranks * residues
    step_ranks = 4
    columns = step_ranks * residues
    steps = half_ranks // step_ranks
    mine = lax.axis_index("seq")
    swap = [(0, 1), (1, 0)]

    other_cot = lax.ppermute(coupling_cotangent, "seq", swap)
    gain = standardizer_scaling.reshape(1, -1)
    left_w = left_projection_matrix.T
    right_w = right_projection_matrix.T

    left, right, sorted_w = pl.pallas_call(
        project_kernel,
        out_shape=(
            jax.ShapeDtypeStruct((seqs, LANES), BF16),
            jax.ShapeDtypeStruct((seqs, LANES), BF16),
            jax.ShapeDtypeStruct(coupling_matrix.shape, BF16),
        ),
        scratch_shapes=[pltpu.VMEM(coupling_matrix.shape, F32)],
        name="project",
    )(
        homolog_matrix,
        gain,
        standardizer_offset.reshape(1, -1),
        left_w,
        left_offset_vector.reshape(1, -1),
        right_w,
        right_offset_vector.reshape(1, -1),
        coupling_matrix,
    )

    whole = lambda shape: pl.BlockSpec(shape, lambda g: (0,) * len(shape))
    cot_block = pl.BlockSpec((residues, columns, LANES), lambda g: (0, g, 0))
    outer_block = pl.BlockSpec((2, columns * depth, LANES), lambda g: (0, g, 0))
    send_block = pl.BlockSpec((2, step_ranks, 2 * seqs, LANES), lambda g: (0, g, 0, 0))
    send, outer = pl.pallas_call(
        functools.partial(cot_kernel, scale),
        grid=(steps,),
        in_specs=[
            cot_block,
            cot_block,
            whole(sorted_w.shape),
            whole(left.shape),
            whole(right.shape),
        ],
        out_specs=(send_block, outer_block),
        out_shape=(
            jax.ShapeDtypeStruct((2, half_ranks, 2 * seqs, LANES), BF16),
            jax.ShapeDtypeStruct((2, half_columns * depth, LANES), BF16),
        ),
        scratch_shapes=[pltpu.VMEM((2 * columns * depth, LANES), F32)],
        name="cotangent",
    )(coupling_cotangent, other_cot, sorted_w, left, right)

    got = lax.all_to_all(
        send.reshape(ranks, 2 * seqs, LANES), "res", split_axis=0, concat_axis=0, tiled=True
    ).reshape(send.shape)

    leaving = lax.dynamic_index_in_dim(got, 1 - mine, 0, keepdims=False)[:, 0:seqs, :]
    far = lax.ppermute(jnp.concatenate([leaving, left[None]], axis=0), "seq", swap)

    gradient = pl.pallas_call(
        functools.partial(grad_kernel, steps),
        grid=(steps,),
        in_specs=[
            send_block,
            outer_block,
            whole(homolog_matrix.shape),
            whole(gain.shape),
            whole(left_w.shape),
            whole(right_w.shape),
        ],
        out_specs=whole(homolog_matrix.shape),
        out_shape=jax.ShapeDtypeStruct(homolog_matrix.shape, BF16),
        scratch_shapes=[pltpu.VMEM((seqs, LANES), F32)] * 2,
        name="gradient",
    )(got, outer, homolog_matrix, gain, left_w, right_w)

    pair_delta = pl.pallas_call(
        functools.partial(pair_kernel, scale),
        grid=(steps,),
        in_specs=[
            pl.BlockSpec((2, step_ranks, seqs, LANES), lambda g: (0, g, 0, 0)),
            pl.BlockSpec((step_ranks, seqs, LANES), lambda g: (g, 0, 0)),
            whole(left.shape),
            pl.BlockSpec((None, seqs, LANES), lambda g: (half_ranks, 0, 0)),
            whole(sorted_w.shape),
            whole((1, LANES)),
        ],
        out_specs=cot_block,
        out_shape=jax.ShapeDtypeStruct(coupling_cotangent.shape, BF16),
        scratch_shapes=[pltpu.VMEM((columns * depth, LANES), F32)],
        name="pair",
    )(got, far, left, far, sorted_w, coupling_offset.reshape(1, -1))
    return (pair_delta, gradient)


def fetch(source, target, semaphore):
    copy = pltpu.make_async_copy(source, target, semaphore)
    copy.start()
    return copy


def start_copies(pairs, semaphores):
    copies = [
        pltpu.make_async_copy(source, target, semaphores.at[place])
        for place, (source, target) in enumerate(pairs)
    ]
    for copy in copies:
        copy.start()
    return copies


def small_project_kernel(
    x_hbm, gain_hbm, offset_hbm, left_w_hbm, left_b_hbm, right_w_hbm, right_b_hbm, pair_offset_hbm,
    cot_hbm, both_ref, normed_ref, inv_std_ref, spread_w_ref, gain_ref, pair_offset_ref, cot_ref,
    x_ref, offset_ref, left_w_ref, left_b_ref, right_w_ref, right_b_ref, wide_ref, semaphores,
):
    seqs, residues, _ = x_ref.shape
    depth = left_w_ref.shape[0]
    parts = 4
    part = seqs // parts
    copies = start_copies(
        tuple(
            (x_hbm.at[pl.ds(place * part, part)], x_ref.at[pl.ds(place * part, part)])
            for place in range(parts)
        )
        + (
            (left_w_hbm, left_w_ref),
            (right_w_hbm, right_w_ref),
            (gain_hbm, gain_ref),
            (offset_hbm, offset_ref),
            (left_b_hbm, left_b_ref),
            (right_b_hbm, right_b_ref),
            (cot_hbm, cot_ref),
            (pair_offset_hbm, pair_offset_ref),
        ),
        semaphores,
    )
    for copy in copies[:parts]:
        copy.wait()
    rows = x_ref[...].astype(F32).reshape(seqs * residues, x_ref.shape[2])
    normed, inv_std = normalise(rows)
    for copy in copies[parts:]:
        copy.wait()
    ln_out = (normed * gain_ref[...] + offset_ref[...]).astype(BF16)
    blocks = lane_block((seqs, LANES), depth)
    weight = jnp.concatenate(
        [left_w_ref[...]] * residues + [right_w_ref[...]] * residues, axis=0
    )
    wide = lax.dot_general(ln_out, weight, NT, preferred_element_type=F32)
    for place, bias_ref in enumerate((left_b_ref, right_b_ref)):
        bias = jnp.concatenate([bias_ref[...]] * residues, axis=1)
        wide_ref[place, 0 : seqs * residues, :] = wide[:, place * LANES : (place + 1) * LANES]
        own = pick(
            blocks, [wide_ref[place, pl.ds(p, seqs, stride=residues), :] for p in range(residues)]
        )
        both_ref[place] = (own + bias).astype(BF16)
    normed_ref[...] = normed
    inv_std_ref[...] = jnp.broadcast_to(inv_std, inv_std_ref.shape)
    spread_w_ref[...] = weight


def outer_flat(scale, cot, sorted_wt_ref):
    return jnp.dot(cot, sorted_wt_ref[...], preferred_element_type=F32) * scale


def outer_rows(flat, residues, turn_ref):
    columns = flat.shape[0] // residues
    depth = LANES // residues
    for tile in range(depth * depth // LANES):
        block = flat[:, tile * LANES : (tile + 1) * LANES]
        turned = exchange_blocks(
            [block[i * columns : (i + 1) * columns] for i in range(residues)], depth
        )
        for e in range(residues):
            turn_ref[pl.ds(tile * residues + e, columns, stride=depth), :] = turned[e]
    return turn_ref[0 : columns * depth, :].astype(BF16)


def outer_tiles(flat, residues):
    columns = flat.shape[0] // residues
    return jnp.concatenate(
        [
            jnp.concatenate(
                [
                    flat[i * columns + start : i * columns + start + 8, tile : tile + LANES]
                    for start in range(0, columns, 8)
                    for tile in range(0, flat.shape[1], LANES)
                ],
                axis=0,
            )
            for i in range(residues)
        ],
        axis=1,
    ).astype(BF16)


def blocks_apart(left, repeat, residues):
    depth = LANES // residues
    wide = jnp.dot(left, repeat, preferred_element_type=F32)
    blocks = lane_block(wide.shape, depth) % residues
    return jnp.concatenate(
        [jnp.where(blocks == e, wide, 0.0).astype(BF16) for e in range(residues)], axis=0
    )


def column_pieces(left, outer, repeat, residues):
    seqs = left.shape[0]
    partial = lax.dot_general(
        blocks_apart(left, repeat, residues), outer, NT, preferred_element_type=F32
    )
    rows = [partial[e * seqs : (e + 1) * seqs] for e in range(residues)]
    turned = [pltpu.roll(row, LANES // 2, 1) for row in rows]
    low = lane_block(rows[0].shape, LANES // 2) == 0
    return [
        [jnp.where(low, rows[e], turned[e + 1]) for e in (0, 2)],
        [jnp.where(low, turned[e], rows[e + 1]) for e in (0, 2)],
    ]


def small_own_kernel(scale, own_ref, other_ref, w_ref, both_ref, spread_w_ref,
                     keep_ref, outer_near_ref, outer_far_ref, sorted_w_ref, sorted_wt_ref,
                     repeat_ref, columns_w_ref, turn_refs, wide_ref):
    residues, columns, _ = own_ref.shape
    depth = LANES // residues
    wide_ref[0 : w_ref.shape[0], :] = w_ref[...].astype(F32)
    for d in range(depth):
        sorted_w_ref[d * depth : (d + 1) * depth, :] = wide_ref[
            pl.ds(d, depth, stride=depth), :
        ].astype(BF16)
    sorted_wt_ref[...] = sorted_w_ref[...].T
    shape = (LANES, LANES)
    row = lax.broadcasted_iota(jnp.int32, shape, 0)
    lane = lax.broadcasted_iota(jnp.int32, shape, 1)
    for place in range(residues):
        repeat_ref[:, place * LANES : (place + 1) * LANES] = jnp.where(
            row == place * depth + lane % depth, 1.0, 0.0
        ).astype(BF16)
    shape = (columns_w_ref.shape[0], depth)
    row = lax.broadcasted_iota(jnp.int32, shape, 0)
    lane = lax.broadcasted_iota(jnp.int32, shape, 1)
    place = (row >> 3 & 7) * residues + 2 * (row >> 2 & 1) + (row >> 6)
    chosen = jnp.where(lane == place, 1.0, 0.0).astype(BF16)
    columns_w_ref[...] = jnp.dot(
        chosen, spread_w_ref[LANES : LANES + depth, :], preferred_element_type=F32
    ).astype(BF16)

    rank = lax.axis_index("res")
    own_is_near = lax.axis_index("seq") == lax.shift_right_logical(rank, 2)
    own = own_ref[...].reshape(residues * columns, LANES)
    other = other_ref[...].reshape(residues * columns, LANES)
    flat = outer_flat(scale, jnp.where(own_is_near, own, other), sorted_wt_ref)
    pieces = column_pieces(both_ref[0], outer_tiles(flat, residues), repeat_ref[...], residues)
    for block in range(2):
        for tile in range(2):
            keep_ref[block, tile] = pieces[block][tile]
    outer_near_ref[...] = outer_rows(flat, residues, turn_refs[0])
    flat = outer_flat(scale, jnp.where(own_is_near, other, own), sorted_wt_ref)
    outer_far_ref[...] = outer_rows(flat, residues, turn_refs[1])


def small_partner_kernel(scale, residues, got_ref, sorted_wt_ref, keep_ref, both_ref, repeat_ref,
                         leaving_ref, right_ref, swap_ref):
    rank = lax.axis_index("res")
    seqs = got_ref.shape[1]
    cot = got_ref[2:4].reshape(2 * seqs, LANES)
    outer = outer_tiles(outer_flat(scale, cot, sorted_wt_ref), residues)
    pieces = column_pieces(got_ref[0], outer, repeat_ref[...], residues)
    right_ref[0] = both_ref[1]
    right_ref[1] = got_ref[1]
    own_is_near = lax.axis_index("seq") == lax.shift_right_logical(rank, 2)
    swap_ref[0] = jnp.where(own_is_near, got_ref[1], both_ref[1])
    swap_ref[1] = both_ref[0]
    first = lane_block((seqs, LANES), residues) % 2 == 0
    for block in range(2):
        low, high = [
            (keep_ref[block, tile] + pieces[block][tile]).astype(BF16) for tile in range(2)
        ]
        chips = (
            jnp.where(first, low, pltpu.roll(high, residues, 1)),
            jnp.where(first, pltpu.roll(low, LANES - residues, 1), high),
        )
        for chip in range(2):
            leaving_ref[lax.bitwise_xor(rank & 3, 2 * block + chip), 2] = chips[chip]
    for place in range(leaving_ref.shape[0]):
        leaving_ref[place, 0] = both_ref[1]
        leaving_ref[place, 1] = got_ref[1]


def small_finish_kernel(
    scale, right_ref, part_refs, swapped_ref, swapped_late_ref, both_ref, outer_near_ref, outer_far_ref,
    own_part_ref, normed_ref, inv_std_ref, gain_ref, spread_w_ref, columns_w_ref, sorted_w_ref, offset_ref,
    grad_hbm, pair_hbm, grad_ref, pair_ref, near_ref, beyond_ref, turn_ref, lines_ref, semaphores,
):
    seqs, residues, _ = grad_ref.shape
    columns = pair_ref.shape[1]
    depth = LANES // residues
    ranks = columns // residues
    rank = lax.axis_index("res")
    mine = lax.axis_index("seq")
    here = rank & 3

    blocks_of = [right_ref] + list(part_refs)
    right_all = jnp.concatenate(
        [ref[0] for ref in blocks_of] + [ref[1] for ref in blocks_of], axis=1
    )
    spots = [
        pl.ds(pl.multiple_of(lax.bitwise_xor(here, mask) * LANES, LANES), LANES)
        for mask in range(ranks)
    ]
    outer = jnp.concatenate(
        [outer_near_ref[spot, :] for spot in spots] + [outer_far_ref[spot, :] for spot in spots],
        axis=0,
    )
    left_cot = jnp.dot(right_all, outer, preferred_element_type=F32)
    right_cot = own_part_ref[2].astype(F32)
    for part_ref in part_refs:
        right_cot = right_cot + part_ref[2].astype(F32)
    blocks = lane_block((seqs, LANES), depth)
    column = lane_block((seqs, LANES), 1) % residues
    spread = jnp.concatenate(
        [
            jnp.concatenate(
                [
                    jnp.where(blocks == place, left_cot, 0.0),
                    jnp.where(column == place, right_cot, 0.0),
                ],
                axis=1,
            )
            for place in range(residues)
        ],
        axis=0,
    )
    rows = residues * seqs
    parts = jnp.concatenate(split_two(spread), axis=0)
    weight = jnp.concatenate([spread_w_ref[0:LANES, :], columns_w_ref[...]], axis=0)
    ln_cot = jnp.dot(parts, weight, preferred_element_type=F32)
    ln_cot = ln_cot[0:rows] + ln_cot[rows : 2 * rows]
    tiles = range(lines_ref.shape[0])
    for place in range(residues):
        for tile in tiles:
            lines_ref[tile, pl.ds(place, seqs, stride=residues), :] = ln_cot[
                place * seqs : (place + 1) * seqs, tile * LANES : (tile + 1) * LANES
            ]
    gained = jnp.concatenate([lines_ref[tile, 0:rows, :] for tile in tiles], axis=1) * gain_ref[...]
    normed = normed_ref[...]
    grad = inv_std_ref[:, 0:1] * (
        gained
        - jnp.mean(gained, axis=-1, keepdims=True)
        - normed * jnp.mean(gained * normed, axis=-1, keepdims=True)
    )
    grad_ref[...] = grad.reshape(grad_ref.shape).astype(BF16)
    grad_copy = pltpu.make_async_copy(grad_ref, grad_hbm, semaphores.at[0])
    grad_copy.start()

    half = jnp.where(mine == lax.shift_right_logical(rank, 2), 0, 1)
    for mask, ref in enumerate(blocks_of):
        near_ref[mask] = ref[half]
    beyond_ref[0] = swapped_ref[0]
    beyond_ref[1] = part_refs[0][3]
    beyond_ref[2] = part_refs[1][3]
    beyond_ref[3] = swapped_late_ref[...]
    masks = [lax.bitwise_xor(here, place) for place in range(ranks)]
    right = jnp.concatenate(
        [
            jnp.concatenate([ref[mask] for mask in masks], axis=1)
            for ref in (near_ref, beyond_ref)
        ],
        axis=0,
    )
    left = jnp.concatenate([both_ref[0], swapped_ref[1]], axis=0)
    turn_ref[0 : columns * depth, :] = lax.dot_general(right, left, TN, preferred_element_type=F32) * scale
    tiles = []
    for tile in range(depth * depth // LANES):
        turned = exchange_blocks(
            [
                turn_ref[pl.ds(tile * residues + e, columns, stride=depth), :]
                for e in range(residues)
            ],
            depth,
        )
        tiles.append(jnp.concatenate(turned, axis=0))
    flat = jnp.concatenate(tiles, axis=1)
    rows = residues * columns
    parts = jnp.concatenate(split_two(flat), axis=0)
    pair = jnp.dot(parts, sorted_w_ref[...], preferred_element_type=F32)
    pair = pair[0:rows] + pair[rows : 2 * rows]
    pair_ref[...] = (pair + offset_ref[...]).astype(BF16).reshape(pair_ref.shape)
    pair_copy = pltpu.make_async_copy(pair_ref, pair_hbm, semaphores.at[1])
    pair_copy.start()
    grad_copy.wait()
    pair_copy.wait()


def small_slice(
    homolog_matrix,
    standardizer_scaling,
    standardizer_offset,
    left_projection_matrix,
    left_offset_vector,
    right_projection_matrix,
    right_offset_vector,
    coupling_matrix,
    coupling_offset,
    coupling_cotangent,
):
    seqs, residues, features = homolog_matrix.shape
    depth = left_projection_matrix.shape[1]
    ranks = lax.axis_size("res")
    rows = seqs * residues
    scale = 1.0 / (seqs * lax.axis_size("seq"))
    rank = lax.axis_index("res")
    mine = lax.axis_index("seq")
    swap = [(0, 1), (1, 0)]
    limit = pltpu.CompilerParams(vmem_limit_bytes=8 * 1024 * 1024)
    vmem = pl.BlockSpec(memory_space=pltpu.VMEM)
    like = jax.ShapeDtypeStruct

    other_cot = lax.ppermute(coupling_cotangent, "seq", swap)
    hbm = pl.BlockSpec(memory_space=pltpu.HBM)
    pin = lambda array: pltpu.with_memory_space_constraint(array, pltpu.HBM)
    both, normed, inv_std, spread_w, gain, pair_offset, own_cot = pl.pallas_call(
        small_project_kernel,
        in_specs=[hbm] * 9,
        out_specs=[vmem] * 7,
        out_shape=(
            like((2, seqs, LANES), BF16),
            like((rows, features), F32),
            like((rows, LANES), F32),
            like((2 * LANES, features), BF16),
            like((1, features), F32),
            like((1, LANES), F32),
            like(coupling_cotangent.shape, BF16),
        ),
        scratch_shapes=[
            pltpu.VMEM(homolog_matrix.shape, BF16),
            pltpu.VMEM((1, features), F32),
            pltpu.VMEM((depth, features), BF16),
            pltpu.VMEM((1, depth), F32),
            pltpu.VMEM((depth, features), BF16),
            pltpu.VMEM((1, depth), F32),
            pltpu.VMEM((2, rows + 8, LANES), F32),
            pltpu.SemaphoreType.DMA((12,)),
        ],
        compiler_params=limit,
        name="project",
    )(
        *[
            pin(array)
            for array in (
                homolog_matrix,
                standardizer_scaling.reshape(1, -1),
                standardizer_offset.reshape(1, -1),
                left_projection_matrix.T,
                left_offset_vector.reshape(1, -1),
                right_projection_matrix.T,
                right_offset_vector.reshape(1, -1),
                coupling_offset.reshape(1, -1),
                coupling_cotangent,
            )
        ]
    )

    def swap_over(mask, value):
        return lax.ppermute(value, "res", [(source, source ^ mask) for source in range(ranks)])

    own_is_near = mine == lax.shift_right_logical(rank, 2)
    far_cot = jnp.where(own_is_near, other_cot, own_cot).reshape(2, seqs, LANES)
    beyond_two = swap_over(4, jnp.concatenate([both, far_cot]))

    half_rows = ranks // 2 * LANES
    turn = pltpu.VMEM((half_rows + depth, LANES), F32)
    keep, outer_near, outer_far, sorted_w, sorted_wt, repeat, columns_w = pl.pallas_call(
        functools.partial(small_own_kernel, scale),
        in_specs=[vmem] * 5,
        out_specs=[vmem] * 7,
        out_shape=(
            like((2, 2, seqs, LANES), F32),
            like((half_rows, LANES), BF16),
            like((half_rows, LANES), BF16),
            like(coupling_matrix.shape, BF16),
            like(coupling_matrix.shape[::-1], BF16),
            like((LANES, residues * LANES), BF16),
            like((LANES, features), BF16),
        ),
        scratch_shapes=[
            [turn, turn],
            pltpu.VMEM((coupling_matrix.shape[0] + depth, LANES), F32),
        ],
        compiler_params=limit,
        name="own_pieces",
    )(own_cot, other_cot, coupling_matrix, both, spread_w)

    leaving_parts, right, leaving = pl.pallas_call(
        functools.partial(small_partner_kernel, scale, residues),
        in_specs=[vmem] * 5,
        out_specs=[vmem] * 3,
        out_shape=(
            like((ranks // 2, 3, seqs, LANES), BF16),
            like((2, seqs, LANES), BF16),
            like((2, seqs, LANES), BF16),
        ),
        compiler_params=limit,
        name="partner_pieces",
    )(beyond_two, sorted_wt, keep, both, repeat)

    swapped = lax.ppermute(leaving, "seq", swap)
    diagonal = swap_over(3, leaving_parts[3])
    across, beside = [
        swap_over(mask, jnp.concatenate([leaving_parts[mask], swapped[0:1]])) for mask in (2, 1)
    ]
    swapped_late = lax.ppermute(
        jnp.where(own_is_near, diagonal[1], diagonal[0]), "seq", swap
    )

    pair_delta, gradient = pl.pallas_call(
        functools.partial(small_finish_kernel, scale),
        in_specs=[vmem, [vmem] * 3] + [vmem] * 13,
        out_specs=[pl.BlockSpec(memory_space=pl.ANY)] * 2,
        out_shape=(
            like(homolog_matrix.shape, BF16),
            like(coupling_cotangent.shape, BF16),
        ),
        scratch_shapes=[
            pltpu.VMEM(homolog_matrix.shape, BF16),
            pltpu.VMEM(coupling_cotangent.shape, BF16),
            pltpu.VMEM((ranks // 2, seqs, LANES), BF16),
            pltpu.VMEM((ranks // 2, seqs, LANES), BF16),
            turn,
            pltpu.VMEM((features // LANES, rows + 8, LANES), F32),
            pltpu.SemaphoreType.DMA((2,)),
        ],
        compiler_params=limit,
        name="finish",
    )(
        right,
        [beside, across, diagonal],
        swapped,
        swapped_late,
        both,
        outer_near,
        outer_far,
        leaving_parts[0],
        normed,
        inv_std,
        gain,
        spread_w,
        columns_w,
        sorted_w,
        pair_offset,
    )[::-1]
    return (pair_delta, gradient)


def body(*arrays):
    if lax.axis_size("res") == 8:
        return small_slice(*arrays)
    return wide_slice(*arrays)


def solution(mesh):
    return jax.shard_map(
        body,
        mesh=mesh,
        in_specs=(
            P(("grp", "seq"), "res", None),
            P(),
            P(),
            P(),
            P(),
            P(),
            P(),
            P(),
            P(),
            P(("grp", "res"), "seq", None),
        ),
        out_specs=(P(("grp", "res"), "seq", None), P(("grp", "seq"), "res", None)),
        check_vma=False,
    )
```

```python
import functools

import jax
import jax.numpy as jnp
from jax import lax
from jax.experimental import pallas as pl
from jax.experimental.pallas import tpu as pltpu
from jax.sharding import PartitionSpec as P

LANES = 128
BF16 = jnp.bfloat16
F32 = jnp.float32
NT = (((1,), (1,)), ((), ()))
TN = (((0,), (0,)), ((), ()))


def lane_block(shape, width):
    return lax.broadcasted_iota(jnp.int32, shape, 1) // width


def pick(blocks, pieces):
    result = pieces[0]
    for place in range(1, len(pieces)):
        result = jnp.where(blocks == place, pieces[place], result)
    return result


def split_three(value):
    top = value.astype(BF16)
    rest = value - top.astype(F32)
    middle = rest.astype(BF16)
    low = (rest - middle.astype(F32)).astype(BF16)
    return top, middle, low


def exchange_blocks(pieces, width):
    first, second, third, fourth = pieces
    blocks = lane_block(first.shape, width)
    odd, high = blocks % 2 == 1, blocks >= 2
    roll = lambda value, count: pltpu.roll(value, count * width, 1)
    first, second = jnp.where(odd, roll(second, 1), first), jnp.where(odd, second, roll(first, 3))
    third, fourth = jnp.where(odd, roll(fourth, 1), third), jnp.where(odd, fourth, roll(third, 3))
    return [
        jnp.where(high, roll(third, 2), first),
        jnp.where(high, roll(fourth, 2), second),
        jnp.where(high, third, roll(first, 2)),
        jnp.where(high, fourth, roll(second, 2)),
    ]


def split_two(value):
    top = value.astype(BF16)
    return top, (value - top.astype(F32)).astype(BF16)


def normalise(rows):
    centred = rows - jnp.mean(rows, axis=-1, keepdims=True)
    inv_std = lax.rsqrt(jnp.mean(centred * centred, axis=-1, keepdims=True) + 1e-05)
    return centred * inv_std, inv_std


def residue_rows(x_ref):
    return jnp.concatenate(
        [x_ref[:, place, :].astype(F32) for place in range(x_ref.shape[1])], axis=0
    )


def project_kernel(
    x_ref, gain_ref, offset_ref, left_w_ref, left_b_ref, right_w_ref, right_b_ref, w_ref,
    left_ref, right_ref, sorted_w_ref, wide_ref,
):
    seqs, residues, _ = x_ref.shape
    depth = left_w_ref.shape[0]
    normed, _ = normalise(residue_rows(x_ref))
    ln_out = (normed * gain_ref[...] + offset_ref[...]).astype(BF16)
    blocks = lane_block((seqs, LANES), depth)
    for weight_ref, bias_ref, out_ref in (
        (left_w_ref, left_b_ref, left_ref),
        (right_w_ref, right_b_ref, right_ref),
    ):
        weight = jnp.concatenate([weight_ref[...]] * residues, axis=0)
        bias = jnp.concatenate([bias_ref[...]] * residues, axis=1)
        wide = lax.dot_general(ln_out, weight, NT, preferred_element_type=F32)
        own = pick(blocks, [wide[p * seqs : (p + 1) * seqs] for p in range(residues)])
        out_ref[...] = (own + bias).astype(BF16)
    wide_ref[...] = w_ref[...].astype(F32)
    for d in range(depth):
        sorted_w_ref[d * depth : (d + 1) * depth, :] = wide_ref[
            pl.ds(d, depth, stride=depth), :
        ].astype(BF16)


def cot_kernel(scale, own_ref, other_ref, sorted_w_ref, left_ref, right_ref,
               send_ref, outer_ref, turn_ref):
    residues, columns, _ = own_ref.shape
    depth = sorted_w_ref.shape[0] // (LANES // residues)
    depth = LANES // residues
    first = lax.axis_index("seq") == 0
    own = own_ref[...].reshape(residues * columns, LANES)
    other = other_ref[...].reshape(residues * columns, LANES)
    low = jnp.where(first, own, other)
    high = jnp.where(first, other, own)
    both = jnp.concatenate([low, high], axis=0)
    flat = lax.dot_general(both, sorted_w_ref[...], NT, preferred_element_type=F32) * scale
    blocks = lane_block((columns, LANES), depth)
    for half in range(2):
        for tile in range(depth * depth // LANES):
            block = flat[
                half * residues * columns : (half + 1) * residues * columns,
                tile * LANES : (tile + 1) * LANES,
            ]
            turned = [block] + [pltpu.roll(block, depth * t, 1) for t in range(1, residues)]
            for e in range(residues):
                piece = pick(
                    blocks,
                    [
                        turned[(i - e) % residues][i * columns : (i + 1) * columns]
                        for i in range(residues)
                    ],
                )
                turn_ref[pl.ds(half * columns * depth + tile * residues + e, columns, stride=depth), :] = piece
    outer = turn_ref[...].astype(BF16)
    half_rows = columns * depth
    partial = lax.dot_general(left_ref[...], outer, NT, preferred_element_type=F32).astype(BF16)
    seqs = left_ref.shape[0]
    ranks = columns // residues
    for half in range(2):
        outer_ref[half] = outer[half * half_rows : (half + 1) * half_rows]
        for rank in range(ranks):
            at = (half * ranks + rank) * LANES
            send_ref[half, rank, 0:seqs, :] = right_ref[...]
            send_ref[half, rank, seqs : 2 * seqs, :] = partial[:, at : at + LANES]


def grad_kernel(steps, got_ref, outer_ref, x_ref, gain_ref, left_w_ref, right_w_ref,
                grad_ref, left_cot_ref, right_cot_ref):
    step = pl.program_id(0)
    _, ranks, twice, _ = got_ref.shape
    seqs = twice // 2
    residues = x_ref.shape[1]
    depth = LANES // residues

    @pl.when(step == 0)
    def _():
        left_cot_ref[...] = jnp.zeros_like(left_cot_ref)
        right_cot_ref[...] = jnp.zeros_like(right_cot_ref)

    places = [(half, rank) for half in range(2) for rank in range(ranks)]
    right_all = jnp.concatenate([got_ref[h, r, 0:seqs, :] for h, r in places], axis=1)
    outer = jnp.concatenate([outer_ref[0], outer_ref[1]], axis=0)
    left_cot_ref[...] += jnp.dot(right_all, outer, preferred_element_type=F32)
    total = got_ref[0, 0, seqs:twice, :].astype(F32)
    for h, r in places[1:]:
        total = total + got_ref[h, r, seqs:twice, :].astype(F32)
    right_cot_ref[...] += total

    @pl.when(step == steps - 1)
    def _():
        blocks = lane_block((seqs, LANES), depth)
        left_cot, right_cot = left_cot_ref[...], right_cot_ref[...]
        spread = jnp.concatenate(
            [
                jnp.concatenate(
                    [
                        jnp.where(blocks == place, left_cot, 0.0),
                        jnp.where(blocks == place, right_cot, 0.0),
                    ],
                    axis=1,
                )
                for place in range(residues)
            ],
            axis=0,
        )
        weight = jnp.concatenate(
            [left_w_ref[...]] * residues + [right_w_ref[...]] * residues, axis=0
        )
        rows = residues * seqs
        parts = jnp.concatenate(split_three(spread), axis=0)
        ln_cot = jnp.dot(parts, weight, preferred_element_type=F32)
        ln_cot = ln_cot[0:rows] + (ln_cot[rows : 2 * rows] + ln_cot[2 * rows : 3 * rows])
        gained = ln_cot * gain_ref[...]
        normed, inv_std = normalise(residue_rows(x_ref))
        grad = inv_std * (
            gained
            - jnp.mean(gained, axis=-1, keepdims=True)
            - normed * jnp.mean(gained * normed, axis=-1, keepdims=True)
        )
        for place in range(residues):
            grad_ref[:, place, :] = grad[place * seqs : (place + 1) * seqs].astype(BF16)


def pair_kernel(scale, got_ref, far_ref, left_ref, far_left_ref, sorted_w_ref, offset_ref,
                pair_ref, turn_ref):
    residues, columns, _ = pair_ref.shape
    depth = LANES // residues
    ranks = columns // residues
    mine = lax.axis_index("seq")
    near = jnp.concatenate([got_ref[mine, r] for r in range(ranks)], axis=1)
    far = jnp.concatenate([far_ref[r] for r in range(ranks)], axis=1)
    right = jnp.concatenate([near, far], axis=0)
    left = jnp.concatenate([left_ref[...], far_left_ref[...]], axis=0)
    turn_ref[...] = lax.dot_general(right, left, TN, preferred_element_type=F32) * scale
    blocks = lane_block((columns, LANES), depth)
    tiles = []
    for tile in range(depth * depth // LANES):
        pieces = [
            turn_ref[pl.ds(tile * residues + e, columns, stride=depth), :]
            for e in range(residues)
        ]
        rows = jnp.concatenate(pieces, axis=0)
        turned = [rows] + [pltpu.roll(rows, depth * t, 1) for t in range(1, residues)]
        tiles.append(
            jnp.concatenate(
                [
                    pick(
                        blocks,
                        [
                            turned[(e - i) % residues][e * columns : (e + 1) * columns]
                            for e in range(residues)
                        ],
                    )
                    for i in range(residues)
                ],
                axis=0,
            )
        )
    flat = jnp.concatenate(tiles, axis=1)
    rows = residues * columns
    parts = jnp.concatenate(split_three(flat), axis=0)
    pair = jnp.dot(parts, sorted_w_ref[...], preferred_element_type=F32)
    pair = pair[0:rows] + (pair[rows : 2 * rows] + pair[2 * rows : 3 * rows])
    pair_ref[...] = (pair + offset_ref[...]).astype(BF16).reshape(pair_ref.shape)


def wide_slice(
    homolog_matrix,
    standardizer_scaling,
    standardizer_offset,
    left_projection_matrix,
    left_offset_vector,
    right_projection_matrix,
    right_offset_vector,
    coupling_matrix,
    coupling_offset,
    coupling_cotangent,
):
    seqs, residues, features = homolog_matrix.shape
    depth = left_projection_matrix.shape[1]
    ranks = lax.axis_size("res")
    scale = 1.0 / (seqs * lax.axis_size("seq"))
    half_ranks = ranks // 2
    half_columns = half_ranks * residues
    step_ranks = 4
    columns = step_ranks * residues
    steps = half_ranks // step_ranks
    mine = lax.axis_index("seq")
    swap = [(0, 1), (1, 0)]

    other_cot = lax.ppermute(coupling_cotangent, "seq", swap)
    gain = standardizer_scaling.reshape(1, -1)
    left_w = left_projection_matrix.T
    right_w = right_projection_matrix.T

    left, right, sorted_w = pl.pallas_call(
        project_kernel,
        out_shape=(
            jax.ShapeDtypeStruct((seqs, LANES), BF16),
            jax.ShapeDtypeStruct((seqs, LANES), BF16),
            jax.ShapeDtypeStruct(coupling_matrix.shape, BF16),
        ),
        scratch_shapes=[pltpu.VMEM(coupling_matrix.shape, F32)],
        name="project",
    )(
        homolog_matrix,
        gain,
        standardizer_offset.reshape(1, -1),
        left_w,
        left_offset_vector.reshape(1, -1),
        right_w,
        right_offset_vector.reshape(1, -1),
        coupling_matrix,
    )

    whole = lambda shape: pl.BlockSpec(shape, lambda g: (0,) * len(shape))
    cot_block = pl.BlockSpec((residues, columns, LANES), lambda g: (0, g, 0))
    outer_block = pl.BlockSpec((2, columns * depth, LANES), lambda g: (0, g, 0))
    send_block = pl.BlockSpec((2, step_ranks, 2 * seqs, LANES), lambda g: (0, g, 0, 0))
    send, outer = pl.pallas_call(
        functools.partial(cot_kernel, scale),
        grid=(steps,),
        in_specs=[
            cot_block,
            cot_block,
            whole(sorted_w.shape),
            whole(left.shape),
            whole(right.shape),
        ],
        out_specs=(send_block, outer_block),
        out_shape=(
            jax.ShapeDtypeStruct((2, half_ranks, 2 * seqs, LANES), BF16),
            jax.ShapeDtypeStruct((2, half_columns * depth, LANES), BF16),
        ),
        scratch_shapes=[pltpu.VMEM((2 * columns * depth, LANES), F32)],
        name="cotangent",
    )(coupling_cotangent, other_cot, sorted_w, left, right)

    got = lax.all_to_all(
        send.reshape(ranks, 2 * seqs, LANES), "res", split_axis=0, concat_axis=0, tiled=True
    ).reshape(send.shape)

    leaving = lax.dynamic_index_in_dim(got, 1 - mine, 0, keepdims=False)[:, 0:seqs, :]
    far = lax.ppermute(jnp.concatenate([leaving, left[None]], axis=0), "seq", swap)

    gradient = pl.pallas_call(
        functools.partial(grad_kernel, steps),
        grid=(steps,),
        in_specs=[
            send_block,
            outer_block,
            whole(homolog_matrix.shape),
            whole(gain.shape),
            whole(left_w.shape),
            whole(right_w.shape),
        ],
        out_specs=whole(homolog_matrix.shape),
        out_shape=jax.ShapeDtypeStruct(homolog_matrix.shape, BF16),
        scratch_shapes=[pltpu.VMEM((seqs, LANES), F32)] * 2,
        name="gradient",
    )(got, outer, homolog_matrix, gain, left_w, right_w)

    pair_delta = pl.pallas_call(
        functools.partial(pair_kernel, scale),
        grid=(steps,),
        in_specs=[
            pl.BlockSpec((2, step_ranks, seqs, LANES), lambda g: (0, g, 0, 0)),
            pl.BlockSpec((step_ranks, seqs, LANES), lambda g: (g, 0, 0)),
            whole(left.shape),
            pl.BlockSpec((None, seqs, LANES), lambda g: (half_ranks, 0, 0)),
            whole(sorted_w.shape),
            whole((1, LANES)),
        ],
        out_specs=cot_block,
        out_shape=jax.ShapeDtypeStruct(coupling_cotangent.shape, BF16),
        scratch_shapes=[pltpu.VMEM((columns * depth, LANES), F32)],
        name="pair",
    )(got, far, left, far, sorted_w, coupling_offset.reshape(1, -1))
    return (pair_delta, gradient)


def fetch(source, target, semaphore):
    copy = pltpu.make_async_copy(source, target, semaphore)
    copy.start()
    return copy


def start_copies(pairs, semaphores):
    copies = [
        pltpu.make_async_copy(source, target, semaphores.at[place])
        for place, (source, target) in enumerate(pairs)
    ]
    for copy in copies:
        copy.start()
    return copies


def small_project_kernel(
    x_hbm, gain_hbm, offset_hbm, left_w_hbm, left_b_hbm, right_w_hbm, right_b_hbm, pair_offset_hbm,
    cot_hbm, both_ref, normed_ref, inv_std_ref, spread_w_ref, gain_ref, pair_offset_ref, cot_ref,
    x_ref, offset_ref, left_w_ref, left_b_ref, right_w_ref, right_b_ref, wide_ref, semaphores,
):
    seqs, residues, _ = x_ref.shape
    depth = left_w_ref.shape[0]
    parts = 4
    part = seqs // parts
    copies = start_copies(
        tuple(
            (x_hbm.at[pl.ds(place * part, part)], x_ref.at[pl.ds(place * part, part)])
            for place in range(parts)
        )
        + (
            (left_w_hbm, left_w_ref),
            (right_w_hbm, right_w_ref),
            (gain_hbm, gain_ref),
            (offset_hbm, offset_ref),
            (left_b_hbm, left_b_ref),
            (right_b_hbm, right_b_ref),
            (cot_hbm, cot_ref),
            (pair_offset_hbm, pair_offset_ref),
        ),
        semaphores,
    )
    for copy in copies[:parts]:
        copy.wait()
    rows = x_ref[...].astype(F32).reshape(seqs * residues, x_ref.shape[2])
    normed, inv_std = normalise(rows)
    for copy in copies[parts:]:
        copy.wait()
    ln_out = (normed * gain_ref[...] + offset_ref[...]).astype(BF16)
    blocks = lane_block((seqs, LANES), depth)
    weight = jnp.concatenate(
        [left_w_ref[...]] * residues + [right_w_ref[...]] * residues, axis=0
    )
    wide = lax.dot_general(ln_out, weight, NT, preferred_element_type=F32)
    for place, bias_ref in enumerate((left_b_ref, right_b_ref)):
        bias = jnp.concatenate([bias_ref[...]] * residues, axis=1)
        wide_ref[place, 0 : seqs * residues, :] = wide[:, place * LANES : (place + 1) * LANES]
        own = pick(
            blocks, [wide_ref[place, pl.ds(p, seqs, stride=residues), :] for p in range(residues)]
        )
        both_ref[place] = (own + bias).astype(BF16)
    normed_ref[...] = normed
    inv_std_ref[...] = jnp.broadcast_to(inv_std, inv_std_ref.shape)
    spread_w_ref[...] = weight


def outer_flat(cot, sorted_wt_ref):
    return jnp.dot(cot, sorted_wt_ref[...], preferred_element_type=F32)


def outer_rows(flat, residues, turn_ref):
    columns = flat.shape[0] // residues
    depth = LANES // residues
    for tile in range(depth * depth // LANES):
        block = flat[:, tile * LANES : (tile + 1) * LANES]
        turned = exchange_blocks(
            [block[i * columns : (i + 1) * columns] for i in range(residues)], depth
        )
        for e in range(residues):
            turn_ref[pl.ds(tile * residues + e, columns, stride=depth), :] = turned[e]
    return turn_ref[0 : columns * depth, :].astype(BF16)


def outer_tiles(flat, residues):
    columns = flat.shape[0] // residues
    return jnp.concatenate(
        [
            jnp.concatenate(
                [
                    flat[i * columns + start : i * columns + start + 8, tile : tile + LANES]
                    for start in range(0, columns, 8)
                    for tile in range(0, flat.shape[1], LANES)
                ],
                axis=0,
            )
            for i in range(residues)
        ],
        axis=1,
    ).astype(BF16)


def blocks_apart(left, residues):
    depth = LANES // residues
    left = left.astype(F32)
    turned = [left] + [pltpu.roll(left, depth * t, 1) for t in range(1, residues)]
    blocks = lane_block(left.shape, depth)
    return jnp.concatenate(
        [
            jnp.concatenate(
                [
                    jnp.where(blocks == e, turned[(e - i) % residues], 0.0).astype(BF16)
                    for i in range(residues)
                ],
                axis=1,
            )
            for e in range(residues)
        ],
        axis=0,
    )


def column_pieces(left, outer, residues):
    seqs = left.shape[0]
    partial = lax.dot_general(
        blocks_apart(left, residues), outer, NT, preferred_element_type=F32
    )
    rows = [partial[e * seqs : (e + 1) * seqs] for e in range(residues)]
    turned = [pltpu.roll(row, LANES // 2, 1) for row in rows]
    low = lane_block(rows[0].shape, LANES // 2) == 0
    first = lane_block(rows[0].shape, residues) % 2 == 0
    pieces = []
    for block in (
        [jnp.where(low, rows[e], turned[e + 1]) for e in (0, 2)],
        [jnp.where(low, turned[e], rows[e + 1]) for e in (0, 2)],
    ):
        pieces.append(jnp.where(first, block[0], pltpu.roll(block[1], residues, 1)))
        pieces.append(jnp.where(first, pltpu.roll(block[0], LANES - residues, 1), block[1]))
    return pieces


def small_own_kernel(scale, own_ref, other_ref, w_ref, both_ref, spread_w_ref,
                     keep_ref, outer_near_ref, outer_far_ref, sorted_w_ref, sorted_wt_ref,
                     columns_w_ref, turn_refs, wide_ref):
    residues, columns, _ = own_ref.shape
    depth = LANES // residues
    wide_ref[0 : w_ref.shape[0], :] = w_ref[...].astype(F32)
    for d in range(depth):
        sorted_w_ref[d * depth : (d + 1) * depth, :] = wide_ref[
            pl.ds(d, depth, stride=depth), :
        ].astype(BF16)
    sorted_wt_ref[...] = (sorted_w_ref[...].astype(F32) * scale).astype(BF16).T
    shape = (columns_w_ref.shape[0], depth)
    row = lax.broadcasted_iota(jnp.int32, shape, 0)
    lane = lax.broadcasted_iota(jnp.int32, shape, 1)
    place = (row >> 3 & 7) * residues + 2 * (row >> 2 & 1) + (row >> 6)
    chosen = jnp.where(lane == place, 1.0, 0.0).astype(BF16)
    columns_w_ref[...] = jnp.dot(
        chosen, spread_w_ref[LANES : LANES + depth, :], preferred_element_type=F32
    ).astype(BF16)

    rank = lax.axis_index("res")
    own_is_near = lax.axis_index("seq") == lax.shift_right_logical(rank, 2)
    own = own_ref[...].reshape(residues * columns, LANES)
    other = other_ref[...].reshape(residues * columns, LANES)
    flat = outer_flat(jnp.where(own_is_near, own, other), sorted_wt_ref)
    pieces = column_pieces(both_ref[0], outer_tiles(flat, residues), residues)
    for place, piece in enumerate(pieces):
        keep_ref[place] = piece
    outer_near_ref[...] = outer_rows(flat, residues, turn_refs[0])
    flat = outer_flat(jnp.where(own_is_near, other, own), sorted_wt_ref)
    outer_far_ref[...] = outer_rows(flat, residues, turn_refs[1])


def small_partner_kernel(residues, got_ref, sorted_wt_ref, keep_ref, both_ref,
                         leaving_ref, keep_out_ref, right_ref, swap_ref):
    rank = lax.axis_index("res")
    seqs = got_ref.shape[1]
    cot = got_ref[2:4].reshape(2 * seqs, LANES)
    outer = outer_tiles(outer_flat(cot, sorted_wt_ref), residues)
    pieces = column_pieces(got_ref[0], outer, residues)
    right_ref[0] = both_ref[1]
    right_ref[1] = got_ref[1]
    own_is_near = lax.axis_index("seq") == lax.shift_right_logical(rank, 2)
    swap_ref[0] = jnp.where(own_is_near, got_ref[1], both_ref[1])
    swap_ref[1] = both_ref[0]
    for place, piece in enumerate(pieces):
        distance = lax.bitwise_xor(rank & 3, place)
        total = keep_ref[place] + piece
        keep_out_ref[distance] = total
        leaving_ref[distance, 2] = total.astype(BF16)
    for place in range(leaving_ref.shape[0]):
        leaving_ref[place, 0] = both_ref[1]
        leaving_ref[place, 1] = got_ref[1]


def small_finish_kernel(
    scale, right_ref, part_refs, swapped_ref, swapped_late_ref, both_ref, outer_near_ref, outer_far_ref,
    keep_ref, normed_ref, inv_std_ref, gain_ref, spread_w_ref, columns_w_ref, sorted_w_ref, offset_ref,
    grad_hbm, pair_hbm, grad_ref, pair_ref, near_ref, beyond_ref, turn_ref, lines_ref, semaphores,
):
    seqs, residues, _ = grad_ref.shape
    columns = pair_ref.shape[1]
    depth = LANES // residues
    ranks = columns // residues
    rank = lax.axis_index("res")
    mine = lax.axis_index("seq")
    here = rank & 3

    blocks_of = [right_ref] + list(part_refs)
    right_all = jnp.concatenate(
        [ref[0] for ref in blocks_of] + [ref[1] for ref in blocks_of], axis=1
    )
    spots = [
        pl.ds(pl.multiple_of(lax.bitwise_xor(here, mask) * LANES, LANES), LANES)
        for mask in range(ranks)
    ]
    outer = jnp.concatenate(
        [outer_near_ref[spot, :] for spot in spots] + [outer_far_ref[spot, :] for spot in spots],
        axis=0,
    )
    left_cot = jnp.dot(right_all, outer, preferred_element_type=F32)
    right_cot = keep_ref[0]
    for part_ref in part_refs:
        right_cot = right_cot + part_ref[2].astype(F32)
    blocks = lane_block((seqs, LANES), depth)
    column = lane_block((seqs, LANES), 1) % residues
    spread = jnp.concatenate(
        [
            jnp.concatenate(
                [
                    jnp.where(blocks == place, left_cot, 0.0),
                    jnp.where(column == place, right_cot, 0.0),
                ],
                axis=1,
            )
            for place in range(residues)
        ],
        axis=0,
    )
    rows = residues * seqs
    parts = jnp.concatenate(split_two(spread), axis=0)
    weight = jnp.concatenate([spread_w_ref[0:LANES, :], columns_w_ref[...]], axis=0)
    ln_cot = jnp.dot(parts, weight, preferred_element_type=F32)
    ln_cot = ln_cot[0:rows] + ln_cot[rows : 2 * rows]
    tiles = range(lines_ref.shape[0])
    for place in range(residues):
        for tile in tiles:
            lines_ref[tile, pl.ds(place, seqs, stride=residues), :] = ln_cot[
                place * seqs : (place + 1) * seqs, tile * LANES : (tile + 1) * LANES
            ]
    gained = jnp.concatenate([lines_ref[tile, 0:rows, :] for tile in tiles], axis=1) * gain_ref[...]
    normed = normed_ref[...]
    grad = inv_std_ref[:, 0:1] * (
        gained
        - jnp.mean(gained, axis=-1, keepdims=True)
        - normed * jnp.mean(gained * normed, axis=-1, keepdims=True)
    )
    grad_ref[...] = grad.reshape(grad_ref.shape).astype(BF16)
    grad_copy = pltpu.make_async_copy(grad_ref, grad_hbm, semaphores.at[0])
    grad_copy.start()

    half = jnp.where(mine == lax.shift_right_logical(rank, 2), 0, 1)
    for mask, ref in enumerate(blocks_of):
        near_ref[mask] = ref[half]
    beyond_ref[0] = swapped_ref[0]
    beyond_ref[1] = part_refs[0][3]
    beyond_ref[2] = part_refs[1][3]
    beyond_ref[3] = swapped_late_ref[...]
    masks = [lax.bitwise_xor(here, place) for place in range(ranks)]
    right = jnp.concatenate(
        [
            jnp.concatenate([ref[mask] for mask in masks], axis=1)
            for ref in (near_ref, beyond_ref)
        ],
        axis=0,
    )
    left = jnp.concatenate([both_ref[0], swapped_ref[1]], axis=0)
    turn_ref[0 : columns * depth, :] = lax.dot_general(right, left, TN, preferred_element_type=F32) * scale
    tiles = []
    for tile in range(depth * depth // LANES):
        turned = exchange_blocks(
            [
                turn_ref[pl.ds(tile * residues + e, columns, stride=depth), :]
                for e in range(residues)
            ],
            depth,
        )
        tiles.append(jnp.concatenate(turned, axis=0))
    flat = jnp.concatenate(tiles, axis=1)
    rows = residues * columns
    parts = jnp.concatenate(split_two(flat), axis=0)
    pair = jnp.dot(parts, sorted_w_ref[...], preferred_element_type=F32)
    pair = pair[0:rows] + pair[rows : 2 * rows]
    pair_ref[...] = (pair + offset_ref[...]).astype(BF16).reshape(pair_ref.shape)
    pair_copy = pltpu.make_async_copy(pair_ref, pair_hbm, semaphores.at[1])
    pair_copy.start()
    grad_copy.wait()
    pair_copy.wait()


def small_slice(
    homolog_matrix,
    standardizer_scaling,
    standardizer_offset,
    left_projection_matrix,
    left_offset_vector,
    right_projection_matrix,
    right_offset_vector,
    coupling_matrix,
    coupling_offset,
    coupling_cotangent,
):
    seqs, residues, features = homolog_matrix.shape
    depth = left_projection_matrix.shape[1]
    ranks = lax.axis_size("res")
    rows = seqs * residues
    scale = 1.0 / (seqs * lax.axis_size("seq"))
    rank = lax.axis_index("res")
    mine = lax.axis_index("seq")
    swap = [(0, 1), (1, 0)]
    limit = pltpu.CompilerParams(vmem_limit_bytes=8 * 1024 * 1024)
    vmem = pl.BlockSpec(memory_space=pltpu.VMEM)
    like = jax.ShapeDtypeStruct

    other_cot = lax.ppermute(coupling_cotangent, "seq", swap)
    hbm = pl.BlockSpec(memory_space=pltpu.HBM)
    pin = lambda array: pltpu.with_memory_space_constraint(array, pltpu.HBM)
    both, normed, inv_std, spread_w, gain, pair_offset, own_cot = pl.pallas_call(
        small_project_kernel,
        in_specs=[hbm] * 9,
        out_specs=[vmem] * 7,
        out_shape=(
            like((2, seqs, LANES), BF16),
            like((rows, features), F32),
            like((rows, LANES), F32),
            like((2 * LANES, features), BF16),
            like((1, features), F32),
            like((1, LANES), F32),
            like(coupling_cotangent.shape, BF16),
        ),
        scratch_shapes=[
            pltpu.VMEM(homolog_matrix.shape, BF16),
            pltpu.VMEM((1, features), F32),
            pltpu.VMEM((depth, features), BF16),
            pltpu.VMEM((1, depth), F32),
            pltpu.VMEM((depth, features), BF16),
            pltpu.VMEM((1, depth), F32),
            pltpu.VMEM((2, rows + 8, LANES), F32),
            pltpu.SemaphoreType.DMA((12,)),
        ],
        compiler_params=limit,
        name="project",
    )(
        *[
            pin(array)
            for array in (
                homolog_matrix,
                standardizer_scaling.reshape(1, -1),
                standardizer_offset.reshape(1, -1),
                left_projection_matrix.T,
                left_offset_vector.reshape(1, -1),
                right_projection_matrix.T,
                right_offset_vector.reshape(1, -1),
                coupling_offset.reshape(1, -1),
                coupling_cotangent,
            )
        ]
    )

    def swap_over(mask, value):
        return lax.ppermute(value, "res", [(source, source ^ mask) for source in range(ranks)])

    own_is_near = mine == lax.shift_right_logical(rank, 2)
    far_cot = jnp.where(own_is_near, other_cot, own_cot).reshape(2, seqs, LANES)
    beyond_two = swap_over(4, jnp.concatenate([both, far_cot]))

    half_rows = ranks // 2 * LANES
    turn = pltpu.VMEM((half_rows + depth, LANES), F32)
    keep, outer_near, outer_far, sorted_w, sorted_wt, columns_w = pl.pallas_call(
        functools.partial(small_own_kernel, scale),
        in_specs=[vmem] * 5,
        out_specs=[vmem] * 6,
        out_shape=(
            like((ranks // 2, seqs, LANES), F32),
            like((half_rows, LANES), BF16),
            like((half_rows, LANES), BF16),
            like(coupling_matrix.shape, BF16),
            like(coupling_matrix.shape[::-1], BF16),
            like((LANES, features), BF16),
        ),
        scratch_shapes=[
            [turn, turn],
            pltpu.VMEM((coupling_matrix.shape[0] + depth, LANES), F32),
        ],
        compiler_params=limit,
        name="own_pieces",
    )(own_cot, other_cot, coupling_matrix, both, spread_w)

    leaving_parts, keep, right, leaving = pl.pallas_call(
        functools.partial(small_partner_kernel, residues),
        in_specs=[vmem] * 4,
        out_specs=[vmem] * 4,
        out_shape=(
            like((ranks // 2, 3, seqs, LANES), BF16),
            like((ranks // 2, seqs, LANES), F32),
            like((2, seqs, LANES), BF16),
            like((2, seqs, LANES), BF16),
        ),
        compiler_params=limit,
        name="partner_pieces",
    )(beyond_two, sorted_wt, keep, both)

    swapped = lax.ppermute(leaving, "seq", swap)
    diagonal = swap_over(3, leaving_parts[3])
    across, beside = [
        swap_over(mask, jnp.concatenate([leaving_parts[mask], swapped[0:1]])) for mask in (2, 1)
    ]
    swapped_late = lax.ppermute(
        jnp.where(own_is_near, diagonal[1], diagonal[0]), "seq", swap
    )

    pair_delta, gradient = pl.pallas_call(
        functools.partial(small_finish_kernel, scale),
        in_specs=[vmem, [vmem] * 3] + [vmem] * 13,
        out_specs=[pl.BlockSpec(memory_space=pl.ANY)] * 2,
        out_shape=(
            like(homolog_matrix.shape, BF16),
            like(coupling_cotangent.shape, BF16),
        ),
        scratch_shapes=[
            pltpu.VMEM(homolog_matrix.shape, BF16),
            pltpu.VMEM(coupling_cotangent.shape, BF16),
            pltpu.VMEM((ranks // 2, seqs, LANES), BF16),
            pltpu.VMEM((ranks // 2, seqs, LANES), BF16),
            turn,
            pltpu.VMEM((features // LANES, rows + 8, LANES), F32),
            pltpu.SemaphoreType.DMA((2,)),
        ],
        compiler_params=limit,
        name="finish",
    )(
        right,
        [beside, across, diagonal],
        swapped,
        swapped_late,
        both,
        outer_near,
        outer_far,
        keep,
        normed,
        inv_std,
        gain,
        spread_w,
        columns_w,
        sorted_w,
        pair_offset,
    )[::-1]
    return (pair_delta, gradient)


def body(*arrays):
    sequences = arrays[0].shape[0] * lax.axis_size("seq")
    if lax.axis_size("res") == 8 and sequences & (sequences - 1) == 0:
        return small_slice(*arrays)
    return wide_slice(*arrays)


def solution(mesh):
    return jax.shard_map(
        body,
        mesh=mesh,
        in_specs=(
            P(("grp", "seq"), "res", None),
            P(),
            P(),
            P(),
            P(),
            P(),
            P(),
            P(),
            P(),
            P(("grp", "res"), "seq", None),
        ),
        out_specs=(P(("grp", "res"), "seq", None), P(("grp", "seq"), "res", None)),
        check_vma=False,
    )
```

```python
import functools

import jax
import jax.numpy as jnp
from jax import lax
from jax.experimental import pallas as pl
from jax.experimental.pallas import tpu as pltpu
from jax.sharding import PartitionSpec as P

LANES = 128
BF16 = jnp.bfloat16
F32 = jnp.float32
NT = (((1,), (1,)), ((), ()))
TN = (((0,), (0,)), ((), ()))


def lane_block(shape, width):
    return lax.broadcasted_iota(jnp.int32, shape, 1) // width


def pick(blocks, pieces):
    result = pieces[0]
    for place in range(1, len(pieces)):
        result = jnp.where(blocks == place, pieces[place], result)
    return result


def split_three(value):
    top = value.astype(BF16)
    rest = value - top.astype(F32)
    middle = rest.astype(BF16)
    low = (rest - middle.astype(F32)).astype(BF16)
    return top, middle, low


def exchange_blocks(pieces, width):
    first, second, third, fourth = pieces
    blocks = lane_block(first.shape, width)
    odd, high = blocks % 2 == 1, blocks >= 2
    roll = lambda value, count: pltpu.roll(value, count * width, 1)
    first, second = jnp.where(odd, roll(second, 1), first), jnp.where(odd, second, roll(first, 3))
    third, fourth = jnp.where(odd, roll(fourth, 1), third), jnp.where(odd, fourth, roll(third, 3))
    return [
        jnp.where(high, roll(third, 2), first),
        jnp.where(high, roll(fourth, 2), second),
        jnp.where(high, third, roll(first, 2)),
        jnp.where(high, fourth, roll(second, 2)),
    ]


def split_two(value):
    top = value.astype(BF16)
    return top, (value - top.astype(F32)).astype(BF16)


def normalise(rows):
    centred = rows - jnp.mean(rows, axis=-1, keepdims=True)
    inv_std = lax.rsqrt(jnp.mean(centred * centred, axis=-1, keepdims=True) + 1e-05)
    return centred * inv_std, inv_std


def residue_rows(x_ref):
    return jnp.concatenate(
        [x_ref[:, place, :].astype(F32) for place in range(x_ref.shape[1])], axis=0
    )


def project_kernel(
    x_ref, gain_ref, offset_ref, left_w_ref, left_b_ref, right_w_ref, right_b_ref, w_ref,
    left_ref, right_ref, sorted_w_ref, wide_ref,
):
    seqs, residues, _ = x_ref.shape
    depth = left_w_ref.shape[0]
    normed, _ = normalise(residue_rows(x_ref))
    ln_out = (normed * gain_ref[...] + offset_ref[...]).astype(BF16)
    blocks = lane_block((seqs, LANES), depth)
    for weight_ref, bias_ref, out_ref in (
        (left_w_ref, left_b_ref, left_ref),
        (right_w_ref, right_b_ref, right_ref),
    ):
        weight = jnp.concatenate([weight_ref[...]] * residues, axis=0)
        bias = jnp.concatenate([bias_ref[...]] * residues, axis=1)
        wide = lax.dot_general(ln_out, weight, NT, preferred_element_type=F32)
        own = pick(blocks, [wide[p * seqs : (p + 1) * seqs] for p in range(residues)])
        out_ref[...] = (own + bias).astype(BF16)
    wide_ref[...] = w_ref[...].astype(F32)
    for d in range(depth):
        sorted_w_ref[d * depth : (d + 1) * depth, :] = wide_ref[
            pl.ds(d, depth, stride=depth), :
        ].astype(BF16)


def cot_kernel(scale, own_ref, other_ref, sorted_w_ref, left_ref, right_ref,
               send_ref, outer_ref, turn_ref):
    residues, columns, _ = own_ref.shape
    depth = sorted_w_ref.shape[0] // (LANES // residues)
    depth = LANES // residues
    first = lax.axis_index("seq") == 0
    own = own_ref[...].reshape(residues * columns, LANES)
    other = other_ref[...].reshape(residues * columns, LANES)
    low = jnp.where(first, own, other)
    high = jnp.where(first, other, own)
    both = jnp.concatenate([low, high], axis=0)
    flat = lax.dot_general(both, sorted_w_ref[...], NT, preferred_element_type=F32) * scale
    blocks = lane_block((columns, LANES), depth)
    for half in range(2):
        for tile in range(depth * depth // LANES):
            block = flat[
                half * residues * columns : (half + 1) * residues * columns,
                tile * LANES : (tile + 1) * LANES,
            ]
            turned = [block] + [pltpu.roll(block, depth * t, 1) for t in range(1, residues)]
            for e in range(residues):
                piece = pick(
                    blocks,
                    [
                        turned[(i - e) % residues][i * columns : (i + 1) * columns]
                        for i in range(residues)
                    ],
                )
                turn_ref[pl.ds(half * columns * depth + tile * residues + e, columns, stride=depth), :] = piece
    outer = turn_ref[...].astype(BF16)
    half_rows = columns * depth
    partial = lax.dot_general(left_ref[...], outer, NT, preferred_element_type=F32).astype(BF16)
    seqs = left_ref.shape[0]
    ranks = columns // residues
    for half in range(2):
        outer_ref[half] = outer[half * half_rows : (half + 1) * half_rows]
        for rank in range(ranks):
            at = (half * ranks + rank) * LANES
            send_ref[half, rank, 0:seqs, :] = right_ref[...]
            send_ref[half, rank, seqs : 2 * seqs, :] = partial[:, at : at + LANES]


def grad_kernel(steps, got_ref, outer_ref, x_ref, gain_ref, left_w_ref, right_w_ref,
                grad_ref, left_cot_ref, right_cot_ref):
    step = pl.program_id(0)
    _, ranks, twice, _ = got_ref.shape
    seqs = twice // 2
    residues = x_ref.shape[1]
    depth = LANES // residues

    @pl.when(step == 0)
    def _():
        left_cot_ref[...] = jnp.zeros_like(left_cot_ref)
        right_cot_ref[...] = jnp.zeros_like(right_cot_ref)

    places = [(half, rank) for half in range(2) for rank in range(ranks)]
    right_all = jnp.concatenate([got_ref[h, r, 0:seqs, :] for h, r in places], axis=1)
    outer = jnp.concatenate([outer_ref[0], outer_ref[1]], axis=0)
    left_cot_ref[...] += jnp.dot(right_all, outer, preferred_element_type=F32)
    total = got_ref[0, 0, seqs:twice, :].astype(F32)
    for h, r in places[1:]:
        total = total + got_ref[h, r, seqs:twice, :].astype(F32)
    right_cot_ref[...] += total

    @pl.when(step == steps - 1)
    def _():
        blocks = lane_block((seqs, LANES), depth)
        left_cot, right_cot = left_cot_ref[...], right_cot_ref[...]
        spread = jnp.concatenate(
            [
                jnp.concatenate(
                    [
                        jnp.where(blocks == place, left_cot, 0.0),
                        jnp.where(blocks == place, right_cot, 0.0),
                    ],
                    axis=1,
                )
                for place in range(residues)
            ],
            axis=0,
        )
        weight = jnp.concatenate(
            [left_w_ref[...]] * residues + [right_w_ref[...]] * residues, axis=0
        )
        rows = residues * seqs
        parts = jnp.concatenate(split_three(spread), axis=0)
        ln_cot = jnp.dot(parts, weight, preferred_element_type=F32)
        ln_cot = ln_cot[0:rows] + (ln_cot[rows : 2 * rows] + ln_cot[2 * rows : 3 * rows])
        gained = ln_cot * gain_ref[...]
        normed, inv_std = normalise(residue_rows(x_ref))
        grad = inv_std * (
            gained
            - jnp.mean(gained, axis=-1, keepdims=True)
            - normed * jnp.mean(gained * normed, axis=-1, keepdims=True)
        )
        for place in range(residues):
            grad_ref[:, place, :] = grad[place * seqs : (place + 1) * seqs].astype(BF16)


def pair_kernel(scale, got_ref, far_ref, left_ref, far_left_ref, sorted_w_ref, offset_ref,
                pair_ref, turn_ref):
    residues, columns, _ = pair_ref.shape
    depth = LANES // residues
    ranks = columns // residues
    mine = lax.axis_index("seq")
    near = jnp.concatenate([got_ref[mine, r] for r in range(ranks)], axis=1)
    far = jnp.concatenate([far_ref[r] for r in range(ranks)], axis=1)
    right = jnp.concatenate([near, far], axis=0)
    left = jnp.concatenate([left_ref[...], far_left_ref[...]], axis=0)
    turn_ref[...] = lax.dot_general(right, left, TN, preferred_element_type=F32) * scale
    blocks = lane_block((columns, LANES), depth)
    tiles = []
    for tile in range(depth * depth // LANES):
        pieces = [
            turn_ref[pl.ds(tile * residues + e, columns, stride=depth), :]
            for e in range(residues)
        ]
        rows = jnp.concatenate(pieces, axis=0)
        turned = [rows] + [pltpu.roll(rows, depth * t, 1) for t in range(1, residues)]
        tiles.append(
            jnp.concatenate(
                [
                    pick(
                        blocks,
                        [
                            turned[(e - i) % residues][e * columns : (e + 1) * columns]
                            for e in range(residues)
                        ],
                    )
                    for i in range(residues)
                ],
                axis=0,
            )
        )
    flat = jnp.concatenate(tiles, axis=1)
    rows = residues * columns
    parts = jnp.concatenate(split_three(flat), axis=0)
    pair = jnp.dot(parts, sorted_w_ref[...], preferred_element_type=F32)
    pair = pair[0:rows] + (pair[rows : 2 * rows] + pair[2 * rows : 3 * rows])
    pair_ref[...] = (pair + offset_ref[...]).astype(BF16).reshape(pair_ref.shape)


def wide_slice(
    homolog_matrix,
    standardizer_scaling,
    standardizer_offset,
    left_projection_matrix,
    left_offset_vector,
    right_projection_matrix,
    right_offset_vector,
    coupling_matrix,
    coupling_offset,
    coupling_cotangent,
):
    seqs, residues, features = homolog_matrix.shape
    depth = left_projection_matrix.shape[1]
    ranks = lax.axis_size("res")
    scale = 1.0 / (seqs * lax.axis_size("seq"))
    half_ranks = ranks // 2
    half_columns = half_ranks * residues
    step_ranks = 4
    columns = step_ranks * residues
    steps = half_ranks // step_ranks
    mine = lax.axis_index("seq")
    swap = [(0, 1), (1, 0)]

    other_cot = lax.ppermute(coupling_cotangent, "seq", swap)
    gain = standardizer_scaling.reshape(1, -1)
    left_w = left_projection_matrix.T
    right_w = right_projection_matrix.T

    left, right, sorted_w = pl.pallas_call(
        project_kernel,
        out_shape=(
            jax.ShapeDtypeStruct((seqs, LANES), BF16),
            jax.ShapeDtypeStruct((seqs, LANES), BF16),
            jax.ShapeDtypeStruct(coupling_matrix.shape, BF16),
        ),
        scratch_shapes=[pltpu.VMEM(coupling_matrix.shape, F32)],
        name="project",
    )(
        homolog_matrix,
        gain,
        standardizer_offset.reshape(1, -1),
        left_w,
        left_offset_vector.reshape(1, -1),
        right_w,
        right_offset_vector.reshape(1, -1),
        coupling_matrix,
    )

    whole = lambda shape: pl.BlockSpec(shape, lambda g: (0,) * len(shape))
    cot_block = pl.BlockSpec((residues, columns, LANES), lambda g: (0, g, 0))
    outer_block = pl.BlockSpec((2, columns * depth, LANES), lambda g: (0, g, 0))
    send_block = pl.BlockSpec((2, step_ranks, 2 * seqs, LANES), lambda g: (0, g, 0, 0))
    send, outer = pl.pallas_call(
        functools.partial(cot_kernel, scale),
        grid=(steps,),
        in_specs=[
            cot_block,
            cot_block,
            whole(sorted_w.shape),
            whole(left.shape),
            whole(right.shape),
        ],
        out_specs=(send_block, outer_block),
        out_shape=(
            jax.ShapeDtypeStruct((2, half_ranks, 2 * seqs, LANES), BF16),
            jax.ShapeDtypeStruct((2, half_columns * depth, LANES), BF16),
        ),
        scratch_shapes=[pltpu.VMEM((2 * columns * depth, LANES), F32)],
        name="cotangent",
    )(coupling_cotangent, other_cot, sorted_w, left, right)

    got = lax.all_to_all(
        send.reshape(ranks, 2 * seqs, LANES), "res", split_axis=0, concat_axis=0, tiled=True
    ).reshape(send.shape)

    leaving = lax.dynamic_index_in_dim(got, 1 - mine, 0, keepdims=False)[:, 0:seqs, :]
    far = lax.ppermute(jnp.concatenate([leaving, left[None]], axis=0), "seq", swap)

    gradient = pl.pallas_call(
        functools.partial(grad_kernel, steps),
        grid=(steps,),
        in_specs=[
            send_block,
            outer_block,
            whole(homolog_matrix.shape),
            whole(gain.shape),
            whole(left_w.shape),
            whole(right_w.shape),
        ],
        out_specs=whole(homolog_matrix.shape),
        out_shape=jax.ShapeDtypeStruct(homolog_matrix.shape, BF16),
        scratch_shapes=[pltpu.VMEM((seqs, LANES), F32)] * 2,
        name="gradient",
    )(got, outer, homolog_matrix, gain, left_w, right_w)

    pair_delta = pl.pallas_call(
        functools.partial(pair_kernel, scale),
        grid=(steps,),
        in_specs=[
            pl.BlockSpec((2, step_ranks, seqs, LANES), lambda g: (0, g, 0, 0)),
            pl.BlockSpec((step_ranks, seqs, LANES), lambda g: (g, 0, 0)),
            whole(left.shape),
            pl.BlockSpec((None, seqs, LANES), lambda g: (half_ranks, 0, 0)),
            whole(sorted_w.shape),
            whole((1, LANES)),
        ],
        out_specs=cot_block,
        out_shape=jax.ShapeDtypeStruct(coupling_cotangent.shape, BF16),
        scratch_shapes=[pltpu.VMEM((columns * depth, LANES), F32)],
        name="pair",
    )(got, far, left, far, sorted_w, coupling_offset.reshape(1, -1))
    return (pair_delta, gradient)


def fetch(source, target, semaphore):
    copy = pltpu.make_async_copy(source, target, semaphore)
    copy.start()
    return copy


def start_copies(pairs, semaphores):
    copies = [
        pltpu.make_async_copy(source, target, semaphores.at[place])
        for place, (source, target) in enumerate(pairs)
    ]
    for copy in copies:
        copy.start()
    return copies


def small_project_kernel(
    x_hbm, gain_hbm, offset_hbm, left_w_hbm, left_b_hbm, right_w_hbm, right_b_hbm, pair_offset_hbm,
    cot_hbm, both_ref, normed_ref, inv_std_ref, spread_w_ref, gain_ref, pair_offset_ref, cot_ref,
    x_ref, offset_ref, left_w_ref, left_b_ref, right_w_ref, right_b_ref, wide_ref, semaphores,
):
    seqs, residues, _ = x_ref.shape
    depth = left_w_ref.shape[0]
    parts = 4
    part = seqs // parts
    copies = start_copies(
        tuple(
            (x_hbm.at[pl.ds(place * part, part)], x_ref.at[pl.ds(place * part, part)])
            for place in range(parts)
        )
        + (
            (left_w_hbm, left_w_ref),
            (right_w_hbm, right_w_ref),
            (gain_hbm, gain_ref),
            (offset_hbm, offset_ref),
            (left_b_hbm, left_b_ref),
            (right_b_hbm, right_b_ref),
            (cot_hbm, cot_ref),
            (pair_offset_hbm, pair_offset_ref),
        ),
        semaphores,
    )
    for copy in copies[:parts]:
        copy.wait()
    rows = x_ref[...].astype(F32).reshape(seqs * residues, x_ref.shape[2])
    normed, inv_std = normalise(rows)
    for copy in copies[parts:]:
        copy.wait()
    ln_out = (normed * gain_ref[...] + offset_ref[...]).astype(BF16)
    blocks = lane_block((seqs, LANES), depth)
    weight = jnp.concatenate(
        [left_w_ref[...]] * residues + [right_w_ref[...]] * residues, axis=0
    )
    wide = lax.dot_general(ln_out, weight, NT, preferred_element_type=F32)
    for place, bias_ref in enumerate((left_b_ref, right_b_ref)):
        bias = jnp.concatenate([bias_ref[...]] * residues, axis=1)
        wide_ref[place, 0 : seqs * residues, :] = wide[:, place * LANES : (place + 1) * LANES]
        own = pick(
            blocks, [wide_ref[place, pl.ds(p, seqs, stride=residues), :] for p in range(residues)]
        )
        both_ref[place] = (own + bias).astype(BF16)
    normed_ref[...] = normed
    inv_std_ref[...] = jnp.broadcast_to(inv_std, inv_std_ref.shape)
    spread_w_ref[...] = weight


def outer_flat(cot, sorted_wt_ref):
    return jnp.dot(cot, sorted_wt_ref[...], preferred_element_type=F32)


def outer_rows(flat, residues, turn_ref):
    columns = flat.shape[0] // residues
    depth = LANES // residues
    for tile in range(depth * depth // LANES):
        block = flat[:, tile * LANES : (tile + 1) * LANES]
        turned = exchange_blocks(
            [block[i * columns : (i + 1) * columns] for i in range(residues)], depth
        )
        for e in range(residues):
            turn_ref[pl.ds(tile * residues + e, columns, stride=depth), :] = turned[e]
    return turn_ref[0 : columns * depth, :].astype(BF16)


def outer_tiles(flat, residues):
    columns = flat.shape[0] // residues
    return jnp.concatenate(
        [
            jnp.concatenate(
                [
                    flat[i * columns + start : i * columns + start + 8, tile : tile + LANES]
                    for start in range(0, columns, 8)
                    for tile in range(0, flat.shape[1], LANES)
                ],
                axis=0,
            )
            for i in range(residues)
        ],
        axis=1,
    ).astype(BF16)


def blocks_apart(left, residues):
    depth = LANES // residues
    left = left.astype(F32)
    turned = [left] + [pltpu.roll(left, depth * t, 1) for t in range(1, residues)]
    blocks = lane_block(left.shape, depth)
    return jnp.concatenate(
        [
            jnp.concatenate(
                [
                    jnp.where(blocks == e, turned[(e - i) % residues], 0.0).astype(BF16)
                    for i in range(residues)
                ],
                axis=1,
            )
            for e in range(residues)
        ],
        axis=0,
    )


def column_pieces(left, outer, residues):
    seqs = left.shape[0]
    partial = lax.dot_general(
        blocks_apart(left, residues), outer, NT, preferred_element_type=F32
    )
    rows = [partial[e * seqs : (e + 1) * seqs] for e in range(residues)]
    half = lane_block(rows[0].shape, LANES // 2)
    source = 2 * (lane_block(rows[0].shape, residues) % 2) + half
    pieces = []
    for chip in range(residues):
        turned = []
        for e, row in enumerate(rows):
            count = (LANES // 2 * (e % 2 - chip // 2) + residues * (e // 2 - chip % 2)) % LANES
            turned.append(pltpu.roll(row, count, 1) if count else row)
        pieces.append(pick(source, turned))
    return pieces


def small_own_kernel(scale, own_ref, other_ref, w_ref, both_ref, spread_w_ref,
                     keep_ref, outer_near_ref, outer_far_ref, sorted_w_ref, sorted_wt_ref,
                     columns_w_ref, turn_refs, wide_ref):
    residues, columns, _ = own_ref.shape
    depth = LANES // residues
    wide_ref[0 : w_ref.shape[0], :] = w_ref[...].astype(F32)
    for d in range(depth):
        sorted_w_ref[d * depth : (d + 1) * depth, :] = wide_ref[
            pl.ds(d, depth, stride=depth), :
        ].astype(BF16)
    sorted_wt_ref[...] = (sorted_w_ref[...].astype(F32) * scale).astype(BF16).T
    shape = (columns_w_ref.shape[0], depth)
    row = lax.broadcasted_iota(jnp.int32, shape, 0)
    lane = lax.broadcasted_iota(jnp.int32, shape, 1)
    place = (row >> 3 & 7) * residues + 2 * (row >> 2 & 1) + (row >> 6)
    chosen = jnp.where(lane == place, 1.0, 0.0).astype(BF16)
    columns_w_ref[...] = jnp.dot(
        chosen, spread_w_ref[LANES : LANES + depth, :], preferred_element_type=F32
    ).astype(BF16)

    rank = lax.axis_index("res")
    own_is_near = lax.axis_index("seq") == lax.shift_right_logical(rank, 2)
    own = own_ref[...].reshape(residues * columns, LANES)
    other = other_ref[...].reshape(residues * columns, LANES)
    flat = outer_flat(jnp.where(own_is_near, own, other), sorted_wt_ref)
    pieces = column_pieces(both_ref[0], outer_tiles(flat, residues), residues)
    for place, piece in enumerate(pieces):
        keep_ref[place] = piece
    outer_near_ref[...] = outer_rows(flat, residues, turn_refs[0])
    flat = outer_flat(jnp.where(own_is_near, other, own), sorted_wt_ref)
    outer_far_ref[...] = outer_rows(flat, residues, turn_refs[1])


def small_partner_kernel(residues, got_ref, sorted_wt_ref, keep_ref, both_ref,
                         leaving_ref, keep_out_ref, right_ref, swap_ref):
    rank = lax.axis_index("res")
    seqs = got_ref.shape[1]
    cot = got_ref[2:4].reshape(2 * seqs, LANES)
    outer = outer_tiles(outer_flat(cot, sorted_wt_ref), residues)
    pieces = column_pieces(got_ref[0], outer, residues)
    right_ref[0] = both_ref[1]
    right_ref[1] = got_ref[1]
    own_is_near = lax.axis_index("seq") == lax.shift_right_logical(rank, 2)
    swap_ref[0] = jnp.where(own_is_near, got_ref[1], both_ref[1])
    swap_ref[1] = both_ref[0]
    for place, piece in enumerate(pieces):
        distance = lax.bitwise_xor(rank & 3, place)
        total = keep_ref[place] + piece
        keep_out_ref[distance] = total
        leaving_ref[distance, 2] = total.astype(BF16)
    for place in range(leaving_ref.shape[0]):
        leaving_ref[place, 0] = both_ref[1]
        leaving_ref[place, 1] = got_ref[1]


def small_finish_kernel(
    scale, right_ref, part_refs, swapped_ref, swapped_late_ref, both_ref, outer_near_ref, outer_far_ref,
    keep_ref, normed_ref, inv_std_ref, gain_ref, spread_w_ref, columns_w_ref, sorted_w_ref, offset_ref,
    grad_hbm, pair_hbm, grad_ref, pair_ref, near_ref, beyond_ref, turn_ref, lines_ref, semaphores,
):
    seqs, residues, _ = grad_ref.shape
    columns = pair_ref.shape[1]
    depth = LANES // residues
    ranks = columns // residues
    rank = lax.axis_index("res")
    mine = lax.axis_index("seq")
    here = rank & 3

    blocks_of = [right_ref] + list(part_refs)
    right_all = jnp.concatenate(
        [ref[0] for ref in blocks_of] + [ref[1] for ref in blocks_of], axis=1
    )
    spots = [
        pl.ds(pl.multiple_of(lax.bitwise_xor(here, mask) * LANES, LANES), LANES)
        for mask in range(ranks)
    ]
    outer = jnp.concatenate(
        [outer_near_ref[spot, :] for spot in spots] + [outer_far_ref[spot, :] for spot in spots],
        axis=0,
    )
    left_cot = jnp.dot(right_all, outer, preferred_element_type=F32)
    right_cot = keep_ref[0]
    for part_ref in part_refs:
        right_cot = right_cot + part_ref[2].astype(F32)
    blocks = lane_block((seqs, LANES), depth)
    column = lane_block((seqs, LANES), 1) % residues
    spread = jnp.concatenate(
        [
            jnp.concatenate(
                [
                    jnp.where(blocks == place, left_cot, 0.0),
                    jnp.where(column == place, right_cot, 0.0),
                ],
                axis=1,
            )
            for place in range(residues)
        ],
        axis=0,
    )
    rows = residues * seqs
    parts = jnp.concatenate(split_two(spread), axis=0)
    weight = jnp.concatenate([spread_w_ref[0:LANES, :], columns_w_ref[...]], axis=0)
    ln_cot = jnp.dot(parts, weight, preferred_element_type=F32)
    ln_cot = ln_cot[0:rows] + ln_cot[rows : 2 * rows]
    tiles = range(lines_ref.shape[0])
    for place in range(residues):
        for tile in tiles:
            lines_ref[tile, pl.ds(place, seqs, stride=residues), :] = ln_cot[
                place * seqs : (place + 1) * seqs, tile * LANES : (tile + 1) * LANES
            ]
    gained = jnp.concatenate([lines_ref[tile, 0:rows, :] for tile in tiles], axis=1) * gain_ref[...]
    normed = normed_ref[...]
    grad = inv_std_ref[:, 0:1] * (
        gained
        - jnp.mean(gained, axis=-1, keepdims=True)
        - normed * jnp.mean(gained * normed, axis=-1, keepdims=True)
    )
    grad_ref[...] = grad.reshape(grad_ref.shape).astype(BF16)
    grad_copy = pltpu.make_async_copy(grad_ref, grad_hbm, semaphores.at[0])
    grad_copy.start()

    half = jnp.where(mine == lax.shift_right_logical(rank, 2), 0, 1)
    for mask, ref in enumerate(blocks_of):
        near_ref[mask] = ref[half]
    beyond_ref[0] = swapped_ref[0]
    beyond_ref[1] = part_refs[0][3]
    beyond_ref[2] = part_refs[1][3]
    beyond_ref[3] = swapped_late_ref[...]
    masks = [lax.bitwise_xor(here, place) for place in range(ranks)]
    right = jnp.concatenate(
        [
            jnp.concatenate([ref[mask] for mask in masks], axis=1)
            for ref in (near_ref, beyond_ref)
        ],
        axis=0,
    )
    left = jnp.concatenate([both_ref[0], swapped_ref[1]], axis=0)
    turn_ref[0 : columns * depth, :] = lax.dot_general(right, left, TN, preferred_element_type=F32) * scale
    tiles = []
    for tile in range(depth * depth // LANES):
        turned = exchange_blocks(
            [
                turn_ref[pl.ds(tile * residues + e, columns, stride=depth), :]
                for e in range(residues)
            ],
            depth,
        )
        tiles.append(jnp.concatenate(turned, axis=0))
    flat = jnp.concatenate(tiles, axis=1)
    rows = residues * columns
    parts = jnp.concatenate(split_two(flat), axis=0)
    pair = jnp.dot(parts, sorted_w_ref[...], preferred_element_type=F32)
    pair = pair[0:rows] + pair[rows : 2 * rows]
    pair_ref[...] = (pair + offset_ref[...]).astype(BF16).reshape(pair_ref.shape)
    pair_copy = pltpu.make_async_copy(pair_ref, pair_hbm, semaphores.at[1])
    pair_copy.start()
    grad_copy.wait()
    pair_copy.wait()


def small_slice(
    homolog_matrix,
    standardizer_scaling,
    standardizer_offset,
    left_projection_matrix,
    left_offset_vector,
    right_projection_matrix,
    right_offset_vector,
    coupling_matrix,
    coupling_offset,
    coupling_cotangent,
):
    seqs, residues, features = homolog_matrix.shape
    depth = left_projection_matrix.shape[1]
    ranks = lax.axis_size("res")
    rows = seqs * residues
    scale = 1.0 / (seqs * lax.axis_size("seq"))
    rank = lax.axis_index("res")
    mine = lax.axis_index("seq")
    swap = [(0, 1), (1, 0)]
    limit = pltpu.CompilerParams(vmem_limit_bytes=8 * 1024 * 1024)
    vmem = pl.BlockSpec(memory_space=pltpu.VMEM)
    like = jax.ShapeDtypeStruct

    other_cot = lax.ppermute(coupling_cotangent, "seq", swap)
    hbm = pl.BlockSpec(memory_space=pltpu.HBM)
    pin = lambda array: pltpu.with_memory_space_constraint(array, pltpu.HBM)
    both, normed, inv_std, spread_w, gain, pair_offset, own_cot = pl.pallas_call(
        small_project_kernel,
        in_specs=[hbm] * 9,
        out_specs=[vmem] * 7,
        out_shape=(
            like((2, seqs, LANES), BF16),
            like((rows, features), F32),
            like((rows, LANES), F32),
            like((2 * LANES, features), BF16),
            like((1, features), F32),
            like((1, LANES), F32),
            like(coupling_cotangent.shape, BF16),
        ),
        scratch_shapes=[
            pltpu.VMEM(homolog_matrix.shape, BF16),
            pltpu.VMEM((1, features), F32),
            pltpu.VMEM((depth, features), BF16),
            pltpu.VMEM((1, depth), F32),
            pltpu.VMEM((depth, features), BF16),
            pltpu.VMEM((1, depth), F32),
            pltpu.VMEM((2, rows + 8, LANES), F32),
            pltpu.SemaphoreType.DMA((12,)),
        ],
        compiler_params=limit,
        name="project",
    )(
        *[
            pin(array)
            for array in (
                homolog_matrix,
                standardizer_scaling.reshape(1, -1),
                standardizer_offset.reshape(1, -1),
                left_projection_matrix.T,
                left_offset_vector.reshape(1, -1),
                right_projection_matrix.T,
                right_offset_vector.reshape(1, -1),
                coupling_offset.reshape(1, -1),
                coupling_cotangent,
            )
        ]
    )

    def swap_over(mask, value):
        return lax.ppermute(value, "res", [(source, source ^ mask) for source in range(ranks)])

    own_is_near = mine == lax.shift_right_logical(rank, 2)
    far_cot = jnp.where(own_is_near, other_cot, own_cot).reshape(2, seqs, LANES)
    beyond_two = swap_over(4, jnp.concatenate([both, far_cot]))

    half_rows = ranks // 2 * LANES
    turn = pltpu.VMEM((half_rows + depth, LANES), F32)
    keep, outer_near, outer_far, sorted_w, sorted_wt, columns_w = pl.pallas_call(
        functools.partial(small_own_kernel, scale),
        in_specs=[vmem] * 5,
        out_specs=[vmem] * 6,
        out_shape=(
            like((ranks // 2, seqs, LANES), F32),
            like((half_rows, LANES), BF16),
            like((half_rows, LANES), BF16),
            like(coupling_matrix.shape, BF16),
            like(coupling_matrix.shape[::-1], BF16),
            like((LANES, features), BF16),
        ),
        scratch_shapes=[
            [turn, turn],
            pltpu.VMEM((coupling_matrix.shape[0] + depth, LANES), F32),
        ],
        compiler_params=limit,
        name="own_pieces",
    )(own_cot, other_cot, coupling_matrix, both, spread_w)

    leaving_parts, keep, right, leaving = pl.pallas_call(
        functools.partial(small_partner_kernel, residues),
        in_specs=[vmem] * 4,
        out_specs=[vmem] * 4,
        out_shape=(
            like((ranks // 2, 3, seqs, LANES), BF16),
            like((ranks // 2, seqs, LANES), F32),
            like((2, seqs, LANES), BF16),
            like((2, seqs, LANES), BF16),
        ),
        compiler_params=limit,
        name="partner_pieces",
    )(beyond_two, sorted_wt, keep, both)

    swapped = lax.ppermute(leaving, "seq", swap)
    diagonal = swap_over(3, leaving_parts[3])
    across, beside = [
        swap_over(mask, jnp.concatenate([leaving_parts[mask], swapped[0:1]])) for mask in (2, 1)
    ]
    swapped_late = lax.ppermute(
        jnp.where(own_is_near, diagonal[1], diagonal[0]), "seq", swap
    )

    pair_delta, gradient = pl.pallas_call(
        functools.partial(small_finish_kernel, scale),
        in_specs=[vmem, [vmem] * 3] + [vmem] * 13,
        out_specs=[pl.BlockSpec(memory_space=pl.ANY)] * 2,
        out_shape=(
            like(homolog_matrix.shape, BF16),
            like(coupling_cotangent.shape, BF16),
        ),
        scratch_shapes=[
            pltpu.VMEM(homolog_matrix.shape, BF16),
            pltpu.VMEM(coupling_cotangent.shape, BF16),
            pltpu.VMEM((ranks // 2, seqs, LANES), BF16),
            pltpu.VMEM((ranks // 2, seqs, LANES), BF16),
            turn,
            pltpu.VMEM((features // LANES, rows + 8, LANES), F32),
            pltpu.SemaphoreType.DMA((2,)),
        ],
        compiler_params=limit,
        name="finish",
    )(
        right,
        [beside, across, diagonal],
        swapped,
        swapped_late,
        both,
        outer_near,
        outer_far,
        keep,
        normed,
        inv_std,
        gain,
        spread_w,
        columns_w,
        sorted_w,
        pair_offset,
    )[::-1]
    return (pair_delta, gradient)


def body(*arrays):
    sequences = arrays[0].shape[0] * lax.axis_size("seq")
    if lax.axis_size("res") == 8 and sequences & (sequences - 1) == 0:
        return small_slice(*arrays)
    return wide_slice(*arrays)


def solution(mesh):
    return jax.shard_map(
        body,
        mesh=mesh,
        in_specs=(
            P(("grp", "seq"), "res", None),
            P(),
            P(),
            P(),
            P(),
            P(),
            P(),
            P(),
            P(),
            P(("grp", "res"), "seq", None),
        ),
        out_specs=(P(("grp", "res"), "seq", None), P(("grp", "seq"), "res", None)),
        check_vma=False,
    )
```

```python
import functools

import jax
import jax.numpy as jnp
from jax import lax
from jax.experimental import pallas as pl
from jax.experimental.pallas import tpu as pltpu
from jax.sharding import PartitionSpec as P

LANES = 128
BF16 = jnp.bfloat16
F32 = jnp.float32
NT = (((1,), (1,)), ((), ()))
TN = (((0,), (0,)), ((), ()))


def lane_block(shape, width):
    return lax.broadcasted_iota(jnp.int32, shape, 1) // width


def pick(blocks, pieces):
    result = pieces[0]
    for place in range(1, len(pieces)):
        result = jnp.where(blocks == place, pieces[place], result)
    return result


def split_three(value):
    top = value.astype(BF16)
    rest = value - top.astype(F32)
    middle = rest.astype(BF16)
    low = (rest - middle.astype(F32)).astype(BF16)
    return top, middle, low


def exchange_blocks(pieces, width):
    count = len(pieces)
    blocks = lane_block(pieces[0].shape, width)
    return [
        pick(
            blocks,
            [
                pltpu.roll(piece, width * ((e - i) % count), 1) if e != i else piece
                for e, piece in enumerate(pieces)
            ],
        )
        for i in range(count)
    ]


def split_two(value):
    top = value.astype(BF16)
    return top, (value - top.astype(F32)).astype(BF16)


def normalise(rows):
    centred = rows - jnp.mean(rows, axis=-1, keepdims=True)
    inv_std = lax.rsqrt(jnp.mean(centred * centred, axis=-1, keepdims=True) + 1e-05)
    return centred * inv_std, inv_std


def residue_rows(x_ref):
    return jnp.concatenate(
        [x_ref[:, place, :].astype(F32) for place in range(x_ref.shape[1])], axis=0
    )


def project_kernel(
    x_ref, gain_ref, offset_ref, left_w_ref, left_b_ref, right_w_ref, right_b_ref, w_ref,
    left_ref, right_ref, sorted_w_ref, wide_ref,
):
    seqs, residues, _ = x_ref.shape
    depth = left_w_ref.shape[0]
    normed, _ = normalise(residue_rows(x_ref))
    ln_out = (normed * gain_ref[...] + offset_ref[...]).astype(BF16)
    blocks = lane_block((seqs, LANES), depth)
    for weight_ref, bias_ref, out_ref in (
        (left_w_ref, left_b_ref, left_ref),
        (right_w_ref, right_b_ref, right_ref),
    ):
        weight = jnp.concatenate([weight_ref[...]] * residues, axis=0)
        bias = jnp.concatenate([bias_ref[...]] * residues, axis=1)
        wide = lax.dot_general(ln_out, weight, NT, preferred_element_type=F32)
        own = pick(blocks, [wide[p * seqs : (p + 1) * seqs] for p in range(residues)])
        out_ref[...] = (own + bias).astype(BF16)
    wide_ref[...] = w_ref[...].astype(F32)
    for d in range(depth):
        sorted_w_ref[d * depth : (d + 1) * depth, :] = wide_ref[
            pl.ds(d, depth, stride=depth), :
        ].astype(BF16)


def cot_kernel(scale, own_ref, other_ref, sorted_w_ref, left_ref, right_ref,
               send_ref, outer_ref, turn_ref):
    residues, columns, _ = own_ref.shape
    depth = sorted_w_ref.shape[0] // (LANES // residues)
    depth = LANES // residues
    first = lax.axis_index("seq") == 0
    own = own_ref[...].reshape(residues * columns, LANES)
    other = other_ref[...].reshape(residues * columns, LANES)
    low = jnp.where(first, own, other)
    high = jnp.where(first, other, own)
    both = jnp.concatenate([low, high], axis=0)
    flat = lax.dot_general(both, sorted_w_ref[...], NT, preferred_element_type=F32) * scale
    blocks = lane_block((columns, LANES), depth)
    for half in range(2):
        for tile in range(depth * depth // LANES):
            block = flat[
                half * residues * columns : (half + 1) * residues * columns,
                tile * LANES : (tile + 1) * LANES,
            ]
            turned = [block] + [pltpu.roll(block, depth * t, 1) for t in range(1, residues)]
            for e in range(residues):
                piece = pick(
                    blocks,
                    [
                        turned[(i - e) % residues][i * columns : (i + 1) * columns]
                        for i in range(residues)
                    ],
                )
                turn_ref[pl.ds(half * columns * depth + tile * residues + e, columns, stride=depth), :] = piece
    outer = turn_ref[...].astype(BF16)
    half_rows = columns * depth
    partial = lax.dot_general(left_ref[...], outer, NT, preferred_element_type=F32).astype(BF16)
    seqs = left_ref.shape[0]
    ranks = columns // residues
    for half in range(2):
        outer_ref[half] = outer[half * half_rows : (half + 1) * half_rows]
        for rank in range(ranks):
            at = (half * ranks + rank) * LANES
            send_ref[half, rank, 0:seqs, :] = right_ref[...]
            send_ref[half, rank, seqs : 2 * seqs, :] = partial[:, at : at + LANES]


def grad_kernel(steps, got_ref, outer_ref, x_ref, gain_ref, left_w_ref, right_w_ref,
                grad_ref, left_cot_ref, right_cot_ref):
    step = pl.program_id(0)
    _, ranks, twice, _ = got_ref.shape
    seqs = twice // 2
    residues = x_ref.shape[1]
    depth = LANES // residues

    @pl.when(step == 0)
    def _():
        left_cot_ref[...] = jnp.zeros_like(left_cot_ref)
        right_cot_ref[...] = jnp.zeros_like(right_cot_ref)

    places = [(half, rank) for half in range(2) for rank in range(ranks)]
    right_all = jnp.concatenate([got_ref[h, r, 0:seqs, :] for h, r in places], axis=1)
    outer = jnp.concatenate([outer_ref[0], outer_ref[1]], axis=0)
    left_cot_ref[...] += jnp.dot(right_all, outer, preferred_element_type=F32)
    total = got_ref[0, 0, seqs:twice, :].astype(F32)
    for h, r in places[1:]:
        total = total + got_ref[h, r, seqs:twice, :].astype(F32)
    right_cot_ref[...] += total

    @pl.when(step == steps - 1)
    def _():
        blocks = lane_block((seqs, LANES), depth)
        left_cot, right_cot = left_cot_ref[...], right_cot_ref[...]
        spread = jnp.concatenate(
            [
                jnp.concatenate(
                    [
                        jnp.where(blocks == place, left_cot, 0.0),
                        jnp.where(blocks == place, right_cot, 0.0),
                    ],
                    axis=1,
                )
                for place in range(residues)
            ],
            axis=0,
        )
        weight = jnp.concatenate(
            [left_w_ref[...]] * residues + [right_w_ref[...]] * residues, axis=0
        )
        rows = residues * seqs
        parts = jnp.concatenate(split_three(spread), axis=0)
        ln_cot = jnp.dot(parts, weight, preferred_element_type=F32)
        ln_cot = ln_cot[0:rows] + (ln_cot[rows : 2 * rows] + ln_cot[2 * rows : 3 * rows])
        gained = ln_cot * gain_ref[...]
        normed, inv_std = normalise(residue_rows(x_ref))
        grad = inv_std * (
            gained
            - jnp.mean(gained, axis=-1, keepdims=True)
            - normed * jnp.mean(gained * normed, axis=-1, keepdims=True)
        )
        for place in range(residues):
            grad_ref[:, place, :] = grad[place * seqs : (place + 1) * seqs].astype(BF16)


def pair_kernel(scale, got_ref, far_ref, left_ref, far_left_ref, sorted_w_ref, offset_ref,
                pair_ref, turn_ref):
    residues, columns, _ = pair_ref.shape
    depth = LANES // residues
    ranks = columns // residues
    mine = lax.axis_index("seq")
    near = jnp.concatenate([got_ref[mine, r] for r in range(ranks)], axis=1)
    far = jnp.concatenate([far_ref[r] for r in range(ranks)], axis=1)
    right = jnp.concatenate([near, far], axis=0)
    left = jnp.concatenate([left_ref[...], far_left_ref[...]], axis=0)
    turn_ref[...] = lax.dot_general(right, left, TN, preferred_element_type=F32) * scale
    blocks = lane_block((columns, LANES), depth)
    tiles = []
    for tile in range(depth * depth // LANES):
        pieces = [
            turn_ref[pl.ds(tile * residues + e, columns, stride=depth), :]
            for e in range(residues)
        ]
        rows = jnp.concatenate(pieces, axis=0)
        turned = [rows] + [pltpu.roll(rows, depth * t, 1) for t in range(1, residues)]
        tiles.append(
            jnp.concatenate(
                [
                    pick(
                        blocks,
                        [
                            turned[(e - i) % residues][e * columns : (e + 1) * columns]
                            for e in range(residues)
                        ],
                    )
                    for i in range(residues)
                ],
                axis=0,
            )
        )
    flat = jnp.concatenate(tiles, axis=1)
    rows = residues * columns
    parts = jnp.concatenate(split_three(flat), axis=0)
    pair = jnp.dot(parts, sorted_w_ref[...], preferred_element_type=F32)
    pair = pair[0:rows] + (pair[rows : 2 * rows] + pair[2 * rows : 3 * rows])
    pair_ref[...] = (pair + offset_ref[...]).astype(BF16).reshape(pair_ref.shape)


def wide_slice(
    homolog_matrix,
    standardizer_scaling,
    standardizer_offset,
    left_projection_matrix,
    left_offset_vector,
    right_projection_matrix,
    right_offset_vector,
    coupling_matrix,
    coupling_offset,
    coupling_cotangent,
):
    seqs, residues, features = homolog_matrix.shape
    depth = left_projection_matrix.shape[1]
    ranks = lax.axis_size("res")
    scale = 1.0 / (seqs * lax.axis_size("seq"))
    half_ranks = ranks // 2
    half_columns = half_ranks * residues
    step_ranks = 4
    columns = step_ranks * residues
    steps = half_ranks // step_ranks
    mine = lax.axis_index("seq")
    swap = [(0, 1), (1, 0)]

    other_cot = lax.ppermute(coupling_cotangent, "seq", swap)
    gain = standardizer_scaling.reshape(1, -1)
    left_w = left_projection_matrix.T
    right_w = right_projection_matrix.T

    left, right, sorted_w = pl.pallas_call(
        project_kernel,
        out_shape=(
            jax.ShapeDtypeStruct((seqs, LANES), BF16),
            jax.ShapeDtypeStruct((seqs, LANES), BF16),
            jax.ShapeDtypeStruct(coupling_matrix.shape, BF16),
        ),
        scratch_shapes=[pltpu.VMEM(coupling_matrix.shape, F32)],
        name="project",
    )(
        homolog_matrix,
        gain,
        standardizer_offset.reshape(1, -1),
        left_w,
        left_offset_vector.reshape(1, -1),
        right_w,
        right_offset_vector.reshape(1, -1),
        coupling_matrix,
    )

    whole = lambda shape: pl.BlockSpec(shape, lambda g: (0,) * len(shape))
    cot_block = pl.BlockSpec((residues, columns, LANES), lambda g: (0, g, 0))
    outer_block = pl.BlockSpec((2, columns * depth, LANES), lambda g: (0, g, 0))
    send_block = pl.BlockSpec((2, step_ranks, 2 * seqs, LANES), lambda g: (0, g, 0, 0))
    send, outer = pl.pallas_call(
        functools.partial(cot_kernel, scale),
        grid=(steps,),
        in_specs=[
            cot_block,
            cot_block,
            whole(sorted_w.shape),
            whole(left.shape),
            whole(right.shape),
        ],
        out_specs=(send_block, outer_block),
        out_shape=(
            jax.ShapeDtypeStruct((2, half_ranks, 2 * seqs, LANES), BF16),
            jax.ShapeDtypeStruct((2, half_columns * depth, LANES), BF16),
        ),
        scratch_shapes=[pltpu.VMEM((2 * columns * depth, LANES), F32)],
        name="cotangent",
    )(coupling_cotangent, other_cot, sorted_w, left, right)

    got = lax.all_to_all(
        send.reshape(ranks, 2 * seqs, LANES), "res", split_axis=0, concat_axis=0, tiled=True
    ).reshape(send.shape)

    leaving = lax.dynamic_index_in_dim(got, 1 - mine, 0, keepdims=False)[:, 0:seqs, :]
    far = lax.ppermute(jnp.concatenate([leaving, left[None]], axis=0), "seq", swap)

    gradient = pl.pallas_call(
        functools.partial(grad_kernel, steps),
        grid=(steps,),
        in_specs=[
            send_block,
            outer_block,
            whole(homolog_matrix.shape),
            whole(gain.shape),
            whole(left_w.shape),
            whole(right_w.shape),
        ],
        out_specs=whole(homolog_matrix.shape),
        out_shape=jax.ShapeDtypeStruct(homolog_matrix.shape, BF16),
        scratch_shapes=[pltpu.VMEM((seqs, LANES), F32)] * 2,
        name="gradient",
    )(got, outer, homolog_matrix, gain, left_w, right_w)

    pair_delta = pl.pallas_call(
        functools.partial(pair_kernel, scale),
        grid=(steps,),
        in_specs=[
            pl.BlockSpec((2, step_ranks, seqs, LANES), lambda g: (0, g, 0, 0)),
            pl.BlockSpec((step_ranks, seqs, LANES), lambda g: (g, 0, 0)),
            whole(left.shape),
            pl.BlockSpec((None, seqs, LANES), lambda g: (half_ranks, 0, 0)),
            whole(sorted_w.shape),
            whole((1, LANES)),
        ],
        out_specs=cot_block,
        out_shape=jax.ShapeDtypeStruct(coupling_cotangent.shape, BF16),
        scratch_shapes=[pltpu.VMEM((columns * depth, LANES), F32)],
        name="pair",
    )(got, far, left, far, sorted_w, coupling_offset.reshape(1, -1))
    return (pair_delta, gradient)


def fetch(source, target, semaphore):
    copy = pltpu.make_async_copy(source, target, semaphore)
    copy.start()
    return copy


def start_copies(pairs, semaphores):
    copies = [
        pltpu.make_async_copy(source, target, semaphores.at[place])
        for place, (source, target) in enumerate(pairs)
    ]
    for copy in copies:
        copy.start()
    return copies


def small_project_kernel(
    x_hbm, gain_hbm, offset_hbm, left_w_hbm, left_b_hbm, right_w_hbm, right_b_hbm, pair_offset_hbm,
    cot_hbm, both_ref, normed_ref, inv_std_ref, spread_w_ref, gain_ref, pair_offset_ref, cot_ref,
    x_ref, offset_ref, left_w_ref, left_b_ref, right_w_ref, right_b_ref, wide_ref, semaphores,
):
    seqs, residues, _ = x_ref.shape
    depth = left_w_ref.shape[0]
    parts = 4
    part = seqs // parts
    copies = start_copies(
        tuple(
            (x_hbm.at[pl.ds(place * part, part)], x_ref.at[pl.ds(place * part, part)])
            for place in range(parts)
        )
        + (
            (left_w_hbm, left_w_ref),
            (right_w_hbm, right_w_ref),
            (gain_hbm, gain_ref),
            (offset_hbm, offset_ref),
            (left_b_hbm, left_b_ref),
            (right_b_hbm, right_b_ref),
            (cot_hbm, cot_ref),
            (pair_offset_hbm, pair_offset_ref),
        ),
        semaphores,
    )
    for copy in copies[:parts]:
        copy.wait()
    rows = x_ref[...].astype(F32).reshape(seqs * residues, x_ref.shape[2])
    normed, inv_std = normalise(rows)
    for copy in copies[parts:]:
        copy.wait()
    ln_out = (normed * gain_ref[...] + offset_ref[...]).astype(BF16)
    blocks = lane_block((seqs, LANES), depth)
    weight = jnp.concatenate(
        [left_w_ref[...]] * residues + [right_w_ref[...]] * residues, axis=0
    )
    wide = lax.dot_general(ln_out, weight, NT, preferred_element_type=F32)
    for place, bias_ref in enumerate((left_b_ref, right_b_ref)):
        bias = jnp.concatenate([bias_ref[...]] * residues, axis=1)
        wide_ref[place, 0 : seqs * residues, :] = wide[:, place * LANES : (place + 1) * LANES]
        own = pick(
            blocks, [wide_ref[place, pl.ds(p, seqs, stride=residues), :] for p in range(residues)]
        )
        both_ref[place] = (own + bias).astype(BF16)
    normed_ref[...] = normed
    inv_std_ref[...] = jnp.broadcast_to(inv_std, inv_std_ref.shape)
    spread_w_ref[...] = weight


def outer_flat(cot, sorted_wt_ref):
    return jnp.dot(cot, sorted_wt_ref[...], preferred_element_type=F32)


def outer_rows(flat, residues, turn_ref):
    columns = flat.shape[0] // residues
    depth = LANES // residues
    for tile in range(depth * depth // LANES):
        block = flat[:, tile * LANES : (tile + 1) * LANES]
        turned = exchange_blocks(
            [block[i * columns : (i + 1) * columns] for i in range(residues)], depth
        )
        for e in range(residues):
            turn_ref[pl.ds(tile * residues + e, columns, stride=depth), :] = turned[e]
    return turn_ref[0 : columns * depth, :].astype(BF16)


def outer_tiles(flat, residues):
    columns = flat.shape[0] // residues
    return jnp.concatenate(
        [
            jnp.concatenate(
                [
                    flat[i * columns + start : i * columns + start + 8, tile : tile + LANES]
                    for start in range(0, columns, 8)
                    for tile in range(0, flat.shape[1], LANES)
                ],
                axis=0,
            )
            for i in range(residues)
        ],
        axis=1,
    ).astype(BF16)


def blocks_apart(left, residues):
    depth = LANES // residues
    left = left.astype(F32)
    turned = [left] + [pltpu.roll(left, depth * t, 1) for t in range(1, residues)]
    blocks = lane_block(left.shape, depth)
    return jnp.concatenate(
        [
            jnp.concatenate(
                [
                    jnp.where(blocks == e, turned[(e - i) % residues], 0.0).astype(BF16)
                    for i in range(residues)
                ],
                axis=1,
            )
            for e in range(residues)
        ],
        axis=0,
    )


def column_pieces(left, outer, residues):
    seqs = left.shape[0]
    partial = lax.dot_general(
        blocks_apart(left, residues), outer, NT, preferred_element_type=F32
    )
    rows = [partial[e * seqs : (e + 1) * seqs] for e in range(residues)]
    half = lane_block(rows[0].shape, LANES // 2)
    source = 2 * (lane_block(rows[0].shape, residues) % 2) + half
    pieces = []
    for chip in range(residues):
        turned = []
        for e, row in enumerate(rows):
            count = (LANES // 2 * (e % 2 - chip // 2) + residues * (e // 2 - chip % 2)) % LANES
            turned.append(pltpu.roll(row, count, 1) if count else row)
        pieces.append(pick(source, turned))
    return pieces


def small_own_kernel(scale, own_ref, other_ref, w_ref, both_ref, spread_w_ref,
                     keep_ref, outer_near_ref, outer_far_ref, sorted_w_ref, sorted_wt_ref,
                     columns_w_ref, turn_refs, wide_ref):
    residues, columns, _ = own_ref.shape
    depth = LANES // residues
    wide_ref[0 : w_ref.shape[0], :] = w_ref[...].astype(F32)
    for d in range(depth):
        sorted_w_ref[d * depth : (d + 1) * depth, :] = wide_ref[
            pl.ds(d, depth, stride=depth), :
        ].astype(BF16)
    sorted_wt_ref[...] = (sorted_w_ref[...].astype(F32) * scale).astype(BF16).T
    shape = (columns_w_ref.shape[0], depth)
    row = lax.broadcasted_iota(jnp.int32, shape, 0)
    lane = lax.broadcasted_iota(jnp.int32, shape, 1)
    place = (row >> 3 & 7) * residues + 2 * (row >> 2 & 1) + (row >> 6)
    chosen = jnp.where(lane == place, 1.0, 0.0).astype(BF16)
    columns_w_ref[...] = jnp.dot(
        chosen, spread_w_ref[LANES : LANES + depth, :], preferred_element_type=F32
    ).astype(BF16)

    rank = lax.axis_index("res")
    own_is_near = lax.axis_index("seq") == lax.shift_right_logical(rank, 2)
    own = own_ref[...].reshape(residues * columns, LANES)
    other = other_ref[...].reshape(residues * columns, LANES)
    flat = outer_flat(jnp.where(own_is_near, own, other), sorted_wt_ref)
    pieces = column_pieces(both_ref[0], outer_tiles(flat, residues), residues)
    for place, piece in enumerate(pieces):
        keep_ref[place] = piece
    outer_near_ref[...] = outer_rows(flat, residues, turn_refs[0])
    flat = outer_flat(jnp.where(own_is_near, other, own), sorted_wt_ref)
    outer_far_ref[...] = outer_rows(flat, residues, turn_refs[1])


def small_partner_kernel(residues, got_ref, sorted_wt_ref, keep_ref, both_ref,
                         leaving_ref, keep_out_ref, right_ref, swap_ref):
    rank = lax.axis_index("res")
    seqs = got_ref.shape[1]
    cot = got_ref[2:4].reshape(2 * seqs, LANES)
    outer = outer_tiles(outer_flat(cot, sorted_wt_ref), residues)
    pieces = column_pieces(got_ref[0], outer, residues)
    right_ref[0] = both_ref[1]
    right_ref[1] = got_ref[1]
    own_is_near = lax.axis_index("seq") == lax.shift_right_logical(rank, 2)
    swap_ref[0] = jnp.where(own_is_near, got_ref[1], both_ref[1])
    swap_ref[1] = both_ref[0]
    for place, piece in enumerate(pieces):
        distance = lax.bitwise_xor(rank & 3, place)
        total = keep_ref[place] + piece
        keep_out_ref[distance] = total
        leaving_ref[distance, 2] = total.astype(BF16)
    for place in range(leaving_ref.shape[0]):
        leaving_ref[place, 0] = both_ref[1]
        leaving_ref[place, 1] = got_ref[1]


def small_finish_kernel(
    scale, right_ref, part_refs, swapped_ref, swapped_late_ref, both_ref, outer_near_ref, outer_far_ref,
    keep_ref, normed_ref, inv_std_ref, gain_ref, spread_w_ref, columns_w_ref, sorted_w_ref, offset_ref,
    grad_hbm, pair_hbm, grad_ref, pair_ref, near_ref, beyond_ref, turn_ref, lines_ref, semaphores,
):
    seqs, residues, _ = grad_ref.shape
    columns = pair_ref.shape[1]
    depth = LANES // residues
    ranks = columns // residues
    rank = lax.axis_index("res")
    mine = lax.axis_index("seq")
    here = rank & 3

    blocks_of = [right_ref] + list(part_refs)
    right_all = jnp.concatenate(
        [ref[0] for ref in blocks_of] + [ref[1] for ref in blocks_of], axis=1
    )
    spots = [
        pl.ds(pl.multiple_of(lax.bitwise_xor(here, mask) * LANES, LANES), LANES)
        for mask in range(ranks)
    ]
    outer = jnp.concatenate(
        [outer_near_ref[spot, :] for spot in spots] + [outer_far_ref[spot, :] for spot in spots],
        axis=0,
    )
    left_cot = jnp.dot(right_all, outer, preferred_element_type=F32)
    right_cot = keep_ref[0]
    for part_ref in part_refs:
        right_cot = right_cot + part_ref[2].astype(F32)
    blocks = lane_block((seqs, LANES), depth)
    column = lane_block((seqs, LANES), 1) % residues
    spread = jnp.concatenate(
        [
            jnp.concatenate(
                [
                    jnp.where(blocks == place, left_cot, 0.0),
                    jnp.where(column == place, right_cot, 0.0),
                ],
                axis=1,
            )
            for place in range(residues)
        ],
        axis=0,
    )
    rows = residues * seqs
    parts = jnp.concatenate(split_two(spread), axis=0)
    weight = jnp.concatenate([spread_w_ref[0:LANES, :], columns_w_ref[...]], axis=0)
    ln_cot = jnp.dot(parts, weight, preferred_element_type=F32)
    ln_cot = ln_cot[0:rows] + ln_cot[rows : 2 * rows]
    tiles = range(lines_ref.shape[0])
    for place in range(residues):
        for tile in tiles:
            lines_ref[tile, pl.ds(place, seqs, stride=residues), :] = ln_cot[
                place * seqs : (place + 1) * seqs, tile * LANES : (tile + 1) * LANES
            ]
    gained = jnp.concatenate([lines_ref[tile, 0:rows, :] for tile in tiles], axis=1) * gain_ref[...]
    normed = normed_ref[...]
    inv_std = jnp.concatenate([inv_std_ref[...]] * len(tiles), axis=1)
    grad = inv_std * (
        gained
        - jnp.mean(gained, axis=-1, keepdims=True)
        - normed * jnp.mean(gained * normed, axis=-1, keepdims=True)
    )
    grad_ref[...] = grad.reshape(grad_ref.shape).astype(BF16)
    grad_copy = pltpu.make_async_copy(grad_ref, grad_hbm, semaphores.at[0])
    grad_copy.start()

    half = jnp.where(mine == lax.shift_right_logical(rank, 2), 0, 1)
    for mask, ref in enumerate(blocks_of):
        near_ref[mask] = ref[half]
    beyond_ref[0] = swapped_ref[0]
    beyond_ref[1] = part_refs[0][3]
    beyond_ref[2] = part_refs[1][3]
    beyond_ref[3] = swapped_late_ref[...]
    masks = [lax.bitwise_xor(here, place) for place in range(ranks)]
    right = jnp.concatenate(
        [
            jnp.concatenate([ref[mask] for mask in masks], axis=1)
            for ref in (near_ref, beyond_ref)
        ],
        axis=0,
    )
    left = jnp.concatenate([both_ref[0], swapped_ref[1]], axis=0)
    turn_ref[0 : columns * depth, :] = lax.dot_general(right, left, TN, preferred_element_type=F32) * scale
    tiles = []
    for tile in range(depth * depth // LANES):
        turned = exchange_blocks(
            [
                turn_ref[pl.ds(tile * residues + e, columns, stride=depth), :]
                for e in range(residues)
            ],
            depth,
        )
        tiles.append(jnp.concatenate(turned, axis=0))
    flat = jnp.concatenate(tiles, axis=1)
    rows = residues * columns
    parts = jnp.concatenate(split_two(flat), axis=0)
    pair = jnp.dot(parts, sorted_w_ref[...], preferred_element_type=F32)
    pair = pair[0:rows] + pair[rows : 2 * rows]
    pair_ref[...] = (pair + offset_ref[...]).astype(BF16).reshape(pair_ref.shape)
    pair_copy = pltpu.make_async_copy(pair_ref, pair_hbm, semaphores.at[1])
    pair_copy.start()
    grad_copy.wait()
    pair_copy.wait()


def small_slice(
    homolog_matrix,
    standardizer_scaling,
    standardizer_offset,
    left_projection_matrix,
    left_offset_vector,
    right_projection_matrix,
    right_offset_vector,
    coupling_matrix,
    coupling_offset,
    coupling_cotangent,
):
    seqs, residues, features = homolog_matrix.shape
    depth = left_projection_matrix.shape[1]
    ranks = lax.axis_size("res")
    rows = seqs * residues
    scale = 1.0 / (seqs * lax.axis_size("seq"))
    rank = lax.axis_index("res")
    mine = lax.axis_index("seq")
    swap = [(0, 1), (1, 0)]
    limit = pltpu.CompilerParams(vmem_limit_bytes=8 * 1024 * 1024)
    vmem = pl.BlockSpec(memory_space=pltpu.VMEM)
    like = jax.ShapeDtypeStruct

    other_cot = lax.ppermute(coupling_cotangent, "seq", swap)
    hbm = pl.BlockSpec(memory_space=pltpu.HBM)
    pin = lambda array: pltpu.with_memory_space_constraint(array, pltpu.HBM)
    both, normed, inv_std, spread_w, gain, pair_offset, own_cot = pl.pallas_call(
        small_project_kernel,
        in_specs=[hbm] * 9,
        out_specs=[vmem] * 7,
        out_shape=(
            like((2, seqs, LANES), BF16),
            like((rows, features), F32),
            like((rows, LANES), F32),
            like((2 * LANES, features), BF16),
            like((1, features), F32),
            like((1, LANES), F32),
            like(coupling_cotangent.shape, BF16),
        ),
        scratch_shapes=[
            pltpu.VMEM(homolog_matrix.shape, BF16),
            pltpu.VMEM((1, features), F32),
            pltpu.VMEM((depth, features), BF16),
            pltpu.VMEM((1, depth), F32),
            pltpu.VMEM((depth, features), BF16),
            pltpu.VMEM((1, depth), F32),
            pltpu.VMEM((2, rows + 8, LANES), F32),
            pltpu.SemaphoreType.DMA((12,)),
        ],
        compiler_params=limit,
        name="project",
    )(
        *[
            pin(array)
            for array in (
                homolog_matrix,
                standardizer_scaling.reshape(1, -1),
                standardizer_offset.reshape(1, -1),
                left_projection_matrix.T,
                left_offset_vector.reshape(1, -1),
                right_projection_matrix.T,
                right_offset_vector.reshape(1, -1),
                coupling_offset.reshape(1, -1),
                coupling_cotangent,
            )
        ]
    )

    def swap_over(mask, value):
        return lax.ppermute(value, "res", [(source, source ^ mask) for source in range(ranks)])

    own_is_near = mine == lax.shift_right_logical(rank, 2)
    far_cot = jnp.where(own_is_near, other_cot, own_cot).reshape(2, seqs, LANES)
    beyond_two = swap_over(4, jnp.concatenate([both, far_cot]))

    half_rows = ranks // 2 * LANES
    turn = pltpu.VMEM((half_rows + depth, LANES), F32)
    keep, outer_near, outer_far, sorted_w, sorted_wt, columns_w = pl.pallas_call(
        functools.partial(small_own_kernel, scale),
        in_specs=[vmem] * 5,
        out_specs=[vmem] * 6,
        out_shape=(
            like((ranks // 2, seqs, LANES), F32),
            like((half_rows, LANES), BF16),
            like((half_rows, LANES), BF16),
            like(coupling_matrix.shape, BF16),
            like(coupling_matrix.shape[::-1], BF16),
            like((LANES, features), BF16),
        ),
        scratch_shapes=[
            [turn, turn],
            pltpu.VMEM((coupling_matrix.shape[0] + depth, LANES), F32),
        ],
        compiler_params=limit,
        name="own_pieces",
    )(own_cot, other_cot, coupling_matrix, both, spread_w)

    leaving_parts, keep, right, leaving = pl.pallas_call(
        functools.partial(small_partner_kernel, residues),
        in_specs=[vmem] * 4,
        out_specs=[vmem] * 4,
        out_shape=(
            like((ranks // 2, 3, seqs, LANES), BF16),
            like((ranks // 2, seqs, LANES), F32),
            like((2, seqs, LANES), BF16),
            like((2, seqs, LANES), BF16),
        ),
        compiler_params=limit,
        name="partner_pieces",
    )(beyond_two, sorted_wt, keep, both)

    swapped = lax.ppermute(leaving, "seq", swap)
    diagonal = swap_over(3, leaving_parts[3])
    across, beside = [
        swap_over(mask, jnp.concatenate([leaving_parts[mask], swapped[0:1]])) for mask in (2, 1)
    ]
    swapped_late = lax.ppermute(
        jnp.where(own_is_near, diagonal[1], diagonal[0]), "seq", swap
    )

    pair_delta, gradient = pl.pallas_call(
        functools.partial(small_finish_kernel, scale),
        in_specs=[vmem, [vmem] * 3] + [vmem] * 13,
        out_specs=[pl.BlockSpec(memory_space=pl.ANY)] * 2,
        out_shape=(
            like(homolog_matrix.shape, BF16),
            like(coupling_cotangent.shape, BF16),
        ),
        scratch_shapes=[
            pltpu.VMEM(homolog_matrix.shape, BF16),
            pltpu.VMEM(coupling_cotangent.shape, BF16),
            pltpu.VMEM((ranks // 2, seqs, LANES), BF16),
            pltpu.VMEM((ranks // 2, seqs, LANES), BF16),
            turn,
            pltpu.VMEM((features // LANES, rows + 8, LANES), F32),
            pltpu.SemaphoreType.DMA((2,)),
        ],
        compiler_params=limit,
        name="finish",
    )(
        right,
        [beside, across, diagonal],
        swapped,
        swapped_late,
        both,
        outer_near,
        outer_far,
        keep,
        normed,
        inv_std,
        gain,
        spread_w,
        columns_w,
        sorted_w,
        pair_offset,
    )[::-1]
    return (pair_delta, gradient)


def body(*arrays):
    sequences = arrays[0].shape[0] * lax.axis_size("seq")
    if lax.axis_size("res") == 8 and sequences & (sequences - 1) == 0:
        return small_slice(*arrays)
    return wide_slice(*arrays)


def solution(mesh):
    return jax.shard_map(
        body,
        mesh=mesh,
        in_specs=(
            P(("grp", "seq"), "res", None),
            P(),
            P(),
            P(),
            P(),
            P(),
            P(),
            P(),
            P(),
            P(("grp", "res"), "seq", None),
        ),
        out_specs=(P(("grp", "res"), "seq", None), P(("grp", "seq"), "res", None)),
        check_vma=False,
    )
```

```python
import functools

import jax
import jax.numpy as jnp
from jax import lax
from jax.experimental import pallas as pl
from jax.experimental.pallas import tpu as pltpu
from jax.sharding import PartitionSpec as P

LANES = 128
BF16 = jnp.bfloat16
F32 = jnp.float32
NT = (((1,), (1,)), ((), ()))
TN = (((0,), (0,)), ((), ()))


def lane_block(shape, width):
    return lax.broadcasted_iota(jnp.int32, shape, 1) // width


def pick(blocks, pieces):
    result = pieces[0]
    for place in range(1, len(pieces)):
        result = jnp.where(blocks == place, pieces[place], result)
    return result


def split_three(value):
    top = value.astype(BF16)
    rest = value - top.astype(F32)
    middle = rest.astype(BF16)
    low = (rest - middle.astype(F32)).astype(BF16)
    return top, middle, low


def exchange_blocks(pieces, width):
    first, second, third, fourth = pieces
    blocks = lane_block(first.shape, width)
    odd, high = blocks % 2 == 1, blocks >= 2
    roll = lambda value, count: pltpu.roll(value, count * width, 1)
    first, second = jnp.where(odd, roll(second, 1), first), jnp.where(odd, second, roll(first, 3))
    third, fourth = jnp.where(odd, roll(fourth, 1), third), jnp.where(odd, fourth, roll(third, 3))
    return [
        jnp.where(high, roll(third, 2), first),
        jnp.where(high, roll(fourth, 2), second),
        jnp.where(high, third, roll(first, 2)),
        jnp.where(high, fourth, roll(second, 2)),
    ]


def split_two(value):
    top = value.astype(BF16)
    return top, (value - top.astype(F32)).astype(BF16)


def normalise(rows):
    centred = rows - jnp.mean(rows, axis=-1, keepdims=True)
    inv_std = lax.rsqrt(jnp.mean(centred * centred, axis=-1, keepdims=True) + 1e-05)
    return centred * inv_std, inv_std


def residue_rows(x_ref):
    return jnp.concatenate(
        [x_ref[:, place, :].astype(F32) for place in range(x_ref.shape[1])], axis=0
    )


def project_kernel(
    x_ref, gain_ref, offset_ref, left_w_ref, left_b_ref, right_w_ref, right_b_ref, w_ref,
    left_ref, right_ref, sorted_w_ref, wide_ref,
):
    seqs, residues, _ = x_ref.shape
    depth = left_w_ref.shape[0]
    normed, _ = normalise(residue_rows(x_ref))
    ln_out = (normed * gain_ref[...] + offset_ref[...]).astype(BF16)
    blocks = lane_block((seqs, LANES), depth)
    for weight_ref, bias_ref, out_ref in (
        (left_w_ref, left_b_ref, left_ref),
        (right_w_ref, right_b_ref, right_ref),
    ):
        weight = jnp.concatenate([weight_ref[...]] * residues, axis=0)
        bias = jnp.concatenate([bias_ref[...]] * residues, axis=1)
        wide = lax.dot_general(ln_out, weight, NT, preferred_element_type=F32)
        own = pick(blocks, [wide[p * seqs : (p + 1) * seqs] for p in range(residues)])
        out_ref[...] = (own + bias).astype(BF16)
    wide_ref[...] = w_ref[...].astype(F32)
    for d in range(depth):
        sorted_w_ref[d * depth : (d + 1) * depth, :] = wide_ref[
            pl.ds(d, depth, stride=depth), :
        ].astype(BF16)


def cot_kernel(scale, own_ref, other_ref, sorted_w_ref, left_ref, right_ref,
               send_ref, outer_ref, turn_ref):
    residues, columns, _ = own_ref.shape
    depth = sorted_w_ref.shape[0] // (LANES // residues)
    depth = LANES // residues
    first = lax.axis_index("seq") == 0
    own = own_ref[...].reshape(residues * columns, LANES)
    other = other_ref[...].reshape(residues * columns, LANES)
    low = jnp.where(first, own, other)
    high = jnp.where(first, other, own)
    both = jnp.concatenate([low, high], axis=0)
    flat = lax.dot_general(both, sorted_w_ref[...], NT, preferred_element_type=F32) * scale
    blocks = lane_block((columns, LANES), depth)
    for half in range(2):
        for tile in range(depth * depth // LANES):
            block = flat[
                half * residues * columns : (half + 1) * residues * columns,
                tile * LANES : (tile + 1) * LANES,
            ]
            turned = [block] + [pltpu.roll(block, depth * t, 1) for t in range(1, residues)]
            for e in range(residues):
                piece = pick(
                    blocks,
                    [
                        turned[(i - e) % residues][i * columns : (i + 1) * columns]
                        for i in range(residues)
                    ],
                )
                turn_ref[pl.ds(half * columns * depth + tile * residues + e, columns, stride=depth), :] = piece
    outer = turn_ref[...].astype(BF16)
    half_rows = columns * depth
    partial = lax.dot_general(left_ref[...], outer, NT, preferred_element_type=F32).astype(BF16)
    seqs = left_ref.shape[0]
    ranks = columns // residues
    for half in range(2):
        outer_ref[half] = outer[half * half_rows : (half + 1) * half_rows]
        for rank in range(ranks):
            at = (half * ranks + rank) * LANES
            send_ref[half, rank, 0:seqs, :] = right_ref[...]
            send_ref[half, rank, seqs : 2 * seqs, :] = partial[:, at : at + LANES]


def grad_kernel(steps, got_ref, outer_ref, x_ref, gain_ref, left_w_ref, right_w_ref,
                grad_ref, left_cot_ref, right_cot_ref):
    step = pl.program_id(0)
    _, ranks, twice, _ = got_ref.shape
    seqs = twice // 2
    residues = x_ref.shape[1]
    depth = LANES // residues

    @pl.when(step == 0)
    def _():
        left_cot_ref[...] = jnp.zeros_like(left_cot_ref)
        right_cot_ref[...] = jnp.zeros_like(right_cot_ref)

    places = [(half, rank) for half in range(2) for rank in range(ranks)]
    right_all = jnp.concatenate([got_ref[h, r, 0:seqs, :] for h, r in places], axis=1)
    outer = jnp.concatenate([outer_ref[0], outer_ref[1]], axis=0)
    left_cot_ref[...] += jnp.dot(right_all, outer, preferred_element_type=F32)
    total = got_ref[0, 0, seqs:twice, :].astype(F32)
    for h, r in places[1:]:
        total = total + got_ref[h, r, seqs:twice, :].astype(F32)
    right_cot_ref[...] += total

    @pl.when(step == steps - 1)
    def _():
        blocks = lane_block((seqs, LANES), depth)
        left_cot, right_cot = left_cot_ref[...], right_cot_ref[...]
        spread = jnp.concatenate(
            [
                jnp.concatenate(
                    [
                        jnp.where(blocks == place, left_cot, 0.0),
                        jnp.where(blocks == place, right_cot, 0.0),
                    ],
                    axis=1,
                )
                for place in range(residues)
            ],
            axis=0,
        )
        weight = jnp.concatenate(
            [left_w_ref[...]] * residues + [right_w_ref[...]] * residues, axis=0
        )
        rows = residues * seqs
        parts = jnp.concatenate(split_three(spread), axis=0)
        ln_cot = jnp.dot(parts, weight, preferred_element_type=F32)
        ln_cot = ln_cot[0:rows] + (ln_cot[rows : 2 * rows] + ln_cot[2 * rows : 3 * rows])
        gained = ln_cot * gain_ref[...]
        normed, inv_std = normalise(residue_rows(x_ref))
        grad = inv_std * (
            gained
            - jnp.mean(gained, axis=-1, keepdims=True)
            - normed * jnp.mean(gained * normed, axis=-1, keepdims=True)
        )
        for place in range(residues):
            grad_ref[:, place, :] = grad[place * seqs : (place + 1) * seqs].astype(BF16)


def pair_kernel(scale, got_ref, far_ref, left_ref, far_left_ref, sorted_w_ref, offset_ref,
                pair_ref, turn_ref):
    residues, columns, _ = pair_ref.shape
    depth = LANES // residues
    ranks = columns // residues
    mine = lax.axis_index("seq")
    near = jnp.concatenate([got_ref[mine, r] for r in range(ranks)], axis=1)
    far = jnp.concatenate([far_ref[r] for r in range(ranks)], axis=1)
    right = jnp.concatenate([near, far], axis=0)
    left = jnp.concatenate([left_ref[...], far_left_ref[...]], axis=0)
    turn_ref[...] = lax.dot_general(right, left, TN, preferred_element_type=F32) * scale
    blocks = lane_block((columns, LANES), depth)
    tiles = []
    for tile in range(depth * depth // LANES):
        pieces = [
            turn_ref[pl.ds(tile * residues + e, columns, stride=depth), :]
            for e in range(residues)
        ]
        rows = jnp.concatenate(pieces, axis=0)
        turned = [rows] + [pltpu.roll(rows, depth * t, 1) for t in range(1, residues)]
        tiles.append(
            jnp.concatenate(
                [
                    pick(
                        blocks,
                        [
                            turned[(e - i) % residues][e * columns : (e + 1) * columns]
                            for e in range(residues)
                        ],
                    )
                    for i in range(residues)
                ],
                axis=0,
            )
        )
    flat = jnp.concatenate(tiles, axis=1)
    rows = residues * columns
    parts = jnp.concatenate(split_three(flat), axis=0)
    pair = jnp.dot(parts, sorted_w_ref[...], preferred_element_type=F32)
    pair = pair[0:rows] + (pair[rows : 2 * rows] + pair[2 * rows : 3 * rows])
    pair_ref[...] = (pair + offset_ref[...]).astype(BF16).reshape(pair_ref.shape)


def wide_slice(
    homolog_matrix,
    standardizer_scaling,
    standardizer_offset,
    left_projection_matrix,
    left_offset_vector,
    right_projection_matrix,
    right_offset_vector,
    coupling_matrix,
    coupling_offset,
    coupling_cotangent,
):
    seqs, residues, features = homolog_matrix.shape
    depth = left_projection_matrix.shape[1]
    ranks = lax.axis_size("res")
    scale = 1.0 / (seqs * lax.axis_size("seq"))
    half_ranks = ranks // 2
    half_columns = half_ranks * residues
    step_ranks = 4
    columns = step_ranks * residues
    steps = half_ranks // step_ranks
    mine = lax.axis_index("seq")
    swap = [(0, 1), (1, 0)]

    other_cot = lax.ppermute(coupling_cotangent, "seq", swap)
    gain = standardizer_scaling.reshape(1, -1)
    left_w = left_projection_matrix.T
    right_w = right_projection_matrix.T

    left, right, sorted_w = pl.pallas_call(
        project_kernel,
        out_shape=(
            jax.ShapeDtypeStruct((seqs, LANES), BF16),
            jax.ShapeDtypeStruct((seqs, LANES), BF16),
            jax.ShapeDtypeStruct(coupling_matrix.shape, BF16),
        ),
        scratch_shapes=[pltpu.VMEM(coupling_matrix.shape, F32)],
        name="project",
    )(
        homolog_matrix,
        gain,
        standardizer_offset.reshape(1, -1),
        left_w,
        left_offset_vector.reshape(1, -1),
        right_w,
        right_offset_vector.reshape(1, -1),
        coupling_matrix,
    )

    whole = lambda shape: pl.BlockSpec(shape, lambda g: (0,) * len(shape))
    cot_block = pl.BlockSpec((residues, columns, LANES), lambda g: (0, g, 0))
    outer_block = pl.BlockSpec((2, columns * depth, LANES), lambda g: (0, g, 0))
    send_block = pl.BlockSpec((2, step_ranks, 2 * seqs, LANES), lambda g: (0, g, 0, 0))
    send, outer = pl.pallas_call(
        functools.partial(cot_kernel, scale),
        grid=(steps,),
        in_specs=[
            cot_block,
            cot_block,
            whole(sorted_w.shape),
            whole(left.shape),
            whole(right.shape),
        ],
        out_specs=(send_block, outer_block),
        out_shape=(
            jax.ShapeDtypeStruct((2, half_ranks, 2 * seqs, LANES), BF16),
            jax.ShapeDtypeStruct((2, half_columns * depth, LANES), BF16),
        ),
        scratch_shapes=[pltpu.VMEM((2 * columns * depth, LANES), F32)],
        name="cotangent",
    )(coupling_cotangent, other_cot, sorted_w, left, right)

    got = lax.all_to_all(
        send.reshape(ranks, 2 * seqs, LANES), "res", split_axis=0, concat_axis=0, tiled=True
    ).reshape(send.shape)

    leaving = lax.dynamic_index_in_dim(got, 1 - mine, 0, keepdims=False)[:, 0:seqs, :]
    far = lax.ppermute(jnp.concatenate([leaving, left[None]], axis=0), "seq", swap)

    gradient = pl.pallas_call(
        functools.partial(grad_kernel, steps),
        grid=(steps,),
        in_specs=[
            send_block,
            outer_block,
            whole(homolog_matrix.shape),
            whole(gain.shape),
            whole(left_w.shape),
            whole(right_w.shape),
        ],
        out_specs=whole(homolog_matrix.shape),
        out_shape=jax.ShapeDtypeStruct(homolog_matrix.shape, BF16),
        scratch_shapes=[pltpu.VMEM((seqs, LANES), F32)] * 2,
        name="gradient",
    )(got, outer, homolog_matrix, gain, left_w, right_w)

    pair_delta = pl.pallas_call(
        functools.partial(pair_kernel, scale),
        grid=(steps,),
        in_specs=[
            pl.BlockSpec((2, step_ranks, seqs, LANES), lambda g: (0, g, 0, 0)),
            pl.BlockSpec((step_ranks, seqs, LANES), lambda g: (g, 0, 0)),
            whole(left.shape),
            pl.BlockSpec((None, seqs, LANES), lambda g: (half_ranks, 0, 0)),
            whole(sorted_w.shape),
            whole((1, LANES)),
        ],
        out_specs=cot_block,
        out_shape=jax.ShapeDtypeStruct(coupling_cotangent.shape, BF16),
        scratch_shapes=[pltpu.VMEM((columns * depth, LANES), F32)],
        name="pair",
    )(got, far, left, far, sorted_w, coupling_offset.reshape(1, -1))
    return (pair_delta, gradient)


def fetch(source, target, semaphore):
    copy = pltpu.make_async_copy(source, target, semaphore)
    copy.start()
    return copy


def start_copies(pairs, semaphores):
    copies = [
        pltpu.make_async_copy(source, target, semaphores.at[place])
        for place, (source, target) in enumerate(pairs)
    ]
    for copy in copies:
        copy.start()
    return copies


def small_project_kernel(
    x_hbm, gain_hbm, offset_hbm, left_w_hbm, left_b_hbm, right_w_hbm, right_b_hbm, pair_offset_hbm,
    cot_hbm, both_ref, normed_ref, inv_std_ref, spread_w_ref, gain_ref, pair_offset_ref, cot_ref,
    x_ref, offset_ref, left_w_ref, left_b_ref, right_w_ref, right_b_ref, wide_ref, semaphores,
):
    seqs, residues, _ = x_ref.shape
    depth = left_w_ref.shape[0]
    parts = 4
    part = seqs // parts
    copies = start_copies(
        tuple(
            (x_hbm.at[pl.ds(place * part, part)], x_ref.at[pl.ds(place * part, part)])
            for place in range(parts)
        )
        + (
            (left_w_hbm, left_w_ref),
            (right_w_hbm, right_w_ref),
            (gain_hbm, gain_ref),
            (offset_hbm, offset_ref),
            (left_b_hbm, left_b_ref),
            (right_b_hbm, right_b_ref),
            (cot_hbm, cot_ref),
            (pair_offset_hbm, pair_offset_ref),
        ),
        semaphores,
    )
    for copy in copies[:parts]:
        copy.wait()
    rows = x_ref[...].astype(F32).reshape(seqs * residues, x_ref.shape[2])
    normed, inv_std = normalise(rows)
    for copy in copies[parts:]:
        copy.wait()
    ln_out = (normed * gain_ref[...] + offset_ref[...]).astype(BF16)
    blocks = lane_block((seqs, LANES), depth)
    weight = jnp.concatenate(
        [left_w_ref[...]] * residues + [right_w_ref[...]] * residues, axis=0
    )
    wide = lax.dot_general(ln_out, weight, NT, preferred_element_type=F32)
    for place, bias_ref in enumerate((left_b_ref, right_b_ref)):
        bias = jnp.concatenate([bias_ref[...]] * residues, axis=1)
        wide_ref[place, 0 : seqs * residues, :] = wide[:, place * LANES : (place + 1) * LANES]
        own = pick(
            blocks, [wide_ref[place, pl.ds(p, seqs, stride=residues), :] for p in range(residues)]
        )
        both_ref[place] = (own + bias).astype(BF16)
    normed_ref[...] = normed
    inv_std_ref[...] = jnp.broadcast_to(inv_std, inv_std_ref.shape)
    spread_w_ref[...] = weight


def outer_flat(cot, sorted_wt_ref):
    return jnp.dot(cot, sorted_wt_ref[...], preferred_element_type=F32)


def outer_rows(flat, residues, turn_ref):
    columns = flat.shape[0] // residues
    depth = LANES // residues
    for tile in range(depth * depth // LANES):
        block = flat[:, tile * LANES : (tile + 1) * LANES]
        turned = exchange_blocks(
            [block[i * columns : (i + 1) * columns] for i in range(residues)], depth
        )
        for e in range(residues):
            turn_ref[pl.ds(tile * residues + e, columns, stride=depth), :] = turned[e]
    return turn_ref[0 : columns * depth, :].astype(BF16)


def outer_tiles(flat, residues):
    columns = flat.shape[0] // residues
    return jnp.concatenate(
        [
            jnp.concatenate(
                [
                    flat[i * columns + start : i * columns + start + 8, tile : tile + LANES]
                    for start in range(0, columns, 8)
                    for tile in range(0, flat.shape[1], LANES)
                ],
                axis=0,
            )
            for i in range(residues)
        ],
        axis=1,
    ).astype(BF16)


def blocks_apart(left, residues):
    depth = LANES // residues
    left = left.astype(F32)
    turned = [left] + [pltpu.roll(left, depth * t, 1) for t in range(1, residues)]
    blocks = lane_block(left.shape, depth)
    return jnp.concatenate(
        [
            jnp.concatenate(
                [
                    jnp.where(blocks == e, turned[(e - i) % residues], 0.0).astype(BF16)
                    for i in range(residues)
                ],
                axis=1,
            )
            for e in range(residues)
        ],
        axis=0,
    )


def column_pieces(left, outer, residues):
    seqs = left.shape[0]
    partial = lax.dot_general(
        blocks_apart(left, residues), outer, NT, preferred_element_type=F32
    )
    rows = [partial[e * seqs : (e + 1) * seqs] for e in range(residues)]
    half = lane_block(rows[0].shape, LANES // 2)
    source = 2 * (lane_block(rows[0].shape, residues) % 2) + half
    pieces = []
    for chip in range(residues):
        turned = []
        for e, row in enumerate(rows):
            count = (LANES // 2 * (e % 2 - chip // 2) + residues * (e // 2 - chip % 2)) % LANES
            turned.append(pltpu.roll(row, count, 1) if count else row)
        pieces.append(pick(source, turned))
    return pieces


def small_own_kernel(scale, own_ref, other_ref, w_ref, both_ref, spread_w_ref,
                     keep_ref, outer_near_ref, outer_far_ref, sorted_w_ref, sorted_wt_ref,
                     columns_w_ref, turn_refs, wide_ref):
    residues, columns, _ = own_ref.shape
    depth = LANES // residues
    wide_ref[0 : w_ref.shape[0], :] = w_ref[...].astype(F32)
    for d in range(depth):
        sorted_w_ref[d * depth : (d + 1) * depth, :] = wide_ref[
            pl.ds(d, depth, stride=depth), :
        ].astype(BF16)
    sorted_wt_ref[...] = (sorted_w_ref[...].astype(F32) * scale).astype(BF16).T
    shape = (columns_w_ref.shape[0], depth)
    row = lax.broadcasted_iota(jnp.int32, shape, 0)
    lane = lax.broadcasted_iota(jnp.int32, shape, 1)
    place = (row >> 3 & 7) * residues + 2 * (row >> 2 & 1) + (row >> 6)
    chosen = jnp.where(lane == place, 1.0, 0.0).astype(BF16)
    columns_w_ref[...] = jnp.dot(
        chosen, spread_w_ref[LANES : LANES + depth, :], preferred_element_type=F32
    ).astype(BF16)

    rank = lax.axis_index("res")
    own_is_near = lax.axis_index("seq") == lax.shift_right_logical(rank, 2)
    own = own_ref[...].reshape(residues * columns, LANES)
    other = other_ref[...].reshape(residues * columns, LANES)
    flat = outer_flat(jnp.where(own_is_near, own, other), sorted_wt_ref)
    pieces = column_pieces(both_ref[0], outer_tiles(flat, residues), residues)
    for place, piece in enumerate(pieces):
        keep_ref[place] = piece
    outer_near_ref[...] = outer_rows(flat, residues, turn_refs[0])
    flat = outer_flat(jnp.where(own_is_near, other, own), sorted_wt_ref)
    outer_far_ref[...] = outer_rows(flat, residues, turn_refs[1])


def small_partner_kernel(residues, got_ref, sorted_wt_ref, keep_ref, both_ref,
                         leaving_ref, keep_out_ref, right_ref):
    rank = lax.axis_index("res")
    seqs = got_ref.shape[1]
    cot = got_ref[2:4].reshape(2 * seqs, LANES)
    outer = outer_tiles(outer_flat(cot, sorted_wt_ref), residues)
    pieces = column_pieces(got_ref[0], outer, residues)
    right_ref[0] = both_ref[1]
    right_ref[1] = got_ref[1]
    for place, piece in enumerate(pieces):
        distance = lax.bitwise_xor(rank & 3, place)
        total = keep_ref[place] + piece
        keep_out_ref[distance] = total
        leaving_ref[distance, 2] = total.astype(BF16)
    for place in range(leaving_ref.shape[0]):
        leaving_ref[place, 0] = both_ref[1]
        leaving_ref[place, 1] = got_ref[1]


def small_finish_kernel(
    scale, right_ref, part_refs, swapped_ref, swapped_late_ref, both_ref, outer_near_ref, outer_far_ref,
    keep_ref, normed_ref, inv_std_ref, gain_ref, spread_w_ref, columns_w_ref, sorted_w_ref, offset_ref,
    grad_hbm, pair_hbm, grad_ref, pair_ref, near_ref, beyond_ref, turn_ref, lines_ref, semaphores,
):
    part_refs = [part_refs[1], part_refs[0], part_refs[2]]
    seqs, residues, _ = grad_ref.shape
    columns = pair_ref.shape[1]
    depth = LANES // residues
    ranks = columns // residues
    rank = lax.axis_index("res")
    mine = lax.axis_index("seq")
    here = rank & 3

    blocks_of = [right_ref] + list(part_refs)
    right_all = jnp.concatenate(
        [ref[0] for ref in blocks_of] + [ref[1] for ref in blocks_of], axis=1
    )
    spots = [
        pl.ds(pl.multiple_of(lax.bitwise_xor(here, mask) * LANES, LANES), LANES)
        for mask in range(ranks)
    ]
    outer = jnp.concatenate(
        [outer_near_ref[spot, :] for spot in spots] + [outer_far_ref[spot, :] for spot in spots],
        axis=0,
    )
    left_cot = jnp.dot(right_all, outer, preferred_element_type=F32)
    right_cot = keep_ref[0]
    for part_ref in part_refs:
        right_cot = right_cot + part_ref[2].astype(F32)
    blocks = lane_block((seqs, LANES), depth)
    column = lane_block((seqs, LANES), 1) % residues
    spread = jnp.concatenate(
        [
            jnp.concatenate(
                [
                    jnp.where(blocks == place, left_cot, 0.0),
                    jnp.where(column == place, right_cot, 0.0),
                ],
                axis=1,
            )
            for place in range(residues)
        ],
        axis=0,
    )
    rows = residues * seqs
    parts = jnp.concatenate(split_two(spread), axis=0)
    weight = jnp.concatenate([spread_w_ref[0:LANES, :], columns_w_ref[...]], axis=0)
    ln_cot = jnp.dot(parts, weight, preferred_element_type=F32)
    ln_cot = ln_cot[0:rows] + ln_cot[rows : 2 * rows]
    tiles = range(lines_ref.shape[0])
    for place in range(residues):
        for tile in tiles:
            lines_ref[tile, pl.ds(place, seqs, stride=residues), :] = ln_cot[
                place * seqs : (place + 1) * seqs, tile * LANES : (tile + 1) * LANES
            ]
    gained = jnp.concatenate([lines_ref[tile, 0:rows, :] for tile in tiles], axis=1) * gain_ref[...]
    normed = normed_ref[...]
    grad = inv_std_ref[:, 0:1] * (
        gained
        - jnp.mean(gained, axis=-1, keepdims=True)
        - normed * jnp.mean(gained * normed, axis=-1, keepdims=True)
    )
    grad_ref[...] = grad.reshape(grad_ref.shape).astype(BF16)
    grad_copy = pltpu.make_async_copy(grad_ref, grad_hbm, semaphores.at[0])
    grad_copy.start()

    half = jnp.where(mine == lax.shift_right_logical(rank, 2), 0, 1)
    for mask, ref in enumerate(blocks_of):
        near_ref[mask] = ref[half]
    beyond_ref[0] = swapped_ref[0]
    beyond_ref[1] = part_refs[0][3]
    beyond_ref[2] = part_refs[1][3]
    beyond_ref[3] = swapped_late_ref[...]
    masks = [lax.bitwise_xor(here, place) for place in range(ranks)]
    right = jnp.concatenate(
        [
            jnp.concatenate([ref[mask] for mask in masks], axis=1)
            for ref in (near_ref, beyond_ref)
        ],
        axis=0,
    )
    left = jnp.concatenate([both_ref[0], swapped_ref[1]], axis=0)
    turn_ref[0 : columns * depth, :] = lax.dot_general(right, left, TN, preferred_element_type=F32) * scale
    tiles = []
    for tile in range(depth * depth // LANES):
        turned = exchange_blocks(
            [
                turn_ref[pl.ds(tile * residues + e, columns, stride=depth), :]
                for e in range(residues)
            ],
            depth,
        )
        tiles.append(jnp.concatenate(turned, axis=0))
    flat = jnp.concatenate(tiles, axis=1)
    rows = residues * columns
    parts = jnp.concatenate(split_two(flat), axis=0)
    pair = jnp.dot(parts, sorted_w_ref[...], preferred_element_type=F32)
    pair = pair[0:rows] + pair[rows : 2 * rows]
    pair_ref[...] = (pair + offset_ref[...]).astype(BF16).reshape(pair_ref.shape)
    pair_copy = pltpu.make_async_copy(pair_ref, pair_hbm, semaphores.at[1])
    pair_copy.start()
    grad_copy.wait()
    pair_copy.wait()


def small_slice(
    homolog_matrix,
    standardizer_scaling,
    standardizer_offset,
    left_projection_matrix,
    left_offset_vector,
    right_projection_matrix,
    right_offset_vector,
    coupling_matrix,
    coupling_offset,
    coupling_cotangent,
):
    seqs, residues, features = homolog_matrix.shape
    depth = left_projection_matrix.shape[1]
    ranks = lax.axis_size("res")
    rows = seqs * residues
    scale = 1.0 / (seqs * lax.axis_size("seq"))
    rank = lax.axis_index("res")
    mine = lax.axis_index("seq")
    swap = [(0, 1), (1, 0)]
    limit = pltpu.CompilerParams(vmem_limit_bytes=8 * 1024 * 1024)
    vmem = pl.BlockSpec(memory_space=pltpu.VMEM)
    like = jax.ShapeDtypeStruct

    other_cot = lax.ppermute(coupling_cotangent, "seq", swap)
    hbm = pl.BlockSpec(memory_space=pltpu.HBM)
    pin = lambda array: pltpu.with_memory_space_constraint(array, pltpu.HBM)
    both, normed, inv_std, spread_w, gain, pair_offset, own_cot = pl.pallas_call(
        small_project_kernel,
        in_specs=[hbm] * 9,
        out_specs=[vmem] * 7,
        out_shape=(
            like((2, seqs, LANES), BF16),
            like((rows, features), F32),
            like((rows, LANES), F32),
            like((2 * LANES, features), BF16),
            like((1, features), F32),
            like((1, LANES), F32),
            like(coupling_cotangent.shape, BF16),
        ),
        scratch_shapes=[
            pltpu.VMEM(homolog_matrix.shape, BF16),
            pltpu.VMEM((1, features), F32),
            pltpu.VMEM((depth, features), BF16),
            pltpu.VMEM((1, depth), F32),
            pltpu.VMEM((depth, features), BF16),
            pltpu.VMEM((1, depth), F32),
            pltpu.VMEM((2, rows + 8, LANES), F32),
            pltpu.SemaphoreType.DMA((12,)),
        ],
        compiler_params=limit,
        name="project",
    )(
        *[
            pin(array)
            for array in (
                homolog_matrix,
                standardizer_scaling.reshape(1, -1),
                standardizer_offset.reshape(1, -1),
                left_projection_matrix.T,
                left_offset_vector.reshape(1, -1),
                right_projection_matrix.T,
                right_offset_vector.reshape(1, -1),
                coupling_offset.reshape(1, -1),
                coupling_cotangent,
            )
        ]
    )

    def swap_over(mask, value):
        return lax.ppermute(value, "res", [(source, source ^ mask) for source in range(ranks)])

    own_is_near = mine == lax.shift_right_logical(rank, 2)
    far_cot = jnp.where(own_is_near, other_cot, own_cot).reshape(2, seqs, LANES)
    beyond_two = swap_over(4, jnp.concatenate([both, far_cot]))

    half_rows = ranks // 2 * LANES
    turn = pltpu.VMEM((half_rows + depth, LANES), F32)
    keep, outer_near, outer_far, sorted_w, sorted_wt, columns_w = pl.pallas_call(
        functools.partial(small_own_kernel, scale),
        in_specs=[vmem] * 5,
        out_specs=[vmem] * 6,
        out_shape=(
            like((ranks // 2, seqs, LANES), F32),
            like((half_rows, LANES), BF16),
            like((half_rows, LANES), BF16),
            like(coupling_matrix.shape, BF16),
            like(coupling_matrix.shape[::-1], BF16),
            like((LANES, features), BF16),
        ),
        scratch_shapes=[
            [turn, turn],
            pltpu.VMEM((coupling_matrix.shape[0] + depth, LANES), F32),
        ],
        compiler_params=limit,
        name="own_pieces",
    )(own_cot, other_cot, coupling_matrix, both, spread_w)

    needed = jnp.where(own_is_near, beyond_two[1], both[1])
    swapped = lax.ppermute(jnp.stack([needed, both[0]]), "seq", swap)

    leaving_parts, keep, right = pl.pallas_call(
        functools.partial(small_partner_kernel, residues),
        in_specs=[vmem] * 4,
        out_specs=[vmem] * 3,
        out_shape=(
            like((ranks // 2, 3, seqs, LANES), BF16),
            like((ranks // 2, seqs, LANES), F32),
            like((2, seqs, LANES), BF16),
        ),
        compiler_params=limit,
        name="partner_pieces",
    )(beyond_two, sorted_wt, keep, both)

    diagonal = swap_over(3, leaving_parts[3])
    beside, across = [
        swap_over(mask, jnp.concatenate([leaving_parts[mask], swapped[0:1]])) for mask in (1, 2)
    ]
    swapped_late = lax.ppermute(
        jnp.where(own_is_near, diagonal[1], diagonal[0]), "seq", swap
    )

    pair_delta, gradient = pl.pallas_call(
        functools.partial(small_finish_kernel, scale),
        in_specs=[vmem, [vmem] * 3] + [vmem] * 13,
        out_specs=[pl.BlockSpec(memory_space=pl.ANY)] * 2,
        out_shape=(
            like(homolog_matrix.shape, BF16),
            like(coupling_cotangent.shape, BF16),
        ),
        scratch_shapes=[
            pltpu.VMEM(homolog_matrix.shape, BF16),
            pltpu.VMEM(coupling_cotangent.shape, BF16),
            pltpu.VMEM((ranks // 2, seqs, LANES), BF16),
            pltpu.VMEM((ranks // 2, seqs, LANES), BF16),
            turn,
            pltpu.VMEM((features // LANES, rows + 8, LANES), F32),
            pltpu.SemaphoreType.DMA((2,)),
        ],
        compiler_params=limit,
        name="finish",
    )(
        right,
        [across, beside, diagonal],
        swapped,
        swapped_late,
        both,
        outer_near,
        outer_far,
        keep,
        normed,
        inv_std,
        gain,
        spread_w,
        columns_w,
        sorted_w,
        pair_offset,
    )[::-1]
    return (pair_delta, gradient)


def body(*arrays):
    sequences = arrays[0].shape[0] * lax.axis_size("seq")
    if lax.axis_size("res") == 8 and sequences & (sequences - 1) == 0:
        return small_slice(*arrays)
    return wide_slice(*arrays)


def solution(mesh):
    return jax.shard_map(
        body,
        mesh=mesh,
        in_specs=(
            P(("grp", "seq"), "res", None),
            P(),
            P(),
            P(),
            P(),
            P(),
            P(),
            P(),
            P(),
            P(("grp", "res"), "seq", None),
        ),
        out_specs=(P(("grp", "res"), "seq", None), P(("grp", "seq"), "res", None)),
        check_vma=False,
    )
```

```python
import functools

import jax
import jax.numpy as jnp
from jax import lax
from jax.experimental import pallas as pl
from jax.experimental.pallas import tpu as pltpu
from jax.sharding import PartitionSpec as P

LANES = 128
BF16 = jnp.bfloat16
F32 = jnp.float32
NT = (((1,), (1,)), ((), ()))
TN = (((0,), (0,)), ((), ()))


def lane_block(shape, width):
    return lax.broadcasted_iota(jnp.int32, shape, 1) // width


def pick(blocks, pieces):
    result = pieces[0]
    for place in range(1, len(pieces)):
        result = jnp.where(blocks == place, pieces[place], result)
    return result


def split_three(value):
    top = value.astype(BF16)
    rest = value - top.astype(F32)
    middle = rest.astype(BF16)
    low = (rest - middle.astype(F32)).astype(BF16)
    return top, middle, low


def exchange_blocks(pieces, width):
    first, second, third, fourth = pieces
    blocks = lane_block(first.shape, width)
    odd, high = blocks % 2 == 1, blocks >= 2
    roll = lambda value, count: pltpu.roll(value, count * width, 1)
    first, second = jnp.where(odd, roll(second, 1), first), jnp.where(odd, second, roll(first, 3))
    third, fourth = jnp.where(odd, roll(fourth, 1), third), jnp.where(odd, fourth, roll(third, 3))
    return [
        jnp.where(high, roll(third, 2), first),
        jnp.where(high, roll(fourth, 2), second),
        jnp.where(high, third, roll(first, 2)),
        jnp.where(high, fourth, roll(second, 2)),
    ]


def split_two(value):
    top = value.astype(BF16)
    return top, (value - top.astype(F32)).astype(BF16)


def normalise(rows):
    centred = rows - jnp.mean(rows, axis=-1, keepdims=True)
    inv_std = lax.rsqrt(jnp.mean(centred * centred, axis=-1, keepdims=True) + 1e-05)
    return centred * inv_std, inv_std


def residue_rows(x_ref):
    return jnp.concatenate(
        [x_ref[:, place, :].astype(F32) for place in range(x_ref.shape[1])], axis=0
    )


def project_kernel(
    x_ref, gain_ref, offset_ref, left_w_ref, left_b_ref, right_w_ref, right_b_ref, w_ref,
    left_ref, right_ref, sorted_w_ref, wide_ref,
):
    seqs, residues, _ = x_ref.shape
    depth = left_w_ref.shape[0]
    normed, _ = normalise(residue_rows(x_ref))
    ln_out = (normed * gain_ref[...] + offset_ref[...]).astype(BF16)
    blocks = lane_block((seqs, LANES), depth)
    for weight_ref, bias_ref, out_ref in (
        (left_w_ref, left_b_ref, left_ref),
        (right_w_ref, right_b_ref, right_ref),
    ):
        weight = jnp.concatenate([weight_ref[...]] * residues, axis=0)
        bias = jnp.concatenate([bias_ref[...]] * residues, axis=1)
        wide = lax.dot_general(ln_out, weight, NT, preferred_element_type=F32)
        own = pick(blocks, [wide[p * seqs : (p + 1) * seqs] for p in range(residues)])
        out_ref[...] = (own + bias).astype(BF16)
    wide_ref[...] = w_ref[...].astype(F32)
    for d in range(depth):
        sorted_w_ref[d * depth : (d + 1) * depth, :] = wide_ref[
            pl.ds(d, depth, stride=depth), :
        ].astype(BF16)


def cot_kernel(scale, own_ref, other_ref, sorted_w_ref, left_ref, right_ref,
               send_ref, outer_ref, turn_ref):
    residues, columns, _ = own_ref.shape
    depth = sorted_w_ref.shape[0] // (LANES // residues)
    depth = LANES // residues
    first = lax.axis_index("seq") == 0
    own = own_ref[...].reshape(residues * columns, LANES)
    other = other_ref[...].reshape(residues * columns, LANES)
    low = jnp.where(first, own, other)
    high = jnp.where(first, other, own)
    both = jnp.concatenate([low, high], axis=0)
    flat = lax.dot_general(both, sorted_w_ref[...], NT, preferred_element_type=F32) * scale
    blocks = lane_block((columns, LANES), depth)
    for half in range(2):
        for tile in range(depth * depth // LANES):
            block = flat[
                half * residues * columns : (half + 1) * residues * columns,
                tile * LANES : (tile + 1) * LANES,
            ]
            turned = [block] + [pltpu.roll(block, depth * t, 1) for t in range(1, residues)]
            for e in range(residues):
                piece = pick(
                    blocks,
                    [
                        turned[(i - e) % residues][i * columns : (i + 1) * columns]
                        for i in range(residues)
                    ],
                )
                turn_ref[pl.ds(half * columns * depth + tile * residues + e, columns, stride=depth), :] = piece
    outer = turn_ref[...].astype(BF16)
    half_rows = columns * depth
    partial = lax.dot_general(left_ref[...], outer, NT, preferred_element_type=F32).astype(BF16)
    seqs = left_ref.shape[0]
    ranks = columns // residues
    for half in range(2):
        outer_ref[half] = outer[half * half_rows : (half + 1) * half_rows]
        for rank in range(ranks):
            at = (half * ranks + rank) * LANES
            send_ref[half, rank, 0:seqs, :] = right_ref[...]
            send_ref[half, rank, seqs : 2 * seqs, :] = partial[:, at : at + LANES]


def grad_kernel(steps, got_ref, outer_ref, x_ref, gain_ref, left_w_ref, right_w_ref,
                grad_ref, left_cot_ref, right_cot_ref):
    step = pl.program_id(0)
    _, ranks, twice, _ = got_ref.shape
    seqs = twice // 2
    residues = x_ref.shape[1]
    depth = LANES // residues

    @pl.when(step == 0)
    def _():
        left_cot_ref[...] = jnp.zeros_like(left_cot_ref)
        right_cot_ref[...] = jnp.zeros_like(right_cot_ref)

    places = [(half, rank) for half in range(2) for rank in range(ranks)]
    right_all = jnp.concatenate([got_ref[h, r, 0:seqs, :] for h, r in places], axis=1)
    outer = jnp.concatenate([outer_ref[0], outer_ref[1]], axis=0)
    left_cot_ref[...] += jnp.dot(right_all, outer, preferred_element_type=F32)
    total = got_ref[0, 0, seqs:twice, :].astype(F32)
    for h, r in places[1:]:
        total = total + got_ref[h, r, seqs:twice, :].astype(F32)
    right_cot_ref[...] += total

    @pl.when(step == steps - 1)
    def _():
        blocks = lane_block((seqs, LANES), depth)
        left_cot, right_cot = left_cot_ref[...], right_cot_ref[...]
        spread = jnp.concatenate(
            [
                jnp.concatenate(
                    [
                        jnp.where(blocks == place, left_cot, 0.0),
                        jnp.where(blocks == place, right_cot, 0.0),
                    ],
                    axis=1,
                )
                for place in range(residues)
            ],
            axis=0,
        )
        weight = jnp.concatenate(
            [left_w_ref[...]] * residues + [right_w_ref[...]] * residues, axis=0
        )
        rows = residues * seqs
        parts = jnp.concatenate(split_three(spread), axis=0)
        ln_cot = jnp.dot(parts, weight, preferred_element_type=F32)
        ln_cot = ln_cot[0:rows] + (ln_cot[rows : 2 * rows] + ln_cot[2 * rows : 3 * rows])
        gained = ln_cot * gain_ref[...]
        normed, inv_std = normalise(residue_rows(x_ref))
        grad = inv_std * (
            gained
            - jnp.mean(gained, axis=-1, keepdims=True)
            - normed * jnp.mean(gained * normed, axis=-1, keepdims=True)
        )
        for place in range(residues):
            grad_ref[:, place, :] = grad[place * seqs : (place + 1) * seqs].astype(BF16)


def pair_kernel(scale, got_ref, far_ref, left_ref, far_left_ref, sorted_w_ref, offset_ref,
                pair_ref, turn_ref):
    residues, columns, _ = pair_ref.shape
    depth = LANES // residues
    ranks = columns // residues
    mine = lax.axis_index("seq")
    near = jnp.concatenate([got_ref[mine, r] for r in range(ranks)], axis=1)
    far = jnp.concatenate([far_ref[r] for r in range(ranks)], axis=1)
    right = jnp.concatenate([near, far], axis=0)
    left = jnp.concatenate([left_ref[...], far_left_ref[...]], axis=0)
    turn_ref[...] = lax.dot_general(right, left, TN, preferred_element_type=F32) * scale
    blocks = lane_block((columns, LANES), depth)
    tiles = []
    for tile in range(depth * depth // LANES):
        pieces = [
            turn_ref[pl.ds(tile * residues + e, columns, stride=depth), :]
            for e in range(residues)
        ]
        rows = jnp.concatenate(pieces, axis=0)
        turned = [rows] + [pltpu.roll(rows, depth * t, 1) for t in range(1, residues)]
        tiles.append(
            jnp.concatenate(
                [
                    pick(
                        blocks,
                        [
                            turned[(e - i) % residues][e * columns : (e + 1) * columns]
                            for e in range(residues)
                        ],
                    )
                    for i in range(residues)
                ],
                axis=0,
            )
        )
    flat = jnp.concatenate(tiles, axis=1)
    rows = residues * columns
    parts = jnp.concatenate(split_three(flat), axis=0)
    pair = jnp.dot(parts, sorted_w_ref[...], preferred_element_type=F32)
    pair = pair[0:rows] + (pair[rows : 2 * rows] + pair[2 * rows : 3 * rows])
    pair_ref[...] = (pair + offset_ref[...]).astype(BF16).reshape(pair_ref.shape)


def wide_slice(
    homolog_matrix,
    standardizer_scaling,
    standardizer_offset,
    left_projection_matrix,
    left_offset_vector,
    right_projection_matrix,
    right_offset_vector,
    coupling_matrix,
    coupling_offset,
    coupling_cotangent,
):
    seqs, residues, features = homolog_matrix.shape
    depth = left_projection_matrix.shape[1]
    ranks = lax.axis_size("res")
    scale = 1.0 / (seqs * lax.axis_size("seq"))
    half_ranks = ranks // 2
    half_columns = half_ranks * residues
    step_ranks = 4
    columns = step_ranks * residues
    steps = half_ranks // step_ranks
    mine = lax.axis_index("seq")
    swap = [(0, 1), (1, 0)]

    other_cot = lax.ppermute(coupling_cotangent, "seq", swap)
    gain = standardizer_scaling.reshape(1, -1)
    left_w = left_projection_matrix.T
    right_w = right_projection_matrix.T

    left, right, sorted_w = pl.pallas_call(
        project_kernel,
        out_shape=(
            jax.ShapeDtypeStruct((seqs, LANES), BF16),
            jax.ShapeDtypeStruct((seqs, LANES), BF16),
            jax.ShapeDtypeStruct(coupling_matrix.shape, BF16),
        ),
        scratch_shapes=[pltpu.VMEM(coupling_matrix.shape, F32)],
        name="project",
    )(
        homolog_matrix,
        gain,
        standardizer_offset.reshape(1, -1),
        left_w,
        left_offset_vector.reshape(1, -1),
        right_w,
        right_offset_vector.reshape(1, -1),
        coupling_matrix,
    )

    whole = lambda shape: pl.BlockSpec(shape, lambda g: (0,) * len(shape))
    cot_block = pl.BlockSpec((residues, columns, LANES), lambda g: (0, g, 0))
    outer_block = pl.BlockSpec((2, columns * depth, LANES), lambda g: (0, g, 0))
    send_block = pl.BlockSpec((2, step_ranks, 2 * seqs, LANES), lambda g: (0, g, 0, 0))
    send, outer = pl.pallas_call(
        functools.partial(cot_kernel, scale),
        grid=(steps,),
        in_specs=[
            cot_block,
            cot_block,
            whole(sorted_w.shape),
            whole(left.shape),
            whole(right.shape),
        ],
        out_specs=(send_block, outer_block),
        out_shape=(
            jax.ShapeDtypeStruct((2, half_ranks, 2 * seqs, LANES), BF16),
            jax.ShapeDtypeStruct((2, half_columns * depth, LANES), BF16),
        ),
        scratch_shapes=[pltpu.VMEM((2 * columns * depth, LANES), F32)],
        name="cotangent",
    )(coupling_cotangent, other_cot, sorted_w, left, right)

    got = lax.all_to_all(
        send.reshape(ranks, 2 * seqs, LANES), "res", split_axis=0, concat_axis=0, tiled=True
    ).reshape(send.shape)

    leaving = lax.dynamic_index_in_dim(got, 1 - mine, 0, keepdims=False)[:, 0:seqs, :]
    far = lax.ppermute(jnp.concatenate([leaving, left[None]], axis=0), "seq", swap)

    gradient = pl.pallas_call(
        functools.partial(grad_kernel, steps),
        grid=(steps,),
        in_specs=[
            send_block,
            outer_block,
            whole(homolog_matrix.shape),
            whole(gain.shape),
            whole(left_w.shape),
            whole(right_w.shape),
        ],
        out_specs=whole(homolog_matrix.shape),
        out_shape=jax.ShapeDtypeStruct(homolog_matrix.shape, BF16),
        scratch_shapes=[pltpu.VMEM((seqs, LANES), F32)] * 2,
        name="gradient",
    )(got, outer, homolog_matrix, gain, left_w, right_w)

    pair_delta = pl.pallas_call(
        functools.partial(pair_kernel, scale),
        grid=(steps,),
        in_specs=[
            pl.BlockSpec((2, step_ranks, seqs, LANES), lambda g: (0, g, 0, 0)),
            pl.BlockSpec((step_ranks, seqs, LANES), lambda g: (g, 0, 0)),
            whole(left.shape),
            pl.BlockSpec((None, seqs, LANES), lambda g: (half_ranks, 0, 0)),
            whole(sorted_w.shape),
            whole((1, LANES)),
        ],
        out_specs=cot_block,
        out_shape=jax.ShapeDtypeStruct(coupling_cotangent.shape, BF16),
        scratch_shapes=[pltpu.VMEM((columns * depth, LANES), F32)],
        name="pair",
    )(got, far, left, far, sorted_w, coupling_offset.reshape(1, -1))
    return (pair_delta, gradient)


def fetch(source, target, semaphore):
    copy = pltpu.make_async_copy(source, target, semaphore)
    copy.start()
    return copy


def start_copies(pairs, semaphores):
    copies = [
        pltpu.make_async_copy(source, target, semaphores.at[place])
        for place, (source, target) in enumerate(pairs)
    ]
    for copy in copies:
        copy.start()
    return copies


def small_project_kernel(
    x_hbm, gain_hbm, offset_hbm, left_w_hbm, left_b_hbm, right_w_hbm, right_b_hbm, pair_offset_hbm,
    cot_hbm, both_ref, normed_ref, inv_std_ref, spread_w_ref, gain_ref, pair_offset_ref, cot_ref,
    x_ref, offset_ref, left_w_ref, left_b_ref, right_w_ref, right_b_ref, wide_ref, semaphores,
):
    seqs, residues, _ = x_ref.shape
    depth = left_w_ref.shape[0]
    parts = 4
    part = seqs // parts
    copies = start_copies(
        tuple(
            (x_hbm.at[pl.ds(place * part, part)], x_ref.at[pl.ds(place * part, part)])
            for place in range(parts)
        )
        + (
            (left_w_hbm, left_w_ref),
            (right_w_hbm, right_w_ref),
            (gain_hbm, gain_ref),
            (offset_hbm, offset_ref),
            (left_b_hbm, left_b_ref),
            (right_b_hbm, right_b_ref),
            (cot_hbm, cot_ref),
            (pair_offset_hbm, pair_offset_ref),
        ),
        semaphores,
    )
    for copy in copies[:parts]:
        copy.wait()
    rows = x_ref[...].astype(F32).reshape(seqs * residues, x_ref.shape[2])
    normed, inv_std = normalise(rows)
    for copy in copies[parts:]:
        copy.wait()
    ln_out = (normed * gain_ref[...] + offset_ref[...]).astype(BF16)
    blocks = lane_block((seqs, LANES), depth)
    weight = jnp.concatenate(
        [left_w_ref[...]] * residues + [right_w_ref[...]] * residues, axis=0
    )
    wide = lax.dot_general(ln_out, weight, NT, preferred_element_type=F32)
    for place, bias_ref in enumerate((left_b_ref, right_b_ref)):
        bias = jnp.concatenate([bias_ref[...]] * residues, axis=1)
        wide_ref[place, 0 : seqs * residues, :] = wide[:, place * LANES : (place + 1) * LANES]
        own = pick(
            blocks, [wide_ref[place, pl.ds(p, seqs, stride=residues), :] for p in range(residues)]
        )
        both_ref[place] = (own + bias).astype(BF16)
    normed_ref[...] = normed
    inv_std_ref[...] = jnp.broadcast_to(inv_std, inv_std_ref.shape)
    spread_w_ref[...] = weight


def outer_flat(cot, sorted_wt_ref):
    return jnp.dot(cot, sorted_wt_ref[...], preferred_element_type=F32)


def outer_rows(flat, residues, turn_ref):
    columns = flat.shape[0] // residues
    depth = LANES // residues
    for tile in range(depth * depth // LANES):
        block = flat[:, tile * LANES : (tile + 1) * LANES]
        turned = exchange_blocks(
            [block[i * columns : (i + 1) * columns] for i in range(residues)], depth
        )
        for e in range(residues):
            turn_ref[pl.ds(tile * residues + e, columns, stride=depth), :] = turned[e]
    return turn_ref[0 : columns * depth, :].astype(BF16)


def outer_tiles(flat, residues):
    columns = flat.shape[0] // residues
    return jnp.concatenate(
        [
            jnp.concatenate(
                [
                    flat[i * columns + start : i * columns + start + 8, tile : tile + LANES]
                    for start in range(0, columns, 8)
                    for tile in range(0, flat.shape[1], LANES)
                ],
                axis=0,
            )
            for i in range(residues)
        ],
        axis=1,
    ).astype(BF16)


def blocks_apart(left, residues):
    depth = LANES // residues
    left = left.astype(F32)
    turned = [left] + [pltpu.roll(left, depth * t, 1) for t in range(1, residues)]
    blocks = lane_block(left.shape, depth)
    return jnp.concatenate(
        [
            jnp.concatenate(
                [
                    jnp.where(blocks == e, turned[(e - i) % residues], 0.0).astype(BF16)
                    for i in range(residues)
                ],
                axis=1,
            )
            for e in range(residues)
        ],
        axis=0,
    )


def column_pieces(left, outer, residues):
    seqs = left.shape[0]
    partial = lax.dot_general(
        blocks_apart(left, residues), outer, NT, preferred_element_type=F32
    )
    rows = [partial[e * seqs : (e + 1) * seqs] for e in range(residues)]
    half = lane_block(rows[0].shape, LANES // 2)
    source = 2 * (lane_block(rows[0].shape, residues) % 2) + half
    pieces = []
    for chip in range(residues):
        turned = []
        for e, row in enumerate(rows):
            count = (LANES // 2 * (e % 2 - chip // 2) + residues * (e // 2 - chip % 2)) % LANES
            turned.append(pltpu.roll(row, count, 1) if count else row)
        pieces.append(pick(source, turned))
    return pieces


def small_own_kernel(scale, own_ref, other_ref, w_ref, both_ref, spread_w_ref,
                     keep_ref, outer_near_ref, outer_far_ref, sorted_w_ref, sorted_wt_ref,
                     columns_w_ref, turn_refs, wide_ref):
    residues, columns, _ = own_ref.shape
    depth = LANES // residues
    wide_ref[0 : w_ref.shape[0], :] = w_ref[...].astype(F32)
    for d in range(depth):
        sorted_w_ref[d * depth : (d + 1) * depth, :] = wide_ref[
            pl.ds(d, depth, stride=depth), :
        ].astype(BF16)
    sorted_wt_ref[...] = (sorted_w_ref[...].astype(F32) * scale).astype(BF16).T
    shape = (columns_w_ref.shape[0], depth)
    row = lax.broadcasted_iota(jnp.int32, shape, 0)
    lane = lax.broadcasted_iota(jnp.int32, shape, 1)
    place = (row >> 3 & 7) * residues + 2 * (row >> 2 & 1) + (row >> 6)
    chosen = jnp.where(lane == place, 1.0, 0.0).astype(BF16)
    columns_w_ref[...] = jnp.dot(
        chosen, spread_w_ref[LANES : LANES + depth, :], preferred_element_type=F32
    ).astype(BF16)

    rank = lax.axis_index("res")
    own_is_near = lax.axis_index("seq") == lax.shift_right_logical(rank, 2)
    own = own_ref[...].reshape(residues * columns, LANES)
    other = other_ref[...].reshape(residues * columns, LANES)
    flat = outer_flat(jnp.where(own_is_near, own, other), sorted_wt_ref)
    pieces = column_pieces(both_ref[0], outer_tiles(flat, residues), residues)
    for place, piece in enumerate(pieces):
        keep_ref[place] = piece
    outer_near_ref[...] = outer_rows(flat, residues, turn_refs[0])
    flat = outer_flat(jnp.where(own_is_near, other, own), sorted_wt_ref)
    outer_far_ref[...] = outer_rows(flat, residues, turn_refs[1])


def small_partner_kernel(residues, got_ref, sorted_wt_ref, keep_ref, both_ref,
                         leaving_ref, keep_out_ref, right_ref):
    rank = lax.axis_index("res")
    seqs = got_ref.shape[1]
    cot = got_ref[2:4].reshape(2 * seqs, LANES)
    outer = outer_tiles(outer_flat(cot, sorted_wt_ref), residues)
    pieces = column_pieces(got_ref[0], outer, residues)
    right_ref[0] = both_ref[1]
    right_ref[1] = got_ref[1]
    for place, piece in enumerate(pieces):
        distance = lax.bitwise_xor(rank & 3, place)
        total = keep_ref[place] + piece
        keep_out_ref[distance] = total
        leaving_ref[distance, 2] = total.astype(BF16)
    for place in range(leaving_ref.shape[0]):
        leaving_ref[place, 0] = both_ref[1]
        leaving_ref[place, 1] = got_ref[1]


def small_finish_kernel(
    scale, right_ref, part_refs, swapped_ref, swapped_late_ref, both_ref, outer_near_ref, outer_far_ref,
    keep_ref, normed_ref, inv_std_ref, gain_ref, spread_w_ref, columns_w_ref, sorted_w_ref, offset_ref,
    grad_hbm, pair_hbm, grad_ref, pair_ref, near_ref, beyond_ref, turn_ref, lines_ref, semaphores,
):
    seqs, residues, _ = grad_ref.shape
    columns = pair_ref.shape[1]
    depth = LANES // residues
    ranks = columns // residues
    rank = lax.axis_index("res")
    mine = lax.axis_index("seq")
    here = rank & 3

    blocks_of = [right_ref] + list(part_refs)
    right_all = jnp.concatenate(
        [ref[0] for ref in blocks_of] + [ref[1] for ref in blocks_of], axis=1
    )
    spots = [
        pl.ds(pl.multiple_of(lax.bitwise_xor(here, mask) * LANES, LANES), LANES)
        for mask in range(ranks)
    ]
    outer = jnp.concatenate(
        [outer_near_ref[spot, :] for spot in spots] + [outer_far_ref[spot, :] for spot in spots],
        axis=0,
    )
    left_cot = jnp.dot(right_all, outer, preferred_element_type=F32)
    right_cot = keep_ref[0]
    for part_ref in part_refs:
        right_cot = right_cot + part_ref[2].astype(F32)
    blocks = lane_block((seqs, LANES), depth)
    column = lane_block((seqs, LANES), 1) % residues
    spread = jnp.concatenate(
        [
            jnp.concatenate(
                [
                    jnp.where(blocks == place, left_cot, 0.0),
                    jnp.where(column == place, right_cot, 0.0),
                ],
                axis=1,
            )
            for place in range(residues)
        ],
        axis=0,
    )
    rows = residues * seqs
    parts = jnp.concatenate(split_two(spread), axis=0)
    weight = jnp.concatenate([spread_w_ref[0:LANES, :], columns_w_ref[...]], axis=0)
    ln_cot = jnp.dot(parts, weight, preferred_element_type=F32)
    ln_cot = ln_cot[0:rows] + ln_cot[rows : 2 * rows]
    tiles = range(lines_ref.shape[0])
    for place in range(residues):
        for tile in tiles:
            lines_ref[tile, pl.ds(place, seqs, stride=residues), :] = ln_cot[
                place * seqs : (place + 1) * seqs, tile * LANES : (tile + 1) * LANES
            ]
    gained = jnp.concatenate([lines_ref[tile, 0:rows, :] for tile in tiles], axis=1) * gain_ref[...]
    normed = normed_ref[...]
    grad = inv_std_ref[:, 0:1] * (
        gained
        - jnp.mean(gained, axis=-1, keepdims=True)
        - normed * jnp.mean(gained * normed, axis=-1, keepdims=True)
    )
    grad_ref[...] = grad.reshape(grad_ref.shape).astype(BF16)
    grad_copy = pltpu.make_async_copy(grad_ref, grad_hbm, semaphores.at[0])
    grad_copy.start()

    half = jnp.where(mine == lax.shift_right_logical(rank, 2), 0, 1)
    for mask, ref in enumerate(blocks_of):
        near_ref[mask] = ref[half]
    beyond_ref[0] = swapped_ref[0]
    beyond_ref[1] = part_refs[0][3]
    beyond_ref[2] = part_refs[1][3]
    beyond_ref[3] = swapped_late_ref[...]
    masks = [lax.bitwise_xor(here, place) for place in range(ranks)]
    right = jnp.concatenate(
        [
            jnp.concatenate([ref[mask] for mask in masks], axis=1)
            for ref in (near_ref, beyond_ref)
        ],
        axis=0,
    )
    left = jnp.concatenate([both_ref[0], swapped_ref[1]], axis=0)
    turn_ref[0 : columns * depth, :] = lax.dot_general(right, left, TN, preferred_element_type=F32) * scale
    tiles = []
    for tile in range(depth * depth // LANES):
        turned = exchange_blocks(
            [
                turn_ref[pl.ds(tile * residues + e, columns, stride=depth), :]
                for e in range(residues)
            ],
            depth,
        )
        tiles.append(jnp.concatenate(turned, axis=0))
    flat = jnp.concatenate(tiles, axis=1)
    rows = residues * columns
    parts = jnp.concatenate(split_two(flat), axis=0)
    pair = jnp.dot(parts, sorted_w_ref[...], preferred_element_type=F32)
    pair = pair[0:rows] + pair[rows : 2 * rows]
    pair_ref[...] = (pair + offset_ref[...]).astype(BF16).reshape(pair_ref.shape)
    pair_copy = pltpu.make_async_copy(pair_ref, pair_hbm, semaphores.at[1])
    pair_copy.start()
    grad_copy.wait()
    pair_copy.wait()


def small_slice(
    homolog_matrix,
    standardizer_scaling,
    standardizer_offset,
    left_projection_matrix,
    left_offset_vector,
    right_projection_matrix,
    right_offset_vector,
    coupling_matrix,
    coupling_offset,
    coupling_cotangent,
):
    seqs, residues, features = homolog_matrix.shape
    depth = left_projection_matrix.shape[1]
    ranks = lax.axis_size("res")
    rows = seqs * residues
    scale = 1.0 / (seqs * lax.axis_size("seq"))
    rank = lax.axis_index("res")
    mine = lax.axis_index("seq")
    swap = [(0, 1), (1, 0)]
    limit = pltpu.CompilerParams(vmem_limit_bytes=8 * 1024 * 1024)
    vmem = pl.BlockSpec(memory_space=pltpu.VMEM)
    like = jax.ShapeDtypeStruct

    other_cot = lax.ppermute(coupling_cotangent, "seq", swap)
    hbm = pl.BlockSpec(memory_space=pltpu.HBM)
    pin = lambda array: pltpu.with_memory_space_constraint(array, pltpu.HBM)
    both, normed, inv_std, spread_w, gain, pair_offset, own_cot = pl.pallas_call(
        small_project_kernel,
        in_specs=[hbm] * 9,
        out_specs=[vmem] * 7,
        out_shape=(
            like((2, seqs, LANES), BF16),
            like((rows, features), F32),
            like((rows, LANES), F32),
            like((2 * LANES, features), BF16),
            like((1, features), F32),
            like((1, LANES), F32),
            like(coupling_cotangent.shape, BF16),
        ),
        scratch_shapes=[
            pltpu.VMEM(homolog_matrix.shape, BF16),
            pltpu.VMEM((1, features), F32),
            pltpu.VMEM((depth, features), BF16),
            pltpu.VMEM((1, depth), F32),
            pltpu.VMEM((depth, features), BF16),
            pltpu.VMEM((1, depth), F32),
            pltpu.VMEM((2, rows + 8, LANES), F32),
            pltpu.SemaphoreType.DMA((12,)),
        ],
        compiler_params=limit,
        name="project",
    )(
        *[
            pin(array)
            for array in (
                homolog_matrix,
                standardizer_scaling.reshape(1, -1),
                standardizer_offset.reshape(1, -1),
                left_projection_matrix.T,
                left_offset_vector.reshape(1, -1),
                right_projection_matrix.T,
                right_offset_vector.reshape(1, -1),
                coupling_offset.reshape(1, -1),
                coupling_cotangent,
            )
        ]
    )

    def swap_over(mask, value):
        return lax.ppermute(value, "res", [(source, source ^ mask) for source in range(ranks)])

    own_is_near = mine == lax.shift_right_logical(rank, 2)
    far_cot = jnp.where(own_is_near, other_cot, own_cot).reshape(2, seqs, LANES)
    beyond_two = swap_over(4, jnp.concatenate([both, far_cot]))

    half_rows = ranks // 2 * LANES
    turn = pltpu.VMEM((half_rows + depth, LANES), F32)
    keep, outer_near, outer_far, sorted_w, sorted_wt, columns_w = pl.pallas_call(
        functools.partial(small_own_kernel, scale),
        in_specs=[vmem] * 5,
        out_specs=[vmem] * 6,
        out_shape=(
            like((ranks // 2, seqs, LANES), F32),
            like((half_rows, LANES), BF16),
            like((half_rows, LANES), BF16),
            like(coupling_matrix.shape, BF16),
            like(coupling_matrix.shape[::-1], BF16),
            like((LANES, features), BF16),
        ),
        scratch_shapes=[
            [turn, turn],
            pltpu.VMEM((coupling_matrix.shape[0] + depth, LANES), F32),
        ],
        compiler_params=limit,
        name="own_pieces",
    )(own_cot, other_cot, coupling_matrix, both, spread_w)

    needed = jnp.where(own_is_near, beyond_two[1], both[1])
    swapped = lax.ppermute(jnp.stack([needed, both[0]]), "seq", swap)

    leaving_parts, keep, right = pl.pallas_call(
        functools.partial(small_partner_kernel, residues),
        in_specs=[vmem] * 4,
        out_specs=[vmem] * 3,
        out_shape=(
            like((ranks // 2, 3, seqs, LANES), BF16),
            like((ranks // 2, seqs, LANES), F32),
            like((2, seqs, LANES), BF16),
        ),
        compiler_params=limit,
        name="partner_pieces",
    )(beyond_two, sorted_wt, keep, both)

    diagonal = swap_over(3, leaving_parts[3])
    beside, across = [
        swap_over(mask, jnp.concatenate([leaving_parts[mask], swapped[0:1]])) for mask in (1, 2)
    ]
    swapped_late = lax.ppermute(
        jnp.where(own_is_near, diagonal[1], diagonal[0]), "seq", swap
    )

    pair_delta, gradient = pl.pallas_call(
        functools.partial(small_finish_kernel, scale),
        in_specs=[vmem, [vmem] * 3] + [vmem] * 13,
        out_specs=[pl.BlockSpec(memory_space=pl.ANY)] * 2,
        out_shape=(
            like(homolog_matrix.shape, BF16),
            like(coupling_cotangent.shape, BF16),
        ),
        scratch_shapes=[
            pltpu.VMEM(homolog_matrix.shape, BF16),
            pltpu.VMEM(coupling_cotangent.shape, BF16),
            pltpu.VMEM((ranks // 2, seqs, LANES), BF16),
            pltpu.VMEM((ranks // 2, seqs, LANES), BF16),
            turn,
            pltpu.VMEM((features // LANES, rows + 8, LANES), F32),
            pltpu.SemaphoreType.DMA((2,)),
        ],
        compiler_params=limit,
        name="finish",
    )(
        right,
        [beside, across, diagonal],
        swapped,
        swapped_late,
        both,
        outer_near,
        outer_far,
        keep,
        normed,
        inv_std,
        gain,
        spread_w,
        columns_w,
        sorted_w,
        pair_offset,
    )[::-1]
    return (pair_delta, gradient)


def body(*arrays):
    sequences = arrays[0].shape[0] * lax.axis_size("seq")
    if lax.axis_size("res") == 8 and sequences & (sequences - 1) == 0:
        return small_slice(*arrays)
    return wide_slice(*arrays)


def solution(mesh):
    return jax.shard_map(
        body,
        mesh=mesh,
        in_specs=(
            P(("grp", "seq"), "res", None),
            P(),
            P(),
            P(),
            P(),
            P(),
            P(),
            P(),
            P(),
            P(("grp", "res"), "seq", None),
        ),
        out_specs=(P(("grp", "res"), "seq", None), P(("grp", "seq"), "res", None)),
        check_vma=False,
    )
```

```python
import functools

import jax
import jax.numpy as jnp
from jax import lax
from jax.experimental import pallas as pl
from jax.experimental.pallas import tpu as pltpu
from jax.sharding import PartitionSpec as P

LANES = 128
BF16 = jnp.bfloat16
F32 = jnp.float32
NT = (((1,), (1,)), ((), ()))
TN = (((0,), (0,)), ((), ()))


def lane_block(shape, width):
    return lax.broadcasted_iota(jnp.int32, shape, 1) // width


def pick(blocks, pieces):
    result = pieces[0]
    for place in range(1, len(pieces)):
        result = jnp.where(blocks == place, pieces[place], result)
    return result


def split_three(value):
    top = value.astype(BF16)
    rest = value - top.astype(F32)
    middle = rest.astype(BF16)
    low = (rest - middle.astype(F32)).astype(BF16)
    return top, middle, low


def exchange_blocks(pieces, width):
    first, second, third, fourth = pieces
    blocks = lane_block(first.shape, width)
    odd, high = blocks % 2 == 1, blocks >= 2
    roll = lambda value, count: pltpu.roll(value, count * width, 1)
    first, second = jnp.where(odd, roll(second, 1), first), jnp.where(odd, second, roll(first, 3))
    third, fourth = jnp.where(odd, roll(fourth, 1), third), jnp.where(odd, fourth, roll(third, 3))
    return [
        jnp.where(high, roll(third, 2), first),
        jnp.where(high, roll(fourth, 2), second),
        jnp.where(high, third, roll(first, 2)),
        jnp.where(high, fourth, roll(second, 2)),
    ]


def split_two(value):
    top = value.astype(BF16)
    return top, (value - top.astype(F32)).astype(BF16)


def normalise(rows):
    centred = rows - jnp.mean(rows, axis=-1, keepdims=True)
    inv_std = lax.rsqrt(jnp.mean(centred * centred, axis=-1, keepdims=True) + 1e-05)
    return centred * inv_std, inv_std


def residue_rows(x_ref):
    return jnp.concatenate(
        [x_ref[:, place, :].astype(F32) for place in range(x_ref.shape[1])], axis=0
    )


def project_kernel(
    x_ref, gain_ref, offset_ref, left_w_ref, left_b_ref, right_w_ref, right_b_ref, w_ref,
    left_ref, right_ref, sorted_w_ref, wide_ref,
):
    seqs, residues, _ = x_ref.shape
    depth = left_w_ref.shape[0]
    normed, _ = normalise(residue_rows(x_ref))
    ln_out = (normed * gain_ref[...] + offset_ref[...]).astype(BF16)
    blocks = lane_block((seqs, LANES), depth)
    for weight_ref, bias_ref, out_ref in (
        (left_w_ref, left_b_ref, left_ref),
        (right_w_ref, right_b_ref, right_ref),
    ):
        weight = jnp.concatenate([weight_ref[...]] * residues, axis=0)
        bias = jnp.concatenate([bias_ref[...]] * residues, axis=1)
        wide = lax.dot_general(ln_out, weight, NT, preferred_element_type=F32)
        own = pick(blocks, [wide[p * seqs : (p + 1) * seqs] for p in range(residues)])
        out_ref[...] = (own + bias).astype(BF16)
    wide_ref[...] = w_ref[...].astype(F32)
    for d in range(depth):
        sorted_w_ref[d * depth : (d + 1) * depth, :] = wide_ref[
            pl.ds(d, depth, stride=depth), :
        ].astype(BF16)


def cot_kernel(scale, own_ref, other_ref, sorted_w_ref, left_ref, right_ref,
               send_ref, outer_ref, turn_ref):
    residues, columns, _ = own_ref.shape
    depth = sorted_w_ref.shape[0] // (LANES // residues)
    depth = LANES // residues
    first = lax.axis_index("seq") == 0
    own = own_ref[...].reshape(residues * columns, LANES)
    other = other_ref[...].reshape(residues * columns, LANES)
    low = jnp.where(first, own, other)
    high = jnp.where(first, other, own)
    both = jnp.concatenate([low, high], axis=0)
    flat = lax.dot_general(both, sorted_w_ref[...], NT, preferred_element_type=F32) * scale
    blocks = lane_block((columns, LANES), depth)
    for half in range(2):
        for tile in range(depth * depth // LANES):
            block = flat[
                half * residues * columns : (half + 1) * residues * columns,
                tile * LANES : (tile + 1) * LANES,
            ]
            turned = [block] + [pltpu.roll(block, depth * t, 1) for t in range(1, residues)]
            for e in range(residues):
                piece = pick(
                    blocks,
                    [
                        turned[(i - e) % residues][i * columns : (i + 1) * columns]
                        for i in range(residues)
                    ],
                )
                turn_ref[pl.ds(half * columns * depth + tile * residues + e, columns, stride=depth), :] = piece
    outer = turn_ref[...].astype(BF16)
    half_rows = columns * depth
    partial = lax.dot_general(left_ref[...], outer, NT, preferred_element_type=F32).astype(BF16)
    seqs = left_ref.shape[0]
    ranks = columns // residues
    for half in range(2):
        outer_ref[half] = outer[half * half_rows : (half + 1) * half_rows]
        for rank in range(ranks):
            at = (half * ranks + rank) * LANES
            send_ref[half, rank, 0:seqs, :] = right_ref[...]
            send_ref[half, rank, seqs : 2 * seqs, :] = partial[:, at : at + LANES]


def grad_kernel(steps, got_ref, outer_ref, x_ref, gain_ref, left_w_ref, right_w_ref,
                grad_ref, left_cot_ref, right_cot_ref):
    step = pl.program_id(0)
    _, ranks, twice, _ = got_ref.shape
    seqs = twice // 2
    residues = x_ref.shape[1]
    depth = LANES // residues

    @pl.when(step == 0)
    def _():
        left_cot_ref[...] = jnp.zeros_like(left_cot_ref)
        right_cot_ref[...] = jnp.zeros_like(right_cot_ref)

    places = [(half, rank) for half in range(2) for rank in range(ranks)]
    right_all = jnp.concatenate([got_ref[h, r, 0:seqs, :] for h, r in places], axis=1)
    outer = jnp.concatenate([outer_ref[0], outer_ref[1]], axis=0)
    left_cot_ref[...] += jnp.dot(right_all, outer, preferred_element_type=F32)
    total = got_ref[0, 0, seqs:twice, :].astype(F32)
    for h, r in places[1:]:
        total = total + got_ref[h, r, seqs:twice, :].astype(F32)
    right_cot_ref[...] += total

    @pl.when(step == steps - 1)
    def _():
        blocks = lane_block((seqs, LANES), depth)
        left_cot, right_cot = left_cot_ref[...], right_cot_ref[...]
        spread = jnp.concatenate(
            [
                jnp.concatenate(
                    [
                        jnp.where(blocks == place, left_cot, 0.0),
                        jnp.where(blocks == place, right_cot, 0.0),
                    ],
                    axis=1,
                )
                for place in range(residues)
            ],
            axis=0,
        )
        weight = jnp.concatenate(
            [left_w_ref[...]] * residues + [right_w_ref[...]] * residues, axis=0
        )
        rows = residues * seqs
        parts = jnp.concatenate(split_three(spread), axis=0)
        ln_cot = jnp.dot(parts, weight, preferred_element_type=F32)
        ln_cot = ln_cot[0:rows] + (ln_cot[rows : 2 * rows] + ln_cot[2 * rows : 3 * rows])
        gained = ln_cot * gain_ref[...]
        normed, inv_std = normalise(residue_rows(x_ref))
        grad = inv_std * (
            gained
            - jnp.mean(gained, axis=-1, keepdims=True)
            - normed * jnp.mean(gained * normed, axis=-1, keepdims=True)
        )
        for place in range(residues):
            grad_ref[:, place, :] = grad[place * seqs : (place + 1) * seqs].astype(BF16)


def pair_kernel(scale, got_ref, far_ref, left_ref, far_left_ref, sorted_w_ref, offset_ref,
                pair_ref, turn_ref):
    residues, columns, _ = pair_ref.shape
    depth = LANES // residues
    ranks = columns // residues
    mine = lax.axis_index("seq")
    near = jnp.concatenate([got_ref[mine, r] for r in range(ranks)], axis=1)
    far = jnp.concatenate([far_ref[r] for r in range(ranks)], axis=1)
    right = jnp.concatenate([near, far], axis=0)
    left = jnp.concatenate([left_ref[...], far_left_ref[...]], axis=0)
    turn_ref[...] = lax.dot_general(right, left, TN, preferred_element_type=F32) * scale
    blocks = lane_block((columns, LANES), depth)
    tiles = []
    for tile in range(depth * depth // LANES):
        pieces = [
            turn_ref[pl.ds(tile * residues + e, columns, stride=depth), :]
            for e in range(residues)
        ]
        rows = jnp.concatenate(pieces, axis=0)
        turned = [rows] + [pltpu.roll(rows, depth * t, 1) for t in range(1, residues)]
        tiles.append(
            jnp.concatenate(
                [
                    pick(
                        blocks,
                        [
                            turned[(e - i) % residues][e * columns : (e + 1) * columns]
                            for e in range(residues)
                        ],
                    )
                    for i in range(residues)
                ],
                axis=0,
            )
        )
    flat = jnp.concatenate(tiles, axis=1)
    rows = residues * columns
    parts = jnp.concatenate(split_three(flat), axis=0)
    pair = jnp.dot(parts, sorted_w_ref[...], preferred_element_type=F32)
    pair = pair[0:rows] + (pair[rows : 2 * rows] + pair[2 * rows : 3 * rows])
    pair_ref[...] = (pair + offset_ref[...]).astype(BF16).reshape(pair_ref.shape)


def wide_slice(
    homolog_matrix,
    standardizer_scaling,
    standardizer_offset,
    left_projection_matrix,
    left_offset_vector,
    right_projection_matrix,
    right_offset_vector,
    coupling_matrix,
    coupling_offset,
    coupling_cotangent,
):
    seqs, residues, features = homolog_matrix.shape
    depth = left_projection_matrix.shape[1]
    ranks = lax.axis_size("res")
    scale = 1.0 / (seqs * lax.axis_size("seq"))
    half_ranks = ranks // 2
    half_columns = half_ranks * residues
    step_ranks = 4
    columns = step_ranks * residues
    steps = half_ranks // step_ranks
    mine = lax.axis_index("seq")
    swap = [(0, 1), (1, 0)]

    other_cot = lax.ppermute(coupling_cotangent, "seq", swap)
    gain = standardizer_scaling.reshape(1, -1)
    left_w = left_projection_matrix.T
    right_w = right_projection_matrix.T

    left, right, sorted_w = pl.pallas_call(
        project_kernel,
        out_shape=(
            jax.ShapeDtypeStruct((seqs, LANES), BF16),
            jax.ShapeDtypeStruct((seqs, LANES), BF16),
            jax.ShapeDtypeStruct(coupling_matrix.shape, BF16),
        ),
        scratch_shapes=[pltpu.VMEM(coupling_matrix.shape, F32)],
        name="project",
    )(
        homolog_matrix,
        gain,
        standardizer_offset.reshape(1, -1),
        left_w,
        left_offset_vector.reshape(1, -1),
        right_w,
        right_offset_vector.reshape(1, -1),
        coupling_matrix,
    )

    whole = lambda shape: pl.BlockSpec(shape, lambda g: (0,) * len(shape))
    cot_block = pl.BlockSpec((residues, columns, LANES), lambda g: (0, g, 0))
    outer_block = pl.BlockSpec((2, columns * depth, LANES), lambda g: (0, g, 0))
    send_block = pl.BlockSpec((2, step_ranks, 2 * seqs, LANES), lambda g: (0, g, 0, 0))
    send, outer = pl.pallas_call(
        functools.partial(cot_kernel, scale),
        grid=(steps,),
        in_specs=[
            cot_block,
            cot_block,
            whole(sorted_w.shape),
            whole(left.shape),
            whole(right.shape),
        ],
        out_specs=(send_block, outer_block),
        out_shape=(
            jax.ShapeDtypeStruct((2, half_ranks, 2 * seqs, LANES), BF16),
            jax.ShapeDtypeStruct((2, half_columns * depth, LANES), BF16),
        ),
        scratch_shapes=[pltpu.VMEM((2 * columns * depth, LANES), F32)],
        name="cotangent",
    )(coupling_cotangent, other_cot, sorted_w, left, right)

    got = lax.all_to_all(
        send.reshape(ranks, 2 * seqs, LANES), "res", split_axis=0, concat_axis=0, tiled=True
    ).reshape(send.shape)

    leaving = lax.dynamic_index_in_dim(got, 1 - mine, 0, keepdims=False)[:, 0:seqs, :]
    far = lax.ppermute(jnp.concatenate([leaving, left[None]], axis=0), "seq", swap)

    gradient = pl.pallas_call(
        functools.partial(grad_kernel, steps),
        grid=(steps,),
        in_specs=[
            send_block,
            outer_block,
            whole(homolog_matrix.shape),
            whole(gain.shape),
            whole(left_w.shape),
            whole(right_w.shape),
        ],
        out_specs=whole(homolog_matrix.shape),
        out_shape=jax.ShapeDtypeStruct(homolog_matrix.shape, BF16),
        scratch_shapes=[pltpu.VMEM((seqs, LANES), F32)] * 2,
        name="gradient",
    )(got, outer, homolog_matrix, gain, left_w, right_w)

    pair_delta = pl.pallas_call(
        functools.partial(pair_kernel, scale),
        grid=(steps,),
        in_specs=[
            pl.BlockSpec((2, step_ranks, seqs, LANES), lambda g: (0, g, 0, 0)),
            pl.BlockSpec((step_ranks, seqs, LANES), lambda g: (g, 0, 0)),
            whole(left.shape),
            pl.BlockSpec((None, seqs, LANES), lambda g: (half_ranks, 0, 0)),
            whole(sorted_w.shape),
            whole((1, LANES)),
        ],
        out_specs=cot_block,
        out_shape=jax.ShapeDtypeStruct(coupling_cotangent.shape, BF16),
        scratch_shapes=[pltpu.VMEM((columns * depth, LANES), F32)],
        name="pair",
    )(got, far, left, far, sorted_w, coupling_offset.reshape(1, -1))
    return (pair_delta, gradient)


def fetch(source, target, semaphore):
    copy = pltpu.make_async_copy(source, target, semaphore)
    copy.start()
    return copy


def start_copies(pairs, semaphores):
    copies = [
        pltpu.make_async_copy(source, target, semaphores.at[place])
        for place, (source, target) in enumerate(pairs)
    ]
    for copy in copies:
        copy.start()
    return copies


def small_project_kernel(
    x_hbm, gain_hbm, offset_hbm, left_w_hbm, left_b_hbm, right_w_hbm, right_b_hbm, pair_offset_hbm,
    cot_hbm, both_ref, normed_ref, inv_std_ref, spread_w_ref, gain_ref, pair_offset_ref, cot_ref,
    x_ref, offset_ref, left_w_ref, left_b_ref, right_w_ref, right_b_ref, wide_ref, semaphores,
):
    seqs, residues, _ = x_ref.shape
    depth = left_w_ref.shape[0]
    parts = 4
    part = seqs // parts
    copies = start_copies(
        tuple(
            (x_hbm.at[pl.ds(place * part, part)], x_ref.at[pl.ds(place * part, part)])
            for place in range(parts)
        )
        + (
            (left_w_hbm, left_w_ref),
            (right_w_hbm, right_w_ref),
            (gain_hbm, gain_ref),
            (offset_hbm, offset_ref),
            (left_b_hbm, left_b_ref),
            (right_b_hbm, right_b_ref),
            (cot_hbm, cot_ref),
            (pair_offset_hbm, pair_offset_ref),
        ),
        semaphores,
    )
    for copy in copies[:parts]:
        copy.wait()
    rows = x_ref[...].astype(F32).reshape(seqs * residues, x_ref.shape[2])
    normed, inv_std = normalise(rows)
    for copy in copies[parts:]:
        copy.wait()
    ln_out = (normed * gain_ref[...] + offset_ref[...]).astype(BF16)
    blocks = lane_block((seqs, LANES), depth)
    weight = jnp.concatenate(
        [left_w_ref[...]] * residues + [right_w_ref[...]] * residues, axis=0
    )
    wide = lax.dot_general(ln_out, weight, NT, preferred_element_type=F32)
    for place, bias_ref in enumerate((left_b_ref, right_b_ref)):
        bias = jnp.concatenate([bias_ref[...]] * residues, axis=1)
        wide_ref[place, 0 : seqs * residues, :] = wide[:, place * LANES : (place + 1) * LANES]
        own = pick(
            blocks, [wide_ref[place, pl.ds(p, seqs, stride=residues), :] for p in range(residues)]
        )
        both_ref[place] = (own + bias).astype(BF16)
    normed_ref[...] = normed
    inv_std_ref[...] = jnp.broadcast_to(inv_std, inv_std_ref.shape)
    spread_w_ref[...] = weight


def outer_flat(cot, sorted_wt_ref):
    return jnp.dot(cot, sorted_wt_ref[...], preferred_element_type=F32)


def outer_rows(flat, residues, turn_ref):
    columns = flat.shape[0] // residues
    depth = LANES // residues
    for tile in range(depth * depth // LANES):
        block = flat[:, tile * LANES : (tile + 1) * LANES]
        turned = exchange_blocks(
            [block[i * columns : (i + 1) * columns] for i in range(residues)], depth
        )
        for e in range(residues):
            turn_ref[pl.ds(tile * residues + e, columns, stride=depth), :] = turned[e]
    return turn_ref[0 : columns * depth, :].astype(BF16)


def outer_tiles(flat, residues):
    columns = flat.shape[0] // residues
    return jnp.concatenate(
        [
            jnp.concatenate(
                [
                    flat[i * columns + start : i * columns + start + 8, tile : tile + LANES]
                    for start in range(0, columns, 8)
                    for tile in range(0, flat.shape[1], LANES)
                ],
                axis=0,
            )
            for i in range(residues)
        ],
        axis=1,
    ).astype(BF16)


def blocks_apart(left, residues):
    depth = LANES // residues
    left = left.astype(F32)
    turned = [left] + [pltpu.roll(left, depth * t, 1) for t in range(1, residues)]
    blocks = lane_block(left.shape, depth)
    return jnp.concatenate(
        [
            jnp.concatenate(
                [
                    jnp.where(blocks == e, turned[(e - i) % residues], 0.0).astype(BF16)
                    for i in range(residues)
                ],
                axis=1,
            )
            for e in range(residues)
        ],
        axis=0,
    )


def column_pieces(left, outer, residues):
    seqs = left.shape[0]
    partial = lax.dot_general(
        blocks_apart(left, residues), outer, NT, preferred_element_type=F32
    )
    rows = [partial[e * seqs : (e + 1) * seqs] for e in range(residues)]
    half = lane_block(rows[0].shape, LANES // 2)
    source = 2 * (lane_block(rows[0].shape, residues) % 2) + half
    pieces = []
    for chip in range(residues):
        turned = []
        for e, row in enumerate(rows):
            count = (LANES // 2 * (e % 2 - chip // 2) + residues * (e // 2 - chip % 2)) % LANES
            turned.append(pltpu.roll(row, count, 1) if count else row)
        pieces.append(pick(source, turned))
    return pieces


def small_own_kernel(scale, own_ref, other_ref, w_ref, both_ref, spread_w_ref,
                     keep_ref, outer_near_ref, outer_far_ref, sorted_w_ref, sorted_wt_ref,
                     columns_w_ref, turn_refs, wide_ref):
    residues, columns, _ = own_ref.shape
    depth = LANES // residues
    wide_ref[0 : w_ref.shape[0], :] = w_ref[...].astype(F32)
    for d in range(depth):
        sorted_w_ref[d * depth : (d + 1) * depth, :] = wide_ref[
            pl.ds(d, depth, stride=depth), :
        ].astype(BF16)
    sorted_wt_ref[...] = (sorted_w_ref[...].astype(F32) * scale).astype(BF16).T
    shape = (columns_w_ref.shape[0], depth)
    row = lax.broadcasted_iota(jnp.int32, shape, 0)
    lane = lax.broadcasted_iota(jnp.int32, shape, 1)
    place = (row >> 3 & 7) * residues + 2 * (row >> 2 & 1) + (row >> 6)
    chosen = jnp.where(lane == place, 1.0, 0.0).astype(BF16)
    columns_w_ref[...] = jnp.dot(
        chosen, spread_w_ref[LANES : LANES + depth, :], preferred_element_type=F32
    ).astype(BF16)

    rank = lax.axis_index("res")
    own_is_near = lax.axis_index("seq") == lax.shift_right_logical(rank, 2)
    own = own_ref[...].reshape(residues * columns, LANES)
    other = other_ref[...].reshape(residues * columns, LANES)
    flat = outer_flat(jnp.where(own_is_near, own, other), sorted_wt_ref)
    pieces = column_pieces(both_ref[0], outer_tiles(flat, residues), residues)
    for place, piece in enumerate(pieces):
        keep_ref[place] = piece
    outer_near_ref[...] = outer_rows(flat, residues, turn_refs[0])
    flat = outer_flat(jnp.where(own_is_near, other, own), sorted_wt_ref)
    outer_far_ref[...] = outer_rows(flat, residues, turn_refs[1])


def small_partner_kernel(residues, got_ref, sorted_wt_ref, keep_ref, both_ref,
                         leaving_ref, keep_out_ref, right_ref):
    rank = lax.axis_index("res")
    seqs = got_ref.shape[1]
    cot = got_ref[2:4].reshape(2 * seqs, LANES)
    outer = outer_tiles(outer_flat(cot, sorted_wt_ref), residues)
    pieces = column_pieces(got_ref[0], outer, residues)
    right_ref[0] = both_ref[1]
    right_ref[1] = got_ref[1]
    for place, piece in enumerate(pieces):
        distance = lax.bitwise_xor(rank & 3, place)
        total = keep_ref[place] + piece
        keep_out_ref[distance] = total
        leaving_ref[distance, 2] = total.astype(BF16)
    for place in range(leaving_ref.shape[0]):
        leaving_ref[place, 0] = both_ref[1]
        leaving_ref[place, 1] = got_ref[1]


def small_finish_kernel(
    scale, right_ref, part_refs, swapped_ref, swapped_late_ref, both_ref, outer_near_ref, outer_far_ref,
    keep_ref, normed_ref, inv_std_ref, gain_ref, spread_w_ref, columns_w_ref, sorted_w_ref, offset_ref,
    grad_hbm, pair_hbm, grad_ref, pair_ref, near_ref, beyond_ref, turn_ref, lines_ref, semaphores,
):
    part_refs = [part_refs[1], part_refs[0], part_refs[2]]
    seqs, residues, _ = grad_ref.shape
    columns = pair_ref.shape[1]
    depth = LANES // residues
    ranks = columns // residues
    rank = lax.axis_index("res")
    mine = lax.axis_index("seq")
    here = rank & 3

    blocks_of = [right_ref] + list(part_refs)
    half = jnp.where(mine == lax.shift_right_logical(rank, 2), 0, 1)
    for mask, ref in enumerate(blocks_of):
        near_ref[mask] = ref[half]
    beyond_ref[0] = swapped_ref[0]
    beyond_ref[1] = part_refs[0][3]
    beyond_ref[2] = part_refs[1][3]
    beyond_ref[3] = swapped_late_ref[...]
    masks = [lax.bitwise_xor(here, place) for place in range(ranks)]
    right = jnp.concatenate(
        [
            jnp.concatenate([ref[mask] for mask in masks], axis=1)
            for ref in (near_ref, beyond_ref)
        ],
        axis=0,
    )
    left = jnp.concatenate([both_ref[0], swapped_ref[1]], axis=0)
    turn_ref[0 : columns * depth, :] = lax.dot_general(right, left, TN, preferred_element_type=F32) * scale
    tiles = []
    for tile in range(depth * depth // LANES):
        turned = exchange_blocks(
            [
                turn_ref[pl.ds(tile * residues + e, columns, stride=depth), :]
                for e in range(residues)
            ],
            depth,
        )
        tiles.append(jnp.concatenate(turned, axis=0))
    flat = jnp.concatenate(tiles, axis=1)
    rows = residues * columns
    parts = jnp.concatenate(split_two(flat), axis=0)
    pair = jnp.dot(parts, sorted_w_ref[...], preferred_element_type=F32)
    pair = pair[0:rows] + pair[rows : 2 * rows]
    pair_ref[...] = (pair + offset_ref[...]).astype(BF16).reshape(pair_ref.shape)
    pair_copy = pltpu.make_async_copy(pair_ref, pair_hbm, semaphores.at[1])
    pair_copy.start()

    right_all = jnp.concatenate(
        [ref[0] for ref in blocks_of] + [ref[1] for ref in blocks_of], axis=1
    )
    spots = [
        pl.ds(pl.multiple_of(lax.bitwise_xor(here, mask) * LANES, LANES), LANES)
        for mask in range(ranks)
    ]
    outer = jnp.concatenate(
        [outer_near_ref[spot, :] for spot in spots] + [outer_far_ref[spot, :] for spot in spots],
        axis=0,
    )
    left_cot = jnp.dot(right_all, outer, preferred_element_type=F32)
    right_cot = keep_ref[0]
    for part_ref in part_refs:
        right_cot = right_cot + part_ref[2].astype(F32)
    blocks = lane_block((seqs, LANES), depth)
    column = lane_block((seqs, LANES), 1) % residues
    spread = jnp.concatenate(
        [
            jnp.concatenate(
                [
                    jnp.where(blocks == place, left_cot, 0.0),
                    jnp.where(column == place, right_cot, 0.0),
                ],
                axis=1,
            )
            for place in range(residues)
        ],
        axis=0,
    )
    rows = residues * seqs
    parts = jnp.concatenate(split_two(spread), axis=0)
    weight = jnp.concatenate([spread_w_ref[0:LANES, :], columns_w_ref[...]], axis=0)
    ln_cot = jnp.dot(parts, weight, preferred_element_type=F32)
    ln_cot = ln_cot[0:rows] + ln_cot[rows : 2 * rows]
    tiles = range(lines_ref.shape[0])
    for place in range(residues):
        for tile in tiles:
            lines_ref[tile, pl.ds(place, seqs, stride=residues), :] = ln_cot[
                place * seqs : (place + 1) * seqs, tile * LANES : (tile + 1) * LANES
            ]
    gained = jnp.concatenate([lines_ref[tile, 0:rows, :] for tile in tiles], axis=1) * gain_ref[...]
    normed = normed_ref[...]
    grad = inv_std_ref[:, 0:1] * (
        gained
        - jnp.mean(gained, axis=-1, keepdims=True)
        - normed * jnp.mean(gained * normed, axis=-1, keepdims=True)
    )
    grad_ref[...] = grad.reshape(grad_ref.shape).astype(BF16)
    grad_copy = pltpu.make_async_copy(grad_ref, grad_hbm, semaphores.at[0])
    grad_copy.start()
    grad_copy.wait()
    pair_copy.wait()


def small_slice(
    homolog_matrix,
    standardizer_scaling,
    standardizer_offset,
    left_projection_matrix,
    left_offset_vector,
    right_projection_matrix,
    right_offset_vector,
    coupling_matrix,
    coupling_offset,
    coupling_cotangent,
):
    seqs, residues, features = homolog_matrix.shape
    depth = left_projection_matrix.shape[1]
    ranks = lax.axis_size("res")
    rows = seqs * residues
    scale = 1.0 / (seqs * lax.axis_size("seq"))
    rank = lax.axis_index("res")
    mine = lax.axis_index("seq")
    swap = [(0, 1), (1, 0)]
    limit = pltpu.CompilerParams(vmem_limit_bytes=8 * 1024 * 1024)
    vmem = pl.BlockSpec(memory_space=pltpu.VMEM)
    like = jax.ShapeDtypeStruct

    other_cot = lax.ppermute(coupling_cotangent, "seq", swap)
    hbm = pl.BlockSpec(memory_space=pltpu.HBM)
    pin = lambda array: pltpu.with_memory_space_constraint(array, pltpu.HBM)
    both, normed, inv_std, spread_w, gain, pair_offset, own_cot = pl.pallas_call(
        small_project_kernel,
        in_specs=[hbm] * 9,
        out_specs=[vmem] * 7,
        out_shape=(
            like((2, seqs, LANES), BF16),
            like((rows, features), F32),
            like((rows, LANES), F32),
            like((2 * LANES, features), BF16),
            like((1, features), F32),
            like((1, LANES), F32),
            like(coupling_cotangent.shape, BF16),
        ),
        scratch_shapes=[
            pltpu.VMEM(homolog_matrix.shape, BF16),
            pltpu.VMEM((1, features), F32),
            pltpu.VMEM((depth, features), BF16),
            pltpu.VMEM((1, depth), F32),
            pltpu.VMEM((depth, features), BF16),
            pltpu.VMEM((1, depth), F32),
            pltpu.VMEM((2, rows + 8, LANES), F32),
            pltpu.SemaphoreType.DMA((12,)),
        ],
        compiler_params=limit,
        name="project",
    )(
        *[
            pin(array)
            for array in (
                homolog_matrix,
                standardizer_scaling.reshape(1, -1),
                standardizer_offset.reshape(1, -1),
                left_projection_matrix.T,
                left_offset_vector.reshape(1, -1),
                right_projection_matrix.T,
                right_offset_vector.reshape(1, -1),
                coupling_offset.reshape(1, -1),
                coupling_cotangent,
            )
        ]
    )

    def swap_over(mask, value):
        return lax.ppermute(value, "res", [(source, source ^ mask) for source in range(ranks)])

    own_is_near = mine == lax.shift_right_logical(rank, 2)
    far_cot = jnp.where(own_is_near, other_cot, own_cot).reshape(2, seqs, LANES)
    beyond_two = swap_over(4, jnp.concatenate([both, far_cot]))

    half_rows = ranks // 2 * LANES
    turn = pltpu.VMEM((half_rows + depth, LANES), F32)
    keep, outer_near, outer_far, sorted_w, sorted_wt, columns_w = pl.pallas_call(
        functools.partial(small_own_kernel, scale),
        in_specs=[vmem] * 5,
        out_specs=[vmem] * 6,
        out_shape=(
            like((ranks // 2, seqs, LANES), F32),
            like((half_rows, LANES), BF16),
            like((half_rows, LANES), BF16),
            like(coupling_matrix.shape, BF16),
            like(coupling_matrix.shape[::-1], BF16),
            like((LANES, features), BF16),
        ),
        scratch_shapes=[
            [turn, turn],
            pltpu.VMEM((coupling_matrix.shape[0] + depth, LANES), F32),
        ],
        compiler_params=limit,
        name="own_pieces",
    )(own_cot, other_cot, coupling_matrix, both, spread_w)

    needed = jnp.where(own_is_near, beyond_two[1], both[1])
    swapped = lax.ppermute(jnp.stack([needed, both[0]]), "seq", swap)

    leaving_parts, keep, right = pl.pallas_call(
        functools.partial(small_partner_kernel, residues),
        in_specs=[vmem] * 4,
        out_specs=[vmem] * 3,
        out_shape=(
            like((ranks // 2, 3, seqs, LANES), BF16),
            like((ranks // 2, seqs, LANES), F32),
            like((2, seqs, LANES), BF16),
        ),
        compiler_params=limit,
        name="partner_pieces",
    )(beyond_two, sorted_wt, keep, both)

    diagonal = swap_over(3, leaving_parts[3])
    beside, across = [
        swap_over(mask, jnp.concatenate([leaving_parts[mask], swapped[0:1]])) for mask in (1, 2)
    ]
    swapped_late = lax.ppermute(
        jnp.where(own_is_near, diagonal[1], diagonal[0]), "seq", swap
    )

    pair_delta, gradient = pl.pallas_call(
        functools.partial(small_finish_kernel, scale),
        in_specs=[vmem, [vmem] * 3] + [vmem] * 13,
        out_specs=[pl.BlockSpec(memory_space=pl.ANY)] * 2,
        out_shape=(
            like(homolog_matrix.shape, BF16),
            like(coupling_cotangent.shape, BF16),
        ),
        scratch_shapes=[
            pltpu.VMEM(homolog_matrix.shape, BF16),
            pltpu.VMEM(coupling_cotangent.shape, BF16),
            pltpu.VMEM((ranks // 2, seqs, LANES), BF16),
            pltpu.VMEM((ranks // 2, seqs, LANES), BF16),
            turn,
            pltpu.VMEM((features // LANES, rows + 8, LANES), F32),
            pltpu.SemaphoreType.DMA((2,)),
        ],
        compiler_params=limit,
        name="finish",
    )(
        right,
        [across, beside, diagonal],
        swapped,
        swapped_late,
        both,
        outer_near,
        outer_far,
        keep,
        normed,
        inv_std,
        gain,
        spread_w,
        columns_w,
        sorted_w,
        pair_offset,
    )[::-1]
    return (pair_delta, gradient)


def body(*arrays):
    sequences = arrays[0].shape[0] * lax.axis_size("seq")
    if lax.axis_size("res") == 8 and sequences & (sequences - 1) == 0:
        return small_slice(*arrays)
    return wide_slice(*arrays)


def solution(mesh):
    return jax.shard_map(
        body,
        mesh=mesh,
        in_specs=(
            P(("grp", "seq"), "res", None),
            P(),
            P(),
            P(),
            P(),
            P(),
            P(),
            P(),
            P(),
            P(("grp", "res"), "seq", None),
        ),
        out_specs=(P(("grp", "res"), "seq", None), P(("grp", "seq"), "res", None)),
        check_vma=False,
    )
```

```python
import functools

import jax
import jax.numpy as jnp
from jax import lax
from jax.experimental import pallas as pl
from jax.experimental.pallas import tpu as pltpu
from jax.sharding import PartitionSpec as P

LANES = 128
BF16 = jnp.bfloat16
F32 = jnp.float32
NT = (((1,), (1,)), ((), ()))
TN = (((0,), (0,)), ((), ()))


def lane_block(shape, width):
    return lax.broadcasted_iota(jnp.int32, shape, 1) // width


def pick(blocks, pieces):
    result = pieces[0]
    for place in range(1, len(pieces)):
        result = jnp.where(blocks == place, pieces[place], result)
    return result


def split_three(value):
    top = value.astype(BF16)
    rest = value - top.astype(F32)
    middle = rest.astype(BF16)
    low = (rest - middle.astype(F32)).astype(BF16)
    return top, middle, low


def exchange_blocks(pieces, width):
    first, second, third, fourth = pieces
    blocks = lane_block(first.shape, width)
    odd, high = blocks % 2 == 1, blocks >= 2
    roll = lambda value, count: pltpu.roll(value, count * width, 1)
    first, second = jnp.where(odd, roll(second, 1), first), jnp.where(odd, second, roll(first, 3))
    third, fourth = jnp.where(odd, roll(fourth, 1), third), jnp.where(odd, fourth, roll(third, 3))
    return [
        jnp.where(high, roll(third, 2), first),
        jnp.where(high, roll(fourth, 2), second),
        jnp.where(high, third, roll(first, 2)),
        jnp.where(high, fourth, roll(second, 2)),
    ]


def split_two(value):
    top = value.astype(BF16)
    return top, (value - top.astype(F32)).astype(BF16)


def normalise(rows):
    centred = rows - jnp.mean(rows, axis=-1, keepdims=True)
    inv_std = lax.rsqrt(jnp.mean(centred * centred, axis=-1, keepdims=True) + 1e-05)
    return centred * inv_std, inv_std


def residue_rows(x_ref):
    return jnp.concatenate(
        [x_ref[:, place, :].astype(F32) for place in range(x_ref.shape[1])], axis=0
    )


def project_kernel(
    x_ref, gain_ref, offset_ref, left_w_ref, left_b_ref, right_w_ref, right_b_ref, w_ref,
    left_ref, right_ref, sorted_w_ref, wide_ref,
):
    seqs, residues, _ = x_ref.shape
    depth = left_w_ref.shape[0]
    normed, _ = normalise(residue_rows(x_ref))
    ln_out = (normed * gain_ref[...] + offset_ref[...]).astype(BF16)
    blocks = lane_block((seqs, LANES), depth)
    for weight_ref, bias_ref, out_ref in (
        (left_w_ref, left_b_ref, left_ref),
        (right_w_ref, right_b_ref, right_ref),
    ):
        weight = jnp.concatenate([weight_ref[...]] * residues, axis=0)
        bias = jnp.concatenate([bias_ref[...]] * residues, axis=1)
        wide = lax.dot_general(ln_out, weight, NT, preferred_element_type=F32)
        own = pick(blocks, [wide[p * seqs : (p + 1) * seqs] for p in range(residues)])
        out_ref[...] = (own + bias).astype(BF16)
    wide_ref[...] = w_ref[...].astype(F32)
    for d in range(depth):
        sorted_w_ref[d * depth : (d + 1) * depth, :] = wide_ref[
            pl.ds(d, depth, stride=depth), :
        ].astype(BF16)


def cot_kernel(scale, own_ref, other_ref, sorted_w_ref, left_ref, right_ref,
               send_ref, outer_ref, turn_ref):
    residues, columns, _ = own_ref.shape
    depth = sorted_w_ref.shape[0] // (LANES // residues)
    depth = LANES // residues
    first = lax.axis_index("seq") == 0
    own = own_ref[...].reshape(residues * columns, LANES)
    other = other_ref[...].reshape(residues * columns, LANES)
    low = jnp.where(first, own, other)
    high = jnp.where(first, other, own)
    both = jnp.concatenate([low, high], axis=0)
    flat = lax.dot_general(both, sorted_w_ref[...], NT, preferred_element_type=F32) * scale
    blocks = lane_block((columns, LANES), depth)
    for half in range(2):
        for tile in range(depth * depth // LANES):
            block = flat[
                half * residues * columns : (half + 1) * residues * columns,
                tile * LANES : (tile + 1) * LANES,
            ]
            turned = [block] + [pltpu.roll(block, depth * t, 1) for t in range(1, residues)]
            for e in range(residues):
                piece = pick(
                    blocks,
                    [
                        turned[(i - e) % residues][i * columns : (i + 1) * columns]
                        for i in range(residues)
                    ],
                )
                turn_ref[pl.ds(half * columns * depth + tile * residues + e, columns, stride=depth), :] = piece
    outer = turn_ref[...].astype(BF16)
    half_rows = columns * depth
    partial = lax.dot_general(left_ref[...], outer, NT, preferred_element_type=F32).astype(BF16)
    seqs = left_ref.shape[0]
    ranks = columns // residues
    for half in range(2):
        outer_ref[half] = outer[half * half_rows : (half + 1) * half_rows]
        for rank in range(ranks):
            at = (half * ranks + rank) * LANES
            send_ref[half, rank, 0:seqs, :] = right_ref[...]
            send_ref[half, rank, seqs : 2 * seqs, :] = partial[:, at : at + LANES]


def grad_kernel(steps, got_ref, outer_ref, x_ref, gain_ref, left_w_ref, right_w_ref,
                grad_ref, left_cot_ref, right_cot_ref):
    step = pl.program_id(0)
    _, ranks, twice, _ = got_ref.shape
    seqs = twice // 2
    residues = x_ref.shape[1]
    depth = LANES // residues

    @pl.when(step == 0)
    def _():
        left_cot_ref[...] = jnp.zeros_like(left_cot_ref)
        right_cot_ref[...] = jnp.zeros_like(right_cot_ref)

    places = [(half, rank) for half in range(2) for rank in range(ranks)]
    right_all = jnp.concatenate([got_ref[h, r, 0:seqs, :] for h, r in places], axis=1)
    outer = jnp.concatenate([outer_ref[0], outer_ref[1]], axis=0)
    left_cot_ref[...] += jnp.dot(right_all, outer, preferred_element_type=F32)
    total = got_ref[0, 0, seqs:twice, :].astype(F32)
    for h, r in places[1:]:
        total = total + got_ref[h, r, seqs:twice, :].astype(F32)
    right_cot_ref[...] += total

    @pl.when(step == steps - 1)
    def _():
        blocks = lane_block((seqs, LANES), depth)
        left_cot, right_cot = left_cot_ref[...], right_cot_ref[...]
        spread = jnp.concatenate(
            [
                jnp.concatenate(
                    [
                        jnp.where(blocks == place, left_cot, 0.0),
                        jnp.where(blocks == place, right_cot, 0.0),
                    ],
                    axis=1,
                )
                for place in range(residues)
            ],
            axis=0,
        )
        weight = jnp.concatenate(
            [left_w_ref[...]] * residues + [right_w_ref[...]] * residues, axis=0
        )
        rows = residues * seqs
        parts = jnp.concatenate(split_three(spread), axis=0)
        ln_cot = jnp.dot(parts, weight, preferred_element_type=F32)
        ln_cot = ln_cot[0:rows] + (ln_cot[rows : 2 * rows] + ln_cot[2 * rows : 3 * rows])
        gained = ln_cot * gain_ref[...]
        normed, inv_std = normalise(residue_rows(x_ref))
        grad = inv_std * (
            gained
            - jnp.mean(gained, axis=-1, keepdims=True)
            - normed * jnp.mean(gained * normed, axis=-1, keepdims=True)
        )
        for place in range(residues):
            grad_ref[:, place, :] = grad[place * seqs : (place + 1) * seqs].astype(BF16)


def pair_kernel(scale, got_ref, far_ref, left_ref, far_left_ref, sorted_w_ref, offset_ref,
                pair_ref, turn_ref):
    residues, columns, _ = pair_ref.shape
    depth = LANES // residues
    ranks = columns // residues
    mine = lax.axis_index("seq")
    near = jnp.concatenate([got_ref[mine, r] for r in range(ranks)], axis=1)
    far = jnp.concatenate([far_ref[r] for r in range(ranks)], axis=1)
    right = jnp.concatenate([near, far], axis=0)
    left = jnp.concatenate([left_ref[...], far_left_ref[...]], axis=0)
    turn_ref[...] = lax.dot_general(right, left, TN, preferred_element_type=F32) * scale
    blocks = lane_block((columns, LANES), depth)
    tiles = []
    for tile in range(depth * depth // LANES):
        pieces = [
            turn_ref[pl.ds(tile * residues + e, columns, stride=depth), :]
            for e in range(residues)
        ]
        rows = jnp.concatenate(pieces, axis=0)
        turned = [rows] + [pltpu.roll(rows, depth * t, 1) for t in range(1, residues)]
        tiles.append(
            jnp.concatenate(
                [
                    pick(
                        blocks,
                        [
                            turned[(e - i) % residues][e * columns : (e + 1) * columns]
                            for e in range(residues)
                        ],
                    )
                    for i in range(residues)
                ],
                axis=0,
            )
        )
    flat = jnp.concatenate(tiles, axis=1)
    rows = residues * columns
    parts = jnp.concatenate(split_three(flat), axis=0)
    pair = jnp.dot(parts, sorted_w_ref[...], preferred_element_type=F32)
    pair = pair[0:rows] + (pair[rows : 2 * rows] + pair[2 * rows : 3 * rows])
    pair_ref[...] = (pair + offset_ref[...]).astype(BF16).reshape(pair_ref.shape)


def wide_slice(
    homolog_matrix,
    standardizer_scaling,
    standardizer_offset,
    left_projection_matrix,
    left_offset_vector,
    right_projection_matrix,
    right_offset_vector,
    coupling_matrix,
    coupling_offset,
    coupling_cotangent,
):
    seqs, residues, features = homolog_matrix.shape
    depth = left_projection_matrix.shape[1]
    ranks = lax.axis_size("res")
    scale = 1.0 / (seqs * lax.axis_size("seq"))
    half_ranks = ranks // 2
    half_columns = half_ranks * residues
    step_ranks = 4
    columns = step_ranks * residues
    steps = half_ranks // step_ranks
    mine = lax.axis_index("seq")
    swap = [(0, 1), (1, 0)]

    other_cot = lax.ppermute(coupling_cotangent, "seq", swap)
    gain = standardizer_scaling.reshape(1, -1)
    left_w = left_projection_matrix.T
    right_w = right_projection_matrix.T

    left, right, sorted_w = pl.pallas_call(
        project_kernel,
        out_shape=(
            jax.ShapeDtypeStruct((seqs, LANES), BF16),
            jax.ShapeDtypeStruct((seqs, LANES), BF16),
            jax.ShapeDtypeStruct(coupling_matrix.shape, BF16),
        ),
        scratch_shapes=[pltpu.VMEM(coupling_matrix.shape, F32)],
        name="project",
    )(
        homolog_matrix,
        gain,
        standardizer_offset.reshape(1, -1),
        left_w,
        left_offset_vector.reshape(1, -1),
        right_w,
        right_offset_vector.reshape(1, -1),
        coupling_matrix,
    )

    whole = lambda shape: pl.BlockSpec(shape, lambda g: (0,) * len(shape))
    cot_block = pl.BlockSpec((residues, columns, LANES), lambda g: (0, g, 0))
    outer_block = pl.BlockSpec((2, columns * depth, LANES), lambda g: (0, g, 0))
    send_block = pl.BlockSpec((2, step_ranks, 2 * seqs, LANES), lambda g: (0, g, 0, 0))
    send, outer = pl.pallas_call(
        functools.partial(cot_kernel, scale),
        grid=(steps,),
        in_specs=[
            cot_block,
            cot_block,
            whole(sorted_w.shape),
            whole(left.shape),
            whole(right.shape),
        ],
        out_specs=(send_block, outer_block),
        out_shape=(
            jax.ShapeDtypeStruct((2, half_ranks, 2 * seqs, LANES), BF16),
            jax.ShapeDtypeStruct((2, half_columns * depth, LANES), BF16),
        ),
        scratch_shapes=[pltpu.VMEM((2 * columns * depth, LANES), F32)],
        name="cotangent",
    )(coupling_cotangent, other_cot, sorted_w, left, right)

    got = lax.all_to_all(
        send.reshape(ranks, 2 * seqs, LANES), "res", split_axis=0, concat_axis=0, tiled=True
    ).reshape(send.shape)

    leaving = lax.dynamic_index_in_dim(got, 1 - mine, 0, keepdims=False)[:, 0:seqs, :]
    far = lax.ppermute(jnp.concatenate([leaving, left[None]], axis=0), "seq", swap)

    gradient = pl.pallas_call(
        functools.partial(grad_kernel, steps),
        grid=(steps,),
        in_specs=[
            send_block,
            outer_block,
            whole(homolog_matrix.shape),
            whole(gain.shape),
            whole(left_w.shape),
            whole(right_w.shape),
        ],
        out_specs=whole(homolog_matrix.shape),
        out_shape=jax.ShapeDtypeStruct(homolog_matrix.shape, BF16),
        scratch_shapes=[pltpu.VMEM((seqs, LANES), F32)] * 2,
        name="gradient",
    )(got, outer, homolog_matrix, gain, left_w, right_w)

    pair_delta = pl.pallas_call(
        functools.partial(pair_kernel, scale),
        grid=(steps,),
        in_specs=[
            pl.BlockSpec((2, step_ranks, seqs, LANES), lambda g: (0, g, 0, 0)),
            pl.BlockSpec((step_ranks, seqs, LANES), lambda g: (g, 0, 0)),
            whole(left.shape),
            pl.BlockSpec((None, seqs, LANES), lambda g: (half_ranks, 0, 0)),
            whole(sorted_w.shape),
            whole((1, LANES)),
        ],
        out_specs=cot_block,
        out_shape=jax.ShapeDtypeStruct(coupling_cotangent.shape, BF16),
        scratch_shapes=[pltpu.VMEM((columns * depth, LANES), F32)],
        name="pair",
    )(got, far, left, far, sorted_w, coupling_offset.reshape(1, -1))
    return (pair_delta, gradient)


def fetch(source, target, semaphore):
    copy = pltpu.make_async_copy(source, target, semaphore)
    copy.start()
    return copy


def start_copies(pairs, semaphores):
    copies = [
        pltpu.make_async_copy(source, target, semaphores.at[place])
        for place, (source, target) in enumerate(pairs)
    ]
    for copy in copies:
        copy.start()
    return copies


def small_project_kernel(
    x_hbm, gain_hbm, offset_hbm, left_w_hbm, left_b_hbm, right_w_hbm, right_b_hbm, pair_offset_hbm,
    cot_hbm, both_ref, normed_ref, inv_std_ref, spread_w_ref, gain_ref, pair_offset_ref, cot_ref,
    x_ref, offset_ref, left_w_ref, left_b_ref, right_w_ref, right_b_ref, wide_ref, semaphores,
):
    seqs, residues, _ = x_ref.shape
    depth = left_w_ref.shape[0]
    parts = 4
    part = seqs // parts
    copies = start_copies(
        tuple(
            (x_hbm.at[pl.ds(place * part, part)], x_ref.at[pl.ds(place * part, part)])
            for place in range(parts)
        )
        + (
            (left_w_hbm, left_w_ref),
            (right_w_hbm, right_w_ref),
            (gain_hbm, gain_ref),
            (offset_hbm, offset_ref),
            (left_b_hbm, left_b_ref),
            (right_b_hbm, right_b_ref),
            (cot_hbm, cot_ref),
            (pair_offset_hbm, pair_offset_ref),
        ),
        semaphores,
    )
    for copy in copies[:parts]:
        copy.wait()
    rows = x_ref[...].astype(F32).reshape(seqs * residues, x_ref.shape[2])
    normed, inv_std = normalise(rows)
    for copy in copies[parts:]:
        copy.wait()
    ln_out = (normed * gain_ref[...] + offset_ref[...]).astype(BF16)
    blocks = lane_block((seqs, LANES), depth)
    weight = jnp.concatenate(
        [left_w_ref[...]] * residues + [right_w_ref[...]] * residues, axis=0
    )
    wide = lax.dot_general(ln_out, weight, NT, preferred_element_type=F32)
    for place, bias_ref in enumerate((left_b_ref, right_b_ref)):
        bias = jnp.concatenate([bias_ref[...]] * residues, axis=1)
        wide_ref[place, 0 : seqs * residues, :] = wide[:, place * LANES : (place + 1) * LANES]
        own = pick(
            blocks, [wide_ref[place, pl.ds(p, seqs, stride=residues), :] for p in range(residues)]
        )
        both_ref[place] = (own + bias).astype(BF16)
    normed_ref[...] = normed
    inv_std_ref[...] = jnp.broadcast_to(inv_std, inv_std_ref.shape)
    spread_w_ref[...] = weight


def outer_flat(cot, sorted_wt_ref):
    return jnp.dot(cot, sorted_wt_ref[...], preferred_element_type=F32)


def outer_rows(flat, residues, turn_ref):
    columns = flat.shape[0] // residues
    depth = LANES // residues
    for tile in range(depth * depth // LANES):
        block = flat[:, tile * LANES : (tile + 1) * LANES]
        turned = exchange_blocks(
            [block[i * columns : (i + 1) * columns] for i in range(residues)], depth
        )
        for e in range(residues):
            turn_ref[pl.ds(tile * residues + e, columns, stride=depth), :] = turned[e]
    return turn_ref[0 : columns * depth, :].astype(BF16)


def outer_tiles(flat, residues):
    columns = flat.shape[0] // residues
    return jnp.concatenate(
        [
            jnp.concatenate(
                [
                    flat[i * columns + start : i * columns + start + 8, tile : tile + LANES]
                    for start in range(0, columns, 8)
                    for tile in range(0, flat.shape[1], LANES)
                ],
                axis=0,
            )
            for i in range(residues)
        ],
        axis=1,
    ).astype(BF16)


def blocks_apart(left, residues):
    depth = LANES // residues
    left = left.astype(F32)
    turned = [left] + [pltpu.roll(left, depth * t, 1) for t in range(1, residues)]
    blocks = lane_block(left.shape, depth)
    return jnp.concatenate(
        [
            jnp.concatenate(
                [
                    jnp.where(blocks == e, turned[(e - i) % residues], 0.0).astype(BF16)
                    for i in range(residues)
                ],
                axis=1,
            )
            for e in range(residues)
        ],
        axis=0,
    )


def column_pieces(left, outer, residues):
    seqs = left.shape[0]
    partial = lax.dot_general(
        blocks_apart(left, residues), outer, NT, preferred_element_type=F32
    )
    rows = [partial[e * seqs : (e + 1) * seqs] for e in range(residues)]
    half = lane_block(rows[0].shape, LANES // 2)
    source = 2 * (lane_block(rows[0].shape, residues) % 2) + half
    pieces = []
    for chip in range(residues):
        turned = []
        for e, row in enumerate(rows):
            count = (LANES // 2 * (e % 2 - chip // 2) + residues * (e // 2 - chip % 2)) % LANES
            turned.append(pltpu.roll(row, count, 1) if count else row)
        pieces.append(pick(source, turned))
    return pieces


def small_own_kernel(scale, own_ref, other_ref, w_ref, both_ref, spread_w_ref,
                     keep_ref, outer_near_ref, outer_far_ref, sorted_w_ref, sorted_wt_ref,
                     columns_w_ref, turn_refs, wide_ref):
    residues, columns, _ = own_ref.shape
    depth = LANES // residues
    wide_ref[0 : w_ref.shape[0], :] = w_ref[...].astype(F32)
    for d in range(depth):
        sorted_w_ref[d * depth : (d + 1) * depth, :] = wide_ref[
            pl.ds(d, depth, stride=depth), :
        ].astype(BF16)
    sorted_wt_ref[...] = (sorted_w_ref[...].astype(F32) * scale).astype(BF16).T
    shape = (columns_w_ref.shape[0], depth)
    row = lax.broadcasted_iota(jnp.int32, shape, 0)
    lane = lax.broadcasted_iota(jnp.int32, shape, 1)
    place = (row >> 3 & 7) * residues + 2 * (row >> 2 & 1) + (row >> 6)
    chosen = jnp.where(lane == place, 1.0, 0.0).astype(BF16)
    columns_w_ref[...] = jnp.dot(
        chosen, spread_w_ref[LANES : LANES + depth, :], preferred_element_type=F32
    ).astype(BF16)

    rank = lax.axis_index("res")
    own_is_near = lax.axis_index("seq") == lax.shift_right_logical(rank, 2)
    own = own_ref[...].reshape(residues * columns, LANES)
    other = other_ref[...].reshape(residues * columns, LANES)
    flat = outer_flat(jnp.where(own_is_near, own, other), sorted_wt_ref)
    pieces = column_pieces(both_ref[0], outer_tiles(flat, residues), residues)
    for place, piece in enumerate(pieces):
        keep_ref[place] = piece
    outer_near_ref[...] = outer_rows(flat, residues, turn_refs[0])
    flat = outer_flat(jnp.where(own_is_near, other, own), sorted_wt_ref)
    outer_far_ref[...] = outer_rows(flat, residues, turn_refs[1])


def small_partner_kernel(residues, got_ref, sorted_wt_ref, keep_ref, both_ref,
                         leaving_ref, keep_out_ref, right_ref):
    rank = lax.axis_index("res")
    seqs = got_ref.shape[1]
    cot = got_ref[2:4].reshape(2 * seqs, LANES)
    outer = outer_tiles(outer_flat(cot, sorted_wt_ref), residues)
    pieces = column_pieces(got_ref[0], outer, residues)
    right_ref[0] = both_ref[1]
    right_ref[1] = got_ref[1]
    for place, piece in enumerate(pieces):
        distance = lax.bitwise_xor(rank & 3, place)
        total = keep_ref[place] + piece
        keep_out_ref[distance] = total
        leaving_ref[distance, 2] = total.astype(BF16)
    for place in range(leaving_ref.shape[0]):
        leaving_ref[place, 0] = both_ref[1]
        leaving_ref[place, 1] = got_ref[1]


def small_finish_kernel(
    scale, right_ref, part_refs, swapped_ref, swapped_late_ref, both_ref, outer_near_ref, outer_far_ref,
    keep_ref, normed_ref, inv_std_ref, gain_ref, spread_w_ref, columns_w_ref, sorted_w_ref, offset_ref,
    grad_hbm, pair_hbm, grad_ref, pair_ref, near_ref, beyond_ref, turn_ref, lines_ref, semaphores,
):
    part_refs = [part_refs[1], part_refs[0], part_refs[2]]
    seqs, residues, _ = grad_ref.shape
    columns = pair_ref.shape[1]
    depth = LANES // residues
    ranks = columns // residues
    rank = lax.axis_index("res")
    mine = lax.axis_index("seq")
    here = rank & 3

    blocks_of = [right_ref] + list(part_refs)
    right_all = jnp.concatenate(
        [ref[0] for ref in blocks_of] + [ref[1] for ref in blocks_of], axis=1
    )
    spots = [
        pl.ds(pl.multiple_of(lax.bitwise_xor(here, mask) * LANES, LANES), LANES)
        for mask in range(ranks)
    ]
    outer = jnp.concatenate(
        [outer_near_ref[spot, :] for spot in spots] + [outer_far_ref[spot, :] for spot in spots],
        axis=0,
    )
    left_cot = jnp.dot(right_all, outer, preferred_element_type=F32)
    right_cot = keep_ref[0]
    for part_ref in part_refs:
        right_cot = right_cot + part_ref[2].astype(F32)
    blocks = lane_block((seqs, LANES), depth)
    column = lane_block((seqs, LANES), 1) % residues
    spread = jnp.concatenate(
        [
            jnp.concatenate(
                [
                    jnp.where(blocks == place, left_cot, 0.0),
                    jnp.where(column == place, right_cot, 0.0),
                ],
                axis=1,
            )
            for place in range(residues)
        ],
        axis=0,
    )
    rows = residues * seqs
    parts = jnp.concatenate(split_two(spread), axis=0)
    weight = jnp.concatenate([spread_w_ref[0:LANES, :], columns_w_ref[...]], axis=0)
    ln_cot = jnp.dot(parts, weight, preferred_element_type=F32)
    ln_cot = ln_cot[0:rows] + ln_cot[rows : 2 * rows]
    tiles = range(lines_ref.shape[0])
    for place in range(residues):
        for tile in tiles:
            lines_ref[tile, pl.ds(place, seqs, stride=residues), :] = ln_cot[
                place * seqs : (place + 1) * seqs, tile * LANES : (tile + 1) * LANES
            ]
    gained = jnp.concatenate([lines_ref[tile, 0:rows, :] for tile in tiles], axis=1) * gain_ref[...]
    normed = normed_ref[...]
    inv_std = jnp.concatenate([inv_std_ref[...]] * len(tiles), axis=1)
    grad = inv_std * (
        gained
        - jnp.mean(gained, axis=-1, keepdims=True)
        - normed * jnp.mean(gained * normed, axis=-1, keepdims=True)
    )
    grad_ref[...] = grad.reshape(grad_ref.shape).astype(BF16)
    grad_copy = pltpu.make_async_copy(grad_ref, grad_hbm, semaphores.at[0])
    grad_copy.start()

    half = jnp.where(mine == lax.shift_right_logical(rank, 2), 0, 1)
    for mask, ref in enumerate(blocks_of):
        near_ref[mask] = ref[half]
    beyond_ref[0] = swapped_ref[0]
    beyond_ref[1] = part_refs[0][3]
    beyond_ref[2] = part_refs[1][3]
    beyond_ref[3] = swapped_late_ref[...]
    masks = [lax.bitwise_xor(here, place) for place in range(ranks)]
    right = jnp.concatenate(
        [
            jnp.concatenate([ref[mask] for mask in masks], axis=1)
            for ref in (near_ref, beyond_ref)
        ],
        axis=0,
    )
    left = jnp.concatenate([both_ref[0], swapped_ref[1]], axis=0)
    turn_ref[0 : columns * depth, :] = lax.dot_general(right, left, TN, preferred_element_type=F32) * scale
    tiles = []
    for tile in range(depth * depth // LANES):
        turned = exchange_blocks(
            [
                turn_ref[pl.ds(tile * residues + e, columns, stride=depth), :]
                for e in range(residues)
            ],
            depth,
        )
        tiles.append(jnp.concatenate(turned, axis=0))
    flat = jnp.concatenate(tiles, axis=1)
    rows = residues * columns
    parts = jnp.concatenate(split_two(flat), axis=0)
    pair = jnp.dot(parts, sorted_w_ref[...], preferred_element_type=F32)
    pair = pair[0:rows] + pair[rows : 2 * rows]
    pair_ref[...] = (pair + offset_ref[...]).astype(BF16).reshape(pair_ref.shape)
    pair_copy = pltpu.make_async_copy(pair_ref, pair_hbm, semaphores.at[1])
    pair_copy.start()
    grad_copy.wait()
    pair_copy.wait()


def small_slice(
    homolog_matrix,
    standardizer_scaling,
    standardizer_offset,
    left_projection_matrix,
    left_offset_vector,
    right_projection_matrix,
    right_offset_vector,
    coupling_matrix,
    coupling_offset,
    coupling_cotangent,
):
    seqs, residues, features = homolog_matrix.shape
    depth = left_projection_matrix.shape[1]
    ranks = lax.axis_size("res")
    rows = seqs * residues
    scale = 1.0 / (seqs * lax.axis_size("seq"))
    rank = lax.axis_index("res")
    mine = lax.axis_index("seq")
    swap = [(0, 1), (1, 0)]
    limit = pltpu.CompilerParams(vmem_limit_bytes=8 * 1024 * 1024)
    vmem = pl.BlockSpec(memory_space=pltpu.VMEM)
    like = jax.ShapeDtypeStruct

    other_cot = lax.ppermute(coupling_cotangent, "seq", swap)
    hbm = pl.BlockSpec(memory_space=pltpu.HBM)
    pin = lambda array: pltpu.with_memory_space_constraint(array, pltpu.HBM)
    both, normed, inv_std, spread_w, gain, pair_offset, own_cot = pl.pallas_call(
        small_project_kernel,
        in_specs=[hbm] * 9,
        out_specs=[vmem] * 7,
        out_shape=(
            like((2, seqs, LANES), BF16),
            like((rows, features), F32),
            like((rows, LANES), F32),
            like((2 * LANES, features), BF16),
            like((1, features), F32),
            like((1, LANES), F32),
            like(coupling_cotangent.shape, BF16),
        ),
        scratch_shapes=[
            pltpu.VMEM(homolog_matrix.shape, BF16),
            pltpu.VMEM((1, features), F32),
            pltpu.VMEM((depth, features), BF16),
            pltpu.VMEM((1, depth), F32),
            pltpu.VMEM((depth, features), BF16),
            pltpu.VMEM((1, depth), F32),
            pltpu.VMEM((2, rows + 8, LANES), F32),
            pltpu.SemaphoreType.DMA((12,)),
        ],
        compiler_params=limit,
        name="project",
    )(
        *[
            pin(array)
            for array in (
                homolog_matrix,
                standardizer_scaling.reshape(1, -1),
                standardizer_offset.reshape(1, -1),
                left_projection_matrix.T,
                left_offset_vector.reshape(1, -1),
                right_projection_matrix.T,
                right_offset_vector.reshape(1, -1),
                coupling_offset.reshape(1, -1),
                coupling_cotangent,
            )
        ]
    )

    def swap_over(mask, value):
        return lax.ppermute(value, "res", [(source, source ^ mask) for source in range(ranks)])

    own_is_near = mine == lax.shift_right_logical(rank, 2)
    far_cot = jnp.where(own_is_near, other_cot, own_cot).reshape(2, seqs, LANES)
    beyond_two = swap_over(4, jnp.concatenate([both, far_cot]))

    half_rows = ranks // 2 * LANES
    turn = pltpu.VMEM((half_rows + depth, LANES), F32)
    keep, outer_near, outer_far, sorted_w, sorted_wt, columns_w = pl.pallas_call(
        functools.partial(small_own_kernel, scale),
        in_specs=[vmem] * 5,
        out_specs=[vmem] * 6,
        out_shape=(
            like((ranks // 2, seqs, LANES), F32),
            like((half_rows, LANES), BF16),
            like((half_rows, LANES), BF16),
            like(coupling_matrix.shape, BF16),
            like(coupling_matrix.shape[::-1], BF16),
            like((LANES, features), BF16),
        ),
        scratch_shapes=[
            [turn, turn],
            pltpu.VMEM((coupling_matrix.shape[0] + depth, LANES), F32),
        ],
        compiler_params=limit,
        name="own_pieces",
    )(own_cot, other_cot, coupling_matrix, both, spread_w)

    needed = jnp.where(own_is_near, beyond_two[1], both[1])
    swapped = lax.ppermute(jnp.stack([needed, both[0]]), "seq", swap)

    leaving_parts, keep, right = pl.pallas_call(
        functools.partial(small_partner_kernel, residues),
        in_specs=[vmem] * 4,
        out_specs=[vmem] * 3,
        out_shape=(
            like((ranks // 2, 3, seqs, LANES), BF16),
            like((ranks // 2, seqs, LANES), F32),
            like((2, seqs, LANES), BF16),
        ),
        compiler_params=limit,
        name="partner_pieces",
    )(beyond_two, sorted_wt, keep, both)

    diagonal = swap_over(3, leaving_parts[3])
    beside, across = [
        swap_over(mask, jnp.concatenate([leaving_parts[mask], swapped[0:1]])) for mask in (1, 2)
    ]
    swapped_late = lax.ppermute(
        jnp.where(own_is_near, diagonal[1], diagonal[0]), "seq", swap
    )

    pair_delta, gradient = pl.pallas_call(
        functools.partial(small_finish_kernel, scale),
        in_specs=[vmem, [vmem] * 3] + [vmem] * 13,
        out_specs=[pl.BlockSpec(memory_space=pl.ANY)] * 2,
        out_shape=(
            like(homolog_matrix.shape, BF16),
            like(coupling_cotangent.shape, BF16),
        ),
        scratch_shapes=[
            pltpu.VMEM(homolog_matrix.shape, BF16),
            pltpu.VMEM(coupling_cotangent.shape, BF16),
            pltpu.VMEM((ranks // 2, seqs, LANES), BF16),
            pltpu.VMEM((ranks // 2, seqs, LANES), BF16),
            turn,
            pltpu.VMEM((features // LANES, rows + 8, LANES), F32),
            pltpu.SemaphoreType.DMA((2,)),
        ],
        compiler_params=limit,
        name="finish",
    )(
        right,
        [across, beside, diagonal],
        swapped,
        swapped_late,
        both,
        outer_near,
        outer_far,
        keep,
        normed,
        inv_std,
        gain,
        spread_w,
        columns_w,
        sorted_w,
        pair_offset,
    )[::-1]
    return (pair_delta, gradient)


def body(*arrays):
    sequences = arrays[0].shape[0] * lax.axis_size("seq")
    if lax.axis_size("res") == 8 and sequences & (sequences - 1) == 0:
        return small_slice(*arrays)
    return wide_slice(*arrays)


def solution(mesh):
    return jax.shard_map(
        body,
        mesh=mesh,
        in_specs=(
            P(("grp", "seq"), "res", None),
            P(),
            P(),
            P(),
            P(),
            P(),
            P(),
            P(),
            P(),
            P(("grp", "res"), "seq", None),
        ),
        out_specs=(P(("grp", "res"), "seq", None), P(("grp", "seq"), "res", None)),
        check_vma=False,
    )
```
